32 devices in a mesh: wide: 8 (over y, x, core), narrow: 4 (over z).
Axes of the slice: x: 2, y: 2, z: 4, core: 2. Of those that a mesh axis runs over, the one named last changes fastest.
Arguments:
- views: bfloat16 [8, 4, 256, 576], P('wide', None, 'narrow'), may hold values from -6 to 6
- render_w: float32 [8, 12, 4, 64, 64], P('wide'), may hold values from 0.02 to 0.3
- targets: bfloat16 [8, 12, 3, 16384], P('wide', None, None, 'narrow'), may hold values from 0 to 1
- pix_mask: int32 [8, 12, 16384], P('wide', None, 'narrow'), may hold values 0 or 1
- pairs: int32 [8, 2, 8192], P('wide', None, 'narrow'), may hold values from 0 to 49151, as said below
- view_count: int32 [8], P('wide'), may hold values from 1 to 12, as said below
- pair_total: int32 [1], replicated, may hold values from 8192 to 65536
- embed_weight: float32 [576, 1024], P(None, ('wide', 'narrow')), may hold values from -0.25 to 0.25
- embed_first: float32 [576, 1024], P(None, ('wide', 'narrow')), may hold values from -1.9073486e-06 to 1.9073486e-06
- embed_second: float32 [576, 1024], P(None, ('wide', 'narrow')), may hold values from 3.766475e-13 to 1.50659e-12
- mixer_weight: float32 [1024, 3072], P(('wide', 'narrow')), may hold values from -0.1875 to 0.1875
- mixer_first: float32 [1024, 3072], P(('wide', 'narrow')), may hold values from -1.9073486e-06 to 1.9073486e-06
- mixer_second: float32 [1024, 3072], P(('wide', 'narrow')), may hold values from 3.766475e-13 to 1.50659e-12
- merge_weight: float32 [1024, 1024], P(('wide', 'narrow')), may hold values from -0.75 to 0.75
- merge_first: float32 [1024, 1024], P(('wide', 'narrow')), may hold values from -1.9073486e-06 to 1.9073486e-06
- merge_second: float32 [1024, 1024], P(('wide', 'narrow')), may hold values from 3.766475e-13 to 1.50659e-12
- expand_weight: float32 [1024, 4096], P(('wide', 'narrow')), may hold values from -0.1875 to 0.1875
- expand_first: float32 [1024, 4096], P(('wide', 'narrow')), may hold values from -1.9073486e-06 to 1.9073486e-06
- expand_second: float32 [1024, 4096], P(('wide', 'narrow')), may hold values from 3.766475e-13 to 1.50659e-12
- shrink_weight: float32 [4096, 1024], P(('wide', 'narrow')), may hold values from -0.09375 to 0.09375
- shrink_first: float32 [4096, 1024], P(('wide', 'narrow')), may hold values from -1.9073486e-06 to 1.9073486e-06
- shrink_second: float32 [4096, 1024], P(('wide', 'narrow')), may hold values from 3.766475e-13 to 1.50659e-12
- unpatch_weight: float32 [1024, 768], P(('wide', 'narrow')), may hold values from -0.1875 to 0.1875
- unpatch_first: float32 [1024, 768], P(('wide', 'narrow')), may hold values from -1.9073486e-06 to 1.9073486e-06
- unpatch_second: float32 [1024, 768], P(('wide', 'narrow')), may hold values from 3.766475e-13 to 1.50659e-12
- norm_params: float32 [6, 1024], P(None, ('wide', 'narrow')), may hold values from 0.5 to 1.5
- norm_first: float32 [6, 1024], P(None, ('wide', 'narrow')), may hold values from -1.9073486e-06 to 1.9073486e-06
- norm_second: float32 [6, 1024], P(None, ('wide', 'narrow')), may hold values from 3.766475e-13 to 1.50659e-12
Outputs:
- embed_new: float32 [576, 1024], P(None, ('wide', 'narrow'))
- embed_first_new: float32 [576, 1024], P(None, ('wide', 'narrow'))
- embed_second_new: float32 [576, 1024], P(None, ('wide', 'narrow'))
- mixer_new: float32 [1024, 3072], P(('wide', 'narrow'))
- mixer_first_new: float32 [1024, 3072], P(('wide', 'narrow'))
- mixer_second_new: float32 [1024, 3072], P(('wide', 'narrow'))
- merge_new: float32 [1024, 1024], P(('wide', 'narrow'))
- merge_first_new: float32 [1024, 1024], P(('wide', 'narrow'))
- merge_second_new: float32 [1024, 1024], P(('wide', 'narrow'))
- expand_new: float32 [1024, 4096], P(('wide', 'narrow'))
- expand_first_new: float32 [1024, 4096], P(('wide', 'narrow'))
- expand_second_new: float32 [1024, 4096], P(('wide', 'narrow'))
- shrink_new: float32 [4096, 1024], P(('wide', 'narrow'))
- shrink_first_new: float32 [4096, 1024], P(('wide', 'narrow'))
- shrink_second_new: float32 [4096, 1024], P(('wide', 'narrow'))
- unpatch_new: float32 [1024, 768], P(('wide', 'narrow'))
- unpatch_first_new: float32 [1024, 768], P(('wide', 'narrow'))
- unpatch_second_new: float32 [1024, 768], P(('wide', 'narrow'))
- norm_new: float32 [6, 1024], P(None, ('wide', 'narrow'))
- norm_first_new: float32 [6, 1024], P(None, ('wide', 'narrow'))
- norm_second_new: float32 [6, 1024], P(None, ('wide', 'narrow'))
- loss: float32 [], replicated
- grad_norm: float32 [], replicated
The draws below stay inside these ranges and needn't reach their ends.
Inputs may be any that keep to these rules, and one draw needn't show every extreme that they name: `pairs`: each column holds two pixels of one device's block of the same target slot and patch, next to each other in a row or in a column of the patch, indexed as in the reference program. `view_count`: mostly few views; some scene has 12.
All inputs are finite; a program needn't handle non-finite values. No bound on the sum of `pix_mask` on one device may be relied on, other than what follows from the above.
Results may differ from the reference program's by a relative error of at most 0.02.
Values may be sent and summed in bfloat16 or wider, within the bound.
A program may use at most 192 MiB of HBM per device.

```python
import math
import jax
import jax.numpy as jnp
from jax import lax

D = 1024
HEADS = 16
HD = 64
FF = 4096
P_SIZE = 8
NVIEW = 4
TMAX = 12
STEP = 10
QDEV = 64
PP = 64
PD = 576
GP = 768
Q = 256
SEQ = 1024
PAIRS_DEV = 2048
SCENES = 8
NPARAM = 13965312
N_NARROW = 4


def draw_pairs(key, part):
    key = jax.random.fold_in(key, 11)
    first_key, pick_key = jax.random.split(key)
    span = TMAX * QDEV * P_SIZE * P_SIZE
    shape = (SCENES, N_NARROW * PAIRS_DEV)
    first = jax.random.randint(first_key, shape, 0, span)
    picker = jax.random.randint(pick_key, shape, 0, 2)
    across = first + 1 - 2 * (first % 2)
    downward = first + P_SIZE - 2 * P_SIZE * (first // P_SIZE % 2)
    second = jnp.where(picker == 0, across, downward)
    return jnp.stack([first, second], 1).astype(jnp.int32)


def draw_view_count(key, part):
    key = jax.random.fold_in(key, 5)
    key_one, key_two, key_three, key_four = jax.random.split(key, 4)
    factor_one = jax.random.randint(key_one, (SCENES,), 0, TMAX)
    factor_two = jax.random.randint(key_two, (SCENES,), 0, TMAX)
    factor_three = jax.random.randint(key_three, (SCENES,), 0, TMAX)
    counts = 1 + factor_one * factor_two * factor_three // ((TMAX - 1) * (TMAX - 1))
    places = jax.random.permutation(key_four, SCENES)
    counts = counts.at[places[0]].set(TMAX).at[places[1]].set(1)
    return counts.astype(jnp.int32)


def plant(result, own_key, least, top_value):
    longest = result.shape.index(max(result.shape))
    spots = []
    for shift in (0, 1):
        where = [jax.random.randint(jax.random.fold_in(own_key, axis), (), 0, length) for axis, length in enumerate(result.shape)]
        where[longest] = (where[longest] + shift) % result.shape[longest]
        spots.append(tuple(where))
    return result.at[spots[0]].set(least).at[spots[1]].set(top_value)


def shard_levels(rng, shape, cuts, low, top_value):
    def one(axis_at, parts):
        draws = jax.random.uniform(jax.random.fold_in(jax.random.fold_in(rng, 6), axis_at), (parts,), jnp.float32, low / len(cuts), top_value / len(cuts))
        return jnp.repeat(jnp.exp(draws), shape[axis_at] // parts).reshape((-1,) + (1,) * (len(shape) - axis_at - 1))

    factor_of = one(*cuts[0])
    for cut in cuts[1:]:
        factor_of = factor_of * one(*cut)
    return factor_of


def scatter_about(key, shape, deviation, limit, pieces=(), dtype=jnp.bfloat16):
    factor_of = shard_levels(key, shape, pieces, -0.22, 0.18) if pieces else 1.0
    result = jax.random.normal(key, shape, jnp.float32) * deviation * factor_of
    return jnp.minimum(jnp.maximum(result, -limit), limit).astype(dtype)


def setup_inputs(seed: int = 0) -> dict:
    key_list = jax.random.split(jax.random.key(seed), 29)
    views = scatter_about(key_list[0], (SCENES, NVIEW, Q, PD), 1.0, 6.0, ((0, 8), (2, 4)))
    render_w = jnp.clip(jnp.exp(math.log(0.3) - 2.7080503 * jax.random.uniform(key_list[1], (SCENES, TMAX, NVIEW, PP, PP), jnp.float32) ** shard_levels(key_list[1], (SCENES, TMAX, NVIEW, PP, PP), ((0, 8),), -0.2, 0.2)), 0.02, 0.3)
    targets = jnp.clip(1.0 * jax.random.uniform(key_list[2], (SCENES, TMAX, 3, Q * PP), jnp.float32) ** shard_levels(key_list[2], (SCENES, TMAX, 3, Q * PP), ((0, 8), (3, 4)), -0.2, 0.2), 0.0, 1.0).astype(jnp.bfloat16)
    pix_mask = plant((jax.random.randint(key_list[3], (SCENES, TMAX, Q * PP), 0, 4) < 3).astype(jnp.int32), jax.random.fold_in(key_list[3], 1), 0, 1)
    pairs = draw_pairs(jax.random.fold_in(key_list[28], 71), 0)
    view_count = draw_view_count(jax.random.fold_in(key_list[28], 71), 0)
    pair_total = jax.random.randint(key_list[6], (1,), SCENES * N_NARROW * PAIRS_DEV // 8, SCENES * N_NARROW * PAIRS_DEV + 1).astype(jnp.int32)
    embed_weight = scatter_about(key_list[7], (PD, D), PD ** -0.5, 0.25, ((1, 32),), jnp.float32)
    embed_first = scatter_about(key_list[8], (PD, D), (0.00111 * NPARAM ** -0.5), 1.9073486328125e-06, ((1, 32),), jnp.float32)
    embed_second = jnp.clip(jnp.exp(math.log(1.5065899916510972e-12) - 1.3862944 * jax.random.uniform(key_list[9], (PD, D), jnp.float32) ** shard_levels(key_list[9], (PD, D), ((1, 32),), -0.2, 0.2)), 3.766474979127743e-13, 1.5065899916510972e-12)
    mixer_weight = scatter_about(key_list[10], (D, 3 * D), D ** -0.5, 0.1875, ((0, 32),), jnp.float32)
    mixer_first = scatter_about(key_list[11], (D, 3 * D), (0.00111 * NPARAM ** -0.5), 1.9073486328125e-06, ((0, 32),), jnp.float32)
    mixer_second = jnp.clip(jnp.exp(math.log(1.5065899916510972e-12) - 1.3862944 * jax.random.uniform(key_list[12], (D, 3 * D), jnp.float32) ** shard_levels(key_list[12], (D, 3 * D), ((0, 32),), -0.2, 0.2)), 3.766474979127743e-13, 1.5065899916510972e-12)
    merge_weight = scatter_about(key_list[13], (D, D), (max(1, D * 64 // SEQ)) ** -0.5, 0.75, ((0, 32),), jnp.float32)
    merge_first = scatter_about(key_list[14], (D, D), (0.00111 * NPARAM ** -0.5), 1.9073486328125e-06, ((0, 32),), jnp.float32)
    merge_second = jnp.clip(jnp.exp(math.log(1.5065899916510972e-12) - 1.3862944 * jax.random.uniform(key_list[15], (D, D), jnp.float32) ** shard_levels(key_list[15], (D, D), ((0, 32),), -0.2, 0.2)), 3.766474979127743e-13, 1.5065899916510972e-12)
    expand_weight = scatter_about(key_list[16], (D, FF), D ** -0.5, 0.1875, ((0, 32),), jnp.float32)
    expand_first = scatter_about(key_list[17], (D, FF), (0.00111 * NPARAM ** -0.5), 1.9073486328125e-06, ((0, 32),), jnp.float32)
    expand_second = jnp.clip(jnp.exp(math.log(1.5065899916510972e-12) - 1.3862944 * jax.random.uniform(key_list[18], (D, FF), jnp.float32) ** shard_levels(key_list[18], (D, FF), ((0, 32),), -0.2, 0.2)), 3.766474979127743e-13, 1.5065899916510972e-12)
    shrink_weight = scatter_about(key_list[19], (FF, D), FF ** -0.5, 0.09375, ((0, 32),), jnp.float32)
    shrink_first = scatter_about(key_list[20], (FF, D), (0.00111 * NPARAM ** -0.5), 1.9073486328125e-06, ((0, 32),), jnp.float32)
    shrink_second = jnp.clip(jnp.exp(math.log(1.5065899916510972e-12) - 1.3862944 * jax.random.uniform(key_list[21], (FF, D), jnp.float32) ** shard_levels(key_list[21], (FF, D), ((0, 32),), -0.2, 0.2)), 3.766474979127743e-13, 1.5065899916510972e-12)
    unpatch_weight = scatter_about(key_list[22], (D, GP), D ** -0.5, 0.1875, ((0, 32),), jnp.float32)
    unpatch_first = scatter_about(key_list[23], (D, GP), (0.00111 * NPARAM ** -0.5), 1.9073486328125e-06, ((0, 32),), jnp.float32)
    unpatch_second = jnp.clip(jnp.exp(math.log(1.5065899916510972e-12) - 1.3862944 * jax.random.uniform(key_list[24], (D, GP), jnp.float32) ** shard_levels(key_list[24], (D, GP), ((0, 32),), -0.2, 0.2)), 3.766474979127743e-13, 1.5065899916510972e-12)
    norm_params = jnp.clip(1.0 + 0.1 * jax.random.normal(key_list[25], (6, D), jnp.float32), 0.5, 1.5)
    norm_first = scatter_about(key_list[26], (6, D), (0.00111 * NPARAM ** -0.5), 1.9073486328125e-06, ((1, 32),), jnp.float32)
    norm_second = jnp.clip(jnp.exp(math.log(1.5065899916510972e-12) - 1.3862944 * jax.random.uniform(key_list[27], (6, D), jnp.float32) ** shard_levels(key_list[27], (6, D), ((1, 32),), -0.2, 0.2)), 3.766474979127743e-13, 1.5065899916510972e-12)
    return dict(views=views, render_w=render_w, targets=targets, pix_mask=pix_mask, pairs=pairs, view_count=view_count, pair_total=pair_total, embed_weight=embed_weight, embed_first=embed_first, embed_second=embed_second, mixer_weight=mixer_weight, mixer_first=mixer_first, mixer_second=mixer_second, merge_weight=merge_weight, merge_first=merge_first, merge_second=merge_second, expand_weight=expand_weight, expand_first=expand_first, expand_second=expand_second, shrink_weight=shrink_weight, shrink_first=shrink_first, shrink_second=shrink_second, unpatch_weight=unpatch_weight, unpatch_first=unpatch_first, unpatch_second=unpatch_second, norm_params=norm_params, norm_first=norm_first, norm_second=norm_second)


HIGHEST = lax.Precision.HIGHEST
DEPTH_WEIGHT = 1.0
CLIP_NORM = 0.01
BETA_ONE = 0.9
BETA_TWO = 0.95
ADAM_EPS = 1e-08
DECAY = 0.05
RATES = (0.05, 0.05, 0.5, 0.05, 0.05, 0.05, 0.8)

@jax.custom_vjp
def low(v):
    return lax.optimization_barrier(v.astype(jnp.bfloat16)).astype(jnp.float32)

@jax.custom_vjp
def low_back(v):
    return v

def low_keep(v):
    return (low(v), None)

def low_pass(kept, grad):
    return (grad,)

def back_keep(v):
    return (v, None)

def back_low(kept, grad):
    return (low(grad),)
low.defvjp(low_keep, low_pass)
low_back.defvjp(back_keep, back_low)

def matmul(left, right):
    return jnp.dot(left, right, precision=HIGHEST, preferred_element_type=jnp.float32)

def layer_norm(values, gain, shift):
    centred = values - lax.optimization_barrier(jnp.mean(values, -1, keepdims=True))
    spread = lax.optimization_barrier(jnp.mean(centred * centred, -1, keepdims=True))
    return centred * lax.rsqrt(spread + 1e-05) * gain + shift

def attend(queries, keys, values):
    length = queries.shape[0]
    blocked = min(512, length)

    def one_block(query_block):
        scores = low_back(jnp.einsum('qhd,khd->hqk', query_block, keys, precision=HIGHEST) * HD ** (-0.5))
        exponentials = jnp.exp(scores - lax.optimization_barrier(jnp.max(scores, -1, keepdims=True)))
        softmaxed = low(exponentials / lax.optimization_barrier(jnp.sum(exponentials, -1, keepdims=True)))
        return jnp.einsum('hqk,khd->qhd', softmaxed, values, precision=HIGHEST)
    output = lax.map(jax.checkpoint(one_block), queries.reshape(length // blocked, blocked, HEADS, HD))
    return output.reshape(length, HEADS * HD)

def render_terms(gaussians, render_weights, target_image, pixel_mask, pair_index, view_total):
    colour = jax.nn.sigmoid(gaussians[:, :, 0:3])
    opacity = jax.nn.sigmoid(gaussians[:, :, 3])
    depth = jax.nn.softplus(gaussians[:, :, 4])
    extent = jax.nn.sigmoid(gaussians[:, :, 5] + gaussians[:, :, 6] + gaussians[:, :, 7])
    rotation = gaussians[:, :, 8:12]
    facing = rotation[:, :, 0] * rotation[:, :, 0] / (1.0 + lax.optimization_barrier(jnp.sum(rotation * rotation, 2)))
    footprint = opacity * extent * facing
    features = jnp.concatenate([colour * footprint[:, :, None], footprint[:, :, None], (depth * footprint)[:, :, None]], 2)
    rendered = jnp.einsum('tvap,vqca->tcqp', render_weights, features, precision=HIGHEST)
    pixels = target_image.shape[-1]
    colour_out = rendered[:, 0:3].reshape(TMAX, 3, pixels)
    depth_out = (rendered[:, 4] / (1.0 + rendered[:, 3])).reshape(TMAX * pixels)
    live = (pixel_mask * (jnp.arange(TMAX)[:, None] < view_total)).astype(jnp.float32)
    colour_error = colour_out - target_image
    colour_term = jnp.sum(live[:, None, :] * colour_error * colour_error)
    flat_live = live.reshape(TMAX * pixels)
    pair_live = flat_live[pair_index[0]] * flat_live[pair_index[1]]
    depth_gap = depth_out[pair_index[0]] - depth_out[pair_index[1]]
    return colour_term + DEPTH_WEIGHT * jnp.sum(pair_live * depth_gap * depth_gap)

def scene_term(params, scene_views, render_weights, target_image, pixel_mask, pair_index, view_total):
    embed, mixer, merge, expand, shrink, unpatch, norm = [low(weight) for weight in params]
    patches = scene_views.reshape(NVIEW * Q, PD)
    embedded = low_back(matmul(patches, embed))
    normed_one = low(layer_norm(embedded, norm[0], norm[3]))
    mixed = low_back(low(matmul(normed_one, mixer))).reshape(NVIEW * Q, 3, HEADS, HD)
    attended = low_back(low(attend(mixed[:, 0], mixed[:, 1], mixed[:, 2])))
    residual_one = embedded + low_back(matmul(attended, merge))
    normed_two = low(layer_norm(residual_one, norm[1], norm[4]))
    expanded = low_back(matmul(normed_two, expand))
    activated = low(jax.nn.gelu(expanded, approximate=False))
    residual_two = residual_one + low_back(matmul(activated, shrink))
    normed_three = low(layer_norm(residual_two, norm[2], norm[5]))
    gaussians = low_back(matmul(normed_three, unpatch))
    per_block = gaussians.reshape(NVIEW, N_NARROW, QDEV, 12, PP).transpose(1, 0, 2, 3, 4)
    target_blocks = target_image.reshape(TMAX, 3, N_NARROW, QDEV * PP).transpose(2, 0, 1, 3)
    mask_blocks = pixel_mask.reshape(TMAX, N_NARROW, QDEV * PP).transpose(1, 0, 2)
    pair_blocks = pair_index.reshape(2, N_NARROW, PAIRS_DEV).transpose(1, 0, 2)
    terms = jax.vmap(render_terms, in_axes=(0, None, 0, 0, 0, None))(per_block, render_weights, target_blocks, mask_blocks, pair_blocks, view_total)
    return jnp.sum(terms)

def adamw(weight, first, second, grad, rate):
    first = BETA_ONE * first + (1.0 - BETA_ONE) * grad
    second = BETA_TWO * second + (1.0 - BETA_TWO) * grad * grad
    first_hat = first / (1.0 - BETA_ONE ** STEP)
    second_hat = second / (1.0 - BETA_TWO ** STEP)
    weight = weight - rate * (first_hat / (jnp.sqrt(second_hat) + ADAM_EPS) + DECAY * weight)
    return (weight, first, second)

def reference(views, render_w, targets, pix_mask, pairs, view_count, pair_total, embed_weight, embed_first, embed_second, mixer_weight, mixer_first, mixer_second, merge_weight, merge_first, merge_second, expand_weight, expand_first, expand_second, shrink_weight, shrink_first, shrink_second, unpatch_weight, unpatch_first, unpatch_second, norm_params, norm_first, norm_second):
    weights = (embed_weight, mixer_weight, merge_weight, expand_weight, shrink_weight, unpatch_weight, norm_params)
    firsts = (embed_first, mixer_first, merge_first, expand_first, shrink_first, unpatch_first, norm_first)
    seconds = (embed_second, mixer_second, merge_second, expand_second, shrink_second, unpatch_second, norm_second)
    divisor = pair_total[0].astype(jnp.float32)

    def scene(carry, inputs):
        grads, running = carry
        scene_views, render_weights, target_image, pixel_mask, pair_index, view_total = inputs

        def scaled(params):
            return scene_term(params, scene_views.astype(jnp.float32), render_weights, target_image.astype(jnp.float32), pixel_mask, pair_index, view_total) / divisor
        value, pullback = jax.vjp(scaled, weights)
        more, = pullback(jnp.ones_like(value))
        return ((jax.tree.map(jnp.add, grads, more), running + value), None)
    zeros = tuple((jnp.zeros_like(weight) for weight in weights))
    (grads, loss), unused = lax.scan(scene, (zeros, jnp.zeros((), jnp.float32)), (views, render_w, targets, pix_mask, pairs, view_count))
    squares = sum((jnp.sum(grad * grad) for grad in grads))
    grad_norm = jnp.sqrt(squares)
    factor = jnp.minimum(1.0, CLIP_NORM / (grad_norm + 1e-06))
    updated = [adamw(weights[which], firsts[which], seconds[which], grads[which] * factor, RATES[which]) for which in range(7)]
    return (updated[0][0], updated[0][1], updated[0][2], updated[1][0], updated[1][1], updated[1][2], updated[2][0], updated[2][1], updated[2][2], updated[3][0], updated[3][1], updated[3][2], updated[4][0], updated[4][1], updated[4][2], updated[5][0], updated[5][1], updated[5][2], updated[6][0], updated[6][1], updated[6][2], loss, grad_norm)
```

```python
import functools

import jax
import jax.numpy as jnp
from jax import lax
from jax.experimental import pallas as pl
from jax.experimental.pallas import tpu as pltpu
from jax.sharding import PartitionSpec as P

D = 1024
HD = 64
P_SIZE = 8
PP = 64
NVIEW = 4
TMAX = 12
STEP = 10
LANES = 128
MIB = 1024 * 1024

DEPTH_WEIGHT = 1.0
CLIP_NORM = 0.01
BETA_ONE = 0.9
BETA_TWO = 0.95
ADAM_EPS = 1e-08
DECAY = 0.05
RATES = (0.05, 0.05, 0.5, 0.05, 0.05, 0.05, 0.8)
MESH = pl.DeviceIdType.MESH
HIGHEST = lax.Precision.HIGHEST
F32 = jnp.float32
BF16 = jnp.bfloat16


def matmul(left, right):
    return jnp.dot(left, right, preferred_element_type=F32)


def outer_sum(left, right):
    return lax.dot_general(left, right, (((0,), (0,)), ((), ())), preferred_element_type=F32)


def back_mul(grad, weight):
    return lax.dot_general(grad, weight, (((1,), (1,)), ((), ())), preferred_element_type=F32)


def layer_norm(values, gain, shift):
    centred = values - jnp.mean(values, -1, keepdims=True)
    spread = jnp.mean(centred * centred, -1, keepdims=True)
    return centred * lax.rsqrt(spread + 1e-05) * gain + shift


def exact_gelu(values):
    return jax.nn.gelu(values, approximate=False)


def attention_forward(queries, keys, values):
    length, heads = (queries.shape[0], queries.shape[1])
    blocked = min(512, length)
    scale = HD ** (-0.5)

    def one_block(query_block):
        scores = (
            jnp.einsum("qhd,khd->hqk", query_block, keys, preferred_element_type=jnp.float32)
            * scale
        )
        highest = jnp.max(scores, -1, keepdims=True)
        exponentials = jnp.exp(scores - highest)
        summed = jnp.sum(exponentials, -1, keepdims=True)
        softmaxed = (exponentials / summed).astype(jnp.bfloat16)
        output = jnp.einsum("hqk,khd->qhd", softmaxed, values, preferred_element_type=jnp.float32)
        return (output.astype(jnp.bfloat16), (highest + jnp.log(summed))[:, :, 0])

    output, logsum = lax.map(one_block, queries.reshape(length // blocked, blocked, heads, HD))
    return (output.reshape(length, heads * HD), logsum)


def attention_backward(queries, keys, values, logsum, out_grad):
    length, heads = (queries.shape[0], queries.shape[1])
    blocked = min(512, length)
    scale = HD ** (-0.5)

    def one_block(carry, inputs):
        key_grad, value_grad = carry
        query_block, logsum_block, grad_block = inputs
        scores = (
            jnp.einsum("qhd,khd->hqk", query_block, keys, preferred_element_type=jnp.float32)
            * scale
        )
        softmaxed = jnp.exp(scores - logsum_block[:, :, None])
        value_grad = value_grad + jnp.einsum(
            "hqk,qhd->khd",
            softmaxed.astype(jnp.bfloat16),
            grad_block,
            preferred_element_type=jnp.float32,
        )
        prob_grad = jnp.einsum(
            "qhd,khd->hqk", grad_block, values, preferred_element_type=jnp.float32
        )
        score_grad = softmaxed * (prob_grad - jnp.sum(softmaxed * prob_grad, -1, keepdims=True))
        score_low = score_grad.astype(jnp.bfloat16)
        query_grad = (
            jnp.einsum("hqk,khd->qhd", score_low, keys, preferred_element_type=jnp.float32) * scale
        )
        key_grad = (
            key_grad
            + jnp.einsum("hqk,qhd->khd", score_low, query_block, preferred_element_type=jnp.float32)
            * scale
        )
        return ((key_grad, value_grad), query_grad)

    zeros = jnp.zeros((length, heads, HD), jnp.float32)
    shaped = (
        queries.reshape(length // blocked, blocked, heads, HD),
        logsum,
        out_grad.reshape(length // blocked, blocked, heads, HD),
    )
    (key_grad, value_grad), query_grad = lax.scan(one_block, (zeros, zeros), shaped)
    return (query_grad.reshape(length, heads, HD), key_grad, value_grad)


def adamw(weight, first, second, grad, rate):
    first = BETA_ONE * first + (1.0 - BETA_ONE) * grad
    second = BETA_TWO * second + (1.0 - BETA_TWO) * grad * grad
    first_hat = first / (1.0 - BETA_ONE**STEP)
    second_hat = second / (1.0 - BETA_TWO**STEP)
    weight = weight - rate * (first_hat / (jnp.sqrt(second_hat) + ADAM_EPS) + DECAY * weight)
    return (weight, first, second)


def chip_bits(chips):
    bits, step = [], 1
    while step < chips:
        bits.append(step)
        step *= 2
    return bits


def flip(chip, mask):
    for bit in chip_bits(mask + 1):
        if mask & bit:
            chip = chip + (1 - 2 * (chip // bit % 2)) * bit
    return chip


def column_halves(width):
    first = -(-width // (2 * LANES)) * LANES
    return ((0, first), (first, width - first))


def work_items(widths, order):
    return [(which,) + half + (side,) for which in order for side, half in enumerate(column_halves(widths[which]))]


class Place:
    def __init__(self, wide, narrow):
        self.wide, self.narrow = wide, narrow
        self.chips = wide // 2
        self.bits = chip_bits(self.chips)
        self.w = lax.axis_index("wide")
        self.n = lax.axis_index("narrow")
        self.chip = self.w // 2
        self.core = self.w % 2
        self.twin = (2 * self.chip + 1 - self.core, self.n)

    def across(self, mask):
        return (2 * flip(self.chip, mask) + self.core, self.n)

    def along(self, step):
        return (self.w, lax.rem(self.n + step, self.narrow))

    def neighbours(self):
        return (
            [self.twin]
            + [self.across(bit) for bit in self.bits]
            + [self.along(step) for step in range(1, self.narrow)]
        )


def greet(peers):
    barrier = pltpu.get_barrier_semaphore()
    for peer in peers:
        pl.semaphore_signal(barrier, inc=1, device_id=peer, device_id_type=MESH)
    pl.semaphore_wait(barrier, len(peers))


def gather_kernel(items, wide, narrow, count, *refs):
    ins, outs = refs[:count], refs[count : 2 * count]
    own_sem, send_sem, recv_sem = refs[2 * count :]
    place = Place(wide, narrow)
    chips = place.chips
    greet(place.neighbours())

    own = []
    for which in range(count):
        copy = pltpu.make_async_copy(
            ins[which], outs[which].at[place.chip, place.core, place.n], own_sem.at[which]
        )
        copy.start()
        own.append(copy)

    def remote(item, src, dst, slot, peer):
        return pltpu.make_async_remote_copy(
            src_ref=src,
            dst_ref=dst,
            send_sem=send_sem.at[item, slot],
            recv_sem=recv_sem.at[item, slot],
            device_id=peer,
            device_id_type=MESH,
        )

    def group(item, mask):
        which, start, width, _ = items[item]
        return outs[which].at[flip(place.chip, mask), place.core, :, :, pl.ds(start, width)]

    def along(item, step):
        which, start, width, _ = items[item]
        return remote(
            item,
            ins[which].at[:, pl.ds(start, width)],
            outs[which].at[place.chip, place.core, place.n, :, pl.ds(start, width)],
            2 * chips + step - 1,
            place.along(step),
        )

    def bits_of(item):
        return place.bits if items[item][3] == 0 else place.bits[::-1]

    def across(item, mask, bit):
        return remote(item, group(item, mask), group(item, mask), mask ^ bit, place.across(bit))

    def to_twin(item, mask):
        return remote(item, group(item, mask), group(item, mask), chips + mask, place.twin)

    started = []

    def start(copy):
        copy.start()
        started.append(copy)

    def start_along(item):
        for step in range(1, narrow):
            start(along(item, step))

    def stage(item, number):
        bits = bits_of(item)
        if number == 0:
            if item % 2 == 0:
                own[items[item][0]].wait()
            for step in range(1, narrow):
                along(item, step).wait_recv()
            held = [0]
            fresh = [0]
        else:
            held = [0]
            for bit in bits[: number - 1]:
                held = held + [mask ^ bit for mask in held]
            fresh = [mask ^ bits[number - 1] for mask in held]
            for mask in fresh:
                across(item, mask ^ bits[number - 1], bits[number - 1]).wait_recv()
            held = held + fresh
        if number < len(bits):
            for mask in held:
                start(across(item, mask, bits[number]))
        for mask in fresh:
            start(to_twin(item, mask))

    total = len(items)
    ahead = 4
    for item in range(min(ahead, total)):
        start_along(item)
    depth = len(place.bits) + 1
    for tick in range(0, total + 2 * (depth - 1), 2):
        for number in reversed(range(depth)):
            for item in (tick - 2 * number, tick - 2 * number + 1):
                if 0 <= item < total:
                    stage(item, number)
        for item in (tick + ahead, tick + ahead + 1):
            if item < total:
                start_along(item)
    for item in range(total):
        for mask in range(chips):
            to_twin(item, mask).wait_recv()
    for copy in started:
        copy.wait_send()


def gather_all(shards, wide, narrow):
    count = len(shards)
    widths = [shard.shape[1] for shard in shards]
    items = work_items(widths, range(count))
    slots = wide + narrow - 1
    shapes = [
        jax.ShapeDtypeStruct((wide // 2, 2, narrow) + shard.shape, shard.dtype) for shard in shards
    ]
    whole = pl.pallas_call(
        functools.partial(gather_kernel, items, wide, narrow, count),
        out_shape=shapes,
        in_specs=[pl.BlockSpec(memory_space=pl.ANY)] * count,
        out_specs=[pl.BlockSpec(memory_space=pl.ANY)] * count,
        scratch_shapes=[
            pltpu.SemaphoreType.DMA((count,)),
            pltpu.SemaphoreType.DMA((len(items), slots)),
            pltpu.SemaphoreType.DMA((len(items), slots)),
        ],
        compiler_params=pltpu.CompilerParams(collective_id=0, has_side_effects=True),
        name="gather_weights",
    )(*shards)
    return [full.reshape(-1, width) for full, width in zip(whole, widths)]


def tile_of(width):
    for tile in (512, 384, 256, 128):
        if width % tile == 0:
            return tile
    return width


def reduce_kernel(items, wide, narrow, count, *refs):
    lefts, rights = refs[:count], refs[count : 2 * count]
    extra, term = refs[2 * count : 2 * count + 2]
    outs = refs[2 * count + 2 : 3 * count + 2]
    sums = refs[3 * count + 2]
    scratch = list(refs[3 * count + 3 :])
    place = Place(wide, narrow)
    chips = place.chips
    total = len(items)
    sent = [scratch.pop(0) for _ in items]
    held = [scratch.pop(0) for _ in items]
    passed = [[scratch.pop(0) for _ in place.bits] for _ in items]
    last = [scratch.pop(0) for _ in items]
    wide_tiles, narrow_tiles, send_sem, recv_sem, tile_send, tile_recv = scratch
    peers = [place.twin]
    for step in range(1, wide):
        peers.append((lax.rem(place.w + step, wide), place.n))
    for step in range(1, narrow):
        peers.append(place.along(step))
    greet(peers[1:])

    started = []

    def start(copy):
        copy.start()
        started.append(copy)

    def remote(item, src, dst, slot, peer):
        return pltpu.make_async_remote_copy(
            src_ref=src,
            dst_ref=dst,
            send_sem=send_sem.at[item, slot],
            recv_sem=recv_sem.at[item, slot],
            device_id=peer,
            device_id_type=MESH,
        )

    def bits_of(item):
        return place.bits[::-1] if items[item][3] == 0 else place.bits

    def product(item, mask, core, into, plus):
        which, begin, width, _ = items[item]
        left, right = lefts[which], rights[which]
        rows = into.shape[2]
        tile = tile_of(width)
        together = max(1, min(narrow, 128 // rows))
        owner = flip(place.chip, mask)
        with_extra = which == 0 and begin + width == right.shape[1]

        def one(step, carry):
            across, down = step % (width // tile), step // (width // tile)
            offset = pl.multiple_of(begin + across * tile, LANES)
            local = pl.multiple_of(across * tile, LANES)
            ns = pl.ds(down * together, together)
            lhs = left[owner, core, ns].reshape(together * rows, left.shape[-1])
            value = jnp.dot(lhs, right[:, pl.ds(offset, tile)], preferred_element_type=F32)
            if with_extra:
                more = extra[owner, core, ns].reshape(together * rows, LANES)
                more = jnp.concatenate([jnp.zeros((together * rows, tile - LANES), F32), more], 1)
                value = value + more
            value = value.reshape(together, rows, tile)
            if plus is not None:
                value = value + plus[mask, ns, :, pl.ds(local, tile)].astype(F32)
            into[mask, ns, :, pl.ds(local, tile)] = value.astype(BF16)
            return carry

        assert not with_extra or tile == width
        lax.fori_loop(0, (width // tile) * (narrow // together), one, 0)

    def to_twin(item, mask):
        return remote(item, sent[item].at[mask], held[item].at[mask], mask, place.twin)

    def across(item, mask, bit, number, slot):
        return remote(
            item, held[item].at[mask], passed[item][number].at[slot], chips + mask, place.across(bit)
        )

    def along(item, step):
        target = place.along(step)
        return remote(
            item,
            held[item].at[0, target[1]],
            last[item].at[narrow - step - 1],
            2 * chips + narrow - step - 1,
            target,
        )

    def split(item, number):
        bits = bits_of(item)
        keep = list(range(chips))
        for bit in bits[:number]:
            keep = [mask for mask in keep if not mask & bit]
        if number < len(bits):
            return [m for m in keep if m & bits[number]], [m for m in keep if not m & bits[number]]
        return [], keep

    def add_into(dest, dest_at, src, src_at):
        rows, width = dest.shape[-2:]

        def one(step, carry):
            a = dest[dest_at, step].astype(F32) + src[src_at, step].astype(F32)
            dest[dest_at, step] = a.astype(BF16)
            return carry

        lax.fori_loop(0, narrow, one, 0)

    def send_on(item, number, ready):
        bits = bits_of(item)
        away, keep = split(item, number)
        if number < len(bits):
            for mask in away:
                ready(mask)
                start(across(item, mask, bits[number], number, keep.index(mask ^ bits[number])))
            for mask in keep:
                ready(mask)
        else:
            ready(0)
            for step in range(1, narrow):
                start(along(item, step))

    def stage(item, number):
        bits = bits_of(item)
        if number == 0:

            def ready(mask):
                to_twin(item, mask).wait_recv()
                product(item, mask, place.core, held[item], held[item])

            send_on(item, 0, ready)
        else:
            bit = bits[number - 1]
            _, kept = split(item, number - 1)

            def ready(mask):
                slot = kept.index(mask)
                across(item, mask ^ bit, bit, number - 1, slot).wait_recv()
                add_into(held[item], mask, passed[item][number - 1], slot)

            send_on(item, number, ready)

    def finish(item):
        which, begin, width, _ = items[item]
        value = held[item][0, place.n].astype(F32)
        for step in range(1, narrow):
            along(item, step).wait_recv()
        for slot in range(narrow - 1):
            value = value + last[item][slot].astype(F32)
        outs[which][:, pl.ds(begin, width)] = value
        return jnp.sum(value * value)

    for item in range(total):
        for mask in range(chips):
            product(item, mask, 1 - place.core, sent[item], None)
            start(to_twin(item, mask))
    squares = jnp.zeros((), F32)
    depth = len(place.bits) + 1
    for tick in range(0, total + 2 * depth, 2):
        for number in reversed(range(depth + 1)):
            for item in (tick - 2 * number, tick - 2 * number + 1):
                if 0 <= item < total:
                    if number < depth:
                        stage(item, number)
                    else:
                        squares = squares + finish(item)

    rows = lax.broadcasted_iota(jnp.int32, (8, LANES), 0)
    wide_tiles[place.w] = jnp.where(rows == 0, term[...], squares)

    def tile_copy(buffer, at, slot, peer):
        return pltpu.make_async_remote_copy(
            src_ref=buffer.at[at],
            dst_ref=buffer.at[at],
            send_sem=tile_send.at[slot],
            recv_sem=tile_recv.at[slot],
            device_id=peer,
            device_id_type=MESH,
        )

    for step in range(1, wide):
        start(tile_copy(wide_tiles, place.w, step - 1, (lax.rem(place.w + step, wide), place.n)))
    for step in range(1, wide):
        tile_copy(wide_tiles, place.w, step - 1, (lax.rem(place.w + step, wide), place.n)).wait_recv()
    whole = wide_tiles[0]
    for index in range(1, wide):
        whole = whole + wide_tiles[index]
    narrow_tiles[place.n] = whole
    for step in range(1, narrow):
        start(tile_copy(narrow_tiles, place.n, wide + step - 1, place.along(step)))
    for step in range(1, narrow):
        tile_copy(narrow_tiles, place.n, wide + step - 1, place.along(step)).wait_recv()
    whole = narrow_tiles[0]
    for index in range(1, narrow):
        whole = whole + narrow_tiles[index]
    sums[...] = whole
    for copy in started:
        copy.wait_send()


def reduce_all(lefts, rights, extra, term, wide, narrow, order):
    count = len(lefts)
    chips = wide // 2
    shaped = [left.reshape(chips, 2, narrow, -1, left.shape[1]) for left in lefts]
    extra = extra.reshape(chips, 2, narrow, -1, LANES)
    widths = [right.shape[1] for right in rights]
    rows = [left.shape[3] for left in shaped]
    items = work_items(widths, order)
    slots = 2 * chips + narrow - 1
    scratch = []
    for which, _, width, _ in items:
        scratch.append(pltpu.VMEM((chips, narrow, rows[which], width), BF16))
    for which, _, width, _ in items:
        scratch.append(pltpu.VMEM((chips, narrow, rows[which], width), BF16))
    for which, _, width, _ in items:
        size = chips
        while size > 1:
            size //= 2
            scratch.append(pltpu.VMEM((size, narrow, rows[which], width), BF16))
    for which, _, width, _ in items:
        scratch.append(pltpu.VMEM((narrow - 1, rows[which], width), BF16))
    scratch += [
        pltpu.VMEM((wide, 8, LANES), F32),
        pltpu.VMEM((narrow, 8, LANES), F32),
        pltpu.SemaphoreType.DMA((len(items), slots)),
        pltpu.SemaphoreType.DMA((len(items), slots)),
        pltpu.SemaphoreType.DMA((wide + narrow,)),
        pltpu.SemaphoreType.DMA((wide + narrow,)),
    ]
    vmem = pl.BlockSpec(memory_space=pltpu.VMEM)
    return pl.pallas_call(
        functools.partial(reduce_kernel, items, wide, narrow, count),
        out_shape=[jax.ShapeDtypeStruct((rows[i], widths[i]), F32) for i in range(count)]
        + [jax.ShapeDtypeStruct((8, LANES), F32)],
        in_specs=[vmem] * (2 * count + 2),
        out_specs=[vmem] * (count + 1),
        scratch_shapes=scratch,
        compiler_params=pltpu.CompilerParams(
            collective_id=1, has_side_effects=True, vmem_limit_bytes=60 * MIB
        ),
        name="reduce_grads",
    )(*shaped, *rights, extra, term)


def render_kernel(
    gauss_ref, weight_ref, target_ref, mask_ref, pair_ref, view_ref, total_ref, grad_ref, term_ref, feat, dfeat
):
    quads = gauss_ref.shape[0] // NVIEW
    span = weight_ref.shape[1]
    pairs = pair_ref.shape[1]
    scale = 1.0 / total_ref[0].astype(F32)

    def channel(index):
        return gauss_ref[:, index * PP : (index + 1) * PP]

    def shared():
        opacity = jax.nn.sigmoid(channel(3))
        extent = jax.nn.sigmoid(channel(5) + channel(6) + channel(7))
        lead = channel(8)
        denom = 1.0 + lead * lead + channel(9) * channel(9) + channel(10) * channel(10) + channel(11) * channel(11)
        facing = lead * lead / denom
        raw = channel(4)
        depth = jnp.maximum(raw, 0.0) + jnp.log1p(jnp.exp(-jnp.abs(raw)))
        return opacity, extent, lead, denom, facing, raw, depth

    opacity, extent, lead, denom, facing, raw, depth = shared()
    footprint = opacity * extent * facing
    channels = [jax.nn.sigmoid(channel(index)) * footprint for index in range(3)]
    channels += [footprint, depth * footprint]
    for index, value in enumerate(channels):
        for view in range(NVIEW):
            feat[index * quads : (index + 1) * quads, view * PP : (view + 1) * PP] = value[
                view * quads : (view + 1) * quads
            ]
    rendered = jnp.dot(feat[...], weight_ref[...], precision=HIGHEST, preferred_element_type=F32)
    parts = [rendered[index * quads : (index + 1) * quads] for index in range(5)]
    lane = lax.broadcasted_iota(jnp.int32, (quads, span), 1)
    live = jnp.where(lane < view_ref[0] * PP, mask_ref[...], 0).astype(F32)
    term = jnp.zeros((quads, span), F32)
    slopes = []
    for index in range(3):
        error = parts[index] - target_ref[index * quads : (index + 1) * quads, :].astype(F32)
        term = term + live * error * error
        slopes.append(2.0 * scale * live * error)
    below = 1.0 + parts[3]
    depth_out = parts[4] / below

    first, second = pair_ref[0:1, :], pair_ref[1:2, :]
    least = jnp.minimum(first, second)
    down = (jnp.abs(first - second) == P_SIZE).astype(jnp.int32)
    place = quads * PP
    slot, local = least // place, least % place
    high = down * quads + local // PP
    low = slot * PP + local % PP
    high_hot = (lax.broadcasted_iota(jnp.int32, (2 * quads, pairs), 0) == high).astype(F32).astype(BF16)
    low_hot = (lax.broadcasted_iota(jnp.int32, (span, pairs), 0) == low).astype(F32).astype(BF16)
    counts = back_mul(high_hot, low_hot)
    slope = jnp.zeros((quads, span), F32)
    for which, shift in enumerate((1, P_SIZE)):
        count = counts[which * quads : (which + 1) * quads]
        weight = DEPTH_WEIGHT * count * live * pltpu.roll(live, span - shift, 1)
        gap = depth_out - pltpu.roll(depth_out, span - shift, 1)
        term = term + weight * gap * gap
        pull = 2.0 * scale * weight * gap
        slope = slope + pull - pltpu.roll(pull, shift, 1)
    term_ref[...] = jnp.full(term_ref.shape, jnp.sum(term), F32)
    over = slope / below
    slopes += [-over * depth_out, over]
    stacked = jnp.concatenate(slopes, 0)
    dfeat[...] = lax.dot_general(
        stacked, weight_ref[...], (((1,), (1,)), ((), ())), precision=HIGHEST, preferred_element_type=F32
    )

    def feature_grad(index):
        return jnp.concatenate(
            [
                dfeat[index * quads : (index + 1) * quads, view * PP : (view + 1) * PP]
                for view in range(NVIEW)
            ],
            0,
        )

    def put(index, value):
        grad_ref[:, index * PP : (index + 1) * PP] = value.astype(BF16)

    d_foot = feature_grad(3)
    for index in range(3):
        tint = jax.nn.sigmoid(channel(index))
        upper = feature_grad(index)
        d_foot = d_foot + upper * tint
        put(index, upper * footprint * tint * (1.0 - tint))
    d_last = feature_grad(4)
    d_foot = d_foot + d_last * depth
    put(3, d_foot * extent * facing * opacity * (1.0 - opacity))
    put(4, d_last * footprint * jax.nn.sigmoid(raw))
    d_extent = d_foot * opacity * facing * extent * (1.0 - extent)
    for index in (5, 6, 7):
        put(index, d_extent)
    d_facing = d_foot * opacity * extent
    put(8, d_facing * 2.0 * lead / denom * (1.0 - facing))
    for index in (9, 10, 11):
        put(index, -2.0 * d_facing * facing / denom * channel(index))


def render(gaussians, weights, targets, mask, pairs, view_count, pair_total):
    rows = gaussians.shape[0]
    quads = rows // NVIEW
    slots, views = weights.shape[:2]
    spread = weights.transpose(1, 2, 0, 3).reshape(views * PP, slots * PP)
    wanted = targets.reshape(slots, 3, quads, PP).transpose(1, 2, 0, 3).reshape(3 * quads, slots * PP)
    valid = mask.reshape(slots, quads, PP).transpose(1, 0, 2).reshape(quads, slots * PP)
    vmem = pl.BlockSpec(memory_space=pltpu.VMEM)
    smem = pl.BlockSpec(memory_space=pltpu.SMEM)
    return pl.pallas_call(
        render_kernel,
        out_shape=[
            jax.ShapeDtypeStruct(gaussians.shape, BF16),
            jax.ShapeDtypeStruct((8, LANES), F32),
        ],
        in_specs=[vmem] * 5 + [smem] * 2,
        out_specs=[vmem] * 2,
        scratch_shapes=[pltpu.VMEM((5 * quads, views * PP), F32)] * 2,
        compiler_params=pltpu.CompilerParams(vmem_limit_bytes=48 * MIB),
        name="render",
    )(gaussians, spread, wanted, valid, pairs, view_count, pair_total)


def body(
    views,
    render_w,
    targets,
    pix_mask,
    pairs,
    view_count,
    pair_total,
    embed_weight,
    embed_first,
    embed_second,
    mixer_weight,
    mixer_first,
    mixer_second,
    merge_weight,
    merge_first,
    merge_second,
    expand_weight,
    expand_first,
    expand_second,
    shrink_weight,
    shrink_first,
    shrink_second,
    unpatch_weight,
    unpatch_first,
    unpatch_second,
    norm_params,
    norm_first,
    norm_second,
):
    masters = (embed_weight, mixer_weight, merge_weight, expand_weight, shrink_weight, unpatch_weight, norm_params)
    firsts = (embed_first, mixer_first, merge_first, expand_first, shrink_first, unpatch_first, norm_first)
    seconds = (embed_second, mixer_second, merge_second, expand_second, shrink_second, unpatch_second, norm_second)
    groups = lax.axis_size("narrow")
    wide_count = lax.axis_size("wide")
    features = embed_weight.shape[0]
    kinds = norm_params.shape[0]
    padded = -(-(features + kinds) // LANES) * LANES
    fill = padded - features - kinds
    by_kernel = mixer_weight.shape[0] % 16 == 0

    first_shard = jnp.concatenate([embed_weight.T, norm_params.T], 1)
    first_shard = jnp.pad(first_shard.astype(BF16), ((0, 0), (0, fill)))
    shards = [first_shard] + [weight.astype(BF16) for weight in masters[1:6]]
    if by_kernel:
        weights = gather_all(shards, wide_count, groups)
    else:
        weights = [lax.all_gather(shard, ("wide", "narrow"), axis=0, tiled=True) for shard in shards]
    gains = weights[0][:, features : features + kinds].T.astype(F32)

    patches = views.reshape(-1, features)
    rows = patches.shape[0]
    patches = jnp.pad(patches, ((0, 0), (0, padded - features)))
    embedded = back_mul(patches[:, :features], weights[0][:, :features])
    normed_one, norm_back_one = jax.vjp(layer_norm, embedded, gains[0], gains[3])
    normed_one = normed_one.astype(BF16)
    mixed = matmul(normed_one, weights[1]).astype(BF16).reshape(rows, 3, groups, -1)
    spread = lax.all_to_all(mixed, "narrow", split_axis=2, concat_axis=0, tiled=True)
    length, width = (spread.shape[0], spread.shape[-1])
    local_heads = width // HD
    queries = spread[:, 0, 0].reshape(length, local_heads, HD)
    keys_all = spread[:, 1, 0].reshape(length, local_heads, HD)
    values_all = spread[:, 2, 0].reshape(length, local_heads, HD)
    attended, logsum = attention_forward(queries, keys_all, values_all)
    returned = lax.all_to_all(
        attended.reshape(length, 1, width), "narrow", split_axis=0, concat_axis=1, tiled=True
    ).reshape(rows, D)
    residual_one = embedded + matmul(returned, weights[2])
    normed_two, norm_back_two = jax.vjp(layer_norm, residual_one, gains[1], gains[4])
    normed_two = normed_two.astype(BF16)
    expanded = matmul(normed_two, weights[3])
    activated, gelu_back = jax.vjp(exact_gelu, expanded)
    activated = activated.astype(BF16)
    residual_two = residual_one + matmul(activated, weights[4])
    normed_three, norm_back_three = jax.vjp(layer_norm, residual_two, gains[2], gains[5])
    normed_three = normed_three.astype(BF16)
    gaussians = matmul(normed_three, weights[5])
    divisor = pair_total[0].astype(F32)

    gauss_low, term = render(
        gaussians, render_w[0], targets[0], pix_mask[0], pairs[0], view_count, pair_total
    )
    residual_grad, gain_three, shift_three = norm_back_three(back_mul(gauss_low, weights[5]))
    shrink_low = residual_grad.astype(BF16)
    (expand_grad,) = gelu_back(back_mul(shrink_low, weights[4]))
    expand_low = expand_grad.astype(BF16)
    through_two, gain_two, shift_two = norm_back_two(back_mul(expand_low, weights[3]))
    residual_grad = residual_grad + through_two
    merge_low = residual_grad.astype(BF16)
    out_grad = back_mul(merge_low, weights[2]).astype(BF16).reshape(rows, groups, width)
    head_grad = lax.all_to_all(out_grad, "narrow", split_axis=1, concat_axis=0, tiled=True).reshape(
        length, local_heads, HD
    )
    query_grad, key_grad, value_grad = attention_backward(queries, keys_all, values_all, logsum, head_grad)
    stacked = jnp.stack([query_grad, key_grad, value_grad], 1).astype(BF16).reshape(length, 3, 1, width)
    mixed_grad = lax.all_to_all(stacked, "narrow", split_axis=0, concat_axis=2, tiled=True).reshape(
        rows, 3 * D
    )
    through_one, gain_one, shift_one = norm_back_one(back_mul(mixed_grad, weights[1]))
    embed_grad = (residual_grad + through_one).astype(BF16)
    grad_norms = jnp.stack([gain_one, gain_two, gain_three, shift_one, shift_two, shift_three])

    lefts = [embed_grad.T, normed_one.T, returned.T, normed_two.T, activated.T, normed_three.T]
    rights = [patches, mixed_grad, merge_low, expand_low, shrink_low, gauss_low]
    at = features % LANES
    extra = jnp.pad(grad_norms.T, ((0, 0), (at, LANES - at - kinds)))
    if by_kernel:
        *sums, totals = reduce_all(
            lefts, rights, extra, term, wide_count, groups, (5, 4, 3, 2, 1, 0)
        )
        loss_sum, square_sum = totals[0, 0], totals[1, 0]
    else:
        products = [matmul(left, right) for left, right in zip(lefts, rights)]
        products[0] = products[0].at[:, -LANES:].add(extra)
        sums = [
            lax.psum_scatter(
                product.astype(BF16), ("wide", "narrow"), scatter_dimension=0, tiled=True
            ).astype(F32)
            for product in products
        ]
        squares = sum(jnp.sum(part * part) for part in sums)
        loss_sum, square_sum = lax.psum((term[0, 0], squares), ("wide", "narrow"))
    first_sum = sums[0].T
    grads = [first_sum[:features]] + list(sums[1:]) + [first_sum[features : features + kinds]]
    loss = loss_sum / divisor
    grad_norm = jnp.sqrt(square_sum)
    factor = jnp.minimum(1.0, CLIP_NORM / (grad_norm + 1e-06))
    results = []
    for which in range(7):
        results += adamw(masters[which], firsts[which], seconds[which], grads[which] * factor, RATES[which])
    return tuple(results) + (loss, grad_norm)


def solution(mesh):
    columns = P(None, ("wide", "narrow"))
    rows = P(("wide", "narrow"), None)
    weights = (columns,) * 3 + (rows,) * 15 + (columns,) * 3
    return jax.shard_map(
        body,
        mesh=mesh,
        in_specs=(
            P("wide", None, "narrow", None),
            P("wide", None, None, None, None),
            P("wide", None, None, "narrow"),
            P("wide", None, "narrow"),
            P("wide", None, "narrow"),
            P("wide"),
            P(),
        )
        + weights,
        out_specs=weights + (P(), P()),
        check_vma=False,
    )
```

```python
import functools

import jax
import jax.numpy as jnp
from jax import lax
from jax.experimental import pallas as pl
from jax.experimental.pallas import tpu as pltpu
from jax.sharding import PartitionSpec as P

D = 1024
HD = 64
P_SIZE = 8
PP = 64
NVIEW = 4
TMAX = 12
STEP = 10
LANES = 128
MIB = 1024 * 1024

DEPTH_WEIGHT = 1.0
CLIP_NORM = 0.01
BETA_ONE = 0.9
BETA_TWO = 0.95
ADAM_EPS = 1e-08
DECAY = 0.05
RATES = (0.05, 0.05, 0.5, 0.05, 0.05, 0.05, 0.8)
MESH = pl.DeviceIdType.MESH
HIGHEST = lax.Precision.HIGHEST
F32 = jnp.float32
BF16 = jnp.bfloat16


def matmul(left, right):
    return jnp.dot(left, right, preferred_element_type=F32)


def outer_sum(left, right):
    return lax.dot_general(left, right, (((0,), (0,)), ((), ())), preferred_element_type=F32)


def back_mul(grad, weight):
    return lax.dot_general(grad, weight, (((1,), (1,)), ((), ())), preferred_element_type=F32)


def layer_norm(values, gain, shift):
    centred = values - jnp.mean(values, -1, keepdims=True)
    spread = jnp.mean(centred * centred, -1, keepdims=True)
    return centred * lax.rsqrt(spread + 1e-05) * gain + shift


def exact_gelu(values):
    return jax.nn.gelu(values, approximate=False)


def attention_forward(queries, keys, values):
    length, heads = (queries.shape[0], queries.shape[1])
    blocked = min(512, length)
    scale = HD ** (-0.5)

    def one_block(query_block):
        scores = (
            jnp.einsum("qhd,khd->hqk", query_block, keys, preferred_element_type=jnp.float32)
            * scale
        )
        highest = jnp.max(scores, -1, keepdims=True)
        exponentials = jnp.exp(scores - highest)
        summed = jnp.sum(exponentials, -1, keepdims=True)
        softmaxed = (exponentials / summed).astype(jnp.bfloat16)
        output = jnp.einsum("hqk,khd->qhd", softmaxed, values, preferred_element_type=jnp.float32)
        return (output.astype(jnp.bfloat16), (highest + jnp.log(summed))[:, :, 0])

    output, logsum = lax.map(one_block, queries.reshape(length // blocked, blocked, heads, HD))
    return (output.reshape(length, heads * HD), logsum)


def attention_backward(queries, keys, values, logsum, out_grad):
    length, heads = (queries.shape[0], queries.shape[1])
    blocked = min(512, length)
    scale = HD ** (-0.5)

    def one_block(carry, inputs):
        key_grad, value_grad = carry
        query_block, logsum_block, grad_block = inputs
        scores = (
            jnp.einsum("qhd,khd->hqk", query_block, keys, preferred_element_type=jnp.float32)
            * scale
        )
        softmaxed = jnp.exp(scores - logsum_block[:, :, None])
        value_grad = value_grad + jnp.einsum(
            "hqk,qhd->khd",
            softmaxed.astype(jnp.bfloat16),
            grad_block,
            preferred_element_type=jnp.float32,
        )
        prob_grad = jnp.einsum(
            "qhd,khd->hqk", grad_block, values, preferred_element_type=jnp.float32
        )
        score_grad = softmaxed * (prob_grad - jnp.sum(softmaxed * prob_grad, -1, keepdims=True))
        score_low = score_grad.astype(jnp.bfloat16)
        query_grad = (
            jnp.einsum("hqk,khd->qhd", score_low, keys, preferred_element_type=jnp.float32) * scale
        )
        key_grad = (
            key_grad
            + jnp.einsum("hqk,qhd->khd", score_low, query_block, preferred_element_type=jnp.float32)
            * scale
        )
        return ((key_grad, value_grad), query_grad)

    zeros = jnp.zeros((length, heads, HD), jnp.float32)
    shaped = (
        queries.reshape(length // blocked, blocked, heads, HD),
        logsum,
        out_grad.reshape(length // blocked, blocked, heads, HD),
    )
    (key_grad, value_grad), query_grad = lax.scan(one_block, (zeros, zeros), shaped)
    return (query_grad.reshape(length, heads, HD), key_grad, value_grad)


def adamw(weight, first, second, grad, rate):
    first = BETA_ONE * first + (1.0 - BETA_ONE) * grad
    second = BETA_TWO * second + (1.0 - BETA_TWO) * grad * grad
    first_hat = first / (1.0 - BETA_ONE**STEP)
    second_hat = second / (1.0 - BETA_TWO**STEP)
    weight = weight - rate * (first_hat / (jnp.sqrt(second_hat) + ADAM_EPS) + DECAY * weight)
    return (weight, first, second)


def chip_bits(chips):
    bits, step = [], 1
    while step < chips:
        bits.append(step)
        step *= 2
    return bits


def flip(chip, mask):
    for bit in chip_bits(mask + 1):
        if mask & bit:
            chip = chip + (1 - 2 * (chip // bit % 2)) * bit
    return chip


def column_halves(width):
    first = -(-width // (2 * LANES)) * LANES
    return ((0, first), (first, width - first))


def work_items(widths, order):
    return [(which,) + half + (side,) for which in order for side, half in enumerate(column_halves(widths[which]))]


class Place:
    def __init__(self, wide, narrow):
        self.wide, self.narrow = wide, narrow
        self.chips = wide // 2
        self.bits = chip_bits(self.chips)
        self.w = lax.axis_index("wide")
        self.n = lax.axis_index("narrow")
        self.chip = self.w // 2
        self.core = self.w % 2
        self.twin = (2 * self.chip + 1 - self.core, self.n)

    def across(self, mask):
        return (2 * flip(self.chip, mask) + self.core, self.n)

    def along(self, step):
        return (self.w, lax.rem(self.n + step, self.narrow))

    def neighbours(self):
        return (
            [self.twin]
            + [self.across(bit) for bit in self.bits]
            + [self.along(step) for step in range(1, self.narrow)]
        )


def greet(peers):
    barrier = pltpu.get_barrier_semaphore()
    for peer in peers:
        pl.semaphore_signal(barrier, inc=1, device_id=peer, device_id_type=MESH)
    pl.semaphore_wait(barrier, len(peers))


def normalize(values, gain, shift):
    centred = values - jnp.mean(values, -1, keepdims=True)
    spread = jnp.mean(centred * centred, -1, keepdims=True)
    return centred * lax.rsqrt(spread + 1e-05) * gain + shift


def forward_plan(widths):
    items = []
    for which, cuts in ((0, 1), (1, 3), (2, 1), (3, 4), (5, 1), (4, 4)):
        size = widths[which] // cuts
        for cut in range(cuts):
            for side, (start, width) in enumerate(column_halves(size)):
                items.append((which, cut * size + start, width, side))
    return items


def forward_kernel(items, wide, narrow, lead, ins, outs, scratch, *refs):
    at = dict(zip(ins + outs + scratch, refs))
    buf = {name: at["v_" + name] for name in outs}
    weights = [at["first_weight"]] + [buf["w%d" % which] for which in range(1, 6)]
    shards = [at["s%d" % which] for which in range(6)]
    own_sem, send_sem, recv_sem, swap_send, swap_recv, out_sem = (at[name] for name in SEMS)
    place = Place(wide, narrow)
    chips, me = place.chips, place.n
    tokens = at["patches"].shape[0]
    head_width = D // narrow
    total = len(items)
    started = []

    def start(copy):
        copy.start()
        started.append(copy)

    greet(place.neighbours())
    rows_of = [shard.shape[0] for shard in shards]

    def rows_at(which, chip, core, node=None):
        rows = rows_of[which]
        if node is None:
            return pl.ds(pl.multiple_of((chip * 2 + core) * narrow * rows, rows), narrow * rows)
        return pl.ds(pl.multiple_of(((chip * 2 + core) * narrow + node) * rows, rows), rows)

    own = []
    for which in range(6):
        copy = pltpu.make_async_copy(
            shards[which], weights[which].at[rows_at(which, place.chip, place.core, me), :], own_sem.at[which]
        )
        copy.start()
        own.append(copy)

    def remote(item, src, dst, slot, peer):
        return pltpu.make_async_remote_copy(
            src_ref=src,
            dst_ref=dst,
            send_sem=send_sem.at[item, slot],
            recv_sem=recv_sem.at[item, slot],
            device_id=peer,
            device_id_type=MESH,
        )

    def group(item, mask):
        which, begin, width, _ = items[item]
        return weights[which].at[rows_at(which, flip(place.chip, mask), place.core), pl.ds(begin, width)]

    def along(item, step):
        which, begin, width, _ = items[item]
        return remote(
            item,
            shards[which].at[:, pl.ds(begin, width)],
            weights[which].at[rows_at(which, place.chip, place.core, me), pl.ds(begin, width)],
            2 * chips + step - 1,
            place.along(step),
        )

    def bits_of(item):
        return place.bits if items[item][3] == 0 else place.bits[::-1]

    def across(item, mask, bit):
        return remote(item, group(item, mask), group(item, mask), mask ^ bit, place.across(bit))

    def to_twin(item, mask):
        return remote(item, group(item, mask), group(item, mask), chips + mask, place.twin)

    waited = set()

    def stage(item, number):
        bits = bits_of(item)
        if number > len(bits):
            for mask in range(chips):
                to_twin(item, mask).wait_recv()
            return
        held = [0]
        if number == 0:
            if items[item][0] not in waited:
                waited.add(items[item][0])
                own[items[item][0]].wait()
            for step in range(1, narrow):
                along(item, step).wait_recv()
            fresh = [0]
        else:
            for bit in bits[: number - 1]:
                held = held + [mask ^ bit for mask in held]
            fresh = [mask ^ bits[number - 1] for mask in held]
            for mask in fresh:
                across(item, mask ^ bits[number - 1], bits[number - 1]).wait_recv()
            held = held + fresh
        if number < len(bits):
            for mask in held:
                start(across(item, mask, bits[number]))
        for mask in fresh:
            start(to_twin(item, mask))

    arrived = [False] * total

    def gather():
        ahead = 4
        for item in range(min(ahead, total)):
            for step in range(1, narrow):
                start(along(item, step))
        depth = len(place.bits) + 2
        for tick in range(0, total + 2 * (depth - 1), 2):
            for number in reversed(range(depth)):
                for item in (tick - 2 * number, tick - 2 * number + 1):
                    if 0 <= item < total:
                        stage(item, number)
                        if number == depth - 1:
                            arrived[item] = True
            for item in (tick + ahead, tick + ahead + 1):
                if item < total:
                    for step in range(1, narrow):
                        start(along(item, step))
            yield

    engine = gather()

    def advance(steps=1):
        for _ in range(steps):
            next(engine, None)

    def need(which, columns=None):
        wanted = [
            index
            for index, (owner, begin, width, _) in enumerate(items)
            if owner == which and (columns is None or (begin < columns[1] and begin + width > columns[0]))
        ]
        while not all(arrived[index] for index in wanted):
            next(engine)

    flushed = []

    def flush(name):
        copy = pltpu.make_async_copy(buf[name], at[name], out_sem.at[outs.index(name)])
        copy.start()
        flushed.append(copy)

    def swap(src, dst, kind, step):
        return pltpu.make_async_remote_copy(
            src_ref=src,
            dst_ref=dst,
            send_sem=swap_send.at[kind, step],
            recv_sem=swap_recv.at[kind, step],
            device_id=place.along(step),
            device_id_type=MESH,
        )

    gains = buf["gains"]
    embedded, mid, last = buf["embedded"], buf["mid"], buf["last"]
    normed, hidden, wave = at["normed"], at["hidden"], at["wave"]
    away, qkv, heads_out, returned = at["away"], buf["qkv"], buf["heads_out"], at["returned"]

    need(0)
    width = weights[0].shape[1]
    kind = lax.broadcasted_iota(jnp.int32, (8, LANES), 0)
    spot = lax.broadcasted_iota(jnp.int32, (8, LANES), 1)
    pick = (spot == kind + lead).astype(F32).astype(BF16)
    gains[...] = back_mul(pick, weights[0][:, width - LANES :])
    for block in range(0, D, 256):
        cols = pl.ds(block, 256)
        embedded[:, cols] = back_mul(at["patches"][...], weights[0][pl.ds(block, 256), : at["patches"].shape[1]])
    flush("embedded")
    flush("gains")

    def norm_rows(source, row, dest):
        step_rows = 64

        def one(step, carry):
            rows = pl.ds(pl.multiple_of(step * step_rows, step_rows), step_rows)
            dest[rows, :] = normalize(
                source[rows, :], gains[row : row + 1, :], gains[row + 3 : row + 4, :]
            ).astype(BF16)
            return carry

        lax.fori_loop(0, tokens // step_rows, one, 0)

    norm_rows(embedded, 0, normed)
    need(1)
    for step in list(range(1, narrow)) + [0]:
        owner = lax.rem(me + step, narrow)

        def project(part, carry):
            offset = pl.multiple_of(part * D + owner * head_width, LANES)
            value = matmul(normed[...], weights[1][:, pl.ds(offset, head_width)]).astype(BF16)
            if step:
                away[step - 1, part] = value
            else:
                qkv[me, part] = value
            return carry

        lax.fori_loop(0, 3, project, 0)
        if step:
            start(swap(away.at[step - 1], qkv.at[me], 0, step))
    flush("w1")
    buf["t1"][...] = normed[...].T
    flush("t1")
    advance(2)
    for step in range(1, narrow):
        swap(away.at[step - 1], qkv.at[me], 0, step).wait_recv()
    flush("qkv")

    lane = lax.broadcasted_iota(jnp.int32, (1, LANES), 1)
    scale = HD ** (-0.5)
    length = narrow * tokens
    for step in list(range(1, narrow)) + [0]:
        who = lax.rem(me + step, narrow)
        log_sums = jnp.zeros((tokens, LANES), F32)
        for pair in range(head_width // LANES):
            lanes = pl.ds(pair * LANES, LANES)
            query = qkv[who, 0, :, lanes].astype(F32)
            key = qkv[:, 1, :, lanes].reshape(length, LANES)
            value = qkv[:, 2, :, lanes].reshape(length, LANES)
            out = jnp.zeros((tokens, LANES), F32)
            for side in range(LANES // HD):
                inside = lane // HD == side
                own_query = (query * jnp.where(inside, scale, 0.0)).astype(BF16)
                scores = back_mul(own_query, key)
                highest = jnp.max(scores, -1, keepdims=True)
                exponentials = jnp.exp(scores - highest)
                summed = jnp.sum(exponentials, -1, keepdims=True)
                part = matmul(exponentials.astype(BF16), value) / summed
                out = jnp.where(inside, part, out)
                log_sums = jnp.where(
                    lane == pair * (LANES // HD) + side, highest + jnp.log(summed), log_sums
                )
            heads_out[who, :, lanes] = out.astype(BF16)
        buf["log_sums"][who] = log_sums
        if step:
            start(swap(heads_out.at[who], returned.at[me], 1, step))
            if step % 2 == 0:
                advance()
        else:
            returned[me] = heads_out[who]
    flush("heads_out")
    flush("log_sums")
    need(2)
    for step in range(1, narrow):
        swap(heads_out.at[me], returned.at[me], 1, step).wait_recv()
    for block in range(0, D, 256):
        cols = pl.ds(block, 256)
        value = embedded[:, cols]
        for source in range(narrow):
            value = value + matmul(returned[source], weights[2][pl.ds(source * head_width, head_width), cols])
        mid[:, cols] = value
    flush("w2")
    flush("mid")
    norm_rows(mid, 1, normed)
    for source in range(narrow):
        buf["t2"][pl.ds(source * head_width, head_width), :] = returned[source].T
    buf["t3"][...] = normed[...].T
    flush("t2")
    flush("t3")

    ff = weights[3].shape[1]
    tile = wave.shape[1]
    slopes = buf["slopes"]
    for block in range(0, ff, tile):
        need(3, (block, block + tile))
        wave[...] = matmul(normed[...], weights[3][:, pl.ds(block, tile)])

        def bend(step, carry):
            rows = pl.ds(pl.multiple_of(step * 16, 16), 16)
            x = wave[rows, :]
            half = 0.5 * (1.0 + lax.erf(x * (0.5**0.5)))
            hidden[rows, pl.ds(block, tile)] = (x * half).astype(BF16)
            bell = jnp.exp(-0.5 * x * x) * 0.3989422804014327
            slopes[rows, pl.ds(block, tile)] = (half + x * bell).astype(BF16)
            return carry

        lax.fori_loop(0, tokens // 16, bend, 0)
        buf["t4"][pl.ds(block, tile), :] = hidden[:, pl.ds(block, tile)].T
    flush("w3")
    flush("slopes")
    flush("t4")
    for block in range(0, D, 256):
        need(4, (block, block + 256))
        cols = pl.ds(block, 256)
        last[:, cols] = mid[:, cols] + matmul(hidden[...], weights[4][:, cols])
    flush("w4")
    flush("last")
    norm_rows(last, 2, normed)
    need(5)
    for block in range(0, weights[5].shape[1], 256):
        cols = pl.ds(block, 256)
        buf["gaussians"][:, cols] = matmul(normed[...], weights[5][:, cols])
    flush("w5")
    flush("gaussians")
    buf["t5"][...] = normed[...].T
    flush("t5")
    advance(total)
    for copy in started:
        copy.wait_send()
    for copy in flushed:
        copy.wait()


SEMS = ("own_sem", "send_sem", "recv_sem", "swap_send", "swap_recv", "out_sem")


def forward_all(shards, patches, lead, wide, narrow):
    tokens = patches.shape[0]
    widths = [shard.shape[1] for shard in shards]
    heights = [shard.shape[0] * wide * narrow for shard in shards]
    ff = widths[3]
    head_width = D // narrow
    items = forward_plan(widths)
    slots = wide + narrow - 1
    shapes = {"w%d" % which: ((heights[which], widths[which]), BF16) for which in range(1, 6)}
    shapes.update(
        gains=((8, D), F32),
        embedded=((tokens, D), F32),
        mid=((tokens, D), F32),
        last=((tokens, D), F32),
        slopes=((tokens, ff), BF16),
        t1=((D, tokens), BF16),
        t2=((D, tokens), BF16),
        t3=((D, tokens), BF16),
        t4=((ff, tokens), BF16),
        t5=((D, tokens), BF16),
        qkv=((narrow, 3, tokens, head_width), BF16),
        heads_out=((narrow, tokens, head_width), BF16),
        log_sums=((narrow, tokens, LANES), F32),
        gaussians=((tokens, widths[5]), F32),
    )
    ins = tuple("s%d" % which for which in range(6)) + ("patches",)
    outs = tuple(shapes)
    extras = dict(
        first_weight=pltpu.VMEM((heights[0], widths[0]), BF16),
        normed=pltpu.VMEM((tokens, D), BF16),
        hidden=pltpu.VMEM((tokens, ff), BF16),
        wave=pltpu.VMEM((tokens, 512), F32),
        away=pltpu.VMEM((narrow - 1, 3, tokens, head_width), BF16),
        returned=pltpu.VMEM((narrow, tokens, head_width), BF16),
        own_sem=pltpu.SemaphoreType.DMA((6,)),
        send_sem=pltpu.SemaphoreType.DMA((len(items), slots)),
        recv_sem=pltpu.SemaphoreType.DMA((len(items), slots)),
        swap_send=pltpu.SemaphoreType.DMA((2, narrow)),
        swap_recv=pltpu.SemaphoreType.DMA((2, narrow)),
        out_sem=pltpu.SemaphoreType.DMA((len(outs),)),
    )
    scratch = tuple("v_" + name for name in outs) + tuple(extras)
    anywhere = pl.BlockSpec(memory_space=pl.ANY)
    results = pl.pallas_call(
        functools.partial(forward_kernel, items, wide, narrow, lead, ins, outs, scratch),
        out_shape=[jax.ShapeDtypeStruct(*shapes[name]) for name in outs],
        in_specs=[anywhere] * 6 + [pl.BlockSpec(memory_space=pltpu.VMEM)],
        out_specs=[anywhere] * len(outs),
        scratch_shapes=[pltpu.VMEM(*shapes[name]) for name in outs] + list(extras.values()),
        compiler_params=pltpu.CompilerParams(
            collective_id=0, has_side_effects=True, vmem_limit_bytes=60 * MIB
        ),
        name="forward",
    )(*shards, patches)
    return dict(zip(outs, results))


def tile_of(width):
    for tile in (512, 384, 256, 128):
        if width % tile == 0:
            return tile
    return width


def reduce_kernel(items, wide, narrow, count, *refs):
    lefts, rights = refs[:count], refs[count : 2 * count]
    extra, term = refs[2 * count : 2 * count + 2]
    outs = refs[2 * count + 2 : 3 * count + 2]
    sums = refs[3 * count + 2]
    scratch = list(refs[3 * count + 3 :])
    place = Place(wide, narrow)
    chips = place.chips
    total = len(items)
    sent = [scratch.pop(0) for _ in items]
    held = [scratch.pop(0) for _ in items]
    passed = [[scratch.pop(0) for _ in place.bits] for _ in items]
    last = [scratch.pop(0) for _ in items]
    wide_tiles, narrow_tiles, send_sem, recv_sem, tile_send, tile_recv = scratch
    peers = [place.twin]
    for step in range(1, wide):
        peers.append((lax.rem(place.w + step, wide), place.n))
    for step in range(1, narrow):
        peers.append(place.along(step))
    greet(peers[1:])

    started = []

    def start(copy):
        copy.start()
        started.append(copy)

    def remote(item, src, dst, slot, peer):
        return pltpu.make_async_remote_copy(
            src_ref=src,
            dst_ref=dst,
            send_sem=send_sem.at[item, slot],
            recv_sem=recv_sem.at[item, slot],
            device_id=peer,
            device_id_type=MESH,
        )

    def bits_of(item):
        return place.bits[::-1] if items[item][3] == 0 else place.bits

    def product(item, mask, core, into, plus):
        which, begin, width, _ = items[item]
        left, right = lefts[which], rights[which]
        rows = into.shape[2]
        tile = tile_of(width)
        together = max(1, min(narrow, 128 // rows))
        owner = flip(place.chip, mask)
        with_extra = which == 0 and begin + width == right.shape[1]

        def one(step, carry):
            across, down = step % (width // tile), step // (width // tile)
            offset = pl.multiple_of(begin + across * tile, LANES)
            local = pl.multiple_of(across * tile, LANES)
            ns = pl.ds(down * together, together)
            lhs = left[owner, core, ns].reshape(together * rows, left.shape[-1])
            value = jnp.dot(lhs, right[:, pl.ds(offset, tile)], preferred_element_type=F32)
            if with_extra:
                more = extra[owner, core, ns].reshape(together * rows, LANES)
                more = jnp.concatenate([jnp.zeros((together * rows, tile - LANES), F32), more], 1)
                value = value + more
            value = value.reshape(together, rows, tile)
            if plus is not None:
                value = value + plus[mask, ns, :, pl.ds(local, tile)].astype(F32)
            into[mask, ns, :, pl.ds(local, tile)] = value.astype(BF16)
            return carry

        assert not with_extra or tile == width
        lax.fori_loop(0, (width // tile) * (narrow // together), one, 0)

    def to_twin(item, mask):
        return remote(item, sent[item].at[mask], held[item].at[mask], mask, place.twin)

    def across(item, mask, bit, number, slot):
        return remote(
            item, held[item].at[mask], passed[item][number].at[slot], chips + mask, place.across(bit)
        )

    def along(item, step):
        target = place.along(step)
        return remote(
            item,
            held[item].at[0, target[1]],
            last[item].at[narrow - step - 1],
            2 * chips + narrow - step - 1,
            target,
        )

    def split(item, number):
        bits = bits_of(item)
        keep = list(range(chips))
        for bit in bits[:number]:
            keep = [mask for mask in keep if not mask & bit]
        if number < len(bits):
            return [m for m in keep if m & bits[number]], [m for m in keep if not m & bits[number]]
        return [], keep

    def add_into(dest, dest_at, src, src_at):
        rows, width = dest.shape[-2:]

        def one(step, carry):
            a = dest[dest_at, step].astype(F32) + src[src_at, step].astype(F32)
            dest[dest_at, step] = a.astype(BF16)
            return carry

        lax.fori_loop(0, narrow, one, 0)

    def send_on(item, number, ready):
        bits = bits_of(item)
        away, keep = split(item, number)
        if number < len(bits):
            for mask in away:
                ready(mask)
                start(across(item, mask, bits[number], number, keep.index(mask ^ bits[number])))
            for mask in keep:
                ready(mask)
        else:
            ready(0)
            for step in range(1, narrow):
                start(along(item, step))

    def stage(item, number):
        bits = bits_of(item)
        if number == 0:

            def ready(mask):
                to_twin(item, mask).wait_recv()
                product(item, mask, place.core, held[item], held[item])

            send_on(item, 0, ready)
        else:
            bit = bits[number - 1]
            _, kept = split(item, number - 1)

            def ready(mask):
                slot = kept.index(mask)
                across(item, mask ^ bit, bit, number - 1, slot).wait_recv()
                add_into(held[item], mask, passed[item][number - 1], slot)

            send_on(item, number, ready)

    def finish(item):
        which, begin, width, _ = items[item]
        value = held[item][0, place.n].astype(F32)
        for step in range(1, narrow):
            along(item, step).wait_recv()
        for slot in range(narrow - 1):
            value = value + last[item][slot].astype(F32)
        outs[which][:, pl.ds(begin, width)] = value
        return jnp.sum(value * value)

    for item in range(total):
        for mask in range(chips):
            product(item, mask, 1 - place.core, sent[item], None)
            start(to_twin(item, mask))
    squares = jnp.zeros((), F32)
    depth = len(place.bits) + 1
    for tick in range(0, total + 2 * depth, 2):
        for number in reversed(range(depth + 1)):
            for item in (tick - 2 * number, tick - 2 * number + 1):
                if 0 <= item < total:
                    if number < depth:
                        stage(item, number)
                    else:
                        squares = squares + finish(item)

    rows = lax.broadcasted_iota(jnp.int32, (8, LANES), 0)
    wide_tiles[place.w] = jnp.where(rows == 0, term[...], squares)

    def tile_copy(buffer, at, slot, peer):
        return pltpu.make_async_remote_copy(
            src_ref=buffer.at[at],
            dst_ref=buffer.at[at],
            send_sem=tile_send.at[slot],
            recv_sem=tile_recv.at[slot],
            device_id=peer,
            device_id_type=MESH,
        )

    for step in range(1, wide):
        start(tile_copy(wide_tiles, place.w, step - 1, (lax.rem(place.w + step, wide), place.n)))
    for step in range(1, wide):
        tile_copy(wide_tiles, place.w, step - 1, (lax.rem(place.w + step, wide), place.n)).wait_recv()
    whole = wide_tiles[0]
    for index in range(1, wide):
        whole = whole + wide_tiles[index]
    narrow_tiles[place.n] = whole
    for step in range(1, narrow):
        start(tile_copy(narrow_tiles, place.n, wide + step - 1, place.along(step)))
    for step in range(1, narrow):
        tile_copy(narrow_tiles, place.n, wide + step - 1, place.along(step)).wait_recv()
    whole = narrow_tiles[0]
    for index in range(1, narrow):
        whole = whole + narrow_tiles[index]
    sums[...] = whole
    for copy in started:
        copy.wait_send()


def reduce_all(lefts, rights, extra, term, wide, narrow, order):
    count = len(lefts)
    chips = wide // 2
    shaped = [left.reshape(chips, 2, narrow, -1, left.shape[1]) for left in lefts]
    extra = extra.reshape(chips, 2, narrow, -1, LANES)
    widths = [right.shape[1] for right in rights]
    rows = [left.shape[3] for left in shaped]
    items = work_items(widths, order)
    slots = 2 * chips + narrow - 1
    scratch = []
    for which, _, width, _ in items:
        scratch.append(pltpu.VMEM((chips, narrow, rows[which], width), BF16))
    for which, _, width, _ in items:
        scratch.append(pltpu.VMEM((chips, narrow, rows[which], width), BF16))
    for which, _, width, _ in items:
        size = chips
        while size > 1:
            size //= 2
            scratch.append(pltpu.VMEM((size, narrow, rows[which], width), BF16))
    for which, _, width, _ in items:
        scratch.append(pltpu.VMEM((narrow - 1, rows[which], width), BF16))
    scratch += [
        pltpu.VMEM((wide, 8, LANES), F32),
        pltpu.VMEM((narrow, 8, LANES), F32),
        pltpu.SemaphoreType.DMA((len(items), slots)),
        pltpu.SemaphoreType.DMA((len(items), slots)),
        pltpu.SemaphoreType.DMA((wide + narrow,)),
        pltpu.SemaphoreType.DMA((wide + narrow,)),
    ]
    vmem = pl.BlockSpec(memory_space=pltpu.VMEM)
    return pl.pallas_call(
        functools.partial(reduce_kernel, items, wide, narrow, count),
        out_shape=[jax.ShapeDtypeStruct((rows[i], widths[i]), F32) for i in range(count)]
        + [jax.ShapeDtypeStruct((8, LANES), F32)],
        in_specs=[vmem] * (2 * count + 2),
        out_specs=[vmem] * (count + 1),
        scratch_shapes=scratch,
        compiler_params=pltpu.CompilerParams(
            collective_id=1, has_side_effects=True, vmem_limit_bytes=60 * MIB
        ),
        name="reduce_grads",
    )(*shaped, *rights, extra, term)


def render_kernel(
    gauss_ref, weight_ref, target_ref, mask_ref, pair_ref, view_ref, total_ref, grad_ref, term_ref, feat, dfeat
):
    quads = gauss_ref.shape[0] // NVIEW
    span = weight_ref.shape[1]
    pairs = pair_ref.shape[1]
    scale = 1.0 / total_ref[0].astype(F32)

    def channel(index):
        return gauss_ref[:, index * PP : (index + 1) * PP]

    def shared():
        opacity = jax.nn.sigmoid(channel(3))
        extent = jax.nn.sigmoid(channel(5) + channel(6) + channel(7))
        lead = channel(8)
        denom = 1.0 + lead * lead + channel(9) * channel(9) + channel(10) * channel(10) + channel(11) * channel(11)
        facing = lead * lead / denom
        raw = channel(4)
        depth = jnp.maximum(raw, 0.0) + jnp.log1p(jnp.exp(-jnp.abs(raw)))
        return opacity, extent, lead, denom, facing, raw, depth

    opacity, extent, lead, denom, facing, raw, depth = shared()
    footprint = opacity * extent * facing
    channels = [jax.nn.sigmoid(channel(index)) * footprint for index in range(3)]
    channels += [footprint, depth * footprint]
    for index, value in enumerate(channels):
        for view in range(NVIEW):
            feat[index * quads : (index + 1) * quads, view * PP : (view + 1) * PP] = value[
                view * quads : (view + 1) * quads
            ]
    rendered = jnp.dot(feat[...], weight_ref[...], precision=HIGHEST, preferred_element_type=F32)
    parts = [rendered[index * quads : (index + 1) * quads] for index in range(5)]
    lane = lax.broadcasted_iota(jnp.int32, (quads, span), 1)
    live = jnp.where(lane < view_ref[0] * PP, mask_ref[...], 0).astype(F32)
    term = jnp.zeros((quads, span), F32)
    slopes = []
    for index in range(3):
        error = parts[index] - target_ref[index * quads : (index + 1) * quads, :].astype(F32)
        term = term + live * error * error
        slopes.append(2.0 * scale * live * error)
    below = 1.0 + parts[3]
    depth_out = parts[4] / below

    first, second = pair_ref[0:1, :], pair_ref[1:2, :]
    least = jnp.minimum(first, second)
    down = (jnp.abs(first - second) == P_SIZE).astype(jnp.int32)
    place = quads * PP
    slot, local = least // place, least % place
    high = down * quads + local // PP
    low = slot * PP + local % PP
    high_hot = (lax.broadcasted_iota(jnp.int32, (2 * quads, pairs), 0) == high).astype(F32).astype(BF16)
    low_hot = (lax.broadcasted_iota(jnp.int32, (span, pairs), 0) == low).astype(F32).astype(BF16)
    counts = back_mul(high_hot, low_hot)
    slope = jnp.zeros((quads, span), F32)
    for which, shift in enumerate((1, P_SIZE)):
        count = counts[which * quads : (which + 1) * quads]
        weight = DEPTH_WEIGHT * count * live * pltpu.roll(live, span - shift, 1)
        gap = depth_out - pltpu.roll(depth_out, span - shift, 1)
        term = term + weight * gap * gap
        pull = 2.0 * scale * weight * gap
        slope = slope + pull - pltpu.roll(pull, shift, 1)
    term_ref[...] = jnp.full(term_ref.shape, jnp.sum(term), F32)
    over = slope / below
    slopes += [-over * depth_out, over]
    stacked = jnp.concatenate(slopes, 0)
    dfeat[...] = lax.dot_general(
        stacked, weight_ref[...], (((1,), (1,)), ((), ())), precision=HIGHEST, preferred_element_type=F32
    )

    def feature_grad(index):
        return jnp.concatenate(
            [
                dfeat[index * quads : (index + 1) * quads, view * PP : (view + 1) * PP]
                for view in range(NVIEW)
            ],
            0,
        )

    def put(index, value):
        grad_ref[:, index * PP : (index + 1) * PP] = value.astype(BF16)

    d_foot = feature_grad(3)
    for index in range(3):
        tint = jax.nn.sigmoid(channel(index))
        upper = feature_grad(index)
        d_foot = d_foot + upper * tint
        put(index, upper * footprint * tint * (1.0 - tint))
    d_last = feature_grad(4)
    d_foot = d_foot + d_last * depth
    put(3, d_foot * extent * facing * opacity * (1.0 - opacity))
    put(4, d_last * footprint * jax.nn.sigmoid(raw))
    d_extent = d_foot * opacity * facing * extent * (1.0 - extent)
    for index in (5, 6, 7):
        put(index, d_extent)
    d_facing = d_foot * opacity * extent
    put(8, d_facing * 2.0 * lead / denom * (1.0 - facing))
    for index in (9, 10, 11):
        put(index, -2.0 * d_facing * facing / denom * channel(index))


def render(gaussians, weights, targets, mask, pairs, view_count, pair_total):
    rows = gaussians.shape[0]
    quads = rows // NVIEW
    slots, views = weights.shape[:2]
    spread = weights.transpose(1, 2, 0, 3).reshape(views * PP, slots * PP)
    wanted = targets.reshape(slots, 3, quads, PP).transpose(1, 2, 0, 3).reshape(3 * quads, slots * PP)
    valid = mask.reshape(slots, quads, PP).transpose(1, 0, 2).reshape(quads, slots * PP)
    vmem = pl.BlockSpec(memory_space=pltpu.VMEM)
    smem = pl.BlockSpec(memory_space=pltpu.SMEM)
    return pl.pallas_call(
        render_kernel,
        out_shape=[
            jax.ShapeDtypeStruct(gaussians.shape, BF16),
            jax.ShapeDtypeStruct((8, LANES), F32),
        ],
        in_specs=[vmem] * 5 + [smem] * 2,
        out_specs=[vmem] * 2,
        scratch_shapes=[pltpu.VMEM((5 * quads, views * PP), F32)] * 2,
        compiler_params=pltpu.CompilerParams(vmem_limit_bytes=48 * MIB),
        name="render",
    )(gaussians, spread, wanted, valid, pairs, view_count, pair_total)


def forward_plain(shards, patches, features, kinds):
    weights = [lax.all_gather(shard, ("wide", "narrow"), axis=0, tiled=True) for shard in shards]
    groups = lax.axis_size("narrow")
    rows = patches.shape[0]
    gains = weights[0][:, features : features + kinds].T.astype(F32)
    embedded = back_mul(patches[:, :features], weights[0][:, :features])
    normed_one = layer_norm(embedded, gains[0], gains[3]).astype(BF16)
    mixed = matmul(normed_one, weights[1]).astype(BF16).reshape(rows, 3, groups, -1)
    mixed = mixed.transpose(2, 1, 0, 3)
    qkv = lax.all_to_all(mixed, "narrow", split_axis=0, concat_axis=0, tiled=True)
    width = qkv.shape[-1]
    length = groups * rows
    heads = width // HD
    parts = [qkv[:, part].reshape(length, heads, HD) for part in range(3)]
    attended, logsum = attention_forward(*parts)
    log_sums = logsum.transpose(0, 2, 1).reshape(groups, rows, heads)
    returned = lax.all_to_all(
        attended.reshape(groups, rows, width), "narrow", split_axis=0, concat_axis=0, tiled=True
    )
    returned = returned.transpose(1, 0, 2).reshape(rows, D)
    mid = embedded + matmul(returned, weights[2])
    normed_two = layer_norm(mid, gains[1], gains[4]).astype(BF16)
    expanded = matmul(normed_two, weights[3])
    half = 0.5 * (1.0 + lax.erf(expanded * (0.5**0.5)))
    activated = (expanded * half).astype(BF16)
    bell = jnp.exp(-0.5 * expanded * expanded) * 0.3989422804014327
    slopes = (half + expanded * bell).astype(BF16)
    last = mid + matmul(activated, weights[4])
    normed_three = layer_norm(last, gains[2], gains[5]).astype(BF16)
    kept = {"w%d" % which: weights[which] for which in range(1, 6)}
    kept.update(
        gains=gains,
        embedded=embedded,
        mid=mid,
        last=last,
        slopes=slopes,
        t1=normed_one.T,
        t2=returned.T,
        t3=normed_two.T,
        t4=activated.T,
        t5=normed_three.T,
        qkv=qkv,
        heads_out=attended,
        log_sums=log_sums,
        gaussians=matmul(normed_three, weights[5]),
    )
    return kept


def body(
    views,
    render_w,
    targets,
    pix_mask,
    pairs,
    view_count,
    pair_total,
    embed_weight,
    embed_first,
    embed_second,
    mixer_weight,
    mixer_first,
    mixer_second,
    merge_weight,
    merge_first,
    merge_second,
    expand_weight,
    expand_first,
    expand_second,
    shrink_weight,
    shrink_first,
    shrink_second,
    unpatch_weight,
    unpatch_first,
    unpatch_second,
    norm_params,
    norm_first,
    norm_second,
):
    masters = (embed_weight, mixer_weight, merge_weight, expand_weight, shrink_weight, unpatch_weight, norm_params)
    firsts = (embed_first, mixer_first, merge_first, expand_first, shrink_first, unpatch_first, norm_first)
    seconds = (embed_second, mixer_second, merge_second, expand_second, shrink_second, unpatch_second, norm_second)
    groups = lax.axis_size("narrow")
    wide_count = lax.axis_size("wide")
    features = embed_weight.shape[0]
    kinds = norm_params.shape[0]
    padded = -(-(features + kinds) // LANES) * LANES
    fill = padded - features - kinds
    by_kernel = mixer_weight.shape[0] % 16 == 0

    first_shard = jnp.concatenate([embed_weight.T, norm_params.T], 1)
    first_shard = jnp.pad(first_shard.astype(BF16), ((0, 0), (0, fill)))
    shards = [first_shard] + [weight.astype(BF16) for weight in masters[1:6]]
    patches = views.reshape(-1, features)
    rows = patches.shape[0]
    patches = jnp.pad(patches, ((0, 0), (0, padded - features)))
    if by_kernel:
        kept = forward_all(shards, patches, features % LANES, wide_count, groups)
    else:
        kept = forward_plain(shards, patches, features, kinds)
    gains = kept["gains"]
    weights = [None] + [kept["w%d" % which] for which in range(1, 6)]
    norm_back_one = jax.vjp(layer_norm, kept["embedded"], gains[0], gains[3])[1]
    norm_back_two = jax.vjp(layer_norm, kept["mid"], gains[1], gains[4])[1]
    norm_back_three = jax.vjp(layer_norm, kept["last"], gains[2], gains[5])[1]
    qkv = kept["qkv"]
    width = qkv.shape[-1]
    length = groups * rows
    local_heads = width // HD
    queries, keys_all, values_all = (
        qkv[:, part].reshape(length, local_heads, HD) for part in range(3)
    )
    blocked = min(512, length)
    logsum = kept["log_sums"][:, :, :local_heads].reshape(length // blocked, blocked, local_heads)
    logsum = logsum.transpose(0, 2, 1)
    gaussians = kept["gaussians"]
    divisor = pair_total[0].astype(F32)

    gauss_low, term = render(
        gaussians, render_w[0], targets[0], pix_mask[0], pairs[0], view_count, pair_total
    )
    residual_grad, gain_three, shift_three = norm_back_three(back_mul(gauss_low, weights[5]))
    shrink_low = residual_grad.astype(BF16)
    expand_low = (back_mul(shrink_low, weights[4]) * kept["slopes"].astype(F32)).astype(BF16)
    through_two, gain_two, shift_two = norm_back_two(back_mul(expand_low, weights[3]))
    residual_grad = residual_grad + through_two
    merge_low = residual_grad.astype(BF16)
    out_grad = back_mul(merge_low, weights[2]).astype(BF16).reshape(rows, groups, width)
    head_grad = lax.all_to_all(out_grad, "narrow", split_axis=1, concat_axis=0, tiled=True).reshape(
        length, local_heads, HD
    )
    query_grad, key_grad, value_grad = attention_backward(queries, keys_all, values_all, logsum, head_grad)
    stacked = jnp.stack([query_grad, key_grad, value_grad], 1).astype(BF16).reshape(length, 3, 1, width)
    mixed_grad = lax.all_to_all(stacked, "narrow", split_axis=0, concat_axis=2, tiled=True).reshape(
        rows, 3 * D
    )
    through_one, gain_one, shift_one = norm_back_one(back_mul(mixed_grad, weights[1]))
    embed_grad = (residual_grad + through_one).astype(BF16)
    grad_norms = jnp.stack([gain_one, gain_two, gain_three, shift_one, shift_two, shift_three])

    lefts = [embed_grad.T] + [kept["t%d" % which] for which in range(1, 6)]
    rights = [patches, mixed_grad, merge_low, expand_low, shrink_low, gauss_low]
    at = features % LANES
    extra = jnp.pad(grad_norms.T, ((0, 0), (at, LANES - at - kinds)))
    if by_kernel:
        *sums, totals = reduce_all(
            lefts, rights, extra, term, wide_count, groups, (5, 4, 3, 2, 1, 0)
        )
        loss_sum, square_sum = totals[0, 0], totals[1, 0]
    else:
        products = [matmul(left, right) for left, right in zip(lefts, rights)]
        products[0] = products[0].at[:, -LANES:].add(extra)
        sums = [
            lax.psum_scatter(
                product.astype(BF16), ("wide", "narrow"), scatter_dimension=0, tiled=True
            ).astype(F32)
            for product in products
        ]
        squares = sum(jnp.sum(part * part) for part in sums)
        loss_sum, square_sum = lax.psum((term[0, 0], squares), ("wide", "narrow"))
    first_sum = sums[0].T
    grads = [first_sum[:features]] + list(sums[1:]) + [first_sum[features : features + kinds]]
    loss = loss_sum / divisor
    grad_norm = jnp.sqrt(square_sum)
    factor = jnp.minimum(1.0, CLIP_NORM / (grad_norm + 1e-06))
    results = []
    for which in range(7):
        results += adamw(masters[which], firsts[which], seconds[which], grads[which] * factor, RATES[which])
    return tuple(results) + (loss, grad_norm)


def solution(mesh):
    columns = P(None, ("wide", "narrow"))
    rows = P(("wide", "narrow"), None)
    weights = (columns,) * 3 + (rows,) * 15 + (columns,) * 3
    return jax.shard_map(
        body,
        mesh=mesh,
        in_specs=(
            P("wide", None, "narrow", None),
            P("wide", None, None, None, None),
            P("wide", None, None, "narrow"),
            P("wide", None, "narrow"),
            P("wide", None, "narrow"),
            P("wide"),
            P(),
        )
        + weights,
        out_specs=weights + (P(), P()),
        check_vma=False,
    )
```

```python
import functools

import jax
import jax.numpy as jnp
from jax import lax
from jax.experimental import pallas as pl
from jax.experimental.pallas import tpu as pltpu
from jax.sharding import PartitionSpec as P

D = 1024
HD = 64
P_SIZE = 8
PP = 64
NVIEW = 4
TMAX = 12
STEP = 10
LANES = 128
MIB = 1024 * 1024

DEPTH_WEIGHT = 1.0
CLIP_NORM = 0.01
BETA_ONE = 0.9
BETA_TWO = 0.95
ADAM_EPS = 1e-08
DECAY = 0.05
RATES = (0.05, 0.05, 0.5, 0.05, 0.05, 0.05, 0.8)
MESH = pl.DeviceIdType.MESH
WIDE, NARROW = BOTH = ("wide", "narrow")
HIGHEST = lax.Precision.HIGHEST
F32 = jnp.float32
BF16 = jnp.bfloat16


def matmul(left, right):
    return jnp.dot(left, right, preferred_element_type=F32)


def outer_sum(left, right):
    return lax.dot_general(left, right, (((0,), (0,)), ((), ())), preferred_element_type=F32)


def back_mul(grad, weight):
    return lax.dot_general(grad, weight, (((1,), (1,)), ((), ())), preferred_element_type=F32)


def layer_norm(values, gain, shift):
    centred = values - jnp.mean(values, -1, keepdims=True)
    spread = jnp.mean(centred * centred, -1, keepdims=True)
    return centred * lax.rsqrt(spread + 1e-05) * gain + shift


def exact_gelu(values):
    return jax.nn.gelu(values, approximate=False)


def attention_forward(queries, keys, values):
    length, heads = (queries.shape[0], queries.shape[1])
    blocked = min(512, length)
    scale = HD ** (-0.5)

    def one_block(query_block):
        scores = (
            jnp.einsum("qhd,khd->hqk", query_block, keys, preferred_element_type=jnp.float32)
            * scale
        )
        highest = jnp.max(scores, -1, keepdims=True)
        exponentials = jnp.exp(scores - highest)
        summed = jnp.sum(exponentials, -1, keepdims=True)
        softmaxed = (exponentials / summed).astype(jnp.bfloat16)
        output = jnp.einsum("hqk,khd->qhd", softmaxed, values, preferred_element_type=jnp.float32)
        return (output.astype(jnp.bfloat16), (highest + jnp.log(summed))[:, :, 0])

    output, logsum = lax.map(one_block, queries.reshape(length // blocked, blocked, heads, HD))
    return (output.reshape(length, heads * HD), logsum)


def attention_backward(queries, keys, values, logsum, out_grad):
    length, heads = (queries.shape[0], queries.shape[1])
    blocked = min(512, length)
    scale = HD ** (-0.5)

    def one_block(carry, inputs):
        key_grad, value_grad = carry
        query_block, logsum_block, grad_block = inputs
        scores = (
            jnp.einsum("qhd,khd->hqk", query_block, keys, preferred_element_type=jnp.float32)
            * scale
        )
        softmaxed = jnp.exp(scores - logsum_block[:, :, None])
        value_grad = value_grad + jnp.einsum(
            "hqk,qhd->khd",
            softmaxed.astype(jnp.bfloat16),
            grad_block,
            preferred_element_type=jnp.float32,
        )
        prob_grad = jnp.einsum(
            "qhd,khd->hqk", grad_block, values, preferred_element_type=jnp.float32
        )
        score_grad = softmaxed * (prob_grad - jnp.sum(softmaxed * prob_grad, -1, keepdims=True))
        score_low = score_grad.astype(jnp.bfloat16)
        query_grad = (
            jnp.einsum("hqk,khd->qhd", score_low, keys, preferred_element_type=jnp.float32) * scale
        )
        key_grad = (
            key_grad
            + jnp.einsum("hqk,qhd->khd", score_low, query_block, preferred_element_type=jnp.float32)
            * scale
        )
        return ((key_grad, value_grad), query_grad)

    zeros = jnp.zeros((length, heads, HD), jnp.float32)
    shaped = (
        queries.reshape(length // blocked, blocked, heads, HD),
        logsum,
        out_grad.reshape(length // blocked, blocked, heads, HD),
    )
    (key_grad, value_grad), query_grad = lax.scan(one_block, (zeros, zeros), shaped)
    return (query_grad.reshape(length, heads, HD), key_grad, value_grad)


def adamw(weight, first, second, grad, rate):
    first = BETA_ONE * first + (1.0 - BETA_ONE) * grad
    second = BETA_TWO * second + (1.0 - BETA_TWO) * grad * grad
    first_hat = first / (1.0 - BETA_ONE**STEP)
    second_hat = second / (1.0 - BETA_TWO**STEP)
    weight = weight - rate * (first_hat / (jnp.sqrt(second_hat) + ADAM_EPS) + DECAY * weight)
    return (weight, first, second)


def chip_bits(chips):
    bits, step = [], 1
    while step < chips:
        bits.append(step)
        step *= 2
    return bits


def flip(chip, mask):
    for bit in chip_bits(mask + 1):
        if mask & bit:
            chip = chip + (1 - 2 * (chip // bit % 2)) * bit
    return chip


def column_halves(width):
    first = -(-width // (2 * LANES)) * LANES
    return ((0, first), (first, width - first))


def work_items(widths, order):
    return [(which,) + half + (side,) for which in order for side, half in enumerate(column_halves(widths[which]))]


class Bag:
    def __init__(self, pairs):
        vars(self).update(pairs)


class Place:
    def __init__(self, wide, narrow):
        self.wide, self.narrow = wide, narrow
        self.chips = wide // 2
        self.bits = chip_bits(self.chips)
        self.w = lax.axis_index(WIDE)
        self.n = lax.axis_index(NARROW)
        self.chip = self.w // 2
        self.core = self.w % 2
        self.twin = (2 * self.chip + 1 - self.core, self.n)

    def across(self, mask):
        return (2 * flip(self.chip, mask) + self.core, self.n)

    def along(self, step):
        return (self.w, lax.rem(self.n + step, self.narrow))

    def neighbours(self):
        return (
            [self.twin]
            + [self.across(bit) for bit in self.bits]
            + [self.along(step) for step in range(1, self.narrow)]
        )


def greet(peers):
    barrier = pltpu.get_barrier_semaphore()
    for peer in peers:
        pl.semaphore_signal(barrier, inc=1, device_id=peer, device_id_type=MESH)
    pl.semaphore_wait(barrier, len(peers))


def normalize(values, gain, shift):
    centred = values - jnp.mean(values, -1, keepdims=True)
    spread = jnp.mean(centred * centred, -1, keepdims=True)
    return centred * lax.rsqrt(spread + 1e-05) * gain + shift


def forward_plan(widths):
    items = []
    for which, cuts in ((0, 1), (1, 3), (2, 1), (3, 4), (5, 1), (4, 4)):
        size = widths[which] // cuts
        for cut in range(cuts):
            for side, (start, width) in enumerate(column_halves(size)):
                items.append((which, cut * size + start, width, side))
    return items


def forward_kernel(items, wide, narrow, lead, ins, outs, scratch, *refs):
    at = Bag(zip(ins + scratch, refs[: len(ins)] + refs[len(ins) + len(outs) :]))
    results = refs[len(ins) : len(ins) + len(outs)]
    weights = [at.first_weight, at.w1, at.w2, at.w3, at.w4, at.w5]
    shards = [at.s0, at.s1, at.s2, at.s3, at.s4, at.s5]
    own_sem, send_sem, recv_sem = at.own_sem, at.send_sem, at.recv_sem
    swap_send, swap_recv, out_sem = at.swap_send, at.swap_recv, at.out_sem
    place = Place(wide, narrow)
    chips, me = place.chips, place.n
    tokens = at.patches.shape[0]
    head_width = D // narrow
    total = len(items)
    started = []

    def start(copy):
        copy.start()
        started.append(copy)

    greet(place.neighbours())
    rows_of = [shard.shape[0] for shard in shards]

    def rows_at(which, chip, core, node=None):
        rows = rows_of[which]
        if node is None:
            return pl.ds(pl.multiple_of((chip * 2 + core) * narrow * rows, rows), narrow * rows)
        return pl.ds(pl.multiple_of(((chip * 2 + core) * narrow + node) * rows, rows), rows)

    own = []
    for which in range(6):
        copy = pltpu.make_async_copy(
            shards[which], weights[which].at[rows_at(which, place.chip, place.core, me), :], own_sem.at[which]
        )
        copy.start()
        own.append(copy)

    def remote(item, src, dst, slot, peer):
        return pltpu.make_async_remote_copy(
            src_ref=src,
            dst_ref=dst,
            send_sem=send_sem.at[item, slot],
            recv_sem=recv_sem.at[item, slot],
            device_id=peer,
            device_id_type=MESH,
        )

    def group(item, mask):
        which, begin, width, _ = items[item]
        return weights[which].at[rows_at(which, flip(place.chip, mask), place.core), pl.ds(begin, width)]

    def along(item, step):
        which, begin, width, _ = items[item]
        return remote(
            item,
            shards[which].at[:, pl.ds(begin, width)],
            weights[which].at[rows_at(which, place.chip, place.core, me), pl.ds(begin, width)],
            2 * chips + step - 1,
            place.along(step),
        )

    def bits_of(item):
        return place.bits if items[item][3] == 0 else place.bits[::-1]

    def across(item, mask, bit):
        return remote(item, group(item, mask), group(item, mask), mask ^ bit, place.across(bit))

    def to_twin(item, mask):
        return remote(item, group(item, mask), group(item, mask), chips + mask, place.twin)

    waited = set()

    def stage(item, number):
        bits = bits_of(item)
        if number > len(bits):
            for mask in range(chips):
                to_twin(item, mask).wait_recv()
            return
        held = [0]
        if number == 0:
            if items[item][0] not in waited:
                waited.add(items[item][0])
                own[items[item][0]].wait()
            for step in range(1, narrow):
                along(item, step).wait_recv()
            fresh = [0]
        else:
            for bit in bits[: number - 1]:
                held = held + [mask ^ bit for mask in held]
            fresh = [mask ^ bits[number - 1] for mask in held]
            for mask in fresh:
                across(item, mask ^ bits[number - 1], bits[number - 1]).wait_recv()
            held = held + fresh
        if number < len(bits):
            for mask in held:
                start(across(item, mask, bits[number]))
        for mask in fresh:
            start(to_twin(item, mask))

    arrived = [False] * total

    def gather():
        ahead = 4
        for item in range(min(ahead, total)):
            for step in range(1, narrow):
                start(along(item, step))
        depth = len(place.bits) + 2
        for tick in range(0, total + 2 * (depth - 1), 2):
            for number in reversed(range(depth)):
                for item in (tick - 2 * number, tick - 2 * number + 1):
                    if 0 <= item < total:
                        stage(item, number)
                        if number == depth - 1:
                            arrived[item] = True
            for item in (tick + ahead, tick + ahead + 1):
                if item < total:
                    for step in range(1, narrow):
                        start(along(item, step))
            yield

    engine = gather()

    def advance(steps=1):
        for _ in range(steps):
            next(engine, None)

    def need(which, columns=None):
        wanted = [
            index
            for index, (owner, begin, width, _) in enumerate(items)
            if owner == which and (columns is None or (begin < columns[1] and begin + width > columns[0]))
        ]
        while not all(arrived[index] for index in wanted):
            next(engine)

    flushed = []

    def flush(ref):
        index = [vars(at)[name] is ref for name in outs].index(True)
        copy = pltpu.make_async_copy(ref, results[index], out_sem.at[index])
        copy.start()
        flushed.append(copy)

    def swap(src, dst, kind, step):
        return pltpu.make_async_remote_copy(
            src_ref=src,
            dst_ref=dst,
            send_sem=swap_send.at[kind, step],
            recv_sem=swap_recv.at[kind, step],
            device_id=place.along(step),
            device_id_type=MESH,
        )

    gains = at.gains
    embedded, mid, last = at.embedded, at.mid, at.last
    normed, hidden, wave = at.normed, at.hidden, at.wave
    away, qkv, heads_out, returned = at.away, at.qkv, at.heads_out, at.returned

    need(0)
    width = weights[0].shape[1]
    kind = lax.broadcasted_iota(jnp.int32, (8, LANES), 0)
    spot = lax.broadcasted_iota(jnp.int32, (8, LANES), 1)
    pick = (spot == kind + lead).astype(F32).astype(BF16)
    gains[...] = back_mul(pick, weights[0][:, width - LANES :])
    for block in range(0, D, 256):
        cols = pl.ds(block, 256)
        embedded[:, cols] = back_mul(at.patches[...], weights[0][pl.ds(block, 256), : at.patches.shape[1]])
    flush(at.embedded)
    flush(at.gains)

    def norm_rows(source, row, dest):
        step_rows = 64

        def one(step, carry):
            rows = pl.ds(pl.multiple_of(step * step_rows, step_rows), step_rows)
            dest[rows, :] = normalize(
                source[rows, :], gains[row : row + 1, :], gains[row + 3 : row + 4, :]
            ).astype(BF16)
            return carry

        lax.fori_loop(0, tokens // step_rows, one, 0)

    norm_rows(embedded, 0, normed)
    need(1)
    for step in list(range(1, narrow)) + [0]:
        owner = lax.rem(me + step, narrow)

        def project(part, carry):
            offset = pl.multiple_of(part * D + owner * head_width, LANES)
            value = matmul(normed[...], weights[1][:, pl.ds(offset, head_width)]).astype(BF16)
            if step:
                away[step - 1, part] = value
            else:
                qkv[me, part] = value
            return carry

        lax.fori_loop(0, 3, project, 0)
        if step:
            start(swap(away.at[step - 1], qkv.at[me], 0, step))
    flush(at.w1)
    at.t1[...] = normed[...].T
    flush(at.t1)
    advance(2)
    for step in range(1, narrow):
        swap(away.at[step - 1], qkv.at[me], 0, step).wait_recv()
    flush(at.qkv)

    lane = lax.broadcasted_iota(jnp.int32, (1, LANES), 1)
    scale = HD ** (-0.5)
    length = narrow * tokens
    for step in list(range(1, narrow)) + [0]:
        who = lax.rem(me + step, narrow)
        log_sums = jnp.zeros((tokens, LANES), F32)
        for pair in range(head_width // LANES):
            lanes = pl.ds(pair * LANES, LANES)
            query = qkv[who, 0, :, lanes].astype(F32)
            key = qkv[:, 1, :, lanes].reshape(length, LANES)
            value = qkv[:, 2, :, lanes].reshape(length, LANES)
            out = jnp.zeros((tokens, LANES), F32)
            for side in range(LANES // HD):
                inside = lane // HD == side
                own_query = (query * jnp.where(inside, scale, 0.0)).astype(BF16)
                scores = back_mul(own_query, key)
                highest = jnp.max(scores, -1, keepdims=True)
                exponentials = jnp.exp(scores - highest)
                summed = jnp.sum(exponentials, -1, keepdims=True)
                part = matmul(exponentials.astype(BF16), value) / summed
                out = jnp.where(inside, part, out)
                log_sums = jnp.where(
                    lane == pair * (LANES // HD) + side, highest + jnp.log(summed), log_sums
                )
            heads_out[who, :, lanes] = out.astype(BF16)
        at.log_sums[who] = log_sums
        if step:
            start(swap(heads_out.at[who], returned.at[me], 1, step))
            if step % 2 == 0:
                advance()
        else:
            returned[me] = heads_out[who]
    flush(at.heads_out)
    flush(at.log_sums)
    need(2)
    for step in range(1, narrow):
        swap(heads_out.at[me], returned.at[me], 1, step).wait_recv()
    for block in range(0, D, 256):
        cols = pl.ds(block, 256)
        value = embedded[:, cols]
        for source in range(narrow):
            value = value + matmul(returned[source], weights[2][pl.ds(source * head_width, head_width), cols])
        mid[:, cols] = value
    flush(at.w2)
    flush(at.mid)
    norm_rows(mid, 1, normed)
    for source in range(narrow):
        at.t2[pl.ds(source * head_width, head_width), :] = returned[source].T
    at.t3[...] = normed[...].T
    flush(at.t2)
    flush(at.t3)

    ff = weights[3].shape[1]
    tile = wave.shape[1]
    slopes = at.slopes
    for block in range(0, ff, tile):
        need(3, (block, block + tile))
        wave[...] = matmul(normed[...], weights[3][:, pl.ds(block, tile)])

        def bend(step, carry):
            rows = pl.ds(pl.multiple_of(step * 16, 16), 16)
            x = wave[rows, :]
            half = 0.5 * (1.0 + lax.erf(x * (0.5**0.5)))
            hidden[rows, pl.ds(block, tile)] = (x * half).astype(BF16)
            bell = jnp.exp(-0.5 * x * x) * 0.3989422804014327
            slopes[rows, pl.ds(block, tile)] = (half + x * bell).astype(BF16)
            return carry

        lax.fori_loop(0, tokens // 16, bend, 0)
        at.t4[pl.ds(block, tile), :] = hidden[:, pl.ds(block, tile)].T
    flush(at.w3)
    flush(at.slopes)
    flush(at.t4)
    for block in range(0, D, 256):
        need(4, (block, block + 256))
        cols = pl.ds(block, 256)
        last[:, cols] = mid[:, cols] + matmul(hidden[...], weights[4][:, cols])
    flush(at.w4)
    flush(at.last)
    norm_rows(last, 2, normed)
    need(5)
    for block in range(0, weights[5].shape[1], 256):
        cols = pl.ds(block, 256)
        at.gaussians[:, cols] = matmul(normed[...], weights[5][:, cols])
    flush(at.w5)
    flush(at.gaussians)
    at.t5[...] = normed[...].T
    flush(at.t5)
    advance(total)
    for copy in started:
        copy.wait_send()
    for copy in flushed:
        copy.wait()


def forward_all(shards, patches, lead, wide, narrow):
    tokens = patches.shape[0]
    widths = [shard.shape[1] for shard in shards]
    heights = [shard.shape[0] * wide * narrow for shard in shards]
    ff = widths[3]
    head_width = D // narrow
    items = forward_plan(widths)
    slots = wide + narrow - 1
    full = [((height, width), BF16) for height, width in zip(heights, widths)]
    shapes = dict(
        w1=full[1],
        w2=full[2],
        w3=full[3],
        w4=full[4],
        w5=full[5],
        gains=((8, D), F32),
        embedded=((tokens, D), F32),
        mid=((tokens, D), F32),
        last=((tokens, D), F32),
        slopes=((tokens, ff), BF16),
        t1=((D, tokens), BF16),
        t2=((D, tokens), BF16),
        t3=((D, tokens), BF16),
        t4=((ff, tokens), BF16),
        t5=((D, tokens), BF16),
        qkv=((narrow, 3, tokens, head_width), BF16),
        heads_out=((narrow, tokens, head_width), BF16),
        log_sums=((narrow, tokens, LANES), F32),
        gaussians=((tokens, widths[5]), F32),
    )
    ins = tuple(dict(s0=0, s1=0, s2=0, s3=0, s4=0, s5=0, patches=0))
    outs = tuple(shapes)
    extras = dict(
        first_weight=pltpu.VMEM((heights[0], widths[0]), BF16),
        normed=pltpu.VMEM((tokens, D), BF16),
        hidden=pltpu.VMEM((tokens, ff), BF16),
        wave=pltpu.VMEM((tokens, 512), F32),
        away=pltpu.VMEM((narrow - 1, 3, tokens, head_width), BF16),
        returned=pltpu.VMEM((narrow, tokens, head_width), BF16),
        own_sem=pltpu.SemaphoreType.DMA((6,)),
        send_sem=pltpu.SemaphoreType.DMA((len(items), slots)),
        recv_sem=pltpu.SemaphoreType.DMA((len(items), slots)),
        swap_send=pltpu.SemaphoreType.DMA((2, narrow)),
        swap_recv=pltpu.SemaphoreType.DMA((2, narrow)),
        out_sem=pltpu.SemaphoreType.DMA((len(outs),)),
    )
    scratch = outs + tuple(extras)
    anywhere = pl.BlockSpec(memory_space=pl.ANY)
    results = pl.pallas_call(
        functools.partial(forward_kernel, items, wide, narrow, lead, ins, outs, scratch),
        out_shape=[jax.ShapeDtypeStruct(*shapes[name]) for name in outs],
        in_specs=[anywhere] * 6 + [pl.BlockSpec(memory_space=pltpu.VMEM)],
        out_specs=[anywhere] * len(outs),
        scratch_shapes=[pltpu.VMEM(*shapes[name]) for name in outs] + list(extras.values()),
        compiler_params=pltpu.CompilerParams(
            collective_id=0, has_side_effects=True, vmem_limit_bytes=60 * MIB
        ),
        name="forward",
    )(*shards, patches)
    return Bag(zip(outs, results))


def backward_plan(widths):
    items = []
    for which, cuts in ((5, 1), (4, 2), (3, 2), (2, 1), (1, 3), (0, 1)):
        size = widths[which] // cuts
        for cut in range(cuts):
            for side, (start, width) in enumerate(column_halves(size)):
                items.append((which, cut * size + start, width, side))
    return items


def tile_of(width):
    for tile in (512, 384, 256, 128):
        if width % tile == 0:
            return tile
    return width


def backward_kernel(items, wide, narrow, lead, ins, scratch, *refs):
    src = Bag(zip(ins, refs))
    refs = refs[len(ins) :]
    sums, totals, refs = refs[:6], refs[6], list(refs[7:])
    at = Bag(zip(scratch, refs))
    place = Place(wide, narrow)
    chips, me = place.chips, place.n
    total = len(items)
    refs = refs[len(scratch) :]
    held = [refs.pop(0) for _ in items]
    passed = [[refs.pop(0) for _ in place.bits] for _ in items]
    final = [refs.pop(0) for _ in items]
    spare = [refs.pop(0) for _ in range(6)]
    tokens = src.patches.shape[0]
    head_width = D // narrow
    length = narrow * tokens
    send_sem, recv_sem, tile_send, tile_recv = at.send_sem, at.recv_sem, at.tile_send, at.tile_recv
    swap_send, swap_recv, in_sem, ring_sem = at.swap_send, at.swap_recv, at.in_sem, at.ring_sem
    gains, norms, extra = src.gains, at.norms, at.extra
    stash, d_res, d_norm = at.stash, at.d_res, at.d_norm
    mixed, merge_low, expand_low, shrink_low = at.mixed, at.merge_low, at.expand_low, at.shrink_low

    loaded = [name for name in ins if name in scratch]

    def load(ref):
        index = [vars(at)[name] is ref for name in loaded].index(True)
        return pltpu.make_async_copy(vars(src)[loaded[index]], ref, in_sem.at[index])

    def load_stash(ref):
        return pltpu.make_async_copy(ref, stash, in_sem.at[len(loaded)])

    def ring(ref, slots, rows, columns, index, row):
        slot = lax.rem(index, 2)
        return pltpu.make_async_copy(
            ref.at[pl.ds(pl.multiple_of(row, rows), rows), :],
            slots.at[slot, pl.ds(0, rows), pl.ds(0, columns)],
            ring_sem.at[0 if slots is at.tall else 1, slot],
        )

    slope_rows = at.tall.shape[1]

    def slope_load(index):
        slot = lax.rem(index, 2)
        return pltpu.make_async_copy(
            src.slopes.at[:, pl.ds(pl.multiple_of(index * slope_rows, slope_rows), slope_rows)],
            at.slope_slots.at[slot],
            ring_sem.at[2, slot],
        )

    u_rows, u_cols = 256, src.w5.shape[1]
    load_stash(src.last).start()
    for index in range(2):
        ring(src.w5, at.tall, u_rows, u_cols, index, index * u_rows).start()
        slope_load(index).start()
        ring(src.w3, at.long, 128, src.w3.shape[1], index, index * 128).start()
    for name in loaded:
        load(vars(at)[name]).start()

    peers = [(lax.rem(place.w + step, wide), place.n) for step in range(1, wide)]
    peers += [place.along(step) for step in range(1, narrow)]
    greet(peers)

    started = []

    def start(copy):
        copy.start()
        started.append(copy)

    lefts = [at.embed_t, at.t1, at.t2, at.t3, at.t4, at.t5]
    rights = [src.patches, mixed, merge_low, expand_low, shrink_low, src.gauss]

    def remote(item, src, dst, slot, peer):
        return pltpu.make_async_remote_copy(
            src_ref=src,
            dst_ref=dst,
            send_sem=send_sem.at[item, slot],
            recv_sem=recv_sem.at[item, slot],
            device_id=peer,
            device_id_type=MESH,
        )

    def bits_of(item):
        return place.bits[::-1] if items[item][3] == 0 else place.bits

    def product(item, mask, core, into, plus):
        which, begin, width, _ = items[item]
        left, right = lefts[which], rights[which]
        rows = into.shape[-2]
        tile = tile_of(width)
        together = max(1, min(narrow, 128 // rows))
        first = ((flip(place.chip, mask) * 2 + core) * narrow) * rows
        with_extra = which == 0 and begin + width == right.shape[1]
        assert not with_extra or tile == width
        part, begin = (begin // D, begin % D) if which == 1 else (None, begin)

        def one(step, carry):
            across, down = step % (width // tile), step // (width // tile)
            offset = pl.multiple_of(begin + across * tile, LANES)
            local = pl.multiple_of(across * tile, LANES)
            ns = pl.ds(down * together, together)
            span = together * rows
            where = pl.ds(pl.multiple_of(first + down * span, span), span)
            if part is None:
                rhs = right[:, pl.ds(offset, tile)]
            else:
                rhs = right[part, :, pl.ds(offset, tile)]
            value = jnp.dot(left[where, :], rhs, preferred_element_type=F32)
            if with_extra:
                more = jnp.concatenate([jnp.zeros((span, tile - LANES), F32), extra[where, :]], 1)
                value = value + more
            value = value.reshape(together, rows, tile)
            if plus:
                value = value + into[mask, ns, :, pl.ds(local, tile)].astype(F32)
            into[mask, ns, :, pl.ds(local, tile)] = value.astype(BF16)
            return carry

        lax.fori_loop(0, (width // tile) * (narrow // together), one, 0)

    last_sent = {}
    pushed = set()

    def to_twin(item, mask):
        which, _, width, _ = items[item]
        own = spare[which].at[mask, :, :, pl.ds(0, width)]
        return remote(item, own, held[item].at[mask], mask, place.twin)

    def push(which, part=None):
        for item, (owner, begin, _, _) in enumerate(items):
            if owner != which or (part is not None and begin // D != part):
                continue
            for mask in range(chips):
                if (which, mask) in last_sent:
                    last_sent[which, mask].wait_send()
                product(item, mask, 1 - place.core, spare[which], False)
                copy = to_twin(item, mask)
                copy.start()
                last_sent[which, mask] = copy
            pushed.add(item)

    def across(item, mask, bit, number, slot):
        return remote(
            item, held[item].at[mask], passed[item][number].at[slot], chips + mask, place.across(bit)
        )

    def along(item, step):
        target = place.along(step)
        return remote(
            item,
            held[item].at[0, target[1]],
            final[item].at[narrow - step - 1],
            2 * chips + narrow - step - 1,
            target,
        )

    def split(item, number):
        bits = bits_of(item)
        keep = list(range(chips))
        for bit in bits[:number]:
            keep = [mask for mask in keep if not mask & bit]
        if number < len(bits):
            return [m for m in keep if m & bits[number]], [m for m in keep if not m & bits[number]]
        return [], keep

    def add_into(dest, dest_at, src, src_at):
        def one(step, carry):
            value = dest[dest_at, step].astype(F32) + src[src_at, step].astype(F32)
            dest[dest_at, step] = value.astype(BF16)
            return carry

        lax.fori_loop(0, narrow, one, 0)

    def stage(item, number):
        assert item in pushed
        bits = bits_of(item)
        if number == 0:

            def ready(mask):
                to_twin(item, mask).wait_recv()
                product(item, mask, place.core, held[item], True)

        else:
            bit = bits[number - 1]
            _, kept = split(item, number - 1)

            def ready(mask):
                slot = kept.index(mask)
                across(item, mask ^ bit, bit, number - 1, slot).wait_recv()
                add_into(held[item], mask, passed[item][number - 1], slot)

        away, keep = split(item, number)
        if number < len(bits):
            for mask in away:
                ready(mask)
                start(across(item, mask, bits[number], number, keep.index(mask ^ bits[number])))
            for mask in keep:
                ready(mask)
        else:
            ready(0)
            for step in range(1, narrow):
                start(along(item, step))

    squares = []

    def finish(item):
        which, begin, width, _ = items[item]
        value = held[item][0, me].astype(F32)
        for step in range(1, narrow):
            along(item, step).wait_recv()
        for slot in range(narrow - 1):
            value = value + final[item][slot].astype(F32)
        sums[which][:, pl.ds(begin, width)] = value
        squares.append(jnp.sum(value * value))

    progress = [0] * (total // 2)
    depth = len(place.bits) + 1

    def advance(steps=1):
        for _ in range(steps):
            entered = False
            for pair in range(total // 2):
                number = progress[pair]
                if number > depth or (number == 0 and (entered or 2 * pair not in pushed)):
                    continue
                entered = entered or number == 0
                progress[pair] = number + 1
                for item in (2 * pair, 2 * pair + 1):
                    if number < depth:
                        stage(item, number)
                    else:
                        finish(item)

    norms[...] = jnp.zeros_like(norms)

    def norm_back(row, low, add):
        step_rows = 64

        def one(step, carry):
            rows = pl.ds(pl.multiple_of(step * step_rows, step_rows), step_rows)
            values = stash[rows, :]
            upper = d_norm[rows, :]
            centred = values - jnp.mean(values, -1, keepdims=True)
            rate = lax.rsqrt(jnp.mean(centred * centred, -1, keepdims=True) + 1e-05)
            unit = centred * rate
            norms[row : row + 1, :] += jnp.sum(upper * unit, 0, keepdims=True)
            norms[row + 3 : row + 4, :] += jnp.sum(upper, 0, keepdims=True)
            scaled = upper * gains[row : row + 1, :]
            inner = scaled - jnp.mean(scaled, -1, keepdims=True)
            inner = rate * (inner - unit * jnp.mean(scaled * unit, -1, keepdims=True))
            if add:
                inner = inner + d_res[rows, :]
            d_res[rows, :] = inner
            low[rows, :] = inner.astype(BF16)
            return carry

        lax.fori_loop(0, tokens // step_rows, one, 0)

    load(at.t5).wait()
    push(5)
    load_stash(src.last).wait()
    count = D // u_rows
    tall_rows = slope_rows

    def through_unpatch(index, carry):
        ring(src.w5, at.tall, u_rows, u_cols, index, index * u_rows).wait()
        slot = at.tall.at[lax.rem(index, 2)]
        offset = pl.multiple_of(index * u_rows, u_rows)
        d_norm[:, pl.ds(offset, u_rows)] = back_mul(src.gauss[...], slot[0:u_rows, 0:u_cols])

        @pl.when(index + 2 < count)
        def _():
            ring(src.w5, at.tall, u_rows, u_cols, index + 2, (index + 2) * u_rows).start()

        return carry

    lax.fori_loop(0, count, through_unpatch, 0)
    for index in range(2):
        ring(src.w4, at.tall, tall_rows, D, index, index * tall_rows).start()
    norm_back(2, shrink_low, False)
    load_stash(src.mid).start()
    load(at.t4).wait()
    push(4)
    advance()
    ff = src.w3.shape[1]
    slabs = ff // tall_rows

    def through_shrink(index, carry):
        ring(src.w4, at.tall, tall_rows, D, index, index * tall_rows).wait()
        slope_load(index).wait()
        slot = lax.rem(index, 2)
        value = back_mul(shrink_low[...], at.tall[slot])
        value = value * at.slope_slots[slot].astype(F32)
        expand_low[:, pl.ds(pl.multiple_of(index * tall_rows, tall_rows), tall_rows)] = value.astype(BF16)

        @pl.when(index + 2 < slabs)
        def _():
            ring(src.w4, at.tall, tall_rows, D, index + 2, (index + 2) * tall_rows).start()
            slope_load(index + 2).start()

        return carry

    lax.fori_loop(0, slabs, through_shrink, 0)
    owners = [lax.rem(me + step, narrow) for step in list(range(1, narrow)) + [0]]
    for index in range(2):
        ring(src.w2, at.tall, head_width, D, index, owners[index] * head_width).start()
    load(at.t3).wait()
    push(3)
    advance()

    def through_expand(index, carry):
        ring(src.w3, at.long, 128, ff, index, index * 128).wait()
        offset = pl.multiple_of(index * 128, 128)
        d_norm[:, pl.ds(offset, 128)] = back_mul(expand_low[...], at.long[lax.rem(index, 2)])

        @pl.when(index + 2 < D // 128)
        def _():
            ring(src.w3, at.long, 128, ff, index + 2, (index + 2) * 128).start()

        return carry

    lax.fori_loop(0, D // 128, through_expand, 0)
    for index in range(2):
        ring(src.w1, at.long, 128, 3 * D, index, index * 128).start()
    load_stash(src.mid).wait()
    norm_back(1, merge_low, True)
    load_stash(src.embedded).start()

    def swap(src, dst, kind, step):
        return pltpu.make_async_remote_copy(
            src_ref=src,
            dst_ref=dst,
            send_sem=swap_send.at[kind, step],
            recv_sem=swap_recv.at[kind, step],
            device_id=place.along(step),
            device_id_type=MESH,
        )

    d_heads, away = at.d_heads, at.away
    for index, owner in enumerate(owners):
        ring(src.w2, at.tall, head_width, D, index, owner * head_width).wait()
        value = back_mul(merge_low[...], at.tall[index % 2, 0:head_width, :]).astype(BF16)
        if index < narrow - 1:
            away[index] = value
            start(swap(away.at[index], d_heads.at[me], 0, index + 1))
        else:
            d_heads[me] = value
        if index + 2 < narrow:
            ring(src.w2, at.tall, head_width, D, index + 2, owners[index + 2] * head_width).start()
    load(at.t2).wait()
    push(2)
    advance()
    load(at.qkv).wait()
    load(at.heads_out).wait()
    load(at.log_sums).wait()
    for step in range(1, narrow):
        swap(away.at[step - 1], d_heads.at[me], 0, step).wait_recv()

    qkv, heads_out, log_sums, parts = at.qkv, at.heads_out, at.log_sums, at.parts
    key_t, key_acc, value_acc, query_acc = at.key_t, at.key_acc, at.value_acc, at.query_acc
    lane = lax.broadcasted_iota(jnp.int32, (1, LANES), 1)
    line = lax.broadcasted_iota(jnp.int32, (LANES, 1), 0)
    sides = LANES // HD
    scale = HD ** (-0.5)
    choose = lax.broadcasted_iota(jnp.int32, (8, LANES), 1) // HD
    choose = (choose == lax.broadcasted_iota(jnp.int32, (8, LANES), 0)).astype(F32)

    def part_swap(pair, step):
        lanes = pl.ds(pair * LANES, LANES)
        who = lax.rem(me + step, narrow)
        return swap(
            parts.at[who, :, :, lanes],
            mixed.at[:, :, pl.ds(pl.multiple_of(me * head_width + pair * LANES, LANES), LANES)],
            1 + pair,
            step,
        )

    for pair in range(head_width // LANES):
        lanes = pl.ds(pair * LANES, LANES)
        key_t[...] = qkv[:, 1, :, lanes].reshape(length, LANES).T
        key_acc[...] = jnp.zeros_like(key_acc)
        value_acc[...] = jnp.zeros_like(value_acc)
        for step in range(narrow):
            who = lax.rem(me + step, narrow)
            query = qkv[who, 0, :, lanes].astype(F32)
            upper = d_heads[who, :, lanes].astype(F32)
            kept = heads_out[who, :, lanes].astype(F32)
            delta = lax.dot_general(
                choose,
                upper * kept,
                (((1,), (1,)), ((), ())),
                precision=HIGHEST,
                preferred_element_type=F32,
            )
            log_rows = log_sums[who].T[pair * sides : (pair + 1) * sides, :]
            own_query = [(query * jnp.where(lane // HD == side, scale, 0.0)).astype(BF16) for side in range(sides)]
            own_upper = [(upper * jnp.where(lane // HD == side, 1.0, 0.0)).astype(BF16) for side in range(sides)]
            query_acc[...] = jnp.zeros_like(query_acc)

            def block(source, carry):
                rows = pl.ds(pl.multiple_of(source * tokens, tokens), tokens)
                key, value = qkv[source, 1, :, lanes], qkv[source, 2, :, lanes]
                key_turned = key_t[:, rows].astype(F32)
                for side in range(sides):
                    scores = back_mul(key, own_query[side])
                    probs = jnp.exp(scores - log_rows[side : side + 1, :])
                    d_probs = back_mul(value, own_upper[side])
                    d_scores = (probs * (d_probs - delta[side : side + 1, :])).astype(BF16)
                    value_acc[rows, :] += matmul(probs.astype(BF16), own_upper[side])
                    key_acc[rows, :] += matmul(d_scores, own_query[side])
                    turned = (key_turned * jnp.where(line // HD == side, scale, 0.0)).astype(BF16)
                    query_acc[...] += matmul(turned, d_scores)
                return carry

            lax.fori_loop(0, narrow, block, 0)
            parts[who, 0, :, lanes] = query_acc[...].T.astype(BF16)
            if step % 2 == 1:
                advance()
        for source in range(narrow):
            rows = pl.ds(source * tokens, tokens)
            parts[source, 1, :, lanes] = key_acc[rows, :].astype(BF16)
            parts[source, 2, :, lanes] = value_acc[rows, :].astype(BF16)
        for step in range(1, narrow):
            start(part_swap(pair, step))
        mixed[:, :, pl.ds(pl.multiple_of(me * head_width + pair * LANES, LANES), LANES)] = parts[me, :, :, lanes]
    load(at.t1).wait()
    for pair in range(head_width // LANES):
        for step in range(1, narrow):
            part_swap(pair, step).wait_recv()
    for part in range(3):
        push(1, part)
        advance()

    def through_mixer(index, carry):
        ring(src.w1, at.long, 128, 3 * D, index, index * 128).wait()
        slot = lax.rem(index, 2)
        value = back_mul(mixed[0], at.long[slot, :, 0:D])
        for part in range(1, 3):
            value = value + back_mul(mixed[part], at.long[slot, :, part * D : (part + 1) * D])
        d_norm[:, pl.ds(pl.multiple_of(index * 128, 128), 128)] = value

        @pl.when(index + 2 < D // 128)
        def _():
            ring(src.w1, at.long, 128, 3 * D, index + 2, (index + 2) * 128).start()

        return carry

    lax.fori_loop(0, D // 128, through_mixer, 0)
    load_stash(src.embedded).wait()
    norm_back(0, at.embed_low, True)
    at.embed_t[...] = at.embed_low[...].T
    turned = jnp.concatenate([norms[...], jnp.zeros((LANES - 8, D), F32)], 0).T
    at.extra[...] = pltpu.roll(turned, lead, 1)
    push(0)
    advance(total)
    assert min(progress) > depth

    rows = lax.broadcasted_iota(jnp.int32, (8, LANES), 0)
    wide_tiles, narrow_tiles = at.wide_tiles, at.narrow_tiles
    wide_tiles[place.w] = jnp.where(rows == 0, src.term[...], sum(squares))

    def tile_copy(buffer, index, slot, peer):
        return pltpu.make_async_remote_copy(
            src_ref=buffer.at[index],
            dst_ref=buffer.at[index],
            send_sem=tile_send.at[slot],
            recv_sem=tile_recv.at[slot],
            device_id=peer,
            device_id_type=MESH,
        )

    for step in range(1, wide):
        start(tile_copy(wide_tiles, place.w, step - 1, (lax.rem(place.w + step, wide), place.n)))
    for step in range(1, wide):
        tile_copy(wide_tiles, place.w, step - 1, (lax.rem(place.w + step, wide), place.n)).wait_recv()
    whole = wide_tiles[0]
    for index in range(1, wide):
        whole = whole + wide_tiles[index]
    narrow_tiles[place.n] = whole
    for step in range(1, narrow):
        start(tile_copy(narrow_tiles, place.n, wide + step - 1, place.along(step)))
    for step in range(1, narrow):
        tile_copy(narrow_tiles, place.n, wide + step - 1, place.along(step)).wait_recv()
    whole = narrow_tiles[0]
    for index in range(1, narrow):
        whole = whole + narrow_tiles[index]
    totals[...] = whole
    for copy in list(last_sent.values()) + started:
        copy.wait_send()


def backward_all(kept, patches, gauss, term, lead, wide, narrow):
    tokens = patches.shape[0]
    chips = wide // 2
    weights = [kept.w1, kept.w2, kept.w3, kept.w4, kept.w5]
    heights = [D] + [weight.shape[0] for weight in weights]
    widths = [patches.shape[1]] + [weight.shape[1] for weight in weights]
    rows = [height // (wide * narrow) for height in heights]
    head_width = D // narrow
    length = narrow * tokens
    items = backward_plan(widths)
    slots = 2 * chips + narrow - 1
    streamed = dict(w1=kept.w1, w2=kept.w2, w3=kept.w3, w4=kept.w4, w5=kept.w5)
    streamed.update(last=kept.last, mid=kept.mid, embedded=kept.embedded, slopes=kept.slopes)
    loaded = dict(t5=kept.t5, t4=kept.t4, t3=kept.t3, t2=kept.t2, t1=kept.t1)
    loaded.update(qkv=kept.qkv, heads_out=kept.heads_out, log_sums=kept.log_sums)
    whole = dict(gains=kept.gains, patches=patches, gauss=gauss, term=term)
    operands = {**streamed, **loaded, **whole}
    shapes = [jax.ShapeDtypeStruct((rows[which], widths[which]), F32) for which in range(6)]
    shapes.append(jax.ShapeDtypeStruct((8, LANES), F32))
    scratch = {name: pltpu.VMEM(value.shape, value.dtype) for name, value in loaded.items()}
    scratch.update(
        embed_t=pltpu.VMEM((D, tokens), BF16),
        embed_low=pltpu.VMEM((tokens, D), BF16),
        stash=pltpu.VMEM((tokens, D), F32),
        d_res=pltpu.VMEM((tokens, D), F32),
        d_norm=pltpu.VMEM((tokens, D), F32),
        norms=pltpu.VMEM((8, D), F32),
        extra=pltpu.VMEM((D, LANES), F32),
        shrink_low=pltpu.VMEM((tokens, D), BF16),
        expand_low=pltpu.VMEM((tokens, widths[3]), BF16),
        merge_low=pltpu.VMEM((tokens, D), BF16),
        mixed=pltpu.VMEM((3, tokens, D), BF16),
        tall=pltpu.VMEM((2, 512, D), BF16),
        long=pltpu.VMEM((2, 128, widths[3]), BF16),
        slope_slots=pltpu.VMEM((2, tokens, 512), BF16),
        d_heads=pltpu.VMEM((narrow, tokens, head_width), BF16),
        away=pltpu.VMEM((narrow - 1, tokens, head_width), BF16),
        parts=pltpu.VMEM((narrow, 3, tokens, head_width), BF16),
        key_t=pltpu.VMEM((LANES, length), BF16),
        key_acc=pltpu.VMEM((length, LANES), F32),
        value_acc=pltpu.VMEM((length, LANES), F32),
        query_acc=pltpu.VMEM((LANES, tokens), F32),
        wide_tiles=pltpu.VMEM((wide, 8, LANES), F32),
        narrow_tiles=pltpu.VMEM((narrow, 8, LANES), F32),
        send_sem=pltpu.SemaphoreType.DMA((len(items), slots)),
        recv_sem=pltpu.SemaphoreType.DMA((len(items), slots)),
        tile_send=pltpu.SemaphoreType.DMA((wide + narrow,)),
        tile_recv=pltpu.SemaphoreType.DMA((wide + narrow,)),
        swap_send=pltpu.SemaphoreType.DMA((1 + head_width // LANES, narrow)),
        swap_recv=pltpu.SemaphoreType.DMA((1 + head_width // LANES, narrow)),
        in_sem=pltpu.SemaphoreType.DMA((9,)),
        ring_sem=pltpu.SemaphoreType.DMA((3, 2)),
    )
    lists = [pltpu.VMEM((chips, narrow, rows[which], width), BF16) for which, _, width, _ in items]
    for which, _, width, _ in items:
        for bit in chip_bits(chips):
            lists.append(pltpu.VMEM((chips // (2 * bit), narrow, rows[which], width), BF16))
    lists += [pltpu.VMEM((narrow - 1, rows[which], width), BF16) for which, _, width, _ in items]
    for which in range(6):
        widest = max(width for owner, _, width, _ in items if owner == which)
        lists.append(pltpu.VMEM((chips, narrow, rows[which], widest), BF16))
    vmem = pl.BlockSpec(memory_space=pltpu.VMEM)
    hbm = pl.BlockSpec(memory_space=pl.ANY)
    return pl.pallas_call(
        functools.partial(backward_kernel, items, wide, narrow, lead, tuple(operands), tuple(scratch)),
        out_shape=shapes,
        in_specs=[vmem if name in whole else hbm for name in operands],
        out_specs=[vmem] * len(shapes),
        scratch_shapes=list(scratch.values()) + lists,
        compiler_params=pltpu.CompilerParams(
            collective_id=1, has_side_effects=True, vmem_limit_bytes=63 * MIB
        ),
        name="backward",
    )(*operands.values())


def render_kernel(
    gauss_ref, weight_ref, target_ref, mask_ref, pair_ref, view_ref, total_ref, grad_ref, term_ref, feat, dfeat
):
    quads = gauss_ref.shape[0] // NVIEW
    span = weight_ref.shape[1]
    pairs = pair_ref.shape[1]
    scale = 1.0 / total_ref[0].astype(F32)

    def channel(index):
        return gauss_ref[:, index * PP : (index + 1) * PP]

    def shared():
        opacity = jax.nn.sigmoid(channel(3))
        extent = jax.nn.sigmoid(channel(5) + channel(6) + channel(7))
        lead = channel(8)
        denom = 1.0 + lead * lead + channel(9) * channel(9) + channel(10) * channel(10) + channel(11) * channel(11)
        facing = lead * lead / denom
        raw = channel(4)
        depth = jnp.maximum(raw, 0.0) + jnp.log1p(jnp.exp(-jnp.abs(raw)))
        return opacity, extent, lead, denom, facing, raw, depth

    opacity, extent, lead, denom, facing, raw, depth = shared()
    footprint = opacity * extent * facing
    channels = [jax.nn.sigmoid(channel(index)) * footprint for index in range(3)]
    channels += [footprint, depth * footprint]
    for index, value in enumerate(channels):
        for view in range(NVIEW):
            feat[index * quads : (index + 1) * quads, view * PP : (view + 1) * PP] = value[
                view * quads : (view + 1) * quads
            ]
    rendered = jnp.dot(feat[...], weight_ref[...], precision=HIGHEST, preferred_element_type=F32)
    parts = [rendered[index * quads : (index + 1) * quads] for index in range(5)]
    lane = lax.broadcasted_iota(jnp.int32, (quads, span), 1)
    live = jnp.where(lane < view_ref[0] * PP, mask_ref[...], 0).astype(F32)
    term = jnp.zeros((quads, span), F32)
    slopes = []
    for index in range(3):
        error = parts[index] - target_ref[index * quads : (index + 1) * quads, :].astype(F32)
        term = term + live * error * error
        slopes.append(2.0 * scale * live * error)
    below = 1.0 + parts[3]
    depth_out = parts[4] / below

    first, second = pair_ref[0:1, :], pair_ref[1:2, :]
    least = jnp.minimum(first, second)
    down = (jnp.abs(first - second) == P_SIZE).astype(jnp.int32)
    place = quads * PP
    slot, local = least // place, least % place
    high = down * quads + local // PP
    low = slot * PP + local % PP
    high_hot = (lax.broadcasted_iota(jnp.int32, (2 * quads, pairs), 0) == high).astype(F32).astype(BF16)
    low_hot = (lax.broadcasted_iota(jnp.int32, (span, pairs), 0) == low).astype(F32).astype(BF16)
    counts = back_mul(high_hot, low_hot)
    slope = jnp.zeros((quads, span), F32)
    for which, shift in enumerate((1, P_SIZE)):
        count = counts[which * quads : (which + 1) * quads]
        weight = DEPTH_WEIGHT * count * live * pltpu.roll(live, span - shift, 1)
        gap = depth_out - pltpu.roll(depth_out, span - shift, 1)
        term = term + weight * gap * gap
        pull = 2.0 * scale * weight * gap
        slope = slope + pull - pltpu.roll(pull, shift, 1)
    term_ref[...] = jnp.full(term_ref.shape, jnp.sum(term), F32)
    over = slope / below
    slopes += [-over * depth_out, over]
    stacked = jnp.concatenate(slopes, 0)
    dfeat[...] = lax.dot_general(
        stacked, weight_ref[...], (((1,), (1,)), ((), ())), precision=HIGHEST, preferred_element_type=F32
    )

    def feature_grad(index):
        return jnp.concatenate(
            [
                dfeat[index * quads : (index + 1) * quads, view * PP : (view + 1) * PP]
                for view in range(NVIEW)
            ],
            0,
        )

    def put(index, value):
        grad_ref[:, index * PP : (index + 1) * PP] = value.astype(BF16)

    d_foot = feature_grad(3)
    for index in range(3):
        tint = jax.nn.sigmoid(channel(index))
        upper = feature_grad(index)
        d_foot = d_foot + upper * tint
        put(index, upper * footprint * tint * (1.0 - tint))
    d_last = feature_grad(4)
    d_foot = d_foot + d_last * depth
    put(3, d_foot * extent * facing * opacity * (1.0 - opacity))
    put(4, d_last * footprint * jax.nn.sigmoid(raw))
    d_extent = d_foot * opacity * facing * extent * (1.0 - extent)
    for index in (5, 6, 7):
        put(index, d_extent)
    d_facing = d_foot * opacity * extent
    put(8, d_facing * 2.0 * lead / denom * (1.0 - facing))
    for index in (9, 10, 11):
        put(index, -2.0 * d_facing * facing / denom * channel(index))


def render(gaussians, weights, targets, mask, pairs, view_count, pair_total):
    rows = gaussians.shape[0]
    quads = rows // NVIEW
    slots, views = weights.shape[:2]
    spread = weights.transpose(1, 2, 0, 3).reshape(views * PP, slots * PP)
    wanted = targets.reshape(slots, 3, quads, PP).transpose(1, 2, 0, 3).reshape(3 * quads, slots * PP)
    valid = mask.reshape(slots, quads, PP).transpose(1, 0, 2).reshape(quads, slots * PP)
    vmem = pl.BlockSpec(memory_space=pltpu.VMEM)
    smem = pl.BlockSpec(memory_space=pltpu.SMEM)
    return pl.pallas_call(
        render_kernel,
        out_shape=[
            jax.ShapeDtypeStruct(gaussians.shape, BF16),
            jax.ShapeDtypeStruct((8, LANES), F32),
        ],
        in_specs=[vmem] * 5 + [smem] * 2,
        out_specs=[vmem] * 2,
        scratch_shapes=[pltpu.VMEM((5 * quads, views * PP), F32)] * 2,
        compiler_params=pltpu.CompilerParams(vmem_limit_bytes=48 * MIB),
        name="render",
    )(gaussians, spread, wanted, valid, pairs, view_count, pair_total)


def forward_plain(shards, patches, features, kinds):
    weights = [lax.all_gather(shard, BOTH, axis=0, tiled=True) for shard in shards]
    groups = lax.axis_size(NARROW)
    rows = patches.shape[0]
    gains = weights[0][:, features : features + kinds].T.astype(F32)
    embedded = back_mul(patches[:, :features], weights[0][:, :features])
    normed_one = layer_norm(embedded, gains[0], gains[3]).astype(BF16)
    mixed = matmul(normed_one, weights[1]).astype(BF16).reshape(rows, 3, groups, -1)
    mixed = mixed.transpose(2, 1, 0, 3)
    qkv = lax.all_to_all(mixed, NARROW, split_axis=0, concat_axis=0, tiled=True)
    width = qkv.shape[-1]
    length = groups * rows
    heads = width // HD
    parts = [qkv[:, part].reshape(length, heads, HD) for part in range(3)]
    attended, logsum = attention_forward(*parts)
    log_sums = logsum.transpose(0, 2, 1).reshape(groups, rows, heads)
    returned = lax.all_to_all(
        attended.reshape(groups, rows, width), NARROW, split_axis=0, concat_axis=0, tiled=True
    )
    returned = returned.transpose(1, 0, 2).reshape(rows, D)
    mid = embedded + matmul(returned, weights[2])
    normed_two = layer_norm(mid, gains[1], gains[4]).astype(BF16)
    expanded = matmul(normed_two, weights[3])
    half = 0.5 * (1.0 + lax.erf(expanded * (0.5**0.5)))
    activated = (expanded * half).astype(BF16)
    bell = jnp.exp(-0.5 * expanded * expanded) * 0.3989422804014327
    slopes = (half + expanded * bell).astype(BF16)
    last = mid + matmul(activated, weights[4])
    normed_three = layer_norm(last, gains[2], gains[5]).astype(BF16)
    return Bag(
        dict(
        w1=weights[1],
        w2=weights[2],
        w3=weights[3],
        w4=weights[4],
        w5=weights[5],
        gains=gains,
        embedded=embedded,
        mid=mid,
        last=last,
        slopes=slopes,
        t1=normed_one.T,
        t2=returned.T,
        t3=normed_two.T,
        t4=activated.T,
        t5=normed_three.T,
        qkv=qkv,
        heads_out=attended,
        log_sums=log_sums,
        gaussians=matmul(normed_three, weights[5]),
    ).items())


def backward_plain(kept, patches, gauss_low, term, features, kinds):
    gains = kept.gains
    weights = [None, kept.w1, kept.w2, kept.w3, kept.w4, kept.w5]
    norm_back_one = jax.vjp(layer_norm, kept.embedded, gains[0], gains[3])[1]
    norm_back_two = jax.vjp(layer_norm, kept.mid, gains[1], gains[4])[1]
    norm_back_three = jax.vjp(layer_norm, kept.last, gains[2], gains[5])[1]
    qkv = kept.qkv
    groups, _, rows, width = qkv.shape
    length = groups * rows
    heads = width // HD
    queries, keys, values = (qkv[:, part].reshape(length, heads, HD) for part in range(3))
    blocked = min(512, length)
    logsum = kept.log_sums[:, :, :heads].reshape(length // blocked, blocked, heads)
    residual_grad, gain_three, shift_three = norm_back_three(back_mul(gauss_low, weights[5]))
    shrink_low = residual_grad.astype(BF16)
    expand_low = (back_mul(shrink_low, weights[4]) * kept.slopes.astype(F32)).astype(BF16)
    through_two, gain_two, shift_two = norm_back_two(back_mul(expand_low, weights[3]))
    residual_grad = residual_grad + through_two
    merge_low = residual_grad.astype(BF16)
    out_grad = back_mul(merge_low, weights[2]).astype(BF16).reshape(rows, groups, width)
    head_grad = lax.all_to_all(
        out_grad.transpose(1, 0, 2), NARROW, split_axis=0, concat_axis=0, tiled=True
    ).reshape(length, heads, HD)
    grads = attention_backward(queries, keys, values, logsum.transpose(0, 2, 1), head_grad)
    stacked = jnp.stack(grads, 1).astype(BF16).reshape(groups, rows, 3, width)
    mixed_grad = lax.all_to_all(stacked, NARROW, split_axis=0, concat_axis=0, tiled=True)
    mixed_grad = mixed_grad.transpose(1, 2, 0, 3).reshape(rows, 3 * D)
    through_one, gain_one, shift_one = norm_back_one(back_mul(mixed_grad, weights[1]))
    embed_grad = (residual_grad + through_one).astype(BF16)
    grad_norms = jnp.stack([gain_one, gain_two, gain_three, shift_one, shift_two, shift_three])
    lefts = [embed_grad.T] + [kept.t1, kept.t2, kept.t3, kept.t4, kept.t5]
    rights = [patches, mixed_grad, merge_low, expand_low, shrink_low, gauss_low]
    products = [matmul(left, right) for left, right in zip(lefts, rights)]
    products[0] = products[0].at[:, features : features + kinds].add(grad_norms.T)
    sums = [
        lax.psum_scatter(
            product.astype(BF16), BOTH, scatter_dimension=0, tiled=True
        ).astype(F32)
        for product in products
    ]
    squares = sum(jnp.sum(part * part) for part in sums)
    loss_sum, square_sum = lax.psum((term[0, 0], squares), BOTH)
    return sums, loss_sum, square_sum


def body(
    views,
    render_w,
    targets,
    pix_mask,
    pairs,
    view_count,
    pair_total,
    embed_weight,
    embed_first,
    embed_second,
    mixer_weight,
    mixer_first,
    mixer_second,
    merge_weight,
    merge_first,
    merge_second,
    expand_weight,
    expand_first,
    expand_second,
    shrink_weight,
    shrink_first,
    shrink_second,
    unpatch_weight,
    unpatch_first,
    unpatch_second,
    norm_params,
    norm_first,
    norm_second,
):
    masters = (embed_weight, mixer_weight, merge_weight, expand_weight, shrink_weight, unpatch_weight, norm_params)
    firsts = (embed_first, mixer_first, merge_first, expand_first, shrink_first, unpatch_first, norm_first)
    seconds = (embed_second, mixer_second, merge_second, expand_second, shrink_second, unpatch_second, norm_second)
    groups = lax.axis_size(NARROW)
    wide_count = lax.axis_size(WIDE)
    features = embed_weight.shape[0]
    kinds = norm_params.shape[0]
    padded = -(-(features + kinds) // LANES) * LANES
    fill = padded - features - kinds
    by_kernel = mixer_weight.shape[0] % 16 == 0

    first_shard = jnp.concatenate([embed_weight.T, norm_params.T], 1)
    first_shard = jnp.pad(first_shard.astype(BF16), ((0, 0), (0, fill)))
    shards = [first_shard] + [weight.astype(BF16) for weight in masters[1:6]]
    patches = views.reshape(-1, features)
    rows = patches.shape[0]
    patches = jnp.pad(patches, ((0, 0), (0, padded - features)))
    if by_kernel:
        kept = forward_all(shards, patches, features % LANES, wide_count, groups)
    else:
        kept = forward_plain(shards, patches, features, kinds)
    divisor = pair_total[0].astype(F32)
    gauss_low, term = render(
        kept.gaussians, render_w[0], targets[0], pix_mask[0], pairs[0], view_count, pair_total
    )
    if by_kernel:
        *sums, totals = backward_all(
            kept, patches, gauss_low, term, features % LANES, wide_count, groups
        )
        loss_sum, square_sum = totals[0, 0], totals[1, 0]
    else:
        sums, loss_sum, square_sum = backward_plain(kept, patches, gauss_low, term, features, kinds)
    first_sum = sums[0].T
    grads = [first_sum[:features]] + list(sums[1:]) + [first_sum[features : features + kinds]]
    loss = loss_sum / divisor
    grad_norm = jnp.sqrt(square_sum)
    factor = jnp.minimum(1.0, CLIP_NORM / (grad_norm + 1e-06))
    results = []
    for which in range(7):
        results += adamw(masters[which], firsts[which], seconds[which], grads[which] * factor, RATES[which])
    return tuple(results) + (loss, grad_norm)


def solution(mesh):
    columns = P(None, BOTH)
    rows = P(BOTH, None)
    weights = (columns,) * 3 + (rows,) * 15 + (columns,) * 3
    return jax.shard_map(
        body,
        mesh=mesh,
        in_specs=(
            P(WIDE, None, NARROW, None),
            P(WIDE, None, None, None, None),
            P(WIDE, None, None, NARROW),
            P(WIDE, None, NARROW),
            P(WIDE, None, NARROW),
            P(WIDE),
            P(),
        )
        + weights,
        out_specs=weights + (P(), P()),
        check_vma=False,
    )
```

```python
import functools
import heapq

import jax
import jax.numpy as jnp
from jax import lax
from jax.experimental import pallas as pl
from jax.experimental.pallas import tpu as pltpu
from jax.sharding import PartitionSpec as P

D = 1024
HD = 64
P_SIZE = 8
PP = 64
NVIEW = 4
TMAX = 12
STEP = 10
LANES = 128
MIB = 1024 * 1024

DEPTH_WEIGHT = 1.0
CLIP_NORM = 0.01
BETA_ONE = 0.9
BETA_TWO = 0.95
ADAM_EPS = 1e-08
DECAY = 0.05
RATES = (0.05, 0.05, 0.5, 0.05, 0.05, 0.05, 0.8)
MESH = pl.DeviceIdType.MESH
WIDE, NARROW = BOTH = ("wide", "narrow")
HIGHEST = lax.Precision.HIGHEST
F32 = jnp.float32
BF16 = jnp.bfloat16


def matmul(left, right):
    return jnp.dot(left, right, preferred_element_type=F32)


def outer_sum(left, right):
    return lax.dot_general(left, right, (((0,), (0,)), ((), ())), preferred_element_type=F32)


def back_mul(grad, weight):
    return lax.dot_general(grad, weight, (((1,), (1,)), ((), ())), preferred_element_type=F32)


def layer_norm(values, gain, shift):
    centred = values - jnp.mean(values, -1, keepdims=True)
    spread = jnp.mean(centred * centred, -1, keepdims=True)
    return centred * lax.rsqrt(spread + 1e-05) * gain + shift


def exact_gelu(values):
    return jax.nn.gelu(values, approximate=False)


def attention_forward(queries, keys, values):
    length, heads = (queries.shape[0], queries.shape[1])
    blocked = min(512, length)
    scale = HD ** (-0.5)

    def one_block(query_block):
        scores = (
            jnp.einsum("qhd,khd->hqk", query_block, keys, preferred_element_type=jnp.float32)
            * scale
        )
        highest = jnp.max(scores, -1, keepdims=True)
        exponentials = jnp.exp(scores - highest)
        summed = jnp.sum(exponentials, -1, keepdims=True)
        softmaxed = (exponentials / summed).astype(jnp.bfloat16)
        output = jnp.einsum("hqk,khd->qhd", softmaxed, values, preferred_element_type=jnp.float32)
        return (output.astype(jnp.bfloat16), (highest + jnp.log(summed))[:, :, 0])

    output, logsum = lax.map(one_block, queries.reshape(length // blocked, blocked, heads, HD))
    return (output.reshape(length, heads * HD), logsum)


def attention_backward(queries, keys, values, logsum, out_grad):
    length, heads = (queries.shape[0], queries.shape[1])
    blocked = min(512, length)
    scale = HD ** (-0.5)

    def one_block(carry, inputs):
        key_grad, value_grad = carry
        query_block, logsum_block, grad_block = inputs
        scores = (
            jnp.einsum("qhd,khd->hqk", query_block, keys, preferred_element_type=jnp.float32)
            * scale
        )
        softmaxed = jnp.exp(scores - logsum_block[:, :, None])
        value_grad = value_grad + jnp.einsum(
            "hqk,qhd->khd",
            softmaxed.astype(jnp.bfloat16),
            grad_block,
            preferred_element_type=jnp.float32,
        )
        prob_grad = jnp.einsum(
            "qhd,khd->hqk", grad_block, values, preferred_element_type=jnp.float32
        )
        score_grad = softmaxed * (prob_grad - jnp.sum(softmaxed * prob_grad, -1, keepdims=True))
        score_low = score_grad.astype(jnp.bfloat16)
        query_grad = (
            jnp.einsum("hqk,khd->qhd", score_low, keys, preferred_element_type=jnp.float32) * scale
        )
        key_grad = (
            key_grad
            + jnp.einsum("hqk,qhd->khd", score_low, query_block, preferred_element_type=jnp.float32)
            * scale
        )
        return ((key_grad, value_grad), query_grad)

    zeros = jnp.zeros((length, heads, HD), jnp.float32)
    shaped = (
        queries.reshape(length // blocked, blocked, heads, HD),
        logsum,
        out_grad.reshape(length // blocked, blocked, heads, HD),
    )
    (key_grad, value_grad), query_grad = lax.scan(one_block, (zeros, zeros), shaped)
    return (query_grad.reshape(length, heads, HD), key_grad, value_grad)


def adamw(weight, first, second, grad, rate):
    first = BETA_ONE * first + (1.0 - BETA_ONE) * grad
    second = BETA_TWO * second + (1.0 - BETA_TWO) * grad * grad
    first_hat = first / (1.0 - BETA_ONE**STEP)
    second_hat = second / (1.0 - BETA_TWO**STEP)
    weight = weight - rate * (first_hat / (jnp.sqrt(second_hat) + ADAM_EPS) + DECAY * weight)
    return (weight, first, second)


def chip_bits(chips):
    bits, step = [], 1
    while step < chips:
        bits.append(step)
        step *= 2
    return bits


def flip(chip, mask):
    for bit in chip_bits(mask + 1):
        if mask & bit:
            chip = chip + (1 - 2 * (chip // bit % 2)) * bit
    return chip


def column_halves(width):
    first = -(-width // (2 * LANES)) * LANES
    return ((0, first), (first, width - first))


def work_items(widths, order):
    return [(which,) + half + (side,) for which in order for side, half in enumerate(column_halves(widths[which]))]


class Bag:
    def __init__(self, pairs):
        vars(self).update(pairs)


class Place:
    def __init__(self, wide, narrow):
        self.wide, self.narrow = wide, narrow
        self.chips = wide // 2
        self.bits = chip_bits(self.chips)
        self.w = lax.axis_index(WIDE)
        self.n = lax.axis_index(NARROW)
        self.chip = self.w // 2
        self.core = self.w % 2
        self.twin = (2 * self.chip + 1 - self.core, self.n)

    def across(self, mask):
        return (2 * flip(self.chip, mask) + self.core, self.n)

    def along(self, step):
        return (self.w, lax.rem(self.n + step, self.narrow))

    def neighbours(self):
        return (
            [self.twin]
            + [self.across(bit) for bit in self.bits]
            + [self.along(step) for step in range(1, self.narrow)]
        )


class Planner:
    def __init__(self):
        self.now, self.count = 0.0, 0
        self.free, self.events, self.done, self.spare = {}, [], set(), []

    def transfer(self, link, cost, key, event):
        self.free[link] = max(self.now, self.free.get(link, 0.0)) + cost
        self.count += 1
        heapq.heappush(self.events, (self.free[link] + 2.0, self.count, key, event))

    def step(self):
        when, _, key, event = heapq.heappop(self.events)
        self.now = max(self.now, when) + 0.2
        event()
        self.done.add(key)

    def fill(self, until):
        for index, (keys, cost, work) in enumerate(self.spare):
            if self.now + cost <= until and self.done.issuperset(keys):
                del self.spare[index]
                work()
                self.now += cost
                return True
        return False

    def need(self, keys):
        while not self.done.issuperset(keys):
            if not self.fill(self.events[0][0]):
                self.step()

    def work(self, cost, work):
        while self.events and self.events[0][0] <= self.now:
            self.step()
        work()
        self.now += cost

    def later(self, cost, work, keys=()):
        entry = (tuple(keys), cost, work)
        self.spare.append(entry)
        return entry

    def force(self, entry):
        if entry in self.spare:
            self.spare.remove(entry)
            self.work(entry[1], entry[2])

    def finish(self):
        while self.events or self.spare:
            if not self.fill(self.events[0][0] if self.events else 1e9):
                self.step()


LINK = 100e3
TWIN_LINK = 600e3


def greet(peers):
    barrier = pltpu.get_barrier_semaphore()
    for peer in peers:
        pl.semaphore_signal(barrier, inc=1, device_id=peer, device_id_type=MESH)
    pl.semaphore_wait(barrier, len(peers))


def normalize(values, gain, shift):
    centred = values - jnp.mean(values, -1, keepdims=True)
    spread = jnp.mean(centred * centred, -1, keepdims=True)
    return centred * lax.rsqrt(spread + 1e-05) * gain + shift


def forward_plan(widths):
    items = []
    for which, cuts in ((0, 1), (1, 3), (2, 1), (3, 2), (5, 1), (4, 2)):
        size = widths[which] // cuts
        for cut in range(cuts):
            for side, (start, width) in enumerate(column_halves(size)):
                items.append((which, cut * size + start, width, side))
    return items


def forward_kernel(items, wide, narrow, lead, ins, outs, scratch, *refs):
    at = Bag(zip(ins + scratch, refs[: len(ins)] + refs[len(ins) + len(outs) :]))
    results = refs[len(ins) : len(ins) + len(outs)]
    weights = [at.first_weight, at.w1, at.w2, at.w3, at.w4, at.w5]
    shards = [at.s0, at.s1, at.s2, at.s3, at.s4, at.s5]
    own_sem, send_sem, recv_sem = at.own_sem, at.send_sem, at.recv_sem
    swap_send, swap_recv, out_sem = at.swap_send, at.swap_recv, at.out_sem
    place = Place(wide, narrow)
    chips, me = place.chips, place.n
    tokens = at.patches.shape[0]
    head_width = D // narrow
    total = len(items)
    started = []

    def start(copy):
        copy.start()
        started.append(copy)

    greet(place.neighbours())
    rows_of = [shard.shape[0] for shard in shards]

    def rows_at(which, chip, core, node=None):
        rows = rows_of[which]
        if node is None:
            return pl.ds(pl.multiple_of((chip * 2 + core) * narrow * rows, rows), narrow * rows)
        return pl.ds(pl.multiple_of(((chip * 2 + core) * narrow + node) * rows, rows), rows)

    own = []
    for which in range(6):
        copy = pltpu.make_async_copy(
            shards[which], weights[which].at[rows_at(which, place.chip, place.core, me), :], own_sem.at[which]
        )
        copy.start()
        own.append(copy)

    def remote(item, src, dst, slot, peer):
        return pltpu.make_async_remote_copy(
            src_ref=src,
            dst_ref=dst,
            send_sem=send_sem.at[item, slot],
            recv_sem=recv_sem.at[item, slot],
            device_id=peer,
            device_id_type=MESH,
        )

    def group(item, mask):
        which, begin, width, _ = items[item]
        return weights[which].at[rows_at(which, flip(place.chip, mask), place.core), pl.ds(begin, width)]

    def along(item, step):
        which, begin, width, _ = items[item]
        return remote(
            item,
            shards[which].at[:, pl.ds(begin, width)],
            weights[which].at[rows_at(which, place.chip, place.core, me), pl.ds(begin, width)],
            2 * chips + step - 1,
            place.along(step),
        )

    def bits_of(item):
        return place.bits if items[item][3] == 0 else place.bits[::-1]

    def across(item, mask, bit):
        return remote(item, group(item, mask), group(item, mask), mask ^ bit, place.across(bit))

    def to_twin(item, mask):
        return remote(item, group(item, mask), group(item, mask), chips + mask, place.twin)

    plan = Planner()
    waited = set()
    halves = (narrow // 2) * (narrow - narrow // 2)

    def block_bytes(item):
        which, _, width, _ = items[item]
        return 2 * narrow * rows_of[which] * width

    def twin_event(item, mask):
        return lambda: to_twin(item, mask).wait_recv()

    def onward(item, mask, number):
        bits = bits_of(item)
        size = block_bytes(item)
        for later in range(number, len(bits)):
            start(across(item, mask, bits[later]))
            coming = mask ^ bits[later]
            plan.transfer(
                bits[later], 2 * size / LINK, (item, coming), functools.partial(arrive, item, coming, later)
            )
        start(to_twin(item, mask))
        plan.transfer(-1, size / TWIN_LINK, (item, chips + mask), twin_event(item, mask))

    def arrive(item, mask, number):
        across(item, mask ^ bits_of(item)[number], bits_of(item)[number]).wait_recv()
        onward(item, mask, number + 1)

    def begin_item(item):
        if item >= total:
            return
        for step in range(1, narrow):
            start(along(item, step))
        cost = halves * 2 * block_bytes(item) / narrow / LINK
        plan.transfer(0, cost, (item, 0), functools.partial(line_event, item))

    def line_event(item):
        if items[item][0] not in waited:
            waited.add(items[item][0])
            own[items[item][0]].wait()
        for step in range(1, narrow):
            along(item, step).wait_recv()
        begin_item(item + ahead)
        onward(item, 0, 0)

    ahead = 6
    for item in range(min(ahead, total)):
        begin_item(item)

    def need(which, columns=None):
        plan.need(
            [
                (index, key)
                for index, (owner, begin, width, _) in enumerate(items)
                if owner == which and (columns is None or (begin < columns[1] and begin + width > columns[0]))
                for key in range(2 * chips)
            ]
        )

    flushed = []

    def flush(ref):
        index = [vars(at)[name] is ref for name in outs].index(True)
        copy = pltpu.make_async_copy(ref, results[index], out_sem.at[index])
        copy.start()
        flushed.append(copy)

    def swap(src, dst, kind, step):
        return pltpu.make_async_remote_copy(
            src_ref=src,
            dst_ref=dst,
            send_sem=swap_send.at[kind, step],
            recv_sem=swap_recv.at[kind, step],
            device_id=place.along(step),
            device_id_type=MESH,
        )

    gains = at.gains
    embedded, mid, last = at.embedded, at.mid, at.last
    normed, hidden, wave = at.normed, at.hidden, at.wave
    away, qkv, heads_out, returned = at.away, at.qkv, at.heads_out, at.returned

    def turn(dest, source):
        dest[...] = source[...].T
        flush(dest)

    need(0)
    width = weights[0].shape[1]
    kind = lax.broadcasted_iota(jnp.int32, (8, LANES), 0)
    spot = lax.broadcasted_iota(jnp.int32, (8, LANES), 1)
    pick = (spot == kind + lead).astype(F32).astype(BF16)
    gains[...] = back_mul(pick, weights[0][:, width - LANES :])
    flush(gains)

    def embed(block):
        cols = pl.ds(block, 256)
        embedded[:, cols] = back_mul(at.patches[...], weights[0][pl.ds(block, 256), : at.patches.shape[1]])

    for block in range(0, D, 256):
        plan.work(0.5, functools.partial(embed, block))
    flush(embedded)

    def norm_rows(source, row, dest):
        step_rows = 64

        def one(step, carry):
            rows = pl.ds(pl.multiple_of(step * step_rows, step_rows), step_rows)
            dest[rows, :] = normalize(
                source[rows, :], gains[row : row + 1, :], gains[row + 3 : row + 4, :]
            ).astype(BF16)
            return carry

        lax.fori_loop(0, tokens // step_rows, one, 0)

    plan.work(2.0, lambda: norm_rows(embedded, 0, normed))
    turn_first = plan.later(2.0, lambda: turn(at.t1, normed))
    piece = 2 * halves * 2 * tokens * head_width / LINK

    def project(part, step):
        owner = lax.rem(me + step, narrow)
        offset = pl.multiple_of(part * D + owner * head_width, LANES)
        value = matmul(normed[...], weights[1][:, pl.ds(offset, head_width)]).astype(BF16)
        if step:
            away[step - 1, part] = value
            start(swap(away.at[step - 1, part], qkv.at[me, part], part, step))
        else:
            qkv[me, part] = value

    def swap_event(part):
        for step in range(1, narrow):
            swap(away.at[step - 1, part], qkv.at[me, part], part, step).wait_recv()

    for part in range(3):
        need(1, (part * D, part * D + D))
        for step in list(range(1, narrow)) + [0]:
            plan.work(0.7, functools.partial(project, part, step))
        plan.transfer(0, piece, (-1, part), functools.partial(swap_event, part))
    flush(at.w1)
    plan.need([(-1, part) for part in range(3)])
    flush(qkv)
    plan.need([(-1, 2)])

    lane = lax.broadcasted_iota(jnp.int32, (1, LANES), 1)
    scale = HD ** (-0.5)
    length = narrow * tokens

    def attend(step):
        who = lax.rem(me + step, narrow)
        log_sums = jnp.zeros((tokens, LANES), F32)
        for pair in range(head_width // LANES):
            lanes = pl.ds(pair * LANES, LANES)
            query = qkv[who, 0, :, lanes].astype(F32)
            key = qkv[:, 1, :, lanes].reshape(length, LANES)
            value = qkv[:, 2, :, lanes].reshape(length, LANES)
            out = jnp.zeros((tokens, LANES), F32)
            for side in range(LANES // HD):
                inside = lane // HD == side
                own_query = (query * jnp.where(inside, scale, 0.0)).astype(BF16)
                scores = back_mul(own_query, key)
                highest = jnp.max(scores, -1, keepdims=True)
                exponentials = jnp.exp(scores - highest)
                summed = jnp.sum(exponentials, -1, keepdims=True)
                part = matmul(exponentials.astype(BF16), value) / summed
                out = jnp.where(inside, part, out)
                log_sums = jnp.where(
                    lane == pair * (LANES // HD) + side, highest + jnp.log(summed), log_sums
                )
            heads_out[who, :, lanes] = out.astype(BF16)
        at.log_sums[who] = log_sums
        if step:
            start(swap(heads_out.at[who], returned.at[me], 3, step))
        else:
            returned[me] = heads_out[who]

    def return_event(step):
        return lambda: swap(heads_out.at[me], returned.at[me], 3, step).wait_recv()

    for step in list(range(1, narrow)) + [0]:
        plan.work(3.5, functools.partial(attend, step))
        if step:
            plan.transfer(0, piece / (narrow - 1), (-2, step), return_event(step))
    flush(heads_out)
    flush(at.log_sums)
    need(2)
    plan.need([(-2, step) for step in range(1, narrow)])

    def merge(block):
        cols = pl.ds(block, 256)
        value = embedded[:, cols]
        for source in range(narrow):
            value = value + matmul(returned[source], weights[2][pl.ds(source * head_width, head_width), cols])
        mid[:, cols] = value

    for block in range(0, D, 256):
        plan.work(0.7, functools.partial(merge, block))
    flush(at.w2)
    flush(mid)
    plan.force(turn_first)
    plan.work(2.0, lambda: norm_rows(mid, 1, normed))

    def turn_returned():
        for source in range(narrow):
            at.t2[pl.ds(source * head_width, head_width), :] = returned[source].T
        flush(at.t2)

    plan.later(2.0, turn_returned)
    turn_second = plan.later(2.0, lambda: turn(at.t3, normed))

    ff = weights[3].shape[1]
    tile = wave.shape[1]
    slopes = at.slopes

    def expand(block):
        wave[...] = matmul(normed[...], weights[3][:, pl.ds(block, tile)])

        def bend(step, carry):
            rows = pl.ds(pl.multiple_of(step * 32, 32), 32)
            x = wave[rows, :]
            half = 0.5 * (1.0 + lax.erf(x * (0.5**0.5)))
            hidden[rows, pl.ds(block, tile)] = (x * half).astype(BF16)
            bell = jnp.exp(-0.5 * x * x) * 0.3989422804014327
            slopes[rows, pl.ds(block, tile)] = (half + x * bell).astype(BF16)
            return carry

        lax.fori_loop(0, tokens // 32, bend, 0)

    def turn_hidden(block):
        at.t4[pl.ds(block, tile), :] = hidden[:, pl.ds(block, tile)].T

    for block in range(0, ff, tile):
        need(3, (block, block + tile))
        plan.work(2.5, functools.partial(expand, block))
        plan.later(1.0, functools.partial(turn_hidden, block))
    flush(at.w3)
    flush(slopes)

    def shrink(block):
        cols = pl.ds(block, 256)
        last[:, cols] = mid[:, cols] + matmul(hidden[...], weights[4][:, cols])

    for block in range(0, D, 256):
        need(4, (block, block + 256))
        plan.work(1.0, functools.partial(shrink, block))
    flush(at.w4)
    flush(last)
    plan.force(turn_second)
    plan.work(2.0, lambda: norm_rows(last, 2, normed))
    need(5)

    def unpatch(block):
        cols = pl.ds(block, 256)
        at.gaussians[:, cols] = matmul(normed[...], weights[5][:, cols])

    for block in range(0, weights[5].shape[1], 256):
        plan.work(0.7, functools.partial(unpatch, block))
    flush(at.w5)
    flush(at.gaussians)
    plan.later(2.0, lambda: turn(at.t5, normed))
    plan.finish()
    flush(at.t4)
    for copy in started:
        copy.wait_send()
    for copy in flushed:
        copy.wait()


def forward_all(shards, patches, lead, wide, narrow):
    tokens = patches.shape[0]
    widths = [shard.shape[1] for shard in shards]
    heights = [shard.shape[0] * wide * narrow for shard in shards]
    ff = widths[3]
    head_width = D // narrow
    items = forward_plan(widths)
    slots = wide + narrow - 1
    full = [((height, width), BF16) for height, width in zip(heights, widths)]
    shapes = dict(
        w1=full[1],
        w2=full[2],
        w3=full[3],
        w4=full[4],
        w5=full[5],
        gains=((8, D), F32),
        embedded=((tokens, D), F32),
        mid=((tokens, D), F32),
        last=((tokens, D), F32),
        slopes=((tokens, ff), BF16),
        t1=((D, tokens), BF16),
        t2=((D, tokens), BF16),
        t3=((D, tokens), BF16),
        t4=((ff, tokens), BF16),
        t5=((D, tokens), BF16),
        qkv=((narrow, 3, tokens, head_width), BF16),
        heads_out=((narrow, tokens, head_width), BF16),
        log_sums=((narrow, tokens, LANES), F32),
        gaussians=((tokens, widths[5]), F32),
    )
    ins = tuple(dict(s0=0, s1=0, s2=0, s3=0, s4=0, s5=0, patches=0))
    outs = tuple(shapes)
    extras = dict(
        first_weight=pltpu.VMEM((heights[0], widths[0]), BF16),
        normed=pltpu.VMEM((tokens, D), BF16),
        hidden=pltpu.VMEM((tokens, ff), BF16),
        wave=pltpu.VMEM((tokens, 512), F32),
        away=pltpu.VMEM((narrow - 1, 3, tokens, head_width), BF16),
        returned=pltpu.VMEM((narrow, tokens, head_width), BF16),
        own_sem=pltpu.SemaphoreType.DMA((6,)),
        send_sem=pltpu.SemaphoreType.DMA((len(items), slots)),
        recv_sem=pltpu.SemaphoreType.DMA((len(items), slots)),
        swap_send=pltpu.SemaphoreType.DMA((4, narrow)),
        swap_recv=pltpu.SemaphoreType.DMA((4, narrow)),
        out_sem=pltpu.SemaphoreType.DMA((len(outs),)),
    )
    scratch = outs + tuple(extras)
    anywhere = pl.BlockSpec(memory_space=pl.ANY)
    results = pl.pallas_call(
        functools.partial(forward_kernel, items, wide, narrow, lead, ins, outs, scratch),
        out_shape=[jax.ShapeDtypeStruct(*shapes[name]) for name in outs],
        in_specs=[anywhere] * 6 + [pl.BlockSpec(memory_space=pltpu.VMEM)],
        out_specs=[anywhere] * len(outs),
        scratch_shapes=[pltpu.VMEM(*shapes[name]) for name in outs] + list(extras.values()),
        compiler_params=pltpu.CompilerParams(
            collective_id=0, has_side_effects=True, vmem_limit_bytes=60 * MIB
        ),
        name="forward",
    )(*shards, patches)
    return Bag(zip(outs, results))


def backward_plan(widths):
    items = []
    for which, cuts in ((5, 1), (4, 2), (3, 2), (2, 1), (1, 3), (0, 1)):
        size = widths[which] // cuts
        for cut in range(cuts):
            for side, (start, width) in enumerate(column_halves(size)):
                items.append((which, cut * size + start, width, side))
    return items


def tile_of(width):
    for tile in (512, 384, 256, 128):
        if width % tile == 0:
            return tile
    return width


def backward_kernel(items, wide, narrow, lead, ins, scratch, *refs):
    src = Bag(zip(ins, refs))
    refs = refs[len(ins) :]
    sums, totals, refs = refs[:6], refs[6], list(refs[7:])
    at = Bag(zip(scratch, refs))
    place = Place(wide, narrow)
    chips, me = place.chips, place.n
    total = len(items)
    refs = refs[len(scratch) :]
    held = [refs.pop(0) for _ in items]
    passed = [[refs.pop(0) for _ in place.bits] for _ in items]
    final = [refs.pop(0) for _ in items]
    spare = [refs.pop(0) for _ in range(6)]
    tokens = src.patches.shape[0]
    head_width = D // narrow
    length = narrow * tokens
    send_sem, recv_sem, tile_send, tile_recv = at.send_sem, at.recv_sem, at.tile_send, at.tile_recv
    swap_send, swap_recv, in_sem, ring_sem = at.swap_send, at.swap_recv, at.in_sem, at.ring_sem
    gains, norms, extra = src.gains, at.norms, at.extra
    stash, d_res, d_norm = at.stash, at.d_res, at.d_norm
    mixed, merge_low, expand_low, shrink_low = at.mixed, at.merge_low, at.expand_low, at.shrink_low

    loaded = [name for name in ins if name in scratch]

    def load(ref):
        index = [vars(at)[name] is ref for name in loaded].index(True)
        return pltpu.make_async_copy(vars(src)[loaded[index]], ref, in_sem.at[index])

    def load_stash(ref):
        return pltpu.make_async_copy(ref, stash, in_sem.at[len(loaded)])

    def ring(ref, slots, rows, columns, index, row):
        slot = lax.rem(index, 2)
        return pltpu.make_async_copy(
            ref.at[pl.ds(pl.multiple_of(row, rows), rows), :],
            slots.at[slot, pl.ds(0, rows), pl.ds(0, columns)],
            ring_sem.at[0 if slots is at.tall else 1, slot],
        )

    slope_rows = at.tall.shape[1]

    def slope_load(index):
        slot = lax.rem(index, 2)
        return pltpu.make_async_copy(
            src.slopes.at[:, pl.ds(pl.multiple_of(index * slope_rows, slope_rows), slope_rows)],
            at.slope_slots.at[slot],
            ring_sem.at[2, slot],
        )

    u_rows, u_cols = 256, src.w5.shape[1]
    load_stash(src.last).start()
    for index in range(2):
        ring(src.w5, at.tall, u_rows, u_cols, index, index * u_rows).start()
        slope_load(index).start()
        ring(src.w3, at.long, 128, src.w3.shape[1], index, index * 128).start()
    for name in loaded:
        load(vars(at)[name]).start()

    peers = [(lax.rem(place.w + step, wide), place.n) for step in range(1, wide)]
    peers += [place.along(step) for step in range(1, narrow)]
    greet(peers)

    started = []

    def start(copy):
        copy.start()
        started.append(copy)

    lefts = [at.embed_t, at.t1, at.t2, at.t3, at.t4, at.t5]
    rights = [src.patches, mixed, merge_low, expand_low, shrink_low, src.gauss]

    def remote(item, src, dst, slot, peer):
        return pltpu.make_async_remote_copy(
            src_ref=src,
            dst_ref=dst,
            send_sem=send_sem.at[item, slot],
            recv_sem=recv_sem.at[item, slot],
            device_id=peer,
            device_id_type=MESH,
        )

    def bits_of(item):
        return place.bits[::-1] if items[item][3] == 0 else place.bits

    def product(item, mask, core, into, plus):
        which, begin, width, _ = items[item]
        left, right = lefts[which], rights[which]
        rows = into.shape[-2]
        tile = tile_of(width)
        together = max(1, min(narrow, 128 // rows))
        first = ((flip(place.chip, mask) * 2 + core) * narrow) * rows
        with_extra = which == 0 and begin + width == right.shape[1]
        assert not with_extra or tile == width
        part, begin = (begin // D, begin % D) if which == 1 else (None, begin)

        def one(step, carry):
            across, down = step % (width // tile), step // (width // tile)
            offset = pl.multiple_of(begin + across * tile, LANES)
            local = pl.multiple_of(across * tile, LANES)
            ns = pl.ds(down * together, together)
            span = together * rows
            where = pl.ds(pl.multiple_of(first + down * span, span), span)
            if part is None:
                rhs = right[:, pl.ds(offset, tile)]
            else:
                rhs = right[part, :, pl.ds(offset, tile)]
            value = jnp.dot(left[where, :], rhs, preferred_element_type=F32)
            if with_extra:
                more = jnp.concatenate([jnp.zeros((span, tile - LANES), F32), extra[where, :]], 1)
                value = value + more
            value = value.reshape(together, rows, tile)
            if plus:
                value = value + into[mask, ns, :, pl.ds(local, tile)].astype(F32)
            into[mask, ns, :, pl.ds(local, tile)] = value.astype(BF16)
            return carry

        lax.fori_loop(0, (width // tile) * (narrow // together), one, 0)

    last_sent = {}
    plan = Planner()
    halves = (narrow // 2) * (narrow - narrow // 2)

    def to_twin(item, mask):
        which, _, width, _ = items[item]
        own = spare[which].at[mask, :, :, pl.ds(0, width)]
        return remote(item, own, held[item].at[mask], mask, place.twin)

    def across(item, mask, bit, number, slot):
        return remote(
            item, held[item].at[mask], passed[item][number].at[slot], chips + mask, place.across(bit)
        )

    def along(item, step):
        target = place.along(step)
        return remote(
            item,
            held[item].at[0, target[1]],
            final[item].at[narrow - step - 1],
            2 * chips + narrow - step - 1,
            target,
        )

    def leaves(item, mask):
        bits = bits_of(item)
        return min([number for number, bit in enumerate(bits) if mask & bit], default=len(bits))

    def slot_of(item, mask, number):
        bits = bits_of(item)
        kept = [m for m in range(chips) if not any(m & bit for bit in bits[: number + 1])]
        return kept.index(mask)

    def add_into(dest, dest_at, src, src_at):
        def one(step, carry):
            value = dest[dest_at, step].astype(F32) + src[src_at, step].astype(F32)
            dest[dest_at, step] = value.astype(BF16)
            return carry

        lax.fori_loop(0, narrow, one, 0)

    def block_bytes(item):
        which, _, width, _ = items[item]
        return 2 * spare[which].shape[1] * spare[which].shape[2] * width

    def push(which, part=None):
        for item, (owner, begin, _, _) in enumerate(items):
            if owner != which or (part is not None and begin // D != part):
                continue
            for mask in sorted(range(chips), key=lambda mask: leaves(item, mask)):
                plan.work(block_bytes(item) / 4e5, functools.partial(push_one, item, mask))

    def push_one(item, mask):
        which = items[item][0]
        if (which, mask) in last_sent:
            last_sent[which, mask].wait_send()
        product(item, mask, 1 - place.core, spare[which], False)
        copy = to_twin(item, mask)
        copy.start()
        last_sent[which, mask] = copy
        plan.transfer(-1, block_bytes(item) / TWIN_LINK, (item, 0, mask), functools.partial(own_event, item, mask))

    def own_event(item, mask):
        to_twin(item, mask).wait_recv()
        product(item, mask, place.core, held[item], True)
        plan.now += block_bytes(item) / 4e5
        onward(item, mask, 0)

    def onward(item, mask, number):
        bits = bits_of(item)
        if number == len(bits):
            for step in range(1, narrow):
                start(along(item, step))
            cost = halves * 2 * block_bytes(item) / narrow / LINK
            plan.transfer(0, cost, (item, -1, 0), functools.partial(finish, item))
        elif leaves(item, mask) == number:
            kept = mask ^ bits[number]
            start(across(item, mask, bits[number], number, slot_of(item, kept, number)))
            plan.transfer(
                bits[number],
                2 * block_bytes(item) / LINK,
                (item, 1 + number, kept),
                functools.partial(sum_event, item, kept, number),
            )

    def sum_event(item, mask, number):
        plan.need([(item, before, mask) for before in range(number + 1)])
        bit = bits_of(item)[number]
        slot = slot_of(item, mask, number)
        across(item, mask ^ bit, bit, number, slot).wait_recv()
        add_into(held[item], mask, passed[item][number], slot)
        plan.now += block_bytes(item) / 8e5
        onward(item, mask, number + 1)

    squares = []

    def finish(item):
        which, begin, width, _ = items[item]
        value = held[item][0, me].astype(F32)
        for step in range(1, narrow):
            along(item, step).wait_recv()
        for slot in range(narrow - 1):
            value = value + final[item][slot].astype(F32)
        sums[which][:, pl.ds(begin, width)] = value
        squares.append(jnp.sum(value * value))

    norms[...] = jnp.zeros_like(norms)

    def norm_back(row, low, add):
        step_rows = 64

        def one(step, carry):
            rows = pl.ds(pl.multiple_of(step * step_rows, step_rows), step_rows)
            values = stash[rows, :]
            upper = d_norm[rows, :]
            centred = values - jnp.mean(values, -1, keepdims=True)
            rate = lax.rsqrt(jnp.mean(centred * centred, -1, keepdims=True) + 1e-05)
            unit = centred * rate
            norms[row : row + 1, :] += jnp.sum(upper * unit, 0, keepdims=True)
            norms[row + 3 : row + 4, :] += jnp.sum(upper, 0, keepdims=True)
            scaled = upper * gains[row : row + 1, :]
            inner = scaled - jnp.mean(scaled, -1, keepdims=True)
            inner = rate * (inner - unit * jnp.mean(scaled * unit, -1, keepdims=True))
            if add:
                inner = inner + d_res[rows, :]
            d_res[rows, :] = inner
            low[rows, :] = inner.astype(BF16)
            return carry

        lax.fori_loop(0, tokens // step_rows, one, 0)

    load(at.t5).wait()
    push(5)
    plan.now += 3.0
    load_stash(src.last).wait()
    count = D // u_rows
    tall_rows = slope_rows

    def through_unpatch(index, carry):
        ring(src.w5, at.tall, u_rows, u_cols, index, index * u_rows).wait()
        slot = at.tall.at[lax.rem(index, 2)]
        offset = pl.multiple_of(index * u_rows, u_rows)
        d_norm[:, pl.ds(offset, u_rows)] = back_mul(src.gauss[...], slot[0:u_rows, 0:u_cols])

        @pl.when(index + 2 < count)
        def _():
            ring(src.w5, at.tall, u_rows, u_cols, index + 2, (index + 2) * u_rows).start()

        return carry

    lax.fori_loop(0, count, through_unpatch, 0)
    for index in range(2):
        ring(src.w4, at.tall, tall_rows, D, index, index * tall_rows).start()
    norm_back(2, shrink_low, False)
    load_stash(src.mid).start()
    load(at.t4).wait()
    plan.now += 3.0
    push(4)
    ff = src.w3.shape[1]
    slabs = ff // tall_rows

    def through_shrink(index, carry):
        ring(src.w4, at.tall, tall_rows, D, index, index * tall_rows).wait()
        slope_load(index).wait()
        slot = lax.rem(index, 2)
        value = back_mul(shrink_low[...], at.tall[slot])
        value = value * at.slope_slots[slot].astype(F32)
        expand_low[:, pl.ds(pl.multiple_of(index * tall_rows, tall_rows), tall_rows)] = value.astype(BF16)

        @pl.when(index + 2 < slabs)
        def _():
            ring(src.w4, at.tall, tall_rows, D, index + 2, (index + 2) * tall_rows).start()
            slope_load(index + 2).start()

        return carry

    lax.fori_loop(0, slabs, through_shrink, 0)
    owners = [lax.rem(me + step, narrow) for step in list(range(1, narrow)) + [0]]
    for index in range(2):
        ring(src.w2, at.tall, head_width, D, index, owners[index] * head_width).start()
    load(at.t3).wait()
    plan.now += 6.0
    push(3)

    def through_expand(index, carry):
        ring(src.w3, at.long, 128, ff, index, index * 128).wait()
        offset = pl.multiple_of(index * 128, 128)
        d_norm[:, pl.ds(offset, 128)] = back_mul(expand_low[...], at.long[lax.rem(index, 2)])

        @pl.when(index + 2 < D // 128)
        def _():
            ring(src.w3, at.long, 128, ff, index + 2, (index + 2) * 128).start()

        return carry

    lax.fori_loop(0, D // 128, through_expand, 0)
    for index in range(2):
        ring(src.w1, at.long, 128, 3 * D, index, index * 128).start()
    load_stash(src.mid).wait()
    norm_back(1, merge_low, True)
    load_stash(src.embedded).start()

    def swap(src, dst, kind, step):
        return pltpu.make_async_remote_copy(
            src_ref=src,
            dst_ref=dst,
            send_sem=swap_send.at[kind, step],
            recv_sem=swap_recv.at[kind, step],
            device_id=place.along(step),
            device_id_type=MESH,
        )

    d_heads, away = at.d_heads, at.away
    plan.now += 7.0
    piece = 2 * halves * 2 * tokens * head_width / LINK

    def head_event():
        for step in range(1, narrow):
            swap(away.at[step - 1], d_heads.at[me], 0, step).wait_recv()

    for index, owner in enumerate(owners):
        ring(src.w2, at.tall, head_width, D, index, owner * head_width).wait()
        value = back_mul(merge_low[...], at.tall[index % 2, 0:head_width, :]).astype(BF16)
        if index < narrow - 1:
            away[index] = value
            start(swap(away.at[index], d_heads.at[me], 0, index + 1))
        else:
            d_heads[me] = value
        if index + 2 < narrow:
            ring(src.w2, at.tall, head_width, D, index + 2, owners[index + 2] * head_width).start()
    plan.now += 3.0
    plan.transfer(0, piece, (-1, 0, 0), head_event)
    load(at.t2).wait()
    push(2)
    load(at.qkv).wait()
    load(at.heads_out).wait()
    load(at.log_sums).wait()
    plan.need([(-1, 0, 0)])

    qkv, heads_out, log_sums, parts = at.qkv, at.heads_out, at.log_sums, at.parts
    key_t, key_acc, value_acc, query_acc = at.key_t, at.key_acc, at.value_acc, at.query_acc
    lane = lax.broadcasted_iota(jnp.int32, (1, LANES), 1)
    line = lax.broadcasted_iota(jnp.int32, (LANES, 1), 0)
    sides = LANES // HD
    scale = HD ** (-0.5)
    choose = lax.broadcasted_iota(jnp.int32, (8, LANES), 1) // HD
    choose = (choose == lax.broadcasted_iota(jnp.int32, (8, LANES), 0)).astype(F32)

    def part_swap(pair, step):
        lanes = pl.ds(pair * LANES, LANES)
        who = lax.rem(me + step, narrow)
        return swap(
            parts.at[who, :, :, lanes],
            mixed.at[:, :, pl.ds(pl.multiple_of(me * head_width + pair * LANES, LANES), LANES)],
            1 + pair,
            step,
        )

    def part_event(pair):
        for step in range(1, narrow):
            part_swap(pair, step).wait_recv()

    for pair in range(head_width // LANES):
        lanes = pl.ds(pair * LANES, LANES)
        key_t[...] = qkv[:, 1, :, lanes].reshape(length, LANES).T
        key_acc[...] = jnp.zeros_like(key_acc)
        value_acc[...] = jnp.zeros_like(value_acc)
        def one_block(step, lanes=lanes, pair=pair):
            who = lax.rem(me + step, narrow)
            query = qkv[who, 0, :, lanes].astype(F32)
            upper = d_heads[who, :, lanes].astype(F32)
            kept = heads_out[who, :, lanes].astype(F32)
            delta = lax.dot_general(
                choose,
                upper * kept,
                (((1,), (1,)), ((), ())),
                precision=HIGHEST,
                preferred_element_type=F32,
            )
            log_rows = log_sums[who].T[pair * sides : (pair + 1) * sides, :]
            own_query = [(query * jnp.where(lane // HD == side, scale, 0.0)).astype(BF16) for side in range(sides)]
            own_upper = [(upper * jnp.where(lane // HD == side, 1.0, 0.0)).astype(BF16) for side in range(sides)]
            query_acc[...] = jnp.zeros_like(query_acc)

            def block(source, carry):
                rows = pl.ds(pl.multiple_of(source * tokens, tokens), tokens)
                key, value = qkv[source, 1, :, lanes], qkv[source, 2, :, lanes]
                key_turned = key_t[:, rows].astype(F32)
                for side in range(sides):
                    scores = back_mul(key, own_query[side])
                    probs = jnp.exp(scores - log_rows[side : side + 1, :])
                    d_probs = back_mul(value, own_upper[side])
                    d_scores = (probs * (d_probs - delta[side : side + 1, :])).astype(BF16)
                    value_acc[rows, :] += matmul(probs.astype(BF16), own_upper[side])
                    key_acc[rows, :] += matmul(d_scores, own_query[side])
                    turned = (key_turned * jnp.where(line // HD == side, scale, 0.0)).astype(BF16)
                    query_acc[...] += matmul(turned, d_scores)
                return carry

            lax.fori_loop(0, narrow, block, 0)
            parts[who, 0, :, lanes] = query_acc[...].T.astype(BF16)
        for step in range(narrow):
            plan.work(3.0, functools.partial(one_block, step))
        for source in range(narrow):
            rows = pl.ds(source * tokens, tokens)
            parts[source, 1, :, lanes] = key_acc[rows, :].astype(BF16)
            parts[source, 2, :, lanes] = value_acc[rows, :].astype(BF16)
        for step in range(1, narrow):
            start(part_swap(pair, step))
        plan.now += 1.0
        plan.transfer(0, 1.5 * piece, (-2, 0, pair), functools.partial(part_event, pair))
        mixed[:, :, pl.ds(pl.multiple_of(me * head_width + pair * LANES, LANES), LANES)] = parts[me, :, :, lanes]
    load(at.t1).wait()
    plan.need([(-2, 0, pair) for pair in range(head_width // LANES)])
    for part in range(3):
        push(1, part)

    def through_mixer(index, carry):
        ring(src.w1, at.long, 128, 3 * D, index, index * 128).wait()
        slot = lax.rem(index, 2)
        value = back_mul(mixed[0], at.long[slot, :, 0:D])
        for part in range(1, 3):
            value = value + back_mul(mixed[part], at.long[slot, :, part * D : (part + 1) * D])
        d_norm[:, pl.ds(pl.multiple_of(index * 128, 128), 128)] = value

        @pl.when(index + 2 < D // 128)
        def _():
            ring(src.w1, at.long, 128, 3 * D, index + 2, (index + 2) * 128).start()

        return carry

    plan.work(4.0, lambda: lax.fori_loop(0, D // 128, through_mixer, 0))
    load_stash(src.embedded).wait()
    plan.work(3.0, lambda: norm_back(0, at.embed_low, True))
    at.embed_t[...] = at.embed_low[...].T
    turned = jnp.concatenate([norms[...], jnp.zeros((LANES - 8, D), F32)], 0).T
    at.extra[...] = pltpu.roll(turned, lead, 1)
    push(0)
    plan.finish()

    rows = lax.broadcasted_iota(jnp.int32, (8, LANES), 0)
    wide_tiles, narrow_tiles = at.wide_tiles, at.narrow_tiles
    wide_tiles[place.w] = jnp.where(rows == 0, src.term[...], sum(squares))

    def tile_copy(buffer, index, slot, peer):
        return pltpu.make_async_remote_copy(
            src_ref=buffer.at[index],
            dst_ref=buffer.at[index],
            send_sem=tile_send.at[slot],
            recv_sem=tile_recv.at[slot],
            device_id=peer,
            device_id_type=MESH,
        )

    for step in range(1, wide):
        start(tile_copy(wide_tiles, place.w, step - 1, (lax.rem(place.w + step, wide), place.n)))
    for step in range(1, wide):
        tile_copy(wide_tiles, place.w, step - 1, (lax.rem(place.w + step, wide), place.n)).wait_recv()
    whole = wide_tiles[0]
    for index in range(1, wide):
        whole = whole + wide_tiles[index]
    narrow_tiles[place.n] = whole
    for step in range(1, narrow):
        start(tile_copy(narrow_tiles, place.n, wide + step - 1, place.along(step)))
    for step in range(1, narrow):
        tile_copy(narrow_tiles, place.n, wide + step - 1, place.along(step)).wait_recv()
    whole = narrow_tiles[0]
    for index in range(1, narrow):
        whole = whole + narrow_tiles[index]
    totals[...] = whole
    for copy in list(last_sent.values()) + started:
        copy.wait_send()


def backward_all(kept, patches, gauss, term, lead, wide, narrow):
    tokens = patches.shape[0]
    chips = wide // 2
    weights = [kept.w1, kept.w2, kept.w3, kept.w4, kept.w5]
    heights = [D] + [weight.shape[0] for weight in weights]
    widths = [patches.shape[1]] + [weight.shape[1] for weight in weights]
    rows = [height // (wide * narrow) for height in heights]
    head_width = D // narrow
    length = narrow * tokens
    items = backward_plan(widths)
    slots = 2 * chips + narrow - 1
    streamed = dict(w1=kept.w1, w2=kept.w2, w3=kept.w3, w4=kept.w4, w5=kept.w5)
    streamed.update(last=kept.last, mid=kept.mid, embedded=kept.embedded, slopes=kept.slopes)
    loaded = dict(t5=kept.t5, t4=kept.t4, t3=kept.t3, t2=kept.t2, t1=kept.t1)
    loaded.update(qkv=kept.qkv, heads_out=kept.heads_out, log_sums=kept.log_sums)
    whole = dict(gains=kept.gains, patches=patches, gauss=gauss, term=term)
    operands = {**streamed, **loaded, **whole}
    shapes = [jax.ShapeDtypeStruct((rows[which], widths[which]), F32) for which in range(6)]
    shapes.append(jax.ShapeDtypeStruct((8, LANES), F32))
    scratch = {name: pltpu.VMEM(value.shape, value.dtype) for name, value in loaded.items()}
    scratch.update(
        embed_t=pltpu.VMEM((D, tokens), BF16),
        embed_low=pltpu.VMEM((tokens, D), BF16),
        stash=pltpu.VMEM((tokens, D), F32),
        d_res=pltpu.VMEM((tokens, D), F32),
        d_norm=pltpu.VMEM((tokens, D), F32),
        norms=pltpu.VMEM((8, D), F32),
        extra=pltpu.VMEM((D, LANES), F32),
        shrink_low=pltpu.VMEM((tokens, D), BF16),
        expand_low=pltpu.VMEM((tokens, widths[3]), BF16),
        merge_low=pltpu.VMEM((tokens, D), BF16),
        mixed=pltpu.VMEM((3, tokens, D), BF16),
        tall=pltpu.VMEM((2, 512, D), BF16),
        long=pltpu.VMEM((2, 128, widths[3]), BF16),
        slope_slots=pltpu.VMEM((2, tokens, 512), BF16),
        d_heads=pltpu.VMEM((narrow, tokens, head_width), BF16),
        away=pltpu.VMEM((narrow - 1, tokens, head_width), BF16),
        parts=pltpu.VMEM((narrow, 3, tokens, head_width), BF16),
        key_t=pltpu.VMEM((LANES, length), BF16),
        key_acc=pltpu.VMEM((length, LANES), F32),
        value_acc=pltpu.VMEM((length, LANES), F32),
        query_acc=pltpu.VMEM((LANES, tokens), F32),
        wide_tiles=pltpu.VMEM((wide, 8, LANES), F32),
        narrow_tiles=pltpu.VMEM((narrow, 8, LANES), F32),
        send_sem=pltpu.SemaphoreType.DMA((len(items), slots)),
        recv_sem=pltpu.SemaphoreType.DMA((len(items), slots)),
        tile_send=pltpu.SemaphoreType.DMA((wide + narrow,)),
        tile_recv=pltpu.SemaphoreType.DMA((wide + narrow,)),
        swap_send=pltpu.SemaphoreType.DMA((1 + head_width // LANES, narrow)),
        swap_recv=pltpu.SemaphoreType.DMA((1 + head_width // LANES, narrow)),
        in_sem=pltpu.SemaphoreType.DMA((9,)),
        ring_sem=pltpu.SemaphoreType.DMA((3, 2)),
    )
    lists = [pltpu.VMEM((chips, narrow, rows[which], width), BF16) for which, _, width, _ in items]
    for which, _, width, _ in items:
        for bit in chip_bits(chips):
            lists.append(pltpu.VMEM((chips // (2 * bit), narrow, rows[which], width), BF16))
    lists += [pltpu.VMEM((narrow - 1, rows[which], width), BF16) for which, _, width, _ in items]
    for which in range(6):
        widest = max(width for owner, _, width, _ in items if owner == which)
        lists.append(pltpu.VMEM((chips, narrow, rows[which], widest), BF16))
    vmem = pl.BlockSpec(memory_space=pltpu.VMEM)
    hbm = pl.BlockSpec(memory_space=pl.ANY)
    return pl.pallas_call(
        functools.partial(backward_kernel, items, wide, narrow, lead, tuple(operands), tuple(scratch)),
        out_shape=shapes,
        in_specs=[vmem if name in whole else hbm for name in operands],
        out_specs=[vmem] * len(shapes),
        scratch_shapes=list(scratch.values()) + lists,
        compiler_params=pltpu.CompilerParams(
            collective_id=1, has_side_effects=True, vmem_limit_bytes=63 * MIB
        ),
        name="backward",
    )(*operands.values())


def render_kernel(
    gauss_ref, weight_ref, target_ref, mask_ref, pair_ref, view_ref, total_ref, grad_ref, term_ref, feat, dfeat
):
    quads = gauss_ref.shape[0] // NVIEW
    span = weight_ref.shape[1]
    pairs = pair_ref.shape[1]
    scale = 1.0 / total_ref[0].astype(F32)

    def channel(index):
        return gauss_ref[:, index * PP : (index + 1) * PP]

    def shared():
        opacity = jax.nn.sigmoid(channel(3))
        extent = jax.nn.sigmoid(channel(5) + channel(6) + channel(7))
        lead = channel(8)
        denom = 1.0 + lead * lead + channel(9) * channel(9) + channel(10) * channel(10) + channel(11) * channel(11)
        facing = lead * lead / denom
        raw = channel(4)
        depth = jnp.maximum(raw, 0.0) + jnp.log1p(jnp.exp(-jnp.abs(raw)))
        return opacity, extent, lead, denom, facing, raw, depth

    opacity, extent, lead, denom, facing, raw, depth = shared()
    footprint = opacity * extent * facing
    channels = [jax.nn.sigmoid(channel(index)) * footprint for index in range(3)]
    channels += [footprint, depth * footprint]
    for index, value in enumerate(channels):
        for view in range(NVIEW):
            feat[index * quads : (index + 1) * quads, view * PP : (view + 1) * PP] = value[
                view * quads : (view + 1) * quads
            ]
    rendered = jnp.dot(feat[...], weight_ref[...], precision=HIGHEST, preferred_element_type=F32)
    parts = [rendered[index * quads : (index + 1) * quads] for index in range(5)]
    lane = lax.broadcasted_iota(jnp.int32, (quads, span), 1)
    live = jnp.where(lane < view_ref[0] * PP, mask_ref[...], 0).astype(F32)
    term = jnp.zeros((quads, span), F32)
    slopes = []
    for index in range(3):
        error = parts[index] - target_ref[index * quads : (index + 1) * quads, :].astype(F32)
        term = term + live * error * error
        slopes.append(2.0 * scale * live * error)
    below = 1.0 + parts[3]
    depth_out = parts[4] / below

    first, second = pair_ref[0:1, :], pair_ref[1:2, :]
    least = jnp.minimum(first, second)
    down = (jnp.abs(first - second) == P_SIZE).astype(jnp.int32)
    place = quads * PP
    slot, local = least // place, least % place
    high = down * quads + local // PP
    low = slot * PP + local % PP
    high_hot = (lax.broadcasted_iota(jnp.int32, (2 * quads, pairs), 0) == high).astype(F32).astype(BF16)
    low_hot = (lax.broadcasted_iota(jnp.int32, (span, pairs), 0) == low).astype(F32).astype(BF16)
    counts = back_mul(high_hot, low_hot)
    slope = jnp.zeros((quads, span), F32)
    for which, shift in enumerate((1, P_SIZE)):
        count = counts[which * quads : (which + 1) * quads]
        weight = DEPTH_WEIGHT * count * live * pltpu.roll(live, span - shift, 1)
        gap = depth_out - pltpu.roll(depth_out, span - shift, 1)
        term = term + weight * gap * gap
        pull = 2.0 * scale * weight * gap
        slope = slope + pull - pltpu.roll(pull, shift, 1)
    term_ref[...] = jnp.full(term_ref.shape, jnp.sum(term), F32)
    over = slope / below
    slopes += [-over * depth_out, over]
    stacked = jnp.concatenate(slopes, 0)
    dfeat[...] = lax.dot_general(
        stacked, weight_ref[...], (((1,), (1,)), ((), ())), precision=HIGHEST, preferred_element_type=F32
    )

    def feature_grad(index):
        return jnp.concatenate(
            [
                dfeat[index * quads : (index + 1) * quads, view * PP : (view + 1) * PP]
                for view in range(NVIEW)
            ],
            0,
        )

    def put(index, value):
        grad_ref[:, index * PP : (index + 1) * PP] = value.astype(BF16)

    d_foot = feature_grad(3)
    for index in range(3):
        tint = jax.nn.sigmoid(channel(index))
        upper = feature_grad(index)
        d_foot = d_foot + upper * tint
        put(index, upper * footprint * tint * (1.0 - tint))
    d_last = feature_grad(4)
    d_foot = d_foot + d_last * depth
    put(3, d_foot * extent * facing * opacity * (1.0 - opacity))
    put(4, d_last * footprint * jax.nn.sigmoid(raw))
    d_extent = d_foot * opacity * facing * extent * (1.0 - extent)
    for index in (5, 6, 7):
        put(index, d_extent)
    d_facing = d_foot * opacity * extent
    put(8, d_facing * 2.0 * lead / denom * (1.0 - facing))
    for index in (9, 10, 11):
        put(index, -2.0 * d_facing * facing / denom * channel(index))


def render(gaussians, weights, targets, mask, pairs, view_count, pair_total):
    rows = gaussians.shape[0]
    quads = rows // NVIEW
    slots, views = weights.shape[:2]
    spread = weights.transpose(1, 2, 0, 3).reshape(views * PP, slots * PP)
    wanted = targets.reshape(slots, 3, quads, PP).transpose(1, 2, 0, 3).reshape(3 * quads, slots * PP)
    valid = mask.reshape(slots, quads, PP).transpose(1, 0, 2).reshape(quads, slots * PP)
    vmem = pl.BlockSpec(memory_space=pltpu.VMEM)
    smem = pl.BlockSpec(memory_space=pltpu.SMEM)
    return pl.pallas_call(
        render_kernel,
        out_shape=[
            jax.ShapeDtypeStruct(gaussians.shape, BF16),
            jax.ShapeDtypeStruct((8, LANES), F32),
        ],
        in_specs=[vmem] * 5 + [smem] * 2,
        out_specs=[vmem] * 2,
        scratch_shapes=[pltpu.VMEM((5 * quads, views * PP), F32)] * 2,
        compiler_params=pltpu.CompilerParams(vmem_limit_bytes=48 * MIB),
        name="render",
    )(gaussians, spread, wanted, valid, pairs, view_count, pair_total)


def forward_plain(shards, patches, features, kinds):
    weights = [lax.all_gather(shard, BOTH, axis=0, tiled=True) for shard in shards]
    groups = lax.axis_size(NARROW)
    rows = patches.shape[0]
    gains = weights[0][:, features : features + kinds].T.astype(F32)
    embedded = back_mul(patches[:, :features], weights[0][:, :features])
    normed_one = layer_norm(embedded, gains[0], gains[3]).astype(BF16)
    mixed = matmul(normed_one, weights[1]).astype(BF16).reshape(rows, 3, groups, -1)
    mixed = mixed.transpose(2, 1, 0, 3)
    qkv = lax.all_to_all(mixed, NARROW, split_axis=0, concat_axis=0, tiled=True)
    width = qkv.shape[-1]
    length = groups * rows
    heads = width // HD
    parts = [qkv[:, part].reshape(length, heads, HD) for part in range(3)]
    attended, logsum = attention_forward(*parts)
    log_sums = logsum.transpose(0, 2, 1).reshape(groups, rows, heads)
    returned = lax.all_to_all(
        attended.reshape(groups, rows, width), NARROW, split_axis=0, concat_axis=0, tiled=True
    )
    returned = returned.transpose(1, 0, 2).reshape(rows, D)
    mid = embedded + matmul(returned, weights[2])
    normed_two = layer_norm(mid, gains[1], gains[4]).astype(BF16)
    expanded = matmul(normed_two, weights[3])
    half = 0.5 * (1.0 + lax.erf(expanded * (0.5**0.5)))
    activated = (expanded * half).astype(BF16)
    bell = jnp.exp(-0.5 * expanded * expanded) * 0.3989422804014327
    slopes = (half + expanded * bell).astype(BF16)
    last = mid + matmul(activated, weights[4])
    normed_three = layer_norm(last, gains[2], gains[5]).astype(BF16)
    return Bag(
        dict(
        w1=weights[1],
        w2=weights[2],
        w3=weights[3],
        w4=weights[4],
        w5=weights[5],
        gains=gains,
        embedded=embedded,
        mid=mid,
        last=last,
        slopes=slopes,
        t1=normed_one.T,
        t2=returned.T,
        t3=normed_two.T,
        t4=activated.T,
        t5=normed_three.T,
        qkv=qkv,
        heads_out=attended,
        log_sums=log_sums,
        gaussians=matmul(normed_three, weights[5]),
    ).items())


def backward_plain(kept, patches, gauss_low, term, features, kinds):
    gains = kept.gains
    weights = [None, kept.w1, kept.w2, kept.w3, kept.w4, kept.w5]
    norm_back_one = jax.vjp(layer_norm, kept.embedded, gains[0], gains[3])[1]
    norm_back_two = jax.vjp(layer_norm, kept.mid, gains[1], gains[4])[1]
    norm_back_three = jax.vjp(layer_norm, kept.last, gains[2], gains[5])[1]
    qkv = kept.qkv
    groups, _, rows, width = qkv.shape
    length = groups * rows
    heads = width // HD
    queries, keys, values = (qkv[:, part].reshape(length, heads, HD) for part in range(3))
    blocked = min(512, length)
    logsum = kept.log_sums[:, :, :heads].reshape(length // blocked, blocked, heads)
    residual_grad, gain_three, shift_three = norm_back_three(back_mul(gauss_low, weights[5]))
    shrink_low = residual_grad.astype(BF16)
    expand_low = (back_mul(shrink_low, weights[4]) * kept.slopes.astype(F32)).astype(BF16)
    through_two, gain_two, shift_two = norm_back_two(back_mul(expand_low, weights[3]))
    residual_grad = residual_grad + through_two
    merge_low = residual_grad.astype(BF16)
    out_grad = back_mul(merge_low, weights[2]).astype(BF16).reshape(rows, groups, width)
    head_grad = lax.all_to_all(
        out_grad.transpose(1, 0, 2), NARROW, split_axis=0, concat_axis=0, tiled=True
    ).reshape(length, heads, HD)
    grads = attention_backward(queries, keys, values, logsum.transpose(0, 2, 1), head_grad)
    stacked = jnp.stack(grads, 1).astype(BF16).reshape(groups, rows, 3, width)
    mixed_grad = lax.all_to_all(stacked, NARROW, split_axis=0, concat_axis=0, tiled=True)
    mixed_grad = mixed_grad.transpose(1, 2, 0, 3).reshape(rows, 3 * D)
    through_one, gain_one, shift_one = norm_back_one(back_mul(mixed_grad, weights[1]))
    embed_grad = (residual_grad + through_one).astype(BF16)
    grad_norms = jnp.stack([gain_one, gain_two, gain_three, shift_one, shift_two, shift_three])
    lefts = [embed_grad.T] + [kept.t1, kept.t2, kept.t3, kept.t4, kept.t5]
    rights = [patches, mixed_grad, merge_low, expand_low, shrink_low, gauss_low]
    products = [matmul(left, right) for left, right in zip(lefts, rights)]
    products[0] = products[0].at[:, features : features + kinds].add(grad_norms.T)
    sums = [
        lax.psum_scatter(
            product.astype(BF16), BOTH, scatter_dimension=0, tiled=True
        ).astype(F32)
        for product in products
    ]
    squares = sum(jnp.sum(part * part) for part in sums)
    loss_sum, square_sum = lax.psum((term[0, 0], squares), BOTH)
    return sums, loss_sum, square_sum


def body(
    views,
    render_w,
    targets,
    pix_mask,
    pairs,
    view_count,
    pair_total,
    embed_weight,
    embed_first,
    embed_second,
    mixer_weight,
    mixer_first,
    mixer_second,
    merge_weight,
    merge_first,
    merge_second,
    expand_weight,
    expand_first,
    expand_second,
    shrink_weight,
    shrink_first,
    shrink_second,
    unpatch_weight,
    unpatch_first,
    unpatch_second,
    norm_params,
    norm_first,
    norm_second,
):
    masters = (embed_weight, mixer_weight, merge_weight, expand_weight, shrink_weight, unpatch_weight, norm_params)
    firsts = (embed_first, mixer_first, merge_first, expand_first, shrink_first, unpatch_first, norm_first)
    seconds = (embed_second, mixer_second, merge_second, expand_second, shrink_second, unpatch_second, norm_second)
    groups = lax.axis_size(NARROW)
    wide_count = lax.axis_size(WIDE)
    features = embed_weight.shape[0]
    kinds = norm_params.shape[0]
    padded = -(-(features + kinds) // LANES) * LANES
    fill = padded - features - kinds
    by_kernel = mixer_weight.shape[0] % 16 == 0

    first_shard = jnp.concatenate([embed_weight.T, norm_params.T], 1)
    first_shard = jnp.pad(first_shard.astype(BF16), ((0, 0), (0, fill)))
    shards = [first_shard] + [weight.astype(BF16) for weight in masters[1:6]]
    patches = views.reshape(-1, features)
    rows = patches.shape[0]
    patches = jnp.pad(patches, ((0, 0), (0, padded - features)))
    if by_kernel:
        kept = forward_all(shards, patches, features % LANES, wide_count, groups)
    else:
        kept = forward_plain(shards, patches, features, kinds)
    divisor = pair_total[0].astype(F32)
    gauss_low, term = render(
        kept.gaussians, render_w[0], targets[0], pix_mask[0], pairs[0], view_count, pair_total
    )
    if by_kernel:
        *sums, totals = backward_all(
            kept, patches, gauss_low, term, features % LANES, wide_count, groups
        )
        loss_sum, square_sum = totals[0, 0], totals[1, 0]
    else:
        sums, loss_sum, square_sum = backward_plain(kept, patches, gauss_low, term, features, kinds)
    first_sum = sums[0].T
    grads = [first_sum[:features]] + list(sums[1:]) + [first_sum[features : features + kinds]]
    loss = loss_sum / divisor
    grad_norm = jnp.sqrt(square_sum)
    factor = jnp.minimum(1.0, CLIP_NORM / (grad_norm + 1e-06))
    results = []
    for which in range(7):
        results += adamw(masters[which], firsts[which], seconds[which], grads[which] * factor, RATES[which])
    return tuple(results) + (loss, grad_norm)


def solution(mesh):
    columns = P(None, BOTH)
    rows = P(BOTH, None)
    weights = (columns,) * 3 + (rows,) * 15 + (columns,) * 3
    return jax.shard_map(
        body,
        mesh=mesh,
        in_specs=(
            P(WIDE, None, NARROW, None),
            P(WIDE, None, None, None, None),
            P(WIDE, None, None, NARROW),
            P(WIDE, None, NARROW),
            P(WIDE, None, NARROW),
            P(WIDE),
            P(),
        )
        + weights,
        out_specs=weights + (P(), P()),
        check_vma=False,
    )
```

```python
import functools
import heapq

import jax
import jax.numpy as jnp
from jax import lax
from jax.experimental import pallas as pl
from jax.experimental.pallas import tpu as pltpu
from jax.sharding import PartitionSpec as P

D = 1024
HD = 64
P_SIZE = 8
PP = 64
NVIEW = 4
TMAX = 12
STEP = 10
LANES = 128
MIB = 1024 * 1024

DEPTH_WEIGHT = 1.0
CLIP_NORM = 0.01
BETA_ONE = 0.9
BETA_TWO = 0.95
ADAM_EPS = 1e-08
DECAY = 0.05
RATES = (0.05, 0.05, 0.5, 0.05, 0.05, 0.05, 0.8)
MESH = pl.DeviceIdType.MESH
WIDE, NARROW = BOTH = ("wide", "narrow")
HIGHEST = lax.Precision.HIGHEST
F32 = jnp.float32
BF16 = jnp.bfloat16


def matmul(left, right):
    return jnp.dot(left, right, preferred_element_type=F32)


def outer_sum(left, right):
    return lax.dot_general(left, right, (((0,), (0,)), ((), ())), preferred_element_type=F32)


def back_mul(grad, weight):
    return lax.dot_general(grad, weight, (((1,), (1,)), ((), ())), preferred_element_type=F32)


def layer_norm(values, gain, shift):
    centred = values - jnp.mean(values, -1, keepdims=True)
    spread = jnp.mean(centred * centred, -1, keepdims=True)
    return centred * lax.rsqrt(spread + 1e-05) * gain + shift


def exact_gelu(values):
    return jax.nn.gelu(values, approximate=False)


def attention_forward(queries, keys, values):
    length, heads = (queries.shape[0], queries.shape[1])
    blocked = min(512, length)
    scale = HD ** (-0.5)

    def one_block(query_block):
        scores = (
            jnp.einsum("qhd,khd->hqk", query_block, keys, preferred_element_type=jnp.float32)
            * scale
        )
        highest = jnp.max(scores, -1, keepdims=True)
        exponentials = jnp.exp(scores - highest)
        summed = jnp.sum(exponentials, -1, keepdims=True)
        softmaxed = (exponentials / summed).astype(jnp.bfloat16)
        output = jnp.einsum("hqk,khd->qhd", softmaxed, values, preferred_element_type=jnp.float32)
        return (output.astype(jnp.bfloat16), (highest + jnp.log(summed))[:, :, 0])

    output, logsum = lax.map(one_block, queries.reshape(length // blocked, blocked, heads, HD))
    return (output.reshape(length, heads * HD), logsum)


def attention_backward(queries, keys, values, logsum, out_grad):
    length, heads = (queries.shape[0], queries.shape[1])
    blocked = min(512, length)
    scale = HD ** (-0.5)

    def one_block(carry, inputs):
        key_grad, value_grad = carry
        query_block, logsum_block, grad_block = inputs
        scores = (
            jnp.einsum("qhd,khd->hqk", query_block, keys, preferred_element_type=jnp.float32)
            * scale
        )
        softmaxed = jnp.exp(scores - logsum_block[:, :, None])
        value_grad = value_grad + jnp.einsum(
            "hqk,qhd->khd",
            softmaxed.astype(jnp.bfloat16),
            grad_block,
            preferred_element_type=jnp.float32,
        )
        prob_grad = jnp.einsum(
            "qhd,khd->hqk", grad_block, values, preferred_element_type=jnp.float32
        )
        score_grad = softmaxed * (prob_grad - jnp.sum(softmaxed * prob_grad, -1, keepdims=True))
        score_low = score_grad.astype(jnp.bfloat16)
        query_grad = (
            jnp.einsum("hqk,khd->qhd", score_low, keys, preferred_element_type=jnp.float32) * scale
        )
        key_grad = (
            key_grad
            + jnp.einsum("hqk,qhd->khd", score_low, query_block, preferred_element_type=jnp.float32)
            * scale
        )
        return ((key_grad, value_grad), query_grad)

    zeros = jnp.zeros((length, heads, HD), jnp.float32)
    shaped = (
        queries.reshape(length // blocked, blocked, heads, HD),
        logsum,
        out_grad.reshape(length // blocked, blocked, heads, HD),
    )
    (key_grad, value_grad), query_grad = lax.scan(one_block, (zeros, zeros), shaped)
    return (query_grad.reshape(length, heads, HD), key_grad, value_grad)


def adamw(weight, first, second, grad, rate):
    first = BETA_ONE * first + (1.0 - BETA_ONE) * grad
    second = BETA_TWO * second + (1.0 - BETA_TWO) * grad * grad
    first_hat = first / (1.0 - BETA_ONE**STEP)
    second_hat = second / (1.0 - BETA_TWO**STEP)
    weight = weight - rate * (first_hat / (jnp.sqrt(second_hat) + ADAM_EPS) + DECAY * weight)
    return (weight, first, second)


def chip_bits(chips):
    bits, step = [], 1
    while step < chips:
        bits.append(step)
        step *= 2
    return bits


def flip(chip, mask):
    for bit in chip_bits(mask + 1):
        if mask & bit:
            chip = chip + (1 - 2 * (chip // bit % 2)) * bit
    return chip


def column_halves(width):
    first = -(-width // (2 * LANES)) * LANES
    return ((0, first), (first, width - first))


def work_items(widths, order):
    return [(which,) + half + (side,) for which in order for side, half in enumerate(column_halves(widths[which]))]


class Bag:
    def __init__(self, pairs):
        vars(self).update(pairs)


class Place:
    def __init__(self, wide, narrow):
        self.wide, self.narrow = wide, narrow
        self.chips = wide // 2
        self.bits = chip_bits(self.chips)
        self.w = lax.axis_index(WIDE)
        self.n = lax.axis_index(NARROW)
        self.chip = self.w // 2
        self.core = self.w % 2
        self.twin = (2 * self.chip + 1 - self.core, self.n)

    def across(self, mask):
        return (2 * flip(self.chip, mask) + self.core, self.n)

    def along(self, step):
        return (self.w, lax.rem(self.n + step, self.narrow))

    def neighbours(self):
        return (
            [self.twin]
            + [self.across(bit) for bit in self.bits]
            + [self.along(step) for step in range(1, self.narrow)]
        )


class Planner:
    def __init__(self):
        self.now, self.count = 0.0, 0
        self.free, self.events, self.done, self.spare = {}, [], set(), []
        self.refill = lambda: None

    def transfer(self, link, cost, key, event):
        self.free[link] = max(self.now, self.free.get(link, 0.0)) + cost
        self.count += 1
        heapq.heappush(self.events, (self.free[link] + 2.0, self.count, key, event))

    def step(self):
        when, _, key, event = heapq.heappop(self.events)
        self.now = max(self.now, when) + 0.2
        event()
        self.done.add(key)
        self.refill()

    def fill(self, until):
        for index, (keys, cost, work) in enumerate(self.spare):
            if self.now + cost <= until and self.done.issuperset(keys):
                del self.spare[index]
                work()
                self.now += cost
                return True
        return False

    def need(self, keys):
        while not self.done.issuperset(keys):
            if not self.fill(self.events[0][0]):
                self.step()

    def work(self, cost, work):
        while self.events and self.events[0][0] <= self.now:
            self.step()
        self.refill()
        work()
        self.now += cost

    def later(self, cost, work, keys=()):
        entry = (tuple(keys), cost, work)
        self.spare.append(entry)
        return entry

    def force(self, entry):
        if entry in self.spare:
            self.spare.remove(entry)
            self.work(entry[1], entry[2])

    def finish(self):
        while self.events or self.spare:
            if not self.fill(self.events[0][0] if self.events else 1e9):
                self.step()


LINK = 100e3
TWIN_LINK = 600e3


def greet(peers):
    barrier = pltpu.get_barrier_semaphore()
    for peer in peers:
        pl.semaphore_signal(barrier, inc=1, device_id=peer, device_id_type=MESH)
    pl.semaphore_wait(barrier, len(peers))


def normalize(values, gain, shift):
    centred = values - jnp.mean(values, -1, keepdims=True)
    spread = jnp.mean(centred * centred, -1, keepdims=True)
    return centred * lax.rsqrt(spread + 1e-05) * gain + shift


def forward_plan(widths):
    items = []
    for which, cuts in ((0, 1), (1, 3), (2, 1), (3, 2), (5, 1), (4, 2)):
        size = widths[which] // cuts
        for cut in range(cuts):
            for side, (start, width) in enumerate(column_halves(size)):
                items.append((which, cut * size + start, width, side))
    return items


def forward_kernel(items, wide, narrow, lead, ins, outs, scratch, *refs):
    at = Bag(zip(ins + scratch, refs[: len(ins)] + refs[len(ins) + len(outs) :]))
    results = refs[len(ins) : len(ins) + len(outs)]
    weights = [at.first_weight, at.w1, at.w2, at.w3, at.w4, at.w5]
    shards = [at.c0, at.c1, at.c2, at.c3, at.c4, at.c5]
    raw = [at.s0, at.s1, at.s2, at.s3, at.s4, at.s5]
    own_sem, send_sem, recv_sem = at.own_sem, at.send_sem, at.recv_sem
    swap_send, swap_recv, out_sem = at.swap_send, at.swap_recv, at.out_sem
    place = Place(wide, narrow)
    chips, me = place.chips, place.n
    tokens = at.patches.shape[0]
    head_width = D // narrow
    total = len(items)
    started = []

    def start(copy):
        copy.start()
        started.append(copy)

    features = at.s0.shape[1]
    tail = shards[0].shape[1] - LANES
    kinds = at.norm_raw.shape[0]
    kind = lax.broadcasted_iota(jnp.int32, (kinds, LANES), 0)
    spot = lax.broadcasted_iota(jnp.int32, (kinds, LANES), 1)
    put = (spot == kind + lead).astype(F32).astype(BF16)
    shards[0][:, tail:] = outer_sum(at.norm_raw[...].astype(BF16), put).astype(BF16)
    shards[0][:, 0:features] = at.s0[...].astype(BF16)
    for source, dest in zip(raw[1:], shards[1:]):
        dest[...] = source[...].astype(BF16)
    greet(place.neighbours())
    rows_of = [shard.shape[0] for shard in shards]

    def rows_at(which, chip, core, node=None):
        rows = rows_of[which]
        if node is None:
            return pl.ds(pl.multiple_of((chip * 2 + core) * narrow * rows, rows), narrow * rows)
        return pl.ds(pl.multiple_of(((chip * 2 + core) * narrow + node) * rows, rows), rows)

    own = []
    for which in range(6):
        copy = pltpu.make_async_copy(
            shards[which], weights[which].at[rows_at(which, place.chip, place.core, me), :], own_sem.at[which]
        )
        copy.start()
        own.append(copy)

    def remote(item, src, dst, slot, peer):
        return pltpu.make_async_remote_copy(
            src_ref=src,
            dst_ref=dst,
            send_sem=send_sem.at[item, slot],
            recv_sem=recv_sem.at[item, slot],
            device_id=peer,
            device_id_type=MESH,
        )

    def group(item, mask):
        which, begin, width, _ = items[item]
        return weights[which].at[rows_at(which, flip(place.chip, mask), place.core), pl.ds(begin, width)]

    def along(item, step):
        which, begin, width, _ = items[item]
        return remote(
            item,
            shards[which].at[:, pl.ds(begin, width)],
            weights[which].at[rows_at(which, place.chip, place.core, me), pl.ds(begin, width)],
            2 * chips + step - 1,
            place.along(step),
        )

    def bits_of(item):
        return place.bits if items[item][3] == 0 else place.bits[::-1]

    def across(item, mask, bit):
        return remote(item, group(item, mask), group(item, mask), mask ^ bit, place.across(bit))

    def to_twin(item, mask):
        return remote(item, group(item, mask), group(item, mask), chips + mask, place.twin)

    plan = Planner()
    waited = set()
    halves = (narrow // 2) * (narrow - narrow // 2)

    def block_bytes(item):
        which, _, width, _ = items[item]
        return 2 * narrow * rows_of[which] * width

    def twin_event(item, mask):
        return lambda: to_twin(item, mask).wait_recv()

    def onward(item, mask, number):
        bits = bits_of(item)
        size = block_bytes(item)
        for later in range(number, len(bits)):
            start(across(item, mask, bits[later]))
            coming = mask ^ bits[later]
            plan.transfer(
                bits[later], 2 * size / LINK, (item, coming), functools.partial(arrive, item, coming, later)
            )
        start(to_twin(item, mask))
        plan.transfer(-1, size / TWIN_LINK, (item, chips + mask), twin_event(item, mask))

    def arrive(item, mask, number):
        across(item, mask ^ bits_of(item)[number], bits_of(item)[number]).wait_recv()
        onward(item, mask, number + 1)

    def begin_item(item):
        for step in range(1, narrow):
            start(along(item, step))
        cost = halves * 2 * block_bytes(item) / narrow / LINK
        plan.transfer(0, cost, (item, 0), functools.partial(line_event, item))

    def line_event(item):
        if items[item][0] not in waited:
            waited.add(items[item][0])
            own[items[item][0]].wait()
        for step in range(1, narrow):
            along(item, step).wait_recv()
        onward(item, 0, 0)

    begun = []

    def refill():
        while len(begun) < total and plan.free.get(0, 0.0) < plan.now + 7.0:
            begin_item(len(begun))
            begun.append(True)

    plan.refill = refill
    refill()

    def need(which, columns=None):
        plan.need(
            [
                (index, key)
                for index, (owner, begin, width, _) in enumerate(items)
                if owner == which and (columns is None or (begin < columns[1] and begin + width > columns[0]))
                for key in range(2 * chips)
            ]
        )

    flushed = []

    def flush(ref):
        index = [vars(at)[name] is ref for name in outs].index(True)
        copy = pltpu.make_async_copy(ref, results[index], out_sem.at[index])
        copy.start()
        flushed.append(copy)

    def swap(src, dst, kind, step):
        return pltpu.make_async_remote_copy(
            src_ref=src,
            dst_ref=dst,
            send_sem=swap_send.at[kind, step],
            recv_sem=swap_recv.at[kind, step],
            device_id=place.along(step),
            device_id_type=MESH,
        )

    gains = at.gains
    embedded, mid, last = at.embedded, at.mid, at.last
    normed, hidden, wave = at.normed, at.hidden, at.wave
    away, qkv, heads_out, returned = at.away, at.qkv, at.heads_out, at.returned

    def turn(dest, source):
        dest[...] = source[...].T
        flush(dest)

    need(0)
    width = weights[0].shape[1]
    kind = lax.broadcasted_iota(jnp.int32, (8, LANES), 0)
    spot = lax.broadcasted_iota(jnp.int32, (8, LANES), 1)
    pick = (spot == kind + lead).astype(F32).astype(BF16)
    gains[...] = back_mul(pick, weights[0][:, width - LANES :])
    flush(gains)

    def embed(block):
        cols = pl.ds(block, 256)
        embedded[:, cols] = back_mul(at.patches[...], weights[0][pl.ds(block, 256), : at.patches.shape[1]])

    for block in range(0, D, 256):
        plan.work(0.5, functools.partial(embed, block))
    flush(embedded)

    def norm_rows(source, row, dest):
        step_rows = 64

        def one(step, carry):
            rows = pl.ds(pl.multiple_of(step * step_rows, step_rows), step_rows)
            dest[rows, :] = normalize(
                source[rows, :], gains[row : row + 1, :], gains[row + 3 : row + 4, :]
            ).astype(BF16)
            return carry

        lax.fori_loop(0, tokens // step_rows, one, 0)

    plan.work(2.0, lambda: norm_rows(embedded, 0, normed))
    turn_first = plan.later(2.0, lambda: turn(at.t1, normed))
    piece = 2 * halves * 2 * tokens * head_width / LINK

    def project(part, step):
        owner = lax.rem(me + step, narrow)
        offset = pl.multiple_of(part * D + owner * head_width, LANES)
        value = matmul(normed[...], weights[1][:, pl.ds(offset, head_width)]).astype(BF16)
        if step:
            away[step - 1, part] = value
            start(swap(away.at[step - 1, part], qkv.at[me, part], part, step))
        else:
            qkv[me, part] = value

    def swap_event(part):
        for step in range(1, narrow):
            swap(away.at[step - 1, part], qkv.at[me, part], part, step).wait_recv()

    for part in range(3):
        need(1, (part * D, part * D + D))
        for step in list(range(1, narrow)) + [0]:
            plan.work(0.7, functools.partial(project, part, step))
        plan.transfer(0, piece, (-1, part), functools.partial(swap_event, part))
    flush(at.w1)
    plan.need([(-1, part) for part in range(3)])
    flush(qkv)
    plan.need([(-1, 2)])

    lane = lax.broadcasted_iota(jnp.int32, (1, LANES), 1)
    scale = HD ** (-0.5)
    length = narrow * tokens

    def attend(step):
        who = lax.rem(me + step, narrow)
        log_sums = jnp.zeros((tokens, LANES), F32)
        for pair in range(head_width // LANES):
            lanes = pl.ds(pair * LANES, LANES)
            query = qkv[who, 0, :, lanes].astype(F32)
            key = qkv[:, 1, :, lanes].reshape(length, LANES)
            value = qkv[:, 2, :, lanes].reshape(length, LANES)
            out = jnp.zeros((tokens, LANES), F32)
            for side in range(LANES // HD):
                inside = lane // HD == side
                own_query = (query * jnp.where(inside, scale, 0.0)).astype(BF16)
                scores = back_mul(own_query, key)
                highest = jnp.max(scores, -1, keepdims=True)
                exponentials = jnp.exp(scores - highest)
                summed = jnp.sum(exponentials, -1, keepdims=True)
                part = matmul(exponentials.astype(BF16), value) / summed
                out = jnp.where(inside, part, out)
                log_sums = jnp.where(
                    lane == pair * (LANES // HD) + side, highest + jnp.log(summed), log_sums
                )
            heads_out[who, :, lanes] = out.astype(BF16)
        at.log_sums[who] = log_sums
        if step:
            start(swap(heads_out.at[who], returned.at[me], 3, step))
        else:
            returned[me] = heads_out[who]

    def return_event(step):
        return lambda: swap(heads_out.at[me], returned.at[me], 3, step).wait_recv()

    for step in list(range(1, narrow)) + [0]:
        plan.work(3.5, functools.partial(attend, step))
        if step:
            plan.transfer(0, piece / (narrow - 1), (-2, step), return_event(step))
    flush(heads_out)
    flush(at.log_sums)
    need(2)
    plan.need([(-2, step) for step in range(1, narrow)])

    def merge(block):
        cols = pl.ds(block, 256)
        value = embedded[:, cols]
        for source in range(narrow):
            value = value + matmul(returned[source], weights[2][pl.ds(source * head_width, head_width), cols])
        mid[:, cols] = value

    for block in range(0, D, 256):
        plan.work(0.7, functools.partial(merge, block))
    flush(at.w2)
    flush(mid)
    plan.force(turn_first)
    plan.work(2.0, lambda: norm_rows(mid, 1, normed))

    def turn_returned():
        for source in range(narrow):
            at.t2[pl.ds(source * head_width, head_width), :] = returned[source].T
        flush(at.t2)

    plan.later(2.0, turn_returned)
    turn_second = plan.later(2.0, lambda: turn(at.t3, normed))

    ff = weights[3].shape[1]
    tile = wave.shape[1]
    slopes = at.slopes

    def expand(block):
        wave[...] = matmul(normed[...], weights[3][:, pl.ds(block, tile)])

        def bend(step, carry):
            rows = pl.ds(pl.multiple_of(step * 32, 32), 32)
            x = wave[rows, :]
            half = 0.5 * (1.0 + lax.erf(x * (0.5**0.5)))
            hidden[rows, pl.ds(block, tile)] = (x * half).astype(BF16)
            bell = jnp.exp(-0.5 * x * x) * 0.3989422804014327
            slopes[rows, pl.ds(block, tile)] = (half + x * bell).astype(BF16)
            return carry

        lax.fori_loop(0, tokens // 32, bend, 0)

    def turn_hidden(block):
        at.t4[pl.ds(block, tile), :] = hidden[:, pl.ds(block, tile)].T

    for block in range(0, ff, tile):
        need(3, (block, block + tile))
        plan.work(2.5, functools.partial(expand, block))
        plan.later(1.0, functools.partial(turn_hidden, block))
    flush(at.w3)
    flush(slopes)

    def shrink(block):
        cols = pl.ds(block, 256)
        last[:, cols] = mid[:, cols] + matmul(hidden[...], weights[4][:, cols])

    for block in range(0, D, 256):
        need(4, (block, block + 256))
        plan.work(1.0, functools.partial(shrink, block))
    flush(at.w4)
    flush(last)
    plan.force(turn_second)
    plan.work(2.0, lambda: norm_rows(last, 2, normed))
    need(5)

    def unpatch(block):
        cols = pl.ds(block, 256)
        at.gaussians[:, cols] = matmul(normed[...], weights[5][:, cols])

    for block in range(0, weights[5].shape[1], 256):
        plan.work(0.7, functools.partial(unpatch, block))
    flush(at.w5)
    flush(at.gaussians)
    plan.later(2.0, lambda: turn(at.t5, normed))
    plan.finish()
    flush(at.t4)
    for copy in started:
        copy.wait_send()
    for copy in flushed:
        copy.wait()


def forward_all(shards, norms, patches, lead, wide, narrow):
    tokens = patches.shape[0]
    widths = [patches.shape[1]] + [shard.shape[1] for shard in shards[1:]]
    heights = [shard.shape[0] * wide * narrow for shard in shards]
    ff = widths[3]
    head_width = D // narrow
    items = forward_plan(widths)
    slots = wide + narrow - 1
    full = [((height, width), BF16) for height, width in zip(heights, widths)]
    shapes = dict(
        w1=full[1],
        w2=full[2],
        w3=full[3],
        w4=full[4],
        w5=full[5],
        gains=((8, D), F32),
        embedded=((tokens, D), F32),
        mid=((tokens, D), F32),
        last=((tokens, D), F32),
        slopes=((tokens, ff), BF16),
        t1=((D, tokens), BF16),
        t2=((D, tokens), BF16),
        t3=((D, tokens), BF16),
        t4=((ff, tokens), BF16),
        t5=((D, tokens), BF16),
        qkv=((narrow, 3, tokens, head_width), BF16),
        heads_out=((narrow, tokens, head_width), BF16),
        log_sums=((narrow, tokens, LANES), F32),
        gaussians=((tokens, widths[5]), F32),
    )
    ins = tuple(dict(s0=0, s1=0, s2=0, s3=0, s4=0, s5=0, norm_raw=0, patches=0))
    outs = tuple(shapes)
    extras = dict(
        first_weight=pltpu.VMEM((heights[0], widths[0]), BF16),
        c0=pltpu.VMEM((shards[0].shape[0], widths[0]), BF16),
        c1=pltpu.VMEM(shards[1].shape, BF16),
        c2=pltpu.VMEM(shards[2].shape, BF16),
        c3=pltpu.VMEM(shards[3].shape, BF16),
        c4=pltpu.VMEM(shards[4].shape, BF16),
        c5=pltpu.VMEM(shards[5].shape, BF16),
        normed=pltpu.VMEM((tokens, D), BF16),
        hidden=pltpu.VMEM((tokens, ff), BF16),
        wave=pltpu.VMEM((tokens, 512), F32),
        away=pltpu.VMEM((narrow - 1, 3, tokens, head_width), BF16),
        returned=pltpu.VMEM((narrow, tokens, head_width), BF16),
        own_sem=pltpu.SemaphoreType.DMA((6,)),
        send_sem=pltpu.SemaphoreType.DMA((len(items), slots)),
        recv_sem=pltpu.SemaphoreType.DMA((len(items), slots)),
        swap_send=pltpu.SemaphoreType.DMA((4, narrow)),
        swap_recv=pltpu.SemaphoreType.DMA((4, narrow)),
        out_sem=pltpu.SemaphoreType.DMA((len(outs),)),
    )
    scratch = outs + tuple(extras)
    anywhere = pl.BlockSpec(memory_space=pl.ANY)
    results = pl.pallas_call(
        functools.partial(forward_kernel, items, wide, narrow, lead, ins, outs, scratch),
        out_shape=[jax.ShapeDtypeStruct(*shapes[name]) for name in outs],
        in_specs=[pl.BlockSpec(memory_space=pltpu.VMEM)] * len(ins),
        out_specs=[anywhere] * len(outs),
        scratch_shapes=[pltpu.VMEM(*shapes[name]) for name in outs] + list(extras.values()),
        compiler_params=pltpu.CompilerParams(
            collective_id=0, has_side_effects=True, vmem_limit_bytes=60 * MIB
        ),
        name="forward",
    )(*shards, norms, patches)
    return Bag(zip(outs, results))


def backward_plan(widths):
    items = []
    for which, cuts in ((5, 1), (4, 2), (3, 2), (2, 1), (1, 3), (0, 1)):
        size = widths[which] // cuts
        for cut in range(cuts):
            for side, (start, width) in enumerate(column_halves(size)):
                items.append((which, cut * size + start, width, side))
    return items


def tile_of(width):
    for tile in (512, 384, 256, 128):
        if width % tile == 0:
            return tile
    return width


def backward_kernel(items, wide, narrow, lead, ins, scratch, *refs):
    src = Bag(zip(ins, refs))
    refs = refs[len(ins) :]
    sums, totals, refs = refs[:6], refs[6], list(refs[7:])
    at = Bag(zip(scratch, refs))
    place = Place(wide, narrow)
    chips, me = place.chips, place.n
    total = len(items)
    refs = refs[len(scratch) :]
    held = [refs.pop(0) for _ in items]
    passed = [[refs.pop(0) for _ in place.bits] for _ in items]
    final = [refs.pop(0) for _ in items]
    spare = [refs.pop(0) for _ in range(6)]
    tokens = src.patches.shape[0]
    head_width = D // narrow
    length = narrow * tokens
    send_sem, recv_sem, tile_send, tile_recv = at.send_sem, at.recv_sem, at.tile_send, at.tile_recv
    swap_send, swap_recv, in_sem, ring_sem = at.swap_send, at.swap_recv, at.in_sem, at.ring_sem
    gains, norms, extra = src.gains, at.norms, at.extra
    stash, d_res, d_norm = at.stash, at.d_res, at.d_norm
    mixed, merge_low, expand_low, shrink_low = at.mixed, at.merge_low, at.expand_low, at.shrink_low

    loaded = [name for name in ins if name in scratch]

    def load(ref):
        index = [vars(at)[name] is ref for name in loaded].index(True)
        return pltpu.make_async_copy(vars(src)[loaded[index]], ref, in_sem.at[index])

    def load_stash(ref):
        return pltpu.make_async_copy(ref, stash, in_sem.at[len(loaded)])

    def ring(ref, slots, rows, columns, index, row):
        slot = lax.rem(index, 2)
        return pltpu.make_async_copy(
            ref.at[pl.ds(pl.multiple_of(row, rows), rows), :],
            slots.at[slot, pl.ds(0, rows), pl.ds(0, columns)],
            ring_sem.at[0 if slots is at.tall else 1, slot],
        )

    slope_rows = at.tall.shape[1]

    def slope_load(index):
        slot = lax.rem(index, 2)
        return pltpu.make_async_copy(
            src.slopes.at[:, pl.ds(pl.multiple_of(index * slope_rows, slope_rows), slope_rows)],
            at.slope_slots.at[slot],
            ring_sem.at[2, slot],
        )

    u_rows, u_cols = 256, src.w5.shape[1]
    load_stash(src.last).start()
    for index in range(2):
        ring(src.w5, at.tall, u_rows, u_cols, index, index * u_rows).start()
        slope_load(index).start()
        ring(src.w3, at.long, 128, src.w3.shape[1], index, index * 128).start()
    for name in loaded:
        load(vars(at)[name]).start()

    peers = [(lax.rem(place.w + step, wide), place.n) for step in range(1, wide)]
    peers += [place.along(step) for step in range(1, narrow)]
    greet(peers)

    started = []

    def start(copy):
        copy.start()
        started.append(copy)

    lefts = [at.embed_t, at.t1, at.t2, at.t3, at.t4, at.t5]
    rights = [src.patches, mixed, merge_low, expand_low, shrink_low, src.gauss]

    def remote(item, src, dst, slot, peer):
        return pltpu.make_async_remote_copy(
            src_ref=src,
            dst_ref=dst,
            send_sem=send_sem.at[item, slot],
            recv_sem=recv_sem.at[item, slot],
            device_id=peer,
            device_id_type=MESH,
        )

    def bits_of(item):
        return place.bits[::-1] if items[item][3] == 0 else place.bits

    def groups_of(item):
        size = max(1, 512 // (narrow * spare[items[item][0]].shape[2]))
        masks = list(range(chips))
        if bits_of(item) and bits_of(item)[0] > 1:
            masks = masks[chips // 2 :] + masks[: chips // 2]
        return [sorted(masks[at_mask : at_mask + size]) for at_mask in range(0, chips, size)]

    def product(item, masks, core, into, plus):
        which, begin, width, _ = items[item]
        left, right = lefts[which], rights[which]
        rows = into.shape[-2]
        span = narrow * rows
        tile = tile_of(width)
        firsts = [((flip(place.chip, mask) * 2 + core) * narrow) * rows for mask in masks]
        with_extra = which == 0 and begin + width == right.shape[1]
        assert not with_extra or tile == width
        part, begin = (begin // D, begin % D) if which == 1 else (None, begin)

        def one(step, carry):
            offset = pl.multiple_of(begin + step * tile, LANES)
            local = pl.multiple_of(step * tile, LANES)
            if part is None:
                rhs = right[:, pl.ds(offset, tile)]
            else:
                rhs = right[part, :, pl.ds(offset, tile)]
            spots = [pl.ds(pl.multiple_of(first, span), span) for first in firsts]
            lhs = jnp.concatenate([left[spot, :] for spot in spots], 0)
            value = jnp.dot(lhs, rhs, preferred_element_type=F32)
            for index, mask in enumerate(masks):
                piece = value[index * span : (index + 1) * span]
                if with_extra:
                    blank = jnp.zeros((span, tile - LANES), F32)
                    piece = piece + jnp.concatenate([blank, extra[spots[index], :]], 1)
                piece = piece.reshape(narrow, rows, tile)
                if plus:
                    piece = piece + into[mask, :, :, pl.ds(local, tile)].astype(F32)
                into[mask, :, :, pl.ds(local, tile)] = piece.astype(BF16)
            return carry

        lax.fori_loop(0, width // tile, one, 0)

    last_sent = {}
    plan = Planner()
    halves = (narrow // 2) * (narrow - narrow // 2)

    def to_twin(item, masks):
        which, _, width, _ = items[item]
        some = pl.ds(masks[0], len(masks))
        own = spare[which].at[some, :, :, pl.ds(0, width)]
        return remote(item, own, held[item].at[some], masks[0], place.twin)

    def across(item, mask, bit, number, slot):
        return remote(
            item, held[item].at[mask], passed[item][number].at[slot], chips + mask, place.across(bit)
        )

    def along(item, step):
        target = place.along(step)
        return remote(
            item,
            held[item].at[0, target[1]],
            final[item].at[narrow - step - 1],
            2 * chips + narrow - step - 1,
            target,
        )

    def leaves(item, mask):
        bits = bits_of(item)
        return min([number for number, bit in enumerate(bits) if mask & bit], default=len(bits))

    def slot_of(item, mask, number):
        bits = bits_of(item)
        kept = [m for m in range(chips) if not any(m & bit for bit in bits[: number + 1])]
        return kept.index(mask)

    def add_into(dest, dest_at, src, src_at):
        def one(step, carry):
            value = dest[dest_at, step].astype(F32) + src[src_at, step].astype(F32)
            dest[dest_at, step] = value.astype(BF16)
            return carry

        lax.fori_loop(0, narrow, one, 0)

    def block_bytes(item):
        which, _, width, _ = items[item]
        return 2 * spare[which].shape[1] * spare[which].shape[2] * width

    def push(which, part=None):
        for item, (owner, begin, _, _) in enumerate(items):
            if owner != which or (part is not None and begin // D != part):
                continue
            for masks in groups_of(item):
                cost = len(masks) * block_bytes(item) / 1e6
                plan.work(cost, functools.partial(push_some, item, masks))

    def push_some(item, masks):
        which = items[item][0]
        for key in [key for key in last_sent if key[0] == which and set(key[1]) & set(masks)]:
            last_sent.pop(key).wait_send()
        product(item, masks, 1 - place.core, spare[which], False)
        copy = to_twin(item, masks)
        copy.start()
        last_sent[which, tuple(masks)] = copy
        cost = len(masks) * block_bytes(item) / TWIN_LINK
        plan.transfer(-1, cost, (item, 0, masks[0]), functools.partial(own_event, item, masks))

    def own_event(item, masks):
        to_twin(item, masks).wait_recv()
        product(item, masks, place.core, held[item], True)
        plan.now += len(masks) * block_bytes(item) / 1e6
        plan.done.update((item, 0, mask) for mask in masks)
        for mask in masks:
            onward(item, mask, 0)

    def onward(item, mask, number):
        bits = bits_of(item)
        if number == len(bits):
            for step in range(1, narrow):
                start(along(item, step))
            cost = halves * 2 * block_bytes(item) / narrow / LINK
            plan.transfer(0, cost, (item, -1, 0), functools.partial(finish, item))
        elif leaves(item, mask) == number:
            kept = mask ^ bits[number]
            start(across(item, mask, bits[number], number, slot_of(item, kept, number)))
            plan.transfer(
                bits[number],
                2 * block_bytes(item) / LINK,
                (item, 1 + number, kept),
                functools.partial(sum_event, item, kept, number),
            )

    def sum_event(item, mask, number):
        plan.need([(item, before, mask) for before in range(number + 1)])
        bit = bits_of(item)[number]
        slot = slot_of(item, mask, number)
        across(item, mask ^ bit, bit, number, slot).wait_recv()
        add_into(held[item], mask, passed[item][number], slot)
        plan.now += block_bytes(item) / 8e5
        onward(item, mask, number + 1)

    squares = []

    def finish(item):
        which, begin, width, _ = items[item]
        value = held[item][0, me].astype(F32)
        for step in range(1, narrow):
            along(item, step).wait_recv()
        for slot in range(narrow - 1):
            value = value + final[item][slot].astype(F32)
        sums[which][:, pl.ds(begin, width)] = value
        squares.append(jnp.sum(value * value))

    norms[...] = jnp.zeros_like(norms)

    def norm_back(row, low, add):
        step_rows = 64

        def one(step, carry):
            rows = pl.ds(pl.multiple_of(step * step_rows, step_rows), step_rows)
            values = stash[rows, :]
            upper = d_norm[rows, :]
            centred = values - jnp.mean(values, -1, keepdims=True)
            rate = lax.rsqrt(jnp.mean(centred * centred, -1, keepdims=True) + 1e-05)
            unit = centred * rate
            norms[row : row + 1, :] += jnp.sum(upper * unit, 0, keepdims=True)
            norms[row + 3 : row + 4, :] += jnp.sum(upper, 0, keepdims=True)
            scaled = upper * gains[row : row + 1, :]
            inner = scaled - jnp.mean(scaled, -1, keepdims=True)
            inner = rate * (inner - unit * jnp.mean(scaled * unit, -1, keepdims=True))
            if add:
                inner = inner + d_res[rows, :]
            d_res[rows, :] = inner
            low[rows, :] = inner.astype(BF16)
            return carry

        lax.fori_loop(0, tokens // step_rows, one, 0)

    load(at.t5).wait()
    push(5)
    plan.now += 3.0
    load_stash(src.last).wait()
    count = D // u_rows
    tall_rows = slope_rows

    def through_unpatch(index, carry):
        ring(src.w5, at.tall, u_rows, u_cols, index, index * u_rows).wait()
        slot = at.tall.at[lax.rem(index, 2)]
        offset = pl.multiple_of(index * u_rows, u_rows)
        d_norm[:, pl.ds(offset, u_rows)] = back_mul(src.gauss[...], slot[0:u_rows, 0:u_cols])

        @pl.when(index + 2 < count)
        def _():
            ring(src.w5, at.tall, u_rows, u_cols, index + 2, (index + 2) * u_rows).start()

        return carry

    lax.fori_loop(0, count, through_unpatch, 0)
    for index in range(2):
        ring(src.w4, at.tall, tall_rows, D, index, index * tall_rows).start()
    norm_back(2, shrink_low, False)
    load_stash(src.mid).start()
    load(at.t4).wait()
    plan.now += 3.0
    push(4)
    ff = src.w3.shape[1]
    slabs = ff // tall_rows

    def through_shrink(index, carry):
        ring(src.w4, at.tall, tall_rows, D, index, index * tall_rows).wait()
        slope_load(index).wait()
        slot = lax.rem(index, 2)
        value = back_mul(shrink_low[...], at.tall[slot])
        value = value * at.slope_slots[slot].astype(F32)
        expand_low[:, pl.ds(pl.multiple_of(index * tall_rows, tall_rows), tall_rows)] = value.astype(BF16)

        @pl.when(index + 2 < slabs)
        def _():
            ring(src.w4, at.tall, tall_rows, D, index + 2, (index + 2) * tall_rows).start()
            slope_load(index + 2).start()

        return carry

    lax.fori_loop(0, slabs, through_shrink, 0)
    owners = [lax.rem(me + step, narrow) for step in list(range(1, narrow)) + [0]]
    for index in range(2):
        ring(src.w2, at.tall, head_width, D, index, owners[index] * head_width).start()
    load(at.t3).wait()
    plan.now += 6.0
    push(3)

    def through_expand(index, carry):
        ring(src.w3, at.long, 128, ff, index, index * 128).wait()
        offset = pl.multiple_of(index * 128, 128)
        d_norm[:, pl.ds(offset, 128)] = back_mul(expand_low[...], at.long[lax.rem(index, 2)])

        @pl.when(index + 2 < D // 128)
        def _():
            ring(src.w3, at.long, 128, ff, index + 2, (index + 2) * 128).start()

        return carry

    lax.fori_loop(0, D // 128, through_expand, 0)
    for index in range(2):
        ring(src.w1, at.long, 128, 3 * D, index, index * 128).start()
    load_stash(src.mid).wait()
    norm_back(1, merge_low, True)
    load_stash(src.embedded).start()

    def swap(src, dst, kind, step):
        return pltpu.make_async_remote_copy(
            src_ref=src,
            dst_ref=dst,
            send_sem=swap_send.at[kind, step],
            recv_sem=swap_recv.at[kind, step],
            device_id=place.along(step),
            device_id_type=MESH,
        )

    d_heads, away = at.d_heads, at.away
    plan.now += 7.0
    piece = 2 * halves * 2 * tokens * head_width / LINK

    def head_event():
        for step in range(1, narrow):
            swap(away.at[step - 1], d_heads.at[me], 0, step).wait_recv()

    for index, owner in enumerate(owners):
        ring(src.w2, at.tall, head_width, D, index, owner * head_width).wait()
        value = back_mul(merge_low[...], at.tall[index % 2, 0:head_width, :]).astype(BF16)
        if index < narrow - 1:
            away[index] = value
            start(swap(away.at[index], d_heads.at[me], 0, index + 1))
        else:
            d_heads[me] = value
        if index + 2 < narrow:
            ring(src.w2, at.tall, head_width, D, index + 2, owners[index + 2] * head_width).start()
    plan.now += 3.0
    plan.transfer(0, piece, (-1, 0, 0), head_event)
    load(at.t2).wait()
    push(2)
    load(at.qkv).wait()
    load(at.heads_out).wait()
    load(at.log_sums).wait()
    plan.need([(-1, 0, 0)])

    qkv, heads_out, log_sums, parts = at.qkv, at.heads_out, at.log_sums, at.parts
    key_t, key_acc, value_acc, query_acc = at.key_t, at.key_acc, at.value_acc, at.query_acc
    lane = lax.broadcasted_iota(jnp.int32, (1, LANES), 1)
    line = lax.broadcasted_iota(jnp.int32, (LANES, 1), 0)
    sides = LANES // HD
    scale = HD ** (-0.5)
    choose = lax.broadcasted_iota(jnp.int32, (8, LANES), 1) // HD
    choose = (choose == lax.broadcasted_iota(jnp.int32, (8, LANES), 0)).astype(F32)

    def part_swap(pair, step):
        lanes = pl.ds(pair * LANES, LANES)
        who = lax.rem(me + step, narrow)
        return swap(
            parts.at[who, :, :, lanes],
            mixed.at[:, :, pl.ds(pl.multiple_of(me * head_width + pair * LANES, LANES), LANES)],
            1 + pair,
            step,
        )

    def part_event(pair):
        for step in range(1, narrow):
            part_swap(pair, step).wait_recv()

    for pair in range(head_width // LANES):
        lanes = pl.ds(pair * LANES, LANES)
        key_t[...] = qkv[:, 1, :, lanes].reshape(length, LANES).T
        key_acc[...] = jnp.zeros_like(key_acc)
        value_acc[...] = jnp.zeros_like(value_acc)
        def one_block(step, lanes=lanes, pair=pair):
            who = lax.rem(me + step, narrow)
            query = qkv[who, 0, :, lanes].astype(F32)
            upper = d_heads[who, :, lanes].astype(F32)
            kept = heads_out[who, :, lanes].astype(F32)
            delta = lax.dot_general(
                choose,
                upper * kept,
                (((1,), (1,)), ((), ())),
                precision=HIGHEST,
                preferred_element_type=F32,
            )
            log_rows = log_sums[who].T[pair * sides : (pair + 1) * sides, :]
            own_query = [(query * jnp.where(lane // HD == side, scale, 0.0)).astype(BF16) for side in range(sides)]
            own_upper = [(upper * jnp.where(lane // HD == side, 1.0, 0.0)).astype(BF16) for side in range(sides)]
            query_acc[...] = jnp.zeros_like(query_acc)

            def block(source, carry):
                rows = pl.ds(pl.multiple_of(source * tokens, tokens), tokens)
                key, value = qkv[source, 1, :, lanes], qkv[source, 2, :, lanes]
                key_turned = key_t[:, rows].astype(F32)
                for side in range(sides):
                    scores = back_mul(key, own_query[side])
                    probs = jnp.exp(scores - log_rows[side : side + 1, :])
                    d_probs = back_mul(value, own_upper[side])
                    d_scores = (probs * (d_probs - delta[side : side + 1, :])).astype(BF16)
                    value_acc[rows, :] += matmul(probs.astype(BF16), own_upper[side])
                    key_acc[rows, :] += matmul(d_scores, own_query[side])
                    turned = (key_turned * jnp.where(line // HD == side, scale, 0.0)).astype(BF16)
                    query_acc[...] += matmul(turned, d_scores)
                return carry

            lax.fori_loop(0, narrow, block, 0)
            parts[who, 0, :, lanes] = query_acc[...].T.astype(BF16)
        for step in range(narrow):
            plan.work(3.0, functools.partial(one_block, step))
        for source in range(narrow):
            rows = pl.ds(source * tokens, tokens)
            parts[source, 1, :, lanes] = key_acc[rows, :].astype(BF16)
            parts[source, 2, :, lanes] = value_acc[rows, :].astype(BF16)
        for step in range(1, narrow):
            start(part_swap(pair, step))
        plan.now += 1.0
        plan.transfer(0, 1.5 * piece, (-2, 0, pair), functools.partial(part_event, pair))
        mixed[:, :, pl.ds(pl.multiple_of(me * head_width + pair * LANES, LANES), LANES)] = parts[me, :, :, lanes]
    load(at.t1).wait()
    plan.need([(-2, 0, pair) for pair in range(head_width // LANES)])
    for part in range(3):
        push(1, part)

    def through_mixer(index, carry):
        ring(src.w1, at.long, 128, 3 * D, index, index * 128).wait()
        slot = lax.rem(index, 2)
        value = back_mul(mixed[0], at.long[slot, :, 0:D])
        for part in range(1, 3):
            value = value + back_mul(mixed[part], at.long[slot, :, part * D : (part + 1) * D])
        d_norm[:, pl.ds(pl.multiple_of(index * 128, 128), 128)] = value

        @pl.when(index + 2 < D // 128)
        def _():
            ring(src.w1, at.long, 128, 3 * D, index + 2, (index + 2) * 128).start()

        return carry

    plan.work(4.0, lambda: lax.fori_loop(0, D // 128, through_mixer, 0))
    load_stash(src.embedded).wait()
    plan.work(3.0, lambda: norm_back(0, at.embed_low, True))
    at.embed_t[...] = at.embed_low[...].T
    turned = jnp.concatenate([norms[...], jnp.zeros((LANES - 8, D), F32)], 0).T
    at.extra[...] = pltpu.roll(turned, lead, 1)
    push(0)
    plan.finish()

    rows = lax.broadcasted_iota(jnp.int32, (8, LANES), 0)
    wide_tiles, narrow_tiles = at.wide_tiles, at.narrow_tiles
    wide_tiles[place.w] = jnp.where(rows == 0, src.term[...], sum(squares))

    def tile_copy(buffer, index, slot, peer):
        return pltpu.make_async_remote_copy(
            src_ref=buffer.at[index],
            dst_ref=buffer.at[index],
            send_sem=tile_send.at[slot],
            recv_sem=tile_recv.at[slot],
            device_id=peer,
            device_id_type=MESH,
        )

    for step in range(1, wide):
        start(tile_copy(wide_tiles, place.w, step - 1, (lax.rem(place.w + step, wide), place.n)))
    for step in range(1, wide):
        tile_copy(wide_tiles, place.w, step - 1, (lax.rem(place.w + step, wide), place.n)).wait_recv()
    whole = wide_tiles[0]
    for index in range(1, wide):
        whole = whole + wide_tiles[index]
    narrow_tiles[place.n] = whole
    for step in range(1, narrow):
        start(tile_copy(narrow_tiles, place.n, wide + step - 1, place.along(step)))
    for step in range(1, narrow):
        tile_copy(narrow_tiles, place.n, wide + step - 1, place.along(step)).wait_recv()
    whole = narrow_tiles[0]
    for index in range(1, narrow):
        whole = whole + narrow_tiles[index]
    totals[...] = whole
    for copy in list(last_sent.values()) + started:
        copy.wait_send()


def backward_all(kept, patches, gauss, term, lead, wide, narrow):
    tokens = patches.shape[0]
    chips = wide // 2
    weights = [kept.w1, kept.w2, kept.w3, kept.w4, kept.w5]
    heights = [D] + [weight.shape[0] for weight in weights]
    widths = [patches.shape[1]] + [weight.shape[1] for weight in weights]
    rows = [height // (wide * narrow) for height in heights]
    head_width = D // narrow
    length = narrow * tokens
    items = backward_plan(widths)
    slots = 2 * chips + narrow - 1
    streamed = dict(w1=kept.w1, w2=kept.w2, w3=kept.w3, w4=kept.w4, w5=kept.w5)
    streamed.update(last=kept.last, mid=kept.mid, embedded=kept.embedded, slopes=kept.slopes)
    loaded = dict(t5=kept.t5, t4=kept.t4, t3=kept.t3, t2=kept.t2, t1=kept.t1)
    loaded.update(qkv=kept.qkv, heads_out=kept.heads_out, log_sums=kept.log_sums)
    whole = dict(gains=kept.gains, patches=patches, gauss=gauss, term=term)
    operands = {**streamed, **loaded, **whole}
    shapes = [jax.ShapeDtypeStruct((rows[which], widths[which]), F32) for which in range(6)]
    shapes.append(jax.ShapeDtypeStruct((8, LANES), F32))
    scratch = {name: pltpu.VMEM(value.shape, value.dtype) for name, value in loaded.items()}
    scratch.update(
        embed_t=pltpu.VMEM((D, tokens), BF16),
        embed_low=pltpu.VMEM((tokens, D), BF16),
        stash=pltpu.VMEM((tokens, D), F32),
        d_res=pltpu.VMEM((tokens, D), F32),
        d_norm=pltpu.VMEM((tokens, D), F32),
        norms=pltpu.VMEM((8, D), F32),
        extra=pltpu.VMEM((D, LANES), F32),
        shrink_low=pltpu.VMEM((tokens, D), BF16),
        expand_low=pltpu.VMEM((tokens, widths[3]), BF16),
        merge_low=pltpu.VMEM((tokens, D), BF16),
        mixed=pltpu.VMEM((3, tokens, D), BF16),
        tall=pltpu.VMEM((2, 512, D), BF16),
        long=pltpu.VMEM((2, 128, widths[3]), BF16),
        slope_slots=pltpu.VMEM((2, tokens, 512), BF16),
        d_heads=pltpu.VMEM((narrow, tokens, head_width), BF16),
        away=pltpu.VMEM((narrow - 1, tokens, head_width), BF16),
        parts=pltpu.VMEM((narrow, 3, tokens, head_width), BF16),
        key_t=pltpu.VMEM((LANES, length), BF16),
        key_acc=pltpu.VMEM((length, LANES), F32),
        value_acc=pltpu.VMEM((length, LANES), F32),
        query_acc=pltpu.VMEM((LANES, tokens), F32),
        wide_tiles=pltpu.VMEM((wide, 8, LANES), F32),
        narrow_tiles=pltpu.VMEM((narrow, 8, LANES), F32),
        send_sem=pltpu.SemaphoreType.DMA((len(items), slots)),
        recv_sem=pltpu.SemaphoreType.DMA((len(items), slots)),
        tile_send=pltpu.SemaphoreType.DMA((wide + narrow,)),
        tile_recv=pltpu.SemaphoreType.DMA((wide + narrow,)),
        swap_send=pltpu.SemaphoreType.DMA((1 + head_width // LANES, narrow)),
        swap_recv=pltpu.SemaphoreType.DMA((1 + head_width // LANES, narrow)),
        in_sem=pltpu.SemaphoreType.DMA((9,)),
        ring_sem=pltpu.SemaphoreType.DMA((3, 2)),
    )
    lists = [pltpu.VMEM((chips, narrow, rows[which], width), BF16) for which, _, width, _ in items]
    for which, _, width, _ in items:
        for bit in chip_bits(chips):
            lists.append(pltpu.VMEM((chips // (2 * bit), narrow, rows[which], width), BF16))
    lists += [pltpu.VMEM((narrow - 1, rows[which], width), BF16) for which, _, width, _ in items]
    for which in range(6):
        widest = max(width for owner, _, width, _ in items if owner == which)
        lists.append(pltpu.VMEM((chips, narrow, rows[which], widest), BF16))
    vmem = pl.BlockSpec(memory_space=pltpu.VMEM)
    hbm = pl.BlockSpec(memory_space=pl.ANY)
    return pl.pallas_call(
        functools.partial(backward_kernel, items, wide, narrow, lead, tuple(operands), tuple(scratch)),
        out_shape=shapes,
        in_specs=[vmem if name in whole else hbm for name in operands],
        out_specs=[vmem] * len(shapes),
        scratch_shapes=list(scratch.values()) + lists,
        compiler_params=pltpu.CompilerParams(
            collective_id=1, has_side_effects=True, vmem_limit_bytes=63 * MIB
        ),
        name="backward",
    )(*operands.values())


def render_kernel(
    gauss_ref, weight_ref, target_ref, mask_ref, pair_ref, view_ref, total_ref, grad_ref, term_ref, feat, dfeat
):
    quads = gauss_ref.shape[0] // NVIEW
    span = weight_ref.shape[1]
    pairs = pair_ref.shape[1]
    scale = 1.0 / total_ref[0].astype(F32)

    def channel(index):
        return gauss_ref[:, index * PP : (index + 1) * PP]

    def shared():
        opacity = jax.nn.sigmoid(channel(3))
        extent = jax.nn.sigmoid(channel(5) + channel(6) + channel(7))
        lead = channel(8)
        denom = 1.0 + lead * lead + channel(9) * channel(9) + channel(10) * channel(10) + channel(11) * channel(11)
        facing = lead * lead / denom
        raw = channel(4)
        depth = jnp.maximum(raw, 0.0) + jnp.log1p(jnp.exp(-jnp.abs(raw)))
        return opacity, extent, lead, denom, facing, raw, depth

    opacity, extent, lead, denom, facing, raw, depth = shared()
    footprint = opacity * extent * facing
    channels = [jax.nn.sigmoid(channel(index)) * footprint for index in range(3)]
    channels += [footprint, depth * footprint]
    for index, value in enumerate(channels):
        for view in range(NVIEW):
            feat[index * quads : (index + 1) * quads, view * PP : (view + 1) * PP] = value[
                view * quads : (view + 1) * quads
            ]
    rendered = jnp.dot(feat[...], weight_ref[...], precision=HIGHEST, preferred_element_type=F32)
    parts = [rendered[index * quads : (index + 1) * quads] for index in range(5)]
    lane = lax.broadcasted_iota(jnp.int32, (quads, span), 1)
    live = jnp.where(lane < view_ref[0] * PP, mask_ref[...], 0).astype(F32)
    term = jnp.zeros((quads, span), F32)
    slopes = []
    for index in range(3):
        error = parts[index] - target_ref[index * quads : (index + 1) * quads, :].astype(F32)
        term = term + live * error * error
        slopes.append(2.0 * scale * live * error)
    below = 1.0 + parts[3]
    depth_out = parts[4] / below

    first, second = pair_ref[0:1, :], pair_ref[1:2, :]
    least = jnp.minimum(first, second)
    down = (jnp.abs(first - second) == P_SIZE).astype(jnp.int32)
    place = quads * PP
    slot, local = least // place, least % place
    high = down * quads + local // PP
    low = slot * PP + local % PP
    high_hot = (lax.broadcasted_iota(jnp.int32, (2 * quads, pairs), 0) == high).astype(F32).astype(BF16)
    low_hot = (lax.broadcasted_iota(jnp.int32, (span, pairs), 0) == low).astype(F32).astype(BF16)
    counts = back_mul(high_hot, low_hot)
    slope = jnp.zeros((quads, span), F32)
    for which, shift in enumerate((1, P_SIZE)):
        count = counts[which * quads : (which + 1) * quads]
        weight = DEPTH_WEIGHT * count * live * pltpu.roll(live, span - shift, 1)
        gap = depth_out - pltpu.roll(depth_out, span - shift, 1)
        term = term + weight * gap * gap
        pull = 2.0 * scale * weight * gap
        slope = slope + pull - pltpu.roll(pull, shift, 1)
    term_ref[...] = jnp.full(term_ref.shape, jnp.sum(term), F32)
    over = slope / below
    slopes += [-over * depth_out, over]
    stacked = jnp.concatenate(slopes, 0)
    dfeat[...] = lax.dot_general(
        stacked, weight_ref[...], (((1,), (1,)), ((), ())), precision=HIGHEST, preferred_element_type=F32
    )

    def feature_grad(index):
        return jnp.concatenate(
            [
                dfeat[index * quads : (index + 1) * quads, view * PP : (view + 1) * PP]
                for view in range(NVIEW)
            ],
            0,
        )

    def put(index, value):
        grad_ref[:, index * PP : (index + 1) * PP] = value.astype(BF16)

    d_foot = feature_grad(3)
    for index in range(3):
        tint = jax.nn.sigmoid(channel(index))
        upper = feature_grad(index)
        d_foot = d_foot + upper * tint
        put(index, upper * footprint * tint * (1.0 - tint))
    d_last = feature_grad(4)
    d_foot = d_foot + d_last * depth
    put(3, d_foot * extent * facing * opacity * (1.0 - opacity))
    put(4, d_last * footprint * jax.nn.sigmoid(raw))
    d_extent = d_foot * opacity * facing * extent * (1.0 - extent)
    for index in (5, 6, 7):
        put(index, d_extent)
    d_facing = d_foot * opacity * extent
    put(8, d_facing * 2.0 * lead / denom * (1.0 - facing))
    for index in (9, 10, 11):
        put(index, -2.0 * d_facing * facing / denom * channel(index))


def render(gaussians, weights, targets, mask, pairs, view_count, pair_total):
    rows = gaussians.shape[0]
    quads = rows // NVIEW
    slots, views = weights.shape[:2]
    spread = weights.transpose(1, 2, 0, 3).reshape(views * PP, slots * PP)
    wanted = targets.reshape(slots, 3, quads, PP).transpose(1, 2, 0, 3).reshape(3 * quads, slots * PP)
    valid = mask.reshape(slots, quads, PP).transpose(1, 0, 2).reshape(quads, slots * PP)
    vmem = pl.BlockSpec(memory_space=pltpu.VMEM)
    smem = pl.BlockSpec(memory_space=pltpu.SMEM)
    return pl.pallas_call(
        render_kernel,
        out_shape=[
            jax.ShapeDtypeStruct(gaussians.shape, BF16),
            jax.ShapeDtypeStruct((8, LANES), F32),
        ],
        in_specs=[vmem] * 5 + [smem] * 2,
        out_specs=[vmem] * 2,
        scratch_shapes=[pltpu.VMEM((5 * quads, views * PP), F32)] * 2,
        compiler_params=pltpu.CompilerParams(vmem_limit_bytes=48 * MIB),
        name="render",
    )(gaussians, spread, wanted, valid, pairs, view_count, pair_total)


def forward_plain(shards, patches, features, kinds):
    weights = [lax.all_gather(shard, BOTH, axis=0, tiled=True) for shard in shards]
    groups = lax.axis_size(NARROW)
    rows = patches.shape[0]
    gains = weights[0][:, features : features + kinds].T.astype(F32)
    embedded = back_mul(patches[:, :features], weights[0][:, :features])
    normed_one = layer_norm(embedded, gains[0], gains[3]).astype(BF16)
    mixed = matmul(normed_one, weights[1]).astype(BF16).reshape(rows, 3, groups, -1)
    mixed = mixed.transpose(2, 1, 0, 3)
    qkv = lax.all_to_all(mixed, NARROW, split_axis=0, concat_axis=0, tiled=True)
    width = qkv.shape[-1]
    length = groups * rows
    heads = width // HD
    parts = [qkv[:, part].reshape(length, heads, HD) for part in range(3)]
    attended, logsum = attention_forward(*parts)
    log_sums = logsum.transpose(0, 2, 1).reshape(groups, rows, heads)
    returned = lax.all_to_all(
        attended.reshape(groups, rows, width), NARROW, split_axis=0, concat_axis=0, tiled=True
    )
    returned = returned.transpose(1, 0, 2).reshape(rows, D)
    mid = embedded + matmul(returned, weights[2])
    normed_two = layer_norm(mid, gains[1], gains[4]).astype(BF16)
    expanded = matmul(normed_two, weights[3])
    half = 0.5 * (1.0 + lax.erf(expanded * (0.5**0.5)))
    activated = (expanded * half).astype(BF16)
    bell = jnp.exp(-0.5 * expanded * expanded) * 0.3989422804014327
    slopes = (half + expanded * bell).astype(BF16)
    last = mid + matmul(activated, weights[4])
    normed_three = layer_norm(last, gains[2], gains[5]).astype(BF16)
    return Bag(
        dict(
        w1=weights[1],
        w2=weights[2],
        w3=weights[3],
        w4=weights[4],
        w5=weights[5],
        gains=gains,
        embedded=embedded,
        mid=mid,
        last=last,
        slopes=slopes,
        t1=normed_one.T,
        t2=returned.T,
        t3=normed_two.T,
        t4=activated.T,
        t5=normed_three.T,
        qkv=qkv,
        heads_out=attended,
        log_sums=log_sums,
        gaussians=matmul(normed_three, weights[5]),
    ).items())


def backward_plain(kept, patches, gauss_low, term, features, kinds):
    gains = kept.gains
    weights = [None, kept.w1, kept.w2, kept.w3, kept.w4, kept.w5]
    norm_back_one = jax.vjp(layer_norm, kept.embedded, gains[0], gains[3])[1]
    norm_back_two = jax.vjp(layer_norm, kept.mid, gains[1], gains[4])[1]
    norm_back_three = jax.vjp(layer_norm, kept.last, gains[2], gains[5])[1]
    qkv = kept.qkv
    groups, _, rows, width = qkv.shape
    length = groups * rows
    heads = width // HD
    queries, keys, values = (qkv[:, part].reshape(length, heads, HD) for part in range(3))
    blocked = min(512, length)
    logsum = kept.log_sums[:, :, :heads].reshape(length // blocked, blocked, heads)
    residual_grad, gain_three, shift_three = norm_back_three(back_mul(gauss_low, weights[5]))
    shrink_low = residual_grad.astype(BF16)
    expand_low = (back_mul(shrink_low, weights[4]) * kept.slopes.astype(F32)).astype(BF16)
    through_two, gain_two, shift_two = norm_back_two(back_mul(expand_low, weights[3]))
    residual_grad = residual_grad + through_two
    merge_low = residual_grad.astype(BF16)
    out_grad = back_mul(merge_low, weights[2]).astype(BF16).reshape(rows, groups, width)
    head_grad = lax.all_to_all(
        out_grad.transpose(1, 0, 2), NARROW, split_axis=0, concat_axis=0, tiled=True
    ).reshape(length, heads, HD)
    grads = attention_backward(queries, keys, values, logsum.transpose(0, 2, 1), head_grad)
    stacked = jnp.stack(grads, 1).astype(BF16).reshape(groups, rows, 3, width)
    mixed_grad = lax.all_to_all(stacked, NARROW, split_axis=0, concat_axis=0, tiled=True)
    mixed_grad = mixed_grad.transpose(1, 2, 0, 3).reshape(rows, 3 * D)
    through_one, gain_one, shift_one = norm_back_one(back_mul(mixed_grad, weights[1]))
    embed_grad = (residual_grad + through_one).astype(BF16)
    grad_norms = jnp.stack([gain_one, gain_two, gain_three, shift_one, shift_two, shift_three])
    lefts = [embed_grad.T] + [kept.t1, kept.t2, kept.t3, kept.t4, kept.t5]
    rights = [patches, mixed_grad, merge_low, expand_low, shrink_low, gauss_low]
    products = [matmul(left, right) for left, right in zip(lefts, rights)]
    products[0] = products[0].at[:, features : features + kinds].add(grad_norms.T)
    sums = [
        lax.psum_scatter(
            product.astype(BF16), BOTH, scatter_dimension=0, tiled=True
        ).astype(F32)
        for product in products
    ]
    squares = sum(jnp.sum(part * part) for part in sums)
    loss_sum, square_sum = lax.psum((term[0, 0], squares), BOTH)
    return sums, loss_sum, square_sum


def update_kernel(features, total_ref, sums_ref, *refs):
    grads, refs = refs[:6], refs[6:]
    olds, news = refs[:21], refs[21:42]
    loss_ref, norm_ref, turned = refs[42:]
    square_sum = sums_ref[1:2, 0:1]
    grad_norm = jnp.sqrt(square_sum)
    factor = jnp.minimum(1.0, CLIP_NORM / (grad_norm + 1e-06))
    norm_ref[...] = grad_norm
    loss_ref[...] = sums_ref[0:1, 0:1] / total_ref[0].astype(F32)
    width = grads[0].shape[1]
    turned[...] = grads[0][:, width - LANES :].T
    for which in range(7):
        weight, first, second = olds[3 * which : 3 * which + 3]
        rows, columns = weight.shape
        chunk = min(8, rows)

        def one(step, carry):
            spot = pl.ds(pl.multiple_of(step * chunk, chunk), chunk)
            if which == 0:
                grad = grads[0][spot, 0:columns]
            elif which == 6:
                grad = turned[features % LANES : features % LANES + rows, 0:columns]
            else:
                grad = grads[which][spot, :]
            values = adamw(weight[spot, :], first[spot, :], second[spot, :], grad * factor, RATES[which])
            for dest, value in zip(news[3 * which : 3 * which + 3], values):
                dest[spot, :] = value
            return carry

        lax.fori_loop(0, rows // chunk, one, 0)


def update_all(olds, sums, totals, pair_total, features):
    vmem = pl.BlockSpec(memory_space=pltpu.VMEM)
    smem = pl.BlockSpec(memory_space=pltpu.SMEM)
    shapes = [jax.ShapeDtypeStruct(old.shape, F32) for old in olds]
    return pl.pallas_call(
        functools.partial(update_kernel, features),
        out_shape=shapes + [jax.ShapeDtypeStruct((1, 1), F32)] * 2,
        in_specs=[smem] + [vmem] * 28,
        out_specs=[vmem] * 23,
        scratch_shapes=[pltpu.VMEM((LANES, sums[0].shape[0]), F32)],
        compiler_params=pltpu.CompilerParams(vmem_limit_bytes=40 * MIB),
        name="update",
    )(pair_total, totals, *sums, *olds)


def body(
    views,
    render_w,
    targets,
    pix_mask,
    pairs,
    view_count,
    pair_total,
    embed_weight,
    embed_first,
    embed_second,
    mixer_weight,
    mixer_first,
    mixer_second,
    merge_weight,
    merge_first,
    merge_second,
    expand_weight,
    expand_first,
    expand_second,
    shrink_weight,
    shrink_first,
    shrink_second,
    unpatch_weight,
    unpatch_first,
    unpatch_second,
    norm_params,
    norm_first,
    norm_second,
):
    masters = (embed_weight, mixer_weight, merge_weight, expand_weight, shrink_weight, unpatch_weight, norm_params)
    firsts = (embed_first, mixer_first, merge_first, expand_first, shrink_first, unpatch_first, norm_first)
    seconds = (embed_second, mixer_second, merge_second, expand_second, shrink_second, unpatch_second, norm_second)
    groups = lax.axis_size(NARROW)
    wide_count = lax.axis_size(WIDE)
    features = embed_weight.shape[0]
    kinds = norm_params.shape[0]
    padded = -(-(features + kinds) // LANES) * LANES
    fill = padded - features - kinds
    by_kernel = mixer_weight.shape[0] % 16 == 0

    patches = views.reshape(-1, features)
    rows = patches.shape[0]
    patches = jnp.pad(patches, ((0, 0), (0, padded - features)))
    if by_kernel:
        raw = (embed_weight.T,) + masters[1:6]
        kept = forward_all(raw, norm_params, patches, features % LANES, wide_count, groups)
    else:
        first_shard = jnp.concatenate([embed_weight.T, norm_params.T], 1)
        first_shard = jnp.pad(first_shard.astype(BF16), ((0, 0), (0, fill)))
        shards = [first_shard] + [weight.astype(BF16) for weight in masters[1:6]]
        kept = forward_plain(shards, patches, features, kinds)
    divisor = pair_total[0].astype(F32)
    gauss_low, term = render(
        kept.gaussians, render_w[0], targets[0], pix_mask[0], pairs[0], view_count, pair_total
    )
    if by_kernel:
        *sums, totals = backward_all(
            kept, patches, gauss_low, term, features % LANES, wide_count, groups
        )
        olds = []
        for triple in zip(masters, firsts, seconds):
            olds += triple
        olds[:3] = [old.T for old in olds[:3]]
        *news, loss, grad_norm = update_all(olds, sums, totals, pair_total, features)
        news[:3] = [new.T for new in news[:3]]
        return tuple(news) + (loss[0, 0], grad_norm[0, 0])
    sums, loss_sum, square_sum = backward_plain(kept, patches, gauss_low, term, features, kinds)
    first_sum = sums[0].T
    grads = [first_sum[:features]] + list(sums[1:]) + [first_sum[features : features + kinds]]
    loss = loss_sum / divisor
    grad_norm = jnp.sqrt(square_sum)
    factor = jnp.minimum(1.0, CLIP_NORM / (grad_norm + 1e-06))
    results = []
    for which in range(7):
        results += adamw(masters[which], firsts[which], seconds[which], grads[which] * factor, RATES[which])
    return tuple(results) + (loss, grad_norm)


def solution(mesh):
    columns = P(None, BOTH)
    rows = P(BOTH, None)
    weights = (columns,) * 3 + (rows,) * 15 + (columns,) * 3
    return jax.shard_map(
        body,
        mesh=mesh,
        in_specs=(
            P(WIDE, None, NARROW, None),
            P(WIDE, None, None, None, None),
            P(WIDE, None, None, NARROW),
            P(WIDE, None, NARROW),
            P(WIDE, None, NARROW),
            P(WIDE),
            P(),
        )
        + weights,
        out_specs=weights + (P(), P()),
        check_vma=False,
    )
```

```python
import functools
import heapq

import jax
import jax.numpy as jnp
from jax import lax
from jax.experimental import pallas as pl
from jax.experimental.pallas import tpu as pltpu
from jax.sharding import PartitionSpec as P

D = 1024
HD = 64
P_SIZE = 8
PP = 64
NVIEW = 4
TMAX = 12
STEP = 10
LANES = 128
MIB = 1024 * 1024

DEPTH_WEIGHT = 1.0
CLIP_NORM = 0.01
BETA_ONE = 0.9
BETA_TWO = 0.95
ADAM_EPS = 1e-08
DECAY = 0.05
RATES = (0.05, 0.05, 0.5, 0.05, 0.05, 0.05, 0.8)
MESH = pl.DeviceIdType.MESH
WIDE, NARROW = BOTH = ("wide", "narrow")
HIGHEST = lax.Precision.HIGHEST
F32 = jnp.float32
BF16 = jnp.bfloat16


def matmul(left, right):
    return jnp.dot(left, right, preferred_element_type=F32)


def outer_sum(left, right):
    return lax.dot_general(left, right, (((0,), (0,)), ((), ())), preferred_element_type=F32)


def back_mul(grad, weight):
    return lax.dot_general(grad, weight, (((1,), (1,)), ((), ())), preferred_element_type=F32)


def layer_norm(values, gain, shift):
    centred = values - jnp.mean(values, -1, keepdims=True)
    spread = jnp.mean(centred * centred, -1, keepdims=True)
    return centred * lax.rsqrt(spread + 1e-05) * gain + shift


def exact_gelu(values):
    return jax.nn.gelu(values, approximate=False)


def attention_forward(queries, keys, values):
    length, heads = (queries.shape[0], queries.shape[1])
    blocked = min(512, length)
    scale = HD ** (-0.5)

    def one_block(query_block):
        scores = (
            jnp.einsum("qhd,khd->hqk", query_block, keys, preferred_element_type=jnp.float32)
            * scale
        )
        highest = jnp.max(scores, -1, keepdims=True)
        exponentials = jnp.exp(scores - highest)
        summed = jnp.sum(exponentials, -1, keepdims=True)
        softmaxed = (exponentials / summed).astype(jnp.bfloat16)
        output = jnp.einsum("hqk,khd->qhd", softmaxed, values, preferred_element_type=jnp.float32)
        return (output.astype(jnp.bfloat16), (highest + jnp.log(summed))[:, :, 0])

    output, logsum = lax.map(one_block, queries.reshape(length // blocked, blocked, heads, HD))
    return (output.reshape(length, heads * HD), logsum)


def attention_backward(queries, keys, values, logsum, out_grad):
    length, heads = (queries.shape[0], queries.shape[1])
    blocked = min(512, length)
    scale = HD ** (-0.5)

    def one_block(carry, inputs):
        key_grad, value_grad = carry
        query_block, logsum_block, grad_block = inputs
        scores = (
            jnp.einsum("qhd,khd->hqk", query_block, keys, preferred_element_type=jnp.float32)
            * scale
        )
        softmaxed = jnp.exp(scores - logsum_block[:, :, None])
        value_grad = value_grad + jnp.einsum(
            "hqk,qhd->khd",
            softmaxed.astype(jnp.bfloat16),
            grad_block,
            preferred_element_type=jnp.float32,
        )
        prob_grad = jnp.einsum(
            "qhd,khd->hqk", grad_block, values, preferred_element_type=jnp.float32
        )
        score_grad = softmaxed * (prob_grad - jnp.sum(softmaxed * prob_grad, -1, keepdims=True))
        score_low = score_grad.astype(jnp.bfloat16)
        query_grad = (
            jnp.einsum("hqk,khd->qhd", score_low, keys, preferred_element_type=jnp.float32) * scale
        )
        key_grad = (
            key_grad
            + jnp.einsum("hqk,qhd->khd", score_low, query_block, preferred_element_type=jnp.float32)
            * scale
        )
        return ((key_grad, value_grad), query_grad)

    zeros = jnp.zeros((length, heads, HD), jnp.float32)
    shaped = (
        queries.reshape(length // blocked, blocked, heads, HD),
        logsum,
        out_grad.reshape(length // blocked, blocked, heads, HD),
    )
    (key_grad, value_grad), query_grad = lax.scan(one_block, (zeros, zeros), shaped)
    return (query_grad.reshape(length, heads, HD), key_grad, value_grad)


def adamw(weight, first, second, grad, rate):
    first = BETA_ONE * first + (1.0 - BETA_ONE) * grad
    second = BETA_TWO * second + (1.0 - BETA_TWO) * grad * grad
    first_hat = first / (1.0 - BETA_ONE**STEP)
    second_hat = second / (1.0 - BETA_TWO**STEP)
    weight = weight - rate * (first_hat / (jnp.sqrt(second_hat) + ADAM_EPS) + DECAY * weight)
    return (weight, first, second)


def chip_bits(chips):
    bits, step = [], 1
    while step < chips:
        bits.append(step)
        step *= 2
    return bits


def flip(chip, mask):
    for bit in chip_bits(mask + 1):
        if mask & bit:
            chip = chip + (1 - 2 * (chip // bit % 2)) * bit
    return chip


def column_halves(width):
    first = -(-width // (2 * LANES)) * LANES
    return ((0, first), (first, width - first))


def work_items(widths, order):
    return [(which,) + half + (side,) for which in order for side, half in enumerate(column_halves(widths[which]))]


class Bag:
    def __init__(self, pairs):
        vars(self).update(pairs)


class Place:
    def __init__(self, wide, narrow):
        self.wide, self.narrow = wide, narrow
        self.chips = wide // 2
        self.bits = chip_bits(self.chips)
        self.w = lax.axis_index(WIDE)
        self.n = lax.axis_index(NARROW)
        self.chip = self.w // 2
        self.core = self.w % 2
        self.twin = (2 * self.chip + 1 - self.core, self.n)

    def across(self, mask):
        return (2 * flip(self.chip, mask) + self.core, self.n)

    def along(self, step):
        return (self.w, lax.rem(self.n + step, self.narrow))

    def neighbours(self):
        return (
            [self.twin]
            + [self.across(bit) for bit in self.bits]
            + [self.along(step) for step in range(1, self.narrow)]
        )


class Planner:
    def __init__(self):
        self.now, self.count = 0.0, 0
        self.free, self.events, self.done, self.spare = {}, [], set(), []
        self.refill = lambda: None

    def transfer(self, link, cost, key, event):
        self.free[link] = max(self.now, self.free.get(link, 0.0)) + cost
        self.count += 1
        heapq.heappush(self.events, (self.free[link] + 2.0, self.count, key, event))

    def step(self):
        when, _, key, event = heapq.heappop(self.events)
        self.now = max(self.now, when) + 0.2
        event()
        self.done.add(key)
        self.refill()

    def fill(self, until):
        for index, (keys, cost, work) in enumerate(self.spare):
            if self.now + cost <= until and self.done.issuperset(keys):
                del self.spare[index]
                work()
                self.now += cost
                return True
        return False

    def need(self, keys):
        while not self.done.issuperset(keys):
            if not self.fill(self.events[0][0]):
                self.step()

    def work(self, cost, work):
        while self.events and self.events[0][0] <= self.now:
            self.step()
        self.refill()
        work()
        self.now += cost

    def later(self, cost, work, keys=()):
        entry = (tuple(keys), cost, work)
        self.spare.append(entry)
        return entry

    def force(self, entry):
        if entry in self.spare:
            self.spare.remove(entry)
            self.work(entry[1], entry[2])

    def finish(self):
        self.refill()
        while self.events or self.spare:
            if not self.fill(self.events[0][0] if self.events else 1e9):
                self.step()


LINK = 100e3
Z_AHEAD = 4.0
TWIN_LINK = 600e3


def greet(peers):
    barrier = pltpu.get_barrier_semaphore()
    for peer in peers:
        pl.semaphore_signal(barrier, inc=1, device_id=peer, device_id_type=MESH)
    pl.semaphore_wait(barrier, len(peers))


def normalize(values, gain, shift):
    centred = values - jnp.mean(values, -1, keepdims=True)
    spread = jnp.mean(centred * centred, -1, keepdims=True)
    return centred * lax.rsqrt(spread + 1e-05) * gain + shift


def forward_plan(widths):
    items = []
    for which, cuts in ((0, 1), (1, 3), (2, 1), (3, 2), (5, 1), (4, 2)):
        size = widths[which] // cuts
        for cut in range(cuts):
            for side, (start, width) in enumerate(column_halves(size)):
                items.append((which, cut * size + start, width, side))
    return items


def forward_kernel(items, wide, narrow, lead, ins, outs, scratch, *refs):
    at = Bag(zip(ins + scratch, refs[: len(ins)] + refs[len(ins) + len(outs) :]))
    results = refs[len(ins) : len(ins) + len(outs)]
    weights = [at.first_weight, at.w1, at.w2, at.w3, at.w4, at.w5]
    shards = [at.c0, at.c1, at.c2, at.c3, at.c4, at.c5]
    raw = [at.s0, at.s1, at.s2, at.s3, at.s4, at.s5]
    own_sem, send_sem, recv_sem = at.own_sem, at.send_sem, at.recv_sem
    swap_send, swap_recv, out_sem = at.swap_send, at.swap_recv, at.out_sem
    place = Place(wide, narrow)
    chips, me = place.chips, place.n
    tokens = at.patches.shape[0]
    head_width = D // narrow
    total = len(items)
    started, guarded = [], []

    def start(copy):
        copy.start()
        started.append(copy)

    features = at.s0.shape[1]
    tail = shards[0].shape[1] - LANES
    kinds = at.norm_raw.shape[0]
    kind = lax.broadcasted_iota(jnp.int32, (kinds, LANES), 0)
    spot = lax.broadcasted_iota(jnp.int32, (kinds, LANES), 1)
    put = (spot == kind + lead).astype(F32).astype(BF16)
    shards[0][:, tail:] = outer_sum(at.norm_raw[...].astype(BF16), put).astype(BF16)
    shards[0][:, 0:features] = at.s0[...].astype(BF16)
    for source, dest in zip(raw[1:], shards[1:]):
        dest[...] = source[...].astype(BF16)
    greet(place.neighbours())
    rows_of = [shard.shape[0] for shard in shards]

    def rows_at(which, chip, core, node=None):
        rows = rows_of[which]
        if node is None:
            return pl.ds(pl.multiple_of((chip * 2 + core) * narrow * rows, rows), narrow * rows)
        return pl.ds(pl.multiple_of(((chip * 2 + core) * narrow + node) * rows, rows), rows)

    own = []
    for which in range(6):
        copy = pltpu.make_async_copy(
            shards[which], weights[which].at[rows_at(which, place.chip, place.core, me), :], own_sem.at[which]
        )
        copy.start()
        own.append(copy)

    def remote(item, src, dst, slot, peer):
        return pltpu.make_async_remote_copy(
            src_ref=src,
            dst_ref=dst,
            send_sem=send_sem.at[item, slot],
            recv_sem=recv_sem.at[item, slot],
            device_id=peer,
            device_id_type=MESH,
        )

    def group(item, mask):
        which, begin, width, _ = items[item]
        return weights[which].at[rows_at(which, flip(place.chip, mask), place.core), pl.ds(begin, width)]

    def along(item, sign, hop):
        which, begin, width, _ = items[item]
        columns = pl.ds(begin, width)
        rows = rows_at(which, place.chip, place.core, me - sign * (hop - 1))
        return remote(
            item,
            shards[which].at[:, columns] if hop == 1 else weights[which].at[rows, columns],
            weights[which].at[rows, columns],
            2 * chips + hop - 1 + (narrow - 1 if sign < 0 else 0),
            (place.w, me + sign),
        )

    def has_next(sign):
        return me < narrow - 1 if sign > 0 else me >= 1

    def has_come(sign, hop):
        return me >= hop if sign > 0 else me < narrow - hop

    def start_if(condition, copy):
        @pl.when(condition)
        def _():
            copy.start()

        guarded.append((condition, copy))

    def bits_of(item):
        return place.bits if items[item][3] == 0 else place.bits[::-1]

    def across(item, mask, bit):
        return remote(item, group(item, mask), group(item, mask), mask ^ bit, place.across(bit))

    def to_twin(item, mask):
        return remote(item, group(item, mask), group(item, mask), chips + mask, place.twin)

    plan = Planner()
    waited = set()

    def block_bytes(item):
        which, _, width, _ = items[item]
        return 2 * narrow * rows_of[which] * width

    def twin_event(item, mask):
        return lambda: to_twin(item, mask).wait_recv()

    def onward(item, mask, number):
        bits = bits_of(item)
        size = block_bytes(item)
        for later in range(number, len(bits)):
            start(across(item, mask, bits[later]))
            coming = mask ^ bits[later]
            plan.transfer(
                bits[later], 2 * size / LINK, (item, coming), functools.partial(arrive, item, coming, later)
            )
        start(to_twin(item, mask))
        plan.transfer(-1, size / TWIN_LINK, (item, chips + mask), twin_event(item, mask))

    def arrive(item, mask, number):
        across(item, mask ^ bits_of(item)[number], bits_of(item)[number]).wait_recv()
        onward(item, mask, number + 1)

    def begin_item(item):
        for sign in (1, -1):
            start_if(has_next(sign), along(item, sign, 1))
        line_transfer(item, 1)

    def line_transfer(item, hop):
        cost = 2 * block_bytes(item) / narrow / LINK
        key = (item, 0) if hop == narrow - 1 else (item, -hop)
        plan.transfer(0, cost, key, functools.partial(line_event, item, hop))

    def line_event(item, hop):
        if items[item][0] not in waited:
            waited.add(items[item][0])
            own[items[item][0]].wait()
        for sign in (1, -1):

            @pl.when(has_come(sign, hop))
            def _():
                along(item, sign, hop).wait_recv()

            if hop < narrow - 1:
                start_if(jnp.logical_and(has_come(sign, hop), has_next(sign)), along(item, sign, hop + 1))
        if hop < narrow - 1:
            line_transfer(item, hop + 1)
        else:
            onward(item, 0, 0)

    begun = []

    def refill():
        while len(begun) < total and plan.free.get(0, 0.0) < plan.now + 0.5:
            begin_item(len(begun))
            begun.append(True)

    plan.refill = refill
    refill()

    def need(which, columns=None):
        plan.need(
            [
                (index, key)
                for index, (owner, begin, width, _) in enumerate(items)
                if owner == which and (columns is None or (begin < columns[1] and begin + width > columns[0]))
                for key in range(2 * chips)
            ]
        )

    flushed = []

    def flush(ref):
        index = [vars(at)[name] is ref for name in outs].index(True)
        copy = pltpu.make_async_copy(ref, results[index], out_sem.at[index])
        copy.start()
        flushed.append(copy)

    def swap(src, dst, kind, step):
        return pltpu.make_async_remote_copy(
            src_ref=src,
            dst_ref=dst,
            send_sem=swap_send.at[kind, step],
            recv_sem=swap_recv.at[kind, step],
            device_id=place.along(step),
            device_id_type=MESH,
        )

    gains = at.gains
    embedded, mid, last = at.embedded, at.mid, at.last
    normed, hidden, wave = at.normed, at.hidden, at.wave
    away, qkv, heads_out, returned = at.away, at.qkv, at.heads_out, at.returned

    def turn(dest, source):
        dest[...] = source[...].T
        flush(dest)

    need(0)
    width = weights[0].shape[1]
    kind = lax.broadcasted_iota(jnp.int32, (8, LANES), 0)
    spot = lax.broadcasted_iota(jnp.int32, (8, LANES), 1)
    pick = (spot == kind + lead).astype(F32).astype(BF16)
    gains[...] = back_mul(pick, weights[0][:, width - LANES :])
    flush(gains)

    def embed(block):
        cols = pl.ds(block, 256)
        embedded[:, cols] = back_mul(at.patches[...], weights[0][pl.ds(block, 256), : at.patches.shape[1]])

    for block in range(0, D, 256):
        plan.work(0.5, functools.partial(embed, block))
    flush(embedded)

    def norm_rows(source, row, dest):
        step_rows = 64

        def one(step, carry):
            rows = pl.ds(pl.multiple_of(step * step_rows, step_rows), step_rows)
            dest[rows, :] = normalize(
                source[rows, :], gains[row : row + 1, :], gains[row + 3 : row + 4, :]
            ).astype(BF16)
            return carry

        lax.fori_loop(0, tokens // step_rows, one, 0)

    plan.work(2.0, lambda: norm_rows(embedded, 0, normed))
    turn_first = plan.later(2.0, lambda: turn(at.t1, normed))
    piece = 2 * (narrow - 1) * 2 * tokens * head_width / LINK

    def project(part, step):
        owner = lax.rem(me + step, narrow)
        offset = pl.multiple_of(part * D + owner * head_width, LANES)
        value = matmul(normed[...], weights[1][:, pl.ds(offset, head_width)]).astype(BF16)
        if step:
            away[step - 1, part] = value
            start(swap(away.at[step - 1, part], qkv.at[me, part], part, step))
        else:
            qkv[me, part] = value

    def swap_event(part):
        for step in range(1, narrow):
            swap(away.at[step - 1, part], qkv.at[me, part], part, step).wait_recv()

    for part in range(3):
        need(1, (part * D, part * D + D))
        for step in list(range(1, narrow)) + [0]:
            plan.work(0.7, functools.partial(project, part, step))
        plan.transfer(0, piece, (-1, part), functools.partial(swap_event, part))
    flush(at.w1)
    plan.need([(-1, part) for part in range(3)])
    flush(qkv)
    plan.need([(-1, 2)])

    lane = lax.broadcasted_iota(jnp.int32, (1, LANES), 1)
    scale = HD ** (-0.5)
    length = narrow * tokens

    def attend(step):
        who = lax.rem(me + step, narrow)
        log_sums = jnp.zeros((tokens, LANES), F32)
        for pair in range(head_width // LANES):
            lanes = pl.ds(pair * LANES, LANES)
            query = qkv[who, 0, :, lanes].astype(F32)
            key = qkv[:, 1, :, lanes].reshape(length, LANES)
            value = qkv[:, 2, :, lanes].reshape(length, LANES)
            out = jnp.zeros((tokens, LANES), F32)
            for side in range(LANES // HD):
                inside = lane // HD == side
                own_query = (query * jnp.where(inside, scale, 0.0)).astype(BF16)
                scores = back_mul(own_query, key)
                highest = jnp.max(scores, -1, keepdims=True)
                exponentials = jnp.exp(scores - highest)
                summed = jnp.sum(exponentials, -1, keepdims=True)
                part = matmul(exponentials.astype(BF16), value) / summed
                out = jnp.where(inside, part, out)
                log_sums = jnp.where(
                    lane == pair * (LANES // HD) + side, highest + jnp.log(summed), log_sums
                )
            heads_out[who, :, lanes] = out.astype(BF16)
        at.log_sums[who] = log_sums
        if step:
            start(swap(heads_out.at[who], returned.at[me], 3, step))
        else:
            returned[me] = heads_out[who]

    def return_event(step):
        return lambda: swap(heads_out.at[me], returned.at[me], 3, step).wait_recv()

    for step in list(range(1, narrow)) + [0]:
        plan.work(3.5, functools.partial(attend, step))
        if step:
            plan.transfer(0, piece / (narrow - 1), (-2, step), return_event(step))
    flush(heads_out)
    flush(at.log_sums)
    need(2)
    plan.need([(-2, step) for step in range(1, narrow)])

    def merge(block):
        cols = pl.ds(block, 256)
        value = embedded[:, cols]
        for source in range(narrow):
            value = value + matmul(returned[source], weights[2][pl.ds(source * head_width, head_width), cols])
        mid[:, cols] = value

    for block in range(0, D, 256):
        plan.work(0.7, functools.partial(merge, block))
    flush(at.w2)
    flush(mid)
    plan.force(turn_first)
    plan.work(2.0, lambda: norm_rows(mid, 1, normed))

    def turn_returned():
        for source in range(narrow):
            at.t2[pl.ds(source * head_width, head_width), :] = returned[source].T
        flush(at.t2)

    plan.later(2.0, turn_returned)
    turn_second = plan.later(2.0, lambda: turn(at.t3, normed))

    ff = weights[3].shape[1]
    tile = wave.shape[1]
    slopes = at.slopes

    def expand(block):
        wave[...] = matmul(normed[...], weights[3][:, pl.ds(block, tile)])

        def bend(step, carry):
            rows = pl.ds(pl.multiple_of(step * 32, 32), 32)
            x = wave[rows, :]
            half = 0.5 * (1.0 + lax.erf(x * (0.5**0.5)))
            hidden[rows, pl.ds(block, tile)] = (x * half).astype(BF16)
            bell = jnp.exp(-0.5 * x * x) * 0.3989422804014327
            slopes[rows, pl.ds(block, tile)] = (half + x * bell).astype(BF16)
            return carry

        lax.fori_loop(0, tokens // 32, bend, 0)

    def turn_hidden(block):
        at.t4[pl.ds(block, tile), :] = hidden[:, pl.ds(block, tile)].T

    for block in range(0, ff, tile):
        need(3, (block, block + tile))
        plan.work(2.5, functools.partial(expand, block))
        plan.later(1.0, functools.partial(turn_hidden, block))
    flush(at.w3)
    flush(slopes)

    def shrink(block):
        cols = pl.ds(block, 256)
        last[:, cols] = mid[:, cols] + matmul(hidden[...], weights[4][:, cols])

    for block in range(0, D, 256):
        need(4, (block, block + 256))
        plan.work(1.0, functools.partial(shrink, block))
    flush(at.w4)
    flush(last)
    plan.force(turn_second)
    plan.work(2.0, lambda: norm_rows(last, 2, normed))
    need(5)

    def unpatch(block):
        cols = pl.ds(block, 256)
        at.gaussians[:, cols] = matmul(normed[...], weights[5][:, cols])

    for block in range(0, weights[5].shape[1], 256):
        plan.work(0.7, functools.partial(unpatch, block))
    flush(at.w5)
    flush(at.gaussians)
    plan.later(2.0, lambda: turn(at.t5, normed))
    plan.finish()
    flush(at.t4)
    for copy in started:
        copy.wait_send()
    for condition, copy in guarded:

        @pl.when(condition)
        def _():
            copy.wait_send()

    for copy in flushed:
        copy.wait()


def forward_all(shards, norms, patches, lead, wide, narrow):
    tokens = patches.shape[0]
    widths = [patches.shape[1]] + [shard.shape[1] for shard in shards[1:]]
    heights = [shard.shape[0] * wide * narrow for shard in shards]
    ff = widths[3]
    head_width = D // narrow
    items = forward_plan(widths)
    slots = wide + 2 * (narrow - 1)
    full = [((height, width), BF16) for height, width in zip(heights, widths)]
    shapes = dict(
        w1=full[1],
        w2=full[2],
        w3=full[3],
        w4=full[4],
        w5=full[5],
        gains=((8, D), F32),
        embedded=((tokens, D), F32),
        mid=((tokens, D), F32),
        last=((tokens, D), F32),
        slopes=((tokens, ff), BF16),
        t1=((D, tokens), BF16),
        t2=((D, tokens), BF16),
        t3=((D, tokens), BF16),
        t4=((ff, tokens), BF16),
        t5=((D, tokens), BF16),
        qkv=((narrow, 3, tokens, head_width), BF16),
        heads_out=((narrow, tokens, head_width), BF16),
        log_sums=((narrow, tokens, LANES), F32),
        gaussians=((tokens, widths[5]), F32),
    )
    ins = tuple(dict(s0=0, s1=0, s2=0, s3=0, s4=0, s5=0, norm_raw=0, patches=0))
    outs = tuple(shapes)
    extras = dict(
        first_weight=pltpu.VMEM((heights[0], widths[0]), BF16),
        c0=pltpu.VMEM((shards[0].shape[0], widths[0]), BF16),
        c1=pltpu.VMEM(shards[1].shape, BF16),
        c2=pltpu.VMEM(shards[2].shape, BF16),
        c3=pltpu.VMEM(shards[3].shape, BF16),
        c4=pltpu.VMEM(shards[4].shape, BF16),
        c5=pltpu.VMEM(shards[5].shape, BF16),
        normed=pltpu.VMEM((tokens, D), BF16),
        hidden=pltpu.VMEM((tokens, ff), BF16),
        wave=pltpu.VMEM((tokens, 512), F32),
        away=pltpu.VMEM((narrow - 1, 3, tokens, head_width), BF16),
        returned=pltpu.VMEM((narrow, tokens, head_width), BF16),
        own_sem=pltpu.SemaphoreType.DMA((6,)),
        send_sem=pltpu.SemaphoreType.DMA((len(items), slots)),
        recv_sem=pltpu.SemaphoreType.DMA((len(items), slots)),
        swap_send=pltpu.SemaphoreType.DMA((4, narrow)),
        swap_recv=pltpu.SemaphoreType.DMA((4, narrow)),
        out_sem=pltpu.SemaphoreType.DMA((len(outs),)),
    )
    scratch = outs + tuple(extras)
    anywhere = pl.BlockSpec(memory_space=pl.ANY)
    results = pl.pallas_call(
        functools.partial(forward_kernel, items, wide, narrow, lead, ins, outs, scratch),
        out_shape=[jax.ShapeDtypeStruct(*shapes[name]) for name in outs],
        in_specs=[pl.BlockSpec(memory_space=pltpu.VMEM)] * len(ins),
        out_specs=[anywhere] * len(outs),
        scratch_shapes=[pltpu.VMEM(*shapes[name]) for name in outs] + list(extras.values()),
        compiler_params=pltpu.CompilerParams(
            collective_id=0, has_side_effects=True, vmem_limit_bytes=60 * MIB
        ),
        name="forward",
    )(*shards, norms, patches)
    return Bag(zip(outs, results))


def backward_plan(widths, pairs):
    items = []
    for which, cuts in ((5, 1), (4, 2), (3, 2), (2, 1), (1, pairs), (0, 1)):
        size = widths[which] // cuts
        if which == 1:
            piece = size // 3
            for cut in range(cuts):
                start = cut * size
                items += [(1, start, piece, 0), (1, start + piece, piece, 1)]
                for side, (shift, width) in enumerate(column_halves(piece)):
                    items.append((1, start + 2 * piece + shift, width, side))
            continue
        for cut in range(cuts):
            for side, (start, width) in enumerate(column_halves(size)):
                items.append((which, cut * size + start, width, side))
    return items


def tile_of(width):
    for tile in (512, 384, 256, 128):
        if width % tile == 0:
            return tile
    return width


def backward_kernel(items, wide, narrow, lead, ins, scratch, *refs):
    src = Bag(zip(ins, refs))
    refs = refs[len(ins) :]
    sums, totals, refs = refs[:6], refs[6], list(refs[7:])
    at = Bag(zip(scratch, refs))
    place = Place(wide, narrow)
    chips, me = place.chips, place.n
    total = len(items)
    refs = refs[len(scratch) :]
    held = [refs.pop(0) for _ in items]
    passed = [[refs.pop(0) for _ in place.bits] for _ in items]
    final = [refs.pop(0) for _ in items]
    spare = [refs.pop(0) for _ in range(6)]
    tokens = src.patches.shape[0]
    head_width = D // narrow
    length = narrow * tokens
    reach = narrow * LANES
    send_sem, recv_sem, tile_send, tile_recv = at.send_sem, at.recv_sem, at.tile_send, at.tile_recv
    swap_send, swap_recv, in_sem, ring_sem = at.swap_send, at.swap_recv, at.in_sem, at.ring_sem
    gains, norms, extra = src.gains, at.norms, at.extra
    stash, d_res, d_norm = at.stash, at.d_res, at.d_norm
    mixed, merge_low, expand_low, shrink_low = at.mixed, at.merge_low, at.expand_low, at.shrink_low

    loaded = [name for name in ins if name in scratch]

    def load(ref):
        index = [vars(at)[name] is ref for name in loaded].index(True)
        return pltpu.make_async_copy(vars(src)[loaded[index]], ref, in_sem.at[index])

    def load_stash(ref):
        return pltpu.make_async_copy(ref, stash, in_sem.at[len(loaded)])

    def ring(ref, slots, rows, columns, index, row):
        slot = lax.rem(index, 2)
        return pltpu.make_async_copy(
            ref.at[pl.ds(pl.multiple_of(row, rows), rows), :],
            slots.at[slot, pl.ds(0, rows), pl.ds(0, columns)],
            ring_sem.at[0 if slots is at.tall else 1, slot],
        )

    slope_rows = at.tall.shape[1]

    def slope_load(index):
        slot = lax.rem(index, 2)
        return pltpu.make_async_copy(
            src.slopes.at[:, pl.ds(pl.multiple_of(index * slope_rows, slope_rows), slope_rows)],
            at.slope_slots.at[slot],
            ring_sem.at[2, slot],
        )

    u_rows, u_cols = 256, src.w5.shape[1]
    load_stash(src.last).start()
    for index in range(2):
        ring(src.w5, at.tall, u_rows, u_cols, index, index * u_rows).start()
        slope_load(index).start()
        ring(src.w3, at.long, 128, src.w3.shape[1], index, index * 128).start()
    for name in loaded:
        load(vars(at)[name]).start()

    peers = [(lax.rem(place.w + step, wide), place.n) for step in range(1, wide)]
    peers += [place.along(step) for step in range(1, narrow)]
    greet(peers)

    started, guarded = [], []

    def start(copy):
        copy.start()
        started.append(copy)

    lefts = [at.embed_t, at.t1, at.t2, at.t3, at.t4, at.t5]
    rights = [src.patches, mixed, merge_low, expand_low, shrink_low, src.gauss]

    def remote(item, src, dst, slot, peer):
        return pltpu.make_async_remote_copy(
            src_ref=src,
            dst_ref=dst,
            send_sem=send_sem.at[item, slot],
            recv_sem=recv_sem.at[item, slot],
            device_id=peer,
            device_id_type=MESH,
        )

    def bits_of(item):
        return place.bits[::-1] if items[item][3] == 0 else place.bits

    def groups_of(item):
        size = max(1, 512 // (narrow * spare[items[item][0]].shape[2]))
        masks = list(range(chips))
        if bits_of(item) and bits_of(item)[0] > 1:
            masks = masks[chips // 2 :] + masks[: chips // 2]
        return [sorted(masks[at_mask : at_mask + size]) for at_mask in range(0, chips, size)]

    def product(item, masks, core, into, plus):
        which, begin, width, _ = items[item]
        left, right = lefts[which], rights[which]
        rows = into.shape[-2]
        span = narrow * rows
        tile = tile_of(width)
        firsts = [((flip(place.chip, mask) * 2 + core) * narrow) * rows for mask in masks]
        with_extra = which == 0 and begin + width == right.shape[1]
        assert not with_extra or tile == width
        part, begin = (begin // reach, begin % reach) if which == 1 else (None, begin)

        def one(step, carry):
            offset = pl.multiple_of(begin + step * tile, LANES)
            local = pl.multiple_of(step * tile, LANES)
            if part is None:
                rhs = right[:, pl.ds(offset, tile)]
            else:
                rhs = right[part // 3, part % 3, :, pl.ds(offset, tile)]
            spots = [pl.ds(pl.multiple_of(first, span), span) for first in firsts]
            lhs = jnp.concatenate([left[spot, :] for spot in spots], 0)
            value = jnp.dot(lhs, rhs, preferred_element_type=F32)
            for index, mask in enumerate(masks):
                piece = value[index * span : (index + 1) * span]
                if with_extra:
                    blank = jnp.zeros((span, tile - LANES), F32)
                    piece = piece + jnp.concatenate([blank, extra[spots[index], :]], 1)
                piece = piece.reshape(narrow, rows, tile)
                if plus:
                    piece = piece + into[mask, :, :, pl.ds(local, tile)].astype(F32)
                into[mask, :, :, pl.ds(local, tile)] = piece.astype(BF16)
            return carry

        lax.fori_loop(0, width // tile, one, 0)

    last_sent = {}
    plan = Planner()

    def to_twin(item, masks):
        which, _, width, _ = items[item]
        some = pl.ds(masks[0], len(masks))
        own = spare[which].at[some, :, :, pl.ds(0, width)]
        return remote(item, own, held[item].at[some], masks[0], place.twin)

    def across(item, mask, bit, number, slot):
        return remote(
            item, held[item].at[mask], passed[item][number].at[slot], chips + mask, place.across(bit)
        )

    def along(item, sign, hop):
        count = narrow - hop
        first = hop if sign > 0 else 0
        node = hop if sign > 0 else narrow - 1 - hop
        return remote(
            item,
            held[item].at[0, pl.ds(first, count)],
            final[item].at[pl.ds(first + (1 if sign > 0 else 0), count)],
            2 * chips + (0 if sign > 0 else 1),
            (place.w, node),
        )

    def send_along(item, sign, hop):
        sender = me == (hop - 1 if sign > 0 else narrow - hop)

        @pl.when(sender)
        def _():
            along(item, sign, hop).start()

        guarded.append((sender, along(item, sign, hop)))

    def line_event(item, hop):
        for sign in (1, -1):
            count = narrow - hop - 1
            first = hop + 1 if sign > 0 else 0

            @pl.when(me == (hop if sign > 0 else narrow - 1 - hop))
            def _():
                along(item, sign, hop).wait_recv()

                def one(step, carry):
                    spot = first + step
                    value = held[item][0, spot].astype(F32)
                    value = value + final[item][spot + (1 if sign > 0 else 0)].astype(F32)
                    held[item][0, spot] = value.astype(BF16)
                    return carry

                if count:
                    lax.fori_loop(0, count, one, 0)

            if count:
                send_along(item, sign, hop + 1)
        line_transfer(item, hop + 1)

    def line_transfer(item, hop):
        cost = (narrow - hop) * 2 * block_bytes(item) / narrow / LINK
        event = line_event if hop < narrow else finish
        if hop == narrow:
            return finish(item)
        plan.transfer(0 if hop == 1 else 100 + hop, cost, (item, -hop, 0), functools.partial(event, item, hop))

    def leaves(item, mask):
        bits = bits_of(item)
        return min([number for number, bit in enumerate(bits) if mask & bit], default=len(bits))

    def slot_of(item, mask, number):
        bits = bits_of(item)
        kept = [m for m in range(chips) if not any(m & bit for bit in bits[: number + 1])]
        return kept.index(mask)

    def add_into(dest, dest_at, src, src_at):
        def one(step, carry):
            value = dest[dest_at, step].astype(F32) + src[src_at, step].astype(F32)
            dest[dest_at, step] = value.astype(BF16)
            return carry

        lax.fori_loop(0, narrow, one, 0)

    def block_bytes(item):
        which, _, width, _ = items[item]
        return 2 * spare[which].shape[1] * spare[which].shape[2] * width

    def push(which, pair=None):
        for item, (owner, begin, _, _) in enumerate(items):
            if owner != which or (pair is not None and begin // (3 * reach) != pair):
                continue
            for masks in groups_of(item):
                cost = len(masks) * block_bytes(item) / 1e6
                plan.work(cost, functools.partial(push_some, item, masks))

    def push_some(item, masks):
        which = items[item][0]
        for key in [key for key in last_sent if key[0] == which and set(key[1]) & set(masks)]:
            last_sent.pop(key).wait_send()
        product(item, masks, 1 - place.core, spare[which], False)
        copy = to_twin(item, masks)
        copy.start()
        last_sent[which, tuple(masks)] = copy
        cost = len(masks) * block_bytes(item) / TWIN_LINK
        plan.transfer(-1, cost, (item, 0, masks[0]), functools.partial(own_event, item, masks))

    def own_event(item, masks):
        to_twin(item, masks).wait_recv()
        product(item, masks, place.core, held[item], True)
        plan.now += len(masks) * block_bytes(item) / 1e6
        plan.done.update((item, 0, mask) for mask in masks)
        for mask in masks:
            onward(item, mask, 0)

    def onward(item, mask, number):
        bits = bits_of(item)
        if number == len(bits):
            lined.append(item)
            refill()
        elif leaves(item, mask) == number:
            kept = mask ^ bits[number]
            start(across(item, mask, bits[number], number, slot_of(item, kept, number)))
            plan.transfer(
                bits[number],
                2 * block_bytes(item) / LINK,
                (item, 1 + number, kept),
                functools.partial(sum_event, item, kept, number),
            )

    lined = []

    def refill():
        while lined and plan.free.get(0, 0.0) < plan.now + Z_AHEAD:
            item = lined.pop(0)
            for sign in (1, -1):
                send_along(item, sign, 1)
            line_transfer(item, 1)

    plan.refill = refill

    def sum_event(item, mask, number):
        plan.need([(item, before, mask) for before in range(number + 1)])
        bit = bits_of(item)[number]
        slot = slot_of(item, mask, number)
        across(item, mask ^ bit, bit, number, slot).wait_recv()
        add_into(held[item], mask, passed[item][number], slot)
        plan.now += block_bytes(item) / 8e5
        onward(item, mask, number + 1)

    squares = []

    def finish(item):
        which, begin, width, _ = items[item]
        acc = at.acc.at[pl.ds(0, held[item].shape[2]), pl.ds(0, width)]
        acc[...] = held[item][0, me].astype(F32)

        @pl.when(me >= 1)
        def _():
            acc[...] += final[item][me + 1].astype(F32)

        @pl.when(me < narrow - 1)
        def _():
            acc[...] += final[item][me].astype(F32)

        value = acc[...]
        if which == 1:
            for shift in range(0, width, LANES):
                part, spot = (begin + shift) // reach, (begin + shift) % reach
                column = part % 3 * D + spot // LANES * head_width + part // 3 * LANES
                sums[which][:, pl.ds(column, LANES)] = value[:, shift : shift + LANES]
        else:
            sums[which][:, pl.ds(begin, width)] = value
        squares.append(jnp.sum(value * value))

    norms[...] = jnp.zeros_like(norms)

    def norm_back(row, low, add):
        step_rows = 64

        def one(step, carry):
            rows = pl.ds(pl.multiple_of(step * step_rows, step_rows), step_rows)
            values = stash[rows, :]
            upper = d_norm[rows, :]
            centred = values - jnp.mean(values, -1, keepdims=True)
            rate = lax.rsqrt(jnp.mean(centred * centred, -1, keepdims=True) + 1e-05)
            unit = centred * rate
            norms[row : row + 1, :] += jnp.sum(upper * unit, 0, keepdims=True)
            norms[row + 3 : row + 4, :] += jnp.sum(upper, 0, keepdims=True)
            scaled = upper * gains[row : row + 1, :]
            inner = scaled - jnp.mean(scaled, -1, keepdims=True)
            inner = rate * (inner - unit * jnp.mean(scaled * unit, -1, keepdims=True))
            if add:
                inner = inner + d_res[rows, :]
            d_res[rows, :] = inner
            low[rows, :] = inner.astype(BF16)
            return carry

        lax.fori_loop(0, tokens // step_rows, one, 0)

    load(at.t5).wait()
    plan.now += 5.0
    load_stash(src.last).wait()
    count = D // u_rows
    tall_rows = slope_rows

    def through_unpatch(index, carry):
        ring(src.w5, at.tall, u_rows, u_cols, index, index * u_rows).wait()
        slot = at.tall.at[lax.rem(index, 2)]
        offset = pl.multiple_of(index * u_rows, u_rows)
        d_norm[:, pl.ds(offset, u_rows)] = back_mul(src.gauss[...], slot[0:u_rows, 0:u_cols])

        @pl.when(index + 2 < count)
        def _():
            ring(src.w5, at.tall, u_rows, u_cols, index + 2, (index + 2) * u_rows).start()

        return carry

    lax.fori_loop(0, count, through_unpatch, 0)
    for index in range(2):
        ring(src.w4, at.tall, tall_rows, D, index, index * tall_rows).start()
    norm_back(2, shrink_low, False)
    load_stash(src.mid).start()
    load(at.t4).wait()
    ff = src.w3.shape[1]
    slabs = ff // tall_rows

    def through_shrink(index, carry):
        ring(src.w4, at.tall, tall_rows, D, index, index * tall_rows).wait()
        slope_load(index).wait()
        slot = lax.rem(index, 2)
        value = back_mul(shrink_low[...], at.tall[slot])
        value = value * at.slope_slots[slot].astype(F32)
        expand_low[:, pl.ds(pl.multiple_of(index * tall_rows, tall_rows), tall_rows)] = value.astype(BF16)

        @pl.when(index + 2 < slabs)
        def _():
            ring(src.w4, at.tall, tall_rows, D, index + 2, (index + 2) * tall_rows).start()
            slope_load(index + 2).start()

        return carry

    lax.fori_loop(0, slabs, through_shrink, 0)
    owners = [lax.rem(me + step, narrow) for step in list(range(1, narrow)) + [0]]
    for index in range(2):
        ring(src.w2, at.tall, head_width, D, index, owners[index] * head_width).start()
    load(at.t3).wait()
    plan.now += 6.0

    def through_expand(index, carry):
        ring(src.w3, at.long, 128, ff, index, index * 128).wait()
        offset = pl.multiple_of(index * 128, 128)
        d_norm[:, pl.ds(offset, 128)] = back_mul(expand_low[...], at.long[lax.rem(index, 2)])

        @pl.when(index + 2 < D // 128)
        def _():
            ring(src.w3, at.long, 128, ff, index + 2, (index + 2) * 128).start()

        return carry

    lax.fori_loop(0, D // 128, through_expand, 0)
    for index in range(2):
        ring(src.w1, at.long, 128, 3 * D, index, index * 128).start()
    load_stash(src.mid).wait()
    norm_back(1, merge_low, True)
    load_stash(src.embedded).start()

    def swap(src, dst, kind, step):
        return pltpu.make_async_remote_copy(
            src_ref=src,
            dst_ref=dst,
            send_sem=swap_send.at[kind, step],
            recv_sem=swap_recv.at[kind, step],
            device_id=place.along(step),
            device_id_type=MESH,
        )

    d_heads, away = at.d_heads, at.away
    plan.now += 7.0
    piece = 2 * (narrow - 1) * 2 * tokens * head_width / LINK

    def head_event():
        for step in range(1, narrow):
            swap(away.at[step - 1], d_heads.at[me], 0, step).wait_recv()

    for index, owner in enumerate(owners):
        ring(src.w2, at.tall, head_width, D, index, owner * head_width).wait()
        value = back_mul(merge_low[...], at.tall[index % 2, 0:head_width, :]).astype(BF16)
        if index < narrow - 1:
            away[index] = value
            start(swap(away.at[index], d_heads.at[me], 0, index + 1))
        else:
            d_heads[me] = value
        if index + 2 < narrow:
            ring(src.w2, at.tall, head_width, D, index + 2, owners[index + 2] * head_width).start()
    plan.now += 3.0
    plan.transfer(0, piece, (-1, 0, 0), head_event)
    load(at.t2).wait()
    for which in (5, 4, 3, 2):
        push(which)
    load(at.qkv).wait()
    load(at.heads_out).wait()
    load(at.log_sums).wait()
    plan.need([(-1, 0, 0)])

    qkv, heads_out, log_sums, parts = at.qkv, at.heads_out, at.log_sums, at.parts
    key_t, key_acc, value_acc, query_acc = at.key_t, at.key_acc, at.value_acc, at.query_acc
    lane = lax.broadcasted_iota(jnp.int32, (1, LANES), 1)
    line = lax.broadcasted_iota(jnp.int32, (LANES, 1), 0)
    sides = LANES // HD
    scale = HD ** (-0.5)
    choose = lax.broadcasted_iota(jnp.int32, (8, LANES), 1) // HD
    choose = (choose == lax.broadcasted_iota(jnp.int32, (8, LANES), 0)).astype(F32)

    def part_swap(pair, step):
        lanes = pl.ds(pair * LANES, LANES)
        who = lax.rem(me + step, narrow)
        return swap(
            parts.at[who, :, :, lanes],
            mixed.at[pair, :, :, pl.ds(pl.multiple_of(me * LANES, LANES), LANES)],
            1 + pair,
            step,
        )

    pushed_pairs = []
    load(at.t1).wait()

    def part_event(pair):
        for step in range(1, narrow):
            part_swap(pair, step).wait_recv()

    for pair in range(head_width // LANES):
        lanes = pl.ds(pair * LANES, LANES)
        key_t[...] = qkv[:, 1, :, lanes].reshape(length, LANES).T
        key_acc[...] = jnp.zeros_like(key_acc)
        value_acc[...] = jnp.zeros_like(value_acc)
        def one_block(step, lanes=lanes, pair=pair):
            who = lax.rem(me + step, narrow)
            query = qkv[who, 0, :, lanes].astype(F32)
            upper = d_heads[who, :, lanes].astype(F32)
            kept = heads_out[who, :, lanes].astype(F32)
            delta = lax.dot_general(
                choose,
                upper * kept,
                (((1,), (1,)), ((), ())),
                precision=HIGHEST,
                preferred_element_type=F32,
            )
            log_rows = log_sums[who].T[pair * sides : (pair + 1) * sides, :]
            own_query = [(query * jnp.where(lane // HD == side, scale, 0.0)).astype(BF16) for side in range(sides)]
            own_upper = [(upper * jnp.where(lane // HD == side, 1.0, 0.0)).astype(BF16) for side in range(sides)]
            query_acc[...] = jnp.zeros_like(query_acc)

            def block(source, carry):
                rows = pl.ds(pl.multiple_of(source * tokens, tokens), tokens)
                key, value = qkv[source, 1, :, lanes], qkv[source, 2, :, lanes]
                key_turned = key_t[:, rows].astype(F32)
                for side in range(sides):
                    scores = back_mul(key, own_query[side])
                    probs = jnp.exp(scores - log_rows[side : side + 1, :])
                    d_probs = back_mul(value, own_upper[side])
                    d_scores = (probs * (d_probs - delta[side : side + 1, :])).astype(BF16)
                    value_acc[rows, :] += matmul(probs.astype(BF16), own_upper[side])
                    key_acc[rows, :] += matmul(d_scores, own_query[side])
                    turned = (key_turned * jnp.where(line // HD == side, scale, 0.0)).astype(BF16)
                    query_acc[...] += matmul(turned, d_scores)
                return carry

            lax.fori_loop(0, narrow, block, 0)
            parts[who, 0, :, lanes] = query_acc[...].T.astype(BF16)
        for step in range(narrow):
            plan.work(3.0, functools.partial(one_block, step))
            for earlier in range(pair):
                if earlier not in pushed_pairs and (-2, 0, earlier) in plan.done:
                    pushed_pairs.append(earlier)
                    push(1, earlier)
        for source in range(narrow):
            rows = pl.ds(source * tokens, tokens)
            parts[source, 1, :, lanes] = key_acc[rows, :].astype(BF16)
            parts[source, 2, :, lanes] = value_acc[rows, :].astype(BF16)
        for step in range(1, narrow):
            start(part_swap(pair, step))
        plan.now += 1.0
        plan.transfer(0, 1.5 * piece, (-2, 0, pair), functools.partial(part_event, pair))
        mixed[pair, :, :, pl.ds(pl.multiple_of(me * LANES, LANES), LANES)] = parts[me, :, :, lanes]
    for pair in range(head_width // LANES):
        if pair not in pushed_pairs:
            plan.need([(-2, 0, pair)])
            push(1, pair)

    def through_mixer(index, carry):
        ring(src.w1, at.long, 128, 3 * D, index, index * 128).wait()
        slot = lax.rem(index, 2)
        value = jnp.zeros((tokens, 128), F32)
        for pair in range(head_width // LANES):
            for part in range(3):
                columns = [part * D + owner * head_width + pair * LANES for owner in range(narrow)]
                weight = [at.long[slot, :, column : column + LANES] for column in columns]
                value = value + back_mul(mixed[pair, part], jnp.concatenate(weight, 1))
        d_norm[:, pl.ds(pl.multiple_of(index * 128, 128), 128)] = value

        @pl.when(index + 2 < D // 128)
        def _():
            ring(src.w1, at.long, 128, 3 * D, index + 2, (index + 2) * 128).start()

        return carry

    plan.work(4.0, lambda: lax.fori_loop(0, D // 128, through_mixer, 0))
    load_stash(src.embedded).wait()
    plan.work(3.0, lambda: norm_back(0, at.embed_low, True))
    at.embed_t[...] = at.embed_low[...].T
    turned = jnp.concatenate([norms[...], jnp.zeros((LANES - 8, D), F32)], 0).T
    at.extra[...] = pltpu.roll(turned, lead, 1)
    push(0)
    plan.finish()

    rows = lax.broadcasted_iota(jnp.int32, (8, LANES), 0)
    wide_tiles, narrow_tiles = at.wide_tiles, at.narrow_tiles
    wide_tiles[place.w] = jnp.where(rows == 0, src.term[...], sum(squares))

    def tile_copy(buffer, index, slot, peer):
        return pltpu.make_async_remote_copy(
            src_ref=buffer.at[index],
            dst_ref=buffer.at[index],
            send_sem=tile_send.at[slot],
            recv_sem=tile_recv.at[slot],
            device_id=peer,
            device_id_type=MESH,
        )

    for step in range(1, wide):
        start(tile_copy(wide_tiles, place.w, step - 1, (lax.rem(place.w + step, wide), place.n)))
    for step in range(1, wide):
        tile_copy(wide_tiles, place.w, step - 1, (lax.rem(place.w + step, wide), place.n)).wait_recv()
    whole = wide_tiles[0]
    for index in range(1, wide):
        whole = whole + wide_tiles[index]
    narrow_tiles[place.n] = whole
    for step in range(1, narrow):
        start(tile_copy(narrow_tiles, place.n, wide + step - 1, place.along(step)))
    for step in range(1, narrow):
        tile_copy(narrow_tiles, place.n, wide + step - 1, place.along(step)).wait_recv()
    whole = narrow_tiles[0]
    for index in range(1, narrow):
        whole = whole + narrow_tiles[index]
    totals[...] = whole
    for copy in list(last_sent.values()) + started:
        copy.wait_send()
    for condition, copy in guarded:

        @pl.when(condition)
        def _():
            copy.wait_send()


def backward_all(kept, patches, gauss, term, lead, wide, narrow):
    tokens = patches.shape[0]
    chips = wide // 2
    weights = [kept.w1, kept.w2, kept.w3, kept.w4, kept.w5]
    heights = [D] + [weight.shape[0] for weight in weights]
    widths = [patches.shape[1]] + [weight.shape[1] for weight in weights]
    rows = [height // (wide * narrow) for height in heights]
    head_width = D // narrow
    length = narrow * tokens
    items = backward_plan(widths, head_width // LANES)
    slots = 2 * chips + 2
    streamed = dict(w1=kept.w1, w2=kept.w2, w3=kept.w3, w4=kept.w4, w5=kept.w5)
    streamed.update(last=kept.last, mid=kept.mid, embedded=kept.embedded, slopes=kept.slopes)
    loaded = dict(t5=kept.t5, t4=kept.t4, t3=kept.t3, t2=kept.t2, t1=kept.t1)
    loaded.update(qkv=kept.qkv, heads_out=kept.heads_out, log_sums=kept.log_sums)
    whole = dict(gains=kept.gains, patches=patches, gauss=gauss, term=term)
    operands = {**streamed, **loaded, **whole}
    shapes = [jax.ShapeDtypeStruct((rows[which], widths[which]), F32) for which in range(6)]
    shapes.append(jax.ShapeDtypeStruct((8, LANES), F32))
    scratch = {name: pltpu.VMEM(value.shape, value.dtype) for name, value in loaded.items()}
    scratch.update(
        acc=pltpu.VMEM((max(rows), max(width for _, _, width, _ in items)), F32),
        embed_t=pltpu.VMEM((D, tokens), BF16),
        embed_low=pltpu.VMEM((tokens, D), BF16),
        stash=pltpu.VMEM((tokens, D), F32),
        d_res=pltpu.VMEM((tokens, D), F32),
        d_norm=pltpu.VMEM((tokens, D), F32),
        norms=pltpu.VMEM((8, D), F32),
        extra=pltpu.VMEM((D, LANES), F32),
        shrink_low=pltpu.VMEM((tokens, D), BF16),
        expand_low=pltpu.VMEM((tokens, widths[3]), BF16),
        merge_low=pltpu.VMEM((tokens, D), BF16),
        mixed=pltpu.VMEM((head_width // LANES, 3, tokens, narrow * LANES), BF16),
        tall=pltpu.VMEM((2, 512, D), BF16),
        long=pltpu.VMEM((2, 128, widths[3]), BF16),
        slope_slots=pltpu.VMEM((2, tokens, 512), BF16),
        d_heads=pltpu.VMEM((narrow, tokens, head_width), BF16),
        away=pltpu.VMEM((narrow - 1, tokens, head_width), BF16),
        parts=pltpu.VMEM((narrow, 3, tokens, head_width), BF16),
        key_t=pltpu.VMEM((LANES, length), BF16),
        key_acc=pltpu.VMEM((length, LANES), F32),
        value_acc=pltpu.VMEM((length, LANES), F32),
        query_acc=pltpu.VMEM((LANES, tokens), F32),
        wide_tiles=pltpu.VMEM((wide, 8, LANES), F32),
        narrow_tiles=pltpu.VMEM((narrow, 8, LANES), F32),
        send_sem=pltpu.SemaphoreType.DMA((len(items), slots)),
        recv_sem=pltpu.SemaphoreType.DMA((len(items), slots)),
        tile_send=pltpu.SemaphoreType.DMA((wide + narrow,)),
        tile_recv=pltpu.SemaphoreType.DMA((wide + narrow,)),
        swap_send=pltpu.SemaphoreType.DMA((1 + head_width // LANES, narrow)),
        swap_recv=pltpu.SemaphoreType.DMA((1 + head_width // LANES, narrow)),
        in_sem=pltpu.SemaphoreType.DMA((9,)),
        ring_sem=pltpu.SemaphoreType.DMA((3, 2)),
    )
    lists = [pltpu.VMEM((chips, narrow, rows[which], width), BF16) for which, _, width, _ in items]
    for which, _, width, _ in items:
        for bit in chip_bits(chips):
            lists.append(pltpu.VMEM((chips // (2 * bit), narrow, rows[which], width), BF16))
    lists += [pltpu.VMEM((narrow + 1, rows[which], width), BF16) for which, _, width, _ in items]
    for which in range(6):
        widest = max(width for owner, _, width, _ in items if owner == which)
        lists.append(pltpu.VMEM((chips, narrow, rows[which], widest), BF16))
    vmem = pl.BlockSpec(memory_space=pltpu.VMEM)
    hbm = pl.BlockSpec(memory_space=pl.ANY)
    return pl.pallas_call(
        functools.partial(backward_kernel, items, wide, narrow, lead, tuple(operands), tuple(scratch)),
        out_shape=shapes,
        in_specs=[vmem if name in whole else hbm for name in operands],
        out_specs=[vmem] * len(shapes),
        scratch_shapes=list(scratch.values()) + lists,
        compiler_params=pltpu.CompilerParams(
            collective_id=1, has_side_effects=True, vmem_limit_bytes=63 * MIB
        ),
        name="backward",
    )(*operands.values())


def render_kernel(
    gauss_ref, weight_ref, target_ref, mask_ref, pair_ref, view_ref, total_ref, grad_ref, term_ref, feat, dfeat
):
    quads = gauss_ref.shape[0] // NVIEW
    span = weight_ref.shape[1]
    pairs = pair_ref.shape[1]
    scale = 1.0 / total_ref[0].astype(F32)

    def channel(index):
        return gauss_ref[:, index * PP : (index + 1) * PP]

    def shared():
        opacity = jax.nn.sigmoid(channel(3))
        extent = jax.nn.sigmoid(channel(5) + channel(6) + channel(7))
        lead = channel(8)
        denom = 1.0 + lead * lead + channel(9) * channel(9) + channel(10) * channel(10) + channel(11) * channel(11)
        facing = lead * lead / denom
        raw = channel(4)
        depth = jnp.maximum(raw, 0.0) + jnp.log1p(jnp.exp(-jnp.abs(raw)))
        return opacity, extent, lead, denom, facing, raw, depth

    opacity, extent, lead, denom, facing, raw, depth = shared()
    footprint = opacity * extent * facing
    channels = [jax.nn.sigmoid(channel(index)) * footprint for index in range(3)]
    channels += [footprint, depth * footprint]
    for index, value in enumerate(channels):
        for view in range(NVIEW):
            feat[index * quads : (index + 1) * quads, view * PP : (view + 1) * PP] = value[
                view * quads : (view + 1) * quads
            ]
    rendered = jnp.dot(feat[...], weight_ref[...], precision=HIGHEST, preferred_element_type=F32)
    parts = [rendered[index * quads : (index + 1) * quads] for index in range(5)]
    lane = lax.broadcasted_iota(jnp.int32, (quads, span), 1)
    live = jnp.where(lane < view_ref[0] * PP, mask_ref[...], 0).astype(F32)
    term = jnp.zeros((quads, span), F32)
    slopes = []
    for index in range(3):
        error = parts[index] - target_ref[index * quads : (index + 1) * quads, :].astype(F32)
        term = term + live * error * error
        slopes.append(2.0 * scale * live * error)
    below = 1.0 + parts[3]
    depth_out = parts[4] / below

    first, second = pair_ref[0:1, :], pair_ref[1:2, :]
    least = jnp.minimum(first, second)
    down = (jnp.abs(first - second) == P_SIZE).astype(jnp.int32)
    place = quads * PP
    slot, local = least // place, least % place
    high = down * quads + local // PP
    low = slot * PP + local % PP
    high_hot = (lax.broadcasted_iota(jnp.int32, (2 * quads, pairs), 0) == high).astype(F32).astype(BF16)
    low_hot = (lax.broadcasted_iota(jnp.int32, (span, pairs), 0) == low).astype(F32).astype(BF16)
    counts = back_mul(high_hot, low_hot)
    slope = jnp.zeros((quads, span), F32)
    for which, shift in enumerate((1, P_SIZE)):
        count = counts[which * quads : (which + 1) * quads]
        weight = DEPTH_WEIGHT * count * live * pltpu.roll(live, span - shift, 1)
        gap = depth_out - pltpu.roll(depth_out, span - shift, 1)
        term = term + weight * gap * gap
        pull = 2.0 * scale * weight * gap
        slope = slope + pull - pltpu.roll(pull, shift, 1)
    term_ref[...] = jnp.full(term_ref.shape, jnp.sum(term), F32)
    over = slope / below
    slopes += [-over * depth_out, over]
    stacked = jnp.concatenate(slopes, 0)
    dfeat[...] = lax.dot_general(
        stacked, weight_ref[...], (((1,), (1,)), ((), ())), precision=HIGHEST, preferred_element_type=F32
    )

    def feature_grad(index):
        return jnp.concatenate(
            [
                dfeat[index * quads : (index + 1) * quads, view * PP : (view + 1) * PP]
                for view in range(NVIEW)
            ],
            0,
        )

    def put(index, value):
        grad_ref[:, index * PP : (index + 1) * PP] = value.astype(BF16)

    d_foot = feature_grad(3)
    for index in range(3):
        tint = jax.nn.sigmoid(channel(index))
        upper = feature_grad(index)
        d_foot = d_foot + upper * tint
        put(index, upper * footprint * tint * (1.0 - tint))
    d_last = feature_grad(4)
    d_foot = d_foot + d_last * depth
    put(3, d_foot * extent * facing * opacity * (1.0 - opacity))
    put(4, d_last * footprint * jax.nn.sigmoid(raw))
    d_extent = d_foot * opacity * facing * extent * (1.0 - extent)
    for index in (5, 6, 7):
        put(index, d_extent)
    d_facing = d_foot * opacity * extent
    put(8, d_facing * 2.0 * lead / denom * (1.0 - facing))
    for index in (9, 10, 11):
        put(index, -2.0 * d_facing * facing / denom * channel(index))


def render(gaussians, weights, targets, mask, pairs, view_count, pair_total):
    rows = gaussians.shape[0]
    quads = rows // NVIEW
    slots, views = weights.shape[:2]
    spread = weights.transpose(1, 2, 0, 3).reshape(views * PP, slots * PP)
    wanted = targets.reshape(slots, 3, quads, PP).transpose(1, 2, 0, 3).reshape(3 * quads, slots * PP)
    valid = mask.reshape(slots, quads, PP).transpose(1, 0, 2).reshape(quads, slots * PP)
    vmem = pl.BlockSpec(memory_space=pltpu.VMEM)
    smem = pl.BlockSpec(memory_space=pltpu.SMEM)
    return pl.pallas_call(
        render_kernel,
        out_shape=[
            jax.ShapeDtypeStruct(gaussians.shape, BF16),
            jax.ShapeDtypeStruct((8, LANES), F32),
        ],
        in_specs=[vmem] * 5 + [smem] * 2,
        out_specs=[vmem] * 2,
        scratch_shapes=[pltpu.VMEM((5 * quads, views * PP), F32)] * 2,
        compiler_params=pltpu.CompilerParams(vmem_limit_bytes=48 * MIB),
        name="render",
    )(gaussians, spread, wanted, valid, pairs, view_count, pair_total)


def forward_plain(shards, patches, features, kinds):
    weights = [lax.all_gather(shard, BOTH, axis=0, tiled=True) for shard in shards]
    groups = lax.axis_size(NARROW)
    rows = patches.shape[0]
    gains = weights[0][:, features : features + kinds].T.astype(F32)
    embedded = back_mul(patches[:, :features], weights[0][:, :features])
    normed_one = layer_norm(embedded, gains[0], gains[3]).astype(BF16)
    mixed = matmul(normed_one, weights[1]).astype(BF16).reshape(rows, 3, groups, -1)
    mixed = mixed.transpose(2, 1, 0, 3)
    qkv = lax.all_to_all(mixed, NARROW, split_axis=0, concat_axis=0, tiled=True)
    width = qkv.shape[-1]
    length = groups * rows
    heads = width // HD
    parts = [qkv[:, part].reshape(length, heads, HD) for part in range(3)]
    attended, logsum = attention_forward(*parts)
    log_sums = logsum.transpose(0, 2, 1).reshape(groups, rows, heads)
    returned = lax.all_to_all(
        attended.reshape(groups, rows, width), NARROW, split_axis=0, concat_axis=0, tiled=True
    )
    returned = returned.transpose(1, 0, 2).reshape(rows, D)
    mid = embedded + matmul(returned, weights[2])
    normed_two = layer_norm(mid, gains[1], gains[4]).astype(BF16)
    expanded = matmul(normed_two, weights[3])
    half = 0.5 * (1.0 + lax.erf(expanded * (0.5**0.5)))
    activated = (expanded * half).astype(BF16)
    bell = jnp.exp(-0.5 * expanded * expanded) * 0.3989422804014327
    slopes = (half + expanded * bell).astype(BF16)
    last = mid + matmul(activated, weights[4])
    normed_three = layer_norm(last, gains[2], gains[5]).astype(BF16)
    return Bag(
        dict(
        w1=weights[1],
        w2=weights[2],
        w3=weights[3],
        w4=weights[4],
        w5=weights[5],
        gains=gains,
        embedded=embedded,
        mid=mid,
        last=last,
        slopes=slopes,
        t1=normed_one.T,
        t2=returned.T,
        t3=normed_two.T,
        t4=activated.T,
        t5=normed_three.T,
        qkv=qkv,
        heads_out=attended,
        log_sums=log_sums,
        gaussians=matmul(normed_three, weights[5]),
    ).items())


def backward_plain(kept, patches, gauss_low, term, features, kinds):
    gains = kept.gains
    weights = [None, kept.w1, kept.w2, kept.w3, kept.w4, kept.w5]
    norm_back_one = jax.vjp(layer_norm, kept.embedded, gains[0], gains[3])[1]
    norm_back_two = jax.vjp(layer_norm, kept.mid, gains[1], gains[4])[1]
    norm_back_three = jax.vjp(layer_norm, kept.last, gains[2], gains[5])[1]
    qkv = kept.qkv
    groups, _, rows, width = qkv.shape
    length = groups * rows
    heads = width // HD
    queries, keys, values = (qkv[:, part].reshape(length, heads, HD) for part in range(3))
    blocked = min(512, length)
    logsum = kept.log_sums[:, :, :heads].reshape(length // blocked, blocked, heads)
    residual_grad, gain_three, shift_three = norm_back_three(back_mul(gauss_low, weights[5]))
    shrink_low = residual_grad.astype(BF16)
    expand_low = (back_mul(shrink_low, weights[4]) * kept.slopes.astype(F32)).astype(BF16)
    through_two, gain_two, shift_two = norm_back_two(back_mul(expand_low, weights[3]))
    residual_grad = residual_grad + through_two
    merge_low = residual_grad.astype(BF16)
    out_grad = back_mul(merge_low, weights[2]).astype(BF16).reshape(rows, groups, width)
    head_grad = lax.all_to_all(
        out_grad.transpose(1, 0, 2), NARROW, split_axis=0, concat_axis=0, tiled=True
    ).reshape(length, heads, HD)
    grads = attention_backward(queries, keys, values, logsum.transpose(0, 2, 1), head_grad)
    stacked = jnp.stack(grads, 1).astype(BF16).reshape(groups, rows, 3, width)
    mixed_grad = lax.all_to_all(stacked, NARROW, split_axis=0, concat_axis=0, tiled=True)
    mixed_grad = mixed_grad.transpose(1, 2, 0, 3).reshape(rows, 3 * D)
    through_one, gain_one, shift_one = norm_back_one(back_mul(mixed_grad, weights[1]))
    embed_grad = (residual_grad + through_one).astype(BF16)
    grad_norms = jnp.stack([gain_one, gain_two, gain_three, shift_one, shift_two, shift_three])
    lefts = [embed_grad.T] + [kept.t1, kept.t2, kept.t3, kept.t4, kept.t5]
    rights = [patches, mixed_grad, merge_low, expand_low, shrink_low, gauss_low]
    products = [matmul(left, right) for left, right in zip(lefts, rights)]
    products[0] = products[0].at[:, features : features + kinds].add(grad_norms.T)
    sums = [
        lax.psum_scatter(
            product.astype(BF16), BOTH, scatter_dimension=0, tiled=True
        ).astype(F32)
        for product in products
    ]
    squares = sum(jnp.sum(part * part) for part in sums)
    loss_sum, square_sum = lax.psum((term[0, 0], squares), BOTH)
    return sums, loss_sum, square_sum


def update_kernel(features, total_ref, sums_ref, *refs):
    sources, targets, refs = refs[:27], refs[27:48], refs[48:]
    loss_ref, norm_ref, refs = refs[0], refs[1], refs[2:]
    inside, news, refs = refs[:27], refs[27:48], refs[48:]
    turned, in_sem, out_sem = refs
    loads = [pltpu.make_async_copy(source, dest, in_sem.at[i]) for i, (source, dest) in enumerate(zip(sources, inside))]
    stores = [pltpu.make_async_copy(source, dest, out_sem.at[i]) for i, (source, dest) in enumerate(zip(news, targets))]
    for copy in loads:
        copy.start()
    grads, olds = inside[:6], inside[6:]
    square_sum = sums_ref[1:2, 0:1]
    grad_norm = jnp.sqrt(square_sum)
    factor = jnp.minimum(1.0, CLIP_NORM / (grad_norm + 1e-06))
    norm_ref[...] = grad_norm
    loss_ref[...] = sums_ref[0:1, 0:1] / total_ref[0].astype(F32)
    width = grads[0].shape[1]
    for which in range(7):
        if which < 6:
            loads[which].wait()
        if which == 0:
            turned[...] = grads[0][:, width - LANES :].T
        for copy in loads[6 + 3 * which : 9 + 3 * which]:
            copy.wait()
        weight, first, second = olds[3 * which : 3 * which + 3]
        rows, columns = weight.shape
        chunk = min(8, rows)

        def one(step, carry):
            spot = pl.ds(pl.multiple_of(step * chunk, chunk), chunk)
            if which == 0:
                grad = grads[0][spot, 0:columns]
            elif which == 6:
                grad = turned[features % LANES : features % LANES + rows, 0:columns]
            else:
                grad = grads[which][spot, :]
            values = adamw(weight[spot, :], first[spot, :], second[spot, :], grad * factor, RATES[which])
            for dest, value in zip(news[3 * which : 3 * which + 3], values):
                dest[spot, :] = value
            return carry

        lax.fori_loop(0, rows // chunk, one, 0)
        for copy in stores[3 * which : 3 * which + 3]:
            copy.start()
    for copy in stores:
        copy.wait()


def update_all(olds, sums, totals, pair_total, features):
    vmem = pl.BlockSpec(memory_space=pltpu.VMEM)
    smem = pl.BlockSpec(memory_space=pltpu.SMEM)
    hbm = pl.BlockSpec(memory_space=pltpu.HBM)
    shapes = [jax.ShapeDtypeStruct(old.shape, F32) for old in olds]
    inside = [pltpu.VMEM(value.shape, F32) for value in list(sums) + list(olds)]
    return pl.pallas_call(
        functools.partial(update_kernel, features),
        out_shape=shapes + [jax.ShapeDtypeStruct((1, 1), F32)] * 2,
        in_specs=[smem, vmem] + [hbm] * 27,
        out_specs=[hbm] * 21 + [vmem] * 2,
        scratch_shapes=inside
        + [pltpu.VMEM(old.shape, F32) for old in olds]
        + [
            pltpu.VMEM((LANES, sums[0].shape[0]), F32),
            pltpu.SemaphoreType.DMA((27,)),
            pltpu.SemaphoreType.DMA((21,)),
        ],
        compiler_params=pltpu.CompilerParams(vmem_limit_bytes=60 * MIB),
        name="update",
    )(pair_total, totals, *sums, *olds)


def body(
    views,
    render_w,
    targets,
    pix_mask,
    pairs,
    view_count,
    pair_total,
    embed_weight,
    embed_first,
    embed_second,
    mixer_weight,
    mixer_first,
    mixer_second,
    merge_weight,
    merge_first,
    merge_second,
    expand_weight,
    expand_first,
    expand_second,
    shrink_weight,
    shrink_first,
    shrink_second,
    unpatch_weight,
    unpatch_first,
    unpatch_second,
    norm_params,
    norm_first,
    norm_second,
):
    masters = (embed_weight, mixer_weight, merge_weight, expand_weight, shrink_weight, unpatch_weight, norm_params)
    firsts = (embed_first, mixer_first, merge_first, expand_first, shrink_first, unpatch_first, norm_first)
    seconds = (embed_second, mixer_second, merge_second, expand_second, shrink_second, unpatch_second, norm_second)
    groups = lax.axis_size(NARROW)
    wide_count = lax.axis_size(WIDE)
    features = embed_weight.shape[0]
    kinds = norm_params.shape[0]
    padded = -(-(features + kinds) // LANES) * LANES
    fill = padded - features - kinds
    by_kernel = mixer_weight.shape[0] % 16 == 0

    patches = views.reshape(-1, features)
    rows = patches.shape[0]
    patches = jnp.pad(patches, ((0, 0), (0, padded - features)))
    if by_kernel:
        raw = (embed_weight.T,) + masters[1:6]
        kept = forward_all(raw, norm_params, patches, features % LANES, wide_count, groups)
    else:
        first_shard = jnp.concatenate([embed_weight.T, norm_params.T], 1)
        first_shard = jnp.pad(first_shard.astype(BF16), ((0, 0), (0, fill)))
        shards = [first_shard] + [weight.astype(BF16) for weight in masters[1:6]]
        kept = forward_plain(shards, patches, features, kinds)
    divisor = pair_total[0].astype(F32)
    gauss_low, term = render(
        kept.gaussians, render_w[0], targets[0], pix_mask[0], pairs[0], view_count, pair_total
    )
    if by_kernel:
        *sums, totals = backward_all(
            kept, patches, gauss_low, term, features % LANES, wide_count, groups
        )
        olds = []
        for triple in zip(masters, firsts, seconds):
            olds += triple
        olds[:3] = [old.T for old in olds[:3]]
        *news, loss, grad_norm = update_all(olds, sums, totals, pair_total, features)
        news[:3] = [new.T for new in news[:3]]
        return tuple(news) + (loss[0, 0], grad_norm[0, 0])
    sums, loss_sum, square_sum = backward_plain(kept, patches, gauss_low, term, features, kinds)
    first_sum = sums[0].T
    grads = [first_sum[:features]] + list(sums[1:]) + [first_sum[features : features + kinds]]
    loss = loss_sum / divisor
    grad_norm = jnp.sqrt(square_sum)
    factor = jnp.minimum(1.0, CLIP_NORM / (grad_norm + 1e-06))
    results = []
    for which in range(7):
        results += adamw(masters[which], firsts[which], seconds[which], grads[which] * factor, RATES[which])
    return tuple(results) + (loss, grad_norm)


def solution(mesh):
    columns = P(None, BOTH)
    rows = P(BOTH, None)
    weights = (columns,) * 3 + (rows,) * 15 + (columns,) * 3
    return jax.shard_map(
        body,
        mesh=mesh,
        in_specs=(
            P(WIDE, None, NARROW, None),
            P(WIDE, None, None, None, None),
            P(WIDE, None, None, NARROW),
            P(WIDE, None, NARROW),
            P(WIDE, None, NARROW),
            P(WIDE),
            P(),
        )
        + weights,
        out_specs=weights + (P(), P()),
        check_vma=False,
    )
```

```python
import functools
import heapq

import jax
import jax.numpy as jnp
from jax import lax
from jax.experimental import pallas as pl
from jax.experimental.pallas import tpu as pltpu
from jax.sharding import PartitionSpec as P

D = 1024
HD = 64
P_SIZE = 8
PP = 64
NVIEW = 4
TMAX = 12
STEP = 10
LANES = 128
MIB = 1024 * 1024

DEPTH_WEIGHT = 1.0
CLIP_NORM = 0.01
BETA_ONE = 0.9
BETA_TWO = 0.95
ADAM_EPS = 1e-08
DECAY = 0.05
RATES = (0.05, 0.05, 0.5, 0.05, 0.05, 0.05, 0.8)
MESH = pl.DeviceIdType.MESH
WIDE, NARROW = BOTH = ("wide", "narrow")
HIGHEST = lax.Precision.HIGHEST
F32 = jnp.float32
BF16 = jnp.bfloat16


def matmul(left, right):
    return jnp.dot(left, right, preferred_element_type=F32)


def outer_sum(left, right):
    return lax.dot_general(left, right, (((0,), (0,)), ((), ())), preferred_element_type=F32)


def back_mul(grad, weight):
    return lax.dot_general(grad, weight, (((1,), (1,)), ((), ())), preferred_element_type=F32)


def layer_norm(values, gain, shift):
    centred = values - jnp.mean(values, -1, keepdims=True)
    spread = jnp.mean(centred * centred, -1, keepdims=True)
    return centred * lax.rsqrt(spread + 1e-05) * gain + shift


def exact_gelu(values):
    return jax.nn.gelu(values, approximate=False)


def attention_forward(queries, keys, values):
    length, heads = (queries.shape[0], queries.shape[1])
    blocked = min(512, length)
    scale = HD ** (-0.5)

    def one_block(query_block):
        scores = (
            jnp.einsum("qhd,khd->hqk", query_block, keys, preferred_element_type=jnp.float32)
            * scale
        )
        highest = jnp.max(scores, -1, keepdims=True)
        exponentials = jnp.exp(scores - highest)
        summed = jnp.sum(exponentials, -1, keepdims=True)
        softmaxed = (exponentials / summed).astype(jnp.bfloat16)
        output = jnp.einsum("hqk,khd->qhd", softmaxed, values, preferred_element_type=jnp.float32)
        return (output.astype(jnp.bfloat16), (highest + jnp.log(summed))[:, :, 0])

    output, logsum = lax.map(one_block, queries.reshape(length // blocked, blocked, heads, HD))
    return (output.reshape(length, heads * HD), logsum)


def attention_backward(queries, keys, values, logsum, out_grad):
    length, heads = (queries.shape[0], queries.shape[1])
    blocked = min(512, length)
    scale = HD ** (-0.5)

    def one_block(carry, inputs):
        key_grad, value_grad = carry
        query_block, logsum_block, grad_block = inputs
        scores = (
            jnp.einsum("qhd,khd->hqk", query_block, keys, preferred_element_type=jnp.float32)
            * scale
        )
        softmaxed = jnp.exp(scores - logsum_block[:, :, None])
        value_grad = value_grad + jnp.einsum(
            "hqk,qhd->khd",
            softmaxed.astype(jnp.bfloat16),
            grad_block,
            preferred_element_type=jnp.float32,
        )
        prob_grad = jnp.einsum(
            "qhd,khd->hqk", grad_block, values, preferred_element_type=jnp.float32
        )
        score_grad = softmaxed * (prob_grad - jnp.sum(softmaxed * prob_grad, -1, keepdims=True))
        score_low = score_grad.astype(jnp.bfloat16)
        query_grad = (
            jnp.einsum("hqk,khd->qhd", score_low, keys, preferred_element_type=jnp.float32) * scale
        )
        key_grad = (
            key_grad
            + jnp.einsum("hqk,qhd->khd", score_low, query_block, preferred_element_type=jnp.float32)
            * scale
        )
        return ((key_grad, value_grad), query_grad)

    zeros = jnp.zeros((length, heads, HD), jnp.float32)
    shaped = (
        queries.reshape(length // blocked, blocked, heads, HD),
        logsum,
        out_grad.reshape(length // blocked, blocked, heads, HD),
    )
    (key_grad, value_grad), query_grad = lax.scan(one_block, (zeros, zeros), shaped)
    return (query_grad.reshape(length, heads, HD), key_grad, value_grad)


def adamw(weight, first, second, grad, rate):
    first = BETA_ONE * first + (1.0 - BETA_ONE) * grad
    second = BETA_TWO * second + (1.0 - BETA_TWO) * grad * grad
    first_hat = first / (1.0 - BETA_ONE**STEP)
    second_hat = second / (1.0 - BETA_TWO**STEP)
    weight = weight - rate * (first_hat / (jnp.sqrt(second_hat) + ADAM_EPS) + DECAY * weight)
    return (weight, first, second)


def chip_bits(chips):
    bits, step = [], 1
    while step < chips:
        bits.append(step)
        step *= 2
    return bits


def flip(chip, mask):
    for bit in chip_bits(mask + 1):
        if mask & bit:
            chip = chip + (1 - 2 * (chip // bit % 2)) * bit
    return chip


def column_halves(width):
    first = -(-width // (2 * LANES)) * LANES
    return ((0, first), (first, width - first))


def work_items(widths, order):
    return [(which,) + half + (side,) for which in order for side, half in enumerate(column_halves(widths[which]))]


class Bag:
    def __init__(self, pairs):
        vars(self).update(pairs)


class Place:
    def __init__(self, wide, narrow):
        self.wide, self.narrow = wide, narrow
        self.chips = wide // 2
        self.bits = chip_bits(self.chips)
        self.w = lax.axis_index(WIDE)
        self.n = lax.axis_index(NARROW)
        self.chip = self.w // 2
        self.core = self.w % 2
        self.twin = (2 * self.chip + 1 - self.core, self.n)

    def across(self, mask):
        return (2 * flip(self.chip, mask) + self.core, self.n)

    def along(self, step):
        return (self.w, lax.rem(self.n + step, self.narrow))

    def neighbours(self):
        return (
            [self.twin]
            + [self.across(bit) for bit in self.bits]
            + [self.along(step) for step in range(1, self.narrow)]
        )


class Planner:
    def __init__(self):
        self.now, self.count = 0.0, 0
        self.free, self.events, self.done, self.spare = {}, [], set(), []
        self.refill = lambda: None

    def transfer(self, link, cost, key, event):
        self.free[link] = max(self.now, self.free.get(link, 0.0)) + cost
        self.count += 1
        heapq.heappush(self.events, (self.free[link] + 2.0, self.count, key, event))

    def step(self):
        when, _, key, event = heapq.heappop(self.events)
        self.now = max(self.now, when) + 0.2
        event()
        self.done.add(key)
        self.refill()

    def fill(self, until):
        for index, (keys, cost, work) in enumerate(self.spare):
            if self.now + cost <= until and self.done.issuperset(keys):
                del self.spare[index]
                work()
                self.now += cost
                return True
        return False

    def need(self, keys):
        while not self.done.issuperset(keys):
            if not self.fill(self.events[0][0]):
                self.step()

    def work(self, cost, work):
        while self.events and self.events[0][0] <= self.now:
            self.step()
        self.refill()
        work()
        self.now += cost

    def later(self, cost, work, keys=()):
        entry = (tuple(keys), cost, work)
        self.spare.append(entry)
        return entry

    def force(self, entry):
        if entry in self.spare:
            self.spare.remove(entry)
            self.work(entry[1], entry[2])

    def finish(self):
        self.refill()
        while self.events or self.spare:
            if not self.fill(self.events[0][0] if self.events else 1e9):
                self.step()


LINK = 100e3
Z_AHEAD = 4.0
TWIN_LINK = 600e3


def greet(peers):
    barrier = pltpu.get_barrier_semaphore()
    for peer in peers:
        pl.semaphore_signal(barrier, inc=1, device_id=peer, device_id_type=MESH)
    pl.semaphore_wait(barrier, len(peers))


def normalize(values, gain, shift):
    centred = values - jnp.mean(values, -1, keepdims=True)
    spread = jnp.mean(centred * centred, -1, keepdims=True)
    return centred * lax.rsqrt(spread + 1e-05) * gain + shift


def forward_plan(widths):
    items = []
    for which, cuts in ((0, 1), (1, 3), (2, 1), (3, 2), (5, 1), (4, 2)):
        size = widths[which] // cuts
        for cut in range(cuts):
            for side, (start, width) in enumerate(column_halves(size)):
                items.append((which, cut * size + start, width, side))
    return items


def forward_kernel(items, wide, narrow, lead, ins, outs, scratch, *refs):
    at = Bag(zip(ins + scratch, refs[: len(ins)] + refs[len(ins) + len(outs) :]))
    results = refs[len(ins) : len(ins) + len(outs)]
    weights = [at.first_weight, at.w1, at.w2, at.w3, at.w4, at.w5]
    shards = [at.c0, at.c1, at.c2, at.c3, at.c4, at.c5]
    raw = [at.s0, at.s1, at.s2, at.s3, at.s4, at.s5]
    own_sem, send_sem, recv_sem = at.own_sem, at.send_sem, at.recv_sem
    swap_send, swap_recv, out_sem = at.swap_send, at.swap_recv, at.out_sem
    place = Place(wide, narrow)
    chips, me = place.chips, place.n
    tokens = at.patches.shape[0]
    head_width = D // narrow
    total = len(items)
    started, guarded = [], []

    def start(copy):
        copy.start()
        started.append(copy)

    features = at.s0.shape[1]
    tail = shards[0].shape[1] - LANES
    kinds = at.norm_raw.shape[0]
    kind = lax.broadcasted_iota(jnp.int32, (kinds, LANES), 0)
    spot = lax.broadcasted_iota(jnp.int32, (kinds, LANES), 1)
    put = (spot == kind + lead).astype(F32).astype(BF16)
    shards[0][:, tail:] = outer_sum(at.norm_raw[...].astype(BF16), put).astype(BF16)
    shards[0][:, 0:features] = at.s0[...].astype(BF16)
    for source, dest in zip(raw[1:], shards[1:]):
        dest[...] = source[...].astype(BF16)
    greet(place.neighbours())
    rows_of = [shard.shape[0] for shard in shards]

    def rows_at(which, chip, core, node=None):
        rows = rows_of[which]
        if node is None:
            return pl.ds(pl.multiple_of((chip * 2 + core) * narrow * rows, rows), narrow * rows)
        return pl.ds(pl.multiple_of(((chip * 2 + core) * narrow + node) * rows, rows), rows)

    own = []
    for which in range(6):
        copy = pltpu.make_async_copy(
            shards[which], weights[which].at[rows_at(which, place.chip, place.core, me), :], own_sem.at[which]
        )
        copy.start()
        own.append(copy)

    def remote(item, src, dst, slot, peer):
        return pltpu.make_async_remote_copy(
            src_ref=src,
            dst_ref=dst,
            send_sem=send_sem.at[item, slot],
            recv_sem=recv_sem.at[item, slot],
            device_id=peer,
            device_id_type=MESH,
        )

    def group(item, mask):
        which, begin, width, _ = items[item]
        return weights[which].at[rows_at(which, flip(place.chip, mask), place.core), pl.ds(begin, width)]

    def along(item, sign, hop):
        which, begin, width, _ = items[item]
        columns = pl.ds(begin, width)
        rows = rows_at(which, place.chip, place.core, me - sign * (hop - 1))
        return remote(
            item,
            shards[which].at[:, columns] if hop == 1 else weights[which].at[rows, columns],
            weights[which].at[rows, columns],
            2 * chips + hop - 1 + (narrow - 1 if sign < 0 else 0),
            (place.w, me + sign),
        )

    def has_next(sign):
        return me < narrow - 1 if sign > 0 else me >= 1

    def has_come(sign, hop):
        return me >= hop if sign > 0 else me < narrow - hop

    def start_if(condition, copy):
        @pl.when(condition)
        def _():
            copy.start()

        guarded.append((condition, copy))

    def bits_of(item):
        return place.bits if items[item][3] == 0 else place.bits[::-1]

    def across(item, mask, bit):
        return remote(item, group(item, mask), group(item, mask), mask ^ bit, place.across(bit))

    def to_twin(item, mask):
        return remote(item, group(item, mask), group(item, mask), chips + mask, place.twin)

    plan = Planner()
    waited = set()

    def block_bytes(item):
        which, _, width, _ = items[item]
        return 2 * narrow * rows_of[which] * width

    def twin_event(item, mask):
        return lambda: to_twin(item, mask).wait_recv()

    def onward(item, mask, number):
        bits = bits_of(item)
        size = block_bytes(item)
        for later in range(number, len(bits)):
            start(across(item, mask, bits[later]))
            coming = mask ^ bits[later]
            plan.transfer(
                bits[later], 2 * size / LINK, (item, coming), functools.partial(arrive, item, coming, later)
            )
        start(to_twin(item, mask))
        plan.transfer(-1, size / TWIN_LINK, (item, chips + mask), twin_event(item, mask))

    def arrive(item, mask, number):
        across(item, mask ^ bits_of(item)[number], bits_of(item)[number]).wait_recv()
        onward(item, mask, number + 1)

    def begin_item(item):
        for sign in (1, -1):
            start_if(has_next(sign), along(item, sign, 1))
        line_transfer(item, 1)

    def line_transfer(item, hop):
        cost = 2 * block_bytes(item) / narrow / LINK
        key = (item, 0) if hop == narrow - 1 else (item, -hop)
        plan.transfer(0, cost, key, functools.partial(line_event, item, hop))

    def line_event(item, hop):
        if items[item][0] not in waited:
            waited.add(items[item][0])
            own[items[item][0]].wait()
        for sign in (1, -1):

            @pl.when(has_come(sign, hop))
            def _():
                along(item, sign, hop).wait_recv()

            if hop < narrow - 1:
                start_if(jnp.logical_and(has_come(sign, hop), has_next(sign)), along(item, sign, hop + 1))
        if hop < narrow - 1:
            line_transfer(item, hop + 1)
        else:
            onward(item, 0, 0)

    begun = []

    def refill():
        while len(begun) < total and plan.free.get(0, 0.0) < plan.now + 0.5:
            begin_item(len(begun))
            begun.append(True)

    plan.refill = refill
    refill()

    def need(which, columns=None):
        plan.need(
            [
                (index, key)
                for index, (owner, begin, width, _) in enumerate(items)
                if owner == which and (columns is None or (begin < columns[1] and begin + width > columns[0]))
                for key in range(2 * chips)
            ]
        )

    flushed = []

    def flush(ref):
        index = [vars(at)[name] is ref for name in outs].index(True)
        copy = pltpu.make_async_copy(ref, results[index], out_sem.at[index])
        copy.start()
        flushed.append(copy)

    def swap(src, dst, kind, step):
        return pltpu.make_async_remote_copy(
            src_ref=src,
            dst_ref=dst,
            send_sem=swap_send.at[kind, step],
            recv_sem=swap_recv.at[kind, step],
            device_id=place.along(step),
            device_id_type=MESH,
        )

    gains = at.gains
    embedded, mid, last = at.embedded, at.mid, at.last
    normed, hidden, wave = at.normed, at.hidden, at.wave
    away, qkv, heads_out, returned = at.away, at.qkv, at.heads_out, at.returned

    def turn(dest, source):
        dest[...] = source[...].T
        flush(dest)

    need(0)
    width = weights[0].shape[1]
    kind = lax.broadcasted_iota(jnp.int32, (8, LANES), 0)
    spot = lax.broadcasted_iota(jnp.int32, (8, LANES), 1)
    pick = (spot == kind + lead).astype(F32).astype(BF16)
    gains[...] = back_mul(pick, weights[0][:, width - LANES :])
    flush(gains)

    def embed(block):
        cols = pl.ds(block, 256)
        embedded[:, cols] = back_mul(at.patches[...], weights[0][pl.ds(block, 256), : at.patches.shape[1]])

    for block in range(0, D, 256):
        plan.work(0.5, functools.partial(embed, block))
    flush(embedded)

    def norm_rows(source, row, dest):
        step_rows = 32

        def one(step, carry):
            rows = pl.ds(pl.multiple_of(step * step_rows, step_rows), step_rows)
            dest[rows, :] = normalize(
                source[rows, :], gains[row : row + 1, :], gains[row + 3 : row + 4, :]
            ).astype(BF16)
            return carry

        lax.fori_loop(0, tokens // step_rows, one, 0)

    plan.work(2.0, lambda: norm_rows(embedded, 0, normed))
    turn_first = plan.later(2.0, lambda: turn(at.t1, normed))
    piece = 2 * (narrow - 1) * 2 * tokens * head_width / LINK

    def project(part, step):
        owner = lax.rem(me + step, narrow)
        offset = pl.multiple_of(part * D + owner * head_width, LANES)
        value = matmul(normed[...], weights[1][:, pl.ds(offset, head_width)]).astype(BF16)
        if step:
            away[step - 1, part] = value
            start(swap(away.at[step - 1, part], qkv.at[me, part], part, step))
        else:
            qkv[me, part] = value

    def swap_event(part):
        for step in range(1, narrow):
            swap(away.at[step - 1, part], qkv.at[me, part], part, step).wait_recv()

    for part in range(3):
        need(1, (part * D, part * D + D))
        for step in list(range(1, narrow)) + [0]:
            plan.work(0.7, functools.partial(project, part, step))
        plan.transfer(0, piece, (-1, part), functools.partial(swap_event, part))
    flush(at.w1)
    lane = lax.broadcasted_iota(jnp.int32, (1, LANES), 1)
    scale = HD ** (-0.5)
    length = narrow * tokens
    sides = LANES // HD

    def weigh(step):
        who = lax.rem(me + step, narrow)
        log_sums = jnp.zeros((tokens, LANES), F32)
        sums = jnp.ones((tokens, LANES), F32)
        for pair in range(head_width // LANES):
            lanes = pl.ds(pair * LANES, LANES)
            query = qkv[who, 0, :, lanes].astype(F32)
            key = qkv[:, 1, :, lanes].reshape(length, LANES)
            for side in range(sides):
                head = pair * sides + side
                own_query = (query * jnp.where(lane // HD == side, scale, 0.0)).astype(BF16)
                scores = back_mul(own_query, key)
                highest = jnp.max(scores, -1, keepdims=True)
                exponentials = jnp.exp(scores - highest)
                summed = jnp.sum(exponentials, -1, keepdims=True)
                at.weighed[step, head] = exponentials.astype(BF16)
                log_sums = jnp.where(lane == head, highest + jnp.log(summed), log_sums)
                sums = jnp.where(lane == head, summed, sums)
        at.log_sums[who] = log_sums
        at.weigh_sums[step] = sums

    def attend(step):
        who = lax.rem(me + step, narrow)
        for pair in range(head_width // LANES):
            lanes = pl.ds(pair * LANES, LANES)
            value = qkv[:, 2, :, lanes].reshape(length, LANES)
            out = jnp.zeros((tokens, LANES), F32)
            for side in range(sides):
                head = pair * sides + side
                part = matmul(at.weighed[step, head], value) / at.weigh_sums[step, :, head : head + 1]
                out = jnp.where(lane // HD == side, part, out)
            heads_out[who, :, lanes] = out.astype(BF16)
        if step:
            start(swap(heads_out.at[who], returned.at[me], 3, step))
        else:
            returned[me] = heads_out[who]

    steps = list(range(1, narrow)) + [0]
    plan.need([(-1, 0), (-1, 1)])
    for step in steps:
        plan.work(2.7, functools.partial(weigh, step))
    plan.need([(-1, 2)])
    flush(qkv)

    def return_event(step):
        return lambda: swap(heads_out.at[me], returned.at[me], 3, step).wait_recv()

    for step in steps:
        plan.work(0.9, functools.partial(attend, step))
        if step:
            plan.transfer(0, piece / (narrow - 1), (-2, step), return_event(step))
    flush(heads_out)
    flush(at.log_sums)
    need(2)
    plan.need([(-2, step) for step in range(1, narrow)])

    def merge(block):
        cols = pl.ds(block, 256)
        value = embedded[:, cols]
        for source in range(narrow):
            value = value + matmul(returned[source], weights[2][pl.ds(source * head_width, head_width), cols])
        mid[:, cols] = value

    for block in range(0, D, 256):
        plan.work(0.7, functools.partial(merge, block))
    flush(at.w2)
    flush(mid)
    plan.force(turn_first)
    plan.work(2.0, lambda: norm_rows(mid, 1, normed))

    def turn_returned():
        for source in range(narrow):
            at.t2[pl.ds(source * head_width, head_width), :] = returned[source].T
        flush(at.t2)

    plan.later(2.0, turn_returned)
    turn_second = plan.later(2.0, lambda: turn(at.t3, normed))

    ff = weights[3].shape[1]
    tile = wave.shape[1]
    slopes = at.slopes

    def expand(block):
        wave[...] = matmul(normed[...], weights[3][:, pl.ds(block, tile)])

        def bend(step, carry):
            rows = pl.ds(pl.multiple_of(step * 32, 32), 32)
            x = wave[rows, :]
            half = 0.5 * (1.0 + lax.erf(x * (0.5**0.5)))
            hidden[rows, pl.ds(block, tile)] = (x * half).astype(BF16)
            bell = jnp.exp(-0.5 * x * x) * 0.3989422804014327
            slopes[rows, pl.ds(block, tile)] = (half + x * bell).astype(BF16)
            return carry

        lax.fori_loop(0, tokens // 32, bend, 0)

    for block in range(0, ff, tile):
        need(3, (block, block + tile))
        plan.work(2.5, functools.partial(expand, block))
    flush(at.w3)
    flush(slopes)
    flush(hidden)

    def shrink(block):
        cols = pl.ds(block, 256)
        last[:, cols] = mid[:, cols] + matmul(hidden[...], weights[4][:, cols])

    for block in range(0, D, 256):
        need(4, (block, block + 256))
        plan.work(1.0, functools.partial(shrink, block))
    flush(at.w4)
    flush(last)
    plan.force(turn_second)
    plan.work(2.0, lambda: norm_rows(last, 2, normed))
    need(5)

    def unpatch(block):
        cols = pl.ds(block, 256)
        at.gaussians[:, cols] = matmul(normed[...], weights[5][:, cols])

    for block in range(0, weights[5].shape[1], 256):
        plan.work(0.7, functools.partial(unpatch, block))
    flush(at.w5)
    flush(at.gaussians)
    plan.later(2.0, lambda: turn(at.t5, normed))
    plan.finish()
    for copy in started:
        copy.wait_send()
    for condition, copy in guarded:

        @pl.when(condition)
        def _():
            copy.wait_send()

    for copy in flushed:
        copy.wait()


def forward_all(shards, norms, patches, lead, wide, narrow):
    tokens = patches.shape[0]
    widths = [patches.shape[1]] + [shard.shape[1] for shard in shards[1:]]
    heights = [shard.shape[0] * wide * narrow for shard in shards]
    ff = widths[3]
    head_width = D // narrow
    items = forward_plan(widths)
    slots = wide + 2 * (narrow - 1)
    full = [((height, width), BF16) for height, width in zip(heights, widths)]
    shapes = dict(
        w1=full[1],
        w2=full[2],
        w3=full[3],
        w4=full[4],
        w5=full[5],
        gains=((8, D), F32),
        embedded=((tokens, D), F32),
        mid=((tokens, D), F32),
        last=((tokens, D), F32),
        slopes=((tokens, ff), BF16),
        t1=((D, tokens), BF16),
        t2=((D, tokens), BF16),
        t3=((D, tokens), BF16),
        hidden=((tokens, ff), BF16),
        t5=((D, tokens), BF16),
        qkv=((narrow, 3, tokens, head_width), BF16),
        heads_out=((narrow, tokens, head_width), BF16),
        log_sums=((narrow, tokens, LANES), F32),
        gaussians=((tokens, widths[5]), F32),
    )
    ins = tuple(dict(s0=0, s1=0, s2=0, s3=0, s4=0, s5=0, norm_raw=0, patches=0))
    outs = tuple(shapes)
    extras = dict(
        first_weight=pltpu.VMEM((heights[0], widths[0]), BF16),
        c0=pltpu.VMEM((shards[0].shape[0], widths[0]), BF16),
        c1=pltpu.VMEM(shards[1].shape, BF16),
        c2=pltpu.VMEM(shards[2].shape, BF16),
        c3=pltpu.VMEM(shards[3].shape, BF16),
        c4=pltpu.VMEM(shards[4].shape, BF16),
        c5=pltpu.VMEM(shards[5].shape, BF16),
        normed=pltpu.VMEM((tokens, D), BF16),
        wave=pltpu.VMEM((tokens, 512), F32),
        away=pltpu.VMEM((narrow - 1, 3, tokens, head_width), BF16),
        weighed=pltpu.VMEM((narrow, head_width // HD, tokens, narrow * tokens), BF16),
        weigh_sums=pltpu.VMEM((narrow, tokens, LANES), F32),
        returned=pltpu.VMEM((narrow, tokens, head_width), BF16),
        own_sem=pltpu.SemaphoreType.DMA((6,)),
        send_sem=pltpu.SemaphoreType.DMA((len(items), slots)),
        recv_sem=pltpu.SemaphoreType.DMA((len(items), slots)),
        swap_send=pltpu.SemaphoreType.DMA((4, narrow)),
        swap_recv=pltpu.SemaphoreType.DMA((4, narrow)),
        out_sem=pltpu.SemaphoreType.DMA((len(outs),)),
    )
    scratch = outs + tuple(extras)
    anywhere = pl.BlockSpec(memory_space=pl.ANY)
    results = pl.pallas_call(
        functools.partial(forward_kernel, items, wide, narrow, lead, ins, outs, scratch),
        out_shape=[jax.ShapeDtypeStruct(*shapes[name]) for name in outs],
        in_specs=[pl.BlockSpec(memory_space=pltpu.VMEM)] * len(ins),
        out_specs=[anywhere] * len(outs),
        scratch_shapes=[pltpu.VMEM(*shapes[name]) for name in outs] + list(extras.values()),
        compiler_params=pltpu.CompilerParams(
            collective_id=0, has_side_effects=True, vmem_limit_bytes=60 * MIB
        ),
        name="forward",
    )(*shards, norms, patches)
    return Bag(zip(outs, results))


def backward_plan(widths, pairs):
    items = []
    for which, cuts in ((5, 1), (4, 2), (3, 2), (2, 1), (1, pairs), (0, 1)):
        size = widths[which] // cuts
        if which == 1:
            piece = size // 3
            for cut in range(cuts):
                start = cut * size
                items += [(1, start, piece, 0), (1, start + piece, piece, 1)]
                for side, (shift, width) in enumerate(column_halves(piece)):
                    items.append((1, start + 2 * piece + shift, width, side))
            continue
        for cut in range(cuts):
            for side, (start, width) in enumerate(column_halves(size)):
                items.append((which, cut * size + start, width, side))
    return items


def tile_of(width):
    for tile in (512, 384, 256, 128):
        if width % tile == 0:
            return tile
    return width


def backward_kernel(items, wide, narrow, lead, ins, scratch, *refs):
    src = Bag(zip(ins, refs))
    refs = refs[len(ins) :]
    sums, totals, refs = refs[:6], refs[6], list(refs[7:])
    at = Bag(zip(scratch, refs))
    place = Place(wide, narrow)
    chips, me = place.chips, place.n
    total = len(items)
    refs = refs[len(scratch) :]
    held = [refs.pop(0) for _ in items]
    passed = [[refs.pop(0) for _ in place.bits] for _ in items]
    final = [refs.pop(0) for _ in items]
    spare = [refs.pop(0) for _ in range(6)]
    tokens = src.patches.shape[0]
    head_width = D // narrow
    length = narrow * tokens
    reach = narrow * LANES
    send_sem, recv_sem, tile_send, tile_recv = at.send_sem, at.recv_sem, at.tile_send, at.tile_recv
    swap_send, swap_recv, in_sem, ring_sem = at.swap_send, at.swap_recv, at.in_sem, at.ring_sem
    gains, norms, extra = src.gains, at.norms, at.extra
    stash, d_res, d_norm = at.stash, at.d_res, at.d_norm
    mixed, merge_low, expand_low, shrink_low = at.mixed, at.merge_low, at.expand_low, at.shrink_low

    loaded = [name for name in ins if name in scratch]

    def load(ref):
        index = [vars(at)[name] is ref for name in loaded].index(True)
        return pltpu.make_async_copy(vars(src)[loaded[index]], ref, in_sem.at[index])

    def load_stash(ref):
        return pltpu.make_async_copy(ref, stash, in_sem.at[len(loaded)])

    def ring(ref, slots, rows, columns, index, row):
        slot = lax.rem(index, slots.shape[0])
        return pltpu.make_async_copy(
            ref.at[pl.ds(pl.multiple_of(row, rows), rows), :],
            slots.at[slot, pl.ds(0, rows), pl.ds(0, columns)],
            ring_sem.at[0 if slots is at.tall else 1, slot],
        )

    slope_rows = at.tall.shape[1]
    tall, long = at.tall.shape[0], at.long.shape[0]

    def slope_load(index):
        slot = lax.rem(index, tall)
        return pltpu.make_async_copy(
            src.slopes.at[:, pl.ds(pl.multiple_of(index * slope_rows, slope_rows), slope_rows)],
            at.slope_slots.at[slot],
            ring_sem.at[2, slot],
        )

    u_rows, u_cols = 256, src.w5.shape[1]
    load_stash(src.last).start()
    for index in range(tall):
        ring(src.w5, at.tall, u_rows, u_cols, index, index * u_rows).start()
        slope_load(index).start()
    for index in range(long):
        ring(src.w3, at.long, 128, src.w3.shape[1], index, index * 128).start()
    for name in loaded:
        load(vars(at)[name]).start()

    peers = [(lax.rem(place.w + step, wide), place.n) for step in range(1, wide)]
    peers += [place.along(step) for step in range(1, narrow)]
    greet(peers)

    started, guarded = [], []

    def start(copy):
        copy.start()
        started.append(copy)

    lefts = [at.embed_t, at.t1, at.t2, at.t3, at.shrink_t, at.t5]
    rights = [src.patches, mixed, merge_low, expand_low, at.hidden, src.gauss]

    def remote(item, src, dst, slot, peer):
        return pltpu.make_async_remote_copy(
            src_ref=src,
            dst_ref=dst,
            send_sem=send_sem.at[item, slot],
            recv_sem=recv_sem.at[item, slot],
            device_id=peer,
            device_id_type=MESH,
        )

    def bits_of(item):
        return place.bits[::-1] if items[item][3] == 0 else place.bits

    def groups_of(item):
        size = max(1, 512 // (narrow * spare[items[item][0]].shape[2]))
        if items[item][0] == 4:
            size = chips
        masks = list(range(chips))
        if bits_of(item) and bits_of(item)[0] > 1:
            masks = masks[chips // 2 :] + masks[: chips // 2]
        return [sorted(masks[at_mask : at_mask + size]) for at_mask in range(0, chips, size)]

    def product(item, masks, core, into, plus):
        which, begin, width, _ = items[item]
        left, right = lefts[which], rights[which]
        rows = into.shape[-2]
        span = narrow * rows
        tile = tile_of(width)
        if which == 4:
            size = into.shape[-1]
            for mask in masks:
                column = ((flip(place.chip, mask) * 2 + core) * narrow) * size
                rhs = right[:, pl.ds(pl.multiple_of(column, narrow * size), narrow * size)]
                value = jnp.dot(left[begin : begin + width, :], rhs, preferred_element_type=F32)
                for node in range(narrow):
                    piece = value[:, node * size : (node + 1) * size]
                    if plus:
                        piece = piece + into[mask, node].astype(F32)
                    into[mask, node] = piece.astype(BF16)
            return
        firsts = [((flip(place.chip, mask) * 2 + core) * narrow) * rows for mask in masks]
        with_extra = which == 0 and begin + width == right.shape[1]
        assert not with_extra or tile == width
        part, begin = (begin // reach, begin % reach) if which == 1 else (None, begin)

        def one(step, carry):
            offset = pl.multiple_of(begin + step * tile, LANES)
            local = pl.multiple_of(step * tile, LANES)
            if part is None:
                rhs = right[:, pl.ds(offset, tile)]
            else:
                rhs = right[part // 3, part % 3, :, pl.ds(offset, tile)]
            spots = [pl.ds(pl.multiple_of(first, span), span) for first in firsts]
            lhs = jnp.concatenate([left[spot, :] for spot in spots], 0)
            value = jnp.dot(lhs, rhs, preferred_element_type=F32)
            for index, mask in enumerate(masks):
                piece = value[index * span : (index + 1) * span]
                if with_extra:
                    blank = jnp.zeros((span, tile - LANES), F32)
                    piece = piece + jnp.concatenate([blank, extra[spots[index], :]], 1)
                piece = piece.reshape(narrow, rows, tile)
                if plus:
                    piece = piece + into[mask, :, :, pl.ds(local, tile)].astype(F32)
                into[mask, :, :, pl.ds(local, tile)] = piece.astype(BF16)
            return carry

        lax.fori_loop(0, width // tile, one, 0)

    last_sent = {}
    plan = Planner()

    def to_twin(item, masks):
        which, _, width, _ = items[item]
        some = pl.ds(masks[0], len(masks))
        own = spare[which].at[some] if which == 4 else spare[which].at[some, :, :, pl.ds(0, width)]
        return remote(item, own, held[item].at[some], masks[0], place.twin)

    def across(item, mask, bit, number, slot):
        return remote(
            item, held[item].at[mask], passed[item][number].at[slot], chips + mask, place.across(bit)
        )

    def along(item, sign, hop):
        count = narrow - hop
        first = hop if sign > 0 else 0
        node = hop if sign > 0 else narrow - 1 - hop
        return remote(
            item,
            held[item].at[0, pl.ds(first, count)],
            final[item].at[pl.ds(first + (1 if sign > 0 else 0), count)],
            2 * chips + (0 if sign > 0 else 1),
            (place.w, node),
        )

    def send_along(item, sign, hop):
        sender = me == (hop - 1 if sign > 0 else narrow - hop)

        @pl.when(sender)
        def _():
            along(item, sign, hop).start()

        guarded.append((sender, along(item, sign, hop)))

    def line_event(item, hop):
        for sign in (1, -1):
            count = narrow - hop - 1
            first = hop + 1 if sign > 0 else 0

            @pl.when(me == (hop if sign > 0 else narrow - 1 - hop))
            def _():
                along(item, sign, hop).wait_recv()

                def one(step, carry):
                    spot = first + step
                    value = held[item][0, spot].astype(F32)
                    value = value + final[item][spot + (1 if sign > 0 else 0)].astype(F32)
                    held[item][0, spot] = value.astype(BF16)
                    return carry

                if count:
                    lax.fori_loop(0, count, one, 0)

            if count:
                send_along(item, sign, hop + 1)
        line_transfer(item, hop + 1)

    def line_transfer(item, hop):
        cost = (narrow - hop) * 2 * block_bytes(item) / narrow / LINK
        event = line_event if hop < narrow else finish
        if hop == narrow:
            return finish(item)
        plan.transfer(0 if hop == 1 else 100 + hop, cost, (item, -hop, 0), functools.partial(event, item, hop))

    def leaves(item, mask):
        bits = bits_of(item)
        return min([number for number, bit in enumerate(bits) if mask & bit], default=len(bits))

    def slot_of(item, mask, number):
        bits = bits_of(item)
        kept = [m for m in range(chips) if not any(m & bit for bit in bits[: number + 1])]
        return kept.index(mask)

    def add_into(dest, dest_at, src, src_at):
        dest[dest_at] = (dest[dest_at].astype(F32) + src[src_at].astype(F32)).astype(BF16)

    def block_bytes(item):
        _, nodes, rows, width = held[item].shape
        return 2 * nodes * rows * width

    def push(which, pair=None):
        for item, (owner, begin, _, _) in enumerate(items):
            if owner != which or (pair is not None and begin // (3 * reach) != pair):
                continue
            for masks in groups_of(item):
                cost = len(masks) * block_bytes(item) / 1e6
                plan.work(cost, functools.partial(push_some, item, masks))

    def push_some(item, masks):
        which = items[item][0]
        for key in [key for key in last_sent if key[0] == which and set(key[1]) & set(masks)]:
            last_sent.pop(key).wait_send()
        product(item, masks, 1 - place.core, spare[which], False)
        copy = to_twin(item, masks)
        copy.start()
        last_sent[which, tuple(masks)] = copy
        cost = len(masks) * block_bytes(item) / TWIN_LINK
        plan.transfer(-1, cost, (item, 0, masks[0]), functools.partial(own_event, item, masks))

    def own_event(item, masks):
        to_twin(item, masks).wait_recv()
        product(item, masks, place.core, held[item], True)
        plan.now += len(masks) * block_bytes(item) / 1e6
        plan.done.update((item, 0, mask) for mask in masks)
        for mask in masks:
            onward(item, mask, 0)

    def onward(item, mask, number):
        bits = bits_of(item)
        if number == len(bits):
            lined.append(item)
            refill()
        elif leaves(item, mask) == number:
            kept = mask ^ bits[number]
            start(across(item, mask, bits[number], number, slot_of(item, kept, number)))
            plan.transfer(
                bits[number],
                2 * block_bytes(item) / LINK,
                (item, 1 + number, kept),
                functools.partial(sum_event, item, kept, number),
            )

    lined = []

    def refill():
        while lined and plan.free.get(0, 0.0) < plan.now + Z_AHEAD:
            item = lined.pop(0)
            for sign in (1, -1):
                send_along(item, sign, 1)
            line_transfer(item, 1)

    plan.refill = refill

    def sum_event(item, mask, number):
        plan.need([(item, before, mask) for before in range(number + 1)])
        bit = bits_of(item)[number]
        slot = slot_of(item, mask, number)
        across(item, mask ^ bit, bit, number, slot).wait_recv()
        add_into(held[item], mask, passed[item][number], slot)
        plan.now += block_bytes(item) / 8e5
        onward(item, mask, number + 1)

    squares = []

    def finish(item):
        which, begin, width, _ = items[item]
        acc = at.acc.at[pl.ds(0, held[item].shape[2]), pl.ds(0, held[item].shape[3])]
        acc[...] = held[item][0, me].astype(F32)

        @pl.when(me >= 1)
        def _():
            acc[...] += final[item][me + 1].astype(F32)

        @pl.when(me < narrow - 1)
        def _():
            acc[...] += final[item][me].astype(F32)

        value = acc[...]
        if which == 1:
            for shift in range(0, width, LANES):
                part, spot = (begin + shift) // reach, (begin + shift) % reach
                column = part % 3 * D + spot // LANES * head_width + part // 3 * LANES
                sums[which][:, pl.ds(column, LANES)] = value[:, shift : shift + LANES]
        elif which == 4:
            sums[which][pl.ds(begin, width), :] = value
        else:
            sums[which][:, pl.ds(begin, width)] = value
        squares.append(jnp.sum(value * value))

    norms[...] = jnp.zeros_like(norms)

    def norm_back(row, low, add):
        step_rows = 32

        def one(step, carry):
            rows = pl.ds(pl.multiple_of(step * step_rows, step_rows), step_rows)
            values = stash[rows, :]
            upper = d_norm[rows, :]
            centred = values - jnp.mean(values, -1, keepdims=True)
            rate = lax.rsqrt(jnp.mean(centred * centred, -1, keepdims=True) + 1e-05)
            unit = centred * rate
            norms[row : row + 1, :] += jnp.sum(upper * unit, 0, keepdims=True)
            norms[row + 3 : row + 4, :] += jnp.sum(upper, 0, keepdims=True)
            scaled = upper * gains[row : row + 1, :]
            inner = scaled - jnp.mean(scaled, -1, keepdims=True)
            inner = rate * (inner - unit * jnp.mean(scaled * unit, -1, keepdims=True))
            if add:
                inner = inner + d_res[rows, :]
            d_res[rows, :] = inner
            low[rows, :] = inner.astype(BF16)
            return carry

        lax.fori_loop(0, tokens // step_rows, one, 0)

    load(at.t5).wait()
    plan.now += 5.0
    load_stash(src.last).wait()
    count = D // u_rows
    tall_rows = slope_rows

    def through_unpatch(index, carry):
        ring(src.w5, at.tall, u_rows, u_cols, index, index * u_rows).wait()
        slot = at.tall.at[lax.rem(index, tall)]
        offset = pl.multiple_of(index * u_rows, u_rows)
        d_norm[:, pl.ds(offset, u_rows)] = back_mul(src.gauss[...], slot[0:u_rows, 0:u_cols])

        @pl.when(index + tall < count)
        def _():
            ring(src.w5, at.tall, u_rows, u_cols, index + tall, (index + tall) * u_rows).start()

        return carry

    lax.fori_loop(0, count, through_unpatch, 0)
    for index in range(tall):
        ring(src.w4, at.tall, tall_rows, D, index, index * tall_rows).start()
    norm_back(2, shrink_low, False)
    load_stash(src.mid).start()
    load(at.hidden).wait()
    ff = src.w3.shape[1]
    slabs = ff // tall_rows

    def through_shrink(index, carry):
        ring(src.w4, at.tall, tall_rows, D, index, index * tall_rows).wait()
        slope_load(index).wait()
        slot = lax.rem(index, tall)
        value = back_mul(shrink_low[...], at.tall[slot])
        value = value * at.slope_slots[slot].astype(F32)
        expand_low[:, pl.ds(pl.multiple_of(index * tall_rows, tall_rows), tall_rows)] = value.astype(BF16)

        @pl.when(index + tall < slabs)
        def _():
            ring(src.w4, at.tall, tall_rows, D, index + tall, (index + tall) * tall_rows).start()
            slope_load(index + tall).start()

        return carry

    lax.fori_loop(0, slabs, through_shrink, 0)
    owners = [lax.rem(me + step, narrow) for step in list(range(1, narrow)) + [0]]
    for index in range(min(tall, narrow)):
        ring(src.w2, at.tall, head_width, D, index, owners[index] * head_width).start()
    load(at.t3).wait()
    plan.now += 6.0

    def through_expand(index, carry):
        ring(src.w3, at.long, 128, ff, index, index * 128).wait()
        offset = pl.multiple_of(index * 128, 128)
        d_norm[:, pl.ds(offset, 128)] = back_mul(expand_low[...], at.long[lax.rem(index, long)])

        @pl.when(index + long < D // 128)
        def _():
            ring(src.w3, at.long, 128, ff, index + long, (index + long) * 128).start()

        return carry

    lax.fori_loop(0, D // 128, through_expand, 0)
    for index in range(long):
        ring(src.w1, at.long, 128, 3 * D, index, index * 128).start()
    load_stash(src.mid).wait()
    norm_back(1, merge_low, True)
    load_stash(src.embedded).start()

    def swap(src, dst, kind, step):
        return pltpu.make_async_remote_copy(
            src_ref=src,
            dst_ref=dst,
            send_sem=swap_send.at[kind, step],
            recv_sem=swap_recv.at[kind, step],
            device_id=place.along(step),
            device_id_type=MESH,
        )

    d_heads, away = at.d_heads, at.away
    plan.now += 7.0
    piece = 2 * (narrow - 1) * 2 * tokens * head_width / LINK

    def head_event():
        for step in range(1, narrow):
            swap(away.at[step - 1], d_heads.at[me], 0, step).wait_recv()

    for index, owner in enumerate(owners):
        ring(src.w2, at.tall, head_width, D, index, owner * head_width).wait()
        value = back_mul(merge_low[...], at.tall[index % tall, 0:head_width, :]).astype(BF16)
        if index < narrow - 1:
            away[index] = value
            start(swap(away.at[index], d_heads.at[me], 0, index + 1))
        else:
            d_heads[me] = value
        if index + tall < narrow:
            ring(src.w2, at.tall, head_width, D, index + tall, owners[index + tall] * head_width).start()
    plan.now += 3.0
    plan.transfer(0, piece, (-1, 0, 0), head_event)
    load(at.t2).wait()
    push(5)
    at.shrink_t[...] = shrink_low[...].T
    plan.now += 2.0
    for which in (4, 3, 2):
        push(which)
    load(at.qkv).wait()
    load(at.heads_out).wait()
    load(at.log_sums).wait()
    plan.need([(-1, 0, 0)])

    qkv, heads_out, log_sums, parts = at.qkv, at.heads_out, at.log_sums, at.parts
    key_t, key_acc, value_acc, query_acc = at.key_t, at.key_acc, at.value_acc, at.query_acc
    lane = lax.broadcasted_iota(jnp.int32, (1, LANES), 1)
    sides = LANES // HD
    scale = HD ** (-0.5)
    choose = lax.broadcasted_iota(jnp.int32, (8, LANES), 1) // HD
    choose = (choose == lax.broadcasted_iota(jnp.int32, (8, LANES), 0)).astype(F32)

    def part_swap(pair, step):
        lanes = pl.ds(pair * LANES, LANES)
        who = lax.rem(me + step, narrow)
        return swap(
            parts.at[who, :, :, lanes],
            mixed.at[pair, :, :, pl.ds(pl.multiple_of(me * LANES, LANES), LANES)],
            1 + pair,
            step,
        )

    pushed_pairs = []
    load(at.t1).wait()

    def part_event(pair):
        for step in range(1, narrow):
            part_swap(pair, step).wait_recv()

    for pair in range(head_width // LANES):
        lanes = pl.ds(pair * LANES, LANES)
        key_t[...] = qkv[:, 1, :, lanes].reshape(length, LANES).T
        key_acc[...] = jnp.zeros_like(key_acc)
        value_acc[...] = jnp.zeros_like(value_acc)
        def one_block(step, lanes=lanes, pair=pair):
            who = lax.rem(me + step, narrow)
            query = qkv[who, 0, :, lanes].astype(F32)
            upper = d_heads[who, :, lanes].astype(F32)
            kept = heads_out[who, :, lanes].astype(F32)
            delta = lax.dot_general(
                choose,
                upper * kept,
                (((1,), (1,)), ((), ())),
                precision=HIGHEST,
                preferred_element_type=F32,
            )
            log_rows = log_sums[who].T[pair * sides : (pair + 1) * sides, :]
            masks = [jnp.where(lane // HD == side, 1.0, 0.0) for side in range(sides)]
            own_query = jnp.concatenate([query * (scale * mask) for mask in masks], 0).astype(BF16)
            own_upper = jnp.concatenate([upper * mask for mask in masks], 0).astype(BF16)
            log_row = jnp.concatenate([log_rows[side : side + 1, :] for side in range(sides)], 1)
            delta_row = jnp.concatenate([delta[side : side + 1, :] for side in range(sides)], 1)
            query_acc[...] = jnp.zeros_like(query_acc)

            def block(source, carry):
                rows = pl.ds(pl.multiple_of(source * tokens, tokens), tokens)
                key, value = qkv[source, 1, :, lanes], qkv[source, 2, :, lanes]
                probs = jnp.exp(back_mul(key, own_query) - log_row)
                d_probs = back_mul(value, own_upper)
                d_scores = (probs * (d_probs - delta_row)).astype(BF16)
                value_acc[rows, :] += matmul(probs.astype(BF16), own_upper)
                key_acc[rows, :] += matmul(d_scores, own_query)
                turned = matmul(key_t[:, rows], d_scores)
                for side in range(sides):
                    spot = slice(side * HD, (side + 1) * HD)
                    query_acc[spot, :] += turned[spot, side * tokens : (side + 1) * tokens]
                return carry

            lax.fori_loop(0, narrow, block, 0)
            parts[who, 0, :, lanes] = (query_acc[...].T * scale).astype(BF16)
        for step in range(narrow):
            plan.work(3.0, functools.partial(one_block, step))
            for earlier in range(pair):
                if earlier not in pushed_pairs and (-2, 0, earlier) in plan.done:
                    pushed_pairs.append(earlier)
                    push(1, earlier)
        for source in range(narrow):
            rows = pl.ds(source * tokens, tokens)
            parts[source, 1, :, lanes] = key_acc[rows, :].astype(BF16)
            parts[source, 2, :, lanes] = value_acc[rows, :].astype(BF16)
        for step in range(1, narrow):
            start(part_swap(pair, step))
        plan.now += 1.0
        plan.transfer(0, 1.5 * piece, (-2, 0, pair), functools.partial(part_event, pair))
        mixed[pair, :, :, pl.ds(pl.multiple_of(me * LANES, LANES), LANES)] = parts[me, :, :, lanes]
    for pair in range(head_width // LANES):
        if pair not in pushed_pairs:
            plan.need([(-2, 0, pair)])
            push(1, pair)

    def through_mixer(index, carry):
        ring(src.w1, at.long, 128, 3 * D, index, index * 128).wait()
        slot = lax.rem(index, long)
        value = jnp.zeros((tokens, 128), F32)
        for pair in range(head_width // LANES):
            for part in range(3):
                columns = [part * D + owner * head_width + pair * LANES for owner in range(narrow)]
                weight = [at.long[slot, :, column : column + LANES] for column in columns]
                value = value + back_mul(mixed[pair, part], jnp.concatenate(weight, 1))
        d_norm[:, pl.ds(pl.multiple_of(index * 128, 128), 128)] = value

        @pl.when(index + long < D // 128)
        def _():
            ring(src.w1, at.long, 128, 3 * D, index + long, (index + long) * 128).start()

        return carry

    plan.work(4.0, lambda: lax.fori_loop(0, D // 128, through_mixer, 0))
    load_stash(src.embedded).wait()
    plan.work(3.0, lambda: norm_back(0, at.embed_low, True))
    at.embed_t[...] = at.embed_low[...].T
    turned = jnp.concatenate([norms[...], jnp.zeros((LANES - 8, D), F32)], 0).T
    at.extra[...] = pltpu.roll(turned, lead, 1)
    push(0)
    plan.finish()

    rows = lax.broadcasted_iota(jnp.int32, (8, LANES), 0)
    wide_tiles, narrow_tiles = at.wide_tiles, at.narrow_tiles
    wide_tiles[place.w] = jnp.where(rows == 0, src.term[...], sum(squares))

    def tile_copy(buffer, index, slot, peer):
        return pltpu.make_async_remote_copy(
            src_ref=buffer.at[index],
            dst_ref=buffer.at[index],
            send_sem=tile_send.at[slot],
            recv_sem=tile_recv.at[slot],
            device_id=peer,
            device_id_type=MESH,
        )

    for step in range(1, wide):
        start(tile_copy(wide_tiles, place.w, step - 1, (lax.rem(place.w + step, wide), place.n)))
    for step in range(1, wide):
        tile_copy(wide_tiles, place.w, step - 1, (lax.rem(place.w + step, wide), place.n)).wait_recv()
    whole = wide_tiles[0]
    for index in range(1, wide):
        whole = whole + wide_tiles[index]
    narrow_tiles[place.n] = whole
    for step in range(1, narrow):
        start(tile_copy(narrow_tiles, place.n, wide + step - 1, place.along(step)))
    for step in range(1, narrow):
        tile_copy(narrow_tiles, place.n, wide + step - 1, place.along(step)).wait_recv()
    whole = narrow_tiles[0]
    for index in range(1, narrow):
        whole = whole + narrow_tiles[index]
    totals[...] = whole
    for copy in list(last_sent.values()) + started:
        copy.wait_send()
    for condition, copy in guarded:

        @pl.when(condition)
        def _():
            copy.wait_send()


def backward_all(kept, patches, gauss, term, lead, wide, narrow):
    tokens = patches.shape[0]
    chips = wide // 2
    weights = [kept.w1, kept.w2, kept.w3, kept.w4, kept.w5]
    heights = [D] + [weight.shape[0] for weight in weights]
    widths = [patches.shape[1]] + [weight.shape[1] for weight in weights]
    rows = [height // (wide * narrow) for height in heights]
    head_width = D // narrow
    length = narrow * tokens
    items = backward_plan(widths, head_width // LANES)
    slots = 2 * chips + 2
    streamed = dict(w1=kept.w1, w2=kept.w2, w3=kept.w3, w4=kept.w4, w5=kept.w5)
    streamed.update(last=kept.last, mid=kept.mid, embedded=kept.embedded, slopes=kept.slopes)
    loaded = dict(t5=kept.t5, hidden=kept.hidden, t3=kept.t3, t2=kept.t2, t1=kept.t1)
    loaded.update(qkv=kept.qkv, heads_out=kept.heads_out, log_sums=kept.log_sums)
    whole = dict(gains=kept.gains, patches=patches, gauss=gauss, term=term)
    operands = {**streamed, **loaded, **whole}
    shapes = [jax.ShapeDtypeStruct((rows[which], widths[which]), F32) for which in range(6)]
    shapes[4] = jax.ShapeDtypeStruct((D, rows[4]), F32)
    shapes.append(jax.ShapeDtypeStruct((8, LANES), F32))
    scratch = {name: pltpu.VMEM(value.shape, value.dtype) for name, value in loaded.items()}
    scratch.update(
        acc=pltpu.VMEM((max(rows[3], D // 4), max(width for _, _, width, _ in items)), F32),
        embed_t=pltpu.VMEM((D, tokens), BF16),
        embed_low=pltpu.VMEM((tokens, D), BF16),
        shrink_t=pltpu.VMEM((D, tokens), BF16),
        stash=pltpu.VMEM((tokens, D), F32),
        d_res=pltpu.VMEM((tokens, D), F32),
        d_norm=pltpu.VMEM((tokens, D), F32),
        norms=pltpu.VMEM((8, D), F32),
        extra=pltpu.VMEM((D, LANES), F32),
        shrink_low=pltpu.VMEM((tokens, D), BF16),
        expand_low=pltpu.VMEM((tokens, widths[3]), BF16),
        merge_low=pltpu.VMEM((tokens, D), BF16),
        mixed=pltpu.VMEM((head_width // LANES, 3, tokens, narrow * LANES), BF16),
        tall=pltpu.VMEM((4, 256, D), BF16),
        long=pltpu.VMEM((3, 128, widths[3]), BF16),
        slope_slots=pltpu.VMEM((4, tokens, 256), BF16),
        d_heads=pltpu.VMEM((narrow, tokens, head_width), BF16),
        away=pltpu.VMEM((narrow - 1, tokens, head_width), BF16),
        parts=pltpu.VMEM((narrow, 3, tokens, head_width), BF16),
        key_t=pltpu.VMEM((LANES, length), BF16),
        key_acc=pltpu.VMEM((length, LANES), F32),
        value_acc=pltpu.VMEM((length, LANES), F32),
        query_acc=pltpu.VMEM((LANES, tokens), F32),
        wide_tiles=pltpu.VMEM((wide, 8, LANES), F32),
        narrow_tiles=pltpu.VMEM((narrow, 8, LANES), F32),
        send_sem=pltpu.SemaphoreType.DMA((len(items), slots)),
        recv_sem=pltpu.SemaphoreType.DMA((len(items), slots)),
        tile_send=pltpu.SemaphoreType.DMA((wide + narrow,)),
        tile_recv=pltpu.SemaphoreType.DMA((wide + narrow,)),
        swap_send=pltpu.SemaphoreType.DMA((1 + head_width // LANES, narrow)),
        swap_recv=pltpu.SemaphoreType.DMA((1 + head_width // LANES, narrow)),
        in_sem=pltpu.SemaphoreType.DMA((9,)),
        ring_sem=pltpu.SemaphoreType.DMA((3, 4)),
    )
    blocks = [(width, rows[which]) if which == 4 else (rows[which], width) for which, _, width, _ in items]
    lists = [pltpu.VMEM((chips, narrow) + block, BF16) for block in blocks]
    for block in blocks:
        for bit in chip_bits(chips):
            lists.append(pltpu.VMEM((chips // (2 * bit), narrow) + block, BF16))
    lists += [pltpu.VMEM((narrow + 1,) + block, BF16) for block in blocks]
    for which in range(6):
        widest = max(block for item, block in zip(items, blocks) if item[0] == which)
        lists.append(pltpu.VMEM((chips, narrow) + widest, BF16))
    vmem = pl.BlockSpec(memory_space=pltpu.VMEM)
    hbm = pl.BlockSpec(memory_space=pl.ANY)
    return pl.pallas_call(
        functools.partial(backward_kernel, items, wide, narrow, lead, tuple(operands), tuple(scratch)),
        out_shape=shapes,
        in_specs=[vmem if name in whole else hbm for name in operands],
        out_specs=[vmem] * len(shapes),
        scratch_shapes=list(scratch.values()) + lists,
        compiler_params=pltpu.CompilerParams(
            collective_id=1, has_side_effects=True, vmem_limit_bytes=63 * MIB
        ),
        name="backward",
    )(*operands.values())


def render_kernel(
    gauss_ref, weight_ref, target_ref, mask_ref, pair_ref, view_ref, total_ref, grad_ref, term_ref, feat, dfeat
):
    quads = gauss_ref.shape[0] // NVIEW
    span = weight_ref.shape[1]
    pairs = pair_ref.shape[1]
    scale = 1.0 / total_ref[0].astype(F32)

    def channel(index):
        return gauss_ref[:, index * PP : (index + 1) * PP]

    def shared():
        opacity = jax.nn.sigmoid(channel(3))
        extent = jax.nn.sigmoid(channel(5) + channel(6) + channel(7))
        lead = channel(8)
        denom = 1.0 + lead * lead + channel(9) * channel(9) + channel(10) * channel(10) + channel(11) * channel(11)
        facing = lead * lead / denom
        raw = channel(4)
        depth = jnp.maximum(raw, 0.0) + jnp.log1p(jnp.exp(-jnp.abs(raw)))
        return opacity, extent, lead, denom, facing, raw, depth

    opacity, extent, lead, denom, facing, raw, depth = shared()
    footprint = opacity * extent * facing
    channels = [jax.nn.sigmoid(channel(index)) * footprint for index in range(3)]
    channels += [footprint, depth * footprint]
    for index, value in enumerate(channels):
        for view in range(NVIEW):
            feat[index * quads : (index + 1) * quads, view * PP : (view + 1) * PP] = value[
                view * quads : (view + 1) * quads
            ]
    rendered = jnp.dot(feat[...], weight_ref[...], precision=HIGHEST, preferred_element_type=F32)
    parts = [rendered[index * quads : (index + 1) * quads] for index in range(5)]
    lane = lax.broadcasted_iota(jnp.int32, (quads, span), 1)
    live = jnp.where(lane < view_ref[0] * PP, mask_ref[...], 0).astype(F32)
    term = jnp.zeros((quads, span), F32)
    slopes = []
    for index in range(3):
        error = parts[index] - target_ref[index * quads : (index + 1) * quads, :].astype(F32)
        term = term + live * error * error
        slopes.append(2.0 * scale * live * error)
    below = 1.0 + parts[3]
    depth_out = parts[4] / below

    first, second = pair_ref[0:1, :], pair_ref[1:2, :]
    least = jnp.minimum(first, second)
    down = (jnp.abs(first - second) == P_SIZE).astype(jnp.int32)
    place = quads * PP
    slot, local = least // place, least % place
    high = down * quads + local // PP
    low = slot * PP + local % PP
    high_hot = (lax.broadcasted_iota(jnp.int32, (2 * quads, pairs), 0) == high).astype(F32).astype(BF16)
    low_hot = (lax.broadcasted_iota(jnp.int32, (span, pairs), 0) == low).astype(F32).astype(BF16)
    counts = back_mul(high_hot, low_hot)
    slope = jnp.zeros((quads, span), F32)
    for which, shift in enumerate((1, P_SIZE)):
        count = counts[which * quads : (which + 1) * quads]
        weight = DEPTH_WEIGHT * count * live * pltpu.roll(live, span - shift, 1)
        gap = depth_out - pltpu.roll(depth_out, span - shift, 1)
        term = term + weight * gap * gap
        pull = 2.0 * scale * weight * gap
        slope = slope + pull - pltpu.roll(pull, shift, 1)
    term_ref[...] = jnp.full(term_ref.shape, jnp.sum(term), F32)
    over = slope / below
    slopes += [-over * depth_out, over]
    stacked = jnp.concatenate(slopes, 0)
    dfeat[...] = lax.dot_general(
        stacked, weight_ref[...], (((1,), (1,)), ((), ())), precision=HIGHEST, preferred_element_type=F32
    )

    def feature_grad(index):
        return jnp.concatenate(
            [
                dfeat[index * quads : (index + 1) * quads, view * PP : (view + 1) * PP]
                for view in range(NVIEW)
            ],
            0,
        )

    def put(index, value):
        grad_ref[:, index * PP : (index + 1) * PP] = value.astype(BF16)

    d_foot = feature_grad(3)
    for index in range(3):
        tint = jax.nn.sigmoid(channel(index))
        upper = feature_grad(index)
        d_foot = d_foot + upper * tint
        put(index, upper * footprint * tint * (1.0 - tint))
    d_last = feature_grad(4)
    d_foot = d_foot + d_last * depth
    put(3, d_foot * extent * facing * opacity * (1.0 - opacity))
    put(4, d_last * footprint * jax.nn.sigmoid(raw))
    d_extent = d_foot * opacity * facing * extent * (1.0 - extent)
    for index in (5, 6, 7):
        put(index, d_extent)
    d_facing = d_foot * opacity * extent
    put(8, d_facing * 2.0 * lead / denom * (1.0 - facing))
    for index in (9, 10, 11):
        put(index, -2.0 * d_facing * facing / denom * channel(index))


def render(gaussians, weights, targets, mask, pairs, view_count, pair_total):
    rows = gaussians.shape[0]
    quads = rows // NVIEW
    slots, views = weights.shape[:2]
    spread = weights.transpose(1, 2, 0, 3).reshape(views * PP, slots * PP)
    wanted = targets.reshape(slots, 3, quads, PP).transpose(1, 2, 0, 3).reshape(3 * quads, slots * PP)
    valid = mask.reshape(slots, quads, PP).transpose(1, 0, 2).reshape(quads, slots * PP)
    vmem = pl.BlockSpec(memory_space=pltpu.VMEM)
    smem = pl.BlockSpec(memory_space=pltpu.SMEM)
    return pl.pallas_call(
        render_kernel,
        out_shape=[
            jax.ShapeDtypeStruct(gaussians.shape, BF16),
            jax.ShapeDtypeStruct((8, LANES), F32),
        ],
        in_specs=[vmem] * 5 + [smem] * 2,
        out_specs=[vmem] * 2,
        scratch_shapes=[pltpu.VMEM((5 * quads, views * PP), F32)] * 2,
        compiler_params=pltpu.CompilerParams(vmem_limit_bytes=48 * MIB),
        name="render",
    )(gaussians, spread, wanted, valid, pairs, view_count, pair_total)


def forward_plain(shards, patches, features, kinds):
    weights = [lax.all_gather(shard, BOTH, axis=0, tiled=True) for shard in shards]
    groups = lax.axis_size(NARROW)
    rows = patches.shape[0]
    gains = weights[0][:, features : features + kinds].T.astype(F32)
    embedded = back_mul(patches[:, :features], weights[0][:, :features])
    normed_one = layer_norm(embedded, gains[0], gains[3]).astype(BF16)
    mixed = matmul(normed_one, weights[1]).astype(BF16).reshape(rows, 3, groups, -1)
    mixed = mixed.transpose(2, 1, 0, 3)
    qkv = lax.all_to_all(mixed, NARROW, split_axis=0, concat_axis=0, tiled=True)
    width = qkv.shape[-1]
    length = groups * rows
    heads = width // HD
    parts = [qkv[:, part].reshape(length, heads, HD) for part in range(3)]
    attended, logsum = attention_forward(*parts)
    log_sums = logsum.transpose(0, 2, 1).reshape(groups, rows, heads)
    returned = lax.all_to_all(
        attended.reshape(groups, rows, width), NARROW, split_axis=0, concat_axis=0, tiled=True
    )
    returned = returned.transpose(1, 0, 2).reshape(rows, D)
    mid = embedded + matmul(returned, weights[2])
    normed_two = layer_norm(mid, gains[1], gains[4]).astype(BF16)
    expanded = matmul(normed_two, weights[3])
    half = 0.5 * (1.0 + lax.erf(expanded * (0.5**0.5)))
    activated = (expanded * half).astype(BF16)
    bell = jnp.exp(-0.5 * expanded * expanded) * 0.3989422804014327
    slopes = (half + expanded * bell).astype(BF16)
    last = mid + matmul(activated, weights[4])
    normed_three = layer_norm(last, gains[2], gains[5]).astype(BF16)
    return Bag(
        dict(
        w1=weights[1],
        w2=weights[2],
        w3=weights[3],
        w4=weights[4],
        w5=weights[5],
        gains=gains,
        embedded=embedded,
        mid=mid,
        last=last,
        slopes=slopes,
        t1=normed_one.T,
        t2=returned.T,
        t3=normed_two.T,
        hidden=activated,
        t5=normed_three.T,
        qkv=qkv,
        heads_out=attended,
        log_sums=log_sums,
        gaussians=matmul(normed_three, weights[5]),
    ).items())


def backward_plain(kept, patches, gauss_low, term, features, kinds):
    gains = kept.gains
    weights = [None, kept.w1, kept.w2, kept.w3, kept.w4, kept.w5]
    norm_back_one = jax.vjp(layer_norm, kept.embedded, gains[0], gains[3])[1]
    norm_back_two = jax.vjp(layer_norm, kept.mid, gains[1], gains[4])[1]
    norm_back_three = jax.vjp(layer_norm, kept.last, gains[2], gains[5])[1]
    qkv = kept.qkv
    groups, _, rows, width = qkv.shape
    length = groups * rows
    heads = width // HD
    queries, keys, values = (qkv[:, part].reshape(length, heads, HD) for part in range(3))
    blocked = min(512, length)
    logsum = kept.log_sums[:, :, :heads].reshape(length // blocked, blocked, heads)
    residual_grad, gain_three, shift_three = norm_back_three(back_mul(gauss_low, weights[5]))
    shrink_low = residual_grad.astype(BF16)
    expand_low = (back_mul(shrink_low, weights[4]) * kept.slopes.astype(F32)).astype(BF16)
    through_two, gain_two, shift_two = norm_back_two(back_mul(expand_low, weights[3]))
    residual_grad = residual_grad + through_two
    merge_low = residual_grad.astype(BF16)
    out_grad = back_mul(merge_low, weights[2]).astype(BF16).reshape(rows, groups, width)
    head_grad = lax.all_to_all(
        out_grad.transpose(1, 0, 2), NARROW, split_axis=0, concat_axis=0, tiled=True
    ).reshape(length, heads, HD)
    grads = attention_backward(queries, keys, values, logsum.transpose(0, 2, 1), head_grad)
    stacked = jnp.stack(grads, 1).astype(BF16).reshape(groups, rows, 3, width)
    mixed_grad = lax.all_to_all(stacked, NARROW, split_axis=0, concat_axis=0, tiled=True)
    mixed_grad = mixed_grad.transpose(1, 2, 0, 3).reshape(rows, 3 * D)
    through_one, gain_one, shift_one = norm_back_one(back_mul(mixed_grad, weights[1]))
    embed_grad = (residual_grad + through_one).astype(BF16)
    grad_norms = jnp.stack([gain_one, gain_two, gain_three, shift_one, shift_two, shift_three])
    lefts = [embed_grad.T, kept.t1, kept.t2, kept.t3, kept.hidden.T, kept.t5]
    rights = [patches, mixed_grad, merge_low, expand_low, shrink_low, gauss_low]
    products = [matmul(left, right) for left, right in zip(lefts, rights)]
    products[0] = products[0].at[:, features : features + kinds].add(grad_norms.T)
    sums = [
        lax.psum_scatter(
            product.astype(BF16), BOTH, scatter_dimension=0, tiled=True
        ).astype(F32)
        for product in products
    ]
    squares = sum(jnp.sum(part * part) for part in sums)
    loss_sum, square_sum = lax.psum((term[0, 0], squares), BOTH)
    return sums, loss_sum, square_sum


def update_kernel(features, total_ref, sums_ref, *refs):
    sources, targets, refs = refs[:27], refs[27:48], refs[48:]
    loss_ref, norm_ref, refs = refs[0], refs[1], refs[2:]
    inside, news, refs = refs[:27], refs[27:48], refs[48:]
    turned, turned_four, in_sem, out_sem = refs
    loads = [pltpu.make_async_copy(source, dest, in_sem.at[i]) for i, (source, dest) in enumerate(zip(sources, inside))]
    stores = [pltpu.make_async_copy(source, dest, out_sem.at[i]) for i, (source, dest) in enumerate(zip(news, targets))]
    for copy in loads:
        copy.start()
    grads, olds = inside[:6], inside[6:]
    square_sum = sums_ref[1:2, 0:1]
    grad_norm = jnp.sqrt(square_sum)
    factor = jnp.minimum(1.0, CLIP_NORM / (grad_norm + 1e-06))
    norm_ref[...] = grad_norm
    loss_ref[...] = sums_ref[0:1, 0:1] / total_ref[0].astype(F32)
    width = grads[0].shape[1]
    for which in range(7):
        if which < 6:
            loads[which].wait()
        if which == 0:
            turned[...] = grads[0][:, width - LANES :].T
        if which == 4:
            turned_four[...] = grads[4][...].T
        for copy in loads[6 + 3 * which : 9 + 3 * which]:
            copy.wait()
        weight, first, second = olds[3 * which : 3 * which + 3]
        rows, columns = weight.shape
        chunk = min(8, rows)

        def one(step, carry):
            spot = pl.ds(pl.multiple_of(step * chunk, chunk), chunk)
            if which == 0:
                grad = grads[0][spot, 0:columns]
            elif which == 4:
                grad = turned_four[spot, :]
            elif which == 6:
                grad = turned[features % LANES : features % LANES + rows, 0:columns]
            else:
                grad = grads[which][spot, :]
            values = adamw(weight[spot, :], first[spot, :], second[spot, :], grad * factor, RATES[which])
            for dest, value in zip(news[3 * which : 3 * which + 3], values):
                dest[spot, :] = value
            return carry

        lax.fori_loop(0, rows // chunk, one, 0)
        for copy in stores[3 * which : 3 * which + 3]:
            copy.start()
    for copy in stores:
        copy.wait()


def update_all(olds, sums, totals, pair_total, features):
    vmem = pl.BlockSpec(memory_space=pltpu.VMEM)
    smem = pl.BlockSpec(memory_space=pltpu.SMEM)
    hbm = pl.BlockSpec(memory_space=pltpu.HBM)
    shapes = [jax.ShapeDtypeStruct(old.shape, F32) for old in olds]
    inside = [pltpu.VMEM(value.shape, F32) for value in list(sums) + list(olds)]
    return pl.pallas_call(
        functools.partial(update_kernel, features),
        out_shape=shapes + [jax.ShapeDtypeStruct((1, 1), F32)] * 2,
        in_specs=[smem, vmem] + [hbm] * 27,
        out_specs=[hbm] * 21 + [vmem] * 2,
        scratch_shapes=inside
        + [pltpu.VMEM(old.shape, F32) for old in olds]
        + [
            pltpu.VMEM((LANES, sums[0].shape[0]), F32),
            pltpu.VMEM(olds[12].shape, F32),
            pltpu.SemaphoreType.DMA((27,)),
            pltpu.SemaphoreType.DMA((21,)),
        ],
        compiler_params=pltpu.CompilerParams(vmem_limit_bytes=60 * MIB),
        name="update",
    )(pair_total, totals, *sums, *olds)


def body(
    views,
    render_w,
    targets,
    pix_mask,
    pairs,
    view_count,
    pair_total,
    embed_weight,
    embed_first,
    embed_second,
    mixer_weight,
    mixer_first,
    mixer_second,
    merge_weight,
    merge_first,
    merge_second,
    expand_weight,
    expand_first,
    expand_second,
    shrink_weight,
    shrink_first,
    shrink_second,
    unpatch_weight,
    unpatch_first,
    unpatch_second,
    norm_params,
    norm_first,
    norm_second,
):
    masters = (embed_weight, mixer_weight, merge_weight, expand_weight, shrink_weight, unpatch_weight, norm_params)
    firsts = (embed_first, mixer_first, merge_first, expand_first, shrink_first, unpatch_first, norm_first)
    seconds = (embed_second, mixer_second, merge_second, expand_second, shrink_second, unpatch_second, norm_second)
    groups = lax.axis_size(NARROW)
    wide_count = lax.axis_size(WIDE)
    features = embed_weight.shape[0]
    kinds = norm_params.shape[0]
    padded = -(-(features + kinds) // LANES) * LANES
    fill = padded - features - kinds
    by_kernel = mixer_weight.shape[0] % 16 == 0 and shrink_weight.shape[0] % LANES == 0

    patches = views.reshape(-1, features)
    rows = patches.shape[0]
    patches = jnp.pad(patches, ((0, 0), (0, padded - features)))
    if by_kernel:
        raw = (embed_weight.T,) + masters[1:6]
        kept = forward_all(raw, norm_params, patches, features % LANES, wide_count, groups)
    else:
        first_shard = jnp.concatenate([embed_weight.T, norm_params.T], 1)
        first_shard = jnp.pad(first_shard.astype(BF16), ((0, 0), (0, fill)))
        shards = [first_shard] + [weight.astype(BF16) for weight in masters[1:6]]
        kept = forward_plain(shards, patches, features, kinds)
    divisor = pair_total[0].astype(F32)
    gauss_low, term = render(
        kept.gaussians, render_w[0], targets[0], pix_mask[0], pairs[0], view_count, pair_total
    )
    if by_kernel:
        *sums, totals = backward_all(
            kept, patches, gauss_low, term, features % LANES, wide_count, groups
        )
        olds = []
        for triple in zip(masters, firsts, seconds):
            olds += triple
        olds[:3] = [old.T for old in olds[:3]]
        *news, loss, grad_norm = update_all(olds, sums, totals, pair_total, features)
        news[:3] = [new.T for new in news[:3]]
        return tuple(news) + (loss[0, 0], grad_norm[0, 0])
    sums, loss_sum, square_sum = backward_plain(kept, patches, gauss_low, term, features, kinds)
    first_sum = sums[0].T
    grads = [first_sum[:features]] + list(sums[1:]) + [first_sum[features : features + kinds]]
    loss = loss_sum / divisor
    grad_norm = jnp.sqrt(square_sum)
    factor = jnp.minimum(1.0, CLIP_NORM / (grad_norm + 1e-06))
    results = []
    for which in range(7):
        results += adamw(masters[which], firsts[which], seconds[which], grads[which] * factor, RATES[which])
    return tuple(results) + (loss, grad_norm)


def solution(mesh):
    columns = P(None, BOTH)
    rows = P(BOTH, None)
    weights = (columns,) * 3 + (rows,) * 15 + (columns,) * 3
    return jax.shard_map(
        body,
        mesh=mesh,
        in_specs=(
            P(WIDE, None, NARROW, None),
            P(WIDE, None, None, None, None),
            P(WIDE, None, None, NARROW),
            P(WIDE, None, NARROW),
            P(WIDE, None, NARROW),
            P(WIDE),
            P(),
        )
        + weights,
        out_specs=weights + (P(), P()),
        check_vma=False,
    )
```

```python
import functools
import heapq

import jax
import jax.numpy as jnp
from jax import lax
from jax.experimental import pallas as pl
from jax.experimental.pallas import tpu as pltpu
from jax.sharding import PartitionSpec as P

D = 1024
HD = 64
P_SIZE = 8
PP = 64
NVIEW = 4
TMAX = 12
STEP = 10
LANES = 128
MIB = 1024 * 1024

DEPTH_WEIGHT = 1.0
CLIP_NORM = 0.01
BETA_ONE = 0.9
BETA_TWO = 0.95
ADAM_EPS = 1e-08
DECAY = 0.05
RATES = (0.05, 0.05, 0.5, 0.05, 0.05, 0.05, 0.8)
MESH = pl.DeviceIdType.MESH
WIDE, NARROW = BOTH = ("wide", "narrow")
HIGHEST = lax.Precision.HIGHEST
F32 = jnp.float32
BF16 = jnp.bfloat16


def matmul(left, right):
    return jnp.dot(left, right, preferred_element_type=F32)


def outer_sum(left, right):
    return lax.dot_general(left, right, (((0,), (0,)), ((), ())), preferred_element_type=F32)


def back_mul(grad, weight):
    return lax.dot_general(grad, weight, (((1,), (1,)), ((), ())), preferred_element_type=F32)


def layer_norm(values, gain, shift):
    centred = values - jnp.mean(values, -1, keepdims=True)
    spread = jnp.mean(centred * centred, -1, keepdims=True)
    return centred * lax.rsqrt(spread + 1e-05) * gain + shift


def exact_gelu(values):
    return jax.nn.gelu(values, approximate=False)


def attention_forward(queries, keys, values):
    length, heads = (queries.shape[0], queries.shape[1])
    blocked = min(512, length)
    scale = HD ** (-0.5)

    def one_block(query_block):
        scores = (
            jnp.einsum("qhd,khd->hqk", query_block, keys, preferred_element_type=jnp.float32)
            * scale
        )
        highest = jnp.max(scores, -1, keepdims=True)
        exponentials = jnp.exp(scores - highest)
        summed = jnp.sum(exponentials, -1, keepdims=True)
        softmaxed = (exponentials / summed).astype(jnp.bfloat16)
        output = jnp.einsum("hqk,khd->qhd", softmaxed, values, preferred_element_type=jnp.float32)
        return (output.astype(jnp.bfloat16), (highest + jnp.log(summed))[:, :, 0])

    output, logsum = lax.map(one_block, queries.reshape(length // blocked, blocked, heads, HD))
    return (output.reshape(length, heads * HD), logsum)


def attention_backward(queries, keys, values, logsum, out_grad):
    length, heads = (queries.shape[0], queries.shape[1])
    blocked = min(512, length)
    scale = HD ** (-0.5)

    def one_block(carry, inputs):
        key_grad, value_grad = carry
        query_block, logsum_block, grad_block = inputs
        scores = (
            jnp.einsum("qhd,khd->hqk", query_block, keys, preferred_element_type=jnp.float32)
            * scale
        )
        softmaxed = jnp.exp(scores - logsum_block[:, :, None])
        value_grad = value_grad + jnp.einsum(
            "hqk,qhd->khd",
            softmaxed.astype(jnp.bfloat16),
            grad_block,
            preferred_element_type=jnp.float32,
        )
        prob_grad = jnp.einsum(
            "qhd,khd->hqk", grad_block, values, preferred_element_type=jnp.float32
        )
        score_grad = softmaxed * (prob_grad - jnp.sum(softmaxed * prob_grad, -1, keepdims=True))
        score_low = score_grad.astype(jnp.bfloat16)
        query_grad = (
            jnp.einsum("hqk,khd->qhd", score_low, keys, preferred_element_type=jnp.float32) * scale
        )
        key_grad = (
            key_grad
            + jnp.einsum("hqk,qhd->khd", score_low, query_block, preferred_element_type=jnp.float32)
            * scale
        )
        return ((key_grad, value_grad), query_grad)

    zeros = jnp.zeros((length, heads, HD), jnp.float32)
    shaped = (
        queries.reshape(length // blocked, blocked, heads, HD),
        logsum,
        out_grad.reshape(length // blocked, blocked, heads, HD),
    )
    (key_grad, value_grad), query_grad = lax.scan(one_block, (zeros, zeros), shaped)
    return (query_grad.reshape(length, heads, HD), key_grad, value_grad)


def adamw(weight, first, second, grad, rate):
    first = BETA_ONE * first + (1.0 - BETA_ONE) * grad
    second = BETA_TWO * second + (1.0 - BETA_TWO) * grad * grad
    first_hat = first / (1.0 - BETA_ONE**STEP)
    second_hat = second / (1.0 - BETA_TWO**STEP)
    weight = weight - rate * (first_hat / (jnp.sqrt(second_hat) + ADAM_EPS) + DECAY * weight)
    return (weight, first, second)


def chip_bits(chips):
    bits, step = [], 1
    while step < chips:
        bits.append(step)
        step *= 2
    return bits


def flip(chip, mask):
    for bit in chip_bits(mask + 1):
        if mask & bit:
            chip = chip + (1 - 2 * (chip // bit % 2)) * bit
    return chip


def column_halves(width):
    first = -(-width // (2 * LANES)) * LANES
    return ((0, first), (first, width - first))


def work_items(widths, order):
    return [(which,) + half + (side,) for which in order for side, half in enumerate(column_halves(widths[which]))]


class Bag:
    def __init__(self, pairs):
        vars(self).update(pairs)


class Place:
    def __init__(self, wide, narrow):
        self.wide, self.narrow = wide, narrow
        self.chips = wide // 2
        self.bits = chip_bits(self.chips)
        self.w = lax.axis_index(WIDE)
        self.n = lax.axis_index(NARROW)
        self.chip = self.w // 2
        self.core = self.w % 2
        self.twin = (2 * self.chip + 1 - self.core, self.n)

    def across(self, mask):
        return (2 * flip(self.chip, mask) + self.core, self.n)

    def along(self, step):
        return (self.w, lax.rem(self.n + step, self.narrow))

    def neighbours(self):
        return (
            [self.twin]
            + [self.across(bit) for bit in self.bits]
            + [self.along(step) for step in range(1, self.narrow)]
        )


class Planner:
    def __init__(self):
        self.now, self.count = 0.0, 0
        self.free, self.events, self.done, self.spare = {}, [], set(), []
        self.refill = lambda: None

    def transfer(self, link, cost, key, event):
        self.free[link] = max(self.now, self.free.get(link, 0.0)) + cost
        self.count += 1
        heapq.heappush(self.events, (self.free[link] + 2.0, self.count, key, event))

    def step(self):
        when, _, key, event = heapq.heappop(self.events)
        self.now = max(self.now, when) + 0.2
        event()
        self.done.add(key)
        self.refill()

    def fill(self, until):
        for index, (keys, cost, work) in enumerate(self.spare):
            if self.now + cost <= until and self.done.issuperset(keys):
                del self.spare[index]
                work()
                self.now += cost
                return True
        return False

    def need(self, keys):
        while not self.done.issuperset(keys):
            if not self.fill(self.events[0][0]):
                self.step()

    def work(self, cost, work):
        while self.events and self.events[0][0] <= self.now:
            self.step()
        self.refill()
        work()
        self.now += cost

    def later(self, cost, work, keys=()):
        entry = (tuple(keys), cost, work)
        self.spare.append(entry)
        return entry

    def force(self, entry):
        if entry in self.spare:
            self.spare.remove(entry)
            self.work(entry[1], entry[2])

    def finish(self):
        self.refill()
        while self.events or self.spare:
            if not self.fill(self.events[0][0] if self.events else 1e9):
                self.step()


LINK = 90e3
Z_AHEAD = 4.0
Z_EARLY = 1.0
Z_LATE = 2.0
TWIN_LINK = 600e3


def greet(peers):
    barrier = pltpu.get_barrier_semaphore()
    for peer in peers:
        pl.semaphore_signal(barrier, inc=1, device_id=peer, device_id_type=MESH)
    pl.semaphore_wait(barrier, len(peers))


def normalize(values, gain, shift):
    centred = values - jnp.mean(values, -1, keepdims=True)
    spread = jnp.mean(centred * centred, -1, keepdims=True)
    return centred * lax.rsqrt(spread + 1e-05) * gain + shift


def forward_plan(widths):
    items = []
    for which, cuts in ((0, 1), (1, 3), (2, 1), (3, 2), (5, 1), (4, 2)):
        size = widths[which] // cuts
        for cut in range(cuts):
            for side, (start, width) in enumerate(column_halves(size)):
                items.append((which, cut * size + start, width, side))
    return items


def forward_kernel(items, wide, narrow, lead, ins, outs, scratch, *refs):
    at = Bag(zip(ins + scratch, refs[: len(ins)] + refs[len(ins) + len(outs) :]))
    results = refs[len(ins) : len(ins) + len(outs)]
    weights = [at.first_weight, at.w1, at.w2, at.w3, at.w4, at.w5]
    shards = [at.c0, at.c1, at.c2, at.c3, at.c4, at.c5]
    raw = [at.s0, at.s1, at.s2, at.s3, at.s4, at.s5]
    own_sem, send_sem, recv_sem = at.own_sem, at.send_sem, at.recv_sem
    swap_send, swap_recv, out_sem = at.swap_send, at.swap_recv, at.out_sem
    place = Place(wide, narrow)
    chips, me = place.chips, place.n
    tokens = at.patches.shape[0]
    head_width = D // narrow
    total = len(items)
    started, guarded = [], []

    def start(copy):
        copy.start()
        started.append(copy)

    features = at.s0.shape[1]
    tail = shards[0].shape[1] - LANES
    kinds = at.norm_raw.shape[0]
    kind = lax.broadcasted_iota(jnp.int32, (kinds, LANES), 0)
    spot = lax.broadcasted_iota(jnp.int32, (kinds, LANES), 1)
    put = (spot == kind + lead).astype(F32).astype(BF16)
    shards[0][:, tail:] = outer_sum(at.norm_raw[...].astype(BF16), put).astype(BF16)
    shards[0][:, 0:features] = at.s0[...].astype(BF16)
    for source, dest in zip(raw[1:], shards[1:]):
        dest[...] = source[...].astype(BF16)
    greet(place.neighbours())
    rows_of = [shard.shape[0] for shard in shards]

    def rows_at(which, chip, core, node=None):
        rows = rows_of[which]
        if node is None:
            return pl.ds(pl.multiple_of((chip * 2 + core) * narrow * rows, rows), narrow * rows)
        return pl.ds(pl.multiple_of(((chip * 2 + core) * narrow + node) * rows, rows), rows)

    own = []
    for which in range(6):
        copy = pltpu.make_async_copy(
            shards[which], weights[which].at[rows_at(which, place.chip, place.core, me), :], own_sem.at[which]
        )
        copy.start()
        own.append(copy)

    def remote(item, src, dst, slot, peer):
        return pltpu.make_async_remote_copy(
            src_ref=src,
            dst_ref=dst,
            send_sem=send_sem.at[item, slot],
            recv_sem=recv_sem.at[item, slot],
            device_id=peer,
            device_id_type=MESH,
        )

    def group(item, mask):
        which, begin, width, _ = items[item]
        return weights[which].at[rows_at(which, flip(place.chip, mask), place.core), pl.ds(begin, width)]

    def along(item, sign, hop):
        which, begin, width, _ = items[item]
        columns = pl.ds(begin, width)
        rows = rows_at(which, place.chip, place.core, me - sign * (hop - 1))
        return remote(
            item,
            shards[which].at[:, columns] if hop == 1 else weights[which].at[rows, columns],
            weights[which].at[rows, columns],
            2 * chips + hop - 1 + (narrow - 1 if sign < 0 else 0),
            (place.w, me + sign),
        )

    def has_next(sign):
        return me < narrow - 1 if sign > 0 else me >= 1

    def has_come(sign, hop):
        return me >= hop if sign > 0 else me < narrow - hop

    def start_if(condition, copy):
        @pl.when(condition)
        def _():
            copy.start()

        guarded.append((condition, copy))

    def bits_of(item):
        return place.bits if items[item][3] == 0 else place.bits[::-1]

    def across(item, mask, bit):
        return remote(item, group(item, mask), group(item, mask), mask ^ bit, place.across(bit))

    def to_twin(item, mask):
        return remote(item, group(item, mask), group(item, mask), chips + mask, place.twin)

    plan = Planner()
    waited = set()

    def block_bytes(item):
        which, _, width, _ = items[item]
        return 2 * narrow * rows_of[which] * width

    def twin_event(item, mask):
        return lambda: to_twin(item, mask).wait_recv()

    def onward(item, mask, number):
        bits = bits_of(item)
        size = block_bytes(item)
        for later in range(number, len(bits)):
            start(across(item, mask, bits[later]))
            coming = mask ^ bits[later]
            plan.transfer(
                bits[later], 2 * size / LINK, (item, coming), functools.partial(arrive, item, coming, later)
            )
        start(to_twin(item, mask))
        plan.transfer(-1, size / TWIN_LINK, (item, chips + mask), twin_event(item, mask))

    def arrive(item, mask, number):
        across(item, mask ^ bits_of(item)[number], bits_of(item)[number]).wait_recv()
        onward(item, mask, number + 1)

    def begin_item(item):
        for sign in (1, -1):
            start_if(has_next(sign), along(item, sign, 1))
        line_transfer(item, 1)

    def line_transfer(item, hop):
        cost = 2 * block_bytes(item) / narrow / LINK
        key = (item, 0) if hop == narrow - 1 else (item, -hop)
        plan.transfer(0, cost, key, functools.partial(line_event, item, hop))

    def line_event(item, hop):
        if items[item][0] not in waited:
            waited.add(items[item][0])
            own[items[item][0]].wait()
        for sign in (1, -1):

            @pl.when(has_come(sign, hop))
            def _():
                along(item, sign, hop).wait_recv()

            if hop < narrow - 1:
                start_if(jnp.logical_and(has_come(sign, hop), has_next(sign)), along(item, sign, hop + 1))
        if hop < narrow - 1:
            line_transfer(item, hop + 1)
        else:
            onward(item, 0, 0)

    begun, ahead = [], [Z_EARLY]

    def refill():
        while len(begun) < total and plan.free.get(0, 0.0) < plan.now + ahead[-1]:
            begin_item(len(begun))
            begun.append(True)

    plan.refill = refill
    refill()

    def need(which, columns=None):
        plan.need(
            [
                (index, key)
                for index, (owner, begin, width, _) in enumerate(items)
                if owner == which and (columns is None or (begin < columns[1] and begin + width > columns[0]))
                for key in range(2 * chips)
            ]
        )

    flushed = []

    def flush(ref):
        index = [vars(at)[name] is ref for name in outs].index(True)
        copy = pltpu.make_async_copy(ref, results[index], out_sem.at[index])
        copy.start()
        flushed.append(copy)

    def swap(src, dst, kind, step):
        return pltpu.make_async_remote_copy(
            src_ref=src,
            dst_ref=dst,
            send_sem=swap_send.at[kind, step],
            recv_sem=swap_recv.at[kind, step],
            device_id=place.along(step),
            device_id_type=MESH,
        )

    gains = at.gains
    embedded, mid, last = at.embedded, at.mid, at.last
    normed, hidden, wave = at.normed, at.hidden, at.wave
    away, qkv, heads_out, returned = at.away, at.qkv, at.heads_out, at.returned

    def turn(dest, source):
        dest[...] = source[...].T
        flush(dest)

    need(0)
    width = weights[0].shape[1]
    kind = lax.broadcasted_iota(jnp.int32, (8, LANES), 0)
    spot = lax.broadcasted_iota(jnp.int32, (8, LANES), 1)
    pick = (spot == kind + lead).astype(F32).astype(BF16)
    gains[...] = back_mul(pick, weights[0][:, width - LANES :])
    flush(gains)

    def embed(block):
        cols = pl.ds(block, 256)
        embedded[:, cols] = back_mul(at.patches[...], weights[0][pl.ds(block, 256), : at.patches.shape[1]])

    for block in range(0, D, 256):
        plan.work(0.5, functools.partial(embed, block))
    flush(embedded)

    def norm_rows(source, row, dest):
        step_rows = 32

        def one(step, carry):
            rows = pl.ds(pl.multiple_of(step * step_rows, step_rows), step_rows)
            dest[rows, :] = normalize(
                source[rows, :], gains[row : row + 1, :], gains[row + 3 : row + 4, :]
            ).astype(BF16)
            return carry

        lax.fori_loop(0, tokens // step_rows, one, 0)

    plan.work(2.0, lambda: norm_rows(embedded, 0, normed))
    turn_first = plan.later(2.0, lambda: turn(at.t1, normed))
    piece = 2 * (narrow - 1) * 2 * tokens * head_width / LINK

    def project(part, step):
        owner = lax.rem(me + step, narrow)
        offset = pl.multiple_of(part * D + owner * head_width, LANES)
        value = matmul(normed[...], weights[1][:, pl.ds(offset, head_width)]).astype(BF16)
        if step:
            away[step - 1, part] = value
            start(swap(away.at[step - 1, part], qkv.at[me, part], part, step))
        else:
            qkv[me, part] = value

    def swap_event(part):
        for step in range(1, narrow):
            swap(away.at[step - 1, part], qkv.at[me, part], part, step).wait_recv()

    for part in range(3):
        need(1, (part * D, part * D + D))
        for step in list(range(1, narrow)) + [0]:
            plan.work(0.7, functools.partial(project, part, step))
        plan.transfer(0, piece, (-1, part), functools.partial(swap_event, part))
    flush(at.w1)
    lane = lax.broadcasted_iota(jnp.int32, (1, LANES), 1)
    scale = HD ** (-0.5)
    length = narrow * tokens
    sides = LANES // HD

    def weigh(step):
        who = lax.rem(me + step, narrow)
        log_sums = jnp.zeros((tokens, LANES), F32)
        sums = jnp.ones((tokens, LANES), F32)
        for pair in range(head_width // LANES):
            lanes = pl.ds(pair * LANES, LANES)
            query = qkv[who, 0, :, lanes].astype(F32)
            key = qkv[:, 1, :, lanes].reshape(length, LANES)
            for side in range(sides):
                head = pair * sides + side
                own_query = (query * jnp.where(lane // HD == side, scale, 0.0)).astype(BF16)
                scores = back_mul(own_query, key)
                highest = jnp.max(scores, -1, keepdims=True)
                exponentials = jnp.exp(scores - highest)
                summed = jnp.sum(exponentials, -1, keepdims=True)
                at.weighed[step, head] = exponentials.astype(BF16)
                log_sums = jnp.where(lane == head, highest + jnp.log(summed), log_sums)
                sums = jnp.where(lane == head, summed, sums)
        at.log_sums[who] = log_sums
        at.weigh_sums[step] = sums

    def attend(step):
        who = lax.rem(me + step, narrow)
        for pair in range(head_width // LANES):
            lanes = pl.ds(pair * LANES, LANES)
            value = qkv[:, 2, :, lanes].reshape(length, LANES)
            out = jnp.zeros((tokens, LANES), F32)
            for side in range(sides):
                head = pair * sides + side
                part = matmul(at.weighed[step, head], value) / at.weigh_sums[step, :, head : head + 1]
                out = jnp.where(lane // HD == side, part, out)
            heads_out[who, :, lanes] = out.astype(BF16)
        if step:
            start(swap(heads_out.at[who], returned.at[me], 3, step))
        else:
            returned[me] = heads_out[who]

    steps = list(range(1, narrow)) + [0]
    ahead.append(Z_LATE)
    plan.need([(-1, 0), (-1, 1)])
    for step in steps:
        plan.work(2.7, functools.partial(weigh, step))
    plan.need([(-1, 2)])
    flush(qkv)

    def return_event(step):
        return lambda: swap(heads_out.at[me], returned.at[me], 3, step).wait_recv()

    for step in steps:
        plan.work(0.9, functools.partial(attend, step))
        if step:
            plan.transfer(0, piece / (narrow - 1), (-2, step), return_event(step))
    flush(heads_out)
    flush(at.log_sums)
    need(2)
    plan.need([(-2, step) for step in range(1, narrow)])

    def merge(block):
        cols = pl.ds(block, 256)
        value = embedded[:, cols]
        for source in range(narrow):
            value = value + matmul(returned[source], weights[2][pl.ds(source * head_width, head_width), cols])
        mid[:, cols] = value

    for block in range(0, D, 256):
        plan.work(0.7, functools.partial(merge, block))
    flush(at.w2)
    flush(mid)
    plan.force(turn_first)
    plan.work(2.0, lambda: norm_rows(mid, 1, normed))

    def turn_returned():
        for source in range(narrow):
            at.t2[pl.ds(source * head_width, head_width), :] = returned[source].T
        flush(at.t2)

    plan.later(2.0, turn_returned)
    turn_second = plan.later(2.0, lambda: turn(at.t3, normed))

    ff = weights[3].shape[1]
    tile = wave.shape[1]
    slopes = at.slopes

    def expand(block):
        wave[...] = matmul(normed[...], weights[3][:, pl.ds(block, tile)])

        def bend(step, carry):
            rows = pl.ds(pl.multiple_of(step * 32, 32), 32)
            x = wave[rows, :]
            half = 0.5 * (1.0 + lax.erf(x * (0.5**0.5)))
            hidden[rows, pl.ds(block, tile)] = (x * half).astype(BF16)
            bell = jnp.exp(-0.5 * x * x) * 0.3989422804014327
            slopes[rows, pl.ds(block, tile)] = (half + x * bell).astype(BF16)
            return carry

        lax.fori_loop(0, tokens // 32, bend, 0)

    for block in range(0, ff, tile):
        need(3, (block, block + tile))
        plan.work(2.5, functools.partial(expand, block))
    flush(at.w3)
    flush(slopes)
    flush(hidden)

    def shrink(block):
        cols = pl.ds(block, 256)
        last[:, cols] = mid[:, cols] + matmul(hidden[...], weights[4][:, cols])

    for block in range(0, D, 256):
        need(4, (block, block + 256))
        plan.work(1.0, functools.partial(shrink, block))
    flush(at.w4)
    flush(last)
    plan.force(turn_second)
    plan.work(2.0, lambda: norm_rows(last, 2, normed))
    need(5)

    def unpatch(block):
        cols = pl.ds(block, 256)
        at.gaussians[:, cols] = matmul(normed[...], weights[5][:, cols])

    for block in range(0, weights[5].shape[1], 256):
        plan.work(0.7, functools.partial(unpatch, block))
    flush(at.w5)
    flush(at.gaussians)
    plan.later(2.0, lambda: turn(at.t5, normed))
    plan.finish()
    for copy in started:
        copy.wait_send()
    for condition, copy in guarded:

        @pl.when(condition)
        def _():
            copy.wait_send()

    for copy in flushed:
        copy.wait()


def forward_all(shards, norms, patches, lead, wide, narrow):
    tokens = patches.shape[0]
    widths = [patches.shape[1]] + [shard.shape[1] for shard in shards[1:]]
    heights = [shard.shape[0] * wide * narrow for shard in shards]
    ff = widths[3]
    head_width = D // narrow
    items = forward_plan(widths)
    slots = wide + 2 * (narrow - 1)
    full = [((height, width), BF16) for height, width in zip(heights, widths)]
    shapes = dict(
        w1=full[1],
        w2=full[2],
        w3=full[3],
        w4=full[4],
        w5=full[5],
        gains=((8, D), F32),
        embedded=((tokens, D), F32),
        mid=((tokens, D), F32),
        last=((tokens, D), F32),
        slopes=((tokens, ff), BF16),
        t1=((D, tokens), BF16),
        t2=((D, tokens), BF16),
        t3=((D, tokens), BF16),
        hidden=((tokens, ff), BF16),
        t5=((D, tokens), BF16),
        qkv=((narrow, 3, tokens, head_width), BF16),
        heads_out=((narrow, tokens, head_width), BF16),
        log_sums=((narrow, tokens, LANES), F32),
        gaussians=((tokens, widths[5]), F32),
    )
    ins = tuple(dict(s0=0, s1=0, s2=0, s3=0, s4=0, s5=0, norm_raw=0, patches=0))
    outs = tuple(shapes)
    extras = dict(
        first_weight=pltpu.VMEM((heights[0], widths[0]), BF16),
        c0=pltpu.VMEM((shards[0].shape[0], widths[0]), BF16),
        c1=pltpu.VMEM(shards[1].shape, BF16),
        c2=pltpu.VMEM(shards[2].shape, BF16),
        c3=pltpu.VMEM(shards[3].shape, BF16),
        c4=pltpu.VMEM(shards[4].shape, BF16),
        c5=pltpu.VMEM(shards[5].shape, BF16),
        normed=pltpu.VMEM((tokens, D), BF16),
        wave=pltpu.VMEM((tokens, 512), F32),
        away=pltpu.VMEM((narrow - 1, 3, tokens, head_width), BF16),
        weighed=pltpu.VMEM((narrow, head_width // HD, tokens, narrow * tokens), BF16),
        weigh_sums=pltpu.VMEM((narrow, tokens, LANES), F32),
        returned=pltpu.VMEM((narrow, tokens, head_width), BF16),
        own_sem=pltpu.SemaphoreType.DMA((6,)),
        send_sem=pltpu.SemaphoreType.DMA((len(items), slots)),
        recv_sem=pltpu.SemaphoreType.DMA((len(items), slots)),
        swap_send=pltpu.SemaphoreType.DMA((4, narrow)),
        swap_recv=pltpu.SemaphoreType.DMA((4, narrow)),
        out_sem=pltpu.SemaphoreType.DMA((len(outs),)),
    )
    scratch = outs + tuple(extras)
    anywhere = pl.BlockSpec(memory_space=pl.ANY)
    results = pl.pallas_call(
        functools.partial(forward_kernel, items, wide, narrow, lead, ins, outs, scratch),
        out_shape=[jax.ShapeDtypeStruct(*shapes[name]) for name in outs],
        in_specs=[pl.BlockSpec(memory_space=pltpu.VMEM)] * len(ins),
        out_specs=[anywhere] * len(outs),
        scratch_shapes=[pltpu.VMEM(*shapes[name]) for name in outs] + list(extras.values()),
        compiler_params=pltpu.CompilerParams(
            collective_id=0, has_side_effects=True, vmem_limit_bytes=60 * MIB
        ),
        name="forward",
    )(*shards, norms, patches)
    return Bag(zip(outs, results))


def backward_plan(widths, pairs):
    items = []
    for which, cuts in ((5, 1), (4, 2), (3, 2), (2, 1), (1, pairs), (0, 1)):
        size = widths[which] // cuts
        if which == 1:
            piece = size // 3
            for cut in range(cuts):
                start = cut * size
                items += [(1, start, piece, 0), (1, start + piece, piece, 1)]
                for side, (shift, width) in enumerate(column_halves(piece)):
                    items.append((1, start + 2 * piece + shift, width, side))
            continue
        for cut in range(cuts):
            for side, (start, width) in enumerate(column_halves(size)):
                items.append((which, cut * size + start, width, side))
    return items


def tile_of(width):
    for tile in (512, 384, 256, 128):
        if width % tile == 0:
            return tile
    return width


def backward_kernel(items, wide, narrow, lead, ins, scratch, *refs):
    src = Bag(zip(ins, refs))
    refs = refs[len(ins) :]
    sums, totals, refs = refs[:6], refs[6], list(refs[7:])
    at = Bag(zip(scratch, refs))
    place = Place(wide, narrow)
    chips, me = place.chips, place.n
    total = len(items)
    refs = refs[len(scratch) :]
    held = [refs.pop(0) for _ in items]
    passed = [[refs.pop(0) for _ in place.bits] for _ in items]
    final = [refs.pop(0) for _ in items]
    spare = [refs.pop(0) for _ in range(6)]
    tokens = src.patches.shape[0]
    head_width = D // narrow
    length = narrow * tokens
    reach = narrow * LANES
    send_sem, recv_sem, tile_send, tile_recv = at.send_sem, at.recv_sem, at.tile_send, at.tile_recv
    swap_send, swap_recv, in_sem, ring_sem = at.swap_send, at.swap_recv, at.in_sem, at.ring_sem
    gains, norms, extra = src.gains, at.norms, at.extra
    stash, d_res, d_norm = at.stash, at.d_res, at.d_norm
    mixed, merge_low, expand_low, shrink_low = at.mixed, at.merge_low, at.expand_low, at.shrink_low

    loaded = [name for name in ins if name in scratch]

    def load(ref):
        index = [vars(at)[name] is ref for name in loaded].index(True)
        return pltpu.make_async_copy(vars(src)[loaded[index]], ref, in_sem.at[index])

    def load_stash(ref):
        return pltpu.make_async_copy(ref, stash, in_sem.at[len(loaded)])

    def ring(ref, slots, rows, columns, index, row):
        slot = lax.rem(index, slots.shape[0])
        return pltpu.make_async_copy(
            ref.at[pl.ds(pl.multiple_of(row, rows), rows), :],
            slots.at[slot, pl.ds(0, rows), pl.ds(0, columns)],
            ring_sem.at[0 if slots is at.tall else 1, slot],
        )

    slope_rows = at.tall.shape[1]
    tall, long = at.tall.shape[0], at.long.shape[0]

    def slope_load(index):
        slot = lax.rem(index, tall)
        return pltpu.make_async_copy(
            src.slopes.at[:, pl.ds(pl.multiple_of(index * slope_rows, slope_rows), slope_rows)],
            at.slope_slots.at[slot],
            ring_sem.at[2, slot],
        )

    u_rows, u_cols = 256, src.w5.shape[1]
    load_stash(src.last).start()
    for index in range(tall):
        ring(src.w5, at.tall, u_rows, u_cols, index, index * u_rows).start()
        slope_load(index).start()
    for index in range(long):
        ring(src.w3, at.long, 128, src.w3.shape[1], index, index * 128).start()
    for name in loaded:
        load(vars(at)[name]).start()

    peers = [(lax.rem(place.w + step, wide), place.n) for step in range(1, wide)]
    peers += [place.along(step) for step in range(1, narrow)]
    greet(peers)

    started, guarded = [], []

    def start(copy):
        copy.start()
        started.append(copy)

    lefts = [at.embed_t, at.t1, at.t2, at.t3, at.shrink_t, at.t5]
    rights = [src.patches, mixed, merge_low, expand_low, at.hidden, src.gauss]

    def remote(item, src, dst, slot, peer):
        return pltpu.make_async_remote_copy(
            src_ref=src,
            dst_ref=dst,
            send_sem=send_sem.at[item, slot],
            recv_sem=recv_sem.at[item, slot],
            device_id=peer,
            device_id_type=MESH,
        )

    def bits_of(item):
        return place.bits[::-1] if items[item][3] == 0 else place.bits

    def groups_of(item):
        size = max(1, 512 // (narrow * spare[items[item][0]].shape[2]))
        if items[item][0] == 4:
            size = chips
        masks = list(range(chips))
        if bits_of(item) and bits_of(item)[0] > 1:
            masks = masks[chips // 2 :] + masks[: chips // 2]
        return [sorted(masks[at_mask : at_mask + size]) for at_mask in range(0, chips, size)]

    def product(item, masks, core, into, plus):
        which, begin, width, _ = items[item]
        left, right = lefts[which], rights[which]
        rows = into.shape[-2]
        span = narrow * rows
        tile = tile_of(width)
        if which == 4:
            size = into.shape[-1]
            for mask in masks:
                column = ((flip(place.chip, mask) * 2 + core) * narrow) * size
                rhs = right[:, pl.ds(pl.multiple_of(column, narrow * size), narrow * size)]
                value = jnp.dot(left[begin : begin + width, :], rhs, preferred_element_type=F32)
                for node in range(narrow):
                    piece = value[:, node * size : (node + 1) * size]
                    if plus:
                        piece = piece + into[mask, node].astype(F32)
                    into[mask, node] = piece.astype(BF16)
            return
        firsts = [((flip(place.chip, mask) * 2 + core) * narrow) * rows for mask in masks]
        with_extra = which == 0 and begin + width == right.shape[1]
        assert not with_extra or tile == width
        part, begin = (begin // reach, begin % reach) if which == 1 else (None, begin)

        def one(step, carry):
            offset = pl.multiple_of(begin + step * tile, LANES)
            local = pl.multiple_of(step * tile, LANES)
            if part is None:
                rhs = right[:, pl.ds(offset, tile)]
            else:
                rhs = right[part // 3, part % 3, :, pl.ds(offset, tile)]
            spots = [pl.ds(pl.multiple_of(first, span), span) for first in firsts]
            lhs = jnp.concatenate([left[spot, :] for spot in spots], 0)
            value = jnp.dot(lhs, rhs, preferred_element_type=F32)
            for index, mask in enumerate(masks):
                piece = value[index * span : (index + 1) * span]
                if with_extra:
                    blank = jnp.zeros((span, tile - LANES), F32)
                    piece = piece + jnp.concatenate([blank, extra[spots[index], :]], 1)
                piece = piece.reshape(narrow, rows, tile)
                if plus:
                    piece = piece + into[mask, :, :, pl.ds(local, tile)].astype(F32)
                into[mask, :, :, pl.ds(local, tile)] = piece.astype(BF16)
            return carry

        lax.fori_loop(0, width // tile, one, 0)

    last_sent = {}
    plan = Planner()

    def to_twin(item, masks):
        which, _, width, _ = items[item]
        some = pl.ds(masks[0], len(masks))
        own = spare[which].at[some] if which == 4 else spare[which].at[some, :, :, pl.ds(0, width)]
        return remote(item, own, held[item].at[some], masks[0], place.twin)

    def across(item, mask, bit, number, slot):
        return remote(
            item, held[item].at[mask], passed[item][number].at[slot], chips + mask, place.across(bit)
        )

    def along(item, sign, hop):
        count = narrow - hop
        first = hop if sign > 0 else 0
        node = hop if sign > 0 else narrow - 1 - hop
        return remote(
            item,
            held[item].at[0, pl.ds(first, count)],
            final[item].at[pl.ds(first + (1 if sign > 0 else 0), count)],
            2 * chips + (0 if sign > 0 else 1),
            (place.w, node),
        )

    def send_along(item, sign, hop):
        sender = me == (hop - 1 if sign > 0 else narrow - hop)

        @pl.when(sender)
        def _():
            along(item, sign, hop).start()

        guarded.append((sender, along(item, sign, hop)))

    def straight(item, step):
        target = place.along(step)
        return remote(
            item,
            held[item].at[0, target[1]],
            final[item].at[narrow - step - 1],
            2 * chips + narrow - step - 1,
            target,
        )

    def is_straight(item):
        return items[item][0] == 0

    def straight_event(item):
        acc = acc_of(item)
        acc[...] = held[item][0, me].astype(F32)
        for step in range(1, narrow):
            straight(item, step).wait_recv()
        for slot in range(narrow - 1):
            acc[...] += final[item][slot].astype(F32)
        finish(item, acc)

    def line_event(item, hop):
        for sign in (1, -1):
            count = narrow - hop - 1
            first = hop + 1 if sign > 0 else 0

            @pl.when(me == (hop if sign > 0 else narrow - 1 - hop))
            def _():
                along(item, sign, hop).wait_recv()

                def one(step, carry):
                    spot = first + step
                    value = held[item][0, spot].astype(F32)
                    value = value + final[item][spot + (1 if sign > 0 else 0)].astype(F32)
                    held[item][0, spot] = value.astype(BF16)
                    return carry

                if count:
                    lax.fori_loop(0, count, one, 0)

            if count:
                send_along(item, sign, hop + 1)
        line_transfer(item, hop + 1)

    def line_transfer(item, hop):
        cost = (narrow - hop) * 2 * block_bytes(item) / narrow / LINK
        if hop == narrow:
            return line_end(item)
        plan.transfer(0 if hop == 1 else 100 + hop, cost, (item, -hop, 0), functools.partial(line_event, item, hop))

    def leaves(item, mask):
        bits = bits_of(item)
        return min([number for number, bit in enumerate(bits) if mask & bit], default=len(bits))

    def slot_of(item, mask, number):
        bits = bits_of(item)
        kept = [m for m in range(chips) if not any(m & bit for bit in bits[: number + 1])]
        return kept.index(mask)

    def add_into(dest, dest_at, src, src_at):
        dest[dest_at] = (dest[dest_at].astype(F32) + src[src_at].astype(F32)).astype(BF16)

    def block_bytes(item):
        _, nodes, rows, width = held[item].shape
        return 2 * nodes * rows * width

    def push(which, pair=None):
        for item, (owner, begin, _, _) in enumerate(items):
            if owner != which or (pair is not None and begin // (3 * reach) != pair):
                continue
            for masks in groups_of(item):
                cost = len(masks) * block_bytes(item) / 1e6
                plan.work(cost, functools.partial(push_some, item, masks))

    def push_some(item, masks):
        which = items[item][0]
        for key in [key for key in last_sent if key[0] == which and set(key[1]) & set(masks)]:
            last_sent.pop(key).wait_send()
        product(item, masks, 1 - place.core, spare[which], False)
        copy = to_twin(item, masks)
        copy.start()
        last_sent[which, tuple(masks)] = copy
        cost = len(masks) * block_bytes(item) / TWIN_LINK
        plan.transfer(-1, cost, (item, 0, masks[0]), functools.partial(own_event, item, masks))

    def own_event(item, masks):
        to_twin(item, masks).wait_recv()
        product(item, masks, place.core, held[item], True)
        plan.now += len(masks) * block_bytes(item) / 1e6
        plan.done.update((item, 0, mask) for mask in masks)
        for mask in masks:
            onward(item, mask, 0)

    def onward(item, mask, number):
        bits = bits_of(item)
        if number == len(bits):
            lined.append(item)
            refill()
        elif leaves(item, mask) == number:
            kept = mask ^ bits[number]
            start(across(item, mask, bits[number], number, slot_of(item, kept, number)))
            plan.transfer(
                bits[number],
                2 * block_bytes(item) / LINK,
                (item, 1 + number, kept),
                functools.partial(sum_event, item, kept, number),
            )

    lined = []

    def refill():
        while lined and plan.free.get(0, 0.0) < plan.now + Z_AHEAD:
            item = lined.pop(0)
            if is_straight(item):
                for step in range(1, narrow):
                    start(straight(item, step))
                cost = 2 * (narrow // 2) ** 2 * block_bytes(item) / narrow / LINK
                plan.transfer(0, cost, (item, -1, 0), functools.partial(straight_event, item))
                continue
            for sign in (1, -1):
                send_along(item, sign, 1)
            line_transfer(item, 1)

    plan.refill = refill

    def sum_event(item, mask, number):
        plan.need([(item, before, mask) for before in range(number + 1)])
        bit = bits_of(item)[number]
        slot = slot_of(item, mask, number)
        across(item, mask ^ bit, bit, number, slot).wait_recv()
        add_into(held[item], mask, passed[item][number], slot)
        plan.now += block_bytes(item) / 8e5
        onward(item, mask, number + 1)

    squares = []

    def acc_of(item):
        return at.acc.at[pl.ds(0, held[item].shape[2]), pl.ds(0, held[item].shape[3])]

    def line_end(item):
        acc = acc_of(item)
        acc[...] = held[item][0, me].astype(F32)

        @pl.when(me >= 1)
        def _():
            acc[...] += final[item][me + 1].astype(F32)

        @pl.when(me < narrow - 1)
        def _():
            acc[...] += final[item][me].astype(F32)

        finish(item, acc)

    def finish(item, acc):
        which, begin, width, _ = items[item]
        value = acc[...]
        if which == 1:
            for shift in range(0, width, LANES):
                part, spot = (begin + shift) // reach, (begin + shift) % reach
                column = part % 3 * D + spot // LANES * head_width + part // 3 * LANES
                sums[which][:, pl.ds(column, LANES)] = value[:, shift : shift + LANES]
        elif which == 4:
            sums[which][pl.ds(begin, width), :] = value
        else:
            sums[which][:, pl.ds(begin, width)] = value
        squares.append(jnp.sum(value * value))

    norms[...] = jnp.zeros_like(norms)

    def norm_back(row, low, add):
        step_rows = 32

        def one(step, carry):
            rows = pl.ds(pl.multiple_of(step * step_rows, step_rows), step_rows)
            values = stash[rows, :]
            upper = d_norm[rows, :]
            centred = values - jnp.mean(values, -1, keepdims=True)
            rate = lax.rsqrt(jnp.mean(centred * centred, -1, keepdims=True) + 1e-05)
            unit = centred * rate
            norms[row : row + 1, :] += jnp.sum(upper * unit, 0, keepdims=True)
            norms[row + 3 : row + 4, :] += jnp.sum(upper, 0, keepdims=True)
            scaled = upper * gains[row : row + 1, :]
            inner = scaled - jnp.mean(scaled, -1, keepdims=True)
            inner = rate * (inner - unit * jnp.mean(scaled * unit, -1, keepdims=True))
            if add:
                inner = inner + d_res[rows, :]
            d_res[rows, :] = inner
            low[rows, :] = inner.astype(BF16)
            return carry

        lax.fori_loop(0, tokens // step_rows, one, 0)

    def loop_work(cost, count, pieces, body):
        for piece in range(pieces):
            low, high = count * piece // pieces, count * (piece + 1) // pieces
            plan.work(cost / pieces, functools.partial(lax.fori_loop, low, high, body, 0))

    load(at.t5).wait()
    push(5)
    load_stash(src.last).wait()
    count = D // u_rows
    tall_rows = slope_rows

    def through_unpatch(index, carry):
        ring(src.w5, at.tall, u_rows, u_cols, index, index * u_rows).wait()
        slot = at.tall.at[lax.rem(index, tall)]
        offset = pl.multiple_of(index * u_rows, u_rows)
        d_norm[:, pl.ds(offset, u_rows)] = back_mul(src.gauss[...], slot[0:u_rows, 0:u_cols])

        @pl.when(index + tall < count)
        def _():
            ring(src.w5, at.tall, u_rows, u_cols, index + tall, (index + tall) * u_rows).start()

        return carry

    loop_work(2.5, count, 1, through_unpatch)
    for index in range(tall):
        ring(src.w4, at.tall, tall_rows, D, index, index * tall_rows).start()
    plan.work(2.5, lambda: norm_back(2, shrink_low, False))
    load_stash(src.mid).start()
    load(at.hidden).wait()

    def turn_shrink():
        at.shrink_t[...] = shrink_low[...].T

    plan.work(2.0, turn_shrink)
    push(4)
    ff = src.w3.shape[1]
    slabs = ff // tall_rows

    def through_shrink(index, carry):
        ring(src.w4, at.tall, tall_rows, D, index, index * tall_rows).wait()
        slope_load(index).wait()
        slot = lax.rem(index, tall)
        value = back_mul(shrink_low[...], at.tall[slot])
        value = value * at.slope_slots[slot].astype(F32)
        expand_low[:, pl.ds(pl.multiple_of(index * tall_rows, tall_rows), tall_rows)] = value.astype(BF16)

        @pl.when(index + tall < slabs)
        def _():
            ring(src.w4, at.tall, tall_rows, D, index + tall, (index + tall) * tall_rows).start()
            slope_load(index + tall).start()

        return carry

    loop_work(6.0, slabs, 2, through_shrink)
    owners = [lax.rem(me + step, narrow) for step in list(range(1, narrow)) + [0]]
    for index in range(min(tall, narrow)):
        ring(src.w2, at.tall, head_width, D, index, owners[index] * head_width).start()
    load(at.t3).wait()

    def through_expand(index, carry):
        ring(src.w3, at.long, 128, ff, index, index * 128).wait()
        offset = pl.multiple_of(index * 128, 128)
        d_norm[:, pl.ds(offset, 128)] = back_mul(expand_low[...], at.long[lax.rem(index, long)])

        @pl.when(index + long < D // 128)
        def _():
            ring(src.w3, at.long, 128, ff, index + long, (index + long) * 128).start()

        return carry

    loop_work(5.0, D // 128, 2, through_expand)
    for index in range(long):
        ring(src.w1, at.long, 128, 3 * D, index, index * 128).start()
    load_stash(src.mid).wait()
    plan.work(2.0, lambda: norm_back(1, merge_low, True))
    load_stash(src.embedded).start()

    def swap(src, dst, kind, step):
        return pltpu.make_async_remote_copy(
            src_ref=src,
            dst_ref=dst,
            send_sem=swap_send.at[kind, step],
            recv_sem=swap_recv.at[kind, step],
            device_id=place.along(step),
            device_id_type=MESH,
        )

    d_heads, away = at.d_heads, at.away
    piece = 2 * (narrow - 1) * 2 * tokens * head_width / LINK

    def head_event():
        for step in range(1, narrow):
            swap(away.at[step - 1], d_heads.at[me], 0, step).wait_recv()

    def through_merge(index, owner):
        ring(src.w2, at.tall, head_width, D, index, owner * head_width).wait()
        value = back_mul(merge_low[...], at.tall[index % tall, 0:head_width, :]).astype(BF16)
        if index < narrow - 1:
            away[index] = value
            start(swap(away.at[index], d_heads.at[me], 0, index + 1))
        else:
            d_heads[me] = value
        if index + tall < narrow:
            ring(src.w2, at.tall, head_width, D, index + tall, owners[index + tall] * head_width).start()

    for index, owner in enumerate(owners):
        plan.work(0.7, functools.partial(through_merge, index, owner))
    plan.transfer(0, piece, (-1, 0, 0), head_event)
    load(at.t2).wait()
    push(3)
    push(2)
    load(at.qkv).wait()
    load(at.heads_out).wait()
    load(at.log_sums).wait()
    plan.need([(-1, 0, 0)])

    qkv, heads_out, log_sums, parts = at.qkv, at.heads_out, at.log_sums, at.parts
    key_t, key_acc, value_acc, query_acc = at.key_t, at.key_acc, at.value_acc, at.query_acc
    lane = lax.broadcasted_iota(jnp.int32, (1, LANES), 1)
    sides = LANES // HD
    scale = HD ** (-0.5)
    choose = lax.broadcasted_iota(jnp.int32, (8, LANES), 1) // HD
    choose = (choose == lax.broadcasted_iota(jnp.int32, (8, LANES), 0)).astype(F32)

    def part_swap(pair, step):
        lanes = pl.ds(pair * LANES, LANES)
        who = lax.rem(me + step, narrow)
        return swap(
            parts.at[who, :, :, lanes],
            mixed.at[pair, :, :, pl.ds(pl.multiple_of(me * LANES, LANES), LANES)],
            1 + pair,
            step,
        )

    pushed_pairs = []
    load(at.t1).wait()

    def part_event(pair):
        for step in range(1, narrow):
            part_swap(pair, step).wait_recv()

    for pair in range(head_width // LANES):
        lanes = pl.ds(pair * LANES, LANES)
        key_t[...] = qkv[:, 1, :, lanes].reshape(length, LANES).T
        key_acc[...] = jnp.zeros_like(key_acc)
        value_acc[...] = jnp.zeros_like(value_acc)
        def one_block(step, lanes=lanes, pair=pair):
            who = lax.rem(me + step, narrow)
            query = qkv[who, 0, :, lanes].astype(F32)
            upper = d_heads[who, :, lanes].astype(F32)
            kept = heads_out[who, :, lanes].astype(F32)
            delta = lax.dot_general(
                choose,
                upper * kept,
                (((1,), (1,)), ((), ())),
                precision=HIGHEST,
                preferred_element_type=F32,
            )
            log_rows = log_sums[who].T[pair * sides : (pair + 1) * sides, :]
            masks = [jnp.where(lane // HD == side, 1.0, 0.0) for side in range(sides)]
            own_query = jnp.concatenate([query * (scale * mask) for mask in masks], 0).astype(BF16)
            own_upper = jnp.concatenate([upper * mask for mask in masks], 0).astype(BF16)
            log_row = jnp.concatenate([log_rows[side : side + 1, :] for side in range(sides)], 1)
            delta_row = jnp.concatenate([delta[side : side + 1, :] for side in range(sides)], 1)
            query_acc[...] = jnp.zeros_like(query_acc)

            def block(source, carry):
                rows = pl.ds(pl.multiple_of(source * tokens, tokens), tokens)
                key, value = qkv[source, 1, :, lanes], qkv[source, 2, :, lanes]
                probs = jnp.exp(back_mul(key, own_query) - log_row)
                d_probs = back_mul(value, own_upper)
                d_scores = (probs * (d_probs - delta_row)).astype(BF16)
                value_acc[rows, :] += matmul(probs.astype(BF16), own_upper)
                key_acc[rows, :] += matmul(d_scores, own_query)
                turned = matmul(key_t[:, rows], d_scores)
                for side in range(sides):
                    spot = slice(side * HD, (side + 1) * HD)
                    query_acc[spot, :] += turned[spot, side * tokens : (side + 1) * tokens]
                return carry

            lax.fori_loop(0, narrow, block, 0)
            parts[who, 0, :, lanes] = (query_acc[...].T * scale).astype(BF16)
        for step in range(narrow):
            plan.work(3.0, functools.partial(one_block, step))
            for earlier in range(pair):
                if earlier not in pushed_pairs and (-2, 0, earlier) in plan.done:
                    pushed_pairs.append(earlier)
                    push(1, earlier)
        for source in range(narrow):
            rows = pl.ds(source * tokens, tokens)
            parts[source, 1, :, lanes] = key_acc[rows, :].astype(BF16)
            parts[source, 2, :, lanes] = value_acc[rows, :].astype(BF16)
        for step in range(1, narrow):
            start(part_swap(pair, step))
        plan.now += 1.0
        plan.transfer(0, 1.5 * piece, (-2, 0, pair), functools.partial(part_event, pair))
        mixed[pair, :, :, pl.ds(pl.multiple_of(me * LANES, LANES), LANES)] = parts[me, :, :, lanes]
    for pair in range(head_width // LANES):
        if pair not in pushed_pairs:
            plan.need([(-2, 0, pair)])
            push(1, pair)

    def through_mixer(index, carry):
        ring(src.w1, at.long, 128, 3 * D, index, index * 128).wait()
        slot = lax.rem(index, long)
        value = jnp.zeros((tokens, 128), F32)
        for pair in range(head_width // LANES):
            for part in range(3):
                columns = [part * D + owner * head_width + pair * LANES for owner in range(narrow)]
                weight = [at.long[slot, :, column : column + LANES] for column in columns]
                value = value + back_mul(mixed[pair, part], jnp.concatenate(weight, 1))
        d_norm[:, pl.ds(pl.multiple_of(index * 128, 128), 128)] = value

        @pl.when(index + long < D // 128)
        def _():
            ring(src.w1, at.long, 128, 3 * D, index + long, (index + long) * 128).start()

        return carry

    plan.work(4.0, lambda: lax.fori_loop(0, D // 128, through_mixer, 0))
    load_stash(src.embedded).wait()
    plan.work(3.0, lambda: norm_back(0, at.embed_low, True))
    at.embed_t[...] = at.embed_low[...].T
    turned = jnp.concatenate([norms[...], jnp.zeros((LANES - 8, D), F32)], 0).T
    at.extra[...] = pltpu.roll(turned, lead, 1)
    push(0)
    plan.finish()

    rows = lax.broadcasted_iota(jnp.int32, (8, LANES), 0)
    wide_tiles, narrow_tiles = at.wide_tiles, at.narrow_tiles
    wide_tiles[place.w] = jnp.where(rows == 0, src.term[...], sum(squares))

    def tile_copy(buffer, index, slot, peer):
        return pltpu.make_async_remote_copy(
            src_ref=buffer.at[index],
            dst_ref=buffer.at[index],
            send_sem=tile_send.at[slot],
            recv_sem=tile_recv.at[slot],
            device_id=peer,
            device_id_type=MESH,
        )

    for step in range(1, wide):
        start(tile_copy(wide_tiles, place.w, step - 1, (lax.rem(place.w + step, wide), place.n)))
    for step in range(1, wide):
        tile_copy(wide_tiles, place.w, step - 1, (lax.rem(place.w + step, wide), place.n)).wait_recv()
    whole = wide_tiles[0]
    for index in range(1, wide):
        whole = whole + wide_tiles[index]
    narrow_tiles[place.n] = whole
    for step in range(1, narrow):
        start(tile_copy(narrow_tiles, place.n, wide + step - 1, place.along(step)))
    for step in range(1, narrow):
        tile_copy(narrow_tiles, place.n, wide + step - 1, place.along(step)).wait_recv()
    whole = narrow_tiles[0]
    for index in range(1, narrow):
        whole = whole + narrow_tiles[index]
    totals[...] = whole
    for copy in list(last_sent.values()) + started:
        copy.wait_send()
    for condition, copy in guarded:

        @pl.when(condition)
        def _():
            copy.wait_send()


def backward_all(kept, patches, gauss, term, lead, wide, narrow):
    tokens = patches.shape[0]
    chips = wide // 2
    weights = [kept.w1, kept.w2, kept.w3, kept.w4, kept.w5]
    heights = [D] + [weight.shape[0] for weight in weights]
    widths = [patches.shape[1]] + [weight.shape[1] for weight in weights]
    rows = [height // (wide * narrow) for height in heights]
    head_width = D // narrow
    length = narrow * tokens
    items = backward_plan(widths, head_width // LANES)
    slots = 2 * chips + narrow + 1
    streamed = dict(w1=kept.w1, w2=kept.w2, w3=kept.w3, w4=kept.w4, w5=kept.w5)
    streamed.update(last=kept.last, mid=kept.mid, embedded=kept.embedded, slopes=kept.slopes)
    loaded = dict(t5=kept.t5, hidden=kept.hidden, t3=kept.t3, t2=kept.t2, t1=kept.t1)
    loaded.update(qkv=kept.qkv, heads_out=kept.heads_out, log_sums=kept.log_sums)
    whole = dict(gains=kept.gains, patches=patches, gauss=gauss, term=term)
    operands = {**streamed, **loaded, **whole}
    shapes = [jax.ShapeDtypeStruct((rows[which], widths[which]), F32) for which in range(6)]
    shapes[4] = jax.ShapeDtypeStruct((D, rows[4]), F32)
    shapes.append(jax.ShapeDtypeStruct((8, LANES), F32))
    scratch = {name: pltpu.VMEM(value.shape, value.dtype) for name, value in loaded.items()}
    scratch.update(
        acc=pltpu.VMEM((max(rows[3], D // 4), max(width for _, _, width, _ in items)), F32),
        embed_t=pltpu.VMEM((D, tokens), BF16),
        embed_low=pltpu.VMEM((tokens, D), BF16),
        shrink_t=pltpu.VMEM((D, tokens), BF16),
        stash=pltpu.VMEM((tokens, D), F32),
        d_res=pltpu.VMEM((tokens, D), F32),
        d_norm=pltpu.VMEM((tokens, D), F32),
        norms=pltpu.VMEM((8, D), F32),
        extra=pltpu.VMEM((D, LANES), F32),
        shrink_low=pltpu.VMEM((tokens, D), BF16),
        expand_low=pltpu.VMEM((tokens, widths[3]), BF16),
        merge_low=pltpu.VMEM((tokens, D), BF16),
        mixed=pltpu.VMEM((head_width // LANES, 3, tokens, narrow * LANES), BF16),
        tall=pltpu.VMEM((4, 256, D), BF16),
        long=pltpu.VMEM((3, 128, widths[3]), BF16),
        slope_slots=pltpu.VMEM((4, tokens, 256), BF16),
        d_heads=pltpu.VMEM((narrow, tokens, head_width), BF16),
        away=pltpu.VMEM((narrow - 1, tokens, head_width), BF16),
        parts=pltpu.VMEM((narrow, 3, tokens, head_width), BF16),
        key_t=pltpu.VMEM((LANES, length), BF16),
        key_acc=pltpu.VMEM((length, LANES), F32),
        value_acc=pltpu.VMEM((length, LANES), F32),
        query_acc=pltpu.VMEM((LANES, tokens), F32),
        wide_tiles=pltpu.VMEM((wide, 8, LANES), F32),
        narrow_tiles=pltpu.VMEM((narrow, 8, LANES), F32),
        send_sem=pltpu.SemaphoreType.DMA((len(items), slots)),
        recv_sem=pltpu.SemaphoreType.DMA((len(items), slots)),
        tile_send=pltpu.SemaphoreType.DMA((wide + narrow,)),
        tile_recv=pltpu.SemaphoreType.DMA((wide + narrow,)),
        swap_send=pltpu.SemaphoreType.DMA((1 + head_width // LANES, narrow)),
        swap_recv=pltpu.SemaphoreType.DMA((1 + head_width // LANES, narrow)),
        in_sem=pltpu.SemaphoreType.DMA((9,)),
        ring_sem=pltpu.SemaphoreType.DMA((3, 4)),
    )
    blocks = [(width, rows[which]) if which == 4 else (rows[which], width) for which, _, width, _ in items]
    lists = [pltpu.VMEM((chips, narrow) + block, BF16) for block in blocks]
    for block in blocks:
        for bit in chip_bits(chips):
            lists.append(pltpu.VMEM((chips // (2 * bit), narrow) + block, BF16))
    lists += [pltpu.VMEM((narrow + 1,) + block, BF16) for block in blocks]
    for which in range(6):
        widest = max(block for item, block in zip(items, blocks) if item[0] == which)
        lists.append(pltpu.VMEM((chips, narrow) + widest, BF16))
    vmem = pl.BlockSpec(memory_space=pltpu.VMEM)
    hbm = pl.BlockSpec(memory_space=pl.ANY)
    return pl.pallas_call(
        functools.partial(backward_kernel, items, wide, narrow, lead, tuple(operands), tuple(scratch)),
        out_shape=shapes,
        in_specs=[vmem if name in whole else hbm for name in operands],
        out_specs=[vmem] * len(shapes),
        scratch_shapes=list(scratch.values()) + lists,
        compiler_params=pltpu.CompilerParams(
            collective_id=1, has_side_effects=True, vmem_limit_bytes=63 * MIB
        ),
        name="backward",
    )(*operands.values())


def render_kernel(
    gauss_ref, weight_ref, target_ref, mask_ref, pair_ref, view_ref, total_ref, grad_ref, term_ref, feat, dfeat
):
    quads = gauss_ref.shape[0] // NVIEW
    span = weight_ref.shape[1]
    pairs = pair_ref.shape[1]
    scale = 1.0 / total_ref[0].astype(F32)

    def channel(index):
        return gauss_ref[:, index * PP : (index + 1) * PP]

    def shared():
        opacity = jax.nn.sigmoid(channel(3))
        extent = jax.nn.sigmoid(channel(5) + channel(6) + channel(7))
        lead = channel(8)
        denom = 1.0 + lead * lead + channel(9) * channel(9) + channel(10) * channel(10) + channel(11) * channel(11)
        facing = lead * lead / denom
        raw = channel(4)
        depth = jnp.maximum(raw, 0.0) + jnp.log1p(jnp.exp(-jnp.abs(raw)))
        return opacity, extent, lead, denom, facing, raw, depth

    opacity, extent, lead, denom, facing, raw, depth = shared()
    footprint = opacity * extent * facing
    channels = [jax.nn.sigmoid(channel(index)) * footprint for index in range(3)]
    channels += [footprint, depth * footprint]
    for index, value in enumerate(channels):
        for view in range(NVIEW):
            feat[index * quads : (index + 1) * quads, view * PP : (view + 1) * PP] = value[
                view * quads : (view + 1) * quads
            ]
    rendered = jnp.dot(feat[...], weight_ref[...], precision=HIGHEST, preferred_element_type=F32)
    parts = [rendered[index * quads : (index + 1) * quads] for index in range(5)]
    lane = lax.broadcasted_iota(jnp.int32, (quads, span), 1)
    live = jnp.where(lane < view_ref[0] * PP, mask_ref[...], 0).astype(F32)
    term = jnp.zeros((quads, span), F32)
    slopes = []
    for index in range(3):
        error = parts[index] - target_ref[index * quads : (index + 1) * quads, :].astype(F32)
        term = term + live * error * error
        slopes.append(2.0 * scale * live * error)
    below = 1.0 + parts[3]
    depth_out = parts[4] / below

    first, second = pair_ref[0:1, :], pair_ref[1:2, :]
    least = jnp.minimum(first, second)
    down = (jnp.abs(first - second) == P_SIZE).astype(jnp.int32)
    place = quads * PP
    slot, local = least // place, least % place
    high = down * quads + local // PP
    low = slot * PP + local % PP
    high_hot = (lax.broadcasted_iota(jnp.int32, (2 * quads, pairs), 0) == high).astype(F32).astype(BF16)
    low_hot = (lax.broadcasted_iota(jnp.int32, (span, pairs), 0) == low).astype(F32).astype(BF16)
    counts = back_mul(high_hot, low_hot)
    slope = jnp.zeros((quads, span), F32)
    for which, shift in enumerate((1, P_SIZE)):
        count = counts[which * quads : (which + 1) * quads]
        weight = DEPTH_WEIGHT * count * live * pltpu.roll(live, span - shift, 1)
        gap = depth_out - pltpu.roll(depth_out, span - shift, 1)
        term = term + weight * gap * gap
        pull = 2.0 * scale * weight * gap
        slope = slope + pull - pltpu.roll(pull, shift, 1)
    term_ref[...] = jnp.full(term_ref.shape, jnp.sum(term), F32)
    over = slope / below
    slopes += [-over * depth_out, over]
    stacked = jnp.concatenate(slopes, 0)
    dfeat[...] = lax.dot_general(
        stacked, weight_ref[...], (((1,), (1,)), ((), ())), precision=HIGHEST, preferred_element_type=F32
    )

    def feature_grad(index):
        return jnp.concatenate(
            [
                dfeat[index * quads : (index + 1) * quads, view * PP : (view + 1) * PP]
                for view in range(NVIEW)
            ],
            0,
        )

    def put(index, value):
        grad_ref[:, index * PP : (index + 1) * PP] = value.astype(BF16)

    d_foot = feature_grad(3)
    for index in range(3):
        tint = jax.nn.sigmoid(channel(index))
        upper = feature_grad(index)
        d_foot = d_foot + upper * tint
        put(index, upper * footprint * tint * (1.0 - tint))
    d_last = feature_grad(4)
    d_foot = d_foot + d_last * depth
    put(3, d_foot * extent * facing * opacity * (1.0 - opacity))
    put(4, d_last * footprint * jax.nn.sigmoid(raw))
    d_extent = d_foot * opacity * facing * extent * (1.0 - extent)
    for index in (5, 6, 7):
        put(index, d_extent)
    d_facing = d_foot * opacity * extent
    put(8, d_facing * 2.0 * lead / denom * (1.0 - facing))
    for index in (9, 10, 11):
        put(index, -2.0 * d_facing * facing / denom * channel(index))


def render(gaussians, weights, targets, mask, pairs, view_count, pair_total):
    rows = gaussians.shape[0]
    quads = rows // NVIEW
    slots, views = weights.shape[:2]
    spread = weights.transpose(1, 2, 0, 3).reshape(views * PP, slots * PP)
    wanted = targets.reshape(slots, 3, quads, PP).transpose(1, 2, 0, 3).reshape(3 * quads, slots * PP)
    valid = mask.reshape(slots, quads, PP).transpose(1, 0, 2).reshape(quads, slots * PP)
    vmem = pl.BlockSpec(memory_space=pltpu.VMEM)
    smem = pl.BlockSpec(memory_space=pltpu.SMEM)
    return pl.pallas_call(
        render_kernel,
        out_shape=[
            jax.ShapeDtypeStruct(gaussians.shape, BF16),
            jax.ShapeDtypeStruct((8, LANES), F32),
        ],
        in_specs=[vmem] * 5 + [smem] * 2,
        out_specs=[vmem] * 2,
        scratch_shapes=[pltpu.VMEM((5 * quads, views * PP), F32)] * 2,
        compiler_params=pltpu.CompilerParams(vmem_limit_bytes=48 * MIB),
        name="render",
    )(gaussians, spread, wanted, valid, pairs, view_count, pair_total)


def forward_plain(shards, patches, features, kinds):
    weights = [lax.all_gather(shard, BOTH, axis=0, tiled=True) for shard in shards]
    groups = lax.axis_size(NARROW)
    rows = patches.shape[0]
    gains = weights[0][:, features : features + kinds].T.astype(F32)
    embedded = back_mul(patches[:, :features], weights[0][:, :features])
    normed_one = layer_norm(embedded, gains[0], gains[3]).astype(BF16)
    mixed = matmul(normed_one, weights[1]).astype(BF16).reshape(rows, 3, groups, -1)
    mixed = mixed.transpose(2, 1, 0, 3)
    qkv = lax.all_to_all(mixed, NARROW, split_axis=0, concat_axis=0, tiled=True)
    width = qkv.shape[-1]
    length = groups * rows
    heads = width // HD
    parts = [qkv[:, part].reshape(length, heads, HD) for part in range(3)]
    attended, logsum = attention_forward(*parts)
    log_sums = logsum.transpose(0, 2, 1).reshape(groups, rows, heads)
    returned = lax.all_to_all(
        attended.reshape(groups, rows, width), NARROW, split_axis=0, concat_axis=0, tiled=True
    )
    returned = returned.transpose(1, 0, 2).reshape(rows, D)
    mid = embedded + matmul(returned, weights[2])
    normed_two = layer_norm(mid, gains[1], gains[4]).astype(BF16)
    expanded = matmul(normed_two, weights[3])
    half = 0.5 * (1.0 + lax.erf(expanded * (0.5**0.5)))
    activated = (expanded * half).astype(BF16)
    bell = jnp.exp(-0.5 * expanded * expanded) * 0.3989422804014327
    slopes = (half + expanded * bell).astype(BF16)
    last = mid + matmul(activated, weights[4])
    normed_three = layer_norm(last, gains[2], gains[5]).astype(BF16)
    return Bag(
        dict(
        w1=weights[1],
        w2=weights[2],
        w3=weights[3],
        w4=weights[4],
        w5=weights[5],
        gains=gains,
        embedded=embedded,
        mid=mid,
        last=last,
        slopes=slopes,
        t1=normed_one.T,
        t2=returned.T,
        t3=normed_two.T,
        hidden=activated,
        t5=normed_three.T,
        qkv=qkv,
        heads_out=attended,
        log_sums=log_sums,
        gaussians=matmul(normed_three, weights[5]),
    ).items())


def backward_plain(kept, patches, gauss_low, term, features, kinds):
    gains = kept.gains
    weights = [None, kept.w1, kept.w2, kept.w3, kept.w4, kept.w5]
    norm_back_one = jax.vjp(layer_norm, kept.embedded, gains[0], gains[3])[1]
    norm_back_two = jax.vjp(layer_norm, kept.mid, gains[1], gains[4])[1]
    norm_back_three = jax.vjp(layer_norm, kept.last, gains[2], gains[5])[1]
    qkv = kept.qkv
    groups, _, rows, width = qkv.shape
    length = groups * rows
    heads = width // HD
    queries, keys, values = (qkv[:, part].reshape(length, heads, HD) for part in range(3))
    blocked = min(512, length)
    logsum = kept.log_sums[:, :, :heads].reshape(length // blocked, blocked, heads)
    residual_grad, gain_three, shift_three = norm_back_three(back_mul(gauss_low, weights[5]))
    shrink_low = residual_grad.astype(BF16)
    expand_low = (back_mul(shrink_low, weights[4]) * kept.slopes.astype(F32)).astype(BF16)
    through_two, gain_two, shift_two = norm_back_two(back_mul(expand_low, weights[3]))
    residual_grad = residual_grad + through_two
    merge_low = residual_grad.astype(BF16)
    out_grad = back_mul(merge_low, weights[2]).astype(BF16).reshape(rows, groups, width)
    head_grad = lax.all_to_all(
        out_grad.transpose(1, 0, 2), NARROW, split_axis=0, concat_axis=0, tiled=True
    ).reshape(length, heads, HD)
    grads = attention_backward(queries, keys, values, logsum.transpose(0, 2, 1), head_grad)
    stacked = jnp.stack(grads, 1).astype(BF16).reshape(groups, rows, 3, width)
    mixed_grad = lax.all_to_all(stacked, NARROW, split_axis=0, concat_axis=0, tiled=True)
    mixed_grad = mixed_grad.transpose(1, 2, 0, 3).reshape(rows, 3 * D)
    through_one, gain_one, shift_one = norm_back_one(back_mul(mixed_grad, weights[1]))
    embed_grad = (residual_grad + through_one).astype(BF16)
    grad_norms = jnp.stack([gain_one, gain_two, gain_three, shift_one, shift_two, shift_three])
    lefts = [embed_grad.T, kept.t1, kept.t2, kept.t3, kept.hidden.T, kept.t5]
    rights = [patches, mixed_grad, merge_low, expand_low, shrink_low, gauss_low]
    products = [matmul(left, right) for left, right in zip(lefts, rights)]
    products[0] = products[0].at[:, features : features + kinds].add(grad_norms.T)
    sums = [
        lax.psum_scatter(
            product.astype(BF16), BOTH, scatter_dimension=0, tiled=True
        ).astype(F32)
        for product in products
    ]
    squares = sum(jnp.sum(part * part) for part in sums)
    loss_sum, square_sum = lax.psum((term[0, 0], squares), BOTH)
    return sums, loss_sum, square_sum


def update_kernel(features, total_ref, sums_ref, *refs):
    sources, targets, refs = refs[:27], refs[27:48], refs[48:]
    loss_ref, norm_ref, refs = refs[0], refs[1], refs[2:]
    inside, news, refs = refs[:27], refs[27:48], refs[48:]
    turned, turned_four, in_sem, out_sem = refs
    loads = [pltpu.make_async_copy(source, dest, in_sem.at[i]) for i, (source, dest) in enumerate(zip(sources, inside))]
    stores = [pltpu.make_async_copy(source, dest, out_sem.at[i]) for i, (source, dest) in enumerate(zip(news, targets))]
    for copy in loads:
        copy.start()
    grads, olds = inside[:6], inside[6:]
    square_sum = sums_ref[1:2, 0:1]
    grad_norm = jnp.sqrt(square_sum)
    factor = jnp.minimum(1.0, CLIP_NORM / (grad_norm + 1e-06))
    norm_ref[...] = grad_norm
    loss_ref[...] = sums_ref[0:1, 0:1] / total_ref[0].astype(F32)
    width = grads[0].shape[1]
    for which in range(7):
        if which < 6:
            loads[which].wait()
        if which == 0:
            turned[...] = grads[0][:, width - LANES :].T
        if which == 4:
            turned_four[...] = grads[4][...].T
        for copy in loads[6 + 3 * which : 9 + 3 * which]:
            copy.wait()
        weight, first, second = olds[3 * which : 3 * which + 3]
        rows, columns = weight.shape
        chunk = min(8, rows)

        def one(step, carry):
            spot = pl.ds(pl.multiple_of(step * chunk, chunk), chunk)
            if which == 0:
                grad = grads[0][spot, 0:columns]
            elif which == 4:
                grad = turned_four[spot, :]
            elif which == 6:
                grad = turned[features % LANES : features % LANES + rows, 0:columns]
            else:
                grad = grads[which][spot, :]
            values = adamw(weight[spot, :], first[spot, :], second[spot, :], grad * factor, RATES[which])
            for dest, value in zip(news[3 * which : 3 * which + 3], values):
                dest[spot, :] = value
            return carry

        lax.fori_loop(0, rows // chunk, one, 0)
        for copy in stores[3 * which : 3 * which + 3]:
            copy.start()
    for copy in stores:
        copy.wait()


def update_all(olds, sums, totals, pair_total, features):
    vmem = pl.BlockSpec(memory_space=pltpu.VMEM)
    smem = pl.BlockSpec(memory_space=pltpu.SMEM)
    hbm = pl.BlockSpec(memory_space=pltpu.HBM)
    shapes = [jax.ShapeDtypeStruct(old.shape, F32) for old in olds]
    inside = [pltpu.VMEM(value.shape, F32) for value in list(sums) + list(olds)]
    return pl.pallas_call(
        functools.partial(update_kernel, features),
        out_shape=shapes + [jax.ShapeDtypeStruct((1, 1), F32)] * 2,
        in_specs=[smem, vmem] + [hbm] * 27,
        out_specs=[hbm] * 21 + [vmem] * 2,
        scratch_shapes=inside
        + [pltpu.VMEM(old.shape, F32) for old in olds]
        + [
            pltpu.VMEM((LANES, sums[0].shape[0]), F32),
            pltpu.VMEM(olds[12].shape, F32),
            pltpu.SemaphoreType.DMA((27,)),
            pltpu.SemaphoreType.DMA((21,)),
        ],
        compiler_params=pltpu.CompilerParams(vmem_limit_bytes=60 * MIB),
        name="update",
    )(pair_total, totals, *sums, *olds)


def body(
    views,
    render_w,
    targets,
    pix_mask,
    pairs,
    view_count,
    pair_total,
    embed_weight,
    embed_first,
    embed_second,
    mixer_weight,
    mixer_first,
    mixer_second,
    merge_weight,
    merge_first,
    merge_second,
    expand_weight,
    expand_first,
    expand_second,
    shrink_weight,
    shrink_first,
    shrink_second,
    unpatch_weight,
    unpatch_first,
    unpatch_second,
    norm_params,
    norm_first,
    norm_second,
):
    masters = (embed_weight, mixer_weight, merge_weight, expand_weight, shrink_weight, unpatch_weight, norm_params)
    firsts = (embed_first, mixer_first, merge_first, expand_first, shrink_first, unpatch_first, norm_first)
    seconds = (embed_second, mixer_second, merge_second, expand_second, shrink_second, unpatch_second, norm_second)
    groups = lax.axis_size(NARROW)
    wide_count = lax.axis_size(WIDE)
    features = embed_weight.shape[0]
    kinds = norm_params.shape[0]
    padded = -(-(features + kinds) // LANES) * LANES
    fill = padded - features - kinds
    by_kernel = mixer_weight.shape[0] % 16 == 0 and shrink_weight.shape[0] % LANES == 0

    patches = views.reshape(-1, features)
    rows = patches.shape[0]
    patches = jnp.pad(patches, ((0, 0), (0, padded - features)))
    if by_kernel:
        raw = (embed_weight.T,) + masters[1:6]
        kept = forward_all(raw, norm_params, patches, features % LANES, wide_count, groups)
    else:
        first_shard = jnp.concatenate([embed_weight.T, norm_params.T], 1)
        first_shard = jnp.pad(first_shard.astype(BF16), ((0, 0), (0, fill)))
        shards = [first_shard] + [weight.astype(BF16) for weight in masters[1:6]]
        kept = forward_plain(shards, patches, features, kinds)
    divisor = pair_total[0].astype(F32)
    gauss_low, term = render(
        kept.gaussians, render_w[0], targets[0], pix_mask[0], pairs[0], view_count, pair_total
    )
    if by_kernel:
        *sums, totals = backward_all(
            kept, patches, gauss_low, term, features % LANES, wide_count, groups
        )
        olds = []
        for triple in zip(masters, firsts, seconds):
            olds += triple
        olds[:3] = [old.T for old in olds[:3]]
        *news, loss, grad_norm = update_all(olds, sums, totals, pair_total, features)
        news[:3] = [new.T for new in news[:3]]
        return tuple(news) + (loss[0, 0], grad_norm[0, 0])
    sums, loss_sum, square_sum = backward_plain(kept, patches, gauss_low, term, features, kinds)
    first_sum = sums[0].T
    grads = [first_sum[:features]] + list(sums[1:]) + [first_sum[features : features + kinds]]
    loss = loss_sum / divisor
    grad_norm = jnp.sqrt(square_sum)
    factor = jnp.minimum(1.0, CLIP_NORM / (grad_norm + 1e-06))
    results = []
    for which in range(7):
        results += adamw(masters[which], firsts[which], seconds[which], grads[which] * factor, RATES[which])
    return tuple(results) + (loss, grad_norm)


def solution(mesh):
    columns = P(None, BOTH)
    rows = P(BOTH, None)
    weights = (columns,) * 3 + (rows,) * 15 + (columns,) * 3
    return jax.shard_map(
        body,
        mesh=mesh,
        in_specs=(
            P(WIDE, None, NARROW, None),
            P(WIDE, None, None, None, None),
            P(WIDE, None, None, NARROW),
            P(WIDE, None, NARROW),
            P(WIDE, None, NARROW),
            P(WIDE),
            P(),
        )
        + weights,
        out_specs=weights + (P(), P()),
        check_vma=False,
    )
```

```python
import functools
import heapq

import jax
import jax.numpy as jnp
from jax import lax
from jax.experimental import pallas as pl
from jax.experimental.pallas import tpu as pltpu
from jax.sharding import PartitionSpec as P

D = 1024
HD = 64
P_SIZE = 8
PP = 64
NVIEW = 4
TMAX = 12
STEP = 10
LANES = 128
MIB = 1024 * 1024

DEPTH_WEIGHT = 1.0
CLIP_NORM = 0.01
BETA_ONE = 0.9
BETA_TWO = 0.95
ADAM_EPS = 1e-08
DECAY = 0.05
RATES = (0.05, 0.05, 0.5, 0.05, 0.05, 0.05, 0.8)
MESH = pl.DeviceIdType.MESH
WIDE, NARROW = BOTH = ("wide", "narrow")
HIGHEST = lax.Precision.HIGHEST
F32 = jnp.float32
BF16 = jnp.bfloat16


def matmul(left, right):
    return jnp.dot(left, right, preferred_element_type=F32)


def outer_sum(left, right):
    return lax.dot_general(left, right, (((0,), (0,)), ((), ())), preferred_element_type=F32)


def back_mul(grad, weight):
    return lax.dot_general(grad, weight, (((1,), (1,)), ((), ())), preferred_element_type=F32)


def layer_norm(values, gain, shift):
    centred = values - jnp.mean(values, -1, keepdims=True)
    spread = jnp.mean(centred * centred, -1, keepdims=True)
    return centred * lax.rsqrt(spread + 1e-05) * gain + shift


def exact_gelu(values):
    return jax.nn.gelu(values, approximate=False)


def attention_forward(queries, keys, values):
    length, heads = (queries.shape[0], queries.shape[1])
    blocked = min(512, length)
    scale = HD ** (-0.5)

    def one_block(query_block):
        scores = (
            jnp.einsum("qhd,khd->hqk", query_block, keys, preferred_element_type=jnp.float32)
            * scale
        )
        highest = jnp.max(scores, -1, keepdims=True)
        exponentials = jnp.exp(scores - highest)
        summed = jnp.sum(exponentials, -1, keepdims=True)
        softmaxed = (exponentials / summed).astype(jnp.bfloat16)
        output = jnp.einsum("hqk,khd->qhd", softmaxed, values, preferred_element_type=jnp.float32)
        return (output.astype(jnp.bfloat16), (highest + jnp.log(summed))[:, :, 0])

    output, logsum = lax.map(one_block, queries.reshape(length // blocked, blocked, heads, HD))
    return (output.reshape(length, heads * HD), logsum)


def attention_backward(queries, keys, values, logsum, out_grad):
    length, heads = (queries.shape[0], queries.shape[1])
    blocked = min(512, length)
    scale = HD ** (-0.5)

    def one_block(carry, inputs):
        key_grad, value_grad = carry
        query_block, logsum_block, grad_block = inputs
        scores = (
            jnp.einsum("qhd,khd->hqk", query_block, keys, preferred_element_type=jnp.float32)
            * scale
        )
        softmaxed = jnp.exp(scores - logsum_block[:, :, None])
        value_grad = value_grad + jnp.einsum(
            "hqk,qhd->khd",
            softmaxed.astype(jnp.bfloat16),
            grad_block,
            preferred_element_type=jnp.float32,
        )
        prob_grad = jnp.einsum(
            "qhd,khd->hqk", grad_block, values, preferred_element_type=jnp.float32
        )
        score_grad = softmaxed * (prob_grad - jnp.sum(softmaxed * prob_grad, -1, keepdims=True))
        score_low = score_grad.astype(jnp.bfloat16)
        query_grad = (
            jnp.einsum("hqk,khd->qhd", score_low, keys, preferred_element_type=jnp.float32) * scale
        )
        key_grad = (
            key_grad
            + jnp.einsum("hqk,qhd->khd", score_low, query_block, preferred_element_type=jnp.float32)
            * scale
        )
        return ((key_grad, value_grad), query_grad)

    zeros = jnp.zeros((length, heads, HD), jnp.float32)
    shaped = (
        queries.reshape(length // blocked, blocked, heads, HD),
        logsum,
        out_grad.reshape(length // blocked, blocked, heads, HD),
    )
    (key_grad, value_grad), query_grad = lax.scan(one_block, (zeros, zeros), shaped)
    return (query_grad.reshape(length, heads, HD), key_grad, value_grad)


def adamw(weight, first, second, grad, rate):
    first = BETA_ONE * first + (1.0 - BETA_ONE) * grad
    second = BETA_TWO * second + (1.0 - BETA_TWO) * grad * grad
    first_hat = first / (1.0 - BETA_ONE**STEP)
    second_hat = second / (1.0 - BETA_TWO**STEP)
    weight = weight - rate * (first_hat / (jnp.sqrt(second_hat) + ADAM_EPS) + DECAY * weight)
    return (weight, first, second)


def chip_bits(chips):
    bits, step = [], 1
    while step < chips:
        bits.append(step)
        step *= 2
    return bits


def flip(chip, mask):
    for bit in chip_bits(mask + 1):
        if mask & bit:
            chip = chip + (1 - 2 * (chip // bit % 2)) * bit
    return chip


def column_halves(width):
    first = -(-width // (2 * LANES)) * LANES
    return ((0, first), (first, width - first))


def work_items(widths, order):
    return [(which,) + half + (side,) for which in order for side, half in enumerate(column_halves(widths[which]))]


class Bag:
    def __init__(self, pairs):
        vars(self).update(pairs)


class Place:
    def __init__(self, wide, narrow):
        self.wide, self.narrow = wide, narrow
        self.chips = wide // 2
        self.bits = chip_bits(self.chips)
        self.w = lax.axis_index(WIDE)
        self.n = lax.axis_index(NARROW)
        self.chip = self.w // 2
        self.core = self.w % 2
        self.twin = (2 * self.chip + 1 - self.core, self.n)

    def across(self, mask):
        return (2 * flip(self.chip, mask) + self.core, self.n)

    def along(self, step):
        return (self.w, lax.rem(self.n + step, self.narrow))

    def neighbours(self):
        return (
            [self.twin]
            + [self.across(bit) for bit in self.bits]
            + [self.along(step) for step in range(1, self.narrow)]
        )


class Planner:
    def __init__(self):
        self.now, self.count = 0.0, 0
        self.free, self.events, self.done, self.spare = {}, [], set(), []
        self.refill = lambda: None

    def transfer(self, link, cost, key, event):
        self.free[link] = max(self.now, self.free.get(link, 0.0)) + cost
        self.count += 1
        heapq.heappush(self.events, (self.free[link] + 2.0, self.count, key, event))

    def step(self):
        when, _, key, event = heapq.heappop(self.events)
        self.now = max(self.now, when) + 0.2
        event()
        self.done.add(key)
        self.refill()

    def fill(self, until):
        for index, (keys, cost, work) in enumerate(self.spare):
            if self.now + cost <= until and self.done.issuperset(keys):
                del self.spare[index]
                work()
                self.now += cost
                return True
        return False

    def need(self, keys):
        while not self.done.issuperset(keys):
            if not self.fill(self.events[0][0]):
                self.step()

    def work(self, cost, work):
        while self.events and self.events[0][0] <= self.now:
            self.step()
        self.refill()
        work()
        self.now += cost

    def later(self, cost, work, keys=()):
        entry = (tuple(keys), cost, work)
        self.spare.append(entry)
        return entry

    def force(self, entry):
        if entry in self.spare:
            self.spare.remove(entry)
            self.work(entry[1], entry[2])

    def finish(self):
        self.refill()
        while self.events or self.spare:
            if not self.fill(self.events[0][0] if self.events else 1e9):
                self.step()


LINK = 90e3
Z_AHEAD = 4.0
RELAYED = (3, 4)
Z_EARLY = 1.0
Z_LATE = 2.0
TWIN_LINK = 600e3


def greet(peers):
    barrier = pltpu.get_barrier_semaphore()
    for peer in peers:
        pl.semaphore_signal(barrier, inc=1, device_id=peer, device_id_type=MESH)
    pl.semaphore_wait(barrier, len(peers))


def normalize(values, gain, shift):
    centred = values - jnp.mean(values, -1, keepdims=True)
    spread = jnp.mean(centred * centred, -1, keepdims=True)
    return centred * lax.rsqrt(spread + 1e-05) * gain + shift


def forward_plan(widths):
    items = []
    for which, cuts in ((0, 1), (1, 3), (2, 1), (3, 2), (5, 1), (4, 2)):
        size = widths[which] // cuts
        for cut in range(cuts):
            for side, (start, width) in enumerate(column_halves(size)):
                items.append((which, cut * size + start, width, side))
    return items


def forward_kernel(items, wide, narrow, lead, ins, outs, scratch, *refs):
    at = Bag(zip(ins + scratch, refs[: len(ins)] + refs[len(ins) + len(outs) :]))
    results = refs[len(ins) : len(ins) + len(outs)]
    weights = [at.first_weight, at.w1, at.w2, at.w3, at.w4, at.w5]
    shards = [at.c0, at.c1, at.c2, at.c3, at.c4, at.c5]
    raw = [at.s0, at.s1, at.s2, at.s3, at.s4, at.s5]
    own_sem, send_sem, recv_sem = at.own_sem, at.send_sem, at.recv_sem
    swap_send, swap_recv, out_sem = at.swap_send, at.swap_recv, at.out_sem
    place = Place(wide, narrow)
    chips, me = place.chips, place.n
    tokens = at.patches.shape[0]
    head_width = D // narrow
    total = len(items)
    started, guarded = [], []

    def start(copy):
        copy.start()
        started.append(copy)

    features = at.s0.shape[1]
    tail = shards[0].shape[1] - LANES
    kinds = at.norm_raw.shape[0]
    kind = lax.broadcasted_iota(jnp.int32, (kinds, LANES), 0)
    spot = lax.broadcasted_iota(jnp.int32, (kinds, LANES), 1)
    put = (spot == kind + lead).astype(F32).astype(BF16)
    shards[0][:, tail:] = outer_sum(at.norm_raw[...].astype(BF16), put).astype(BF16)
    shards[0][:, 0:features] = at.s0[...].astype(BF16)
    for source, dest in zip(raw[1:], shards[1:]):
        dest[...] = source[...].astype(BF16)
    greet(place.neighbours())
    rows_of = [shard.shape[0] for shard in shards]

    def slab(which, node):
        rows = rows_of[which]
        return pl.ds(pl.multiple_of(node * rows, rows), rows)

    def whole_of(which, columns):
        part = weights[which][:, :, :, columns]
        return part.reshape(-1, part.shape[-1])

    own = []
    for which in range(6):
        copy = pltpu.make_async_copy(
            shards[which], weights[which].at[place.chip, place.core, slab(which, me), :], own_sem.at[which]
        )
        copy.start()
        own.append(copy)

    def remote(item, src, dst, slot, peer):
        return pltpu.make_async_remote_copy(
            src_ref=src,
            dst_ref=dst,
            send_sem=send_sem.at[item, slot],
            recv_sem=recv_sem.at[item, slot],
            device_id=peer,
            device_id_type=MESH,
        )

    def group(item, mask):
        which, begin, width, _ = items[item]
        return weights[which].at[flip(place.chip, mask), place.core, :, pl.ds(begin, width)]

    def along(item, sign, hop):
        which, begin, width, _ = items[item]
        columns = pl.ds(begin, width)
        there = weights[which].at[place.chip, place.core, slab(which, me - sign * (hop - 1)), columns]
        return remote(
            item,
            shards[which].at[:, columns] if hop == 1 else there,
            there,
            chips + 1 + hop - 1 + (narrow - 1 if sign < 0 else 0),
            (place.w, me + sign),
        )

    def has_next(sign):
        return me < narrow - 1 if sign > 0 else me >= 1

    def has_come(sign, hop):
        return me >= hop if sign > 0 else me < narrow - hop

    def start_if(condition, copy):
        @pl.when(condition)
        def _():
            copy.start()

        guarded.append((condition, copy))

    def bits_of(item):
        return place.bits if items[item][3] == 0 else place.bits[::-1]

    def across(item, mask, bit):
        return remote(item, group(item, mask), group(item, mask), mask ^ bit, place.across(bit))

    def to_twin(item):
        which, begin, width, _ = items[item]
        there = weights[which].at[:, place.core, :, pl.ds(begin, width)]
        return remote(item, there, there, chips, place.twin)

    plan = Planner()
    waited = set()

    def block_bytes(item):
        which, _, width, _ = items[item]
        return 2 * narrow * rows_of[which] * width

    def twin_event(item):
        to_twin(item).wait_recv()

    here = {}

    def onward(item, mask, number):
        bits = bits_of(item)
        size = block_bytes(item)
        for later in range(number, len(bits)):
            start(across(item, mask, bits[later]))
            coming = mask ^ bits[later]
            plan.transfer(
                bits[later], 2 * size / LINK, (item, coming), functools.partial(arrive, item, coming, later)
            )
        here[item] = here.get(item, 0) + 1
        if here[item] == chips:
            start(to_twin(item))
            plan.transfer(-1, chips * size / TWIN_LINK, (item, chips), functools.partial(twin_event, item))

    def arrive(item, mask, number):
        across(item, mask ^ bits_of(item)[number], bits_of(item)[number]).wait_recv()
        onward(item, mask, number + 1)

    def begin_item(item):
        for sign in (1, -1):
            start_if(has_next(sign), along(item, sign, 1))
        line_transfer(item, 1)

    def line_transfer(item, hop):
        cost = 2 * block_bytes(item) / narrow / LINK
        key = (item, 0) if hop == narrow - 1 else (item, -hop)
        plan.transfer(0, cost, key, functools.partial(line_event, item, hop))

    def line_event(item, hop):
        if items[item][0] not in waited:
            waited.add(items[item][0])
            own[items[item][0]].wait()
        for sign in (1, -1):

            @pl.when(has_come(sign, hop))
            def _():
                along(item, sign, hop).wait_recv()

            if hop < narrow - 1:
                start_if(jnp.logical_and(has_come(sign, hop), has_next(sign)), along(item, sign, hop + 1))
        if hop < narrow - 1:
            line_transfer(item, hop + 1)
        else:
            onward(item, 0, 0)

    begun, ahead = [], [Z_EARLY]

    def refill():
        while len(begun) < total and plan.free.get(0, 0.0) < plan.now + ahead[-1]:
            begin_item(len(begun))
            begun.append(True)

    plan.refill = refill
    refill()

    def need(which, columns=None):
        plan.need(
            [
                (index, key)
                for index, (owner, begin, width, _) in enumerate(items)
                if owner == which and (columns is None or (begin < columns[1] and begin + width > columns[0]))
                for key in range(chips + 1)
            ]
        )

    flushed = []

    def flush(ref):
        index = [vars(at)[name] is ref for name in outs].index(True)
        copy = pltpu.make_async_copy(ref, results[index], out_sem.at[index])
        copy.start()
        flushed.append(copy)

    def swap(src, dst, kind, step):
        return pltpu.make_async_remote_copy(
            src_ref=src,
            dst_ref=dst,
            send_sem=swap_send.at[kind, step],
            recv_sem=swap_recv.at[kind, step],
            device_id=place.along(step),
            device_id_type=MESH,
        )

    gains = at.gains
    embedded, mid, last = at.embedded, at.mid, at.last
    normed, hidden, wave = at.normed, at.hidden, at.wave
    away, qkv, heads_out, returned = at.away, at.qkv, at.heads_out, at.returned

    def turn(dest, source):
        dest[...] = source[...].T
        flush(dest)

    need(0)
    width = weights[0].shape[-1]
    kind = lax.broadcasted_iota(jnp.int32, (8, LANES), 0)
    spot = lax.broadcasted_iota(jnp.int32, (8, LANES), 1)
    pick = (spot == kind + lead).astype(F32).astype(BF16)
    gains[...] = back_mul(pick, whole_of(0, pl.ds(width - LANES, LANES)))
    flush(gains)

    def embed(block):
        cols = pl.ds(block, 256)
        rows = whole_of(0, pl.ds(0, width))[block : block + 256]
        embedded[:, cols] = back_mul(at.patches[...], rows)

    for block in range(0, D, 256):
        plan.work(0.5, functools.partial(embed, block))
    flush(embedded)

    def norm_rows(source, row, dest):
        step_rows = 32

        def one(step, carry):
            rows = pl.ds(pl.multiple_of(step * step_rows, step_rows), step_rows)
            dest[rows, :] = normalize(
                source[rows, :], gains[row : row + 1, :], gains[row + 3 : row + 4, :]
            ).astype(BF16)
            return carry

        lax.fori_loop(0, tokens // step_rows, one, 0)

    plan.work(2.0, lambda: norm_rows(embedded, 0, normed))
    turn_first = plan.later(2.0, lambda: turn(at.t1, normed))
    piece = 2 * (narrow - 1) * 2 * tokens * head_width / LINK

    def project(part, step):
        owner = lax.rem(me + step, narrow)
        offset = pl.multiple_of(part * D + owner * head_width, LANES)
        value = matmul(normed[...], whole_of(1, pl.ds(offset, head_width))).astype(BF16)
        if step:
            away[step - 1, part] = value
            start(swap(away.at[step - 1, part], qkv.at[me, part], part, step))
        else:
            qkv[me, part] = value

    def swap_event(part):
        for step in range(1, narrow):
            swap(away.at[step - 1, part], qkv.at[me, part], part, step).wait_recv()

    for part in range(3):
        need(1, (part * D, part * D + D))
        for step in list(range(1, narrow)) + [0]:
            plan.work(0.7, functools.partial(project, part, step))
        plan.transfer(0, piece, (-1, part), functools.partial(swap_event, part))
    flush(at.w1)
    lane = lax.broadcasted_iota(jnp.int32, (1, LANES), 1)
    scale = HD ** (-0.5)
    length = narrow * tokens
    sides = LANES // HD

    def weigh(step):
        who = lax.rem(me + step, narrow)
        log_sums = jnp.zeros((tokens, LANES), F32)
        sums = jnp.ones((tokens, LANES), F32)
        for pair in range(head_width // LANES):
            lanes = pl.ds(pair * LANES, LANES)
            query = qkv[who, 0, :, lanes].astype(F32)
            key = qkv[:, 1, :, lanes].reshape(length, LANES)
            for side in range(sides):
                head = pair * sides + side
                own_query = (query * jnp.where(lane // HD == side, scale, 0.0)).astype(BF16)
                scores = back_mul(own_query, key)
                highest = jnp.max(scores, -1, keepdims=True)
                exponentials = jnp.exp(scores - highest)
                summed = jnp.sum(exponentials, -1, keepdims=True)
                at.weighed[step, head] = exponentials.astype(BF16)
                log_sums = jnp.where(lane == head, highest + jnp.log(summed), log_sums)
                sums = jnp.where(lane == head, summed, sums)
        at.log_sums[who] = log_sums
        at.weigh_sums[step] = sums

    def attend(step):
        who = lax.rem(me + step, narrow)
        for pair in range(head_width // LANES):
            lanes = pl.ds(pair * LANES, LANES)
            value = qkv[:, 2, :, lanes].reshape(length, LANES)
            out = jnp.zeros((tokens, LANES), F32)
            for side in range(sides):
                head = pair * sides + side
                part = matmul(at.weighed[step, head], value) / at.weigh_sums[step, :, head : head + 1]
                out = jnp.where(lane // HD == side, part, out)
            heads_out[who, :, lanes] = out.astype(BF16)
        if step:
            start(swap(heads_out.at[who], returned.at[me], 3, step))
        else:
            returned[me] = heads_out[who]

    steps = list(range(1, narrow)) + [0]
    ahead.append(Z_LATE)
    plan.need([(-1, 0), (-1, 1)])
    for step in steps:
        plan.work(2.7, functools.partial(weigh, step))
    plan.need([(-1, 2)])
    flush(qkv)

    def return_event(step):
        return lambda: swap(heads_out.at[me], returned.at[me], 3, step).wait_recv()

    for step in steps:
        plan.work(0.9, functools.partial(attend, step))
        if step:
            plan.transfer(0, piece / (narrow - 1), (-2, step), return_event(step))
    flush(heads_out)
    flush(at.log_sums)
    need(2)
    plan.need([(-2, step) for step in range(1, narrow)])

    def merge(block):
        cols = pl.ds(block, 256)
        value = embedded[:, cols]
        weight = whole_of(2, cols)
        for source in range(narrow):
            value = value + matmul(returned[source], weight[source * head_width : (source + 1) * head_width])
        mid[:, cols] = value

    for block in range(0, D, 256):
        plan.work(0.7, functools.partial(merge, block))
    flush(at.w2)
    flush(mid)
    plan.force(turn_first)
    plan.work(2.0, lambda: norm_rows(mid, 1, normed))

    def turn_returned():
        for source in range(narrow):
            at.t2[pl.ds(source * head_width, head_width), :] = returned[source].T
        flush(at.t2)

    plan.later(2.0, turn_returned)
    turn_second = plan.later(2.0, lambda: turn(at.t3, normed))

    ff = weights[3].shape[-1]
    tile = wave.shape[1]
    slopes = at.slopes

    def expand(block):
        wave[...] = matmul(normed[...], whole_of(3, pl.ds(block, tile)))

        def bend(step, carry):
            rows = pl.ds(pl.multiple_of(step * 32, 32), 32)
            x = wave[rows, :]
            half = 0.5 * (1.0 + lax.erf(x * (0.5**0.5)))
            hidden[rows, pl.ds(block, tile)] = (x * half).astype(BF16)
            bell = jnp.exp(-0.5 * x * x) * 0.3989422804014327
            slopes[rows, pl.ds(block, tile)] = (half + x * bell).astype(BF16)
            return carry

        lax.fori_loop(0, tokens // 32, bend, 0)

    for block in range(0, ff, tile):
        need(3, (block, block + tile))
        plan.work(2.5, functools.partial(expand, block))
    flush(at.w3)
    flush(slopes)
    flush(hidden)

    def shrink(block):
        cols = pl.ds(block, 256)
        last[:, cols] = mid[:, cols] + matmul(hidden[...], whole_of(4, cols))

    for block in range(0, D, 256):
        need(4, (block, block + 256))
        plan.work(1.0, functools.partial(shrink, block))
    flush(at.w4)
    flush(last)
    plan.force(turn_second)
    plan.work(2.0, lambda: norm_rows(last, 2, normed))
    need(5)

    def unpatch(block):
        cols = pl.ds(block, 256)
        at.gaussians[:, cols] = matmul(normed[...], whole_of(5, cols))

    for block in range(0, weights[5].shape[-1], 256):
        plan.work(0.7, functools.partial(unpatch, block))
    flush(at.w5)
    flush(at.gaussians)
    plan.later(2.0, lambda: turn(at.t5, normed))
    plan.finish()
    for copy in started:
        copy.wait_send()
    for condition, copy in guarded:

        @pl.when(condition)
        def _():
            copy.wait_send()

    for copy in flushed:
        copy.wait()


def forward_all(shards, norms, patches, lead, wide, narrow):
    tokens = patches.shape[0]
    widths = [patches.shape[1]] + [shard.shape[1] for shard in shards[1:]]
    heights = [shard.shape[0] * wide * narrow for shard in shards]
    ff = widths[3]
    chips = wide // 2
    head_width = D // narrow
    items = forward_plan(widths)
    slots = chips + 1 + 2 * (narrow - 1)
    full = [((chips, 2, height // wide, width), BF16) for height, width in zip(heights, widths)]
    shapes = dict(
        w1=full[1],
        w2=full[2],
        w3=full[3],
        w4=full[4],
        w5=full[5],
        gains=((8, D), F32),
        embedded=((tokens, D), F32),
        mid=((tokens, D), F32),
        last=((tokens, D), F32),
        slopes=((tokens, ff), BF16),
        t1=((D, tokens), BF16),
        t2=((D, tokens), BF16),
        t3=((D, tokens), BF16),
        hidden=((tokens, ff), BF16),
        t5=((D, tokens), BF16),
        qkv=((narrow, 3, tokens, head_width), BF16),
        heads_out=((narrow, tokens, head_width), BF16),
        log_sums=((narrow, tokens, LANES), F32),
        gaussians=((tokens, widths[5]), F32),
    )
    ins = tuple(dict(s0=0, s1=0, s2=0, s3=0, s4=0, s5=0, norm_raw=0, patches=0))
    outs = tuple(shapes)
    extras = dict(
        first_weight=pltpu.VMEM(*full[0]),
        c0=pltpu.VMEM((shards[0].shape[0], widths[0]), BF16),
        c1=pltpu.VMEM(shards[1].shape, BF16),
        c2=pltpu.VMEM(shards[2].shape, BF16),
        c3=pltpu.VMEM(shards[3].shape, BF16),
        c4=pltpu.VMEM(shards[4].shape, BF16),
        c5=pltpu.VMEM(shards[5].shape, BF16),
        normed=pltpu.VMEM((tokens, D), BF16),
        wave=pltpu.VMEM((tokens, 512), F32),
        away=pltpu.VMEM((narrow - 1, 3, tokens, head_width), BF16),
        weighed=pltpu.VMEM((narrow, head_width // HD, tokens, narrow * tokens), BF16),
        weigh_sums=pltpu.VMEM((narrow, tokens, LANES), F32),
        returned=pltpu.VMEM((narrow, tokens, head_width), BF16),
        own_sem=pltpu.SemaphoreType.DMA((6,)),
        send_sem=pltpu.SemaphoreType.DMA((len(items), slots)),
        recv_sem=pltpu.SemaphoreType.DMA((len(items), slots)),
        swap_send=pltpu.SemaphoreType.DMA((4, narrow)),
        swap_recv=pltpu.SemaphoreType.DMA((4, narrow)),
        out_sem=pltpu.SemaphoreType.DMA((len(outs),)),
    )
    scratch = outs + tuple(extras)
    anywhere = pl.BlockSpec(memory_space=pl.ANY)
    results = pl.pallas_call(
        functools.partial(forward_kernel, items, wide, narrow, lead, ins, outs, scratch),
        out_shape=[jax.ShapeDtypeStruct(*shapes[name]) for name in outs],
        in_specs=[pl.BlockSpec(memory_space=pltpu.VMEM)] * len(ins),
        out_specs=[anywhere] * len(outs),
        scratch_shapes=[pltpu.VMEM(*shapes[name]) for name in outs] + list(extras.values()),
        compiler_params=pltpu.CompilerParams(
            collective_id=0, has_side_effects=True, vmem_limit_bytes=60 * MIB
        ),
        name="forward",
    )(*shards, norms, patches)
    results = [result.reshape(-1, result.shape[-1]) for result in results[:5]] + list(results[5:])
    return Bag(zip(outs, results))


def backward_plan(widths, pairs):
    items = []
    for which, cuts in ((5, 1), (4, 1), (3, 1), (2, 1), (1, pairs), (0, 1)):
        size = widths[which] // cuts
        for cut in range(cuts):
            for side, (start, width) in enumerate(column_halves(size)):
                items.append((which, cut * size + start, width, side))
    return items


def tile_of(width):
    for tile in (512, 384, 256, 128):
        if width % tile == 0:
            return tile
    return width


def backward_kernel(items, wide, narrow, lead, ins, scratch, *refs):
    src = Bag(zip(ins, refs))
    refs = refs[len(ins) :]
    sums, totals, refs = refs[:6], refs[6], list(refs[7:])
    at = Bag(zip(scratch, refs))
    place = Place(wide, narrow)
    chips, me = place.chips, place.n
    total = len(items)
    refs = refs[len(scratch) :]
    held = [refs.pop(0) for _ in items]
    passed = [[refs.pop(0) for _ in place.bits] for _ in items]
    final = [refs.pop(0) for _ in items]
    spare = [refs.pop(0) for _ in range(6)]
    tokens = src.patches.shape[0]
    head_width = D // narrow
    length = narrow * tokens
    reach = narrow * LANES
    send_sem, recv_sem, tile_send, tile_recv = at.send_sem, at.recv_sem, at.tile_send, at.tile_recv
    swap_send, swap_recv, in_sem, ring_sem = at.swap_send, at.swap_recv, at.in_sem, at.ring_sem
    gains, norms, extra = src.gains, at.norms, at.extra
    stash, d_res, d_norm = at.stash, at.d_res, at.d_norm
    mixed, merge_low, expand_low, shrink_low = at.mixed, at.merge_low, at.expand_low, at.shrink_low

    loaded = [name for name in ins if name in scratch]

    def load(ref):
        index = [vars(at)[name] is ref for name in loaded].index(True)
        return pltpu.make_async_copy(vars(src)[loaded[index]], ref, in_sem.at[index])

    def load_stash(ref):
        return pltpu.make_async_copy(ref, stash, in_sem.at[len(loaded)])

    def ring(ref, slots, rows, columns, index, row):
        slot = lax.rem(index, slots.shape[0])
        return pltpu.make_async_copy(
            ref.at[pl.ds(pl.multiple_of(row, rows), rows), :],
            slots.at[slot, pl.ds(0, rows), pl.ds(0, columns)],
            ring_sem.at[0 if slots is at.tall else 1, slot],
        )

    slope_rows = at.tall.shape[1]
    tall, long = at.tall.shape[0], at.long.shape[0]

    def slope_load(index):
        slot = lax.rem(index, tall)
        return pltpu.make_async_copy(
            src.slopes.at[:, pl.ds(pl.multiple_of(index * slope_rows, slope_rows), slope_rows)],
            at.slope_slots.at[slot],
            ring_sem.at[2, slot],
        )

    u_rows, u_cols = 256, src.w5.shape[1]
    load_stash(src.last).start()
    for index in range(tall):
        ring(src.w5, at.tall, u_rows, u_cols, index, index * u_rows).start()
        slope_load(index).start()
    for index in range(long):
        ring(src.w3, at.long, 128, src.w3.shape[1], index, index * 128).start()
    for name in loaded:
        load(vars(at)[name]).start()

    peers = [(lax.rem(place.w + step, wide), place.n) for step in range(1, wide)]
    peers += [place.along(step) for step in range(1, narrow)]
    greet(peers)

    started, guarded = [], []

    def start(copy):
        copy.start()
        started.append(copy)

    lefts = [at.embed_t, at.t1, at.t2, at.t3, at.shrink_t, at.t5]
    rights = [src.patches, mixed, merge_low, expand_low, at.hidden, src.gauss]

    def remote(item, src, dst, slot, peer):
        return pltpu.make_async_remote_copy(
            src_ref=src,
            dst_ref=dst,
            send_sem=send_sem.at[item, slot],
            recv_sem=recv_sem.at[item, slot],
            device_id=peer,
            device_id_type=MESH,
        )

    def bits_of(item):
        return place.bits[::-1] if items[item][3] == 0 else place.bits

    def groups_of(item):
        size = max(1, 512 // (narrow * spare[items[item][0]].shape[2]))
        if items[item][0] == 4:
            size = chips
        masks = list(range(chips))
        if bits_of(item) and bits_of(item)[0] > 1:
            masks = masks[chips // 2 :] + masks[: chips // 2]
        return [sorted(masks[at_mask : at_mask + size]) for at_mask in range(0, chips, size)]

    def product(item, masks, core, into, plus):
        which, begin, width, _ = items[item]
        left, right = lefts[which], rights[which]
        rows = into.shape[-2]
        span = narrow * rows
        tile = tile_of(width)
        if which == 4:
            size = into.shape[-1]
            for mask in masks:
                column = ((flip(place.chip, mask) * 2 + core) * narrow) * size
                rhs = right[:, pl.ds(pl.multiple_of(column, narrow * size), narrow * size)]
                value = jnp.dot(left[begin : begin + width, :], rhs, preferred_element_type=F32)
                for node in range(narrow):
                    piece = value[:, node * size : (node + 1) * size]
                    if plus:
                        piece = piece + into[mask, node].astype(F32)
                    into[mask, node] = piece.astype(BF16)
            return
        firsts = [((flip(place.chip, mask) * 2 + core) * narrow) * rows for mask in masks]
        with_extra = which == 0 and begin + width == right.shape[1]
        assert not with_extra or tile == width
        if which == 1:
            tile = LANES * 2

        def one(step, carry):
            offset = pl.multiple_of(begin + step * tile, LANES)
            local = pl.multiple_of(step * tile, LANES)
            if which != 1:
                rhs = right[:, pl.ds(offset, tile)]
            else:
                part, inside = offset // reach, pl.multiple_of(offset % reach, LANES)
                rhs = right[part // 3, part % 3, :, pl.ds(inside, tile)]
            spots = [pl.ds(pl.multiple_of(first, span), span) for first in firsts]
            lhs = jnp.concatenate([left[spot, :] for spot in spots], 0)
            value = jnp.dot(lhs, rhs, preferred_element_type=F32)
            for index, mask in enumerate(masks):
                piece = value[index * span : (index + 1) * span]
                if with_extra:
                    blank = jnp.zeros((span, tile - LANES), F32)
                    piece = piece + jnp.concatenate([blank, extra[spots[index], :]], 1)
                piece = piece.reshape(narrow, rows, tile)
                if plus:
                    piece = piece + into[mask, :, :, pl.ds(local, tile)].astype(F32)
                into[mask, :, :, pl.ds(local, tile)] = piece.astype(BF16)
            return carry

        lax.fori_loop(0, width // tile, one, 0)

    last_sent = {}
    plan = Planner()

    def to_twin(item, masks):
        which, _, width, _ = items[item]
        some = pl.ds(masks[0], len(masks))
        own = spare[which].at[some] if which == 4 else spare[which].at[some, :, :, pl.ds(0, width)]
        return remote(item, own, held[item].at[some], masks[0], place.twin)

    def across(item, mask, bit, number, slot):
        return remote(
            item, held[item].at[mask], passed[item][number].at[slot], chips + mask, place.across(bit)
        )

    def relayed(item):
        return items[item][0] in RELAYED

    def hopping(item, sign, hop):
        count = narrow - hop
        first = hop if sign > 0 else 0
        node = hop if sign > 0 else narrow - 1 - hop
        return remote(
            item,
            held[item].at[0, pl.ds(first, count)],
            final[item].at[pl.ds(first + (1 if sign > 0 else 0), count)],
            2 * chips + (0 if sign > 0 else 1),
            (place.w, node),
        )

    def send_hop(item, sign, hop):
        sender = me == (hop - 1 if sign > 0 else narrow - hop)

        @pl.when(sender)
        def _():
            hopping(item, sign, hop).start()

        guarded.append((sender, hopping(item, sign, hop)))

    def hop_event(item, hop):
        count = narrow - hop - 1
        for sign in (1, -1):
            first = hop + 1 if sign > 0 else 0
            shift = 1 if sign > 0 else 0

            @pl.when(me == (hop if sign > 0 else narrow - 1 - hop))
            def _():
                hopping(item, sign, hop).wait_recv()
                if count:
                    mine, theirs = pl.ds(first, count), pl.ds(first + shift, count)
                    value = held[item][0, mine].astype(F32) + final[item][theirs].astype(F32)
                    held[item][0, mine] = value.astype(BF16)

            if count:
                send_hop(item, sign, hop + 1)
        if count:
            hop_transfer(item, hop + 1)
        else:
            finish(item)

    def hop_transfer(item, hop):
        cost = (narrow - hop) * 2 * block_bytes(item) / narrow / LINK
        event = functools.partial(hop_event, item, hop)
        plan.transfer(0 if hop == 1 else 100 + hop, cost, (item, -hop, 0), event)

    def along(item, step):
        target = place.along(step)
        return remote(
            item,
            held[item].at[0, target[1]],
            final[item].at[narrow - step - 1],
            2 * chips + narrow - step - 1,
            target,
        )

    def leaves(item, mask):
        bits = bits_of(item)
        return min([number for number, bit in enumerate(bits) if mask & bit], default=len(bits))

    def slot_of(item, mask, number):
        bits = bits_of(item)
        kept = [m for m in range(chips) if not any(m & bit for bit in bits[: number + 1])]
        return kept.index(mask)

    def add_into(dest, dest_at, src, src_at):
        dest[dest_at] = (dest[dest_at].astype(F32) + src[src_at].astype(F32)).astype(BF16)

    def block_bytes(item):
        _, nodes, rows, width = held[item].shape
        return 2 * nodes * rows * width

    def push(which, pair=None):
        for item, (owner, begin, _, _) in enumerate(items):
            if owner != which or (pair is not None and begin // (3 * reach) != pair):
                continue
            for masks in groups_of(item):
                cost = len(masks) * block_bytes(item) / 1e6
                plan.work(cost, functools.partial(push_some, item, masks))

    def push_some(item, masks):
        which = items[item][0]
        for key in [key for key in last_sent if key[0] == which and set(key[1]) & set(masks)]:
            last_sent.pop(key).wait_send()
        product(item, masks, 1 - place.core, spare[which], False)
        copy = to_twin(item, masks)
        copy.start()
        last_sent[which, tuple(masks)] = copy
        cost = len(masks) * block_bytes(item) / TWIN_LINK
        plan.transfer(-1, cost, (item, 0, masks[0]), functools.partial(own_event, item, masks))

    def own_event(item, masks):
        to_twin(item, masks).wait_recv()
        product(item, masks, place.core, held[item], True)
        plan.now += len(masks) * block_bytes(item) / 1e6
        plan.done.update((item, 0, mask) for mask in masks)
        for mask in masks:
            onward(item, mask, 0)

    def onward(item, mask, number):
        bits = bits_of(item)
        if number == len(bits):
            lined.append(item)
            refill()
        elif leaves(item, mask) == number:
            kept = mask ^ bits[number]
            start(across(item, mask, bits[number], number, slot_of(item, kept, number)))
            plan.transfer(
                bits[number],
                2 * block_bytes(item) / LINK,
                (item, 1 + number, kept),
                functools.partial(sum_event, item, kept, number),
            )

    lined = []

    def refill():
        while lined and plan.free.get(0, 0.0) < plan.now + Z_AHEAD:
            item = lined.pop(0)
            if relayed(item):
                for sign in (1, -1):
                    send_hop(item, sign, 1)
                hop_transfer(item, 1)
                continue
            for step in range(1, narrow):
                start(along(item, step))
            cost = 2 * (narrow // 2) ** 2 * block_bytes(item) / narrow / LINK
            plan.transfer(0, cost, (item, -1, 0), functools.partial(finish, item))

    plan.refill = refill

    def sum_event(item, mask, number):
        plan.need([(item, before, mask) for before in range(number + 1)])
        bit = bits_of(item)[number]
        slot = slot_of(item, mask, number)
        across(item, mask ^ bit, bit, number, slot).wait_recv()
        add_into(held[item], mask, passed[item][number], slot)
        plan.now += block_bytes(item) / 8e5
        onward(item, mask, number + 1)

    at.squares[...] = jnp.zeros_like(at.squares)

    def finish(item):
        which, begin, width, _ = items[item]
        value = held[item][0, me].astype(F32)
        if relayed(item):
            value = value + jnp.where(me >= 1, final[item][me + 1].astype(F32), 0.0)
            value = value + jnp.where(me < narrow - 1, final[item][me].astype(F32), 0.0)
        else:
            for step in range(1, narrow):
                along(item, step).wait_recv()
            for slot in range(narrow - 1):
                value = value + final[item][slot].astype(F32)
        columns = pl.ds(0, value.shape[1])
        at.squares[:, columns] += jnp.sum(value * value, 0, keepdims=True)
        if which == 1:
            for shift in range(0, width, LANES):
                part, spot = (begin + shift) // reach, (begin + shift) % reach
                column = part % 3 * D + spot // LANES * head_width + part // 3 * LANES
                sums[which][:, pl.ds(column, LANES)] = value[:, shift : shift + LANES]
        elif which == 4:
            sums[which][pl.ds(begin, width), :] = value
        else:
            sums[which][:, pl.ds(begin, width)] = value

    norms[...] = jnp.zeros_like(norms)

    def norm_back(row, low, add):
        step_rows = 32

        def one(step, carry):
            rows = pl.ds(pl.multiple_of(step * step_rows, step_rows), step_rows)
            values = stash[rows, :]
            upper = d_norm[rows, :]
            centred = values - jnp.mean(values, -1, keepdims=True)
            rate = lax.rsqrt(jnp.mean(centred * centred, -1, keepdims=True) + 1e-05)
            unit = centred * rate
            norms[row : row + 1, :] += jnp.sum(upper * unit, 0, keepdims=True)
            norms[row + 3 : row + 4, :] += jnp.sum(upper, 0, keepdims=True)
            scaled = upper * gains[row : row + 1, :]
            inner = scaled - jnp.mean(scaled, -1, keepdims=True)
            inner = rate * (inner - unit * jnp.mean(scaled * unit, -1, keepdims=True))
            if add:
                inner = inner + d_res[rows, :]
            d_res[rows, :] = inner
            low[rows, :] = inner.astype(BF16)
            return carry

        lax.fori_loop(0, tokens // step_rows, one, 0)

    def loop_work(cost, count, pieces, body):
        for piece in range(pieces):
            low, high = count * piece // pieces, count * (piece + 1) // pieces
            plan.work(cost / pieces, functools.partial(lax.fori_loop, low, high, body, 0))

    load(at.t5).wait()
    push(5)
    load_stash(src.last).wait()
    count = D // u_rows
    tall_rows = slope_rows

    def through_unpatch(index, carry):
        ring(src.w5, at.tall, u_rows, u_cols, index, index * u_rows).wait()
        slot = at.tall.at[lax.rem(index, tall)]
        offset = pl.multiple_of(index * u_rows, u_rows)
        d_norm[:, pl.ds(offset, u_rows)] = back_mul(src.gauss[...], slot[0:u_rows, 0:u_cols])

        @pl.when(index + tall < count)
        def _():
            ring(src.w5, at.tall, u_rows, u_cols, index + tall, (index + tall) * u_rows).start()

        return carry

    loop_work(2.5, count, 1, through_unpatch)
    for index in range(tall):
        ring(src.w4, at.tall, tall_rows, D, index, index * tall_rows).start()
    plan.work(2.5, lambda: norm_back(2, shrink_low, False))
    load_stash(src.mid).start()
    load(at.hidden).wait()

    def turn_shrink():
        at.shrink_t[...] = shrink_low[...].T

    plan.work(2.0, turn_shrink)
    push(4)
    ff = src.w3.shape[1]
    slabs = ff // tall_rows

    def through_shrink(index, carry):
        ring(src.w4, at.tall, tall_rows, D, index, index * tall_rows).wait()
        slope_load(index).wait()
        slot = lax.rem(index, tall)
        value = back_mul(shrink_low[...], at.tall[slot])
        value = value * at.slope_slots[slot].astype(F32)
        expand_low[:, pl.ds(pl.multiple_of(index * tall_rows, tall_rows), tall_rows)] = value.astype(BF16)

        @pl.when(index + tall < slabs)
        def _():
            ring(src.w4, at.tall, tall_rows, D, index + tall, (index + tall) * tall_rows).start()
            slope_load(index + tall).start()

        return carry

    loop_work(6.0, slabs, 2, through_shrink)
    owners = [lax.rem(me + step, narrow) for step in list(range(1, narrow)) + [0]]
    for index in range(min(tall, narrow)):
        ring(src.w2, at.tall, head_width, D, index, owners[index] * head_width).start()
    load(at.t3).wait()

    def through_expand(index, carry):
        ring(src.w3, at.long, 128, ff, index, index * 128).wait()
        offset = pl.multiple_of(index * 128, 128)
        d_norm[:, pl.ds(offset, 128)] = back_mul(expand_low[...], at.long[lax.rem(index, long)])

        @pl.when(index + long < D // 128)
        def _():
            ring(src.w3, at.long, 128, ff, index + long, (index + long) * 128).start()

        return carry

    loop_work(5.0, D // 128, 2, through_expand)
    for index in range(long):
        ring(src.w1, at.long, 128, 3 * D, index, index * 128).start()
    load_stash(src.mid).wait()
    plan.work(2.0, lambda: norm_back(1, merge_low, True))
    load_stash(src.embedded).start()

    def swap(src, dst, kind, step):
        return pltpu.make_async_remote_copy(
            src_ref=src,
            dst_ref=dst,
            send_sem=swap_send.at[kind, step],
            recv_sem=swap_recv.at[kind, step],
            device_id=place.along(step),
            device_id_type=MESH,
        )

    d_heads, away = at.d_heads, at.away
    piece = 2 * (narrow - 1) * 2 * tokens * head_width / LINK

    def head_event():
        for step in range(1, narrow):
            swap(away.at[step - 1], d_heads.at[me], 0, step).wait_recv()

    def through_merge(index, owner):
        ring(src.w2, at.tall, head_width, D, index, owner * head_width).wait()
        value = back_mul(merge_low[...], at.tall[index % tall, 0:head_width, :]).astype(BF16)
        if index < narrow - 1:
            away[index] = value
            start(swap(away.at[index], d_heads.at[me], 0, index + 1))
        else:
            d_heads[me] = value
        if index + tall < narrow:
            ring(src.w2, at.tall, head_width, D, index + tall, owners[index + tall] * head_width).start()

    for index, owner in enumerate(owners):
        plan.work(0.7, functools.partial(through_merge, index, owner))
    plan.transfer(0, piece, (-1, 0, 0), head_event)
    load(at.t2).wait()
    push(3)
    push(2)
    load(at.qkv).wait()
    load(at.heads_out).wait()
    load(at.log_sums).wait()
    plan.need([(-1, 0, 0)])

    qkv, heads_out, log_sums, parts = at.qkv, at.heads_out, at.log_sums, at.parts
    key_t, key_acc, value_acc, query_acc = at.key_t, at.key_acc, at.value_acc, at.query_acc
    lane = lax.broadcasted_iota(jnp.int32, (1, LANES), 1)
    sides = LANES // HD
    scale = HD ** (-0.5)
    choose = lax.broadcasted_iota(jnp.int32, (8, LANES), 1) // HD
    choose = (choose == lax.broadcasted_iota(jnp.int32, (8, LANES), 0)).astype(F32)

    def part_swap(pair, step):
        lanes = pl.ds(pair * LANES, LANES)
        who = lax.rem(me + step, narrow)
        return swap(
            parts.at[who, :, :, lanes],
            mixed.at[pair, :, :, pl.ds(pl.multiple_of(me * LANES, LANES), LANES)],
            1 + pair,
            step,
        )

    pushed_pairs = []
    load(at.t1).wait()

    def part_event(pair):
        for step in range(1, narrow):
            part_swap(pair, step).wait_recv()

    for pair in range(head_width // LANES):
        lanes = pl.ds(pair * LANES, LANES)
        key_t[...] = qkv[:, 1, :, lanes].reshape(length, LANES).T
        key_acc[...] = jnp.zeros_like(key_acc)
        value_acc[...] = jnp.zeros_like(value_acc)
        def one_block(step, lanes=lanes, pair=pair):
            who = lax.rem(me + step, narrow)
            query = qkv[who, 0, :, lanes].astype(F32)
            upper = d_heads[who, :, lanes].astype(F32)
            kept = heads_out[who, :, lanes].astype(F32)
            delta = lax.dot_general(
                choose,
                upper * kept,
                (((1,), (1,)), ((), ())),
                precision=HIGHEST,
                preferred_element_type=F32,
            )
            log_rows = log_sums[who].T[pair * sides : (pair + 1) * sides, :]
            masks = [jnp.where(lane // HD == side, 1.0, 0.0) for side in range(sides)]
            own_query = jnp.concatenate([query * (scale * mask) for mask in masks], 0).astype(BF16)
            own_upper = jnp.concatenate([upper * mask for mask in masks], 0).astype(BF16)
            log_row = jnp.concatenate([log_rows[side : side + 1, :] for side in range(sides)], 1)
            delta_row = jnp.concatenate([delta[side : side + 1, :] for side in range(sides)], 1)
            query_acc[...] = jnp.zeros_like(query_acc)

            def block(source, carry):
                rows = pl.ds(pl.multiple_of(source * tokens, tokens), tokens)
                key, value = qkv[source, 1, :, lanes], qkv[source, 2, :, lanes]
                probs = jnp.exp(back_mul(key, own_query) - log_row)
                d_probs = back_mul(value, own_upper)
                d_scores = (probs * (d_probs - delta_row)).astype(BF16)
                value_acc[rows, :] += matmul(probs.astype(BF16), own_upper)
                key_acc[rows, :] += matmul(d_scores, own_query)
                turned = matmul(key_t[:, rows], d_scores)
                for side in range(sides):
                    spot = slice(side * HD, (side + 1) * HD)
                    query_acc[spot, :] += turned[spot, side * tokens : (side + 1) * tokens]
                return carry

            lax.fori_loop(0, narrow, block, 0)
            parts[who, 0, :, lanes] = (query_acc[...].T * scale).astype(BF16)
        for step in range(narrow):
            plan.work(3.0, functools.partial(one_block, step))
            for earlier in range(pair):
                if earlier not in pushed_pairs and (-2, 0, earlier) in plan.done:
                    pushed_pairs.append(earlier)
                    push(1, earlier)
        for source in range(narrow):
            rows = pl.ds(source * tokens, tokens)
            parts[source, 1, :, lanes] = key_acc[rows, :].astype(BF16)
            parts[source, 2, :, lanes] = value_acc[rows, :].astype(BF16)
        for step in range(1, narrow):
            start(part_swap(pair, step))
        plan.now += 1.0
        plan.transfer(0, 1.5 * piece, (-2, 0, pair), functools.partial(part_event, pair))
        mixed[pair, :, :, pl.ds(pl.multiple_of(me * LANES, LANES), LANES)] = parts[me, :, :, lanes]
    for pair in range(head_width // LANES):
        if pair not in pushed_pairs:
            plan.need([(-2, 0, pair)])
            push(1, pair)

    def through_mixer(index, carry):
        ring(src.w1, at.long, 128, 3 * D, index, index * 128).wait()
        slot = lax.rem(index, long)
        value = jnp.zeros((tokens, 128), F32)
        for pair in range(head_width // LANES):
            for part in range(3):
                columns = [part * D + owner * head_width + pair * LANES for owner in range(narrow)]
                weight = [at.long[slot, :, column : column + LANES] for column in columns]
                value = value + back_mul(mixed[pair, part], jnp.concatenate(weight, 1))
        d_norm[:, pl.ds(pl.multiple_of(index * 128, 128), 128)] = value

        @pl.when(index + long < D // 128)
        def _():
            ring(src.w1, at.long, 128, 3 * D, index + long, (index + long) * 128).start()

        return carry

    plan.work(4.0, lambda: lax.fori_loop(0, D // 128, through_mixer, 0))
    load_stash(src.embedded).wait()
    plan.work(3.0, lambda: norm_back(0, at.embed_low, True))
    at.embed_t[...] = at.embed_low[...].T
    turned = jnp.concatenate([norms[...], jnp.zeros((LANES - 8, D), F32)], 0).T
    at.extra[...] = pltpu.roll(turned, lead, 1)
    push(0)
    plan.finish()

    rows = lax.broadcasted_iota(jnp.int32, (8, LANES), 0)
    wide_tiles, narrow_tiles = at.wide_tiles, at.narrow_tiles
    wide_tiles[place.w] = jnp.where(rows == 0, src.term[...], jnp.sum(at.squares[...]))

    def tile_copy(buffer, index, slot, peer):
        return pltpu.make_async_remote_copy(
            src_ref=buffer.at[index],
            dst_ref=buffer.at[index],
            send_sem=tile_send.at[slot],
            recv_sem=tile_recv.at[slot],
            device_id=peer,
            device_id_type=MESH,
        )

    for step in range(1, wide):
        start(tile_copy(wide_tiles, place.w, step - 1, (lax.rem(place.w + step, wide), place.n)))
    for step in range(1, wide):
        tile_copy(wide_tiles, place.w, step - 1, (lax.rem(place.w + step, wide), place.n)).wait_recv()
    whole = wide_tiles[0]
    for index in range(1, wide):
        whole = whole + wide_tiles[index]
    narrow_tiles[place.n] = whole
    for step in range(1, narrow):
        start(tile_copy(narrow_tiles, place.n, wide + step - 1, place.along(step)))
    for step in range(1, narrow):
        tile_copy(narrow_tiles, place.n, wide + step - 1, place.along(step)).wait_recv()
    whole = narrow_tiles[0]
    for index in range(1, narrow):
        whole = whole + narrow_tiles[index]
    totals[...] = whole
    for copy in list(last_sent.values()) + started:
        copy.wait_send()
    for condition, copy in guarded:

        @pl.when(condition)
        def _():
            copy.wait_send()


def backward_all(kept, patches, gauss, term, lead, wide, narrow):
    tokens = patches.shape[0]
    chips = wide // 2
    weights = [kept.w1, kept.w2, kept.w3, kept.w4, kept.w5]
    heights = [D] + [weight.shape[0] for weight in weights]
    widths = [patches.shape[1]] + [weight.shape[1] for weight in weights]
    rows = [height // (wide * narrow) for height in heights]
    head_width = D // narrow
    length = narrow * tokens
    items = backward_plan(widths, head_width // LANES)
    slots = 2 * chips + max(2, narrow - 1)
    streamed = dict(w1=kept.w1, w2=kept.w2, w3=kept.w3, w4=kept.w4, w5=kept.w5)
    streamed.update(last=kept.last, mid=kept.mid, embedded=kept.embedded, slopes=kept.slopes)
    loaded = dict(t5=kept.t5, hidden=kept.hidden, t3=kept.t3, t2=kept.t2, t1=kept.t1)
    loaded.update(qkv=kept.qkv, heads_out=kept.heads_out, log_sums=kept.log_sums)
    whole = dict(gains=kept.gains, patches=patches, gauss=gauss, term=term)
    operands = {**streamed, **loaded, **whole}
    shapes = [jax.ShapeDtypeStruct((rows[which], widths[which]), F32) for which in range(6)]
    shapes[4] = jax.ShapeDtypeStruct((D, rows[4]), F32)
    shapes.append(jax.ShapeDtypeStruct((8, LANES), F32))
    scratch = {name: pltpu.VMEM(value.shape, value.dtype) for name, value in loaded.items()}
    blocks = [(width, rows[which]) if which == 4 else (rows[which], width) for which, _, width, _ in items]
    scratch.update(
        squares=pltpu.VMEM((1, max(block[1] for block in blocks)), F32),
        embed_t=pltpu.VMEM((D, tokens), BF16),
        embed_low=pltpu.VMEM((tokens, D), BF16),
        shrink_t=pltpu.VMEM((D, tokens), BF16),
        stash=pltpu.VMEM((tokens, D), F32),
        d_res=pltpu.VMEM((tokens, D), F32),
        d_norm=pltpu.VMEM((tokens, D), F32),
        norms=pltpu.VMEM((8, D), F32),
        extra=pltpu.VMEM((D, LANES), F32),
        shrink_low=pltpu.VMEM((tokens, D), BF16),
        expand_low=pltpu.VMEM((tokens, widths[3]), BF16),
        merge_low=pltpu.VMEM((tokens, D), BF16),
        mixed=pltpu.VMEM((head_width // LANES, 3, tokens, narrow * LANES), BF16),
        tall=pltpu.VMEM((4, 256, D), BF16),
        long=pltpu.VMEM((3, 128, widths[3]), BF16),
        slope_slots=pltpu.VMEM((4, tokens, 256), BF16),
        d_heads=pltpu.VMEM((narrow, tokens, head_width), BF16),
        away=pltpu.VMEM((narrow - 1, tokens, head_width), BF16),
        parts=pltpu.VMEM((narrow, 3, tokens, head_width), BF16),
        key_t=pltpu.VMEM((LANES, length), BF16),
        key_acc=pltpu.VMEM((length, LANES), F32),
        value_acc=pltpu.VMEM((length, LANES), F32),
        query_acc=pltpu.VMEM((LANES, tokens), F32),
        wide_tiles=pltpu.VMEM((wide, 8, LANES), F32),
        narrow_tiles=pltpu.VMEM((narrow, 8, LANES), F32),
        send_sem=pltpu.SemaphoreType.DMA((len(items), slots)),
        recv_sem=pltpu.SemaphoreType.DMA((len(items), slots)),
        tile_send=pltpu.SemaphoreType.DMA((wide + narrow,)),
        tile_recv=pltpu.SemaphoreType.DMA((wide + narrow,)),
        swap_send=pltpu.SemaphoreType.DMA((1 + head_width // LANES, narrow)),
        swap_recv=pltpu.SemaphoreType.DMA((1 + head_width // LANES, narrow)),
        in_sem=pltpu.SemaphoreType.DMA((9,)),
        ring_sem=pltpu.SemaphoreType.DMA((3, 4)),
    )
    lists = [pltpu.VMEM((chips, narrow) + block, BF16) for block in blocks]
    for block in blocks:
        for bit in chip_bits(chips):
            lists.append(pltpu.VMEM((chips // (2 * bit), narrow) + block, BF16))
    for (which, _, _, _), block in zip(items, blocks):
        lists.append(pltpu.VMEM((narrow + (1 if which in RELAYED else -1),) + block, BF16))
    for which in range(6):
        widest = max(block for item, block in zip(items, blocks) if item[0] == which)
        lists.append(pltpu.VMEM((chips, narrow) + widest, BF16))
    vmem = pl.BlockSpec(memory_space=pltpu.VMEM)
    hbm = pl.BlockSpec(memory_space=pl.ANY)
    return pl.pallas_call(
        functools.partial(backward_kernel, items, wide, narrow, lead, tuple(operands), tuple(scratch)),
        out_shape=shapes,
        in_specs=[vmem if name in whole else hbm for name in operands],
        out_specs=[vmem] * len(shapes),
        scratch_shapes=list(scratch.values()) + lists,
        compiler_params=pltpu.CompilerParams(
            collective_id=1, has_side_effects=True, vmem_limit_bytes=63 * MIB
        ),
        name="backward",
    )(*operands.values())


def render_kernel(
    gauss_ref, weight_ref, target_ref, mask_ref, pair_ref, view_ref, total_ref, grad_ref, term_ref, feat, dfeat
):
    quads = gauss_ref.shape[0] // NVIEW
    span = weight_ref.shape[1]
    pairs = pair_ref.shape[1]
    scale = 1.0 / total_ref[0].astype(F32)

    def channel(index):
        return gauss_ref[:, index * PP : (index + 1) * PP]

    def shared():
        opacity = jax.nn.sigmoid(channel(3))
        extent = jax.nn.sigmoid(channel(5) + channel(6) + channel(7))
        lead = channel(8)
        denom = 1.0 + lead * lead + channel(9) * channel(9) + channel(10) * channel(10) + channel(11) * channel(11)
        facing = lead * lead / denom
        raw = channel(4)
        depth = jnp.maximum(raw, 0.0) + jnp.log1p(jnp.exp(-jnp.abs(raw)))
        return opacity, extent, lead, denom, facing, raw, depth

    opacity, extent, lead, denom, facing, raw, depth = shared()
    footprint = opacity * extent * facing
    channels = [jax.nn.sigmoid(channel(index)) * footprint for index in range(3)]
    channels += [footprint, depth * footprint]
    for index, value in enumerate(channels):
        for view in range(NVIEW):
            feat[index * quads : (index + 1) * quads, view * PP : (view + 1) * PP] = value[
                view * quads : (view + 1) * quads
            ]
    rendered = jnp.dot(feat[...], weight_ref[...], precision=HIGHEST, preferred_element_type=F32)
    parts = [rendered[index * quads : (index + 1) * quads] for index in range(5)]
    lane = lax.broadcasted_iota(jnp.int32, (quads, span), 1)
    live = jnp.where(lane < view_ref[0] * PP, mask_ref[...], 0).astype(F32)
    term = jnp.zeros((quads, span), F32)
    slopes = []
    for index in range(3):
        error = parts[index] - target_ref[index * quads : (index + 1) * quads, :].astype(F32)
        term = term + live * error * error
        slopes.append(2.0 * scale * live * error)
    below = 1.0 + parts[3]
    depth_out = parts[4] / below

    first, second = pair_ref[0:1, :], pair_ref[1:2, :]
    least = jnp.minimum(first, second)
    down = (jnp.abs(first - second) == P_SIZE).astype(jnp.int32)
    place = quads * PP
    slot, local = least // place, least % place
    high = down * quads + local // PP
    low = slot * PP + local % PP
    high_hot = (lax.broadcasted_iota(jnp.int32, (2 * quads, pairs), 0) == high).astype(F32).astype(BF16)
    low_hot = (lax.broadcasted_iota(jnp.int32, (span, pairs), 0) == low).astype(F32).astype(BF16)
    counts = back_mul(high_hot, low_hot)
    slope = jnp.zeros((quads, span), F32)
    for which, shift in enumerate((1, P_SIZE)):
        count = counts[which * quads : (which + 1) * quads]
        weight = DEPTH_WEIGHT * count * live * pltpu.roll(live, span - shift, 1)
        gap = depth_out - pltpu.roll(depth_out, span - shift, 1)
        term = term + weight * gap * gap
        pull = 2.0 * scale * weight * gap
        slope = slope + pull - pltpu.roll(pull, shift, 1)
    term_ref[...] = jnp.full(term_ref.shape, jnp.sum(term), F32)
    over = slope / below
    slopes += [-over * depth_out, over]
    stacked = jnp.concatenate(slopes, 0)
    dfeat[...] = lax.dot_general(
        stacked, weight_ref[...], (((1,), (1,)), ((), ())), precision=HIGHEST, preferred_element_type=F32
    )

    def feature_grad(index):
        return jnp.concatenate(
            [
                dfeat[index * quads : (index + 1) * quads, view * PP : (view + 1) * PP]
                for view in range(NVIEW)
            ],
            0,
        )

    def put(index, value):
        grad_ref[:, index * PP : (index + 1) * PP] = value.astype(BF16)

    d_foot = feature_grad(3)
    for index in range(3):
        tint = jax.nn.sigmoid(channel(index))
        upper = feature_grad(index)
        d_foot = d_foot + upper * tint
        put(index, upper * footprint * tint * (1.0 - tint))
    d_last = feature_grad(4)
    d_foot = d_foot + d_last * depth
    put(3, d_foot * extent * facing * opacity * (1.0 - opacity))
    put(4, d_last * footprint * jax.nn.sigmoid(raw))
    d_extent = d_foot * opacity * facing * extent * (1.0 - extent)
    for index in (5, 6, 7):
        put(index, d_extent)
    d_facing = d_foot * opacity * extent
    put(8, d_facing * 2.0 * lead / denom * (1.0 - facing))
    for index in (9, 10, 11):
        put(index, -2.0 * d_facing * facing / denom * channel(index))


def render(gaussians, weights, targets, mask, pairs, view_count, pair_total):
    rows = gaussians.shape[0]
    quads = rows // NVIEW
    slots, views = weights.shape[:2]
    spread = weights.transpose(1, 2, 0, 3).reshape(views * PP, slots * PP)
    wanted = targets.reshape(slots, 3, quads, PP).transpose(1, 2, 0, 3).reshape(3 * quads, slots * PP)
    valid = mask.reshape(slots, quads, PP).transpose(1, 0, 2).reshape(quads, slots * PP)
    vmem = pl.BlockSpec(memory_space=pltpu.VMEM)
    smem = pl.BlockSpec(memory_space=pltpu.SMEM)
    return pl.pallas_call(
        render_kernel,
        out_shape=[
            jax.ShapeDtypeStruct(gaussians.shape, BF16),
            jax.ShapeDtypeStruct((8, LANES), F32),
        ],
        in_specs=[vmem] * 5 + [smem] * 2,
        out_specs=[vmem] * 2,
        scratch_shapes=[pltpu.VMEM((5 * quads, views * PP), F32)] * 2,
        compiler_params=pltpu.CompilerParams(vmem_limit_bytes=48 * MIB),
        name="render",
    )(gaussians, spread, wanted, valid, pairs, view_count, pair_total)


def forward_plain(shards, patches, features, kinds):
    weights = [lax.all_gather(shard, BOTH, axis=0, tiled=True) for shard in shards]
    groups = lax.axis_size(NARROW)
    rows = patches.shape[0]
    gains = weights[0][:, features : features + kinds].T.astype(F32)
    embedded = back_mul(patches[:, :features], weights[0][:, :features])
    normed_one = layer_norm(embedded, gains[0], gains[3]).astype(BF16)
    mixed = matmul(normed_one, weights[1]).astype(BF16).reshape(rows, 3, groups, -1)
    mixed = mixed.transpose(2, 1, 0, 3)
    qkv = lax.all_to_all(mixed, NARROW, split_axis=0, concat_axis=0, tiled=True)
    width = qkv.shape[-1]
    length = groups * rows
    heads = width // HD
    parts = [qkv[:, part].reshape(length, heads, HD) for part in range(3)]
    attended, logsum = attention_forward(*parts)
    log_sums = logsum.transpose(0, 2, 1).reshape(groups, rows, heads)
    returned = lax.all_to_all(
        attended.reshape(groups, rows, width), NARROW, split_axis=0, concat_axis=0, tiled=True
    )
    returned = returned.transpose(1, 0, 2).reshape(rows, D)
    mid = embedded + matmul(returned, weights[2])
    normed_two = layer_norm(mid, gains[1], gains[4]).astype(BF16)
    expanded = matmul(normed_two, weights[3])
    half = 0.5 * (1.0 + lax.erf(expanded * (0.5**0.5)))
    activated = (expanded * half).astype(BF16)
    bell = jnp.exp(-0.5 * expanded * expanded) * 0.3989422804014327
    slopes = (half + expanded * bell).astype(BF16)
    last = mid + matmul(activated, weights[4])
    normed_three = layer_norm(last, gains[2], gains[5]).astype(BF16)
    return Bag(
        dict(
        w1=weights[1],
        w2=weights[2],
        w3=weights[3],
        w4=weights[4],
        w5=weights[5],
        gains=gains,
        embedded=embedded,
        mid=mid,
        last=last,
        slopes=slopes,
        t1=normed_one.T,
        t2=returned.T,
        t3=normed_two.T,
        hidden=activated,
        t5=normed_three.T,
        qkv=qkv,
        heads_out=attended,
        log_sums=log_sums,
        gaussians=matmul(normed_three, weights[5]),
    ).items())


def backward_plain(kept, patches, gauss_low, term, features, kinds):
    gains = kept.gains
    weights = [None, kept.w1, kept.w2, kept.w3, kept.w4, kept.w5]
    norm_back_one = jax.vjp(layer_norm, kept.embedded, gains[0], gains[3])[1]
    norm_back_two = jax.vjp(layer_norm, kept.mid, gains[1], gains[4])[1]
    norm_back_three = jax.vjp(layer_norm, kept.last, gains[2], gains[5])[1]
    qkv = kept.qkv
    groups, _, rows, width = qkv.shape
    length = groups * rows
    heads = width // HD
    queries, keys, values = (qkv[:, part].reshape(length, heads, HD) for part in range(3))
    blocked = min(512, length)
    logsum = kept.log_sums[:, :, :heads].reshape(length // blocked, blocked, heads)
    residual_grad, gain_three, shift_three = norm_back_three(back_mul(gauss_low, weights[5]))
    shrink_low = residual_grad.astype(BF16)
    expand_low = (back_mul(shrink_low, weights[4]) * kept.slopes.astype(F32)).astype(BF16)
    through_two, gain_two, shift_two = norm_back_two(back_mul(expand_low, weights[3]))
    residual_grad = residual_grad + through_two
    merge_low = residual_grad.astype(BF16)
    out_grad = back_mul(merge_low, weights[2]).astype(BF16).reshape(rows, groups, width)
    head_grad = lax.all_to_all(
        out_grad.transpose(1, 0, 2), NARROW, split_axis=0, concat_axis=0, tiled=True
    ).reshape(length, heads, HD)
    grads = attention_backward(queries, keys, values, logsum.transpose(0, 2, 1), head_grad)
    stacked = jnp.stack(grads, 1).astype(BF16).reshape(groups, rows, 3, width)
    mixed_grad = lax.all_to_all(stacked, NARROW, split_axis=0, concat_axis=0, tiled=True)
    mixed_grad = mixed_grad.transpose(1, 2, 0, 3).reshape(rows, 3 * D)
    through_one, gain_one, shift_one = norm_back_one(back_mul(mixed_grad, weights[1]))
    embed_grad = (residual_grad + through_one).astype(BF16)
    grad_norms = jnp.stack([gain_one, gain_two, gain_three, shift_one, shift_two, shift_three])
    lefts = [embed_grad.T, kept.t1, kept.t2, kept.t3, kept.hidden.T, kept.t5]
    rights = [patches, mixed_grad, merge_low, expand_low, shrink_low, gauss_low]
    products = [matmul(left, right) for left, right in zip(lefts, rights)]
    products[0] = products[0].at[:, features : features + kinds].add(grad_norms.T)
    sums = [
        lax.psum_scatter(
            product.astype(BF16), BOTH, scatter_dimension=0, tiled=True
        ).astype(F32)
        for product in products
    ]
    squares = sum(jnp.sum(part * part) for part in sums)
    loss_sum, square_sum = lax.psum((term[0, 0], squares), BOTH)
    return sums, loss_sum, square_sum


def update_kernel(features, total_ref, sums_ref, *refs):
    sources, targets, refs = refs[:27], refs[27:48], refs[48:]
    loss_ref, norm_ref, refs = refs[0], refs[1], refs[2:]
    inside, news, refs = refs[:27], refs[27:48], refs[48:]
    turned, turned_four, in_sem, out_sem = refs
    loads = [pltpu.make_async_copy(source, dest, in_sem.at[i]) for i, (source, dest) in enumerate(zip(sources, inside))]
    stores = [pltpu.make_async_copy(source, dest, out_sem.at[i]) for i, (source, dest) in enumerate(zip(news, targets))]
    for copy in loads:
        copy.start()
    grads, olds = inside[:6], inside[6:]
    square_sum = sums_ref[1:2, 0:1]
    grad_norm = jnp.sqrt(square_sum)
    factor = jnp.minimum(1.0, CLIP_NORM / (grad_norm + 1e-06))
    norm_ref[...] = grad_norm
    loss_ref[...] = sums_ref[0:1, 0:1] / total_ref[0].astype(F32)
    width = grads[0].shape[1]
    for which in range(7):
        if which < 6:
            loads[which].wait()
        if which == 0:
            turned[...] = grads[0][:, width - LANES :].T
        if which == 4:
            turned_four[...] = grads[4][...].T
        for copy in loads[6 + 3 * which : 9 + 3 * which]:
            copy.wait()
        weight, first, second = olds[3 * which : 3 * which + 3]
        rows, columns = weight.shape
        chunk = min(8, rows)

        def one(step, carry):
            spot = pl.ds(pl.multiple_of(step * chunk, chunk), chunk)
            if which == 0:
                grad = grads[0][spot, 0:columns]
            elif which == 4:
                grad = turned_four[spot, :]
            elif which == 6:
                grad = turned[features % LANES : features % LANES + rows, 0:columns]
            else:
                grad = grads[which][spot, :]
            values = adamw(weight[spot, :], first[spot, :], second[spot, :], grad * factor, RATES[which])
            for dest, value in zip(news[3 * which : 3 * which + 3], values):
                dest[spot, :] = value
            return carry

        lax.fori_loop(0, rows // chunk, one, 0)
        for copy in stores[3 * which : 3 * which + 3]:
            copy.start()
    for copy in stores:
        copy.wait()


def update_all(olds, sums, totals, pair_total, features):
    vmem = pl.BlockSpec(memory_space=pltpu.VMEM)
    smem = pl.BlockSpec(memory_space=pltpu.SMEM)
    hbm = pl.BlockSpec(memory_space=pltpu.HBM)
    shapes = [jax.ShapeDtypeStruct(old.shape, F32) for old in olds]
    inside = [pltpu.VMEM(value.shape, F32) for value in list(sums) + list(olds)]
    return pl.pallas_call(
        functools.partial(update_kernel, features),
        out_shape=shapes + [jax.ShapeDtypeStruct((1, 1), F32)] * 2,
        in_specs=[smem, vmem] + [hbm] * 27,
        out_specs=[hbm] * 21 + [vmem] * 2,
        scratch_shapes=inside
        + [pltpu.VMEM(old.shape, F32) for old in olds]
        + [
            pltpu.VMEM((LANES, sums[0].shape[0]), F32),
            pltpu.VMEM(olds[12].shape, F32),
            pltpu.SemaphoreType.DMA((27,)),
            pltpu.SemaphoreType.DMA((21,)),
        ],
        compiler_params=pltpu.CompilerParams(vmem_limit_bytes=60 * MIB),
        name="update",
    )(pair_total, totals, *sums, *olds)


def body(
    views,
    render_w,
    targets,
    pix_mask,
    pairs,
    view_count,
    pair_total,
    embed_weight,
    embed_first,
    embed_second,
    mixer_weight,
    mixer_first,
    mixer_second,
    merge_weight,
    merge_first,
    merge_second,
    expand_weight,
    expand_first,
    expand_second,
    shrink_weight,
    shrink_first,
    shrink_second,
    unpatch_weight,
    unpatch_first,
    unpatch_second,
    norm_params,
    norm_first,
    norm_second,
):
    masters = (embed_weight, mixer_weight, merge_weight, expand_weight, shrink_weight, unpatch_weight, norm_params)
    firsts = (embed_first, mixer_first, merge_first, expand_first, shrink_first, unpatch_first, norm_first)
    seconds = (embed_second, mixer_second, merge_second, expand_second, shrink_second, unpatch_second, norm_second)
    groups = lax.axis_size(NARROW)
    wide_count = lax.axis_size(WIDE)
    features = embed_weight.shape[0]
    kinds = norm_params.shape[0]
    padded = -(-(features + kinds) // LANES) * LANES
    fill = padded - features - kinds
    by_kernel = mixer_weight.shape[0] % 16 == 0 and shrink_weight.shape[0] % LANES == 0

    patches = views.reshape(-1, features)
    rows = patches.shape[0]
    patches = jnp.pad(patches, ((0, 0), (0, padded - features)))
    if by_kernel:
        raw = (embed_weight.T,) + masters[1:6]
        kept = forward_all(raw, norm_params, patches, features % LANES, wide_count, groups)
    else:
        first_shard = jnp.concatenate([embed_weight.T, norm_params.T], 1)
        first_shard = jnp.pad(first_shard.astype(BF16), ((0, 0), (0, fill)))
        shards = [first_shard] + [weight.astype(BF16) for weight in masters[1:6]]
        kept = forward_plain(shards, patches, features, kinds)
    divisor = pair_total[0].astype(F32)
    gauss_low, term = render(
        kept.gaussians, render_w[0], targets[0], pix_mask[0], pairs[0], view_count, pair_total
    )
    if by_kernel:
        *sums, totals = backward_all(
            kept, patches, gauss_low, term, features % LANES, wide_count, groups
        )
        olds = []
        for triple in zip(masters, firsts, seconds):
            olds += triple
        olds[:3] = [old.T for old in olds[:3]]
        *news, loss, grad_norm = update_all(olds, sums, totals, pair_total, features)
        news[:3] = [new.T for new in news[:3]]
        return tuple(news) + (loss[0, 0], grad_norm[0, 0])
    sums, loss_sum, square_sum = backward_plain(kept, patches, gauss_low, term, features, kinds)
    first_sum = sums[0].T
    grads = [first_sum[:features]] + list(sums[1:]) + [first_sum[features : features + kinds]]
    loss = loss_sum / divisor
    grad_norm = jnp.sqrt(square_sum)
    factor = jnp.minimum(1.0, CLIP_NORM / (grad_norm + 1e-06))
    results = []
    for which in range(7):
        results += adamw(masters[which], firsts[which], seconds[which], grads[which] * factor, RATES[which])
    return tuple(results) + (loss, grad_norm)


def solution(mesh):
    columns = P(None, BOTH)
    rows = P(BOTH, None)
    weights = (columns,) * 3 + (rows,) * 15 + (columns,) * 3
    return jax.shard_map(
        body,
        mesh=mesh,
        in_specs=(
            P(WIDE, None, NARROW, None),
            P(WIDE, None, None, None, None),
            P(WIDE, None, None, NARROW),
            P(WIDE, None, NARROW),
            P(WIDE, None, NARROW),
            P(WIDE),
            P(),
        )
        + weights,
        out_specs=weights + (P(), P()),
        check_vma=False,
    )
```

```python
import functools
import heapq

import jax
import jax.numpy as jnp
from jax import lax
from jax.experimental import pallas as pl
from jax.experimental.pallas import tpu as pltpu
from jax.sharding import PartitionSpec as P

D = 1024
HD = 64
P_SIZE = 8
PP = 64
NVIEW = 4
TMAX = 12
STEP = 10
LANES = 128
MIB = 1024 * 1024

DEPTH_WEIGHT = 1.0
CLIP_NORM = 0.01
BETA_ONE = 0.9
BETA_TWO = 0.95
ADAM_EPS = 1e-08
DECAY = 0.05
RATES = (0.05, 0.05, 0.5, 0.05, 0.05, 0.05, 0.8)
MESH = pl.DeviceIdType.MESH
WIDE, NARROW = BOTH = ("wide", "narrow")
HIGHEST = lax.Precision.HIGHEST
F32 = jnp.float32
BF16 = jnp.bfloat16


def matmul(left, right):
    return jnp.dot(left, right, preferred_element_type=F32)


def outer_sum(left, right):
    return lax.dot_general(left, right, (((0,), (0,)), ((), ())), preferred_element_type=F32)


def back_mul(grad, weight):
    return lax.dot_general(grad, weight, (((1,), (1,)), ((), ())), preferred_element_type=F32)


def layer_norm(values, gain, shift):
    centred = values - jnp.mean(values, -1, keepdims=True)
    spread = jnp.mean(centred * centred, -1, keepdims=True)
    return centred * lax.rsqrt(spread + 1e-05) * gain + shift


def exact_gelu(values):
    return jax.nn.gelu(values, approximate=False)


def attention_forward(queries, keys, values):
    length, heads = (queries.shape[0], queries.shape[1])
    blocked = min(512, length)
    scale = HD ** (-0.5)

    def one_block(query_block):
        scores = (
            jnp.einsum("qhd,khd->hqk", query_block, keys, preferred_element_type=jnp.float32)
            * scale
        )
        highest = jnp.max(scores, -1, keepdims=True)
        exponentials = jnp.exp(scores - highest)
        summed = jnp.sum(exponentials, -1, keepdims=True)
        softmaxed = (exponentials / summed).astype(jnp.bfloat16)
        output = jnp.einsum("hqk,khd->qhd", softmaxed, values, preferred_element_type=jnp.float32)
        return (output.astype(jnp.bfloat16), (highest + jnp.log(summed))[:, :, 0])

    output, logsum = lax.map(one_block, queries.reshape(length // blocked, blocked, heads, HD))
    return (output.reshape(length, heads * HD), logsum)


def attention_backward(queries, keys, values, logsum, out_grad):
    length, heads = (queries.shape[0], queries.shape[1])
    blocked = min(512, length)
    scale = HD ** (-0.5)

    def one_block(carry, inputs):
        key_grad, value_grad = carry
        query_block, logsum_block, grad_block = inputs
        scores = (
            jnp.einsum("qhd,khd->hqk", query_block, keys, preferred_element_type=jnp.float32)
            * scale
        )
        softmaxed = jnp.exp(scores - logsum_block[:, :, None])
        value_grad = value_grad + jnp.einsum(
            "hqk,qhd->khd",
            softmaxed.astype(jnp.bfloat16),
            grad_block,
            preferred_element_type=jnp.float32,
        )
        prob_grad = jnp.einsum(
            "qhd,khd->hqk", grad_block, values, preferred_element_type=jnp.float32
        )
        score_grad = softmaxed * (prob_grad - jnp.sum(softmaxed * prob_grad, -1, keepdims=True))
        score_low = score_grad.astype(jnp.bfloat16)
        query_grad = (
            jnp.einsum("hqk,khd->qhd", score_low, keys, preferred_element_type=jnp.float32) * scale
        )
        key_grad = (
            key_grad
            + jnp.einsum("hqk,qhd->khd", score_low, query_block, preferred_element_type=jnp.float32)
            * scale
        )
        return ((key_grad, value_grad), query_grad)

    zeros = jnp.zeros((length, heads, HD), jnp.float32)
    shaped = (
        queries.reshape(length // blocked, blocked, heads, HD),
        logsum,
        out_grad.reshape(length // blocked, blocked, heads, HD),
    )
    (key_grad, value_grad), query_grad = lax.scan(one_block, (zeros, zeros), shaped)
    return (query_grad.reshape(length, heads, HD), key_grad, value_grad)


def adamw(weight, first, second, grad, rate):
    first = BETA_ONE * first + (1.0 - BETA_ONE) * grad
    second = BETA_TWO * second + (1.0 - BETA_TWO) * grad * grad
    first_hat = first / (1.0 - BETA_ONE**STEP)
    second_hat = second / (1.0 - BETA_TWO**STEP)
    weight = weight - rate * (first_hat / (jnp.sqrt(second_hat) + ADAM_EPS) + DECAY * weight)
    return (weight, first, second)


def chip_bits(chips):
    bits, step = [], 1
    while step < chips:
        bits.append(step)
        step *= 2
    return bits


def flip(chip, mask):
    for bit in chip_bits(mask + 1):
        if mask & bit:
            chip = chip + (1 - 2 * (chip // bit % 2)) * bit
    return chip


def column_halves(width):
    first = -(-width // (2 * LANES)) * LANES
    return ((0, first), (first, width - first))


def work_items(widths, order):
    return [(which,) + half + (side,) for which in order for side, half in enumerate(column_halves(widths[which]))]


class Bag:
    def __init__(self, pairs):
        vars(self).update(pairs)


class Place:
    def __init__(self, wide, narrow):
        self.wide, self.narrow = wide, narrow
        self.chips = wide // 2
        self.bits = chip_bits(self.chips)
        self.w = lax.axis_index(WIDE)
        self.n = lax.axis_index(NARROW)
        self.chip = self.w // 2
        self.core = self.w % 2
        self.twin = (2 * self.chip + 1 - self.core, self.n)

    def across(self, mask):
        return (2 * flip(self.chip, mask) + self.core, self.n)

    def along(self, step):
        return (self.w, lax.rem(self.n + step, self.narrow))

    def neighbours(self):
        return (
            [self.twin]
            + [self.across(bit) for bit in self.bits]
            + [self.along(step) for step in range(1, self.narrow)]
        )


class Planner:
    def __init__(self):
        self.now, self.count = 0.0, 0
        self.free, self.events, self.done, self.spare = {}, [], set(), []
        self.refill = lambda: None

    def transfer(self, link, cost, key, event):
        self.free[link] = max(self.now, self.free.get(link, 0.0)) + cost
        self.count += 1
        heapq.heappush(self.events, (self.free[link] + 2.0, self.count, key, event))

    def step(self):
        when, _, key, event = heapq.heappop(self.events)
        self.now = max(self.now, when) + 0.2
        event()
        self.done.add(key)
        self.refill()

    def fill(self, until):
        for index, (keys, cost, work) in enumerate(self.spare):
            if self.now + cost <= until and self.done.issuperset(keys):
                del self.spare[index]
                work()
                self.now += cost
                return True
        return False

    def need(self, keys):
        while not self.done.issuperset(keys):
            if not self.fill(self.events[0][0]):
                self.step()

    def work(self, cost, work):
        while self.events and self.events[0][0] <= self.now:
            self.step()
        self.refill()
        work()
        self.now += cost

    def later(self, cost, work, keys=()):
        entry = (tuple(keys), cost, work)
        self.spare.append(entry)
        return entry

    def force(self, entry):
        if entry in self.spare:
            self.spare.remove(entry)
            self.work(entry[1], entry[2])

    def finish(self):
        self.refill()
        while self.events or self.spare:
            if not self.fill(self.events[0][0] if self.events else 1e9):
                self.step()


LINK = 90e3
Z_AHEAD = 4.0
RELAYED = (3, 4)
KEY_ROWS = 512
Z_EARLY = 1.0
Z_LATE = 2.0
TWIN_LINK = 600e3


def greet(peers):
    barrier = pltpu.get_barrier_semaphore()
    for peer in peers:
        pl.semaphore_signal(barrier, inc=1, device_id=peer, device_id_type=MESH)
    pl.semaphore_wait(barrier, len(peers))


def normalize(values, gain, shift):
    centred = values - jnp.mean(values, -1, keepdims=True)
    spread = jnp.mean(centred * centred, -1, keepdims=True)
    return centred * lax.rsqrt(spread + 1e-05) * gain + shift


def forward_plan(widths):
    items = []
    for which, cuts in ((0, 1), (1, 3), (2, 1), (3, 2), (5, 1), (4, 2)):
        size = widths[which] // cuts
        for cut in range(cuts):
            for side, (start, width) in enumerate(column_halves(size)):
                items.append((which, cut * size + start, width, side))
    return items


def forward_kernel(items, wide, narrow, lead, ins, outs, scratch, *refs):
    at = Bag(zip(ins + scratch, refs[: len(ins)] + refs[len(ins) + len(outs) :]))
    results = refs[len(ins) : len(ins) + len(outs)]
    weights = [at.first_weight, at.w1, at.w2, at.w3, at.w4, at.w5]
    shards = [at.c0, at.c1, at.c2, at.c3, at.c4, at.c5]
    raw = [at.s0, at.s1, at.s2, at.s3, at.s4, at.s5]
    own_sem, send_sem, recv_sem = at.own_sem, at.send_sem, at.recv_sem
    swap_send, swap_recv, out_sem = at.swap_send, at.swap_recv, at.out_sem
    place = Place(wide, narrow)
    chips, me = place.chips, place.n
    tokens = at.patches.shape[0]
    head_width = D // narrow
    total = len(items)
    started, guarded = [], []

    def start(copy):
        copy.start()
        started.append(copy)

    features = at.s0.shape[1]
    tail = shards[0].shape[1] - LANES
    kinds = at.norm_raw.shape[0]
    kind = lax.broadcasted_iota(jnp.int32, (kinds, LANES), 0)
    spot = lax.broadcasted_iota(jnp.int32, (kinds, LANES), 1)
    put = (spot == kind + lead).astype(F32).astype(BF16)
    shards[0][:, tail:] = outer_sum(at.norm_raw[...].astype(BF16), put).astype(BF16)
    shards[0][:, 0:features] = at.s0[...].astype(BF16)
    for source, dest in zip(raw[1:], shards[1:]):
        dest[...] = source[...].astype(BF16)
    greet(place.neighbours())
    rows_of = [shard.shape[0] for shard in shards]

    def slab(which, node):
        rows = rows_of[which]
        return pl.ds(pl.multiple_of(node * rows, rows), rows)

    def whole_of(which, columns):
        part = weights[which][:, :, :, columns]
        return part.reshape(-1, part.shape[-1])

    own = []
    for which in range(6):
        copy = pltpu.make_async_copy(
            shards[which], weights[which].at[place.chip, place.core, slab(which, me), :], own_sem.at[which]
        )
        copy.start()
        own.append(copy)

    def remote(item, src, dst, slot, peer):
        return pltpu.make_async_remote_copy(
            src_ref=src,
            dst_ref=dst,
            send_sem=send_sem.at[item, slot],
            recv_sem=recv_sem.at[item, slot],
            device_id=peer,
            device_id_type=MESH,
        )

    def group(item, mask):
        which, begin, width, _ = items[item]
        return weights[which].at[flip(place.chip, mask), place.core, :, pl.ds(begin, width)]

    def along(item, sign, hop):
        which, begin, width, _ = items[item]
        columns = pl.ds(begin, width)
        there = weights[which].at[place.chip, place.core, slab(which, me - sign * (hop - 1)), columns]
        return remote(
            item,
            shards[which].at[:, columns] if hop == 1 else there,
            there,
            chips + 1 + hop - 1 + (narrow - 1 if sign < 0 else 0),
            (place.w, me + sign),
        )

    def has_next(sign):
        return me < narrow - 1 if sign > 0 else me >= 1

    def has_come(sign, hop):
        return me >= hop if sign > 0 else me < narrow - hop

    def start_if(condition, copy):
        @pl.when(condition)
        def _():
            copy.start()

        guarded.append((condition, copy))

    def bits_of(item):
        return place.bits if items[item][3] == 0 else place.bits[::-1]

    def across(item, mask, bit):
        return remote(item, group(item, mask), group(item, mask), mask ^ bit, place.across(bit))

    def to_twin(item):
        which, begin, width, _ = items[item]
        there = weights[which].at[:, place.core, :, pl.ds(begin, width)]
        return remote(item, there, there, chips, place.twin)

    plan = Planner()
    waited = set()

    def block_bytes(item):
        which, _, width, _ = items[item]
        return 2 * narrow * rows_of[which] * width

    def twin_event(item):
        to_twin(item).wait_recv()

    here = {}

    def onward(item, mask, number):
        bits = bits_of(item)
        size = block_bytes(item)
        for later in range(number, len(bits)):
            start(across(item, mask, bits[later]))
            coming = mask ^ bits[later]
            plan.transfer(
                bits[later], 2 * size / LINK, (item, coming), functools.partial(arrive, item, coming, later)
            )
        here[item] = here.get(item, 0) + 1
        if here[item] == chips:
            start(to_twin(item))
            plan.transfer(-1, chips * size / TWIN_LINK, (item, chips), functools.partial(twin_event, item))

    def arrive(item, mask, number):
        across(item, mask ^ bits_of(item)[number], bits_of(item)[number]).wait_recv()
        onward(item, mask, number + 1)

    def begin_item(item):
        for sign in (1, -1):
            start_if(has_next(sign), along(item, sign, 1))
        line_transfer(item, 1)

    def line_transfer(item, hop):
        cost = 2 * block_bytes(item) / narrow / LINK
        key = (item, 0) if hop == narrow - 1 else (item, -hop)
        plan.transfer(0, cost, key, functools.partial(line_event, item, hop))

    def line_event(item, hop):
        if items[item][0] not in waited:
            waited.add(items[item][0])
            own[items[item][0]].wait()
        for sign in (1, -1):

            @pl.when(has_come(sign, hop))
            def _():
                along(item, sign, hop).wait_recv()

            if hop < narrow - 1:
                start_if(jnp.logical_and(has_come(sign, hop), has_next(sign)), along(item, sign, hop + 1))
        if hop < narrow - 1:
            line_transfer(item, hop + 1)
        else:
            onward(item, 0, 0)

    begun, ahead = [], [Z_EARLY]

    def refill():
        while len(begun) < total and plan.free.get(0, 0.0) < plan.now + ahead[-1]:
            begin_item(len(begun))
            begun.append(True)

    plan.refill = refill
    refill()

    def need(which, columns=None):
        plan.need(
            [
                (index, key)
                for index, (owner, begin, width, _) in enumerate(items)
                if owner == which and (columns is None or (begin < columns[1] and begin + width > columns[0]))
                for key in range(chips + 1)
            ]
        )

    flushed = []

    def flush(ref):
        index = [vars(at)[name] is ref for name in outs].index(True)
        copy = pltpu.make_async_copy(ref, results[index], out_sem.at[index])
        copy.start()
        flushed.append(copy)

    def swap(src, dst, kind, step):
        return pltpu.make_async_remote_copy(
            src_ref=src,
            dst_ref=dst,
            send_sem=swap_send.at[kind, step],
            recv_sem=swap_recv.at[kind, step],
            device_id=place.along(step),
            device_id_type=MESH,
        )

    gains = at.gains
    embedded, mid, last = at.embedded, at.mid, at.last
    normed, hidden, wave = at.normed, at.hidden, at.wave
    away, qkv, heads_out, returned = at.away, at.qkv, at.heads_out, at.returned

    def turn(dest, source):
        dest[...] = source[...].T
        flush(dest)

    need(0)
    width = weights[0].shape[-1]
    kind = lax.broadcasted_iota(jnp.int32, (8, LANES), 0)
    spot = lax.broadcasted_iota(jnp.int32, (8, LANES), 1)
    pick = (spot == kind + lead).astype(F32).astype(BF16)
    gains[...] = back_mul(pick, whole_of(0, pl.ds(width - LANES, LANES)))
    flush(gains)

    def embed(block):
        cols = pl.ds(block, 256)
        rows = whole_of(0, pl.ds(0, width))[block : block + 256]
        embedded[:, cols] = back_mul(at.patches[...], rows)

    for block in range(0, D, 256):
        plan.work(0.5, functools.partial(embed, block))
    flush(embedded)

    def norm_rows(source, row, dest):
        step_rows = 32

        def one(step, carry):
            rows = pl.ds(pl.multiple_of(step * step_rows, step_rows), step_rows)
            dest[rows, :] = normalize(
                source[rows, :], gains[row : row + 1, :], gains[row + 3 : row + 4, :]
            ).astype(BF16)
            return carry

        lax.fori_loop(0, tokens // step_rows, one, 0)

    plan.work(2.0, lambda: norm_rows(embedded, 0, normed))
    turn_first = plan.later(2.0, lambda: turn(at.t1, normed))
    piece = 2 * (narrow - 1) * 2 * tokens * head_width / LINK

    def project(part, step):
        owner = lax.rem(me + step, narrow)
        offset = pl.multiple_of(part * D + owner * head_width, LANES)
        value = matmul(normed[...], whole_of(1, pl.ds(offset, head_width))).astype(BF16)
        if step:
            away[step - 1, part] = value
            start(swap(away.at[step - 1, part], qkv.at[me, part], part, step))
        else:
            qkv[me, part] = value

    def swap_event(part):
        for step in range(1, narrow):
            swap(away.at[step - 1, part], qkv.at[me, part], part, step).wait_recv()

    for part in range(3):
        need(1, (part * D, part * D + D))
        for step in list(range(1, narrow)) + [0]:
            plan.work(0.7, functools.partial(project, part, step))
        plan.transfer(0, piece, (-1, part), functools.partial(swap_event, part))
    flush(at.w1)
    lane = lax.broadcasted_iota(jnp.int32, (1, LANES), 1)
    scale = HD ** (-0.5)
    length = narrow * tokens
    sides = LANES // HD

    def weigh(step):
        who = lax.rem(me + step, narrow)
        log_sums = jnp.zeros((tokens, LANES), F32)
        sums = jnp.ones((tokens, LANES), F32)
        for pair in range(head_width // LANES):
            lanes = pl.ds(pair * LANES, LANES)
            query = qkv[who, 0, :, lanes].astype(F32)
            key = qkv[:, 1, :, lanes].reshape(length, LANES)
            for side in range(sides):
                head = pair * sides + side
                own_query = (query * jnp.where(lane // HD == side, scale, 0.0)).astype(BF16)
                scores = back_mul(own_query, key)
                highest = jnp.max(scores, -1, keepdims=True)
                exponentials = jnp.exp(scores - highest)
                summed = jnp.sum(exponentials, -1, keepdims=True)
                at.weighed[step, head] = exponentials.astype(BF16)
                log_sums = jnp.where(lane == head, highest + jnp.log(summed), log_sums)
                sums = jnp.where(lane == head, summed, sums)
        at.log_sums[who] = log_sums
        at.weigh_sums[step] = sums

    def attend(step):
        who = lax.rem(me + step, narrow)
        for pair in range(head_width // LANES):
            lanes = pl.ds(pair * LANES, LANES)
            value = qkv[:, 2, :, lanes].reshape(length, LANES)
            out = jnp.zeros((tokens, LANES), F32)
            for side in range(sides):
                head = pair * sides + side
                part = matmul(at.weighed[step, head], value) / at.weigh_sums[step, :, head : head + 1]
                out = jnp.where(lane // HD == side, part, out)
            heads_out[who, :, lanes] = out.astype(BF16)
        if step:
            start(swap(heads_out.at[who], returned.at[me], 3, step))
        else:
            returned[me] = heads_out[who]

    steps = list(range(1, narrow)) + [0]
    ahead.append(Z_LATE)
    plan.need([(-1, 0), (-1, 1)])
    for step in steps:
        plan.work(2.7, functools.partial(weigh, step))
    plan.need([(-1, 2)])
    flush(qkv)

    def return_event(step):
        return lambda: swap(heads_out.at[me], returned.at[me], 3, step).wait_recv()

    for step in steps:
        plan.work(0.9, functools.partial(attend, step))
        if step:
            plan.transfer(0, piece / (narrow - 1), (-2, step), return_event(step))
    flush(heads_out)
    flush(at.log_sums)
    need(2)
    plan.need([(-2, step) for step in range(1, narrow)])

    def merge(block):
        cols = pl.ds(block, 256)
        value = embedded[:, cols]
        weight = whole_of(2, cols)
        for source in range(narrow):
            value = value + matmul(returned[source], weight[source * head_width : (source + 1) * head_width])
        mid[:, cols] = value

    for block in range(0, D, 256):
        plan.work(0.7, functools.partial(merge, block))
    flush(at.w2)
    flush(mid)
    plan.force(turn_first)
    plan.work(2.0, lambda: norm_rows(mid, 1, normed))

    def turn_returned():
        for source in range(narrow):
            at.t2[pl.ds(source * head_width, head_width), :] = returned[source].T
        flush(at.t2)

    plan.later(2.0, turn_returned)
    turn_second = plan.later(2.0, lambda: turn(at.t3, normed))

    ff = weights[3].shape[-1]
    tile = wave.shape[1]
    slopes = at.slopes

    def expand(block):
        wave[...] = matmul(normed[...], whole_of(3, pl.ds(block, tile)))

        def bend(step, carry):
            rows = pl.ds(pl.multiple_of(step * 32, 32), 32)
            x = wave[rows, :]
            half = 0.5 * (1.0 + lax.erf(x * (0.5**0.5)))
            hidden[rows, pl.ds(block, tile)] = (x * half).astype(BF16)
            bell = jnp.exp(-0.5 * x * x) * 0.3989422804014327
            slopes[rows, pl.ds(block, tile)] = (half + x * bell).astype(BF16)
            return carry

        lax.fori_loop(0, tokens // 32, bend, 0)

    for block in range(0, ff, tile):
        need(3, (block, block + tile))
        plan.work(2.5, functools.partial(expand, block))
    flush(at.w3)
    flush(slopes)
    flush(hidden)

    def shrink(block):
        cols = pl.ds(block, 256)
        last[:, cols] = mid[:, cols] + matmul(hidden[...], whole_of(4, cols))

    for block in range(0, D, 256):
        need(4, (block, block + 256))
        plan.work(1.0, functools.partial(shrink, block))
    flush(at.w4)
    flush(last)
    plan.force(turn_second)
    plan.work(2.0, lambda: norm_rows(last, 2, normed))
    need(5)

    def unpatch(block):
        cols = pl.ds(block, 256)
        at.gaussians[:, cols] = matmul(normed[...], whole_of(5, cols))

    for block in range(0, weights[5].shape[-1], 256):
        plan.work(0.7, functools.partial(unpatch, block))
    flush(at.w5)
    flush(at.gaussians)
    plan.later(2.0, lambda: turn(at.t5, normed))
    plan.finish()
    for copy in started:
        copy.wait_send()
    for condition, copy in guarded:

        @pl.when(condition)
        def _():
            copy.wait_send()

    for copy in flushed:
        copy.wait()


def forward_all(shards, norms, patches, lead, wide, narrow):
    tokens = patches.shape[0]
    widths = [patches.shape[1]] + [shard.shape[1] for shard in shards[1:]]
    heights = [shard.shape[0] * wide * narrow for shard in shards]
    ff = widths[3]
    chips = wide // 2
    head_width = D // narrow
    items = forward_plan(widths)
    slots = chips + 1 + 2 * (narrow - 1)
    full = [((chips, 2, height // wide, width), BF16) for height, width in zip(heights, widths)]
    shapes = dict(
        w1=full[1],
        w2=full[2],
        w3=full[3],
        w4=full[4],
        w5=full[5],
        gains=((8, D), F32),
        embedded=((tokens, D), F32),
        mid=((tokens, D), F32),
        last=((tokens, D), F32),
        slopes=((tokens, ff), BF16),
        t1=((D, tokens), BF16),
        t2=((D, tokens), BF16),
        t3=((D, tokens), BF16),
        hidden=((tokens, ff), BF16),
        t5=((D, tokens), BF16),
        qkv=((narrow, 3, tokens, head_width), BF16),
        heads_out=((narrow, tokens, head_width), BF16),
        log_sums=((narrow, tokens, LANES), F32),
        gaussians=((tokens, widths[5]), F32),
    )
    ins = tuple(dict(s0=0, s1=0, s2=0, s3=0, s4=0, s5=0, norm_raw=0, patches=0))
    outs = tuple(shapes)
    extras = dict(
        first_weight=pltpu.VMEM(*full[0]),
        c0=pltpu.VMEM((shards[0].shape[0], widths[0]), BF16),
        c1=pltpu.VMEM(shards[1].shape, BF16),
        c2=pltpu.VMEM(shards[2].shape, BF16),
        c3=pltpu.VMEM(shards[3].shape, BF16),
        c4=pltpu.VMEM(shards[4].shape, BF16),
        c5=pltpu.VMEM(shards[5].shape, BF16),
        normed=pltpu.VMEM((tokens, D), BF16),
        wave=pltpu.VMEM((tokens, 512), F32),
        away=pltpu.VMEM((narrow - 1, 3, tokens, head_width), BF16),
        weighed=pltpu.VMEM((narrow, head_width // HD, tokens, narrow * tokens), BF16),
        weigh_sums=pltpu.VMEM((narrow, tokens, LANES), F32),
        returned=pltpu.VMEM((narrow, tokens, head_width), BF16),
        own_sem=pltpu.SemaphoreType.DMA((6,)),
        send_sem=pltpu.SemaphoreType.DMA((len(items), slots)),
        recv_sem=pltpu.SemaphoreType.DMA((len(items), slots)),
        swap_send=pltpu.SemaphoreType.DMA((4, narrow)),
        swap_recv=pltpu.SemaphoreType.DMA((4, narrow)),
        out_sem=pltpu.SemaphoreType.DMA((len(outs),)),
    )
    scratch = outs + tuple(extras)
    anywhere = pl.BlockSpec(memory_space=pl.ANY)
    results = pl.pallas_call(
        functools.partial(forward_kernel, items, wide, narrow, lead, ins, outs, scratch),
        out_shape=[jax.ShapeDtypeStruct(*shapes[name]) for name in outs],
        in_specs=[pl.BlockSpec(memory_space=pltpu.VMEM)] * len(ins),
        out_specs=[anywhere] * len(outs),
        scratch_shapes=[pltpu.VMEM(*shapes[name]) for name in outs] + list(extras.values()),
        compiler_params=pltpu.CompilerParams(
            collective_id=0, has_side_effects=True, vmem_limit_bytes=60 * MIB
        ),
        name="forward",
    )(*shards, norms, patches)
    results = [result.reshape(-1, result.shape[-1]) for result in results[:5]] + list(results[5:])
    return Bag(zip(outs, results))


def backward_plan(widths, pairs):
    items = []
    for which, cuts in ((5, 1), (4, 2), (3, 2), (2, 1), (1, pairs), (0, 1)):
        size = widths[which] // cuts
        for cut in range(cuts):
            for side, (start, width) in enumerate(column_halves(size)):
                items.append((which, cut * size + start, width, side))
    return items


def tile_of(width):
    for tile in (512, 384, 256, 128):
        if width % tile == 0:
            return tile
    return width


def backward_kernel(items, wide, narrow, lead, ins, scratch, *refs):
    src = Bag(zip(ins, refs))
    refs = refs[len(ins) :]
    sums, totals, refs = refs[:6], refs[6], list(refs[7:])
    at = Bag(zip(scratch, refs))
    place = Place(wide, narrow)
    chips, me = place.chips, place.n
    total = len(items)
    refs = refs[len(scratch) :]
    held = [refs.pop(0) for _ in items]
    passed = [[refs.pop(0) for _ in place.bits] for _ in items]
    final = [refs.pop(0) for _ in items]
    spare = [refs.pop(0) for _ in range(6)]
    tokens = src.patches.shape[0]
    head_width = D // narrow
    length = narrow * tokens
    reach = narrow * LANES
    send_sem, recv_sem, tile_send, tile_recv = at.send_sem, at.recv_sem, at.tile_send, at.tile_recv
    swap_send, swap_recv, in_sem, ring_sem = at.swap_send, at.swap_recv, at.in_sem, at.ring_sem
    gains, norms, extra = src.gains, at.norms, at.extra
    stash, d_res, d_norm = at.stash, at.d_res, at.d_norm
    mixed, merge_low, expand_low, shrink_low = at.mixed, at.merge_low, at.expand_low, at.shrink_low

    loaded = [name for name in ins if name in scratch]

    def load(ref):
        index = [vars(at)[name] is ref for name in loaded].index(True)
        return pltpu.make_async_copy(vars(src)[loaded[index]], ref, in_sem.at[index])

    def load_stash(ref):
        return pltpu.make_async_copy(ref, stash, in_sem.at[len(loaded)])

    def ring(ref, slots, rows, columns, index, row):
        slot = lax.rem(index, slots.shape[0])
        return pltpu.make_async_copy(
            ref.at[pl.ds(pl.multiple_of(row, rows), rows), :],
            slots.at[slot, pl.ds(0, rows), pl.ds(0, columns)],
            ring_sem.at[0 if slots is at.tall else 1, slot],
        )

    slope_rows = at.tall.shape[1]
    tall, long = at.tall.shape[0], at.long.shape[0]

    def slope_load(index):
        slot = lax.rem(index, tall)
        return pltpu.make_async_copy(
            src.slopes.at[:, pl.ds(pl.multiple_of(index * slope_rows, slope_rows), slope_rows)],
            at.slope_slots.at[slot],
            ring_sem.at[2, slot],
        )

    u_rows, u_cols = 256, src.w5.shape[1]
    load_stash(src.last).start()
    for index in range(tall):
        ring(src.w5, at.tall, u_rows, u_cols, index, index * u_rows).start()
        slope_load(index).start()
    wide_rows = at.long.shape[1]
    for index in range(long):
        ring(src.w3, at.long, wide_rows, src.w3.shape[1], index, index * wide_rows).start()
    for name in loaded:
        load(vars(at)[name]).start()

    peers = [(lax.rem(place.w + step, wide), place.n) for step in range(1, wide)]
    peers += [place.along(step) for step in range(1, narrow)]
    greet(peers)

    started, guarded = [], []

    def start(copy):
        copy.start()
        started.append(copy)

    lefts = [at.embed_t, at.t1, at.t2, at.t3, at.shrink_t, at.t5]
    rights = [src.patches, mixed, merge_low, expand_low, at.hidden, src.gauss]

    def remote(item, src, dst, slot, peer):
        return pltpu.make_async_remote_copy(
            src_ref=src,
            dst_ref=dst,
            send_sem=send_sem.at[item, slot],
            recv_sem=recv_sem.at[item, slot],
            device_id=peer,
            device_id_type=MESH,
        )

    def bits_of(item):
        return place.bits[::-1] if items[item][3] == 0 else place.bits

    def groups_of(item):
        size = max(1, 512 // (narrow * spare[items[item][0]].shape[2]))
        if items[item][0] == 4:
            size = chips
        masks = list(range(chips))
        if bits_of(item) and bits_of(item)[0] > 1:
            masks = masks[chips // 2 :] + masks[: chips // 2]
        return [sorted(masks[at_mask : at_mask + size]) for at_mask in range(0, chips, size)]

    def product(item, masks, core, into, plus):
        which, begin, width, _ = items[item]
        left, right = lefts[which], rights[which]
        rows = into.shape[-2]
        span = narrow * rows
        tile = tile_of(width)
        if which == 4:
            size = into.shape[-1]
            for mask in masks:
                column = ((flip(place.chip, mask) * 2 + core) * narrow) * size
                rhs = right[:, pl.ds(pl.multiple_of(column, narrow * size), narrow * size)]
                value = jnp.dot(left[begin : begin + width, :], rhs, preferred_element_type=F32)
                for node in range(narrow):
                    piece = value[:, node * size : (node + 1) * size]
                    if plus:
                        piece = piece + into[mask, node].astype(F32)
                    into[mask, node] = piece.astype(BF16)
            return
        firsts = [((flip(place.chip, mask) * 2 + core) * narrow) * rows for mask in masks]
        with_extra = which == 0 and begin + width == right.shape[1]
        assert not with_extra or tile == width
        if which == 1:
            tile = LANES * 2

        def one(step, carry):
            offset = pl.multiple_of(begin + step * tile, LANES)
            local = pl.multiple_of(step * tile, LANES)
            if which != 1:
                rhs = right[:, pl.ds(offset, tile)]
            else:
                part, inside = offset // reach, pl.multiple_of(offset % reach, LANES)
                rhs = right[part // 3, part % 3, :, pl.ds(inside, tile)]
            spots = [pl.ds(pl.multiple_of(first, span), span) for first in firsts]
            lhs = jnp.concatenate([left[spot, :] for spot in spots], 0)
            value = jnp.dot(lhs, rhs, preferred_element_type=F32)
            for index, mask in enumerate(masks):
                piece = value[index * span : (index + 1) * span]
                if with_extra:
                    blank = jnp.zeros((span, tile - LANES), F32)
                    piece = piece + jnp.concatenate([blank, extra[spots[index], :]], 1)
                piece = piece.reshape(narrow, rows, tile)
                if plus:
                    piece = piece + into[mask, :, :, pl.ds(local, tile)].astype(F32)
                into[mask, :, :, pl.ds(local, tile)] = piece.astype(BF16)
            return carry

        lax.fori_loop(0, width // tile, one, 0)

    last_sent = {}
    plan = Planner()

    def to_twin(item, masks):
        which, _, width, _ = items[item]
        some = pl.ds(masks[0], len(masks))
        own = spare[which].at[some] if which == 4 else spare[which].at[some, :, :, pl.ds(0, width)]
        return remote(item, own, held[item].at[some], masks[0], place.twin)

    def across(item, mask, bit, number, slot):
        return remote(
            item, held[item].at[mask], passed[item][number].at[slot], chips + mask, place.across(bit)
        )

    def relayed(item):
        return items[item][0] in RELAYED

    def hopping(item, sign, hop):
        count = narrow - hop
        first = hop if sign > 0 else 0
        node = hop if sign > 0 else narrow - 1 - hop
        return remote(
            item,
            held[item].at[0, pl.ds(first, count)],
            final[item].at[pl.ds(first + (1 if sign > 0 else 0), count)],
            2 * chips + (0 if sign > 0 else 1),
            (place.w, node),
        )

    def send_hop(item, sign, hop):
        sender = me == (hop - 1 if sign > 0 else narrow - hop)

        @pl.when(sender)
        def _():
            hopping(item, sign, hop).start()

        guarded.append((sender, hopping(item, sign, hop)))

    def hop_event(item, hop):
        count = narrow - hop - 1
        for sign in (1, -1):
            first = hop + 1 if sign > 0 else 0
            shift = 1 if sign > 0 else 0

            @pl.when(me == (hop if sign > 0 else narrow - 1 - hop))
            def _():
                hopping(item, sign, hop).wait_recv()
                if count:
                    mine, theirs = pl.ds(first, count), pl.ds(first + shift, count)
                    value = held[item][0, mine].astype(F32) + final[item][theirs].astype(F32)
                    held[item][0, mine] = value.astype(BF16)

            if count:
                send_hop(item, sign, hop + 1)
        if count:
            hop_transfer(item, hop + 1)
        else:
            finish(item)

    def hop_transfer(item, hop):
        cost = (narrow - hop) * 2 * block_bytes(item) / narrow / LINK
        event = functools.partial(hop_event, item, hop)
        plan.transfer(0 if hop == 1 else 100 + hop, cost, (item, -hop, 0), event)

    def along(item, step):
        target = place.along(step)
        return remote(
            item,
            held[item].at[0, target[1]],
            final[item].at[narrow - step - 1],
            2 * chips + narrow - step - 1,
            target,
        )

    def leaves(item, mask):
        bits = bits_of(item)
        return min([number for number, bit in enumerate(bits) if mask & bit], default=len(bits))

    def slot_of(item, mask, number):
        bits = bits_of(item)
        kept = [m for m in range(chips) if not any(m & bit for bit in bits[: number + 1])]
        return kept.index(mask)

    def add_into(dest, dest_at, src, src_at):
        dest[dest_at] = (dest[dest_at].astype(F32) + src[src_at].astype(F32)).astype(BF16)

    def block_bytes(item):
        _, nodes, rows, width = held[item].shape
        return 2 * nodes * rows * width

    def push(which, pair=None):
        for item, (owner, begin, _, _) in enumerate(items):
            if owner != which or (pair is not None and begin // (3 * reach) != pair):
                continue
            for masks in groups_of(item):
                cost = len(masks) * block_bytes(item) / 1e6
                plan.work(cost, functools.partial(push_some, item, masks))

    def push_some(item, masks):
        which = items[item][0]
        for key in [key for key in last_sent if key[0] == which and set(key[1]) & set(masks)]:
            last_sent.pop(key).wait_send()
        product(item, masks, 1 - place.core, spare[which], False)
        copy = to_twin(item, masks)
        copy.start()
        last_sent[which, tuple(masks)] = copy
        cost = len(masks) * block_bytes(item) / TWIN_LINK
        plan.transfer(-1, cost, (item, 0, masks[0]), functools.partial(own_event, item, masks))

    def own_event(item, masks):
        to_twin(item, masks).wait_recv()
        product(item, masks, place.core, held[item], True)
        plan.now += len(masks) * block_bytes(item) / 1e6
        plan.done.update((item, 0, mask) for mask in masks)
        for mask in masks:
            onward(item, mask, 0)

    def onward(item, mask, number):
        bits = bits_of(item)
        if number == len(bits):
            lined.append(item)
            refill()
        elif leaves(item, mask) == number:
            kept = mask ^ bits[number]
            start(across(item, mask, bits[number], number, slot_of(item, kept, number)))
            plan.transfer(
                bits[number],
                2 * block_bytes(item) / LINK,
                (item, 1 + number, kept),
                functools.partial(sum_event, item, kept, number),
            )

    lined = []

    def refill():
        while lined and plan.free.get(0, 0.0) < plan.now + Z_AHEAD:
            item = lined.pop(0)
            if relayed(item):
                for sign in (1, -1):
                    send_hop(item, sign, 1)
                hop_transfer(item, 1)
                continue
            for step in range(1, narrow):
                start(along(item, step))
            cost = 2 * (narrow // 2) ** 2 * block_bytes(item) / narrow / LINK
            plan.transfer(0, cost, (item, -1, 0), functools.partial(finish, item))

    plan.refill = refill

    def sum_event(item, mask, number):
        plan.need([(item, before, mask) for before in range(number + 1)])
        bit = bits_of(item)[number]
        slot = slot_of(item, mask, number)
        across(item, mask ^ bit, bit, number, slot).wait_recv()
        add_into(held[item], mask, passed[item][number], slot)
        plan.now += block_bytes(item) / 8e5
        onward(item, mask, number + 1)

    at.squares[...] = jnp.zeros_like(at.squares)

    def finish(item):
        which, begin, width, _ = items[item]
        value = held[item][0, me].astype(F32)
        if relayed(item):
            value = value + jnp.where(me >= 1, final[item][me + 1].astype(F32), 0.0)
            value = value + jnp.where(me < narrow - 1, final[item][me].astype(F32), 0.0)
        else:
            for step in range(1, narrow):
                along(item, step).wait_recv()
            for slot in range(narrow - 1):
                value = value + final[item][slot].astype(F32)
        columns = pl.ds(0, value.shape[1])
        at.squares[:, columns] += jnp.sum(value * value, 0, keepdims=True)
        if which == 1:
            for shift in range(0, width, LANES):
                part, spot = (begin + shift) // reach, (begin + shift) % reach
                column = part % 3 * D + spot // LANES * head_width + part // 3 * LANES
                sums[which][:, pl.ds(column, LANES)] = value[:, shift : shift + LANES]
        elif which == 4:
            sums[which][pl.ds(begin, width), :] = value
        else:
            sums[which][:, pl.ds(begin, width)] = value

    norms[...] = jnp.zeros_like(norms)

    def norm_back(row, low, add):
        step_rows = 32

        def one(step, carry):
            rows = pl.ds(pl.multiple_of(step * step_rows, step_rows), step_rows)
            values = stash[rows, :]
            upper = d_norm[rows, :]
            centred = values - jnp.mean(values, -1, keepdims=True)
            rate = lax.rsqrt(jnp.mean(centred * centred, -1, keepdims=True) + 1e-05)
            unit = centred * rate
            norms[row : row + 1, :] += jnp.sum(upper * unit, 0, keepdims=True)
            norms[row + 3 : row + 4, :] += jnp.sum(upper, 0, keepdims=True)
            scaled = upper * gains[row : row + 1, :]
            inner = scaled - jnp.mean(scaled, -1, keepdims=True)
            inner = rate * (inner - unit * jnp.mean(scaled * unit, -1, keepdims=True))
            if add:
                inner = inner + d_res[rows, :]
            d_res[rows, :] = inner
            low[rows, :] = inner.astype(BF16)
            return carry

        lax.fori_loop(0, tokens // step_rows, one, 0)

    def loop_work(cost, count, pieces, body):
        for piece in range(pieces):
            low, high = count * piece // pieces, count * (piece + 1) // pieces
            plan.work(cost / pieces, functools.partial(lax.fori_loop, low, high, body, 0))

    load(at.t5).wait()
    push(5)
    load_stash(src.last).wait()
    count = D // u_rows
    tall_rows = slope_rows

    def through_unpatch(index, carry):
        ring(src.w5, at.tall, u_rows, u_cols, index, index * u_rows).wait()
        slot = at.tall.at[lax.rem(index, tall)]
        offset = pl.multiple_of(index * u_rows, u_rows)
        d_norm[:, pl.ds(offset, u_rows)] = back_mul(src.gauss[...], slot[0:u_rows, 0:u_cols])

        @pl.when(index + tall < count)
        def _():
            ring(src.w5, at.tall, u_rows, u_cols, index + tall, (index + tall) * u_rows).start()

        return carry

    loop_work(2.5, count, 1, through_unpatch)
    for index in range(tall):
        ring(src.w4, at.tall, tall_rows, D, index, index * tall_rows).start()
    plan.work(2.5, lambda: norm_back(2, shrink_low, False))
    load_stash(src.mid).start()
    load(at.hidden).wait()

    def turn_shrink():
        at.shrink_t[...] = shrink_low[...].T

    plan.work(2.0, turn_shrink)
    push(4)
    ff = src.w3.shape[1]
    slabs = ff // tall_rows

    def through_shrink(index, carry):
        ring(src.w4, at.tall, tall_rows, D, index, index * tall_rows).wait()
        slope_load(index).wait()
        slot = lax.rem(index, tall)
        value = back_mul(shrink_low[...], at.tall[slot])
        value = value * at.slope_slots[slot].astype(F32)
        expand_low[:, pl.ds(pl.multiple_of(index * tall_rows, tall_rows), tall_rows)] = value.astype(BF16)

        @pl.when(index + tall < slabs)
        def _():
            ring(src.w4, at.tall, tall_rows, D, index + tall, (index + tall) * tall_rows).start()
            slope_load(index + tall).start()

        return carry

    loop_work(6.0, slabs, 2, through_shrink)
    owners = [lax.rem(me + step, narrow) for step in list(range(1, narrow)) + [0]]
    for index in range(min(tall, narrow)):
        ring(src.w2, at.tall, head_width, D, index, owners[index] * head_width).start()
    load(at.t3).wait()

    def through_expand(index, carry):
        ring(src.w3, at.long, wide_rows, ff, index, index * wide_rows).wait()
        offset = pl.multiple_of(index * wide_rows, wide_rows)
        d_norm[:, pl.ds(offset, wide_rows)] = back_mul(expand_low[...], at.long[lax.rem(index, long)])

        @pl.when(index + long < D // wide_rows)
        def _():
            ring(src.w3, at.long, wide_rows, ff, index + long, (index + long) * wide_rows).start()

        return carry

    loop_work(5.0, D // wide_rows, 2, through_expand)
    for index in range(long):
        ring(src.w1, at.long, wide_rows, 3 * D, index, index * wide_rows).start()
    load_stash(src.mid).wait()
    plan.work(2.0, lambda: norm_back(1, merge_low, True))
    load_stash(src.embedded).start()

    def swap(src, dst, kind, step):
        return pltpu.make_async_remote_copy(
            src_ref=src,
            dst_ref=dst,
            send_sem=swap_send.at[kind, step],
            recv_sem=swap_recv.at[kind, step],
            device_id=place.along(step),
            device_id_type=MESH,
        )

    d_heads, away = at.d_heads, at.away
    piece = 2 * (narrow - 1) * 2 * tokens * head_width / LINK

    def head_event():
        for step in range(1, narrow):
            swap(away.at[step - 1], d_heads.at[me], 0, step).wait_recv()

    def through_merge(index, owner):
        ring(src.w2, at.tall, head_width, D, index, owner * head_width).wait()
        value = back_mul(merge_low[...], at.tall[index % tall, 0:head_width, :]).astype(BF16)
        if index < narrow - 1:
            away[index] = value
            start(swap(away.at[index], d_heads.at[me], 0, index + 1))
        else:
            d_heads[me] = value
        if index + tall < narrow:
            ring(src.w2, at.tall, head_width, D, index + tall, owners[index + tall] * head_width).start()

    for index, owner in enumerate(owners):
        plan.work(0.7, functools.partial(through_merge, index, owner))
    plan.transfer(0, piece, (-1, 0, 0), head_event)
    load(at.t2).wait()
    push(3)
    push(2)
    load(at.qkv).wait()
    load(at.heads_out).wait()
    load(at.log_sums).wait()
    plan.need([(-1, 0, 0)])

    qkv, heads_out, log_sums, parts = at.qkv, at.heads_out, at.log_sums, at.parts
    key_t, key_acc, value_acc, query_acc = at.key_t, at.key_acc, at.value_acc, at.query_acc
    lane = lax.broadcasted_iota(jnp.int32, (1, LANES), 1)
    sides = LANES // HD
    scale = HD ** (-0.5)
    choose = lax.broadcasted_iota(jnp.int32, (8, LANES), 1) // HD
    choose = (choose == lax.broadcasted_iota(jnp.int32, (8, LANES), 0)).astype(F32)

    def part_swap(pair, step):
        lanes = pl.ds(pair * LANES, LANES)
        who = lax.rem(me + step, narrow)
        return swap(
            parts.at[who, :, :, lanes],
            mixed.at[pair, :, :, pl.ds(pl.multiple_of(me * LANES, LANES), LANES)],
            1 + pair,
            step,
        )

    pushed_pairs = []
    load(at.t1).wait()

    def part_event(pair):
        for step in range(1, narrow):
            part_swap(pair, step).wait_recv()

    for pair in range(head_width // LANES):
        lanes = pl.ds(pair * LANES, LANES)
        key_t[...] = qkv[:, 1, :, lanes].reshape(length, LANES).T
        key_acc[...] = jnp.zeros_like(key_acc)
        value_acc[...] = jnp.zeros_like(value_acc)
        def one_block(step, lanes=lanes, pair=pair):
            who = lax.rem(me + step, narrow)
            query = qkv[who, 0, :, lanes].astype(F32)
            upper = d_heads[who, :, lanes].astype(F32)
            kept = heads_out[who, :, lanes].astype(F32)
            delta = lax.dot_general(
                choose,
                upper * kept,
                (((1,), (1,)), ((), ())),
                precision=HIGHEST,
                preferred_element_type=F32,
            )
            log_rows = log_sums[who].T[pair * sides : (pair + 1) * sides, :]
            masks = [jnp.where(lane // HD == side, 1.0, 0.0) for side in range(sides)]
            own_query = jnp.concatenate([query * (scale * mask) for mask in masks], 0).astype(BF16)
            own_upper = jnp.concatenate([upper * mask for mask in masks], 0).astype(BF16)
            log_row = jnp.concatenate([log_rows[side : side + 1, :] for side in range(sides)], 1)
            delta_row = jnp.concatenate([delta[side : side + 1, :] for side in range(sides)], 1)
            query_acc[...] = jnp.zeros_like(query_acc)

            at_once = max(1, KEY_ROWS // tokens)
            for source in range(0, narrow, at_once):
                rows = pl.ds(source * tokens, at_once * tokens)
                some = pl.ds(source, at_once)
                key = qkv[some, 1, :, lanes].reshape(at_once * tokens, LANES)
                value = qkv[some, 2, :, lanes].reshape(at_once * tokens, LANES)
                probs = jnp.exp(back_mul(key, own_query) - log_row)
                d_probs = back_mul(value, own_upper)
                d_scores = (probs * (d_probs - delta_row)).astype(BF16)
                value_acc[rows, :] += matmul(probs.astype(BF16), own_upper)
                key_acc[rows, :] += matmul(d_scores, own_query)
                turned = matmul(key_t[:, rows], d_scores)
                for side in range(sides):
                    spot = slice(side * HD, (side + 1) * HD)
                    query_acc[spot, :] += turned[spot, side * tokens : (side + 1) * tokens]

            parts[who, 0, :, lanes] = (query_acc[...].T * scale).astype(BF16)
        for step in range(narrow):
            plan.work(3.0, functools.partial(one_block, step))
            for earlier in range(pair):
                if earlier not in pushed_pairs and (-2, 0, earlier) in plan.done:
                    pushed_pairs.append(earlier)
                    push(1, earlier)
        for source in range(narrow):
            rows = pl.ds(source * tokens, tokens)
            parts[source, 1, :, lanes] = key_acc[rows, :].astype(BF16)
            parts[source, 2, :, lanes] = value_acc[rows, :].astype(BF16)
        for step in range(1, narrow):
            start(part_swap(pair, step))
        plan.now += 1.0
        plan.transfer(0, 1.5 * piece, (-2, 0, pair), functools.partial(part_event, pair))
        mixed[pair, :, :, pl.ds(pl.multiple_of(me * LANES, LANES), LANES)] = parts[me, :, :, lanes]
    for pair in range(head_width // LANES):
        if pair not in pushed_pairs:
            plan.need([(-2, 0, pair)])
            push(1, pair)

    def through_mixer(index, carry):
        ring(src.w1, at.long, wide_rows, 3 * D, index, index * wide_rows).wait()
        slot = lax.rem(index, long)
        value = jnp.zeros((tokens, wide_rows), F32)
        for pair in range(head_width // LANES):
            for part in range(3):
                columns = [part * D + owner * head_width + pair * LANES for owner in range(narrow)]
                weight = [at.long[slot, :, column : column + LANES] for column in columns]
                value = value + back_mul(mixed[pair, part], jnp.concatenate(weight, 1))
        d_norm[:, pl.ds(pl.multiple_of(index * wide_rows, wide_rows), wide_rows)] = value

        @pl.when(index + long < D // wide_rows)
        def _():
            ring(src.w1, at.long, wide_rows, 3 * D, index + long, (index + long) * wide_rows).start()

        return carry

    plan.work(4.0, lambda: lax.fori_loop(0, D // wide_rows, through_mixer, 0))
    load_stash(src.embedded).wait()
    plan.work(3.0, lambda: norm_back(0, at.embed_low, True))
    at.embed_t[...] = at.embed_low[...].T
    turned = jnp.concatenate([norms[...], jnp.zeros((LANES - 8, D), F32)], 0).T
    at.extra[...] = pltpu.roll(turned, lead, 1)
    push(0)
    plan.finish()

    rows = lax.broadcasted_iota(jnp.int32, (8, LANES), 0)
    wide_tiles, narrow_tiles = at.wide_tiles, at.narrow_tiles
    wide_tiles[place.w] = jnp.where(rows == 0, src.term[...], jnp.sum(at.squares[...]))

    def tile_copy(buffer, index, slot, peer):
        return pltpu.make_async_remote_copy(
            src_ref=buffer.at[index],
            dst_ref=buffer.at[index],
            send_sem=tile_send.at[slot],
            recv_sem=tile_recv.at[slot],
            device_id=peer,
            device_id_type=MESH,
        )

    for step in range(1, wide):
        start(tile_copy(wide_tiles, place.w, step - 1, (lax.rem(place.w + step, wide), place.n)))
    for step in range(1, wide):
        tile_copy(wide_tiles, place.w, step - 1, (lax.rem(place.w + step, wide), place.n)).wait_recv()
    whole = wide_tiles[0]
    for index in range(1, wide):
        whole = whole + wide_tiles[index]
    narrow_tiles[place.n] = whole
    for step in range(1, narrow):
        start(tile_copy(narrow_tiles, place.n, wide + step - 1, place.along(step)))
    for step in range(1, narrow):
        tile_copy(narrow_tiles, place.n, wide + step - 1, place.along(step)).wait_recv()
    whole = narrow_tiles[0]
    for index in range(1, narrow):
        whole = whole + narrow_tiles[index]
    totals[...] = whole
    for copy in list(last_sent.values()) + started:
        copy.wait_send()
    for condition, copy in guarded:

        @pl.when(condition)
        def _():
            copy.wait_send()


def backward_all(kept, patches, gauss, term, lead, wide, narrow):
    tokens = patches.shape[0]
    chips = wide // 2
    weights = [kept.w1, kept.w2, kept.w3, kept.w4, kept.w5]
    heights = [D] + [weight.shape[0] for weight in weights]
    widths = [patches.shape[1]] + [weight.shape[1] for weight in weights]
    rows = [height // (wide * narrow) for height in heights]
    head_width = D // narrow
    length = narrow * tokens
    items = backward_plan(widths, head_width // LANES)
    slots = 2 * chips + max(2, narrow - 1)
    streamed = dict(w1=kept.w1, w2=kept.w2, w3=kept.w3, w4=kept.w4, w5=kept.w5)
    streamed.update(last=kept.last, mid=kept.mid, embedded=kept.embedded, slopes=kept.slopes)
    loaded = dict(t5=kept.t5, hidden=kept.hidden, t3=kept.t3, t2=kept.t2, t1=kept.t1)
    loaded.update(qkv=kept.qkv, heads_out=kept.heads_out, log_sums=kept.log_sums)
    whole = dict(gains=kept.gains, patches=patches, gauss=gauss, term=term)
    operands = {**streamed, **loaded, **whole}
    shapes = [jax.ShapeDtypeStruct((rows[which], widths[which]), F32) for which in range(6)]
    shapes[4] = jax.ShapeDtypeStruct((D, rows[4]), F32)
    shapes.append(jax.ShapeDtypeStruct((8, LANES), F32))
    scratch = {name: pltpu.VMEM(value.shape, value.dtype) for name, value in loaded.items()}
    blocks = [(width, rows[which]) if which == 4 else (rows[which], width) for which, _, width, _ in items]
    scratch.update(
        squares=pltpu.VMEM((1, max(block[1] for block in blocks)), F32),
        embed_t=pltpu.VMEM((D, tokens), BF16),
        embed_low=pltpu.VMEM((tokens, D), BF16),
        shrink_t=pltpu.VMEM((D, tokens), BF16),
        stash=pltpu.VMEM((tokens, D), F32),
        d_res=pltpu.VMEM((tokens, D), F32),
        d_norm=pltpu.VMEM((tokens, D), F32),
        norms=pltpu.VMEM((8, D), F32),
        extra=pltpu.VMEM((D, LANES), F32),
        shrink_low=pltpu.VMEM((tokens, D), BF16),
        expand_low=pltpu.VMEM((tokens, widths[3]), BF16),
        merge_low=pltpu.VMEM((tokens, D), BF16),
        mixed=pltpu.VMEM((head_width // LANES, 3, tokens, narrow * LANES), BF16),
        tall=pltpu.VMEM((4, 256, D), BF16),
        long=pltpu.VMEM((2, 256, widths[3]), BF16),
        slope_slots=pltpu.VMEM((4, tokens, 256), BF16),
        d_heads=pltpu.VMEM((narrow, tokens, head_width), BF16),
        away=pltpu.VMEM((narrow - 1, tokens, head_width), BF16),
        parts=pltpu.VMEM((narrow, 3, tokens, head_width), BF16),
        key_t=pltpu.VMEM((LANES, length), BF16),
        key_acc=pltpu.VMEM((length, LANES), F32),
        value_acc=pltpu.VMEM((length, LANES), F32),
        query_acc=pltpu.VMEM((LANES, tokens), F32),
        wide_tiles=pltpu.VMEM((wide, 8, LANES), F32),
        narrow_tiles=pltpu.VMEM((narrow, 8, LANES), F32),
        send_sem=pltpu.SemaphoreType.DMA((len(items), slots)),
        recv_sem=pltpu.SemaphoreType.DMA((len(items), slots)),
        tile_send=pltpu.SemaphoreType.DMA((wide + narrow,)),
        tile_recv=pltpu.SemaphoreType.DMA((wide + narrow,)),
        swap_send=pltpu.SemaphoreType.DMA((1 + head_width // LANES, narrow)),
        swap_recv=pltpu.SemaphoreType.DMA((1 + head_width // LANES, narrow)),
        in_sem=pltpu.SemaphoreType.DMA((9,)),
        ring_sem=pltpu.SemaphoreType.DMA((3, 4)),
    )
    lists = [pltpu.VMEM((chips, narrow) + block, BF16) for block in blocks]
    for block in blocks:
        for bit in chip_bits(chips):
            lists.append(pltpu.VMEM((chips // (2 * bit), narrow) + block, BF16))
    for (which, _, _, _), block in zip(items, blocks):
        lists.append(pltpu.VMEM((narrow + (1 if which in RELAYED else -1),) + block, BF16))
    for which in range(6):
        widest = max(block for item, block in zip(items, blocks) if item[0] == which)
        lists.append(pltpu.VMEM((chips, narrow) + widest, BF16))
    vmem = pl.BlockSpec(memory_space=pltpu.VMEM)
    hbm = pl.BlockSpec(memory_space=pl.ANY)
    return pl.pallas_call(
        functools.partial(backward_kernel, items, wide, narrow, lead, tuple(operands), tuple(scratch)),
        out_shape=shapes,
        in_specs=[vmem if name in whole else hbm for name in operands],
        out_specs=[vmem] * len(shapes),
        scratch_shapes=list(scratch.values()) + lists,
        compiler_params=pltpu.CompilerParams(
            collective_id=1, has_side_effects=True, vmem_limit_bytes=63 * MIB
        ),
        name="backward",
    )(*operands.values())


def render_kernel(
    gauss_ref, weight_ref, target_ref, mask_ref, pair_ref, view_ref, total_ref, grad_ref, term_ref, feat, dfeat
):
    quads = gauss_ref.shape[0] // NVIEW
    span = weight_ref.shape[1]
    pairs = pair_ref.shape[1]
    scale = 1.0 / total_ref[0].astype(F32)

    def channel(index):
        return gauss_ref[:, index * PP : (index + 1) * PP]

    def shared():
        opacity = jax.nn.sigmoid(channel(3))
        extent = jax.nn.sigmoid(channel(5) + channel(6) + channel(7))
        lead = channel(8)
        denom = 1.0 + lead * lead + channel(9) * channel(9) + channel(10) * channel(10) + channel(11) * channel(11)
        facing = lead * lead / denom
        raw = channel(4)
        depth = jnp.maximum(raw, 0.0) + jnp.log1p(jnp.exp(-jnp.abs(raw)))
        return opacity, extent, lead, denom, facing, raw, depth

    opacity, extent, lead, denom, facing, raw, depth = shared()
    footprint = opacity * extent * facing
    channels = [jax.nn.sigmoid(channel(index)) * footprint for index in range(3)]
    channels += [footprint, depth * footprint]
    for index, value in enumerate(channels):
        for view in range(NVIEW):
            feat[index * quads : (index + 1) * quads, view * PP : (view + 1) * PP] = value[
                view * quads : (view + 1) * quads
            ]
    rendered = jnp.dot(feat[...], weight_ref[...], precision=HIGHEST, preferred_element_type=F32)
    parts = [rendered[index * quads : (index + 1) * quads] for index in range(5)]
    lane = lax.broadcasted_iota(jnp.int32, (quads, span), 1)
    live = jnp.where(lane < view_ref[0] * PP, mask_ref[...], 0).astype(F32)
    term = jnp.zeros((quads, span), F32)
    slopes = []
    for index in range(3):
        error = parts[index] - target_ref[index * quads : (index + 1) * quads, :].astype(F32)
        term = term + live * error * error
        slopes.append(2.0 * scale * live * error)
    below = 1.0 + parts[3]
    depth_out = parts[4] / below

    first, second = pair_ref[0:1, :], pair_ref[1:2, :]
    least = jnp.minimum(first, second)
    down = (jnp.abs(first - second) == P_SIZE).astype(jnp.int32)
    place = quads * PP
    slot, local = least // place, least % place
    high = down * quads + local // PP
    low = slot * PP + local % PP
    high_hot = (lax.broadcasted_iota(jnp.int32, (2 * quads, pairs), 0) == high).astype(F32).astype(BF16)
    low_hot = (lax.broadcasted_iota(jnp.int32, (span, pairs), 0) == low).astype(F32).astype(BF16)
    counts = back_mul(high_hot, low_hot)
    slope = jnp.zeros((quads, span), F32)
    for which, shift in enumerate((1, P_SIZE)):
        count = counts[which * quads : (which + 1) * quads]
        weight = DEPTH_WEIGHT * count * live * pltpu.roll(live, span - shift, 1)
        gap = depth_out - pltpu.roll(depth_out, span - shift, 1)
        term = term + weight * gap * gap
        pull = 2.0 * scale * weight * gap
        slope = slope + pull - pltpu.roll(pull, shift, 1)
    term_ref[...] = jnp.full(term_ref.shape, jnp.sum(term), F32)
    over = slope / below
    slopes += [-over * depth_out, over]
    stacked = jnp.concatenate(slopes, 0)
    dfeat[...] = lax.dot_general(
        stacked, weight_ref[...], (((1,), (1,)), ((), ())), precision=HIGHEST, preferred_element_type=F32
    )

    def feature_grad(index):
        return jnp.concatenate(
            [
                dfeat[index * quads : (index + 1) * quads, view * PP : (view + 1) * PP]
                for view in range(NVIEW)
            ],
            0,
        )

    def put(index, value):
        grad_ref[:, index * PP : (index + 1) * PP] = value.astype(BF16)

    d_foot = feature_grad(3)
    for index in range(3):
        tint = jax.nn.sigmoid(channel(index))
        upper = feature_grad(index)
        d_foot = d_foot + upper * tint
        put(index, upper * footprint * tint * (1.0 - tint))
    d_last = feature_grad(4)
    d_foot = d_foot + d_last * depth
    put(3, d_foot * extent * facing * opacity * (1.0 - opacity))
    put(4, d_last * footprint * jax.nn.sigmoid(raw))
    d_extent = d_foot * opacity * facing * extent * (1.0 - extent)
    for index in (5, 6, 7):
        put(index, d_extent)
    d_facing = d_foot * opacity * extent
    put(8, d_facing * 2.0 * lead / denom * (1.0 - facing))
    for index in (9, 10, 11):
        put(index, -2.0 * d_facing * facing / denom * channel(index))


def render(gaussians, weights, targets, mask, pairs, view_count, pair_total):
    rows = gaussians.shape[0]
    quads = rows // NVIEW
    slots, views = weights.shape[:2]
    spread = weights.transpose(1, 2, 0, 3).reshape(views * PP, slots * PP)
    wanted = targets.reshape(slots, 3, quads, PP).transpose(1, 2, 0, 3).reshape(3 * quads, slots * PP)
    valid = mask.reshape(slots, quads, PP).transpose(1, 0, 2).reshape(quads, slots * PP)
    vmem = pl.BlockSpec(memory_space=pltpu.VMEM)
    smem = pl.BlockSpec(memory_space=pltpu.SMEM)
    return pl.pallas_call(
        render_kernel,
        out_shape=[
            jax.ShapeDtypeStruct(gaussians.shape, BF16),
            jax.ShapeDtypeStruct((8, LANES), F32),
        ],
        in_specs=[vmem] * 5 + [smem] * 2,
        out_specs=[vmem] * 2,
        scratch_shapes=[pltpu.VMEM((5 * quads, views * PP), F32)] * 2,
        compiler_params=pltpu.CompilerParams(vmem_limit_bytes=48 * MIB),
        name="render",
    )(gaussians, spread, wanted, valid, pairs, view_count, pair_total)


def forward_plain(shards, patches, features, kinds):
    weights = [lax.all_gather(shard, BOTH, axis=0, tiled=True) for shard in shards]
    groups = lax.axis_size(NARROW)
    rows = patches.shape[0]
    gains = weights[0][:, features : features + kinds].T.astype(F32)
    embedded = back_mul(patches[:, :features], weights[0][:, :features])
    normed_one = layer_norm(embedded, gains[0], gains[3]).astype(BF16)
    mixed = matmul(normed_one, weights[1]).astype(BF16).reshape(rows, 3, groups, -1)
    mixed = mixed.transpose(2, 1, 0, 3)
    qkv = lax.all_to_all(mixed, NARROW, split_axis=0, concat_axis=0, tiled=True)
    width = qkv.shape[-1]
    length = groups * rows
    heads = width // HD
    parts = [qkv[:, part].reshape(length, heads, HD) for part in range(3)]
    attended, logsum = attention_forward(*parts)
    log_sums = logsum.transpose(0, 2, 1).reshape(groups, rows, heads)
    returned = lax.all_to_all(
        attended.reshape(groups, rows, width), NARROW, split_axis=0, concat_axis=0, tiled=True
    )
    returned = returned.transpose(1, 0, 2).reshape(rows, D)
    mid = embedded + matmul(returned, weights[2])
    normed_two = layer_norm(mid, gains[1], gains[4]).astype(BF16)
    expanded = matmul(normed_two, weights[3])
    half = 0.5 * (1.0 + lax.erf(expanded * (0.5**0.5)))
    activated = (expanded * half).astype(BF16)
    bell = jnp.exp(-0.5 * expanded * expanded) * 0.3989422804014327
    slopes = (half + expanded * bell).astype(BF16)
    last = mid + matmul(activated, weights[4])
    normed_three = layer_norm(last, gains[2], gains[5]).astype(BF16)
    return Bag(
        dict(
        w1=weights[1],
        w2=weights[2],
        w3=weights[3],
        w4=weights[4],
        w5=weights[5],
        gains=gains,
        embedded=embedded,
        mid=mid,
        last=last,
        slopes=slopes,
        t1=normed_one.T,
        t2=returned.T,
        t3=normed_two.T,
        hidden=activated,
        t5=normed_three.T,
        qkv=qkv,
        heads_out=attended,
        log_sums=log_sums,
        gaussians=matmul(normed_three, weights[5]),
    ).items())


def backward_plain(kept, patches, gauss_low, term, features, kinds):
    gains = kept.gains
    weights = [None, kept.w1, kept.w2, kept.w3, kept.w4, kept.w5]
    norm_back_one = jax.vjp(layer_norm, kept.embedded, gains[0], gains[3])[1]
    norm_back_two = jax.vjp(layer_norm, kept.mid, gains[1], gains[4])[1]
    norm_back_three = jax.vjp(layer_norm, kept.last, gains[2], gains[5])[1]
    qkv = kept.qkv
    groups, _, rows, width = qkv.shape
    length = groups * rows
    heads = width // HD
    queries, keys, values = (qkv[:, part].reshape(length, heads, HD) for part in range(3))
    blocked = min(512, length)
    logsum = kept.log_sums[:, :, :heads].reshape(length // blocked, blocked, heads)
    residual_grad, gain_three, shift_three = norm_back_three(back_mul(gauss_low, weights[5]))
    shrink_low = residual_grad.astype(BF16)
    expand_low = (back_mul(shrink_low, weights[4]) * kept.slopes.astype(F32)).astype(BF16)
    through_two, gain_two, shift_two = norm_back_two(back_mul(expand_low, weights[3]))
    residual_grad = residual_grad + through_two
    merge_low = residual_grad.astype(BF16)
    out_grad = back_mul(merge_low, weights[2]).astype(BF16).reshape(rows, groups, width)
    head_grad = lax.all_to_all(
        out_grad.transpose(1, 0, 2), NARROW, split_axis=0, concat_axis=0, tiled=True
    ).reshape(length, heads, HD)
    grads = attention_backward(queries, keys, values, logsum.transpose(0, 2, 1), head_grad)
    stacked = jnp.stack(grads, 1).astype(BF16).reshape(groups, rows, 3, width)
    mixed_grad = lax.all_to_all(stacked, NARROW, split_axis=0, concat_axis=0, tiled=True)
    mixed_grad = mixed_grad.transpose(1, 2, 0, 3).reshape(rows, 3 * D)
    through_one, gain_one, shift_one = norm_back_one(back_mul(mixed_grad, weights[1]))
    embed_grad = (residual_grad + through_one).astype(BF16)
    grad_norms = jnp.stack([gain_one, gain_two, gain_three, shift_one, shift_two, shift_three])
    lefts = [embed_grad.T, kept.t1, kept.t2, kept.t3, kept.hidden.T, kept.t5]
    rights = [patches, mixed_grad, merge_low, expand_low, shrink_low, gauss_low]
    products = [matmul(left, right) for left, right in zip(lefts, rights)]
    products[0] = products[0].at[:, features : features + kinds].add(grad_norms.T)
    sums = [
        lax.psum_scatter(
            product.astype(BF16), BOTH, scatter_dimension=0, tiled=True
        ).astype(F32)
        for product in products
    ]
    squares = sum(jnp.sum(part * part) for part in sums)
    loss_sum, square_sum = lax.psum((term[0, 0], squares), BOTH)
    return sums, loss_sum, square_sum


def update_kernel(features, total_ref, sums_ref, *refs):
    sources, targets, refs = refs[:27], refs[27:48], refs[48:]
    loss_ref, norm_ref, refs = refs[0], refs[1], refs[2:]
    inside, news, refs = refs[:27], refs[27:48], refs[48:]
    turned, turned_four, in_sem, out_sem = refs
    loads = [pltpu.make_async_copy(source, dest, in_sem.at[i]) for i, (source, dest) in enumerate(zip(sources, inside))]
    stores = [pltpu.make_async_copy(source, dest, out_sem.at[i]) for i, (source, dest) in enumerate(zip(news, targets))]
    for copy in loads:
        copy.start()
    grads, olds = inside[:6], inside[6:]
    square_sum = sums_ref[1:2, 0:1]
    grad_norm = jnp.sqrt(square_sum)
    factor = jnp.minimum(1.0, CLIP_NORM / (grad_norm + 1e-06))
    norm_ref[...] = grad_norm
    loss_ref[...] = sums_ref[0:1, 0:1] / total_ref[0].astype(F32)
    width = grads[0].shape[1]
    for which in range(7):
        if which < 6:
            loads[which].wait()
        if which == 0:
            turned[...] = grads[0][:, width - LANES :].T
        if which == 4:
            turned_four[...] = grads[4][...].T
        for copy in loads[6 + 3 * which : 9 + 3 * which]:
            copy.wait()
        weight, first, second = olds[3 * which : 3 * which + 3]
        rows, columns = weight.shape
        chunk = min(8, rows)

        def one(step, carry):
            spot = pl.ds(pl.multiple_of(step * chunk, chunk), chunk)
            if which == 0:
                grad = grads[0][spot, 0:columns]
            elif which == 4:
                grad = turned_four[spot, :]
            elif which == 6:
                grad = turned[features % LANES : features % LANES + rows, 0:columns]
            else:
                grad = grads[which][spot, :]
            values = adamw(weight[spot, :], first[spot, :], second[spot, :], grad * factor, RATES[which])
            for dest, value in zip(news[3 * which : 3 * which + 3], values):
                dest[spot, :] = value
            return carry

        lax.fori_loop(0, rows // chunk, one, 0)
        for copy in stores[3 * which : 3 * which + 3]:
            copy.start()
    for copy in stores:
        copy.wait()


def update_all(olds, sums, totals, pair_total, features):
    vmem = pl.BlockSpec(memory_space=pltpu.VMEM)
    smem = pl.BlockSpec(memory_space=pltpu.SMEM)
    hbm = pl.BlockSpec(memory_space=pltpu.HBM)
    shapes = [jax.ShapeDtypeStruct(old.shape, F32) for old in olds]
    inside = [pltpu.VMEM(value.shape, F32) for value in list(sums) + list(olds)]
    return pl.pallas_call(
        functools.partial(update_kernel, features),
        out_shape=shapes + [jax.ShapeDtypeStruct((1, 1), F32)] * 2,
        in_specs=[smem, vmem] + [hbm] * 27,
        out_specs=[hbm] * 21 + [vmem] * 2,
        scratch_shapes=inside
        + [pltpu.VMEM(old.shape, F32) for old in olds]
        + [
            pltpu.VMEM((LANES, sums[0].shape[0]), F32),
            pltpu.VMEM(olds[12].shape, F32),
            pltpu.SemaphoreType.DMA((27,)),
            pltpu.SemaphoreType.DMA((21,)),
        ],
        compiler_params=pltpu.CompilerParams(vmem_limit_bytes=60 * MIB),
        name="update",
    )(pair_total, totals, *sums, *olds)


def body(
    views,
    render_w,
    targets,
    pix_mask,
    pairs,
    view_count,
    pair_total,
    embed_weight,
    embed_first,
    embed_second,
    mixer_weight,
    mixer_first,
    mixer_second,
    merge_weight,
    merge_first,
    merge_second,
    expand_weight,
    expand_first,
    expand_second,
    shrink_weight,
    shrink_first,
    shrink_second,
    unpatch_weight,
    unpatch_first,
    unpatch_second,
    norm_params,
    norm_first,
    norm_second,
):
    masters = (embed_weight, mixer_weight, merge_weight, expand_weight, shrink_weight, unpatch_weight, norm_params)
    firsts = (embed_first, mixer_first, merge_first, expand_first, shrink_first, unpatch_first, norm_first)
    seconds = (embed_second, mixer_second, merge_second, expand_second, shrink_second, unpatch_second, norm_second)
    groups = lax.axis_size(NARROW)
    wide_count = lax.axis_size(WIDE)
    features = embed_weight.shape[0]
    kinds = norm_params.shape[0]
    padded = -(-(features + kinds) // LANES) * LANES
    fill = padded - features - kinds
    by_kernel = mixer_weight.shape[0] % 16 == 0 and shrink_weight.shape[0] % LANES == 0

    patches = views.reshape(-1, features)
    rows = patches.shape[0]
    patches = jnp.pad(patches, ((0, 0), (0, padded - features)))
    if by_kernel:
        raw = (embed_weight.T,) + masters[1:6]
        kept = forward_all(raw, norm_params, patches, features % LANES, wide_count, groups)
    else:
        first_shard = jnp.concatenate([embed_weight.T, norm_params.T], 1)
        first_shard = jnp.pad(first_shard.astype(BF16), ((0, 0), (0, fill)))
        shards = [first_shard] + [weight.astype(BF16) for weight in masters[1:6]]
        kept = forward_plain(shards, patches, features, kinds)
    divisor = pair_total[0].astype(F32)
    gauss_low, term = render(
        kept.gaussians, render_w[0], targets[0], pix_mask[0], pairs[0], view_count, pair_total
    )
    if by_kernel:
        *sums, totals = backward_all(
            kept, patches, gauss_low, term, features % LANES, wide_count, groups
        )
        olds = []
        for triple in zip(masters, firsts, seconds):
            olds += triple
        olds[:3] = [old.T for old in olds[:3]]
        *news, loss, grad_norm = update_all(olds, sums, totals, pair_total, features)
        news[:3] = [new.T for new in news[:3]]
        return tuple(news) + (loss[0, 0], grad_norm[0, 0])
    sums, loss_sum, square_sum = backward_plain(kept, patches, gauss_low, term, features, kinds)
    first_sum = sums[0].T
    grads = [first_sum[:features]] + list(sums[1:]) + [first_sum[features : features + kinds]]
    loss = loss_sum / divisor
    grad_norm = jnp.sqrt(square_sum)
    factor = jnp.minimum(1.0, CLIP_NORM / (grad_norm + 1e-06))
    results = []
    for which in range(7):
        results += adamw(masters[which], firsts[which], seconds[which], grads[which] * factor, RATES[which])
    return tuple(results) + (loss, grad_norm)


def solution(mesh):
    columns = P(None, BOTH)
    rows = P(BOTH, None)
    weights = (columns,) * 3 + (rows,) * 15 + (columns,) * 3
    return jax.shard_map(
        body,
        mesh=mesh,
        in_specs=(
            P(WIDE, None, NARROW, None),
            P(WIDE, None, None, None, None),
            P(WIDE, None, None, NARROW),
            P(WIDE, None, NARROW),
            P(WIDE, None, NARROW),
            P(WIDE),
            P(),
        )
        + weights,
        out_specs=weights + (P(), P()),
        check_vma=False,
    )
```

```python
import functools
import heapq

import jax
import jax.numpy as jnp
from jax import lax
from jax.experimental import pallas as pl
from jax.experimental.pallas import tpu as pltpu
from jax.sharding import PartitionSpec as P

D = 1024
HD = 64
P_SIZE = 8
PP = 64
NVIEW = 4
TMAX = 12
STEP = 10
LANES = 128
MIB = 1024 * 1024

DEPTH_WEIGHT = 1.0
CLIP_NORM = 0.01
BETA_ONE = 0.9
BETA_TWO = 0.95
ADAM_EPS = 1e-08
DECAY = 0.05
RATES = (0.05, 0.05, 0.5, 0.05, 0.05, 0.05, 0.8)
MESH = pl.DeviceIdType.MESH
WIDE, NARROW = BOTH = ("wide", "narrow")
HIGHEST = lax.Precision.HIGHEST
F32 = jnp.float32
BF16 = jnp.bfloat16


def matmul(left, right):
    return jnp.dot(left, right, preferred_element_type=F32)


def outer_sum(left, right):
    return lax.dot_general(left, right, (((0,), (0,)), ((), ())), preferred_element_type=F32)


def back_mul(grad, weight):
    return lax.dot_general(grad, weight, (((1,), (1,)), ((), ())), preferred_element_type=F32)


def layer_norm(values, gain, shift):
    centred = values - jnp.mean(values, -1, keepdims=True)
    spread = jnp.mean(centred * centred, -1, keepdims=True)
    return centred * lax.rsqrt(spread + 1e-05) * gain + shift


def exact_gelu(values):
    return jax.nn.gelu(values, approximate=False)


def attention_forward(queries, keys, values):
    length, heads = (queries.shape[0], queries.shape[1])
    blocked = min(512, length)
    scale = HD ** (-0.5)

    def one_block(query_block):
        scores = (
            jnp.einsum("qhd,khd->hqk", query_block, keys, preferred_element_type=jnp.float32)
            * scale
        )
        highest = jnp.max(scores, -1, keepdims=True)
        exponentials = jnp.exp(scores - highest)
        summed = jnp.sum(exponentials, -1, keepdims=True)
        softmaxed = (exponentials / summed).astype(jnp.bfloat16)
        output = jnp.einsum("hqk,khd->qhd", softmaxed, values, preferred_element_type=jnp.float32)
        return (output.astype(jnp.bfloat16), (highest + jnp.log(summed))[:, :, 0])

    output, logsum = lax.map(one_block, queries.reshape(length // blocked, blocked, heads, HD))
    return (output.reshape(length, heads * HD), logsum)


def attention_backward(queries, keys, values, logsum, out_grad):
    length, heads = (queries.shape[0], queries.shape[1])
    blocked = min(512, length)
    scale = HD ** (-0.5)

    def one_block(carry, inputs):
        key_grad, value_grad = carry
        query_block, logsum_block, grad_block = inputs
        scores = (
            jnp.einsum("qhd,khd->hqk", query_block, keys, preferred_element_type=jnp.float32)
            * scale
        )
        softmaxed = jnp.exp(scores - logsum_block[:, :, None])
        value_grad = value_grad + jnp.einsum(
            "hqk,qhd->khd",
            softmaxed.astype(jnp.bfloat16),
            grad_block,
            preferred_element_type=jnp.float32,
        )
        prob_grad = jnp.einsum(
            "qhd,khd->hqk", grad_block, values, preferred_element_type=jnp.float32
        )
        score_grad = softmaxed * (prob_grad - jnp.sum(softmaxed * prob_grad, -1, keepdims=True))
        score_low = score_grad.astype(jnp.bfloat16)
        query_grad = (
            jnp.einsum("hqk,khd->qhd", score_low, keys, preferred_element_type=jnp.float32) * scale
        )
        key_grad = (
            key_grad
            + jnp.einsum("hqk,qhd->khd", score_low, query_block, preferred_element_type=jnp.float32)
            * scale
        )
        return ((key_grad, value_grad), query_grad)

    zeros = jnp.zeros((length, heads, HD), jnp.float32)
    shaped = (
        queries.reshape(length // blocked, blocked, heads, HD),
        logsum,
        out_grad.reshape(length // blocked, blocked, heads, HD),
    )
    (key_grad, value_grad), query_grad = lax.scan(one_block, (zeros, zeros), shaped)
    return (query_grad.reshape(length, heads, HD), key_grad, value_grad)


def adamw(weight, first, second, grad, rate):
    first = BETA_ONE * first + (1.0 - BETA_ONE) * grad
    second = BETA_TWO * second + (1.0 - BETA_TWO) * grad * grad
    first_hat = first / (1.0 - BETA_ONE**STEP)
    second_hat = second / (1.0 - BETA_TWO**STEP)
    weight = weight - rate * (first_hat / (jnp.sqrt(second_hat) + ADAM_EPS) + DECAY * weight)
    return (weight, first, second)


def chip_bits(chips):
    bits, step = [], 1
    while step < chips:
        bits.append(step)
        step *= 2
    return bits


def flip(chip, mask):
    for bit in chip_bits(mask + 1):
        if mask & bit:
            chip = chip + (1 - 2 * (chip // bit % 2)) * bit
    return chip


def column_halves(width):
    first = -(-width // (2 * LANES)) * LANES
    return ((0, first), (first, width - first))


def work_items(widths, order):
    return [(which,) + half + (side,) for which in order for side, half in enumerate(column_halves(widths[which]))]


class Bag:
    def __init__(self, pairs):
        vars(self).update(pairs)


class Place:
    def __init__(self, wide, narrow):
        self.wide, self.narrow = wide, narrow
        self.chips = wide // 2
        self.bits = chip_bits(self.chips)
        self.w = lax.axis_index(WIDE)
        self.n = lax.axis_index(NARROW)
        self.chip = self.w // 2
        self.core = self.w % 2
        self.twin = (2 * self.chip + 1 - self.core, self.n)

    def across(self, mask):
        return (2 * flip(self.chip, mask) + self.core, self.n)

    def along(self, step):
        return (self.w, lax.rem(self.n + step, self.narrow))

    def neighbours(self):
        return (
            [self.twin]
            + [self.across(bit) for bit in self.bits]
            + [self.along(step) for step in range(1, self.narrow)]
        )


class Planner:
    def __init__(self):
        self.now, self.count = 0.0, 0
        self.free, self.events, self.done, self.spare = {}, [], set(), []
        self.refill = lambda: None

    def transfer(self, link, cost, key, event):
        self.free[link] = max(self.now, self.free.get(link, 0.0)) + cost
        self.count += 1
        heapq.heappush(self.events, (self.free[link] + 2.0, self.count, key, event))

    def step(self):
        when, _, key, event = heapq.heappop(self.events)
        self.now = max(self.now, when) + 0.2
        event()
        self.done.add(key)
        self.refill()

    def fill(self, until):
        for index, (keys, cost, work) in enumerate(self.spare):
            if self.now + cost <= until and self.done.issuperset(keys):
                del self.spare[index]
                work()
                self.now += cost
                return True
        return False

    def need(self, keys):
        while not self.done.issuperset(keys):
            if not self.fill(self.events[0][0]):
                self.step()

    def work(self, cost, work):
        while self.events and self.events[0][0] <= self.now:
            self.step()
        self.refill()
        work()
        self.now += cost

    def later(self, cost, work, keys=()):
        entry = (tuple(keys), cost, work)
        self.spare.append(entry)
        return entry

    def force(self, entry):
        if entry in self.spare:
            self.spare.remove(entry)
            self.work(entry[1], entry[2])

    def finish(self):
        self.refill()
        while self.events or self.spare:
            if not self.fill(self.events[0][0] if self.events else 1e9):
                self.step()


LINK = 90e3
Z_AHEAD = 4.0
RELAYED = (3, 4)
KEY_ROWS = 512
Z_EARLY = 1.0
Z_LATE = 2.0
TWIN_LINK = 600e3


def greet(peers):
    barrier = pltpu.get_barrier_semaphore()
    for peer in peers:
        pl.semaphore_signal(barrier, inc=1, device_id=peer, device_id_type=MESH)
    return lambda: pl.semaphore_wait(barrier, len(peers))


def normalize(values, gain, shift):
    centred = values - jnp.mean(values, -1, keepdims=True)
    spread = jnp.mean(centred * centred, -1, keepdims=True)
    return centred * lax.rsqrt(spread + 1e-05) * gain + shift


def forward_plan(widths):
    items = []
    for which, cuts in ((0, 1), (1, 3), (2, 1), (3, 2), (5, 1), (4, 2)):
        size = widths[which] // cuts
        for cut in range(cuts):
            for side, (start, width) in enumerate(column_halves(size)):
                items.append((which, cut * size + start, width, side))
    return items


def forward_kernel(items, wide, narrow, lead, ins, outs, scratch, *refs):
    at = Bag(zip(ins + scratch, refs[: len(ins)] + refs[len(ins) + len(outs) :]))
    results = refs[len(ins) : len(ins) + len(outs)]
    weights = [at.first_weight, at.w1, at.w2, at.w3, at.w4, at.w5]
    shards = [at.c0, at.c1, at.c2, at.c3, at.c4, at.c5]
    raw = [at.s0, at.s1, at.s2, at.s3, at.s4, at.s5]
    own_sem, send_sem, recv_sem = at.own_sem, at.send_sem, at.recv_sem
    swap_send, swap_recv, out_sem = at.swap_send, at.swap_recv, at.out_sem
    place = Place(wide, narrow)
    chips, me = place.chips, place.n
    tokens = at.patches.shape[0]
    head_width = D // narrow
    total = len(items)
    started, guarded = [], []

    def start(copy):
        copy.start()
        started.append(copy)

    all_here = greet(place.neighbours())
    features = at.s0.shape[1]
    tail = shards[0].shape[1] - LANES
    kinds = at.norm_raw.shape[0]
    kind = lax.broadcasted_iota(jnp.int32, (kinds, LANES), 0)
    spot = lax.broadcasted_iota(jnp.int32, (kinds, LANES), 1)
    put = (spot == kind + lead).astype(F32).astype(BF16)
    shards[0][:, tail:] = outer_sum(at.norm_raw[...].astype(BF16), put).astype(BF16)
    shards[0][:, 0:features] = at.s0[...].astype(BF16)
    shards[1][...] = raw[1][...].astype(BF16)
    at.padded[...] = jnp.zeros_like(at.padded)
    at.padded[:, 0:features] = at.patches[...]
    all_here()
    rows_of = [shard.shape[0] for shard in shards]

    def slab(which, node):
        rows = rows_of[which]
        return pl.ds(pl.multiple_of(node * rows, rows), rows)

    def whole_of(which, columns):
        part = weights[which][:, :, :, columns]
        return part.reshape(-1, part.shape[-1])

    own = [
        pltpu.make_async_copy(
            shards[which], weights[which].at[place.chip, place.core, slab(which, me), :], own_sem.at[which]
        )
        for which in range(6)
    ]
    for copy in own[:2]:
        copy.start()

    def remote(item, src, dst, slot, peer):
        return pltpu.make_async_remote_copy(
            src_ref=src,
            dst_ref=dst,
            send_sem=send_sem.at[item, slot],
            recv_sem=recv_sem.at[item, slot],
            device_id=peer,
            device_id_type=MESH,
        )

    def group(item, mask):
        which, begin, width, _ = items[item]
        return weights[which].at[flip(place.chip, mask), place.core, :, pl.ds(begin, width)]

    def along(item, sign, hop):
        which, begin, width, _ = items[item]
        columns = pl.ds(begin, width)
        there = weights[which].at[place.chip, place.core, slab(which, me - sign * (hop - 1)), columns]
        return remote(
            item,
            shards[which].at[:, columns] if hop == 1 else there,
            there,
            chips + 1 + hop - 1 + (narrow - 1 if sign < 0 else 0),
            (place.w, me + sign),
        )

    def has_next(sign):
        return me < narrow - 1 if sign > 0 else me >= 1

    def has_come(sign, hop):
        return me >= hop if sign > 0 else me < narrow - hop

    def start_if(condition, copy):
        @pl.when(condition)
        def _():
            copy.start()

        guarded.append((condition, copy))

    def bits_of(item):
        return place.bits if items[item][3] == 0 else place.bits[::-1]

    def across(item, mask, bit):
        return remote(item, group(item, mask), group(item, mask), mask ^ bit, place.across(bit))

    def to_twin(item):
        which, begin, width, _ = items[item]
        there = weights[which].at[:, place.core, :, pl.ds(begin, width)]
        return remote(item, there, there, chips, place.twin)

    plan = Planner()
    waited = set()

    def block_bytes(item):
        which, _, width, _ = items[item]
        return 2 * narrow * rows_of[which] * width

    def twin_event(item):
        to_twin(item).wait_recv()

    here = {}

    def onward(item, mask, number):
        bits = bits_of(item)
        size = block_bytes(item)
        for later in range(number, len(bits)):
            start(across(item, mask, bits[later]))
            coming = mask ^ bits[later]
            plan.transfer(
                bits[later], 2 * size / LINK, (item, coming), functools.partial(arrive, item, coming, later)
            )
        here[item] = here.get(item, 0) + 1
        if here[item] == chips:
            start(to_twin(item))
            plan.transfer(-1, chips * size / TWIN_LINK, (item, chips), functools.partial(twin_event, item))

    def arrive(item, mask, number):
        across(item, mask ^ bits_of(item)[number], bits_of(item)[number]).wait_recv()
        onward(item, mask, number + 1)

    def begin_item(item):
        for sign in (1, -1):
            start_if(has_next(sign), along(item, sign, 1))
        line_transfer(item, 1)

    def line_transfer(item, hop):
        cost = 2 * block_bytes(item) / narrow / LINK
        key = (item, 0) if hop == narrow - 1 else (item, -hop)
        plan.transfer(0, cost, key, functools.partial(line_event, item, hop))

    def line_event(item, hop):
        if items[item][0] not in waited:
            waited.add(items[item][0])
            own[items[item][0]].wait()
        for sign in (1, -1):

            @pl.when(has_come(sign, hop))
            def _():
                along(item, sign, hop).wait_recv()

            if hop < narrow - 1:
                start_if(jnp.logical_and(has_come(sign, hop), has_next(sign)), along(item, sign, hop + 1))
        if hop < narrow - 1:
            line_transfer(item, hop + 1)
        else:
            onward(item, 0, 0)

    begun, ahead = [], [Z_EARLY]

    def refill():
        while len(begun) < total and plan.free.get(0, 0.0) < plan.now + ahead[-1]:
            begin_item(len(begun))
            begun.append(True)

    plan.refill = refill
    refill()
    assert all(items[item][0] < 2 for item in range(len(begun)))
    for which in range(2, 6):
        shards[which][...] = raw[which][...].astype(BF16)
        own[which].start()

    def need(which, columns=None):
        plan.need(
            [
                (index, key)
                for index, (owner, begin, width, _) in enumerate(items)
                if owner == which and (columns is None or (begin < columns[1] and begin + width > columns[0]))
                for key in range(chips + 1)
            ]
        )

    flushed = []

    def flush(ref):
        index = [vars(at)[name] is ref for name in outs].index(True)
        copy = pltpu.make_async_copy(ref, results[index], out_sem.at[index])
        copy.start()
        flushed.append(copy)

    def swap(src, dst, kind, step):
        return pltpu.make_async_remote_copy(
            src_ref=src,
            dst_ref=dst,
            send_sem=swap_send.at[kind, step],
            recv_sem=swap_recv.at[kind, step],
            device_id=place.along(step),
            device_id_type=MESH,
        )

    gains = at.gains
    embedded, mid, last = at.embedded, at.mid, at.last
    normed, hidden, wave = at.normed, at.hidden, at.wave
    away, qkv, heads_out, returned = at.away, at.qkv, at.heads_out, at.returned

    def turn(dest, source):
        dest[...] = source[...].T
        flush(dest)

    plan.later(2.0, lambda: spread_weights(at.render_w, at.spread))
    plan.later(3.0, lambda: count_pairs(at.pairs, at.counts))
    need(0)
    width = weights[0].shape[-1]
    kind = lax.broadcasted_iota(jnp.int32, (8, LANES), 0)
    spot = lax.broadcasted_iota(jnp.int32, (8, LANES), 1)
    pick = (spot == kind + lead).astype(F32).astype(BF16)
    gains[...] = back_mul(pick, whole_of(0, pl.ds(width - LANES, LANES)))
    flush(gains)
    flush(at.padded)

    def embed(block):
        cols = pl.ds(block, 256)
        rows = whole_of(0, pl.ds(0, width))[block : block + 256]
        embedded[:, cols] = back_mul(at.padded[...], rows)

    for block in range(0, D, 256):
        plan.work(0.5, functools.partial(embed, block))
    flush(embedded)

    def norm_rows(source, row, dest):
        step_rows = 32

        def one(step, carry):
            rows = pl.ds(pl.multiple_of(step * step_rows, step_rows), step_rows)
            dest[rows, :] = normalize(
                source[rows, :], gains[row : row + 1, :], gains[row + 3 : row + 4, :]
            ).astype(BF16)
            return carry

        lax.fori_loop(0, tokens // step_rows, one, 0)

    plan.work(2.0, lambda: norm_rows(embedded, 0, normed))
    turn_first = plan.later(2.0, lambda: turn(at.t1, normed))
    piece = 2 * (narrow - 1) * 2 * tokens * head_width / LINK

    def project(part, step):
        owner = lax.rem(me + step, narrow)
        offset = pl.multiple_of(part * D + owner * head_width, LANES)
        value = matmul(normed[...], whole_of(1, pl.ds(offset, head_width))).astype(BF16)
        if step:
            away[step - 1, part] = value
            start(swap(away.at[step - 1, part], qkv.at[me, part], part, step))
        else:
            qkv[me, part] = value

    def swap_event(part):
        for step in range(1, narrow):
            swap(away.at[step - 1, part], qkv.at[me, part], part, step).wait_recv()

    for part in range(3):
        need(1, (part * D, part * D + D))
        for step in list(range(1, narrow)) + [0]:
            plan.work(0.7, functools.partial(project, part, step))
        plan.transfer(0, piece, (-1, part), functools.partial(swap_event, part))
    flush(at.w1)
    lane = lax.broadcasted_iota(jnp.int32, (1, LANES), 1)
    scale = HD ** (-0.5)
    length = narrow * tokens
    sides = LANES // HD

    def weigh(step):
        who = lax.rem(me + step, narrow)
        log_sums = jnp.zeros((tokens, LANES), F32)
        sums = jnp.ones((tokens, LANES), F32)
        for pair in range(head_width // LANES):
            lanes = pl.ds(pair * LANES, LANES)
            query = qkv[who, 0, :, lanes].astype(F32)
            key = qkv[:, 1, :, lanes].reshape(length, LANES)
            for side in range(sides):
                head = pair * sides + side
                own_query = (query * jnp.where(lane // HD == side, scale, 0.0)).astype(BF16)
                scores = back_mul(own_query, key)
                highest = jnp.max(scores, -1, keepdims=True)
                exponentials = jnp.exp(scores - highest)
                summed = jnp.sum(exponentials, -1, keepdims=True)
                at.weighed[step, head] = exponentials.astype(BF16)
                log_sums = jnp.where(lane == head, highest + jnp.log(summed), log_sums)
                sums = jnp.where(lane == head, summed, sums)
        at.log_sums[who] = log_sums
        at.weigh_sums[step] = sums

    def attend(step):
        who = lax.rem(me + step, narrow)
        for pair in range(head_width // LANES):
            lanes = pl.ds(pair * LANES, LANES)
            value = qkv[:, 2, :, lanes].reshape(length, LANES)
            out = jnp.zeros((tokens, LANES), F32)
            for side in range(sides):
                head = pair * sides + side
                part = matmul(at.weighed[step, head], value) / at.weigh_sums[step, :, head : head + 1]
                out = jnp.where(lane // HD == side, part, out)
            heads_out[who, :, lanes] = out.astype(BF16)
        if step:
            start(swap(heads_out.at[who], returned.at[me], 3, step))
        else:
            returned[me] = heads_out[who]

    steps = list(range(1, narrow)) + [0]
    ahead.append(Z_LATE)
    plan.need([(-1, 0), (-1, 1)])
    for step in steps:
        plan.work(2.7, functools.partial(weigh, step))
    plan.need([(-1, 2)])
    flush(qkv)

    def return_event(step):
        return lambda: swap(heads_out.at[me], returned.at[me], 3, step).wait_recv()

    for step in steps:
        plan.work(0.9, functools.partial(attend, step))
        if step:
            plan.transfer(0, piece / (narrow - 1), (-2, step), return_event(step))
    flush(heads_out)
    flush(at.log_sums)
    need(2)
    plan.need([(-2, step) for step in range(1, narrow)])

    def merge(block):
        cols = pl.ds(block, 256)
        value = embedded[:, cols]
        weight = whole_of(2, cols)
        for source in range(narrow):
            value = value + matmul(returned[source], weight[source * head_width : (source + 1) * head_width])
        mid[:, cols] = value

    for block in range(0, D, 256):
        plan.work(0.7, functools.partial(merge, block))
    flush(at.w2)
    flush(mid)
    plan.force(turn_first)
    plan.work(2.0, lambda: norm_rows(mid, 1, normed))

    def turn_returned():
        for source in range(narrow):
            at.t2[pl.ds(source * head_width, head_width), :] = returned[source].T
        flush(at.t2)

    plan.later(2.0, turn_returned)
    turn_second = plan.later(2.0, lambda: turn(at.t3, normed))

    ff = weights[3].shape[-1]
    tile = wave.shape[1]
    slopes = at.slopes

    def expand(block):
        wave[...] = matmul(normed[...], whole_of(3, pl.ds(block, tile)))

        def bend(step, carry):
            rows = pl.ds(pl.multiple_of(step * 32, 32), 32)
            x = wave[rows, :]
            half = 0.5 * (1.0 + lax.erf(x * (0.5**0.5)))
            hidden[rows, pl.ds(block, tile)] = (x * half).astype(BF16)
            bell = jnp.exp(-0.5 * x * x) * 0.3989422804014327
            slopes[rows, pl.ds(block, tile)] = (half + x * bell).astype(BF16)
            return carry

        lax.fori_loop(0, tokens // 32, bend, 0)

    for block in range(0, ff, tile):
        need(3, (block, block + tile))
        plan.work(2.5, functools.partial(expand, block))
    flush(at.w3)
    flush(slopes)
    flush(hidden)

    def shrink(block):
        cols = pl.ds(block, 256)
        last[:, cols] = mid[:, cols] + matmul(hidden[...], whole_of(4, cols))

    for block in range(0, D, 256):
        need(4, (block, block + 256))
        plan.work(1.0, functools.partial(shrink, block))
    flush(at.w4)
    flush(last)
    plan.force(turn_second)
    plan.work(2.0, lambda: norm_rows(last, 2, normed))
    need(5)

    def unpatch(block):
        cols = pl.ds(block, 256)
        at.gaussians[:, cols] = matmul(normed[...], whole_of(5, cols))

    for block in range(0, weights[5].shape[-1], 256):
        plan.work(0.7, functools.partial(unpatch, block))
    flush(at.w5)
    for entry in list(plan.spare):
        plan.force(entry)

    def draw():
        render_block(
            at.gaussians, at.spread, at.wanted, at.valid, at.counts, at.view, at.total, at.gauss, at.term, at.feat, at.dfeat
        )

    plan.work(4.0, draw)
    flush(at.gauss)
    flush(at.term)
    plan.later(2.0, lambda: turn(at.t5, normed))
    plan.finish()
    for copy in started:
        copy.wait_send()
    for condition, copy in guarded:

        @pl.when(condition)
        def _():
            copy.wait_send()

    for copy in flushed:
        copy.wait()


def forward_all(shards, norms, patches, scene, wide, narrow):
    tokens = patches.shape[0]
    features, kinds = patches.shape[1], norms.shape[0]
    lead = features % LANES
    widths = [-(-(features + kinds) // LANES) * LANES] + [shard.shape[1] for shard in shards[1:]]
    heights = [shard.shape[0] * wide * narrow for shard in shards]
    ff = widths[3]
    chips = wide // 2
    quads, slots_t = tokens // NVIEW, scene[0].shape[0]
    head_width = D // narrow
    items = forward_plan(widths)
    slots = chips + 1 + 2 * (narrow - 1)
    full = [((chips, 2, height // wide, width), BF16) for height, width in zip(heights, widths)]
    shapes = dict(
        w1=full[1],
        w2=full[2],
        w3=full[3],
        w4=full[4],
        w5=full[5],
        gains=((8, D), F32),
        embedded=((tokens, D), F32),
        mid=((tokens, D), F32),
        last=((tokens, D), F32),
        slopes=((tokens, ff), BF16),
        t1=((D, tokens), BF16),
        t2=((D, tokens), BF16),
        t3=((D, tokens), BF16),
        hidden=((tokens, ff), BF16),
        t5=((D, tokens), BF16),
        qkv=((narrow, 3, tokens, head_width), BF16),
        heads_out=((narrow, tokens, head_width), BF16),
        log_sums=((narrow, tokens, LANES), F32),
        padded=((tokens, widths[0]), BF16),
        gauss=((tokens, widths[5]), BF16),
        term=((8, LANES), F32),
    )
    ins = tuple(dict(s0=0, s1=0, s2=0, s3=0, s4=0, s5=0, norm_raw=0, patches=0))
    ins += tuple(dict(render_w=0, wanted=0, valid=0, pairs=0, view=0, total=0))
    outs = tuple(shapes)
    extras = dict(
        first_weight=pltpu.VMEM(*full[0]),
        c0=pltpu.VMEM((shards[0].shape[0], widths[0]), BF16),
        c1=pltpu.VMEM(shards[1].shape, BF16),
        c2=pltpu.VMEM(shards[2].shape, BF16),
        c3=pltpu.VMEM(shards[3].shape, BF16),
        c4=pltpu.VMEM(shards[4].shape, BF16),
        c5=pltpu.VMEM(shards[5].shape, BF16),
        gaussians=pltpu.VMEM((tokens, widths[5]), F32),
        spread=pltpu.VMEM((NVIEW * PP, slots_t * PP), F32),
        counts=pltpu.VMEM((2 * quads, slots_t * PP), F32),
        feat=pltpu.VMEM((5 * quads, NVIEW * PP), F32),
        dfeat=pltpu.VMEM((5 * quads, NVIEW * PP), F32),
        normed=pltpu.VMEM((tokens, D), BF16),
        wave=pltpu.VMEM((tokens, 512), F32),
        away=pltpu.VMEM((narrow - 1, 3, tokens, head_width), BF16),
        weighed=pltpu.VMEM((narrow, head_width // HD, tokens, narrow * tokens), BF16),
        weigh_sums=pltpu.VMEM((narrow, tokens, LANES), F32),
        returned=pltpu.VMEM((narrow, tokens, head_width), BF16),
        own_sem=pltpu.SemaphoreType.DMA((6,)),
        send_sem=pltpu.SemaphoreType.DMA((len(items), slots)),
        recv_sem=pltpu.SemaphoreType.DMA((len(items), slots)),
        swap_send=pltpu.SemaphoreType.DMA((4, narrow)),
        swap_recv=pltpu.SemaphoreType.DMA((4, narrow)),
        out_sem=pltpu.SemaphoreType.DMA((len(outs),)),
    )
    scratch = outs + tuple(extras)
    anywhere = pl.BlockSpec(memory_space=pl.ANY)
    results = pl.pallas_call(
        functools.partial(forward_kernel, items, wide, narrow, lead, ins, outs, scratch),
        out_shape=[jax.ShapeDtypeStruct(*shapes[name]) for name in outs],
        in_specs=[pl.BlockSpec(memory_space=pltpu.VMEM)] * (len(ins) - 2)
        + [pl.BlockSpec(memory_space=pltpu.SMEM)] * 2,
        out_specs=[anywhere] * len(outs),
        scratch_shapes=[pltpu.VMEM(*shapes[name]) for name in outs] + list(extras.values()),
        compiler_params=pltpu.CompilerParams(
            collective_id=0, has_side_effects=True, vmem_limit_bytes=63 * MIB
        ),
        name="forward",
    )(*shards, norms, patches, *scene)
    results = [result.reshape(-1, result.shape[-1]) for result in results[:5]] + list(results[5:])
    return Bag(zip(outs, results))


def backward_plan(widths, pairs):
    items = []
    for which, cuts in ((5, 1), (4, 2), (3, 2), (2, 1), (1, pairs), (0, 1)):
        size = widths[which] // cuts
        for cut in range(cuts):
            for side, (start, width) in enumerate(column_halves(size)):
                items.append((which, cut * size + start, width, side))
    return items


def tile_of(width):
    for tile in (512, 384, 256, 128):
        if width % tile == 0:
            return tile
    return width


def backward_kernel(items, wide, narrow, lead, ins, scratch, *refs):
    src = Bag(zip(ins, refs))
    refs = refs[len(ins) :]
    sums, totals, refs = refs[:6], refs[6], list(refs[7:])
    at = Bag(zip(scratch, refs))
    place = Place(wide, narrow)
    chips, me = place.chips, place.n
    total = len(items)
    refs = refs[len(scratch) :]
    held = [refs.pop(0) for _ in items]
    passed = [[refs.pop(0) for _ in place.bits] for _ in items]
    final = [refs.pop(0) for _ in items]
    spare = [refs.pop(0) for _ in range(6)]
    tokens = src.patches.shape[0]
    head_width = D // narrow
    length = narrow * tokens
    reach = narrow * LANES
    send_sem, recv_sem, tile_send, tile_recv = at.send_sem, at.recv_sem, at.tile_send, at.tile_recv
    swap_send, swap_recv, in_sem, ring_sem = at.swap_send, at.swap_recv, at.in_sem, at.ring_sem
    gains, norms, extra = src.gains, at.norms, at.extra
    stash, d_res, d_norm = at.stash, at.d_res, at.d_norm
    mixed, merge_low, expand_low, shrink_low = at.mixed, at.merge_low, at.expand_low, at.shrink_low

    peers = [(lax.rem(place.w + step, wide), place.n) for step in range(1, wide)]
    peers += [place.along(step) for step in range(1, narrow)]
    all_here = greet(peers)

    loaded = [name for name in ins if name in scratch]

    def load(ref):
        index = [vars(at)[name] is ref for name in loaded].index(True)
        return pltpu.make_async_copy(vars(src)[loaded[index]], ref, in_sem.at[index])

    def load_stash(ref):
        return pltpu.make_async_copy(ref, stash, in_sem.at[len(loaded)])

    def ring(ref, slots, rows, columns, index, row):
        slot = lax.rem(index, slots.shape[0])
        return pltpu.make_async_copy(
            ref.at[pl.ds(pl.multiple_of(row, rows), rows), :],
            slots.at[slot, pl.ds(0, rows), pl.ds(0, columns)],
            ring_sem.at[0 if slots is at.tall else 1, slot],
        )

    slope_rows = at.tall.shape[1]
    tall, long = at.tall.shape[0], at.long.shape[0]

    def slope_load(index):
        slot = lax.rem(index, tall)
        return pltpu.make_async_copy(
            src.slopes.at[:, pl.ds(pl.multiple_of(index * slope_rows, slope_rows), slope_rows)],
            at.slope_slots.at[slot],
            ring_sem.at[2, slot],
        )

    u_rows, u_cols = 256, src.w5.shape[1]
    load_stash(src.last).start()
    for index in range(tall):
        ring(src.w5, at.tall, u_rows, u_cols, index, index * u_rows).start()
        slope_load(index).start()
    wide_rows = at.long.shape[1]
    for index in range(long):
        ring(src.w3, at.long, wide_rows, src.w3.shape[1], index, index * wide_rows).start()
    for name in loaded:
        load(vars(at)[name]).start()

    all_here()

    started, guarded = [], []

    def start(copy):
        copy.start()
        started.append(copy)

    lefts = [at.embed_t, at.t1, at.t2, at.t3, at.shrink_t, at.t5]
    rights = [src.patches, mixed, merge_low, expand_low, at.hidden, src.gauss]

    def remote(item, src, dst, slot, peer):
        return pltpu.make_async_remote_copy(
            src_ref=src,
            dst_ref=dst,
            send_sem=send_sem.at[item, slot],
            recv_sem=recv_sem.at[item, slot],
            device_id=peer,
            device_id_type=MESH,
        )

    def bits_of(item):
        return place.bits[::-1] if items[item][3] == 0 else place.bits

    def groups_of(item):
        size = max(1, 512 // (narrow * spare[items[item][0]].shape[2]))
        if items[item][0] == 4:
            size = chips
        masks = list(range(chips))
        if bits_of(item) and bits_of(item)[0] > 1:
            masks = masks[chips // 2 :] + masks[: chips // 2]
        return [sorted(masks[at_mask : at_mask + size]) for at_mask in range(0, chips, size)]

    def product(item, masks, core, into, plus):
        which, begin, width, _ = items[item]
        left, right = lefts[which], rights[which]
        rows = into.shape[-2]
        span = narrow * rows
        tile = tile_of(width)
        if which == 4:
            size = into.shape[-1]
            for mask in masks:
                column = ((flip(place.chip, mask) * 2 + core) * narrow) * size
                rhs = right[:, pl.ds(pl.multiple_of(column, narrow * size), narrow * size)]
                value = jnp.dot(left[begin : begin + width, :], rhs, preferred_element_type=F32)
                for node in range(narrow):
                    piece = value[:, node * size : (node + 1) * size]
                    if plus:
                        piece = piece + into[mask, node].astype(F32)
                    into[mask, node] = piece.astype(BF16)
            return
        firsts = [((flip(place.chip, mask) * 2 + core) * narrow) * rows for mask in masks]
        with_extra = which == 0 and begin + width == right.shape[1]
        assert not with_extra or tile == width
        if which == 1:
            tile = LANES * 2

        def one(step, carry):
            offset = pl.multiple_of(begin + step * tile, LANES)
            local = pl.multiple_of(step * tile, LANES)
            if which != 1:
                rhs = right[:, pl.ds(offset, tile)]
            else:
                part, inside = offset // reach, pl.multiple_of(offset % reach, LANES)
                rhs = right[part // 3, part % 3, :, pl.ds(inside, tile)]
            spots = [pl.ds(pl.multiple_of(first, span), span) for first in firsts]
            lhs = jnp.concatenate([left[spot, :] for spot in spots], 0)
            value = jnp.dot(lhs, rhs, preferred_element_type=F32)
            for index, mask in enumerate(masks):
                piece = value[index * span : (index + 1) * span]
                if with_extra:
                    blank = jnp.zeros((span, tile - LANES), F32)
                    piece = piece + jnp.concatenate([blank, extra[spots[index], :]], 1)
                piece = piece.reshape(narrow, rows, tile)
                if plus:
                    piece = piece + into[mask, :, :, pl.ds(local, tile)].astype(F32)
                into[mask, :, :, pl.ds(local, tile)] = piece.astype(BF16)
            return carry

        lax.fori_loop(0, width // tile, one, 0)

    last_sent = {}
    plan = Planner()

    def to_twin(item, masks):
        which, _, width, _ = items[item]
        some = pl.ds(masks[0], len(masks))
        own = spare[which].at[some] if which == 4 else spare[which].at[some, :, :, pl.ds(0, width)]
        return remote(item, own, held[item].at[some], masks[0], place.twin)

    def across(item, mask, bit, number, slot):
        return remote(
            item, held[item].at[mask], passed[item][number].at[slot], chips + mask, place.across(bit)
        )

    def relayed(item):
        return items[item][0] in RELAYED

    def hopping(item, sign, hop):
        count = narrow - hop
        first = hop if sign > 0 else 0
        node = hop if sign > 0 else narrow - 1 - hop
        return remote(
            item,
            held[item].at[0, pl.ds(first, count)],
            final[item].at[pl.ds(first + (1 if sign > 0 else 0), count)],
            2 * chips + (0 if sign > 0 else 1),
            (place.w, node),
        )

    def send_hop(item, sign, hop):
        sender = me == (hop - 1 if sign > 0 else narrow - hop)

        @pl.when(sender)
        def _():
            hopping(item, sign, hop).start()

        guarded.append((sender, hopping(item, sign, hop)))

    def hop_event(item, hop):
        count = narrow - hop - 1
        for sign in (1, -1):
            first = hop + 1 if sign > 0 else 0
            shift = 1 if sign > 0 else 0

            @pl.when(me == (hop if sign > 0 else narrow - 1 - hop))
            def _():
                hopping(item, sign, hop).wait_recv()
                if count:
                    mine, theirs = pl.ds(first, count), pl.ds(first + shift, count)
                    value = held[item][0, mine].astype(F32) + final[item][theirs].astype(F32)
                    held[item][0, mine] = value.astype(BF16)

            if count:
                send_hop(item, sign, hop + 1)
        if count:
            hop_transfer(item, hop + 1)
        else:
            finish(item)

    def hop_transfer(item, hop):
        cost = (narrow - hop) * 2 * block_bytes(item) / narrow / LINK
        event = functools.partial(hop_event, item, hop)
        plan.transfer(0 if hop == 1 else 100 + hop, cost, (item, -hop, 0), event)

    def along(item, step):
        target = place.along(step)
        return remote(
            item,
            held[item].at[0, target[1]],
            final[item].at[narrow - step - 1],
            2 * chips + narrow - step - 1,
            target,
        )

    def leaves(item, mask):
        bits = bits_of(item)
        return min([number for number, bit in enumerate(bits) if mask & bit], default=len(bits))

    def slot_of(item, mask, number):
        bits = bits_of(item)
        kept = [m for m in range(chips) if not any(m & bit for bit in bits[: number + 1])]
        return kept.index(mask)

    def add_into(dest, dest_at, src, src_at):
        dest[dest_at] = (dest[dest_at].astype(F32) + src[src_at].astype(F32)).astype(BF16)

    def block_bytes(item):
        _, nodes, rows, width = held[item].shape
        return 2 * nodes * rows * width

    def push(which, pair=None):
        for item, (owner, begin, _, _) in enumerate(items):
            if owner != which or (pair is not None and begin // (3 * reach) != pair):
                continue
            for masks in groups_of(item):
                cost = len(masks) * block_bytes(item) / 1e6
                plan.work(cost, functools.partial(push_some, item, masks))

    def push_some(item, masks):
        which = items[item][0]
        for key in [key for key in last_sent if key[0] == which and set(key[1]) & set(masks)]:
            last_sent.pop(key).wait_send()
        product(item, masks, 1 - place.core, spare[which], False)
        copy = to_twin(item, masks)
        copy.start()
        last_sent[which, tuple(masks)] = copy
        cost = len(masks) * block_bytes(item) / TWIN_LINK
        plan.transfer(-1, cost, (item, 0, masks[0]), functools.partial(own_event, item, masks))

    def own_event(item, masks):
        to_twin(item, masks).wait_recv()
        product(item, masks, place.core, held[item], True)
        plan.now += len(masks) * block_bytes(item) / 1e6
        plan.done.update((item, 0, mask) for mask in masks)
        for mask in masks:
            onward(item, mask, 0)

    def onward(item, mask, number):
        bits = bits_of(item)
        if number == len(bits):
            lined.append(item)
            refill()
        elif leaves(item, mask) == number:
            kept = mask ^ bits[number]
            start(across(item, mask, bits[number], number, slot_of(item, kept, number)))
            plan.transfer(
                bits[number],
                2 * block_bytes(item) / LINK,
                (item, 1 + number, kept),
                functools.partial(sum_event, item, kept, number),
            )

    lined = []

    def refill():
        while lined and plan.free.get(0, 0.0) < plan.now + Z_AHEAD:
            item = lined.pop(0)
            if relayed(item):
                for sign in (1, -1):
                    send_hop(item, sign, 1)
                hop_transfer(item, 1)
                continue
            for step in range(1, narrow):
                start(along(item, step))
            cost = 2 * (narrow // 2) ** 2 * block_bytes(item) / narrow / LINK
            plan.transfer(0, cost, (item, -1, 0), functools.partial(finish, item))

    plan.refill = refill

    def sum_event(item, mask, number):
        plan.need([(item, before, mask) for before in range(number + 1)])
        bit = bits_of(item)[number]
        slot = slot_of(item, mask, number)
        across(item, mask ^ bit, bit, number, slot).wait_recv()
        add_into(held[item], mask, passed[item][number], slot)
        plan.now += block_bytes(item) / 8e5
        onward(item, mask, number + 1)

    at.squares[...] = jnp.zeros_like(at.squares)

    def finish(item):
        which, begin, width, _ = items[item]
        value = held[item][0, me].astype(F32)
        if relayed(item):
            value = value + jnp.where(me >= 1, final[item][me + 1].astype(F32), 0.0)
            value = value + jnp.where(me < narrow - 1, final[item][me].astype(F32), 0.0)
        else:
            for step in range(1, narrow):
                along(item, step).wait_recv()
            for slot in range(narrow - 1):
                value = value + final[item][slot].astype(F32)
        columns = pl.ds(0, value.shape[1])
        at.squares[:, columns] += jnp.sum(value * value, 0, keepdims=True)
        if which == 1:
            for shift in range(0, width, LANES):
                part, spot = (begin + shift) // reach, (begin + shift) % reach
                column = part % 3 * D + spot // LANES * head_width + part // 3 * LANES
                sums[which][:, pl.ds(column, LANES)] = value[:, shift : shift + LANES]
        elif which == 4:
            sums[which][pl.ds(begin, width), :] = value
        else:
            sums[which][:, pl.ds(begin, width)] = value

    norms[...] = jnp.zeros_like(norms)

    def norm_back(row, low, add):
        step_rows = 32

        def one(step, carry):
            rows = pl.ds(pl.multiple_of(step * step_rows, step_rows), step_rows)
            values = stash[rows, :]
            upper = d_norm[rows, :]
            centred = values - jnp.mean(values, -1, keepdims=True)
            rate = lax.rsqrt(jnp.mean(centred * centred, -1, keepdims=True) + 1e-05)
            unit = centred * rate
            norms[row : row + 1, :] += jnp.sum(upper * unit, 0, keepdims=True)
            norms[row + 3 : row + 4, :] += jnp.sum(upper, 0, keepdims=True)
            scaled = upper * gains[row : row + 1, :]
            inner = scaled - jnp.mean(scaled, -1, keepdims=True)
            inner = rate * (inner - unit * jnp.mean(scaled * unit, -1, keepdims=True))
            if add:
                inner = inner + d_res[rows, :]
            d_res[rows, :] = inner
            low[rows, :] = inner.astype(BF16)
            return carry

        lax.fori_loop(0, tokens // step_rows, one, 0)

    def loop_work(cost, count, pieces, body):
        for piece in range(pieces):
            low, high = count * piece // pieces, count * (piece + 1) // pieces
            plan.work(cost / pieces, functools.partial(lax.fori_loop, low, high, body, 0))

    load(at.t5).wait()
    push(5)
    load_stash(src.last).wait()
    count = D // u_rows
    tall_rows = slope_rows

    def through_unpatch(index, carry):
        ring(src.w5, at.tall, u_rows, u_cols, index, index * u_rows).wait()
        slot = at.tall.at[lax.rem(index, tall)]
        offset = pl.multiple_of(index * u_rows, u_rows)
        d_norm[:, pl.ds(offset, u_rows)] = back_mul(src.gauss[...], slot[0:u_rows, 0:u_cols])

        @pl.when(index + tall < count)
        def _():
            ring(src.w5, at.tall, u_rows, u_cols, index + tall, (index + tall) * u_rows).start()

        return carry

    loop_work(2.5, count, 1, through_unpatch)
    for index in range(tall):
        ring(src.w4, at.tall, tall_rows, D, index, index * tall_rows).start()
    plan.work(2.5, lambda: norm_back(2, shrink_low, False))
    load_stash(src.mid).start()
    load(at.hidden).wait()

    def turn_shrink():
        at.shrink_t[...] = shrink_low[...].T

    plan.work(2.0, turn_shrink)
    push(4)
    ff = src.w3.shape[1]
    slabs = ff // tall_rows

    def through_shrink(index, carry):
        ring(src.w4, at.tall, tall_rows, D, index, index * tall_rows).wait()
        slope_load(index).wait()
        slot = lax.rem(index, tall)
        value = back_mul(shrink_low[...], at.tall[slot])
        value = value * at.slope_slots[slot].astype(F32)
        expand_low[:, pl.ds(pl.multiple_of(index * tall_rows, tall_rows), tall_rows)] = value.astype(BF16)

        @pl.when(index + tall < slabs)
        def _():
            ring(src.w4, at.tall, tall_rows, D, index + tall, (index + tall) * tall_rows).start()
            slope_load(index + tall).start()

        return carry

    loop_work(6.0, slabs, 2, through_shrink)
    owners = [lax.rem(me + step, narrow) for step in list(range(1, narrow)) + [0]]
    for index in range(min(tall, narrow)):
        ring(src.w2, at.tall, head_width, D, index, owners[index] * head_width).start()
    load(at.t3).wait()

    def through_expand(index, carry):
        ring(src.w3, at.long, wide_rows, ff, index, index * wide_rows).wait()
        offset = pl.multiple_of(index * wide_rows, wide_rows)
        d_norm[:, pl.ds(offset, wide_rows)] = back_mul(expand_low[...], at.long[lax.rem(index, long)])

        @pl.when(index + long < D // wide_rows)
        def _():
            ring(src.w3, at.long, wide_rows, ff, index + long, (index + long) * wide_rows).start()

        return carry

    loop_work(5.0, D // wide_rows, 2, through_expand)
    for index in range(long):
        ring(src.w1, at.long, wide_rows, 3 * D, index, index * wide_rows).start()
    load_stash(src.mid).wait()
    plan.work(2.0, lambda: norm_back(1, merge_low, True))
    load_stash(src.embedded).start()

    def swap(src, dst, kind, step):
        return pltpu.make_async_remote_copy(
            src_ref=src,
            dst_ref=dst,
            send_sem=swap_send.at[kind, step],
            recv_sem=swap_recv.at[kind, step],
            device_id=place.along(step),
            device_id_type=MESH,
        )

    d_heads, away = at.d_heads, at.away
    piece = 2 * (narrow - 1) * 2 * tokens * head_width / LINK

    def head_event():
        for step in range(1, narrow):
            swap(away.at[step - 1], d_heads.at[me], 0, step).wait_recv()

    def through_merge(index, owner):
        ring(src.w2, at.tall, head_width, D, index, owner * head_width).wait()
        value = back_mul(merge_low[...], at.tall[index % tall, 0:head_width, :]).astype(BF16)
        if index < narrow - 1:
            away[index] = value
            start(swap(away.at[index], d_heads.at[me], 0, index + 1))
        else:
            d_heads[me] = value
        if index + tall < narrow:
            ring(src.w2, at.tall, head_width, D, index + tall, owners[index + tall] * head_width).start()

    for index, owner in enumerate(owners):
        plan.work(0.7, functools.partial(through_merge, index, owner))
    plan.transfer(0, piece, (-1, 0, 0), head_event)
    load(at.t2).wait()
    push(3)
    push(2)
    load(at.qkv).wait()
    load(at.heads_out).wait()
    load(at.log_sums).wait()
    plan.need([(-1, 0, 0)])

    qkv, heads_out, log_sums, parts = at.qkv, at.heads_out, at.log_sums, at.parts
    key_t, key_acc, value_acc, query_acc = at.key_t, at.key_acc, at.value_acc, at.query_acc
    lane = lax.broadcasted_iota(jnp.int32, (1, LANES), 1)
    sides = LANES // HD
    scale = HD ** (-0.5)
    choose = lax.broadcasted_iota(jnp.int32, (8, LANES), 1) // HD
    choose = (choose == lax.broadcasted_iota(jnp.int32, (8, LANES), 0)).astype(F32)

    def part_swap(pair, step):
        lanes = pl.ds(pair * LANES, LANES)
        who = lax.rem(me + step, narrow)
        return swap(
            parts.at[who, :, :, lanes],
            mixed.at[pair, :, :, pl.ds(pl.multiple_of(me * LANES, LANES), LANES)],
            1 + pair,
            step,
        )

    pushed_pairs = []
    load(at.t1).wait()

    def part_event(pair):
        for step in range(1, narrow):
            part_swap(pair, step).wait_recv()

    for pair in range(head_width // LANES):
        lanes = pl.ds(pair * LANES, LANES)
        key_t[...] = qkv[:, 1, :, lanes].reshape(length, LANES).T
        key_acc[...] = jnp.zeros_like(key_acc)
        value_acc[...] = jnp.zeros_like(value_acc)
        def one_block(step, lanes=lanes, pair=pair):
            who = lax.rem(me + step, narrow)
            query = qkv[who, 0, :, lanes].astype(F32)
            upper = d_heads[who, :, lanes].astype(F32)
            kept = heads_out[who, :, lanes].astype(F32)
            delta = lax.dot_general(
                choose,
                upper * kept,
                (((1,), (1,)), ((), ())),
                precision=HIGHEST,
                preferred_element_type=F32,
            )
            log_rows = log_sums[who].T[pair * sides : (pair + 1) * sides, :]
            masks = [jnp.where(lane // HD == side, 1.0, 0.0) for side in range(sides)]
            own_query = jnp.concatenate([query * (scale * mask) for mask in masks], 0).astype(BF16)
            own_upper = jnp.concatenate([upper * mask for mask in masks], 0).astype(BF16)
            log_row = jnp.concatenate([log_rows[side : side + 1, :] for side in range(sides)], 1)
            delta_row = jnp.concatenate([delta[side : side + 1, :] for side in range(sides)], 1)
            query_acc[...] = jnp.zeros_like(query_acc)

            at_once = max(1, KEY_ROWS // tokens)
            for source in range(0, narrow, at_once):
                rows = pl.ds(source * tokens, at_once * tokens)
                some = pl.ds(source, at_once)
                key = qkv[some, 1, :, lanes].reshape(at_once * tokens, LANES)
                value = qkv[some, 2, :, lanes].reshape(at_once * tokens, LANES)
                probs = jnp.exp(back_mul(key, own_query) - log_row)
                d_probs = back_mul(value, own_upper)
                d_scores = (probs * (d_probs - delta_row)).astype(BF16)
                value_acc[rows, :] += matmul(probs.astype(BF16), own_upper)
                key_acc[rows, :] += matmul(d_scores, own_query)
                turned = matmul(key_t[:, rows], d_scores)
                for side in range(sides):
                    spot = slice(side * HD, (side + 1) * HD)
                    query_acc[spot, :] += turned[spot, side * tokens : (side + 1) * tokens]

            parts[who, 0, :, lanes] = (query_acc[...].T * scale).astype(BF16)
        for step in range(narrow):
            plan.work(3.0, functools.partial(one_block, step))
            for earlier in range(pair):
                if earlier not in pushed_pairs and (-2, 0, earlier) in plan.done:
                    pushed_pairs.append(earlier)
                    push(1, earlier)
        for source in range(narrow):
            rows = pl.ds(source * tokens, tokens)
            parts[source, 1, :, lanes] = key_acc[rows, :].astype(BF16)
            parts[source, 2, :, lanes] = value_acc[rows, :].astype(BF16)
        for step in range(1, narrow):
            start(part_swap(pair, step))
        plan.now += 1.0
        plan.transfer(0, 1.5 * piece, (-2, 0, pair), functools.partial(part_event, pair))
        mixed[pair, :, :, pl.ds(pl.multiple_of(me * LANES, LANES), LANES)] = parts[me, :, :, lanes]
    for pair in range(head_width // LANES):
        if pair not in pushed_pairs:
            plan.need([(-2, 0, pair)])
            push(1, pair)

    def through_mixer(index, carry):
        ring(src.w1, at.long, wide_rows, 3 * D, index, index * wide_rows).wait()
        slot = lax.rem(index, long)
        value = jnp.zeros((tokens, wide_rows), F32)
        for pair in range(head_width // LANES):
            for part in range(3):
                columns = [part * D + owner * head_width + pair * LANES for owner in range(narrow)]
                weight = [at.long[slot, :, column : column + LANES] for column in columns]
                value = value + back_mul(mixed[pair, part], jnp.concatenate(weight, 1))
        d_norm[:, pl.ds(pl.multiple_of(index * wide_rows, wide_rows), wide_rows)] = value

        @pl.when(index + long < D // wide_rows)
        def _():
            ring(src.w1, at.long, wide_rows, 3 * D, index + long, (index + long) * wide_rows).start()

        return carry

    plan.work(4.0, lambda: lax.fori_loop(0, D // wide_rows, through_mixer, 0))
    load_stash(src.embedded).wait()
    plan.work(3.0, lambda: norm_back(0, at.embed_low, True))
    at.embed_t[...] = at.embed_low[...].T
    turned = jnp.concatenate([norms[...], jnp.zeros((LANES - 8, D), F32)], 0).T
    at.extra[...] = pltpu.roll(turned, lead, 1)
    push(0)
    plan.finish()

    rows = lax.broadcasted_iota(jnp.int32, (8, LANES), 0)
    wide_tiles, narrow_tiles = at.wide_tiles, at.narrow_tiles
    wide_tiles[place.w] = jnp.where(rows == 0, src.term[...], jnp.sum(at.squares[...]))

    def tile_copy(buffer, index, slot, peer):
        return pltpu.make_async_remote_copy(
            src_ref=buffer.at[index],
            dst_ref=buffer.at[index],
            send_sem=tile_send.at[slot],
            recv_sem=tile_recv.at[slot],
            device_id=peer,
            device_id_type=MESH,
        )

    for step in range(1, wide):
        start(tile_copy(wide_tiles, place.w, step - 1, (lax.rem(place.w + step, wide), place.n)))
    for step in range(1, wide):
        tile_copy(wide_tiles, place.w, step - 1, (lax.rem(place.w + step, wide), place.n)).wait_recv()
    whole = wide_tiles[0]
    for index in range(1, wide):
        whole = whole + wide_tiles[index]
    narrow_tiles[place.n] = whole
    for step in range(1, narrow):
        start(tile_copy(narrow_tiles, place.n, wide + step - 1, place.along(step)))
    for step in range(1, narrow):
        tile_copy(narrow_tiles, place.n, wide + step - 1, place.along(step)).wait_recv()
    whole = narrow_tiles[0]
    for index in range(1, narrow):
        whole = whole + narrow_tiles[index]
    totals[...] = whole
    for copy in list(last_sent.values()) + started:
        copy.wait_send()
    for condition, copy in guarded:

        @pl.when(condition)
        def _():
            copy.wait_send()


def backward_all(kept, patches, gauss, term, lead, wide, narrow):
    tokens = patches.shape[0]
    chips = wide // 2
    weights = [kept.w1, kept.w2, kept.w3, kept.w4, kept.w5]
    heights = [D] + [weight.shape[0] for weight in weights]
    widths = [patches.shape[1]] + [weight.shape[1] for weight in weights]
    rows = [height // (wide * narrow) for height in heights]
    head_width = D // narrow
    length = narrow * tokens
    items = backward_plan(widths, head_width // LANES)
    slots = 2 * chips + max(2, narrow - 1)
    streamed = dict(w1=kept.w1, w2=kept.w2, w3=kept.w3, w4=kept.w4, w5=kept.w5)
    streamed.update(last=kept.last, mid=kept.mid, embedded=kept.embedded, slopes=kept.slopes)
    loaded = dict(t5=kept.t5, hidden=kept.hidden, t3=kept.t3, t2=kept.t2, t1=kept.t1)
    loaded.update(qkv=kept.qkv, heads_out=kept.heads_out, log_sums=kept.log_sums)
    whole = dict(gains=kept.gains, patches=patches, gauss=gauss, term=term)
    operands = {**streamed, **loaded, **whole}
    shapes = [jax.ShapeDtypeStruct((rows[which], widths[which]), F32) for which in range(6)]
    shapes[4] = jax.ShapeDtypeStruct((D, rows[4]), F32)
    shapes.append(jax.ShapeDtypeStruct((8, LANES), F32))
    scratch = {name: pltpu.VMEM(value.shape, value.dtype) for name, value in loaded.items()}
    blocks = [(width, rows[which]) if which == 4 else (rows[which], width) for which, _, width, _ in items]
    scratch.update(
        squares=pltpu.VMEM((1, max(block[1] for block in blocks)), F32),
        embed_t=pltpu.VMEM((D, tokens), BF16),
        embed_low=pltpu.VMEM((tokens, D), BF16),
        shrink_t=pltpu.VMEM((D, tokens), BF16),
        stash=pltpu.VMEM((tokens, D), F32),
        d_res=pltpu.VMEM((tokens, D), F32),
        d_norm=pltpu.VMEM((tokens, D), F32),
        norms=pltpu.VMEM((8, D), F32),
        extra=pltpu.VMEM((D, LANES), F32),
        shrink_low=pltpu.VMEM((tokens, D), BF16),
        expand_low=pltpu.VMEM((tokens, widths[3]), BF16),
        merge_low=pltpu.VMEM((tokens, D), BF16),
        mixed=pltpu.VMEM((head_width // LANES, 3, tokens, narrow * LANES), BF16),
        tall=pltpu.VMEM((4, 256, D), BF16),
        long=pltpu.VMEM((2, 256, widths[3]), BF16),
        slope_slots=pltpu.VMEM((4, tokens, 256), BF16),
        d_heads=pltpu.VMEM((narrow, tokens, head_width), BF16),
        away=pltpu.VMEM((narrow - 1, tokens, head_width), BF16),
        parts=pltpu.VMEM((narrow, 3, tokens, head_width), BF16),
        key_t=pltpu.VMEM((LANES, length), BF16),
        key_acc=pltpu.VMEM((length, LANES), F32),
        value_acc=pltpu.VMEM((length, LANES), F32),
        query_acc=pltpu.VMEM((LANES, tokens), F32),
        wide_tiles=pltpu.VMEM((wide, 8, LANES), F32),
        narrow_tiles=pltpu.VMEM((narrow, 8, LANES), F32),
        send_sem=pltpu.SemaphoreType.DMA((len(items), slots)),
        recv_sem=pltpu.SemaphoreType.DMA((len(items), slots)),
        tile_send=pltpu.SemaphoreType.DMA((wide + narrow,)),
        tile_recv=pltpu.SemaphoreType.DMA((wide + narrow,)),
        swap_send=pltpu.SemaphoreType.DMA((1 + head_width // LANES, narrow)),
        swap_recv=pltpu.SemaphoreType.DMA((1 + head_width // LANES, narrow)),
        in_sem=pltpu.SemaphoreType.DMA((9,)),
        ring_sem=pltpu.SemaphoreType.DMA((3, 4)),
    )
    lists = [pltpu.VMEM((chips, narrow) + block, BF16) for block in blocks]
    for block in blocks:
        for bit in chip_bits(chips):
            lists.append(pltpu.VMEM((chips // (2 * bit), narrow) + block, BF16))
    for (which, _, _, _), block in zip(items, blocks):
        lists.append(pltpu.VMEM((narrow + (1 if which in RELAYED else -1),) + block, BF16))
    for which in range(6):
        widest = max(block for item, block in zip(items, blocks) if item[0] == which)
        lists.append(pltpu.VMEM((chips, narrow) + widest, BF16))
    vmem = pl.BlockSpec(memory_space=pltpu.VMEM)
    hbm = pl.BlockSpec(memory_space=pl.ANY)
    return pl.pallas_call(
        functools.partial(backward_kernel, items, wide, narrow, lead, tuple(operands), tuple(scratch)),
        out_shape=shapes,
        in_specs=[vmem if name in whole else hbm for name in operands],
        out_specs=[vmem] * len(shapes),
        scratch_shapes=list(scratch.values()) + lists,
        compiler_params=pltpu.CompilerParams(
            collective_id=1, has_side_effects=True, vmem_limit_bytes=63 * MIB
        ),
        name="backward",
    )(*operands.values())


def spread_weights(source, dest):
    for slot in range(source.shape[0]):
        for view in range(source.shape[1]):
            dest[view * PP : (view + 1) * PP, slot * PP : (slot + 1) * PP] = source[slot, view]


def count_pairs(pair_ref, counts):
    quads, span = counts.shape[0] // 2, counts.shape[1]
    some = 512
    counts[...] = jnp.zeros_like(counts)

    def one(step, carry):
        where = pl.ds(pl.multiple_of(step * some, some), some)
        first, second = pair_ref[0:1, where], pair_ref[1:2, where]
        least = jnp.minimum(first, second)
        down = (jnp.abs(first - second) == P_SIZE).astype(jnp.int32)
        place = quads * PP
        slot, local = least // place, least % place
        high = down * quads + local // PP
        low = slot * PP + local % PP
        high_hot = (lax.broadcasted_iota(jnp.int32, (2 * quads, some), 0) == high).astype(F32).astype(BF16)
        low_hot = (lax.broadcasted_iota(jnp.int32, (span, some), 0) == low).astype(F32).astype(BF16)
        counts[...] += back_mul(high_hot, low_hot)
        return carry

    lax.fori_loop(0, pair_ref.shape[1] // some, one, 0)


def render_kernel(
    gauss_ref, weight_ref, target_ref, mask_ref, pair_ref, view_ref, total_ref, grad_ref, term_ref, feat, dfeat, counts
):
    count_pairs(pair_ref, counts)
    render_block(
        gauss_ref, weight_ref, target_ref, mask_ref, counts, view_ref, total_ref, grad_ref, term_ref, feat, dfeat
    )


def render_block(
    gauss_ref, weight_ref, target_ref, mask_ref, counts, view_ref, total_ref, grad_ref, term_ref, feat, dfeat
):
    quads = gauss_ref.shape[0] // NVIEW
    span = weight_ref.shape[1]
    scale = 1.0 / total_ref[0].astype(F32)

    def channel(index):
        return gauss_ref[:, index * PP : (index + 1) * PP]

    def shared():
        opacity = jax.nn.sigmoid(channel(3))
        extent = jax.nn.sigmoid(channel(5) + channel(6) + channel(7))
        lead = channel(8)
        denom = 1.0 + lead * lead + channel(9) * channel(9) + channel(10) * channel(10) + channel(11) * channel(11)
        facing = lead * lead / denom
        raw = channel(4)
        depth = jnp.maximum(raw, 0.0) + jnp.log1p(jnp.exp(-jnp.abs(raw)))
        return opacity, extent, lead, denom, facing, raw, depth

    opacity, extent, lead, denom, facing, raw, depth = shared()
    footprint = opacity * extent * facing
    channels = [jax.nn.sigmoid(channel(index)) * footprint for index in range(3)]
    channels += [footprint, depth * footprint]
    for index, value in enumerate(channels):
        for view in range(NVIEW):
            feat[index * quads : (index + 1) * quads, view * PP : (view + 1) * PP] = value[
                view * quads : (view + 1) * quads
            ]
    rendered = jnp.dot(feat[...], weight_ref[...], precision=HIGHEST, preferred_element_type=F32)
    parts = [rendered[index * quads : (index + 1) * quads] for index in range(5)]
    lane = lax.broadcasted_iota(jnp.int32, (quads, span), 1)
    live = jnp.where(lane < view_ref[0] * PP, mask_ref[...], 0).astype(F32)
    term = jnp.zeros((quads, span), F32)
    slopes = []
    for index in range(3):
        error = parts[index] - target_ref[index * quads : (index + 1) * quads, :].astype(F32)
        term = term + live * error * error
        slopes.append(2.0 * scale * live * error)
    below = 1.0 + parts[3]
    depth_out = parts[4] / below

    slope = jnp.zeros((quads, span), F32)
    for which, shift in enumerate((1, P_SIZE)):
        count = counts[which * quads : (which + 1) * quads]
        weight = DEPTH_WEIGHT * count * live * pltpu.roll(live, span - shift, 1)
        gap = depth_out - pltpu.roll(depth_out, span - shift, 1)
        term = term + weight * gap * gap
        pull = 2.0 * scale * weight * gap
        slope = slope + pull - pltpu.roll(pull, shift, 1)
    term_ref[...] = jnp.full(term_ref.shape, jnp.sum(term), F32)
    over = slope / below
    slopes += [-over * depth_out, over]
    stacked = jnp.concatenate(slopes, 0)
    dfeat[...] = lax.dot_general(
        stacked, weight_ref[...], (((1,), (1,)), ((), ())), precision=HIGHEST, preferred_element_type=F32
    )

    def feature_grad(index):
        return jnp.concatenate(
            [
                dfeat[index * quads : (index + 1) * quads, view * PP : (view + 1) * PP]
                for view in range(NVIEW)
            ],
            0,
        )

    def put(index, value):
        grad_ref[:, index * PP : (index + 1) * PP] = value.astype(BF16)

    d_foot = feature_grad(3)
    for index in range(3):
        tint = jax.nn.sigmoid(channel(index))
        upper = feature_grad(index)
        d_foot = d_foot + upper * tint
        put(index, upper * footprint * tint * (1.0 - tint))
    d_last = feature_grad(4)
    d_foot = d_foot + d_last * depth
    put(3, d_foot * extent * facing * opacity * (1.0 - opacity))
    put(4, d_last * footprint * jax.nn.sigmoid(raw))
    d_extent = d_foot * opacity * facing * extent * (1.0 - extent)
    for index in (5, 6, 7):
        put(index, d_extent)
    d_facing = d_foot * opacity * extent
    put(8, d_facing * 2.0 * lead / denom * (1.0 - facing))
    for index in (9, 10, 11):
        put(index, -2.0 * d_facing * facing / denom * channel(index))


def scene_targets(targets, mask, quads):
    slots = targets.shape[0]
    wanted = targets.reshape(slots, 3, quads, PP).transpose(1, 2, 0, 3).reshape(3 * quads, slots * PP)
    valid = mask.reshape(slots, quads, PP).transpose(1, 0, 2).reshape(quads, slots * PP)
    return wanted, valid


def render(gaussians, weights, targets, mask, pairs, view_count, pair_total):
    slots, views = weights.shape[:2]
    spread = weights.transpose(1, 2, 0, 3).reshape(views * PP, slots * PP)
    quads = gaussians.shape[0] // NVIEW
    wanted, valid = scene_targets(targets, mask, quads)
    vmem = pl.BlockSpec(memory_space=pltpu.VMEM)
    smem = pl.BlockSpec(memory_space=pltpu.SMEM)
    return pl.pallas_call(
        render_kernel,
        out_shape=[
            jax.ShapeDtypeStruct(gaussians.shape, BF16),
            jax.ShapeDtypeStruct((8, LANES), F32),
        ],
        in_specs=[vmem] * 5 + [smem] * 2,
        out_specs=[vmem] * 2,
        scratch_shapes=[pltpu.VMEM((5 * quads, views * PP), F32)] * 2
        + [pltpu.VMEM((2 * quads, slots * PP), F32)],
        compiler_params=pltpu.CompilerParams(vmem_limit_bytes=48 * MIB),
        name="render",
    )(gaussians, spread, wanted, valid, pairs, view_count, pair_total)


def forward_plain(shards, patches, features, kinds):
    weights = [lax.all_gather(shard, BOTH, axis=0, tiled=True) for shard in shards]
    groups = lax.axis_size(NARROW)
    rows = patches.shape[0]
    gains = weights[0][:, features : features + kinds].T.astype(F32)
    embedded = back_mul(patches[:, :features], weights[0][:, :features])
    normed_one = layer_norm(embedded, gains[0], gains[3]).astype(BF16)
    mixed = matmul(normed_one, weights[1]).astype(BF16).reshape(rows, 3, groups, -1)
    mixed = mixed.transpose(2, 1, 0, 3)
    qkv = lax.all_to_all(mixed, NARROW, split_axis=0, concat_axis=0, tiled=True)
    width = qkv.shape[-1]
    length = groups * rows
    heads = width // HD
    parts = [qkv[:, part].reshape(length, heads, HD) for part in range(3)]
    attended, logsum = attention_forward(*parts)
    log_sums = logsum.transpose(0, 2, 1).reshape(groups, rows, heads)
    returned = lax.all_to_all(
        attended.reshape(groups, rows, width), NARROW, split_axis=0, concat_axis=0, tiled=True
    )
    returned = returned.transpose(1, 0, 2).reshape(rows, D)
    mid = embedded + matmul(returned, weights[2])
    normed_two = layer_norm(mid, gains[1], gains[4]).astype(BF16)
    expanded = matmul(normed_two, weights[3])
    half = 0.5 * (1.0 + lax.erf(expanded * (0.5**0.5)))
    activated = (expanded * half).astype(BF16)
    bell = jnp.exp(-0.5 * expanded * expanded) * 0.3989422804014327
    slopes = (half + expanded * bell).astype(BF16)
    last = mid + matmul(activated, weights[4])
    normed_three = layer_norm(last, gains[2], gains[5]).astype(BF16)
    return Bag(
        dict(
        w1=weights[1],
        w2=weights[2],
        w3=weights[3],
        w4=weights[4],
        w5=weights[5],
        gains=gains,
        embedded=embedded,
        mid=mid,
        last=last,
        slopes=slopes,
        t1=normed_one.T,
        t2=returned.T,
        t3=normed_two.T,
        hidden=activated,
        t5=normed_three.T,
        qkv=qkv,
        heads_out=attended,
        log_sums=log_sums,
        gaussians=matmul(normed_three, weights[5]),
    ).items())


def backward_plain(kept, patches, gauss_low, term, features, kinds):
    gains = kept.gains
    weights = [None, kept.w1, kept.w2, kept.w3, kept.w4, kept.w5]
    norm_back_one = jax.vjp(layer_norm, kept.embedded, gains[0], gains[3])[1]
    norm_back_two = jax.vjp(layer_norm, kept.mid, gains[1], gains[4])[1]
    norm_back_three = jax.vjp(layer_norm, kept.last, gains[2], gains[5])[1]
    qkv = kept.qkv
    groups, _, rows, width = qkv.shape
    length = groups * rows
    heads = width // HD
    queries, keys, values = (qkv[:, part].reshape(length, heads, HD) for part in range(3))
    blocked = min(512, length)
    logsum = kept.log_sums[:, :, :heads].reshape(length // blocked, blocked, heads)
    residual_grad, gain_three, shift_three = norm_back_three(back_mul(gauss_low, weights[5]))
    shrink_low = residual_grad.astype(BF16)
    expand_low = (back_mul(shrink_low, weights[4]) * kept.slopes.astype(F32)).astype(BF16)
    through_two, gain_two, shift_two = norm_back_two(back_mul(expand_low, weights[3]))
    residual_grad = residual_grad + through_two
    merge_low = residual_grad.astype(BF16)
    out_grad = back_mul(merge_low, weights[2]).astype(BF16).reshape(rows, groups, width)
    head_grad = lax.all_to_all(
        out_grad.transpose(1, 0, 2), NARROW, split_axis=0, concat_axis=0, tiled=True
    ).reshape(length, heads, HD)
    grads = attention_backward(queries, keys, values, logsum.transpose(0, 2, 1), head_grad)
    stacked = jnp.stack(grads, 1).astype(BF16).reshape(groups, rows, 3, width)
    mixed_grad = lax.all_to_all(stacked, NARROW, split_axis=0, concat_axis=0, tiled=True)
    mixed_grad = mixed_grad.transpose(1, 2, 0, 3).reshape(rows, 3 * D)
    through_one, gain_one, shift_one = norm_back_one(back_mul(mixed_grad, weights[1]))
    embed_grad = (residual_grad + through_one).astype(BF16)
    grad_norms = jnp.stack([gain_one, gain_two, gain_three, shift_one, shift_two, shift_three])
    lefts = [embed_grad.T, kept.t1, kept.t2, kept.t3, kept.hidden.T, kept.t5]
    rights = [patches, mixed_grad, merge_low, expand_low, shrink_low, gauss_low]
    products = [matmul(left, right) for left, right in zip(lefts, rights)]
    products[0] = products[0].at[:, features : features + kinds].add(grad_norms.T)
    sums = [
        lax.psum_scatter(
            product.astype(BF16), BOTH, scatter_dimension=0, tiled=True
        ).astype(F32)
        for product in products
    ]
    squares = sum(jnp.sum(part * part) for part in sums)
    loss_sum, square_sum = lax.psum((term[0, 0], squares), BOTH)
    return sums, loss_sum, square_sum


def update_kernel(features, total_ref, sums_ref, *refs):
    sources, targets, refs = refs[:27], refs[27:48], refs[48:]
    loss_ref, norm_ref, refs = refs[0], refs[1], refs[2:]
    inside, news, refs = refs[:27], refs[27:48], refs[48:]
    turned, turned_four, in_sem, out_sem = refs
    loads = [pltpu.make_async_copy(source, dest, in_sem.at[i]) for i, (source, dest) in enumerate(zip(sources, inside))]
    stores = [pltpu.make_async_copy(source, dest, out_sem.at[i]) for i, (source, dest) in enumerate(zip(news, targets))]
    for copy in loads:
        copy.start()
    grads, olds = inside[:6], inside[6:]
    square_sum = sums_ref[1:2, 0:1]
    grad_norm = jnp.sqrt(square_sum)
    factor = jnp.minimum(1.0, CLIP_NORM / (grad_norm + 1e-06))
    norm_ref[...] = grad_norm
    loss_ref[...] = sums_ref[0:1, 0:1] / total_ref[0].astype(F32)
    width = grads[0].shape[1]
    for which in range(7):
        if which < 6:
            loads[which].wait()
        if which == 0:
            turned[...] = grads[0][:, width - LANES :].T
        if which == 4:
            turned_four[...] = grads[4][...].T
        for copy in loads[6 + 3 * which : 9 + 3 * which]:
            copy.wait()
        weight, first, second = olds[3 * which : 3 * which + 3]
        rows, columns = weight.shape
        chunk = min(8, rows)

        def one(step, carry):
            spot = pl.ds(pl.multiple_of(step * chunk, chunk), chunk)
            if which == 0:
                grad = grads[0][spot, 0:columns]
            elif which == 4:
                grad = turned_four[spot, :]
            elif which == 6:
                grad = turned[features % LANES : features % LANES + rows, 0:columns]
            else:
                grad = grads[which][spot, :]
            values = adamw(weight[spot, :], first[spot, :], second[spot, :], grad * factor, RATES[which])
            for dest, value in zip(news[3 * which : 3 * which + 3], values):
                dest[spot, :] = value
            return carry

        lax.fori_loop(0, rows // chunk, one, 0)
        for copy in stores[3 * which : 3 * which + 3]:
            copy.start()
    for copy in stores:
        copy.wait()


def update_all(olds, sums, totals, pair_total, features):
    vmem = pl.BlockSpec(memory_space=pltpu.VMEM)
    smem = pl.BlockSpec(memory_space=pltpu.SMEM)
    hbm = pl.BlockSpec(memory_space=pltpu.HBM)
    shapes = [jax.ShapeDtypeStruct(old.shape, F32) for old in olds]
    inside = [pltpu.VMEM(value.shape, F32) for value in list(sums) + list(olds)]
    return pl.pallas_call(
        functools.partial(update_kernel, features),
        out_shape=shapes + [jax.ShapeDtypeStruct((1, 1), F32)] * 2,
        in_specs=[smem, vmem] + [hbm] * 27,
        out_specs=[hbm] * 21 + [vmem] * 2,
        scratch_shapes=inside
        + [pltpu.VMEM(old.shape, F32) for old in olds]
        + [
            pltpu.VMEM((LANES, sums[0].shape[0]), F32),
            pltpu.VMEM(olds[12].shape, F32),
            pltpu.SemaphoreType.DMA((27,)),
            pltpu.SemaphoreType.DMA((21,)),
        ],
        compiler_params=pltpu.CompilerParams(vmem_limit_bytes=60 * MIB),
        name="update",
    )(pair_total, totals, *sums, *olds)


def body(
    views,
    render_w,
    targets,
    pix_mask,
    pairs,
    view_count,
    pair_total,
    embed_weight,
    embed_first,
    embed_second,
    mixer_weight,
    mixer_first,
    mixer_second,
    merge_weight,
    merge_first,
    merge_second,
    expand_weight,
    expand_first,
    expand_second,
    shrink_weight,
    shrink_first,
    shrink_second,
    unpatch_weight,
    unpatch_first,
    unpatch_second,
    norm_params,
    norm_first,
    norm_second,
):
    masters = (embed_weight, mixer_weight, merge_weight, expand_weight, shrink_weight, unpatch_weight, norm_params)
    firsts = (embed_first, mixer_first, merge_first, expand_first, shrink_first, unpatch_first, norm_first)
    seconds = (embed_second, mixer_second, merge_second, expand_second, shrink_second, unpatch_second, norm_second)
    groups = lax.axis_size(NARROW)
    wide_count = lax.axis_size(WIDE)
    features = embed_weight.shape[0]
    kinds = norm_params.shape[0]
    padded = -(-(features + kinds) // LANES) * LANES
    fill = padded - features - kinds
    by_kernel = mixer_weight.shape[0] % 16 == 0 and shrink_weight.shape[0] % LANES == 0

    patches = views.reshape(-1, features)
    if by_kernel:
        raw = (embed_weight.T,) + masters[1:6]
        wanted, valid = scene_targets(targets[0], pix_mask[0], patches.shape[0] // NVIEW)
        scene = (render_w[0], wanted, valid, pairs[0], view_count, pair_total)
        kept = forward_all(raw, norm_params, patches, scene, wide_count, groups)
        *sums, totals = backward_all(
            kept, kept.padded, kept.gauss, kept.term, features % LANES, wide_count, groups
        )
        olds = []
        for triple in zip(masters, firsts, seconds):
            olds += triple
        olds[:3] = [old.T for old in olds[:3]]
        *news, loss, grad_norm = update_all(olds, sums, totals, pair_total, features)
        news[:3] = [new.T for new in news[:3]]
        return tuple(news) + (loss[0, 0], grad_norm[0, 0])
    else:
        patches = jnp.pad(patches, ((0, 0), (0, padded - features)))
        first_shard = jnp.concatenate([embed_weight.T, norm_params.T], 1)
        first_shard = jnp.pad(first_shard.astype(BF16), ((0, 0), (0, fill)))
        shards = [first_shard] + [weight.astype(BF16) for weight in masters[1:6]]
        kept = forward_plain(shards, patches, features, kinds)
    divisor = pair_total[0].astype(F32)
    gauss_low, term = render(
        kept.gaussians, render_w[0], targets[0], pix_mask[0], pairs[0], view_count, pair_total
    )
    sums, loss_sum, square_sum = backward_plain(kept, patches, gauss_low, term, features, kinds)
    first_sum = sums[0].T
    grads = [first_sum[:features]] + list(sums[1:]) + [first_sum[features : features + kinds]]
    loss = loss_sum / divisor
    grad_norm = jnp.sqrt(square_sum)
    factor = jnp.minimum(1.0, CLIP_NORM / (grad_norm + 1e-06))
    results = []
    for which in range(7):
        results += adamw(masters[which], firsts[which], seconds[which], grads[which] * factor, RATES[which])
    return tuple(results) + (loss, grad_norm)


def solution(mesh):
    columns = P(None, BOTH)
    rows = P(BOTH, None)
    weights = (columns,) * 3 + (rows,) * 15 + (columns,) * 3
    return jax.shard_map(
        body,
        mesh=mesh,
        in_specs=(
            P(WIDE, None, NARROW, None),
            P(WIDE, None, None, None, None),
            P(WIDE, None, None, NARROW),
            P(WIDE, None, NARROW),
            P(WIDE, None, NARROW),
            P(WIDE),
            P(),
        )
        + weights,
        out_specs=weights + (P(), P()),
        check_vma=False,
    )
```

```python
import functools
import heapq

import jax
import jax.numpy as jnp
from jax import lax
from jax.experimental import pallas as pl
from jax.experimental.pallas import tpu as pltpu
from jax.sharding import PartitionSpec as P

D = 1024
HD = 64
P_SIZE = 8
PP = 64
NVIEW = 4
TMAX = 12
STEP = 10
LANES = 128
MIB = 1024 * 1024

DEPTH_WEIGHT = 1.0
CLIP_NORM = 0.01
BETA_ONE = 0.9
BETA_TWO = 0.95
ADAM_EPS = 1e-08
DECAY = 0.05
RATES = (0.05, 0.05, 0.5, 0.05, 0.05, 0.05, 0.8)
MESH = pl.DeviceIdType.MESH
WIDE, NARROW = BOTH = ("wide", "narrow")
HIGHEST = lax.Precision.HIGHEST
F32 = jnp.float32
BF16 = jnp.bfloat16


def matmul(left, right):
    return jnp.dot(left, right, preferred_element_type=F32)


def outer_sum(left, right):
    return lax.dot_general(left, right, (((0,), (0,)), ((), ())), preferred_element_type=F32)


def back_mul(grad, weight):
    return lax.dot_general(grad, weight, (((1,), (1,)), ((), ())), preferred_element_type=F32)


def layer_norm(values, gain, shift):
    centred = values - jnp.mean(values, -1, keepdims=True)
    spread = jnp.mean(centred * centred, -1, keepdims=True)
    return centred * lax.rsqrt(spread + 1e-05) * gain + shift


def exact_gelu(values):
    return jax.nn.gelu(values, approximate=False)


def attention_forward(queries, keys, values):
    length, heads = (queries.shape[0], queries.shape[1])
    blocked = min(512, length)
    scale = HD ** (-0.5)

    def one_block(query_block):
        scores = (
            jnp.einsum("qhd,khd->hqk", query_block, keys, preferred_element_type=jnp.float32)
            * scale
        )
        highest = jnp.max(scores, -1, keepdims=True)
        exponentials = jnp.exp(scores - highest)
        summed = jnp.sum(exponentials, -1, keepdims=True)
        softmaxed = (exponentials / summed).astype(jnp.bfloat16)
        output = jnp.einsum("hqk,khd->qhd", softmaxed, values, preferred_element_type=jnp.float32)
        return (output.astype(jnp.bfloat16), (highest + jnp.log(summed))[:, :, 0])

    output, logsum = lax.map(one_block, queries.reshape(length // blocked, blocked, heads, HD))
    return (output.reshape(length, heads * HD), logsum)


def attention_backward(queries, keys, values, logsum, out_grad):
    length, heads = (queries.shape[0], queries.shape[1])
    blocked = min(512, length)
    scale = HD ** (-0.5)

    def one_block(carry, inputs):
        key_grad, value_grad = carry
        query_block, logsum_block, grad_block = inputs
        scores = (
            jnp.einsum("qhd,khd->hqk", query_block, keys, preferred_element_type=jnp.float32)
            * scale
        )
        softmaxed = jnp.exp(scores - logsum_block[:, :, None])
        value_grad = value_grad + jnp.einsum(
            "hqk,qhd->khd",
            softmaxed.astype(jnp.bfloat16),
            grad_block,
            preferred_element_type=jnp.float32,
        )
        prob_grad = jnp.einsum(
            "qhd,khd->hqk", grad_block, values, preferred_element_type=jnp.float32
        )
        score_grad = softmaxed * (prob_grad - jnp.sum(softmaxed * prob_grad, -1, keepdims=True))
        score_low = score_grad.astype(jnp.bfloat16)
        query_grad = (
            jnp.einsum("hqk,khd->qhd", score_low, keys, preferred_element_type=jnp.float32) * scale
        )
        key_grad = (
            key_grad
            + jnp.einsum("hqk,qhd->khd", score_low, query_block, preferred_element_type=jnp.float32)
            * scale
        )
        return ((key_grad, value_grad), query_grad)

    zeros = jnp.zeros((length, heads, HD), jnp.float32)
    shaped = (
        queries.reshape(length // blocked, blocked, heads, HD),
        logsum,
        out_grad.reshape(length // blocked, blocked, heads, HD),
    )
    (key_grad, value_grad), query_grad = lax.scan(one_block, (zeros, zeros), shaped)
    return (query_grad.reshape(length, heads, HD), key_grad, value_grad)


def adamw(weight, first, second, grad, rate):
    first = BETA_ONE * first + (1.0 - BETA_ONE) * grad
    second = BETA_TWO * second + (1.0 - BETA_TWO) * grad * grad
    first_hat = first / (1.0 - BETA_ONE**STEP)
    second_hat = second / (1.0 - BETA_TWO**STEP)
    weight = weight - rate * (first_hat / (jnp.sqrt(second_hat) + ADAM_EPS) + DECAY * weight)
    return (weight, first, second)


def chip_bits(chips):
    bits, step = [], 1
    while step < chips:
        bits.append(step)
        step *= 2
    return bits


def flip(chip, mask):
    for bit in chip_bits(mask + 1):
        if mask & bit:
            chip = chip + (1 - 2 * (chip // bit % 2)) * bit
    return chip


def column_halves(width):
    first = -(-width // (2 * LANES)) * LANES
    return ((0, first), (first, width - first))


def work_items(widths, order):
    return [(which,) + half + (side,) for which in order for side, half in enumerate(column_halves(widths[which]))]


class Bag:
    def __init__(self, pairs):
        vars(self).update(pairs)


class Place:
    def __init__(self, wide, narrow):
        self.wide, self.narrow = wide, narrow
        self.chips = wide // 2
        self.bits = chip_bits(self.chips)
        self.w = lax.axis_index(WIDE)
        self.n = lax.axis_index(NARROW)
        self.chip = self.w // 2
        self.core = self.w % 2
        self.twin = (2 * self.chip + 1 - self.core, self.n)

    def across(self, mask):
        return (2 * flip(self.chip, mask) + self.core, self.n)

    def along(self, step):
        return (self.w, lax.rem(self.n + step, self.narrow))

    def neighbours(self):
        return (
            [self.twin]
            + [self.across(bit) for bit in self.bits]
            + [self.along(step) for step in range(1, self.narrow)]
        )


class Planner:
    def __init__(self):
        self.now, self.count = 0.0, 0
        self.free, self.events, self.done, self.spare = {}, [], set(), []
        self.refill = lambda: None

    def transfer(self, link, cost, key, event):
        self.free[link] = max(self.now, self.free.get(link, 0.0)) + cost
        self.count += 1
        heapq.heappush(self.events, (self.free[link] + 2.0, self.count, key, event))

    def step(self):
        when, _, key, event = heapq.heappop(self.events)
        self.now = max(self.now, when) + 0.2
        event()
        self.done.add(key)
        self.refill()

    def fill(self, until):
        for index, (keys, cost, work) in enumerate(self.spare):
            if self.now + cost <= until and self.done.issuperset(keys):
                del self.spare[index]
                work()
                self.now += cost
                return True
        return False

    def need(self, keys):
        while not self.done.issuperset(keys):
            if not self.fill(self.events[0][0]):
                self.step()

    def work(self, cost, work, rush=False):
        while not rush and self.events and self.events[0][0] <= self.now:
            self.step()
        self.refill()
        work()
        self.now += cost

    def later(self, cost, work, keys=()):
        entry = (tuple(keys), cost, work)
        self.spare.append(entry)
        return entry

    def force(self, entry):
        if entry in self.spare:
            self.spare.remove(entry)
            self.work(entry[1], entry[2])

    def finish(self):
        self.refill()
        while self.events or self.spare:
            if not self.fill(self.events[0][0] if self.events else 1e9):
                self.step()


LINK = 90e3
Z_AHEAD = 4.0
RELAYED = (3, 4)
KEY_ROWS = 1024
Z_EARLY = 1.0
Z_LATE = 2.0
TWIN_LINK = 600e3


def greet(peers):
    barrier = pltpu.get_barrier_semaphore()
    for peer in peers:
        pl.semaphore_signal(barrier, inc=1, device_id=peer, device_id_type=MESH)
    return lambda: pl.semaphore_wait(barrier, len(peers))


def normalize(values, gain, shift):
    centred = values - jnp.mean(values, -1, keepdims=True)
    spread = jnp.mean(centred * centred, -1, keepdims=True)
    return centred * lax.rsqrt(spread + 1e-05) * gain + shift


def forward_plan(widths):
    items = []
    for which, cuts in ((0, 1), (1, 3), (2, 1), (3, 2), (5, 1), (4, 2)):
        size = widths[which] // cuts
        for cut in range(cuts):
            for side, (start, width) in enumerate(column_halves(size)):
                items.append((which, cut * size + start, width, side))
    return items


def forward_kernel(items, wide, narrow, lead, ins, outs, scratch, *refs):
    at = Bag(zip(ins + scratch, refs[: len(ins)] + refs[len(ins) + len(outs) :]))
    results = refs[len(ins) : len(ins) + len(outs)]
    weights = [at.first_weight, at.w1, at.w2, at.w3, at.w4, at.w5]
    shards = [at.c0, at.c1, at.c2, at.c3, at.c4, at.c5]
    raw = [at.s0, at.s1, at.s2, at.s3, at.s4, at.s5]
    own_sem, send_sem, recv_sem = at.own_sem, at.send_sem, at.recv_sem
    swap_send, swap_recv, out_sem = at.swap_send, at.swap_recv, at.out_sem
    place = Place(wide, narrow)
    chips, me = place.chips, place.n
    tokens = at.patches.shape[0]
    head_width = D // narrow
    total = len(items)
    started, guarded = [], []

    def start(copy):
        copy.start()
        started.append(copy)

    all_here = greet(place.neighbours())
    features = at.s0.shape[1]
    tail = shards[0].shape[1] - LANES
    kinds = at.norm_raw.shape[0]
    kind = lax.broadcasted_iota(jnp.int32, (kinds, LANES), 0)
    spot = lax.broadcasted_iota(jnp.int32, (kinds, LANES), 1)
    put = (spot == kind + lead).astype(F32).astype(BF16)
    shards[0][:, tail:] = outer_sum(at.norm_raw[...].astype(BF16), put).astype(BF16)
    shards[0][:, 0:features] = at.s0[...].astype(BF16)
    shards[1][...] = raw[1][...].astype(BF16)
    at.padded[...] = jnp.zeros_like(at.padded)
    at.padded[:, 0:features] = at.patches[...]
    all_here()
    rows_of = [shard.shape[0] for shard in shards]

    def slab(which, node):
        rows = rows_of[which]
        return pl.ds(pl.multiple_of(node * rows, rows), rows)

    def whole_of(which, columns):
        part = weights[which][:, :, :, columns]
        return part.reshape(-1, part.shape[-1])

    own = [
        pltpu.make_async_copy(
            shards[which], weights[which].at[place.chip, place.core, slab(which, me), :], own_sem.at[which]
        )
        for which in range(6)
    ]
    for copy in own[:2]:
        copy.start()

    def remote(item, src, dst, slot, peer):
        return pltpu.make_async_remote_copy(
            src_ref=src,
            dst_ref=dst,
            send_sem=send_sem.at[item, slot],
            recv_sem=recv_sem.at[item, slot],
            device_id=peer,
            device_id_type=MESH,
        )

    def group(item, mask):
        which, begin, width, _ = items[item]
        return weights[which].at[flip(place.chip, mask), place.core, :, pl.ds(begin, width)]

    def along(item, sign, hop):
        which, begin, width, _ = items[item]
        columns = pl.ds(begin, width)
        there = weights[which].at[place.chip, place.core, slab(which, me - sign * (hop - 1)), columns]
        return remote(
            item,
            shards[which].at[:, columns] if hop == 1 else there,
            there,
            chips + 1 + hop - 1 + (narrow - 1 if sign < 0 else 0),
            (place.w, me + sign),
        )

    def has_next(sign):
        return me < narrow - 1 if sign > 0 else me >= 1

    def has_come(sign, hop):
        return me >= hop if sign > 0 else me < narrow - hop

    def start_if(condition, copy):
        @pl.when(condition)
        def _():
            copy.start()

        guarded.append((condition, copy))

    def bits_of(item):
        return place.bits if items[item][3] == 0 else place.bits[::-1]

    def across(item, mask, bit):
        return remote(item, group(item, mask), group(item, mask), mask ^ bit, place.across(bit))

    def to_twin(item):
        which, begin, width, _ = items[item]
        there = weights[which].at[:, place.core, :, pl.ds(begin, width)]
        return remote(item, there, there, chips, place.twin)

    plan = Planner()
    waited = set()

    def block_bytes(item):
        which, _, width, _ = items[item]
        return 2 * narrow * rows_of[which] * width

    def twin_event(item):
        to_twin(item).wait_recv()

    here = {}

    def onward(item, mask, number):
        bits = bits_of(item)
        size = block_bytes(item)
        for later in range(number, len(bits)):
            start(across(item, mask, bits[later]))
            coming = mask ^ bits[later]
            plan.transfer(
                bits[later], 2 * size / LINK, (item, coming), functools.partial(arrive, item, coming, later)
            )
        here[item] = here.get(item, 0) + 1
        if here[item] == chips:
            start(to_twin(item))
            plan.transfer(-1, chips * size / TWIN_LINK, (item, chips), functools.partial(twin_event, item))

    def arrive(item, mask, number):
        across(item, mask ^ bits_of(item)[number], bits_of(item)[number]).wait_recv()
        onward(item, mask, number + 1)

    def begin_item(item):
        for sign in (1, -1):
            start_if(has_next(sign), along(item, sign, 1))
        line_transfer(item, 1)

    def line_transfer(item, hop):
        cost = 2 * block_bytes(item) / narrow / LINK
        key = (item, 0) if hop == narrow - 1 else (item, -hop)
        plan.transfer(0, cost, key, functools.partial(line_event, item, hop))

    def line_event(item, hop):
        if items[item][0] not in waited:
            waited.add(items[item][0])
            own[items[item][0]].wait()
        for sign in (1, -1):

            @pl.when(has_come(sign, hop))
            def _():
                along(item, sign, hop).wait_recv()

            if hop < narrow - 1:
                start_if(jnp.logical_and(has_come(sign, hop), has_next(sign)), along(item, sign, hop + 1))
        if hop < narrow - 1:
            line_transfer(item, hop + 1)
        else:
            onward(item, 0, 0)

    begun, ahead = [], [Z_EARLY]

    def refill():
        while len(begun) < total and plan.free.get(0, 0.0) < plan.now + ahead[-1]:
            begin_item(len(begun))
            begun.append(True)

    plan.refill = refill
    refill()
    assert all(items[item][0] < 2 for item in range(len(begun)))
    for which in range(2, 6):
        shards[which][...] = raw[which][...].astype(BF16)
        own[which].start()

    def need(which, columns=None):
        plan.need(
            [
                (index, key)
                for index, (owner, begin, width, _) in enumerate(items)
                if owner == which and (columns is None or (begin < columns[1] and begin + width > columns[0]))
                for key in range(chips + 1)
            ]
        )

    flushed = []

    def flush(ref):
        index = [vars(at)[name] is ref for name in outs].index(True)
        copy = pltpu.make_async_copy(ref, results[index], out_sem.at[index])
        copy.start()
        flushed.append(copy)

    def swap(src, dst, kind, step):
        return pltpu.make_async_remote_copy(
            src_ref=src,
            dst_ref=dst,
            send_sem=swap_send.at[kind, step],
            recv_sem=swap_recv.at[kind, step],
            device_id=place.along(step),
            device_id_type=MESH,
        )

    gains = at.gains
    embedded, mid, last = at.embedded, at.mid, at.last
    normed, hidden, wave = at.normed, at.hidden, at.wave
    away, qkv, heads_out, returned = at.away, at.qkv, at.heads_out, at.returned

    def turn(dest, source):
        dest[...] = source[...].T
        flush(dest)

    plan.later(2.0, lambda: spread_weights(at.render_w, at.spread))
    plan.later(3.0, lambda: count_pairs(at.pairs, at.counts))
    need(0)
    width = weights[0].shape[-1]
    kind = lax.broadcasted_iota(jnp.int32, (8, LANES), 0)
    spot = lax.broadcasted_iota(jnp.int32, (8, LANES), 1)
    pick = (spot == kind + lead).astype(F32).astype(BF16)
    gains[...] = back_mul(pick, whole_of(0, pl.ds(width - LANES, LANES)))
    flush(gains)
    flush(at.padded)

    def embed(block):
        cols = pl.ds(block, 256)
        rows = whole_of(0, pl.ds(0, width))[block : block + 256]
        embedded[:, cols] = back_mul(at.padded[...], rows)

    for block in range(0, D, 256):
        plan.work(0.5, functools.partial(embed, block))
    flush(embedded)

    def norm_rows(source, row, dest):
        step_rows = 32

        def one(step, carry):
            rows = pl.ds(pl.multiple_of(step * step_rows, step_rows), step_rows)
            dest[rows, :] = normalize(
                source[rows, :], gains[row : row + 1, :], gains[row + 3 : row + 4, :]
            ).astype(BF16)
            return carry

        lax.fori_loop(0, tokens // step_rows, one, 0)

    plan.work(2.0, lambda: norm_rows(embedded, 0, normed))
    turn_first = plan.later(2.0, lambda: turn(at.t1, normed))
    piece = 2 * (narrow - 1) * 2 * tokens * head_width / LINK

    def project(part, step):
        owner = lax.rem(me + step, narrow)
        offset = pl.multiple_of(part * D + owner * head_width, LANES)
        value = matmul(normed[...], whole_of(1, pl.ds(offset, head_width))).astype(BF16)
        if step:
            away[step - 1, part] = value
            start(swap(away.at[step - 1, part], qkv.at[me, part], part, step))
        else:
            qkv[me, part] = value

    def swap_event(part):
        for step in range(1, narrow):
            swap(away.at[step - 1, part], qkv.at[me, part], part, step).wait_recv()

    for part in range(3):
        need(1, (part * D, part * D + D))
        for step in list(range(1, narrow)) + [0]:
            plan.work(0.7, functools.partial(project, part, step))
        plan.transfer(0, piece, (-1, part), functools.partial(swap_event, part))
    flush(at.w1)
    lane = lax.broadcasted_iota(jnp.int32, (1, LANES), 1)
    scale = HD ** (-0.5)
    length = narrow * tokens
    sides = LANES // HD

    def weigh(step):
        who = lax.rem(me + step, narrow)
        log_sums = jnp.zeros((tokens, LANES), F32)
        sums = jnp.ones((tokens, LANES), F32)
        for pair in range(head_width // LANES):
            lanes = pl.ds(pair * LANES, LANES)
            query = qkv[who, 0, :, lanes].astype(F32)
            key = qkv[:, 1, :, lanes].reshape(length, LANES)
            for side in range(sides):
                head = pair * sides + side
                own_query = (query * jnp.where(lane // HD == side, scale, 0.0)).astype(BF16)
                scores = back_mul(own_query, key)
                highest = jnp.max(scores, -1, keepdims=True)
                exponentials = jnp.exp(scores - highest)
                summed = jnp.sum(exponentials, -1, keepdims=True)
                at.weighed[step, head] = exponentials.astype(BF16)
                log_sums = jnp.where(lane == head, highest + jnp.log(summed), log_sums)
                sums = jnp.where(lane == head, summed, sums)
        at.log_sums[who] = log_sums
        at.weigh_sums[step] = sums

    def attend(step):
        who = lax.rem(me + step, narrow)
        for pair in range(head_width // LANES):
            lanes = pl.ds(pair * LANES, LANES)
            value = qkv[:, 2, :, lanes].reshape(length, LANES)
            out = jnp.zeros((tokens, LANES), F32)
            for side in range(sides):
                head = pair * sides + side
                part = matmul(at.weighed[step, head], value) / at.weigh_sums[step, :, head : head + 1]
                out = jnp.where(lane // HD == side, part, out)
            heads_out[who, :, lanes] = out.astype(BF16)
        if step:
            start(swap(heads_out.at[who], returned.at[me], 3, step))
        else:
            returned[me] = heads_out[who]

    steps = list(range(1, narrow)) + [0]
    ahead.append(Z_LATE)
    plan.need([(-1, 0), (-1, 1)])
    for step in steps:
        plan.work(2.7, functools.partial(weigh, step))
    plan.need([(-1, 2)])
    flush(qkv)

    def return_event(step):
        return lambda: swap(heads_out.at[me], returned.at[me], 3, step).wait_recv()

    for step in steps:
        plan.work(0.9, functools.partial(attend, step))
        if step:
            plan.transfer(0, piece / (narrow - 1), (-2, step), return_event(step))
    flush(heads_out)
    flush(at.log_sums)
    need(2)
    plan.need([(-2, step) for step in range(1, narrow)])

    def merge(block):
        cols = pl.ds(block, 256)
        value = embedded[:, cols]
        weight = whole_of(2, cols)
        for source in range(narrow):
            value = value + matmul(returned[source], weight[source * head_width : (source + 1) * head_width])
        mid[:, cols] = value

    for block in range(0, D, 256):
        plan.work(0.7, functools.partial(merge, block))
    flush(at.w2)
    flush(mid)
    plan.force(turn_first)
    plan.work(2.0, lambda: norm_rows(mid, 1, normed))

    def turn_returned():
        for source in range(narrow):
            at.t2[pl.ds(source * head_width, head_width), :] = returned[source].T
        flush(at.t2)

    plan.later(2.0, turn_returned)
    turn_second = plan.later(2.0, lambda: turn(at.t3, normed))

    ff = weights[3].shape[-1]
    tile = wave.shape[1]
    slopes = at.slopes

    def expand(block):
        wave[...] = matmul(normed[...], whole_of(3, pl.ds(block, tile)))

        def bend(step, carry):
            rows = pl.ds(pl.multiple_of(step * 32, 32), 32)
            x = wave[rows, :]
            half = 0.5 * (1.0 + lax.erf(x * (0.5**0.5)))
            hidden[rows, pl.ds(block, tile)] = (x * half).astype(BF16)
            bell = jnp.exp(-0.5 * x * x) * 0.3989422804014327
            slopes[rows, pl.ds(block, tile)] = (half + x * bell).astype(BF16)
            return carry

        lax.fori_loop(0, tokens // 32, bend, 0)

    for block in range(0, ff, tile):
        need(3, (block, block + tile))
        plan.work(2.5, functools.partial(expand, block))
    flush(at.w3)
    flush(slopes)
    flush(hidden)

    def shrink(block):
        cols = pl.ds(block, 256)
        last[:, cols] = mid[:, cols] + matmul(hidden[...], whole_of(4, cols))

    for block in range(0, D, 256):
        need(4, (block, block + 256))
        plan.work(1.0, functools.partial(shrink, block))
    flush(at.w4)
    flush(last)
    plan.force(turn_second)
    plan.work(2.0, lambda: norm_rows(last, 2, normed))
    need(5)

    def unpatch(block):
        cols = pl.ds(block, 256)
        at.gaussians[:, cols] = matmul(normed[...], whole_of(5, cols))

    for block in range(0, weights[5].shape[-1], 256):
        plan.work(0.7, functools.partial(unpatch, block))
    flush(at.w5)
    for entry in list(plan.spare):
        plan.force(entry)

    def draw():
        render_block(
            at.gaussians, at.spread, at.wanted, at.valid, at.counts, at.view, at.total, at.gauss, at.term, at.feat, at.dfeat
        )

    plan.work(4.0, draw)
    flush(at.gauss)
    flush(at.term)
    plan.later(2.0, lambda: turn(at.t5, normed))
    plan.finish()
    for copy in started:
        copy.wait_send()
    for condition, copy in guarded:

        @pl.when(condition)
        def _():
            copy.wait_send()

    for copy in flushed:
        copy.wait()


def forward_all(shards, norms, patches, scene, wide, narrow):
    tokens = patches.shape[0]
    features, kinds = patches.shape[1], norms.shape[0]
    lead = features % LANES
    widths = [-(-(features + kinds) // LANES) * LANES] + [shard.shape[1] for shard in shards[1:]]
    heights = [shard.shape[0] * wide * narrow for shard in shards]
    ff = widths[3]
    chips = wide // 2
    quads, slots_t = tokens // NVIEW, scene[0].shape[0]
    head_width = D // narrow
    items = forward_plan(widths)
    slots = chips + 1 + 2 * (narrow - 1)
    full = [((chips, 2, height // wide, width), BF16) for height, width in zip(heights, widths)]
    shapes = dict(
        w1=full[1],
        w2=full[2],
        w3=full[3],
        w4=full[4],
        w5=full[5],
        gains=((8, D), F32),
        embedded=((tokens, D), F32),
        mid=((tokens, D), F32),
        last=((tokens, D), F32),
        slopes=((tokens, ff), BF16),
        t1=((D, tokens), BF16),
        t2=((D, tokens), BF16),
        t3=((D, tokens), BF16),
        hidden=((tokens, ff), BF16),
        t5=((D, tokens), BF16),
        qkv=((narrow, 3, tokens, head_width), BF16),
        heads_out=((narrow, tokens, head_width), BF16),
        log_sums=((narrow, tokens, LANES), F32),
        padded=((tokens, widths[0]), BF16),
        gauss=((tokens, widths[5]), BF16),
        term=((8, LANES), F32),
    )
    ins = tuple(dict(s0=0, s1=0, s2=0, s3=0, s4=0, s5=0, norm_raw=0, patches=0))
    ins += tuple(dict(render_w=0, wanted=0, valid=0, pairs=0, view=0, total=0))
    outs = tuple(shapes)
    extras = dict(
        first_weight=pltpu.VMEM(*full[0]),
        c0=pltpu.VMEM((shards[0].shape[0], widths[0]), BF16),
        c1=pltpu.VMEM(shards[1].shape, BF16),
        c2=pltpu.VMEM(shards[2].shape, BF16),
        c3=pltpu.VMEM(shards[3].shape, BF16),
        c4=pltpu.VMEM(shards[4].shape, BF16),
        c5=pltpu.VMEM(shards[5].shape, BF16),
        gaussians=pltpu.VMEM((tokens, widths[5]), F32),
        spread=pltpu.VMEM((NVIEW * PP, slots_t * PP), F32),
        counts=pltpu.VMEM((2 * quads, slots_t * PP), F32),
        feat=pltpu.VMEM((5 * quads, NVIEW * PP), F32),
        dfeat=pltpu.VMEM((5 * quads, NVIEW * PP), F32),
        normed=pltpu.VMEM((tokens, D), BF16),
        wave=pltpu.VMEM((tokens, 512), F32),
        away=pltpu.VMEM((narrow - 1, 3, tokens, head_width), BF16),
        weighed=pltpu.VMEM((narrow, head_width // HD, tokens, narrow * tokens), BF16),
        weigh_sums=pltpu.VMEM((narrow, tokens, LANES), F32),
        returned=pltpu.VMEM((narrow, tokens, head_width), BF16),
        own_sem=pltpu.SemaphoreType.DMA((6,)),
        send_sem=pltpu.SemaphoreType.DMA((len(items), slots)),
        recv_sem=pltpu.SemaphoreType.DMA((len(items), slots)),
        swap_send=pltpu.SemaphoreType.DMA((4, narrow)),
        swap_recv=pltpu.SemaphoreType.DMA((4, narrow)),
        out_sem=pltpu.SemaphoreType.DMA((len(outs),)),
    )
    scratch = outs + tuple(extras)
    anywhere = pl.BlockSpec(memory_space=pl.ANY)
    results = pl.pallas_call(
        functools.partial(forward_kernel, items, wide, narrow, lead, ins, outs, scratch),
        out_shape=[jax.ShapeDtypeStruct(*shapes[name]) for name in outs],
        in_specs=[pl.BlockSpec(memory_space=pltpu.VMEM)] * (len(ins) - 2)
        + [pl.BlockSpec(memory_space=pltpu.SMEM)] * 2,
        out_specs=[anywhere] * len(outs),
        scratch_shapes=[pltpu.VMEM(*shapes[name]) for name in outs] + list(extras.values()),
        compiler_params=pltpu.CompilerParams(
            collective_id=0, has_side_effects=True, vmem_limit_bytes=63 * MIB
        ),
        name="forward",
    )(*shards, norms, patches, *scene)
    results = [result.reshape(-1, result.shape[-1]) for result in results[:5]] + list(results[5:])
    return Bag(zip(outs, results))


def backward_plan(widths, pairs):
    items = []
    for which, cuts in ((5, 1), (4, 2), (3, 2), (2, 1), (1, pairs), (0, 1)):
        size = widths[which] // cuts
        for cut in range(cuts):
            for side, (start, width) in enumerate(column_halves(size)):
                items.append((which, cut * size + start, width, side))
    return items


def tile_of(width):
    for tile in (512, 384, 256, 128):
        if width % tile == 0:
            return tile
    return width


def backward_kernel(items, wide, narrow, lead, ins, scratch, *refs):
    src = Bag(zip(ins, refs))
    refs = refs[len(ins) :]
    sums, totals, refs = refs[:6], refs[6], list(refs[7:])
    at = Bag(zip(scratch, refs))
    place = Place(wide, narrow)
    chips, me = place.chips, place.n
    total = len(items)
    refs = refs[len(scratch) :]
    held = [refs.pop(0) for _ in items]
    passed = [[refs.pop(0) for _ in place.bits] for _ in items]
    final = [refs.pop(0) for _ in items]
    spare = [refs.pop(0) for _ in range(6)]
    tokens = src.patches.shape[0]
    head_width = D // narrow
    length = narrow * tokens
    reach = narrow * LANES
    send_sem, recv_sem, tile_send, tile_recv = at.send_sem, at.recv_sem, at.tile_send, at.tile_recv
    swap_send, swap_recv, in_sem, ring_sem = at.swap_send, at.swap_recv, at.in_sem, at.ring_sem
    gains, norms, extra = src.gains, at.norms, at.extra
    stash, d_res, d_norm = at.stash, at.d_res, at.d_norm
    mixed, merge_low, expand_low, shrink_low = at.mixed, at.merge_low, at.expand_low, at.shrink_low

    peers = [(lax.rem(place.w + step, wide), place.n) for step in range(1, wide)]
    peers += [place.along(step) for step in range(1, narrow)]
    all_here = greet(peers)

    loaded = [name for name in ins if name in scratch]

    def load(ref):
        index = [vars(at)[name] is ref for name in loaded].index(True)
        return pltpu.make_async_copy(vars(src)[loaded[index]], ref, in_sem.at[index])

    def load_stash(ref):
        return pltpu.make_async_copy(ref, stash, in_sem.at[len(loaded)])

    def ring(ref, slots, rows, columns, index, row):
        slot = lax.rem(index, slots.shape[0])
        return pltpu.make_async_copy(
            ref.at[pl.ds(pl.multiple_of(row, rows), rows), :],
            slots.at[slot, pl.ds(0, rows), pl.ds(0, columns)],
            ring_sem.at[0 if slots is at.tall else 1, slot],
        )

    slope_rows = at.tall.shape[1]
    tall, long = at.tall.shape[0], at.long.shape[0]

    def slope_load(index):
        slot = lax.rem(index, tall)
        return pltpu.make_async_copy(
            src.slopes.at[:, pl.ds(pl.multiple_of(index * slope_rows, slope_rows), slope_rows)],
            at.slope_slots.at[slot],
            ring_sem.at[2, slot],
        )

    u_rows, u_cols = 256, src.w5.shape[1]
    load_stash(src.last).start()
    for index in range(tall):
        ring(src.w5, at.tall, u_rows, u_cols, index, index * u_rows).start()
        slope_load(index).start()
    wide_rows = at.long.shape[1]
    for index in range(long):
        ring(src.w3, at.long, wide_rows, src.w3.shape[1], index, index * wide_rows).start()
    for name in loaded:
        load(vars(at)[name]).start()

    all_here()

    started, guarded = [], []

    def start(copy):
        copy.start()
        started.append(copy)

    lefts = [at.embed_t, at.t1, at.t2, at.t3, at.shrink_t, at.t5]
    rights = [src.patches, mixed, merge_low, expand_low, at.hidden, src.gauss]

    def remote(item, src, dst, slot, peer):
        return pltpu.make_async_remote_copy(
            src_ref=src,
            dst_ref=dst,
            send_sem=send_sem.at[item, slot],
            recv_sem=recv_sem.at[item, slot],
            device_id=peer,
            device_id_type=MESH,
        )

    def bits_of(item):
        return place.bits[::-1] if items[item][3] == 0 else place.bits

    def groups_of(item):
        size = max(1, 512 // (narrow * spare[items[item][0]].shape[2]))
        if items[item][0] == 4:
            size = chips
        masks = list(range(chips))
        if bits_of(item) and bits_of(item)[0] > 1:
            masks = masks[chips // 2 :] + masks[: chips // 2]
        return [sorted(masks[at_mask : at_mask + size]) for at_mask in range(0, chips, size)]

    def product(item, masks, core, into, plus):
        which, begin, width, _ = items[item]
        left, right = lefts[which], rights[which]
        rows = into.shape[-2]
        span = narrow * rows
        tile = tile_of(width)
        if which == 4:
            size = into.shape[-1]
            for mask in masks:
                column = ((flip(place.chip, mask) * 2 + core) * narrow) * size
                rhs = right[:, pl.ds(pl.multiple_of(column, narrow * size), narrow * size)]
                value = jnp.dot(left[begin : begin + width, :], rhs, preferred_element_type=F32)
                for node in range(narrow):
                    piece = value[:, node * size : (node + 1) * size]
                    if plus:
                        piece = piece + into[mask, node].astype(F32)
                    into[mask, node] = piece.astype(BF16)
            return
        firsts = [((flip(place.chip, mask) * 2 + core) * narrow) * rows for mask in masks]
        with_extra = which == 0 and begin + width == right.shape[1]
        assert not with_extra or tile == width
        if which == 1:
            tile = LANES * 2

        def one(step, carry):
            offset = pl.multiple_of(begin + step * tile, LANES)
            local = pl.multiple_of(step * tile, LANES)
            if which != 1:
                rhs = right[:, pl.ds(offset, tile)]
            else:
                part, inside = offset // reach, pl.multiple_of(offset % reach, LANES)
                rhs = right[part // 3, part % 3, :, pl.ds(inside, tile)]
            spots = [pl.ds(pl.multiple_of(first, span), span) for first in firsts]
            lhs = jnp.concatenate([left[spot, :] for spot in spots], 0)
            value = jnp.dot(lhs, rhs, preferred_element_type=F32)
            for index, mask in enumerate(masks):
                piece = value[index * span : (index + 1) * span]
                if with_extra:
                    blank = jnp.zeros((span, tile - LANES), F32)
                    piece = piece + jnp.concatenate([blank, extra[spots[index], :]], 1)
                piece = piece.reshape(narrow, rows, tile)
                if plus:
                    piece = piece + into[mask, :, :, pl.ds(local, tile)].astype(F32)
                into[mask, :, :, pl.ds(local, tile)] = piece.astype(BF16)
            return carry

        lax.fori_loop(0, width // tile, one, 0)

    last_sent = {}
    plan = Planner()

    def to_twin(item, masks):
        which, _, width, _ = items[item]
        some = pl.ds(masks[0], len(masks))
        own = spare[which].at[some] if which == 4 else spare[which].at[some, :, :, pl.ds(0, width)]
        return remote(item, own, held[item].at[some], masks[0], place.twin)

    def across(item, mask, bit, number, slot):
        return remote(
            item, held[item].at[mask], passed[item][number].at[slot], chips + mask, place.across(bit)
        )

    def relayed(item):
        return items[item][0] in RELAYED

    def hopping(item, sign, hop):
        count = narrow - hop
        first = hop if sign > 0 else 0
        node = hop if sign > 0 else narrow - 1 - hop
        return remote(
            item,
            held[item].at[0, pl.ds(first, count)],
            final[item].at[pl.ds(first + (1 if sign > 0 else 0), count)],
            2 * chips + (0 if sign > 0 else 1),
            (place.w, node),
        )

    def send_hop(item, sign, hop):
        sender = me == (hop - 1 if sign > 0 else narrow - hop)

        @pl.when(sender)
        def _():
            hopping(item, sign, hop).start()

        guarded.append((sender, hopping(item, sign, hop)))

    def hop_event(item, hop):
        count = narrow - hop - 1
        for sign in (1, -1):
            first = hop + 1 if sign > 0 else 0
            shift = 1 if sign > 0 else 0

            @pl.when(me == (hop if sign > 0 else narrow - 1 - hop))
            def _():
                hopping(item, sign, hop).wait_recv()
                if count:
                    mine, theirs = pl.ds(first, count), pl.ds(first + shift, count)
                    value = held[item][0, mine].astype(F32) + final[item][theirs].astype(F32)
                    held[item][0, mine] = value.astype(BF16)

            if count:
                send_hop(item, sign, hop + 1)
        if count:
            hop_transfer(item, hop + 1)
        else:
            finish(item)

    def hop_transfer(item, hop):
        cost = (narrow - hop) * 2 * block_bytes(item) / narrow / LINK
        event = functools.partial(hop_event, item, hop)
        plan.transfer(0 if hop == 1 else 100 + hop, cost, (item, -hop, 0), event)

    def along(item, step):
        target = place.along(step)
        return remote(
            item,
            held[item].at[0, target[1]],
            final[item].at[narrow - step - 1],
            2 * chips + narrow - step - 1,
            target,
        )

    def leaves(item, mask):
        bits = bits_of(item)
        return min([number for number, bit in enumerate(bits) if mask & bit], default=len(bits))

    def slot_of(item, mask, number):
        bits = bits_of(item)
        kept = [m for m in range(chips) if not any(m & bit for bit in bits[: number + 1])]
        return kept.index(mask)

    def add_into(dest, dest_at, src, src_at):
        dest[dest_at] = (dest[dest_at].astype(F32) + src[src_at].astype(F32)).astype(BF16)

    def block_bytes(item):
        _, nodes, rows, width = held[item].shape
        return 2 * nodes * rows * width

    def push(which, pair=None):
        for item, (owner, begin, _, _) in enumerate(items):
            if owner != which or (pair is not None and begin // (3 * reach) != pair):
                continue
            for masks in groups_of(item):
                cost = len(masks) * block_bytes(item) / 1e6
                plan.work(cost, functools.partial(push_some, item, masks))

    def push_some(item, masks):
        which = items[item][0]
        for key in [key for key in last_sent if key[0] == which and set(key[1]) & set(masks)]:
            last_sent.pop(key).wait_send()
        product(item, masks, 1 - place.core, spare[which], False)
        copy = to_twin(item, masks)
        copy.start()
        last_sent[which, tuple(masks)] = copy
        cost = len(masks) * block_bytes(item) / TWIN_LINK
        plan.transfer(-1, cost, (item, 0, masks[0]), functools.partial(own_event, item, masks))

    def own_event(item, masks):
        to_twin(item, masks).wait_recv()
        product(item, masks, place.core, held[item], True)
        plan.now += len(masks) * block_bytes(item) / 1e6
        plan.done.update((item, 0, mask) for mask in masks)
        for mask in masks:
            onward(item, mask, 0)

    def onward(item, mask, number):
        bits = bits_of(item)
        if number == len(bits):
            lined.append(item)
            refill()
        elif leaves(item, mask) == number:
            kept = mask ^ bits[number]
            start(across(item, mask, bits[number], number, slot_of(item, kept, number)))
            plan.transfer(
                bits[number],
                2 * block_bytes(item) / LINK,
                (item, 1 + number, kept),
                functools.partial(sum_event, item, kept, number),
            )

    lined = []

    def refill():
        while lined and plan.free.get(0, 0.0) < plan.now + Z_AHEAD:
            item = lined.pop(0)
            if relayed(item):
                for sign in (1, -1):
                    send_hop(item, sign, 1)
                hop_transfer(item, 1)
                continue
            for step in range(1, narrow):
                start(along(item, step))
            cost = 2 * (narrow // 2) ** 2 * block_bytes(item) / narrow / LINK
            plan.transfer(0, cost, (item, -1, 0), functools.partial(finish, item))

    plan.refill = refill

    def sum_event(item, mask, number):
        plan.need([(item, before, mask) for before in range(number + 1)])
        bit = bits_of(item)[number]
        slot = slot_of(item, mask, number)
        across(item, mask ^ bit, bit, number, slot).wait_recv()
        add_into(held[item], mask, passed[item][number], slot)
        plan.now += block_bytes(item) / 8e5
        onward(item, mask, number + 1)

    at.squares[...] = jnp.zeros_like(at.squares)

    def finish(item):
        which, begin, width, _ = items[item]
        value = held[item][0, me].astype(F32)
        if relayed(item):
            value = value + jnp.where(me >= 1, final[item][me + 1].astype(F32), 0.0)
            value = value + jnp.where(me < narrow - 1, final[item][me].astype(F32), 0.0)
        else:
            for step in range(1, narrow):
                along(item, step).wait_recv()
            for slot in range(narrow - 1):
                value = value + final[item][slot].astype(F32)
        columns = pl.ds(0, value.shape[1])
        at.squares[:, columns] += jnp.sum(value * value, 0, keepdims=True)
        if which == 1:
            for shift in range(0, width, LANES):
                part, spot = (begin + shift) // reach, (begin + shift) % reach
                column = part % 3 * D + spot // LANES * head_width + part // 3 * LANES
                sums[which][:, pl.ds(column, LANES)] = value[:, shift : shift + LANES]
        elif which == 4:
            sums[which][pl.ds(begin, width), :] = value
        else:
            sums[which][:, pl.ds(begin, width)] = value

    norms[...] = jnp.zeros_like(norms)

    def norm_back(row, low, add):
        step_rows = 32

        def one(step, carry):
            rows = pl.ds(pl.multiple_of(step * step_rows, step_rows), step_rows)
            values = stash[rows, :]
            upper = d_norm[rows, :]
            centred = values - jnp.mean(values, -1, keepdims=True)
            rate = lax.rsqrt(jnp.mean(centred * centred, -1, keepdims=True) + 1e-05)
            unit = centred * rate
            norms[row : row + 1, :] += jnp.sum(upper * unit, 0, keepdims=True)
            norms[row + 3 : row + 4, :] += jnp.sum(upper, 0, keepdims=True)
            scaled = upper * gains[row : row + 1, :]
            inner = scaled - jnp.mean(scaled, -1, keepdims=True)
            inner = rate * (inner - unit * jnp.mean(scaled * unit, -1, keepdims=True))
            if add:
                inner = inner + d_res[rows, :]
            d_res[rows, :] = inner
            low[rows, :] = inner.astype(BF16)
            return carry

        lax.fori_loop(0, tokens // step_rows, one, 0)

    def loop_work(cost, count, pieces, body):
        for piece in range(pieces):
            low, high = count * piece // pieces, count * (piece + 1) // pieces
            plan.work(cost / pieces, functools.partial(lax.fori_loop, low, high, body, 0))

    load(at.t5).wait()
    push(5)
    load_stash(src.last).wait()
    count = D // u_rows
    tall_rows = slope_rows

    def through_unpatch(index, carry):
        ring(src.w5, at.tall, u_rows, u_cols, index, index * u_rows).wait()
        slot = at.tall.at[lax.rem(index, tall)]
        offset = pl.multiple_of(index * u_rows, u_rows)
        d_norm[:, pl.ds(offset, u_rows)] = back_mul(src.gauss[...], slot[0:u_rows, 0:u_cols])

        @pl.when(index + tall < count)
        def _():
            ring(src.w5, at.tall, u_rows, u_cols, index + tall, (index + tall) * u_rows).start()

        return carry

    loop_work(2.5, count, 1, through_unpatch)
    for index in range(tall):
        ring(src.w4, at.tall, tall_rows, D, index, index * tall_rows).start()
    plan.work(2.5, lambda: norm_back(2, shrink_low, False))
    load_stash(src.mid).start()
    load(at.hidden).wait()

    def turn_shrink():
        at.shrink_t[...] = shrink_low[...].T

    plan.work(2.0, turn_shrink)
    push(4)
    ff = src.w3.shape[1]
    slabs = ff // tall_rows

    def through_shrink(index, carry):
        ring(src.w4, at.tall, tall_rows, D, index, index * tall_rows).wait()
        slope_load(index).wait()
        slot = lax.rem(index, tall)
        value = back_mul(shrink_low[...], at.tall[slot])
        value = value * at.slope_slots[slot].astype(F32)
        expand_low[:, pl.ds(pl.multiple_of(index * tall_rows, tall_rows), tall_rows)] = value.astype(BF16)

        @pl.when(index + tall < slabs)
        def _():
            ring(src.w4, at.tall, tall_rows, D, index + tall, (index + tall) * tall_rows).start()
            slope_load(index + tall).start()

        return carry

    loop_work(6.0, slabs, 2, through_shrink)
    owners = [lax.rem(me + step, narrow) for step in list(range(1, narrow)) + [0]]
    for index in range(min(tall, narrow)):
        ring(src.w2, at.tall, head_width, D, index, owners[index] * head_width).start()
    load(at.t3).wait()

    def through_expand(index, carry):
        ring(src.w3, at.long, wide_rows, ff, index, index * wide_rows).wait()
        offset = pl.multiple_of(index * wide_rows, wide_rows)
        d_norm[:, pl.ds(offset, wide_rows)] = back_mul(expand_low[...], at.long[lax.rem(index, long)])

        @pl.when(index + long < D // wide_rows)
        def _():
            ring(src.w3, at.long, wide_rows, ff, index + long, (index + long) * wide_rows).start()

        return carry

    loop_work(5.0, D // wide_rows, 2, through_expand)
    for index in range(long):
        ring(src.w1, at.long, wide_rows, 3 * D, index, index * wide_rows).start()
    load_stash(src.mid).wait()
    plan.work(2.0, lambda: norm_back(1, merge_low, True))
    load_stash(src.embedded).start()

    def swap(src, dst, kind, step):
        return pltpu.make_async_remote_copy(
            src_ref=src,
            dst_ref=dst,
            send_sem=swap_send.at[kind, step],
            recv_sem=swap_recv.at[kind, step],
            device_id=place.along(step),
            device_id_type=MESH,
        )

    d_heads, away = at.d_heads, at.away
    piece = 2 * (narrow - 1) * 2 * tokens * head_width / LINK

    def head_event():
        for step in range(1, narrow):
            swap(away.at[step - 1], d_heads.at[me], 0, step).wait_recv()

    def through_merge(index, owner):
        ring(src.w2, at.tall, head_width, D, index, owner * head_width).wait()
        value = back_mul(merge_low[...], at.tall[index % tall, 0:head_width, :]).astype(BF16)
        if index < narrow - 1:
            away[index] = value
            start(swap(away.at[index], d_heads.at[me], 0, index + 1))
        else:
            d_heads[me] = value
        if index + tall < narrow:
            ring(src.w2, at.tall, head_width, D, index + tall, owners[index + tall] * head_width).start()

    for index, owner in enumerate(owners):
        plan.work(0.7, functools.partial(through_merge, index, owner))
    plan.transfer(0, piece, (-1, 0, 0), head_event)
    load(at.t2).wait()
    push(3)
    push(2)
    load(at.qkv).wait()
    load(at.heads_out).wait()
    load(at.log_sums).wait()
    plan.need([(-1, 0, 0)])

    qkv, heads_out, log_sums, parts = at.qkv, at.heads_out, at.log_sums, at.parts
    key_t, key_acc, value_acc, query_acc = at.key_t, at.key_acc, at.value_acc, at.query_acc
    lane = lax.broadcasted_iota(jnp.int32, (1, LANES), 1)
    sides = LANES // HD
    scale = HD ** (-0.5)
    choose = lax.broadcasted_iota(jnp.int32, (8, LANES), 1) // HD
    choose = (choose == lax.broadcasted_iota(jnp.int32, (8, LANES), 0)).astype(F32)

    def part_swap(pair, step):
        lanes = pl.ds(pair * LANES, LANES)
        who = lax.rem(me + step, narrow)
        return swap(
            parts.at[who, :, :, lanes],
            mixed.at[pair, :, :, pl.ds(pl.multiple_of(me * LANES, LANES), LANES)],
            1 + pair,
            step,
        )

    pushed_pairs = []
    load(at.t1).wait()

    def part_event(pair):
        for step in range(1, narrow):
            part_swap(pair, step).wait_recv()

    for pair in range(head_width // LANES):
        lanes = pl.ds(pair * LANES, LANES)
        key_t[...] = qkv[:, 1, :, lanes].reshape(length, LANES).T
        key_acc[...] = jnp.zeros_like(key_acc)
        value_acc[...] = jnp.zeros_like(value_acc)
        def one_block(step, lanes=lanes, pair=pair):
            who = lax.rem(me + step, narrow)
            query = qkv[who, 0, :, lanes].astype(F32)
            upper = d_heads[who, :, lanes].astype(F32)
            kept = heads_out[who, :, lanes].astype(F32)
            delta = lax.dot_general(
                choose,
                upper * kept,
                (((1,), (1,)), ((), ())),
                precision=HIGHEST,
                preferred_element_type=F32,
            )
            log_rows = log_sums[who].T[pair * sides : (pair + 1) * sides, :]
            masks = [jnp.where(lane // HD == side, 1.0, 0.0) for side in range(sides)]
            own_query = jnp.concatenate([query * (scale * mask) for mask in masks], 0).astype(BF16)
            own_upper = jnp.concatenate([upper * mask for mask in masks], 0).astype(BF16)
            log_row = jnp.concatenate([log_rows[side : side + 1, :] for side in range(sides)], 1)
            delta_row = jnp.concatenate([delta[side : side + 1, :] for side in range(sides)], 1)
            query_acc[...] = jnp.zeros_like(query_acc)

            at_once = max(1, KEY_ROWS // tokens)
            for source in range(0, narrow, at_once):
                rows = pl.ds(source * tokens, at_once * tokens)
                some = pl.ds(source, at_once)
                key = qkv[some, 1, :, lanes].reshape(at_once * tokens, LANES)
                value = qkv[some, 2, :, lanes].reshape(at_once * tokens, LANES)
                probs = jnp.exp(back_mul(key, own_query) - log_row)
                d_probs = back_mul(value, own_upper)
                d_scores = (probs * (d_probs - delta_row)).astype(BF16)
                value_acc[rows, :] += matmul(probs.astype(BF16), own_upper)
                key_acc[rows, :] += matmul(d_scores, own_query)
                turned = matmul(key_t[:, rows], d_scores)
                for side in range(sides):
                    spot = slice(side * HD, (side + 1) * HD)
                    query_acc[spot, :] += turned[spot, side * tokens : (side + 1) * tokens]

            parts[who, 0, :, lanes] = (query_acc[...].T * scale).astype(BF16)
        for step in range(narrow):
            plan.work(4.0, functools.partial(one_block, step), step > 0)
            for earlier in range(pair):
                if earlier not in pushed_pairs and (-2, 0, earlier) in plan.done:
                    pushed_pairs.append(earlier)
                    push(1, earlier)
        for source in range(narrow):
            rows = pl.ds(source * tokens, tokens)
            parts[source, 1, :, lanes] = key_acc[rows, :].astype(BF16)
            parts[source, 2, :, lanes] = value_acc[rows, :].astype(BF16)
        for step in range(1, narrow):
            start(part_swap(pair, step))
        plan.now += 1.0
        plan.transfer(0, 1.5 * piece, (-2, 0, pair), functools.partial(part_event, pair))
        mixed[pair, :, :, pl.ds(pl.multiple_of(me * LANES, LANES), LANES)] = parts[me, :, :, lanes]
    for pair in range(head_width // LANES):
        if pair not in pushed_pairs:
            plan.need([(-2, 0, pair)])
            push(1, pair)

    def through_mixer(index, carry):
        ring(src.w1, at.long, wide_rows, 3 * D, index, index * wide_rows).wait()
        slot = lax.rem(index, long)
        value = jnp.zeros((tokens, wide_rows), F32)
        for pair in range(head_width // LANES):
            for part in range(3):
                columns = [part * D + owner * head_width + pair * LANES for owner in range(narrow)]
                weight = [at.long[slot, :, column : column + LANES] for column in columns]
                value = value + back_mul(mixed[pair, part], jnp.concatenate(weight, 1))
        d_norm[:, pl.ds(pl.multiple_of(index * wide_rows, wide_rows), wide_rows)] = value

        @pl.when(index + long < D // wide_rows)
        def _():
            ring(src.w1, at.long, wide_rows, 3 * D, index + long, (index + long) * wide_rows).start()

        return carry

    plan.work(4.0, lambda: lax.fori_loop(0, D // wide_rows, through_mixer, 0))
    load_stash(src.embedded).wait()
    plan.work(3.0, lambda: norm_back(0, at.embed_low, True))
    at.embed_t[...] = at.embed_low[...].T
    turned = jnp.concatenate([norms[...], jnp.zeros((LANES - 8, D), F32)], 0).T
    at.extra[...] = pltpu.roll(turned, lead, 1)
    push(0)
    plan.finish()

    rows = lax.broadcasted_iota(jnp.int32, (8, LANES), 0)
    wide_tiles, narrow_tiles = at.wide_tiles, at.narrow_tiles
    wide_tiles[place.w] = jnp.where(rows == 0, src.term[...], jnp.sum(at.squares[...]))

    def tile_copy(buffer, index, slot, peer):
        return pltpu.make_async_remote_copy(
            src_ref=buffer.at[index],
            dst_ref=buffer.at[index],
            send_sem=tile_send.at[slot],
            recv_sem=tile_recv.at[slot],
            device_id=peer,
            device_id_type=MESH,
        )

    for step in range(1, wide):
        start(tile_copy(wide_tiles, place.w, step - 1, (lax.rem(place.w + step, wide), place.n)))
    for step in range(1, wide):
        tile_copy(wide_tiles, place.w, step - 1, (lax.rem(place.w + step, wide), place.n)).wait_recv()
    whole = wide_tiles[0]
    for index in range(1, wide):
        whole = whole + wide_tiles[index]
    narrow_tiles[place.n] = whole
    for step in range(1, narrow):
        start(tile_copy(narrow_tiles, place.n, wide + step - 1, place.along(step)))
    for step in range(1, narrow):
        tile_copy(narrow_tiles, place.n, wide + step - 1, place.along(step)).wait_recv()
    whole = narrow_tiles[0]
    for index in range(1, narrow):
        whole = whole + narrow_tiles[index]
    totals[...] = whole
    for copy in list(last_sent.values()) + started:
        copy.wait_send()
    for condition, copy in guarded:

        @pl.when(condition)
        def _():
            copy.wait_send()


def backward_all(kept, patches, gauss, term, lead, wide, narrow):
    tokens = patches.shape[0]
    chips = wide // 2
    weights = [kept.w1, kept.w2, kept.w3, kept.w4, kept.w5]
    heights = [D] + [weight.shape[0] for weight in weights]
    widths = [patches.shape[1]] + [weight.shape[1] for weight in weights]
    rows = [height // (wide * narrow) for height in heights]
    head_width = D // narrow
    length = narrow * tokens
    items = backward_plan(widths, head_width // LANES)
    slots = 2 * chips + max(2, narrow - 1)
    streamed = dict(w1=kept.w1, w2=kept.w2, w3=kept.w3, w4=kept.w4, w5=kept.w5)
    streamed.update(last=kept.last, mid=kept.mid, embedded=kept.embedded, slopes=kept.slopes)
    loaded = dict(t5=kept.t5, hidden=kept.hidden, t3=kept.t3, t2=kept.t2, t1=kept.t1)
    loaded.update(qkv=kept.qkv, heads_out=kept.heads_out, log_sums=kept.log_sums)
    whole = dict(gains=kept.gains, patches=patches, gauss=gauss, term=term)
    operands = {**streamed, **loaded, **whole}
    shapes = [jax.ShapeDtypeStruct((rows[which], widths[which]), F32) for which in range(6)]
    shapes[4] = jax.ShapeDtypeStruct((D, rows[4]), F32)
    shapes.append(jax.ShapeDtypeStruct((8, LANES), F32))
    scratch = {name: pltpu.VMEM(value.shape, value.dtype) for name, value in loaded.items()}
    blocks = [(width, rows[which]) if which == 4 else (rows[which], width) for which, _, width, _ in items]
    scratch.update(
        squares=pltpu.VMEM((1, max(block[1] for block in blocks)), F32),
        embed_t=pltpu.VMEM((D, tokens), BF16),
        embed_low=pltpu.VMEM((tokens, D), BF16),
        shrink_t=pltpu.VMEM((D, tokens), BF16),
        stash=pltpu.VMEM((tokens, D), F32),
        d_res=pltpu.VMEM((tokens, D), F32),
        d_norm=pltpu.VMEM((tokens, D), F32),
        norms=pltpu.VMEM((8, D), F32),
        extra=pltpu.VMEM((D, LANES), F32),
        shrink_low=pltpu.VMEM((tokens, D), BF16),
        expand_low=pltpu.VMEM((tokens, widths[3]), BF16),
        merge_low=pltpu.VMEM((tokens, D), BF16),
        mixed=pltpu.VMEM((head_width // LANES, 3, tokens, narrow * LANES), BF16),
        tall=pltpu.VMEM((4, 256, D), BF16),
        long=pltpu.VMEM((2, 256, widths[3]), BF16),
        slope_slots=pltpu.VMEM((4, tokens, 256), BF16),
        d_heads=pltpu.VMEM((narrow, tokens, head_width), BF16),
        away=pltpu.VMEM((narrow - 1, tokens, head_width), BF16),
        parts=pltpu.VMEM((narrow, 3, tokens, head_width), BF16),
        key_t=pltpu.VMEM((LANES, length), BF16),
        key_acc=pltpu.VMEM((length, LANES), F32),
        value_acc=pltpu.VMEM((length, LANES), F32),
        query_acc=pltpu.VMEM((LANES, tokens), F32),
        wide_tiles=pltpu.VMEM((wide, 8, LANES), F32),
        narrow_tiles=pltpu.VMEM((narrow, 8, LANES), F32),
        send_sem=pltpu.SemaphoreType.DMA((len(items), slots)),
        recv_sem=pltpu.SemaphoreType.DMA((len(items), slots)),
        tile_send=pltpu.SemaphoreType.DMA((wide + narrow,)),
        tile_recv=pltpu.SemaphoreType.DMA((wide + narrow,)),
        swap_send=pltpu.SemaphoreType.DMA((1 + head_width // LANES, narrow)),
        swap_recv=pltpu.SemaphoreType.DMA((1 + head_width // LANES, narrow)),
        in_sem=pltpu.SemaphoreType.DMA((9,)),
        ring_sem=pltpu.SemaphoreType.DMA((3, 4)),
    )
    lists = [pltpu.VMEM((chips, narrow) + block, BF16) for block in blocks]
    for block in blocks:
        for bit in chip_bits(chips):
            lists.append(pltpu.VMEM((chips // (2 * bit), narrow) + block, BF16))
    for (which, _, _, _), block in zip(items, blocks):
        lists.append(pltpu.VMEM((narrow + (1 if which in RELAYED else -1),) + block, BF16))
    for which in range(6):
        widest = max(block for item, block in zip(items, blocks) if item[0] == which)
        lists.append(pltpu.VMEM((chips, narrow) + widest, BF16))
    vmem = pl.BlockSpec(memory_space=pltpu.VMEM)
    hbm = pl.BlockSpec(memory_space=pl.ANY)
    return pl.pallas_call(
        functools.partial(backward_kernel, items, wide, narrow, lead, tuple(operands), tuple(scratch)),
        out_shape=shapes,
        in_specs=[vmem if name in whole else hbm for name in operands],
        out_specs=[vmem] * len(shapes),
        scratch_shapes=list(scratch.values()) + lists,
        compiler_params=pltpu.CompilerParams(
            collective_id=1, has_side_effects=True, vmem_limit_bytes=63 * MIB
        ),
        name="backward",
    )(*operands.values())


def spread_weights(source, dest):
    for slot in range(source.shape[0]):
        for view in range(source.shape[1]):
            dest[view * PP : (view + 1) * PP, slot * PP : (slot + 1) * PP] = source[slot, view]


def count_pairs(pair_ref, counts):
    quads, span = counts.shape[0] // 2, counts.shape[1]
    some = 512
    counts[...] = jnp.zeros_like(counts)

    def one(step, carry):
        where = pl.ds(pl.multiple_of(step * some, some), some)
        first, second = pair_ref[0:1, where], pair_ref[1:2, where]
        least = jnp.minimum(first, second)
        down = (jnp.abs(first - second) == P_SIZE).astype(jnp.int32)
        place = quads * PP
        slot, local = least // place, least % place
        high = down * quads + local // PP
        low = slot * PP + local % PP
        high_hot = (lax.broadcasted_iota(jnp.int32, (2 * quads, some), 0) == high).astype(F32).astype(BF16)
        low_hot = (lax.broadcasted_iota(jnp.int32, (span, some), 0) == low).astype(F32).astype(BF16)
        counts[...] += back_mul(high_hot, low_hot)
        return carry

    lax.fori_loop(0, pair_ref.shape[1] // some, one, 0)


def render_kernel(
    gauss_ref, weight_ref, target_ref, mask_ref, pair_ref, view_ref, total_ref, grad_ref, term_ref, feat, dfeat, counts
):
    count_pairs(pair_ref, counts)
    render_block(
        gauss_ref, weight_ref, target_ref, mask_ref, counts, view_ref, total_ref, grad_ref, term_ref, feat, dfeat
    )


def render_block(
    gauss_ref, weight_ref, target_ref, mask_ref, counts, view_ref, total_ref, grad_ref, term_ref, feat, dfeat
):
    quads = gauss_ref.shape[0] // NVIEW
    span = weight_ref.shape[1]
    scale = 1.0 / total_ref[0].astype(F32)

    def channel(index):
        return gauss_ref[:, index * PP : (index + 1) * PP]

    def shared():
        opacity = jax.nn.sigmoid(channel(3))
        extent = jax.nn.sigmoid(channel(5) + channel(6) + channel(7))
        lead = channel(8)
        denom = 1.0 + lead * lead + channel(9) * channel(9) + channel(10) * channel(10) + channel(11) * channel(11)
        facing = lead * lead / denom
        raw = channel(4)
        depth = jnp.maximum(raw, 0.0) + jnp.log1p(jnp.exp(-jnp.abs(raw)))
        return opacity, extent, lead, denom, facing, raw, depth

    opacity, extent, lead, denom, facing, raw, depth = shared()
    footprint = opacity * extent * facing
    channels = [jax.nn.sigmoid(channel(index)) * footprint for index in range(3)]
    channels += [footprint, depth * footprint]
    for index, value in enumerate(channels):
        for view in range(NVIEW):
            feat[index * quads : (index + 1) * quads, view * PP : (view + 1) * PP] = value[
                view * quads : (view + 1) * quads
            ]
    rendered = jnp.dot(feat[...], weight_ref[...], precision=HIGHEST, preferred_element_type=F32)
    parts = [rendered[index * quads : (index + 1) * quads] for index in range(5)]
    lane = lax.broadcasted_iota(jnp.int32, (quads, span), 1)
    live = jnp.where(lane < view_ref[0] * PP, mask_ref[...], 0).astype(F32)
    term = jnp.zeros((quads, span), F32)
    slopes = []
    for index in range(3):
        error = parts[index] - target_ref[index * quads : (index + 1) * quads, :].astype(F32)
        term = term + live * error * error
        slopes.append(2.0 * scale * live * error)
    below = 1.0 + parts[3]
    depth_out = parts[4] / below

    slope = jnp.zeros((quads, span), F32)
    for which, shift in enumerate((1, P_SIZE)):
        count = counts[which * quads : (which + 1) * quads]
        weight = DEPTH_WEIGHT * count * live * pltpu.roll(live, span - shift, 1)
        gap = depth_out - pltpu.roll(depth_out, span - shift, 1)
        term = term + weight * gap * gap
        pull = 2.0 * scale * weight * gap
        slope = slope + pull - pltpu.roll(pull, shift, 1)
    term_ref[...] = jnp.full(term_ref.shape, jnp.sum(term), F32)
    over = slope / below
    slopes += [-over * depth_out, over]
    stacked = jnp.concatenate(slopes, 0)
    dfeat[...] = lax.dot_general(
        stacked, weight_ref[...], (((1,), (1,)), ((), ())), precision=HIGHEST, preferred_element_type=F32
    )

    def feature_grad(index):
        return jnp.concatenate(
            [
                dfeat[index * quads : (index + 1) * quads, view * PP : (view + 1) * PP]
                for view in range(NVIEW)
            ],
            0,
        )

    def put(index, value):
        grad_ref[:, index * PP : (index + 1) * PP] = value.astype(BF16)

    d_foot = feature_grad(3)
    for index in range(3):
        tint = jax.nn.sigmoid(channel(index))
        upper = feature_grad(index)
        d_foot = d_foot + upper * tint
        put(index, upper * footprint * tint * (1.0 - tint))
    d_last = feature_grad(4)
    d_foot = d_foot + d_last * depth
    put(3, d_foot * extent * facing * opacity * (1.0 - opacity))
    put(4, d_last * footprint * jax.nn.sigmoid(raw))
    d_extent = d_foot * opacity * facing * extent * (1.0 - extent)
    for index in (5, 6, 7):
        put(index, d_extent)
    d_facing = d_foot * opacity * extent
    put(8, d_facing * 2.0 * lead / denom * (1.0 - facing))
    for index in (9, 10, 11):
        put(index, -2.0 * d_facing * facing / denom * channel(index))


def scene_targets(targets, mask, quads):
    slots = targets.shape[0]
    wanted = targets.reshape(slots, 3, quads, PP).transpose(1, 2, 0, 3).reshape(3 * quads, slots * PP)
    valid = mask.reshape(slots, quads, PP).transpose(1, 0, 2).reshape(quads, slots * PP)
    return wanted, valid


def render(gaussians, weights, targets, mask, pairs, view_count, pair_total):
    slots, views = weights.shape[:2]
    spread = weights.transpose(1, 2, 0, 3).reshape(views * PP, slots * PP)
    quads = gaussians.shape[0] // NVIEW
    wanted, valid = scene_targets(targets, mask, quads)
    vmem = pl.BlockSpec(memory_space=pltpu.VMEM)
    smem = pl.BlockSpec(memory_space=pltpu.SMEM)
    return pl.pallas_call(
        render_kernel,
        out_shape=[
            jax.ShapeDtypeStruct(gaussians.shape, BF16),
            jax.ShapeDtypeStruct((8, LANES), F32),
        ],
        in_specs=[vmem] * 5 + [smem] * 2,
        out_specs=[vmem] * 2,
        scratch_shapes=[pltpu.VMEM((5 * quads, views * PP), F32)] * 2
        + [pltpu.VMEM((2 * quads, slots * PP), F32)],
        compiler_params=pltpu.CompilerParams(vmem_limit_bytes=48 * MIB),
        name="render",
    )(gaussians, spread, wanted, valid, pairs, view_count, pair_total)


def forward_plain(shards, patches, features, kinds):
    weights = [lax.all_gather(shard, BOTH, axis=0, tiled=True) for shard in shards]
    groups = lax.axis_size(NARROW)
    rows = patches.shape[0]
    gains = weights[0][:, features : features + kinds].T.astype(F32)
    embedded = back_mul(patches[:, :features], weights[0][:, :features])
    normed_one = layer_norm(embedded, gains[0], gains[3]).astype(BF16)
    mixed = matmul(normed_one, weights[1]).astype(BF16).reshape(rows, 3, groups, -1)
    mixed = mixed.transpose(2, 1, 0, 3)
    qkv = lax.all_to_all(mixed, NARROW, split_axis=0, concat_axis=0, tiled=True)
    width = qkv.shape[-1]
    length = groups * rows
    heads = width // HD
    parts = [qkv[:, part].reshape(length, heads, HD) for part in range(3)]
    attended, logsum = attention_forward(*parts)
    log_sums = logsum.transpose(0, 2, 1).reshape(groups, rows, heads)
    returned = lax.all_to_all(
        attended.reshape(groups, rows, width), NARROW, split_axis=0, concat_axis=0, tiled=True
    )
    returned = returned.transpose(1, 0, 2).reshape(rows, D)
    mid = embedded + matmul(returned, weights[2])
    normed_two = layer_norm(mid, gains[1], gains[4]).astype(BF16)
    expanded = matmul(normed_two, weights[3])
    half = 0.5 * (1.0 + lax.erf(expanded * (0.5**0.5)))
    activated = (expanded * half).astype(BF16)
    bell = jnp.exp(-0.5 * expanded * expanded) * 0.3989422804014327
    slopes = (half + expanded * bell).astype(BF16)
    last = mid + matmul(activated, weights[4])
    normed_three = layer_norm(last, gains[2], gains[5]).astype(BF16)
    return Bag(
        dict(
        w1=weights[1],
        w2=weights[2],
        w3=weights[3],
        w4=weights[4],
        w5=weights[5],
        gains=gains,
        embedded=embedded,
        mid=mid,
        last=last,
        slopes=slopes,
        t1=normed_one.T,
        t2=returned.T,
        t3=normed_two.T,
        hidden=activated,
        t5=normed_three.T,
        qkv=qkv,
        heads_out=attended,
        log_sums=log_sums,
        gaussians=matmul(normed_three, weights[5]),
    ).items())


def backward_plain(kept, patches, gauss_low, term, features, kinds):
    gains = kept.gains
    weights = [None, kept.w1, kept.w2, kept.w3, kept.w4, kept.w5]
    norm_back_one = jax.vjp(layer_norm, kept.embedded, gains[0], gains[3])[1]
    norm_back_two = jax.vjp(layer_norm, kept.mid, gains[1], gains[4])[1]
    norm_back_three = jax.vjp(layer_norm, kept.last, gains[2], gains[5])[1]
    qkv = kept.qkv
    groups, _, rows, width = qkv.shape
    length = groups * rows
    heads = width // HD
    queries, keys, values = (qkv[:, part].reshape(length, heads, HD) for part in range(3))
    blocked = min(512, length)
    logsum = kept.log_sums[:, :, :heads].reshape(length // blocked, blocked, heads)
    residual_grad, gain_three, shift_three = norm_back_three(back_mul(gauss_low, weights[5]))
    shrink_low = residual_grad.astype(BF16)
    expand_low = (back_mul(shrink_low, weights[4]) * kept.slopes.astype(F32)).astype(BF16)
    through_two, gain_two, shift_two = norm_back_two(back_mul(expand_low, weights[3]))
    residual_grad = residual_grad + through_two
    merge_low = residual_grad.astype(BF16)
    out_grad = back_mul(merge_low, weights[2]).astype(BF16).reshape(rows, groups, width)
    head_grad = lax.all_to_all(
        out_grad.transpose(1, 0, 2), NARROW, split_axis=0, concat_axis=0, tiled=True
    ).reshape(length, heads, HD)
    grads = attention_backward(queries, keys, values, logsum.transpose(0, 2, 1), head_grad)
    stacked = jnp.stack(grads, 1).astype(BF16).reshape(groups, rows, 3, width)
    mixed_grad = lax.all_to_all(stacked, NARROW, split_axis=0, concat_axis=0, tiled=True)
    mixed_grad = mixed_grad.transpose(1, 2, 0, 3).reshape(rows, 3 * D)
    through_one, gain_one, shift_one = norm_back_one(back_mul(mixed_grad, weights[1]))
    embed_grad = (residual_grad + through_one).astype(BF16)
    grad_norms = jnp.stack([gain_one, gain_two, gain_three, shift_one, shift_two, shift_three])
    lefts = [embed_grad.T, kept.t1, kept.t2, kept.t3, kept.hidden.T, kept.t5]
    rights = [patches, mixed_grad, merge_low, expand_low, shrink_low, gauss_low]
    products = [matmul(left, right) for left, right in zip(lefts, rights)]
    products[0] = products[0].at[:, features : features + kinds].add(grad_norms.T)
    sums = [
        lax.psum_scatter(
            product.astype(BF16), BOTH, scatter_dimension=0, tiled=True
        ).astype(F32)
        for product in products
    ]
    squares = sum(jnp.sum(part * part) for part in sums)
    loss_sum, square_sum = lax.psum((term[0, 0], squares), BOTH)
    return sums, loss_sum, square_sum


def update_kernel(features, total_ref, sums_ref, *refs):
    sources, targets, refs = refs[:27], refs[27:48], refs[48:]
    loss_ref, norm_ref, refs = refs[0], refs[1], refs[2:]
    inside, news, refs = refs[:27], refs[27:48], refs[48:]
    turned, turned_four, in_sem, out_sem = refs
    loads = [pltpu.make_async_copy(source, dest, in_sem.at[i]) for i, (source, dest) in enumerate(zip(sources, inside))]
    stores = [pltpu.make_async_copy(source, dest, out_sem.at[i]) for i, (source, dest) in enumerate(zip(news, targets))]
    for copy in loads:
        copy.start()
    grads, olds = inside[:6], inside[6:]
    square_sum = sums_ref[1:2, 0:1]
    grad_norm = jnp.sqrt(square_sum)
    factor = jnp.minimum(1.0, CLIP_NORM / (grad_norm + 1e-06))
    norm_ref[...] = grad_norm
    loss_ref[...] = sums_ref[0:1, 0:1] / total_ref[0].astype(F32)
    width = grads[0].shape[1]
    for which in range(7):
        if which < 6:
            loads[which].wait()
        if which == 0:
            turned[...] = grads[0][:, width - LANES :].T
        if which == 4:
            turned_four[...] = grads[4][...].T
        for copy in loads[6 + 3 * which : 9 + 3 * which]:
            copy.wait()
        weight, first, second = olds[3 * which : 3 * which + 3]
        rows, columns = weight.shape
        chunk = min(8, rows)

        def one(step, carry):
            spot = pl.ds(pl.multiple_of(step * chunk, chunk), chunk)
            if which == 0:
                grad = grads[0][spot, 0:columns]
            elif which == 4:
                grad = turned_four[spot, :]
            elif which == 6:
                grad = turned[features % LANES : features % LANES + rows, 0:columns]
            else:
                grad = grads[which][spot, :]
            values = adamw(weight[spot, :], first[spot, :], second[spot, :], grad * factor, RATES[which])
            for dest, value in zip(news[3 * which : 3 * which + 3], values):
                dest[spot, :] = value
            return carry

        lax.fori_loop(0, rows // chunk, one, 0)
        for copy in stores[3 * which : 3 * which + 3]:
            copy.start()
    for copy in stores:
        copy.wait()


def update_all(olds, sums, totals, pair_total, features):
    vmem = pl.BlockSpec(memory_space=pltpu.VMEM)
    smem = pl.BlockSpec(memory_space=pltpu.SMEM)
    hbm = pl.BlockSpec(memory_space=pltpu.HBM)
    shapes = [jax.ShapeDtypeStruct(old.shape, F32) for old in olds]
    inside = [pltpu.VMEM(value.shape, F32) for value in list(sums) + list(olds)]
    return pl.pallas_call(
        functools.partial(update_kernel, features),
        out_shape=shapes + [jax.ShapeDtypeStruct((1, 1), F32)] * 2,
        in_specs=[smem, vmem] + [hbm] * 27,
        out_specs=[hbm] * 21 + [vmem] * 2,
        scratch_shapes=inside
        + [pltpu.VMEM(old.shape, F32) for old in olds]
        + [
            pltpu.VMEM((LANES, sums[0].shape[0]), F32),
            pltpu.VMEM(olds[12].shape, F32),
            pltpu.SemaphoreType.DMA((27,)),
            pltpu.SemaphoreType.DMA((21,)),
        ],
        compiler_params=pltpu.CompilerParams(vmem_limit_bytes=60 * MIB),
        name="update",
    )(pair_total, totals, *sums, *olds)


def body(
    views,
    render_w,
    targets,
    pix_mask,
    pairs,
    view_count,
    pair_total,
    embed_weight,
    embed_first,
    embed_second,
    mixer_weight,
    mixer_first,
    mixer_second,
    merge_weight,
    merge_first,
    merge_second,
    expand_weight,
    expand_first,
    expand_second,
    shrink_weight,
    shrink_first,
    shrink_second,
    unpatch_weight,
    unpatch_first,
    unpatch_second,
    norm_params,
    norm_first,
    norm_second,
):
    masters = (embed_weight, mixer_weight, merge_weight, expand_weight, shrink_weight, unpatch_weight, norm_params)
    firsts = (embed_first, mixer_first, merge_first, expand_first, shrink_first, unpatch_first, norm_first)
    seconds = (embed_second, mixer_second, merge_second, expand_second, shrink_second, unpatch_second, norm_second)
    groups = lax.axis_size(NARROW)
    wide_count = lax.axis_size(WIDE)
    features = embed_weight.shape[0]
    kinds = norm_params.shape[0]
    padded = -(-(features + kinds) // LANES) * LANES
    fill = padded - features - kinds
    by_kernel = mixer_weight.shape[0] % 16 == 0 and shrink_weight.shape[0] % LANES == 0

    patches = views.reshape(-1, features)
    if by_kernel:
        raw = (embed_weight.T,) + masters[1:6]
        wanted, valid = scene_targets(targets[0], pix_mask[0], patches.shape[0] // NVIEW)
        scene = (render_w[0], wanted, valid, pairs[0], view_count, pair_total)
        kept = forward_all(raw, norm_params, patches, scene, wide_count, groups)
        *sums, totals = backward_all(
            kept, kept.padded, kept.gauss, kept.term, features % LANES, wide_count, groups
        )
        olds = []
        for triple in zip(masters, firsts, seconds):
            olds += triple
        olds[:3] = [old.T for old in olds[:3]]
        *news, loss, grad_norm = update_all(olds, sums, totals, pair_total, features)
        news[:3] = [new.T for new in news[:3]]
        return tuple(news) + (loss[0, 0], grad_norm[0, 0])
    else:
        patches = jnp.pad(patches, ((0, 0), (0, padded - features)))
        first_shard = jnp.concatenate([embed_weight.T, norm_params.T], 1)
        first_shard = jnp.pad(first_shard.astype(BF16), ((0, 0), (0, fill)))
        shards = [first_shard] + [weight.astype(BF16) for weight in masters[1:6]]
        kept = forward_plain(shards, patches, features, kinds)
    divisor = pair_total[0].astype(F32)
    gauss_low, term = render(
        kept.gaussians, render_w[0], targets[0], pix_mask[0], pairs[0], view_count, pair_total
    )
    sums, loss_sum, square_sum = backward_plain(kept, patches, gauss_low, term, features, kinds)
    first_sum = sums[0].T
    grads = [first_sum[:features]] + list(sums[1:]) + [first_sum[features : features + kinds]]
    loss = loss_sum / divisor
    grad_norm = jnp.sqrt(square_sum)
    factor = jnp.minimum(1.0, CLIP_NORM / (grad_norm + 1e-06))
    results = []
    for which in range(7):
        results += adamw(masters[which], firsts[which], seconds[which], grads[which] * factor, RATES[which])
    return tuple(results) + (loss, grad_norm)


def solution(mesh):
    columns = P(None, BOTH)
    rows = P(BOTH, None)
    weights = (columns,) * 3 + (rows,) * 15 + (columns,) * 3
    return jax.shard_map(
        body,
        mesh=mesh,
        in_specs=(
            P(WIDE, None, NARROW, None),
            P(WIDE, None, None, None, None),
            P(WIDE, None, None, NARROW),
            P(WIDE, None, NARROW),
            P(WIDE, None, NARROW),
            P(WIDE),
            P(),
        )
        + weights,
        out_specs=weights + (P(), P()),
        check_vma=False,
    )
```

```python
import functools
import heapq

import jax
import jax.numpy as jnp
from jax import lax
from jax.experimental import pallas as pl
from jax.experimental.pallas import tpu as pltpu
from jax.sharding import PartitionSpec as P

D = 1024
HD = 64
P_SIZE = 8
PP = 64
NVIEW = 4
TMAX = 12
STEP = 10
LANES = 128
MIB = 1024 * 1024

DEPTH_WEIGHT = 1.0
CLIP_NORM = 0.01
BETA_ONE = 0.9
BETA_TWO = 0.95
ADAM_EPS = 1e-08
DECAY = 0.05
RATES = (0.05, 0.05, 0.5, 0.05, 0.05, 0.05, 0.8)
MESH = pl.DeviceIdType.MESH
WIDE, NARROW = BOTH = ("wide", "narrow")
HIGHEST = lax.Precision.HIGHEST
F32 = jnp.float32
BF16 = jnp.bfloat16


def matmul(left, right):
    return jnp.dot(left, right, preferred_element_type=F32)


def outer_sum(left, right):
    return lax.dot_general(left, right, (((0,), (0,)), ((), ())), preferred_element_type=F32)


def back_mul(grad, weight):
    return lax.dot_general(grad, weight, (((1,), (1,)), ((), ())), preferred_element_type=F32)


def layer_norm(values, gain, shift):
    centred = values - jnp.mean(values, -1, keepdims=True)
    spread = jnp.mean(centred * centred, -1, keepdims=True)
    return centred * lax.rsqrt(spread + 1e-05) * gain + shift


def exact_gelu(values):
    return jax.nn.gelu(values, approximate=False)


def attention_forward(queries, keys, values):
    length, heads = (queries.shape[0], queries.shape[1])
    blocked = min(512, length)
    scale = HD ** (-0.5)

    def one_block(query_block):
        scores = (
            jnp.einsum("qhd,khd->hqk", query_block, keys, preferred_element_type=jnp.float32)
            * scale
        )
        highest = jnp.max(scores, -1, keepdims=True)
        exponentials = jnp.exp(scores - highest)
        summed = jnp.sum(exponentials, -1, keepdims=True)
        softmaxed = (exponentials / summed).astype(jnp.bfloat16)
        output = jnp.einsum("hqk,khd->qhd", softmaxed, values, preferred_element_type=jnp.float32)
        return (output.astype(jnp.bfloat16), (highest + jnp.log(summed))[:, :, 0])

    output, logsum = lax.map(one_block, queries.reshape(length // blocked, blocked, heads, HD))
    return (output.reshape(length, heads * HD), logsum)


def attention_backward(queries, keys, values, logsum, out_grad):
    length, heads = (queries.shape[0], queries.shape[1])
    blocked = min(512, length)
    scale = HD ** (-0.5)

    def one_block(carry, inputs):
        key_grad, value_grad = carry
        query_block, logsum_block, grad_block = inputs
        scores = (
            jnp.einsum("qhd,khd->hqk", query_block, keys, preferred_element_type=jnp.float32)
            * scale
        )
        softmaxed = jnp.exp(scores - logsum_block[:, :, None])
        value_grad = value_grad + jnp.einsum(
            "hqk,qhd->khd",
            softmaxed.astype(jnp.bfloat16),
            grad_block,
            preferred_element_type=jnp.float32,
        )
        prob_grad = jnp.einsum(
            "qhd,khd->hqk", grad_block, values, preferred_element_type=jnp.float32
        )
        score_grad = softmaxed * (prob_grad - jnp.sum(softmaxed * prob_grad, -1, keepdims=True))
        score_low = score_grad.astype(jnp.bfloat16)
        query_grad = (
            jnp.einsum("hqk,khd->qhd", score_low, keys, preferred_element_type=jnp.float32) * scale
        )
        key_grad = (
            key_grad
            + jnp.einsum("hqk,qhd->khd", score_low, query_block, preferred_element_type=jnp.float32)
            * scale
        )
        return ((key_grad, value_grad), query_grad)

    zeros = jnp.zeros((length, heads, HD), jnp.float32)
    shaped = (
        queries.reshape(length // blocked, blocked, heads, HD),
        logsum,
        out_grad.reshape(length // blocked, blocked, heads, HD),
    )
    (key_grad, value_grad), query_grad = lax.scan(one_block, (zeros, zeros), shaped)
    return (query_grad.reshape(length, heads, HD), key_grad, value_grad)


def adamw(weight, first, second, grad, rate):
    first = BETA_ONE * first + (1.0 - BETA_ONE) * grad
    second = BETA_TWO * second + (1.0 - BETA_TWO) * grad * grad
    first_hat = first / (1.0 - BETA_ONE**STEP)
    second_hat = second / (1.0 - BETA_TWO**STEP)
    weight = weight - rate * (first_hat / (jnp.sqrt(second_hat) + ADAM_EPS) + DECAY * weight)
    return (weight, first, second)


def chip_bits(chips):
    bits, step = [], 1
    while step < chips:
        bits.append(step)
        step *= 2
    return bits


def flip(chip, mask):
    for bit in chip_bits(mask + 1):
        if mask & bit:
            chip = chip + (1 - 2 * (chip // bit % 2)) * bit
    return chip


def column_halves(width):
    first = -(-width // (2 * LANES)) * LANES
    return ((0, first), (first, width - first))


def work_items(widths, order):
    return [(which,) + half + (side,) for which in order for side, half in enumerate(column_halves(widths[which]))]


class Bag:
    def __init__(self, pairs):
        vars(self).update(pairs)


class Place:
    def __init__(self, wide, narrow):
        self.wide, self.narrow = wide, narrow
        self.chips = wide // 2
        self.bits = chip_bits(self.chips)
        self.w = lax.axis_index(WIDE)
        self.n = lax.axis_index(NARROW)
        self.chip = self.w // 2
        self.core = self.w % 2
        self.twin = (2 * self.chip + 1 - self.core, self.n)

    def across(self, mask):
        return (2 * flip(self.chip, mask) + self.core, self.n)

    def along(self, step):
        return (self.w, lax.rem(self.n + step, self.narrow))

    def neighbours(self):
        return (
            [self.twin]
            + [self.across(bit) for bit in self.bits]
            + [self.along(step) for step in range(1, self.narrow)]
        )


class Planner:
    def __init__(self):
        self.now, self.count = 0.0, 0
        self.free, self.events, self.done, self.spare = {}, [], set(), []
        self.refill = lambda: None

    def transfer(self, link, cost, key, event):
        self.free[link] = max(self.now, self.free.get(link, 0.0)) + cost
        self.count += 1
        heapq.heappush(self.events, (self.free[link] + 2.0, self.count, key, event))

    def step(self):
        when, _, key, event = heapq.heappop(self.events)
        self.now = max(self.now, when) + 0.2
        event()
        self.done.add(key)
        self.refill()

    def fill(self, until):
        for index, (keys, cost, work) in enumerate(self.spare):
            if self.now + cost <= until and self.done.issuperset(keys):
                del self.spare[index]
                work()
                self.now += cost
                return True
        return False

    def need(self, keys):
        while not self.done.issuperset(keys):
            if not self.fill(self.events[0][0]):
                self.step()

    def work(self, cost, work, rush=False):
        while not rush and self.events and self.events[0][0] <= self.now:
            self.step()
        self.refill()
        work()
        self.now += cost

    def later(self, cost, work, keys=()):
        entry = (tuple(keys), cost, work)
        self.spare.append(entry)
        return entry

    def force(self, entry):
        if entry in self.spare:
            self.spare.remove(entry)
            self.work(entry[1], entry[2])

    def finish(self):
        self.refill()
        while self.events or self.spare:
            if not self.fill(self.events[0][0] if self.events else 1e9):
                self.step()


LINK = 90e3
Z_AHEAD = 4.0
RELAYED = (3, 4)
KEY_ROWS = 512
Z_EARLY = 1.0
Z_LATE = 2.0
TWIN_LINK = 600e3


def greet(peers):
    barrier = pltpu.get_barrier_semaphore()
    for peer in peers:
        pl.semaphore_signal(barrier, inc=1, device_id=peer, device_id_type=MESH)
    return lambda: pl.semaphore_wait(barrier, len(peers))


def normalize(values, gain, shift):
    centred = values - jnp.mean(values, -1, keepdims=True)
    spread = jnp.mean(centred * centred, -1, keepdims=True)
    return centred * lax.rsqrt(spread + 1e-05) * gain + shift


def forward_plan(widths):
    items = []
    for which, cuts in ((0, 1), (1, 3), (2, 1), (3, 2), (5, 1), (4, 2)):
        size = widths[which] // cuts
        for cut in range(cuts):
            for side, (start, width) in enumerate(column_halves(size)):
                items.append((which, cut * size + start, width, side))
    return items


def forward_kernel(items, wide, narrow, lead, ins, outs, scratch, *refs):
    at = Bag(zip(ins + scratch, refs[: len(ins)] + refs[len(ins) + len(outs) :]))
    results = refs[len(ins) : len(ins) + len(outs)]
    weights = [at.first_weight, at.w1, at.w2, at.w3, at.w4, at.w5]
    shards = [at.c0, at.c1, at.c2, at.c3, at.c4, at.c5]
    raw = [at.s0, at.s1, at.s2, at.s3, at.s4, at.s5]
    own_sem, send_sem, recv_sem = at.own_sem, at.send_sem, at.recv_sem
    swap_send, swap_recv, out_sem = at.swap_send, at.swap_recv, at.out_sem
    place = Place(wide, narrow)
    chips, me = place.chips, place.n
    tokens = at.patches.shape[0]
    head_width = D // narrow
    total = len(items)
    started, guarded = [], []

    def start(copy):
        copy.start()
        started.append(copy)

    all_here = greet(place.neighbours())
    features = at.s0.shape[1]
    tail = shards[0].shape[1] - LANES
    kinds = at.norm_raw.shape[0]
    kind = lax.broadcasted_iota(jnp.int32, (kinds, LANES), 0)
    spot = lax.broadcasted_iota(jnp.int32, (kinds, LANES), 1)
    put = (spot == kind + lead).astype(F32).astype(BF16)
    shards[0][:, tail:] = outer_sum(at.norm_raw[...].astype(BF16), put).astype(BF16)
    shards[0][:, 0:features] = at.s0[...].astype(BF16)
    shards[1][...] = raw[1][...].astype(BF16)
    at.padded[...] = jnp.zeros_like(at.padded)
    at.padded[:, 0:features] = at.patches[...]
    all_here()
    rows_of = [shard.shape[0] for shard in shards]

    def slab(which, node):
        rows = rows_of[which]
        return pl.ds(pl.multiple_of(node * rows, rows), rows)

    def whole_of(which, columns):
        part = weights[which][:, :, :, columns]
        return part.reshape(-1, part.shape[-1])

    own = [
        pltpu.make_async_copy(
            shards[which], weights[which].at[place.chip, place.core, slab(which, me), :], own_sem.at[which]
        )
        for which in range(6)
    ]
    for copy in own[:2]:
        copy.start()

    def remote(item, src, dst, slot, peer):
        return pltpu.make_async_remote_copy(
            src_ref=src,
            dst_ref=dst,
            send_sem=send_sem.at[item, slot],
            recv_sem=recv_sem.at[item, slot],
            device_id=peer,
            device_id_type=MESH,
        )

    def group(item, mask):
        which, begin, width, _ = items[item]
        return weights[which].at[flip(place.chip, mask), place.core, :, pl.ds(begin, width)]

    def along(item, sign, hop):
        which, begin, width, _ = items[item]
        columns = pl.ds(begin, width)
        there = weights[which].at[place.chip, place.core, slab(which, me - sign * (hop - 1)), columns]
        return remote(
            item,
            shards[which].at[:, columns] if hop == 1 else there,
            there,
            chips + 1 + hop - 1 + (narrow - 1 if sign < 0 else 0),
            (place.w, me + sign),
        )

    def has_next(sign):
        return me < narrow - 1 if sign > 0 else me >= 1

    def has_come(sign, hop):
        return me >= hop if sign > 0 else me < narrow - hop

    def start_if(condition, copy):
        @pl.when(condition)
        def _():
            copy.start()

        guarded.append((condition, copy))

    def bits_of(item):
        return place.bits if items[item][3] == 0 else place.bits[::-1]

    def across(item, mask, bit):
        return remote(item, group(item, mask), group(item, mask), mask ^ bit, place.across(bit))

    def to_twin(item):
        which, begin, width, _ = items[item]
        there = weights[which].at[:, place.core, :, pl.ds(begin, width)]
        return remote(item, there, there, chips, place.twin)

    plan = Planner()
    waited = set()

    def block_bytes(item):
        which, _, width, _ = items[item]
        return 2 * narrow * rows_of[which] * width

    def twin_event(item):
        to_twin(item).wait_recv()

    here = {}

    def onward(item, mask, number):
        bits = bits_of(item)
        size = block_bytes(item)
        for later in range(number, len(bits)):
            start(across(item, mask, bits[later]))
            coming = mask ^ bits[later]
            plan.transfer(
                bits[later], 2 * size / LINK, (item, coming), functools.partial(arrive, item, coming, later)
            )
        here[item] = here.get(item, 0) + 1
        if here[item] == chips:
            start(to_twin(item))
            plan.transfer(-1, chips * size / TWIN_LINK, (item, chips), functools.partial(twin_event, item))

    def arrive(item, mask, number):
        across(item, mask ^ bits_of(item)[number], bits_of(item)[number]).wait_recv()
        onward(item, mask, number + 1)

    def begin_item(item):
        for sign in (1, -1):
            start_if(has_next(sign), along(item, sign, 1))
        line_transfer(item, 1)

    def line_transfer(item, hop):
        cost = 2 * block_bytes(item) / narrow / LINK
        key = (item, 0) if hop == narrow - 1 else (item, -hop)
        plan.transfer(0, cost, key, functools.partial(line_event, item, hop))

    def line_event(item, hop):
        if items[item][0] not in waited:
            waited.add(items[item][0])
            own[items[item][0]].wait()
        for sign in (1, -1):

            @pl.when(has_come(sign, hop))
            def _():
                along(item, sign, hop).wait_recv()

            if hop < narrow - 1:
                start_if(jnp.logical_and(has_come(sign, hop), has_next(sign)), along(item, sign, hop + 1))
        if hop < narrow - 1:
            line_transfer(item, hop + 1)
        else:
            onward(item, 0, 0)

    begun, ahead = [], [Z_EARLY]

    def refill():
        while len(begun) < total and plan.free.get(0, 0.0) < plan.now + ahead[-1]:
            begin_item(len(begun))
            begun.append(True)

    plan.refill = refill
    refill()
    assert all(items[item][0] < 2 for item in range(len(begun)))
    for which in range(2, 6):
        shards[which][...] = raw[which][...].astype(BF16)
        own[which].start()

    def need(which, columns=None):
        plan.need(
            [
                (index, key)
                for index, (owner, begin, width, _) in enumerate(items)
                if owner == which and (columns is None or (begin < columns[1] and begin + width > columns[0]))
                for key in range(chips + 1)
            ]
        )

    flushed = []

    def flush(ref):
        index = [vars(at)[name] is ref for name in outs].index(True)
        copy = pltpu.make_async_copy(ref, results[index], out_sem.at[index])
        copy.start()
        flushed.append(copy)

    def swap(src, dst, kind, step):
        return pltpu.make_async_remote_copy(
            src_ref=src,
            dst_ref=dst,
            send_sem=swap_send.at[kind, step],
            recv_sem=swap_recv.at[kind, step],
            device_id=place.along(step),
            device_id_type=MESH,
        )

    gains = at.gains
    embedded, mid, last = at.embedded, at.mid, at.last
    normed, hidden, wave = at.normed, at.hidden, at.wave
    away, qkv, heads_out, returned = at.away, at.qkv, at.heads_out, at.returned

    def turn(dest, source):
        dest[...] = source[...].T
        flush(dest)

    plan.later(2.0, lambda: spread_weights(at.render_w, at.spread))
    plan.later(3.0, lambda: count_pairs(at.pairs, at.counts))
    need(0)
    width = weights[0].shape[-1]
    kind = lax.broadcasted_iota(jnp.int32, (8, LANES), 0)
    spot = lax.broadcasted_iota(jnp.int32, (8, LANES), 1)
    pick = (spot == kind + lead).astype(F32).astype(BF16)
    gains[...] = back_mul(pick, whole_of(0, pl.ds(width - LANES, LANES)))
    flush(gains)
    flush(at.padded)

    def embed(block):
        cols = pl.ds(block, 256)
        rows = whole_of(0, pl.ds(0, width))[block : block + 256]
        embedded[:, cols] = back_mul(at.padded[...], rows)

    for block in range(0, D, 256):
        plan.work(0.5, functools.partial(embed, block))
    flush(embedded)

    def norm_rows(source, row, dest):
        step_rows = 32

        def one(step, carry):
            rows = pl.ds(pl.multiple_of(step * step_rows, step_rows), step_rows)
            dest[rows, :] = normalize(
                source[rows, :], gains[row : row + 1, :], gains[row + 3 : row + 4, :]
            ).astype(BF16)
            return carry

        lax.fori_loop(0, tokens // step_rows, one, 0)

    plan.work(2.0, lambda: norm_rows(embedded, 0, normed))
    turn_first = plan.later(2.0, lambda: turn(at.t1, normed))
    piece = 2 * (narrow - 1) * 2 * tokens * head_width / LINK

    def project(part, step):
        owner = lax.rem(me + step, narrow)
        offset = pl.multiple_of(part * D + owner * head_width, LANES)
        value = matmul(normed[...], whole_of(1, pl.ds(offset, head_width))).astype(BF16)
        if step:
            away[step - 1, part] = value
            start(swap(away.at[step - 1, part], qkv.at[me, part], part, step))
        else:
            qkv[me, part] = value

    def swap_event(part):
        for step in range(1, narrow):
            swap(away.at[step - 1, part], qkv.at[me, part], part, step).wait_recv()

    for part in range(3):
        need(1, (part * D, part * D + D))
        for step in list(range(1, narrow)) + [0]:
            plan.work(0.7, functools.partial(project, part, step))
        plan.transfer(0, piece, (-1, part), functools.partial(swap_event, part))
    flush(at.w1)
    lane = lax.broadcasted_iota(jnp.int32, (1, LANES), 1)
    scale = HD ** (-0.5)
    length = narrow * tokens
    sides = LANES // HD

    def weigh(step):
        who = lax.rem(me + step, narrow)
        log_sums = jnp.zeros((tokens, LANES), F32)
        sums = jnp.ones((tokens, LANES), F32)
        for pair in range(head_width // LANES):
            lanes = pl.ds(pair * LANES, LANES)
            query = qkv[who, 0, :, lanes].astype(F32)
            key = qkv[:, 1, :, lanes].reshape(length, LANES)
            for side in range(sides):
                head = pair * sides + side
                own_query = (query * jnp.where(lane // HD == side, scale, 0.0)).astype(BF16)
                scores = back_mul(own_query, key)
                highest = jnp.max(scores, -1, keepdims=True)
                exponentials = jnp.exp(scores - highest)
                summed = jnp.sum(exponentials, -1, keepdims=True)
                at.weighed[step, head] = exponentials.astype(BF16)
                log_sums = jnp.where(lane == head, highest + jnp.log(summed), log_sums)
                sums = jnp.where(lane == head, summed, sums)
        at.log_sums[who] = log_sums
        at.weigh_sums[step] = sums

    def attend(step):
        who = lax.rem(me + step, narrow)
        for pair in range(head_width // LANES):
            lanes = pl.ds(pair * LANES, LANES)
            value = qkv[:, 2, :, lanes].reshape(length, LANES)
            out = jnp.zeros((tokens, LANES), F32)
            for side in range(sides):
                head = pair * sides + side
                part = matmul(at.weighed[step, head], value) / at.weigh_sums[step, :, head : head + 1]
                out = jnp.where(lane // HD == side, part, out)
            heads_out[who, :, lanes] = out.astype(BF16)
        if step:
            start(swap(heads_out.at[who], returned.at[me], 3, step))
        else:
            returned[me] = heads_out[who]

    steps = list(range(1, narrow)) + [0]
    ahead.append(Z_LATE)
    plan.need([(-1, 0), (-1, 1)])
    for step in steps:
        plan.work(2.7, functools.partial(weigh, step))
    plan.need([(-1, 2)])
    flush(qkv)

    def return_event(step):
        return lambda: swap(heads_out.at[me], returned.at[me], 3, step).wait_recv()

    for step in steps:
        plan.work(0.9, functools.partial(attend, step))
        if step:
            plan.transfer(0, piece / (narrow - 1), (-2, step), return_event(step))
    flush(heads_out)
    flush(at.log_sums)
    need(2)
    plan.need([(-2, step) for step in range(1, narrow)])

    def merge(block):
        cols = pl.ds(block, 256)
        value = embedded[:, cols]
        weight = whole_of(2, cols)
        for source in range(narrow):
            value = value + matmul(returned[source], weight[source * head_width : (source + 1) * head_width])
        mid[:, cols] = value

    for block in range(0, D, 256):
        plan.work(0.7, functools.partial(merge, block))
    flush(at.w2)
    flush(mid)
    plan.force(turn_first)
    plan.work(2.0, lambda: norm_rows(mid, 1, normed))

    def turn_returned():
        for source in range(narrow):
            at.t2[pl.ds(source * head_width, head_width), :] = returned[source].T
        flush(at.t2)

    plan.later(2.0, turn_returned)
    turn_second = plan.later(2.0, lambda: turn(at.t3, normed))

    ff = weights[3].shape[-1]
    tile = wave.shape[1]
    slopes = at.slopes

    def expand(block):
        wave[...] = matmul(normed[...], whole_of(3, pl.ds(block, tile)))

        def bend(step, carry):
            rows = pl.ds(pl.multiple_of(step * 32, 32), 32)
            x = wave[rows, :]
            half = 0.5 * (1.0 + lax.erf(x * (0.5**0.5)))
            hidden[rows, pl.ds(block, tile)] = (x * half).astype(BF16)
            bell = jnp.exp(-0.5 * x * x) * 0.3989422804014327
            slopes[rows, pl.ds(block, tile)] = (half + x * bell).astype(BF16)
            return carry

        lax.fori_loop(0, tokens // 32, bend, 0)

    for block in range(0, ff, tile):
        need(3, (block, block + tile))
        plan.work(2.5, functools.partial(expand, block))
    flush(at.w3)
    flush(slopes)
    flush(hidden)

    def shrink(block):
        cols = pl.ds(block, 256)
        last[:, cols] = mid[:, cols] + matmul(hidden[...], whole_of(4, cols))

    for block in range(0, D, 256):
        need(4, (block, block + 256))
        plan.work(1.0, functools.partial(shrink, block))
    flush(at.w4)
    flush(last)
    plan.force(turn_second)
    plan.work(2.0, lambda: norm_rows(last, 2, normed))
    need(5)

    def unpatch(block):
        cols = pl.ds(block, 256)
        at.gaussians[:, cols] = matmul(normed[...], whole_of(5, cols))

    for block in range(0, weights[5].shape[-1], 256):
        plan.work(0.7, functools.partial(unpatch, block))
    flush(at.w5)
    for entry in list(plan.spare):
        plan.force(entry)

    def draw():
        render_block(
            at.gaussians, at.spread, at.wanted, at.valid, at.counts, at.view, at.total, at.gauss, at.term, at.feat, at.dfeat
        )

    plan.work(4.0, draw)
    flush(at.gauss)
    flush(at.term)
    plan.later(2.0, lambda: turn(at.t5, normed))
    plan.finish()
    for copy in started:
        copy.wait_send()
    for condition, copy in guarded:

        @pl.when(condition)
        def _():
            copy.wait_send()

    for copy in flushed:
        copy.wait()


def forward_all(shards, norms, patches, scene, wide, narrow):
    tokens = patches.shape[0]
    features, kinds = patches.shape[1], norms.shape[0]
    lead = features % LANES
    widths = [-(-(features + kinds) // LANES) * LANES] + [shard.shape[1] for shard in shards[1:]]
    heights = [shard.shape[0] * wide * narrow for shard in shards]
    ff = widths[3]
    chips = wide // 2
    quads, slots_t = tokens // NVIEW, scene[0].shape[0]
    head_width = D // narrow
    items = forward_plan(widths)
    slots = chips + 1 + 2 * (narrow - 1)
    full = [((chips, 2, height // wide, width), BF16) for height, width in zip(heights, widths)]
    shapes = dict(
        w1=full[1],
        w2=full[2],
        w3=full[3],
        w4=full[4],
        w5=full[5],
        gains=((8, D), F32),
        embedded=((tokens, D), F32),
        mid=((tokens, D), F32),
        last=((tokens, D), F32),
        slopes=((tokens, ff), BF16),
        t1=((D, tokens), BF16),
        t2=((D, tokens), BF16),
        t3=((D, tokens), BF16),
        hidden=((tokens, ff), BF16),
        t5=((D, tokens), BF16),
        qkv=((narrow, 3, tokens, head_width), BF16),
        heads_out=((narrow, tokens, head_width), BF16),
        log_sums=((narrow, tokens, LANES), F32),
        padded=((tokens, widths[0]), BF16),
        gauss=((tokens, widths[5]), BF16),
        term=((8, LANES), F32),
    )
    ins = tuple(dict(s0=0, s1=0, s2=0, s3=0, s4=0, s5=0, norm_raw=0, patches=0))
    ins += tuple(dict(render_w=0, wanted=0, valid=0, pairs=0, view=0, total=0))
    outs = tuple(shapes)
    extras = dict(
        first_weight=pltpu.VMEM(*full[0]),
        c0=pltpu.VMEM((shards[0].shape[0], widths[0]), BF16),
        c1=pltpu.VMEM(shards[1].shape, BF16),
        c2=pltpu.VMEM(shards[2].shape, BF16),
        c3=pltpu.VMEM(shards[3].shape, BF16),
        c4=pltpu.VMEM(shards[4].shape, BF16),
        c5=pltpu.VMEM(shards[5].shape, BF16),
        gaussians=pltpu.VMEM((tokens, widths[5]), F32),
        spread=pltpu.VMEM((NVIEW * PP, slots_t * PP), F32),
        counts=pltpu.VMEM((2 * quads, slots_t * PP), F32),
        feat=pltpu.VMEM((5 * quads, NVIEW * PP), F32),
        dfeat=pltpu.VMEM((5 * quads, NVIEW * PP), F32),
        normed=pltpu.VMEM((tokens, D), BF16),
        wave=pltpu.VMEM((tokens, 512), F32),
        away=pltpu.VMEM((narrow - 1, 3, tokens, head_width), BF16),
        weighed=pltpu.VMEM((narrow, head_width // HD, tokens, narrow * tokens), BF16),
        weigh_sums=pltpu.VMEM((narrow, tokens, LANES), F32),
        returned=pltpu.VMEM((narrow, tokens, head_width), BF16),
        own_sem=pltpu.SemaphoreType.DMA((6,)),
        send_sem=pltpu.SemaphoreType.DMA((len(items), slots)),
        recv_sem=pltpu.SemaphoreType.DMA((len(items), slots)),
        swap_send=pltpu.SemaphoreType.DMA((4, narrow)),
        swap_recv=pltpu.SemaphoreType.DMA((4, narrow)),
        out_sem=pltpu.SemaphoreType.DMA((len(outs),)),
    )
    scratch = outs + tuple(extras)
    anywhere = pl.BlockSpec(memory_space=pl.ANY)
    results = pl.pallas_call(
        functools.partial(forward_kernel, items, wide, narrow, lead, ins, outs, scratch),
        out_shape=[jax.ShapeDtypeStruct(*shapes[name]) for name in outs],
        in_specs=[pl.BlockSpec(memory_space=pltpu.VMEM)] * (len(ins) - 2)
        + [pl.BlockSpec(memory_space=pltpu.SMEM)] * 2,
        out_specs=[anywhere] * len(outs),
        scratch_shapes=[pltpu.VMEM(*shapes[name]) for name in outs] + list(extras.values()),
        compiler_params=pltpu.CompilerParams(
            collective_id=0, has_side_effects=True, vmem_limit_bytes=63 * MIB
        ),
        name="forward",
    )(*shards, norms, patches, *scene)
    results = [result.reshape(-1, result.shape[-1]) for result in results[:5]] + list(results[5:])
    return Bag(zip(outs, results))


def backward_plan(widths, pairs):
    items = []
    for which, cuts in ((5, 1), (4, 2), (3, 2), (2, 1), (1, pairs), (0, 1)):
        size = widths[which] // cuts
        for cut in range(cuts):
            for side, (start, width) in enumerate(column_halves(size)):
                items.append((which, cut * size + start, width, side))
    return items


def tile_of(width):
    for tile in (512, 384, 256, 128):
        if width % tile == 0:
            return tile
    return width


def backward_kernel(items, wide, narrow, lead, ins, scratch, *refs):
    src = Bag(zip(ins, refs))
    refs = refs[len(ins) :]
    sums, totals, refs = refs[:6], refs[6], list(refs[7:])
    at = Bag(zip(scratch, refs))
    place = Place(wide, narrow)
    chips, me = place.chips, place.n
    total = len(items)
    refs = refs[len(scratch) :]
    held = [refs.pop(0) for _ in items]
    passed = [[refs.pop(0) for _ in place.bits] for _ in items]
    final = [refs.pop(0) for _ in items]
    spare = [refs.pop(0) for _ in range(6)]
    tokens = src.patches.shape[0]
    head_width = D // narrow
    length = narrow * tokens
    reach = narrow * LANES
    send_sem, recv_sem, tile_send, tile_recv = at.send_sem, at.recv_sem, at.tile_send, at.tile_recv
    swap_send, swap_recv, in_sem, ring_sem = at.swap_send, at.swap_recv, at.in_sem, at.ring_sem
    gains, norms, extra = src.gains, at.norms, at.extra
    stash, d_res, d_norm = at.stash, at.d_res, at.d_norm
    mixed, merge_low, expand_low, shrink_low = at.mixed, at.merge_low, at.expand_low, at.shrink_low

    peers = [(lax.rem(place.w + step, wide), place.n) for step in range(1, wide)]
    peers += [place.along(step) for step in range(1, narrow)]
    all_here = greet(peers)

    loaded = [name for name in ins if name in scratch]

    def load(ref):
        index = [vars(at)[name] is ref for name in loaded].index(True)
        return pltpu.make_async_copy(vars(src)[loaded[index]], ref, in_sem.at[index])

    def load_stash(ref):
        return pltpu.make_async_copy(ref, stash, in_sem.at[len(loaded)])

    def ring(ref, slots, rows, columns, index, row):
        slot = lax.rem(index, slots.shape[0])
        return pltpu.make_async_copy(
            ref.at[pl.ds(pl.multiple_of(row, rows), rows), :],
            slots.at[slot, pl.ds(0, rows), pl.ds(0, columns)],
            ring_sem.at[0 if slots is at.tall else 1, slot],
        )

    slope_rows = at.tall.shape[1]
    tall, long = at.tall.shape[0], at.long.shape[0]

    def slope_load(index):
        slot = lax.rem(index, tall)
        return pltpu.make_async_copy(
            src.slopes.at[:, pl.ds(pl.multiple_of(index * slope_rows, slope_rows), slope_rows)],
            at.slope_slots.at[slot],
            ring_sem.at[2, slot],
        )

    u_rows, u_cols = 256, src.w5.shape[1]
    load_stash(src.last).start()
    for index in range(tall):
        ring(src.w5, at.tall, u_rows, u_cols, index, index * u_rows).start()
        slope_load(index).start()
    wide_rows = at.long.shape[1]
    for index in range(long):
        ring(src.w3, at.long, wide_rows, src.w3.shape[1], index, index * wide_rows).start()
    for name in loaded:
        load(vars(at)[name]).start()

    all_here()

    started, guarded = [], []

    def start(copy):
        copy.start()
        started.append(copy)

    lefts = [at.embed_t, at.t1, at.t2, at.t3, at.shrink_t, at.t5]
    rights = [src.patches, mixed, merge_low, expand_low, at.hidden, src.gauss]

    def remote(item, src, dst, slot, peer):
        return pltpu.make_async_remote_copy(
            src_ref=src,
            dst_ref=dst,
            send_sem=send_sem.at[item, slot],
            recv_sem=recv_sem.at[item, slot],
            device_id=peer,
            device_id_type=MESH,
        )

    def bits_of(item):
        return place.bits[::-1] if items[item][3] == 0 else place.bits

    def groups_of(item):
        size = max(1, 512 // (narrow * spare[items[item][0]].shape[2]))
        if items[item][0] == 4:
            size = chips
        masks = list(range(chips))
        if bits_of(item) and bits_of(item)[0] > 1:
            masks = masks[chips // 2 :] + masks[: chips // 2]
        return [sorted(masks[at_mask : at_mask + size]) for at_mask in range(0, chips, size)]

    def product(item, masks, core, into, plus):
        which, begin, width, _ = items[item]
        left, right = lefts[which], rights[which]
        rows = into.shape[-2]
        span = narrow * rows
        tile = tile_of(width)
        if which == 4:
            size = into.shape[-1]
            for mask in masks:
                column = ((flip(place.chip, mask) * 2 + core) * narrow) * size
                rhs = right[:, pl.ds(pl.multiple_of(column, narrow * size), narrow * size)]
                value = jnp.dot(left[begin : begin + width, :], rhs, preferred_element_type=F32)
                for node in range(narrow):
                    piece = value[:, node * size : (node + 1) * size]
                    if plus:
                        piece = piece + into[mask, node].astype(F32)
                    into[mask, node] = piece.astype(BF16)
            return
        firsts = [((flip(place.chip, mask) * 2 + core) * narrow) * rows for mask in masks]
        with_extra = which == 0 and begin + width == right.shape[1]
        assert not with_extra or tile == width
        if which == 1:
            tile = LANES * 2

        def one(step, carry):
            offset = pl.multiple_of(begin + step * tile, LANES)
            local = pl.multiple_of(step * tile, LANES)
            if which != 1:
                rhs = right[:, pl.ds(offset, tile)]
            else:
                part, inside = offset // reach, pl.multiple_of(offset % reach, LANES)
                rhs = right[part // 3, part % 3, :, pl.ds(inside, tile)]
            spots = [pl.ds(pl.multiple_of(first, span), span) for first in firsts]
            lhs = jnp.concatenate([left[spot, :] for spot in spots], 0)
            value = jnp.dot(lhs, rhs, preferred_element_type=F32)
            for index, mask in enumerate(masks):
                piece = value[index * span : (index + 1) * span]
                if with_extra:
                    blank = jnp.zeros((span, tile - LANES), F32)
                    piece = piece + jnp.concatenate([blank, extra[spots[index], :]], 1)
                piece = piece.reshape(narrow, rows, tile)
                if plus:
                    piece = piece + into[mask, :, :, pl.ds(local, tile)].astype(F32)
                into[mask, :, :, pl.ds(local, tile)] = piece.astype(BF16)
            return carry

        lax.fori_loop(0, width // tile, one, 0)

    last_sent = {}
    plan = Planner()

    def to_twin(item, masks):
        which, _, width, _ = items[item]
        some = pl.ds(masks[0], len(masks))
        own = spare[which].at[some] if which == 4 else spare[which].at[some, :, :, pl.ds(0, width)]
        return remote(item, own, held[item].at[some], masks[0], place.twin)

    def across(item, mask, bit, number, slot):
        return remote(
            item, held[item].at[mask], passed[item][number].at[slot], chips + mask, place.across(bit)
        )

    def relayed(item):
        return items[item][0] in RELAYED

    def hopping(item, sign, hop):
        count = narrow - hop
        first = hop if sign > 0 else 0
        node = hop if sign > 0 else narrow - 1 - hop
        return remote(
            item,
            held[item].at[0, pl.ds(first, count)],
            final[item].at[pl.ds(first + (1 if sign > 0 else 0), count)],
            2 * chips + (0 if sign > 0 else 1),
            (place.w, node),
        )

    def send_hop(item, sign, hop):
        sender = me == (hop - 1 if sign > 0 else narrow - hop)

        @pl.when(sender)
        def _():
            hopping(item, sign, hop).start()

        guarded.append((sender, hopping(item, sign, hop)))

    def hop_event(item, hop):
        count = narrow - hop - 1
        for sign in (1, -1):
            first = hop + 1 if sign > 0 else 0
            shift = 1 if sign > 0 else 0

            @pl.when(me == (hop if sign > 0 else narrow - 1 - hop))
            def _():
                hopping(item, sign, hop).wait_recv()
                if count:
                    mine, theirs = pl.ds(first, count), pl.ds(first + shift, count)
                    value = held[item][0, mine].astype(F32) + final[item][theirs].astype(F32)
                    held[item][0, mine] = value.astype(BF16)

            if count:
                send_hop(item, sign, hop + 1)
        if count:
            hop_transfer(item, hop + 1)
        else:
            finish(item)

    def hop_transfer(item, hop):
        cost = (narrow - hop) * 2 * block_bytes(item) / narrow / LINK
        event = functools.partial(hop_event, item, hop)
        plan.transfer(0 if hop == 1 else 100 + hop, cost, (item, -hop, 0), event)

    def along(item, step):
        target = place.along(step)
        return remote(
            item,
            held[item].at[0, target[1]],
            final[item].at[narrow - step - 1],
            2 * chips + narrow - step - 1,
            target,
        )

    def leaves(item, mask):
        bits = bits_of(item)
        return min([number for number, bit in enumerate(bits) if mask & bit], default=len(bits))

    def slot_of(item, mask, number):
        bits = bits_of(item)
        kept = [m for m in range(chips) if not any(m & bit for bit in bits[: number + 1])]
        return kept.index(mask)

    def add_into(dest, dest_at, src, src_at):
        dest[dest_at] = (dest[dest_at].astype(F32) + src[src_at].astype(F32)).astype(BF16)

    def block_bytes(item):
        _, nodes, rows, width = held[item].shape
        return 2 * nodes * rows * width

    def push(which, pair=None):
        for item, (owner, begin, _, _) in enumerate(items):
            if owner != which or (pair is not None and begin // (3 * reach) != pair):
                continue
            for masks in groups_of(item):
                cost = len(masks) * block_bytes(item) / 1e6
                plan.work(cost, functools.partial(push_some, item, masks))

    def push_some(item, masks):
        which = items[item][0]
        for key in [key for key in last_sent if key[0] == which and set(key[1]) & set(masks)]:
            last_sent.pop(key).wait_send()
        product(item, masks, 1 - place.core, spare[which], False)
        copy = to_twin(item, masks)
        copy.start()
        last_sent[which, tuple(masks)] = copy
        cost = len(masks) * block_bytes(item) / TWIN_LINK
        plan.transfer(-1, cost, (item, 0, masks[0]), functools.partial(own_event, item, masks))

    def own_event(item, masks):
        to_twin(item, masks).wait_recv()
        product(item, masks, place.core, held[item], True)
        plan.now += len(masks) * block_bytes(item) / 1e6
        plan.done.update((item, 0, mask) for mask in masks)
        for mask in masks:
            onward(item, mask, 0)

    def onward(item, mask, number):
        bits = bits_of(item)
        if number == len(bits):
            lined.append(item)
            refill()
        elif leaves(item, mask) == number:
            kept = mask ^ bits[number]
            start(across(item, mask, bits[number], number, slot_of(item, kept, number)))
            plan.transfer(
                bits[number],
                2 * block_bytes(item) / LINK,
                (item, 1 + number, kept),
                functools.partial(sum_event, item, kept, number),
            )

    lined = []

    def refill():
        while lined and plan.free.get(0, 0.0) < plan.now + Z_AHEAD:
            item = lined.pop(0)
            if relayed(item):
                for sign in (1, -1):
                    send_hop(item, sign, 1)
                hop_transfer(item, 1)
                continue
            for step in range(1, narrow):
                start(along(item, step))
            cost = 2 * (narrow // 2) ** 2 * block_bytes(item) / narrow / LINK
            plan.transfer(0, cost, (item, -1, 0), functools.partial(finish, item))

    plan.refill = refill

    def sum_event(item, mask, number):
        plan.need([(item, before, mask) for before in range(number + 1)])
        bit = bits_of(item)[number]
        slot = slot_of(item, mask, number)
        across(item, mask ^ bit, bit, number, slot).wait_recv()
        add_into(held[item], mask, passed[item][number], slot)
        plan.now += block_bytes(item) / 8e5
        onward(item, mask, number + 1)

    at.squares[...] = jnp.zeros_like(at.squares)

    def finish(item):
        which, begin, width, _ = items[item]
        value = held[item][0, me].astype(F32)
        if relayed(item):
            value = value + jnp.where(me >= 1, final[item][me + 1].astype(F32), 0.0)
            value = value + jnp.where(me < narrow - 1, final[item][me].astype(F32), 0.0)
        else:
            for step in range(1, narrow):
                along(item, step).wait_recv()
            for slot in range(narrow - 1):
                value = value + final[item][slot].astype(F32)
        columns = pl.ds(0, value.shape[1])
        at.squares[:, columns] += jnp.sum(value * value, 0, keepdims=True)
        if which == 1:
            for shift in range(0, width, LANES):
                part, spot = (begin + shift) // reach, (begin + shift) % reach
                column = part % 3 * D + spot // LANES * head_width + part // 3 * LANES
                sums[which][:, pl.ds(column, LANES)] = value[:, shift : shift + LANES]
        elif which == 4:
            sums[which][pl.ds(begin, width), :] = value
        else:
            sums[which][:, pl.ds(begin, width)] = value

    norms[...] = jnp.zeros_like(norms)

    def norm_back(row, low, add):
        step_rows = 32

        def one(step, carry):
            rows = pl.ds(pl.multiple_of(step * step_rows, step_rows), step_rows)
            values = stash[rows, :]
            upper = d_norm[rows, :]
            centred = values - jnp.mean(values, -1, keepdims=True)
            rate = lax.rsqrt(jnp.mean(centred * centred, -1, keepdims=True) + 1e-05)
            unit = centred * rate
            norms[row : row + 1, :] += jnp.sum(upper * unit, 0, keepdims=True)
            norms[row + 3 : row + 4, :] += jnp.sum(upper, 0, keepdims=True)
            scaled = upper * gains[row : row + 1, :]
            inner = scaled - jnp.mean(scaled, -1, keepdims=True)
            inner = rate * (inner - unit * jnp.mean(scaled * unit, -1, keepdims=True))
            if add:
                inner = inner + d_res[rows, :]
            d_res[rows, :] = inner
            low[rows, :] = inner.astype(BF16)
            return carry

        lax.fori_loop(0, tokens // step_rows, one, 0)

    def loop_work(cost, count, pieces, body):
        for piece in range(pieces):
            low, high = count * piece // pieces, count * (piece + 1) // pieces
            plan.work(cost / pieces, functools.partial(lax.fori_loop, low, high, body, 0))

    load(at.t5).wait()
    push(5)
    load_stash(src.last).wait()
    count = D // u_rows
    tall_rows = slope_rows

    def through_unpatch(index, carry):
        ring(src.w5, at.tall, u_rows, u_cols, index, index * u_rows).wait()
        slot = at.tall.at[lax.rem(index, tall)]
        offset = pl.multiple_of(index * u_rows, u_rows)
        d_norm[:, pl.ds(offset, u_rows)] = back_mul(src.gauss[...], slot[0:u_rows, 0:u_cols])

        @pl.when(index + tall < count)
        def _():
            ring(src.w5, at.tall, u_rows, u_cols, index + tall, (index + tall) * u_rows).start()

        return carry

    loop_work(2.5, count, 1, through_unpatch)
    for index in range(tall):
        ring(src.w4, at.tall, tall_rows, D, index, index * tall_rows).start()
    plan.work(2.5, lambda: norm_back(2, shrink_low, False))
    load_stash(src.mid).start()
    load(at.hidden).wait()

    def turn_shrink():
        at.shrink_t[...] = shrink_low[...].T

    plan.work(2.0, turn_shrink)
    push(4)
    ff = src.w3.shape[1]
    slabs = ff // tall_rows

    def through_shrink(index, carry):
        ring(src.w4, at.tall, tall_rows, D, index, index * tall_rows).wait()
        slope_load(index).wait()
        slot = lax.rem(index, tall)
        value = back_mul(shrink_low[...], at.tall[slot])
        value = value * at.slope_slots[slot].astype(F32)
        expand_low[:, pl.ds(pl.multiple_of(index * tall_rows, tall_rows), tall_rows)] = value.astype(BF16)

        @pl.when(index + tall < slabs)
        def _():
            ring(src.w4, at.tall, tall_rows, D, index + tall, (index + tall) * tall_rows).start()
            slope_load(index + tall).start()

        return carry

    loop_work(6.0, slabs, 2, through_shrink)
    owners = [lax.rem(me + step, narrow) for step in list(range(1, narrow)) + [0]]
    for index in range(min(tall, narrow)):
        ring(src.w2, at.tall, head_width, D, index, owners[index] * head_width).start()
    load(at.t3).wait()

    def through_expand(index, carry):
        ring(src.w3, at.long, wide_rows, ff, index, index * wide_rows).wait()
        offset = pl.multiple_of(index * wide_rows, wide_rows)
        d_norm[:, pl.ds(offset, wide_rows)] = back_mul(expand_low[...], at.long[lax.rem(index, long)])

        @pl.when(index + long < D // wide_rows)
        def _():
            ring(src.w3, at.long, wide_rows, ff, index + long, (index + long) * wide_rows).start()

        return carry

    loop_work(5.0, D // wide_rows, 2, through_expand)
    for index in range(long):
        ring(src.w1, at.long, wide_rows, 3 * D, index, index * wide_rows).start()
    load_stash(src.mid).wait()
    plan.work(2.0, lambda: norm_back(1, merge_low, True))
    load_stash(src.embedded).start()

    def swap(src, dst, kind, step):
        return pltpu.make_async_remote_copy(
            src_ref=src,
            dst_ref=dst,
            send_sem=swap_send.at[kind, step],
            recv_sem=swap_recv.at[kind, step],
            device_id=place.along(step),
            device_id_type=MESH,
        )

    d_heads, away = at.d_heads, at.away
    piece = 2 * (narrow - 1) * 2 * tokens * head_width / LINK

    def head_event():
        for step in range(1, narrow):
            swap(away.at[step - 1], d_heads.at[me], 0, step).wait_recv()

    def through_merge(index, owner):
        ring(src.w2, at.tall, head_width, D, index, owner * head_width).wait()
        value = back_mul(merge_low[...], at.tall[index % tall, 0:head_width, :]).astype(BF16)
        if index < narrow - 1:
            away[index] = value
            start(swap(away.at[index], d_heads.at[me], 0, index + 1))
        else:
            d_heads[me] = value
        if index + tall < narrow:
            ring(src.w2, at.tall, head_width, D, index + tall, owners[index + tall] * head_width).start()

    for index, owner in enumerate(owners):
        plan.work(0.7, functools.partial(through_merge, index, owner))
    plan.transfer(0, piece, (-1, 0, 0), head_event)
    load(at.t2).wait()
    push(3)
    push(2)
    load(at.qkv).wait()
    load(at.heads_out).wait()
    load(at.log_sums).wait()
    plan.need([(-1, 0, 0)])

    qkv, heads_out, log_sums, parts = at.qkv, at.heads_out, at.log_sums, at.parts
    key_t, key_acc, value_acc, query_acc = at.key_t, at.key_acc, at.value_acc, at.query_acc
    lane = lax.broadcasted_iota(jnp.int32, (1, LANES), 1)
    sides = LANES // HD
    scale = HD ** (-0.5)
    choose = lax.broadcasted_iota(jnp.int32, (8, LANES), 1) // HD
    choose = (choose == lax.broadcasted_iota(jnp.int32, (8, LANES), 0)).astype(F32)

    def part_swap(pair, step):
        lanes = pl.ds(pair * LANES, LANES)
        who = lax.rem(me + step, narrow)
        return swap(
            parts.at[who, :, :, lanes],
            mixed.at[pair, :, :, pl.ds(pl.multiple_of(me * LANES, LANES), LANES)],
            1 + pair,
            step,
        )

    pushed_pairs = []
    load(at.t1).wait()

    def part_event(pair):
        for step in range(1, narrow):
            part_swap(pair, step).wait_recv()

    for pair in range(head_width // LANES):
        lanes = pl.ds(pair * LANES, LANES)
        key_t[...] = qkv[:, 1, :, lanes].reshape(length, LANES).T
        key_acc[...] = jnp.zeros_like(key_acc)
        value_acc[...] = jnp.zeros_like(value_acc)
        def one_block(step, lanes=lanes, pair=pair):
            who = lax.rem(me + step, narrow)
            query = qkv[who, 0, :, lanes].astype(F32)
            upper = d_heads[who, :, lanes].astype(F32)
            kept = heads_out[who, :, lanes].astype(F32)
            delta = lax.dot_general(
                choose,
                upper * kept,
                (((1,), (1,)), ((), ())),
                precision=HIGHEST,
                preferred_element_type=F32,
            )
            log_rows = log_sums[who].T[pair * sides : (pair + 1) * sides, :]
            masks = [jnp.where(lane // HD == side, 1.0, 0.0) for side in range(sides)]
            own_query = jnp.concatenate([query * (scale * mask) for mask in masks], 0).astype(BF16)
            own_upper = jnp.concatenate([upper * mask for mask in masks], 0).astype(BF16)
            log_row = jnp.concatenate([log_rows[side : side + 1, :] for side in range(sides)], 1)
            delta_row = jnp.concatenate([delta[side : side + 1, :] for side in range(sides)], 1)
            query_acc[...] = jnp.zeros_like(query_acc)

            at_once = max(1, KEY_ROWS // tokens)
            for source in range(0, narrow, at_once):
                rows = pl.ds(source * tokens, at_once * tokens)
                some = pl.ds(source, at_once)
                key = qkv[some, 1, :, lanes].reshape(at_once * tokens, LANES)
                value = qkv[some, 2, :, lanes].reshape(at_once * tokens, LANES)
                probs = jnp.exp(back_mul(key, own_query) - log_row)
                d_probs = back_mul(value, own_upper)
                d_scores = (probs * (d_probs - delta_row)).astype(BF16)
                value_acc[rows, :] += matmul(probs.astype(BF16), own_upper)
                key_acc[rows, :] += matmul(d_scores, own_query)
                turned = matmul(key_t[:, rows], d_scores)
                for side in range(sides):
                    spot = slice(side * HD, (side + 1) * HD)
                    query_acc[spot, :] += turned[spot, side * tokens : (side + 1) * tokens]

            parts[who, 0, :, lanes] = (query_acc[...].T * scale).astype(BF16)
        for step in range(narrow):
            plan.work(4.0, functools.partial(one_block, step), step > 0)
            for earlier in range(pair):
                if earlier not in pushed_pairs and (-2, 0, earlier) in plan.done:
                    pushed_pairs.append(earlier)
                    push(1, earlier)
        for source in range(narrow):
            rows = pl.ds(source * tokens, tokens)
            parts[source, 1, :, lanes] = key_acc[rows, :].astype(BF16)
            parts[source, 2, :, lanes] = value_acc[rows, :].astype(BF16)
        for step in range(1, narrow):
            start(part_swap(pair, step))
        plan.now += 1.0
        plan.transfer(0, 1.5 * piece, (-2, 0, pair), functools.partial(part_event, pair))
        mixed[pair, :, :, pl.ds(pl.multiple_of(me * LANES, LANES), LANES)] = parts[me, :, :, lanes]
    for pair in range(head_width // LANES):
        if pair not in pushed_pairs:
            plan.need([(-2, 0, pair)])
            push(1, pair)

    def through_mixer(index, carry):
        ring(src.w1, at.long, wide_rows, 3 * D, index, index * wide_rows).wait()
        slot = lax.rem(index, long)
        value = jnp.zeros((tokens, wide_rows), F32)
        for pair in range(head_width // LANES):
            for part in range(3):
                columns = [part * D + owner * head_width + pair * LANES for owner in range(narrow)]
                weight = [at.long[slot, :, column : column + LANES] for column in columns]
                value = value + back_mul(mixed[pair, part], jnp.concatenate(weight, 1))
        d_norm[:, pl.ds(pl.multiple_of(index * wide_rows, wide_rows), wide_rows)] = value

        @pl.when(index + long < D // wide_rows)
        def _():
            ring(src.w1, at.long, wide_rows, 3 * D, index + long, (index + long) * wide_rows).start()

        return carry

    plan.work(4.0, lambda: lax.fori_loop(0, D // wide_rows, through_mixer, 0))
    load_stash(src.embedded).wait()
    plan.work(3.0, lambda: norm_back(0, at.embed_low, True))
    at.embed_t[...] = at.embed_low[...].T
    turned = jnp.concatenate([norms[...], jnp.zeros((LANES - 8, D), F32)], 0).T
    at.extra[...] = pltpu.roll(turned, lead, 1)
    push(0)
    plan.finish()

    rows = lax.broadcasted_iota(jnp.int32, (8, LANES), 0)
    wide_tiles, narrow_tiles = at.wide_tiles, at.narrow_tiles
    wide_tiles[place.w] = jnp.where(rows == 0, src.term[...], jnp.sum(at.squares[...]))

    def tile_copy(buffer, index, slot, peer):
        return pltpu.make_async_remote_copy(
            src_ref=buffer.at[index],
            dst_ref=buffer.at[index],
            send_sem=tile_send.at[slot],
            recv_sem=tile_recv.at[slot],
            device_id=peer,
            device_id_type=MESH,
        )

    for step in range(1, wide):
        start(tile_copy(wide_tiles, place.w, step - 1, (lax.rem(place.w + step, wide), place.n)))
    for step in range(1, wide):
        tile_copy(wide_tiles, place.w, step - 1, (lax.rem(place.w + step, wide), place.n)).wait_recv()
    whole = wide_tiles[0]
    for index in range(1, wide):
        whole = whole + wide_tiles[index]
    narrow_tiles[place.n] = whole
    for step in range(1, narrow):
        start(tile_copy(narrow_tiles, place.n, wide + step - 1, place.along(step)))
    for step in range(1, narrow):
        tile_copy(narrow_tiles, place.n, wide + step - 1, place.along(step)).wait_recv()
    whole = narrow_tiles[0]
    for index in range(1, narrow):
        whole = whole + narrow_tiles[index]
    totals[...] = whole
    for copy in list(last_sent.values()) + started:
        copy.wait_send()
    for condition, copy in guarded:

        @pl.when(condition)
        def _():
            copy.wait_send()


def backward_all(kept, patches, gauss, term, lead, wide, narrow):
    tokens = patches.shape[0]
    chips = wide // 2
    weights = [kept.w1, kept.w2, kept.w3, kept.w4, kept.w5]
    heights = [D] + [weight.shape[0] for weight in weights]
    widths = [patches.shape[1]] + [weight.shape[1] for weight in weights]
    rows = [height // (wide * narrow) for height in heights]
    head_width = D // narrow
    length = narrow * tokens
    items = backward_plan(widths, head_width // LANES)
    slots = 2 * chips + max(2, narrow - 1)
    streamed = dict(w1=kept.w1, w2=kept.w2, w3=kept.w3, w4=kept.w4, w5=kept.w5)
    streamed.update(last=kept.last, mid=kept.mid, embedded=kept.embedded, slopes=kept.slopes)
    loaded = dict(t5=kept.t5, hidden=kept.hidden, t3=kept.t3, t2=kept.t2, t1=kept.t1)
    loaded.update(qkv=kept.qkv, heads_out=kept.heads_out, log_sums=kept.log_sums)
    whole = dict(gains=kept.gains, patches=patches, gauss=gauss, term=term)
    operands = {**streamed, **loaded, **whole}
    shapes = [jax.ShapeDtypeStruct((rows[which], widths[which]), F32) for which in range(6)]
    shapes[4] = jax.ShapeDtypeStruct((D, rows[4]), F32)
    shapes.append(jax.ShapeDtypeStruct((8, LANES), F32))
    scratch = {name: pltpu.VMEM(value.shape, value.dtype) for name, value in loaded.items()}
    blocks = [(width, rows[which]) if which == 4 else (rows[which], width) for which, _, width, _ in items]
    scratch.update(
        squares=pltpu.VMEM((1, max(block[1] for block in blocks)), F32),
        embed_t=pltpu.VMEM((D, tokens), BF16),
        embed_low=pltpu.VMEM((tokens, D), BF16),
        shrink_t=pltpu.VMEM((D, tokens), BF16),
        stash=pltpu.VMEM((tokens, D), F32),
        d_res=pltpu.VMEM((tokens, D), F32),
        d_norm=pltpu.VMEM((tokens, D), F32),
        norms=pltpu.VMEM((8, D), F32),
        extra=pltpu.VMEM((D, LANES), F32),
        shrink_low=pltpu.VMEM((tokens, D), BF16),
        expand_low=pltpu.VMEM((tokens, widths[3]), BF16),
        merge_low=pltpu.VMEM((tokens, D), BF16),
        mixed=pltpu.VMEM((head_width // LANES, 3, tokens, narrow * LANES), BF16),
        tall=pltpu.VMEM((4, 256, D), BF16),
        long=pltpu.VMEM((2, 256, widths[3]), BF16),
        slope_slots=pltpu.VMEM((4, tokens, 256), BF16),
        d_heads=pltpu.VMEM((narrow, tokens, head_width), BF16),
        away=pltpu.VMEM((narrow - 1, tokens, head_width), BF16),
        parts=pltpu.VMEM((narrow, 3, tokens, head_width), BF16),
        key_t=pltpu.VMEM((LANES, length), BF16),
        key_acc=pltpu.VMEM((length, LANES), F32),
        value_acc=pltpu.VMEM((length, LANES), F32),
        query_acc=pltpu.VMEM((LANES, tokens), F32),
        wide_tiles=pltpu.VMEM((wide, 8, LANES), F32),
        narrow_tiles=pltpu.VMEM((narrow, 8, LANES), F32),
        send_sem=pltpu.SemaphoreType.DMA((len(items), slots)),
        recv_sem=pltpu.SemaphoreType.DMA((len(items), slots)),
        tile_send=pltpu.SemaphoreType.DMA((wide + narrow,)),
        tile_recv=pltpu.SemaphoreType.DMA((wide + narrow,)),
        swap_send=pltpu.SemaphoreType.DMA((1 + head_width // LANES, narrow)),
        swap_recv=pltpu.SemaphoreType.DMA((1 + head_width // LANES, narrow)),
        in_sem=pltpu.SemaphoreType.DMA((9,)),
        ring_sem=pltpu.SemaphoreType.DMA((3, 4)),
    )
    lists = [pltpu.VMEM((chips, narrow) + block, BF16) for block in blocks]
    for block in blocks:
        for bit in chip_bits(chips):
            lists.append(pltpu.VMEM((chips // (2 * bit), narrow) + block, BF16))
    for (which, _, _, _), block in zip(items, blocks):
        lists.append(pltpu.VMEM((narrow + (1 if which in RELAYED else -1),) + block, BF16))
    for which in range(6):
        widest = max(block for item, block in zip(items, blocks) if item[0] == which)
        lists.append(pltpu.VMEM((chips, narrow) + widest, BF16))
    vmem = pl.BlockSpec(memory_space=pltpu.VMEM)
    hbm = pl.BlockSpec(memory_space=pl.ANY)
    return pl.pallas_call(
        functools.partial(backward_kernel, items, wide, narrow, lead, tuple(operands), tuple(scratch)),
        out_shape=shapes,
        in_specs=[vmem if name in whole else hbm for name in operands],
        out_specs=[vmem] * len(shapes),
        scratch_shapes=list(scratch.values()) + lists,
        compiler_params=pltpu.CompilerParams(
            collective_id=1, has_side_effects=True, vmem_limit_bytes=63 * MIB
        ),
        name="backward",
    )(*operands.values())


def spread_weights(source, dest):
    for slot in range(source.shape[0]):
        for view in range(source.shape[1]):
            dest[view * PP : (view + 1) * PP, slot * PP : (slot + 1) * PP] = source[slot, view]


def count_pairs(pair_ref, counts):
    quads, span = counts.shape[0] // 2, counts.shape[1]
    some = 512
    counts[...] = jnp.zeros_like(counts)

    def one(step, carry):
        where = pl.ds(pl.multiple_of(step * some, some), some)
        first, second = pair_ref[0:1, where], pair_ref[1:2, where]
        least = jnp.minimum(first, second)
        down = (jnp.abs(first - second) == P_SIZE).astype(jnp.int32)
        place = quads * PP
        slot, local = least // place, least % place
        high = down * quads + local // PP
        low = slot * PP + local % PP
        high_hot = (lax.broadcasted_iota(jnp.int32, (2 * quads, some), 0) == high).astype(F32).astype(BF16)
        low_hot = (lax.broadcasted_iota(jnp.int32, (span, some), 0) == low).astype(F32).astype(BF16)
        counts[...] += back_mul(high_hot, low_hot)
        return carry

    lax.fori_loop(0, pair_ref.shape[1] // some, one, 0)


def render_kernel(
    gauss_ref, weight_ref, target_ref, mask_ref, pair_ref, view_ref, total_ref, grad_ref, term_ref, feat, dfeat, counts
):
    count_pairs(pair_ref, counts)
    render_block(
        gauss_ref, weight_ref, target_ref, mask_ref, counts, view_ref, total_ref, grad_ref, term_ref, feat, dfeat
    )


def render_block(
    gauss_ref, weight_ref, target_ref, mask_ref, counts, view_ref, total_ref, grad_ref, term_ref, feat, dfeat
):
    quads = gauss_ref.shape[0] // NVIEW
    span = weight_ref.shape[1]
    scale = 1.0 / total_ref[0].astype(F32)

    def channel(index):
        return gauss_ref[:, index * PP : (index + 1) * PP]

    def shared():
        opacity = jax.nn.sigmoid(channel(3))
        extent = jax.nn.sigmoid(channel(5) + channel(6) + channel(7))
        lead = channel(8)
        denom = 1.0 + lead * lead + channel(9) * channel(9) + channel(10) * channel(10) + channel(11) * channel(11)
        facing = lead * lead / denom
        raw = channel(4)
        depth = jnp.maximum(raw, 0.0) + jnp.log1p(jnp.exp(-jnp.abs(raw)))
        return opacity, extent, lead, denom, facing, raw, depth

    opacity, extent, lead, denom, facing, raw, depth = shared()
    footprint = opacity * extent * facing
    channels = [jax.nn.sigmoid(channel(index)) * footprint for index in range(3)]
    channels += [footprint, depth * footprint]
    for index, value in enumerate(channels):
        for view in range(NVIEW):
            feat[index * quads : (index + 1) * quads, view * PP : (view + 1) * PP] = value[
                view * quads : (view + 1) * quads
            ]
    rendered = jnp.dot(feat[...], weight_ref[...], precision=HIGHEST, preferred_element_type=F32)
    parts = [rendered[index * quads : (index + 1) * quads] for index in range(5)]
    lane = lax.broadcasted_iota(jnp.int32, (quads, span), 1)
    live = jnp.where(lane < view_ref[0] * PP, mask_ref[...], 0).astype(F32)
    term = jnp.zeros((quads, span), F32)
    slopes = []
    for index in range(3):
        error = parts[index] - target_ref[index * quads : (index + 1) * quads, :].astype(F32)
        term = term + live * error * error
        slopes.append(2.0 * scale * live * error)
    below = 1.0 + parts[3]
    depth_out = parts[4] / below

    slope = jnp.zeros((quads, span), F32)
    for which, shift in enumerate((1, P_SIZE)):
        count = counts[which * quads : (which + 1) * quads]
        weight = DEPTH_WEIGHT * count * live * pltpu.roll(live, span - shift, 1)
        gap = depth_out - pltpu.roll(depth_out, span - shift, 1)
        term = term + weight * gap * gap
        pull = 2.0 * scale * weight * gap
        slope = slope + pull - pltpu.roll(pull, shift, 1)
    term_ref[...] = jnp.full(term_ref.shape, jnp.sum(term), F32)
    over = slope / below
    slopes += [-over * depth_out, over]
    stacked = jnp.concatenate(slopes, 0)
    dfeat[...] = lax.dot_general(
        stacked, weight_ref[...], (((1,), (1,)), ((), ())), precision=HIGHEST, preferred_element_type=F32
    )

    def feature_grad(index):
        return jnp.concatenate(
            [
                dfeat[index * quads : (index + 1) * quads, view * PP : (view + 1) * PP]
                for view in range(NVIEW)
            ],
            0,
        )

    def put(index, value):
        grad_ref[:, index * PP : (index + 1) * PP] = value.astype(BF16)

    d_foot = feature_grad(3)
    for index in range(3):
        tint = jax.nn.sigmoid(channel(index))
        upper = feature_grad(index)
        d_foot = d_foot + upper * tint
        put(index, upper * footprint * tint * (1.0 - tint))
    d_last = feature_grad(4)
    d_foot = d_foot + d_last * depth
    put(3, d_foot * extent * facing * opacity * (1.0 - opacity))
    put(4, d_last * footprint * jax.nn.sigmoid(raw))
    d_extent = d_foot * opacity * facing * extent * (1.0 - extent)
    for index in (5, 6, 7):
        put(index, d_extent)
    d_facing = d_foot * opacity * extent
    put(8, d_facing * 2.0 * lead / denom * (1.0 - facing))
    for index in (9, 10, 11):
        put(index, -2.0 * d_facing * facing / denom * channel(index))


def scene_targets(targets, mask, quads):
    slots = targets.shape[0]
    wanted = targets.reshape(slots, 3, quads, PP).transpose(1, 2, 0, 3).reshape(3 * quads, slots * PP)
    valid = mask.reshape(slots, quads, PP).transpose(1, 0, 2).reshape(quads, slots * PP)
    return wanted, valid


def render(gaussians, weights, targets, mask, pairs, view_count, pair_total):
    slots, views = weights.shape[:2]
    spread = weights.transpose(1, 2, 0, 3).reshape(views * PP, slots * PP)
    quads = gaussians.shape[0] // NVIEW
    wanted, valid = scene_targets(targets, mask, quads)
    vmem = pl.BlockSpec(memory_space=pltpu.VMEM)
    smem = pl.BlockSpec(memory_space=pltpu.SMEM)
    return pl.pallas_call(
        render_kernel,
        out_shape=[
            jax.ShapeDtypeStruct(gaussians.shape, BF16),
            jax.ShapeDtypeStruct((8, LANES), F32),
        ],
        in_specs=[vmem] * 5 + [smem] * 2,
        out_specs=[vmem] * 2,
        scratch_shapes=[pltpu.VMEM((5 * quads, views * PP), F32)] * 2
        + [pltpu.VMEM((2 * quads, slots * PP), F32)],
        compiler_params=pltpu.CompilerParams(vmem_limit_bytes=48 * MIB),
        name="render",
    )(gaussians, spread, wanted, valid, pairs, view_count, pair_total)


def forward_plain(shards, patches, features, kinds):
    weights = [lax.all_gather(shard, BOTH, axis=0, tiled=True) for shard in shards]
    groups = lax.axis_size(NARROW)
    rows = patches.shape[0]
    gains = weights[0][:, features : features + kinds].T.astype(F32)
    embedded = back_mul(patches[:, :features], weights[0][:, :features])
    normed_one = layer_norm(embedded, gains[0], gains[3]).astype(BF16)
    mixed = matmul(normed_one, weights[1]).astype(BF16).reshape(rows, 3, groups, -1)
    mixed = mixed.transpose(2, 1, 0, 3)
    qkv = lax.all_to_all(mixed, NARROW, split_axis=0, concat_axis=0, tiled=True)
    width = qkv.shape[-1]
    length = groups * rows
    heads = width // HD
    parts = [qkv[:, part].reshape(length, heads, HD) for part in range(3)]
    attended, logsum = attention_forward(*parts)
    log_sums = logsum.transpose(0, 2, 1).reshape(groups, rows, heads)
    returned = lax.all_to_all(
        attended.reshape(groups, rows, width), NARROW, split_axis=0, concat_axis=0, tiled=True
    )
    returned = returned.transpose(1, 0, 2).reshape(rows, D)
    mid = embedded + matmul(returned, weights[2])
    normed_two = layer_norm(mid, gains[1], gains[4]).astype(BF16)
    expanded = matmul(normed_two, weights[3])
    half = 0.5 * (1.0 + lax.erf(expanded * (0.5**0.5)))
    activated = (expanded * half).astype(BF16)
    bell = jnp.exp(-0.5 * expanded * expanded) * 0.3989422804014327
    slopes = (half + expanded * bell).astype(BF16)
    last = mid + matmul(activated, weights[4])
    normed_three = layer_norm(last, gains[2], gains[5]).astype(BF16)
    return Bag(
        dict(
        w1=weights[1],
        w2=weights[2],
        w3=weights[3],
        w4=weights[4],
        w5=weights[5],
        gains=gains,
        embedded=embedded,
        mid=mid,
        last=last,
        slopes=slopes,
        t1=normed_one.T,
        t2=returned.T,
        t3=normed_two.T,
        hidden=activated,
        t5=normed_three.T,
        qkv=qkv,
        heads_out=attended,
        log_sums=log_sums,
        gaussians=matmul(normed_three, weights[5]),
    ).items())


def backward_plain(kept, patches, gauss_low, term, features, kinds):
    gains = kept.gains
    weights = [None, kept.w1, kept.w2, kept.w3, kept.w4, kept.w5]
    norm_back_one = jax.vjp(layer_norm, kept.embedded, gains[0], gains[3])[1]
    norm_back_two = jax.vjp(layer_norm, kept.mid, gains[1], gains[4])[1]
    norm_back_three = jax.vjp(layer_norm, kept.last, gains[2], gains[5])[1]
    qkv = kept.qkv
    groups, _, rows, width = qkv.shape
    length = groups * rows
    heads = width // HD
    queries, keys, values = (qkv[:, part].reshape(length, heads, HD) for part in range(3))
    blocked = min(512, length)
    logsum = kept.log_sums[:, :, :heads].reshape(length // blocked, blocked, heads)
    residual_grad, gain_three, shift_three = norm_back_three(back_mul(gauss_low, weights[5]))
    shrink_low = residual_grad.astype(BF16)
    expand_low = (back_mul(shrink_low, weights[4]) * kept.slopes.astype(F32)).astype(BF16)
    through_two, gain_two, shift_two = norm_back_two(back_mul(expand_low, weights[3]))
    residual_grad = residual_grad + through_two
    merge_low = residual_grad.astype(BF16)
    out_grad = back_mul(merge_low, weights[2]).astype(BF16).reshape(rows, groups, width)
    head_grad = lax.all_to_all(
        out_grad.transpose(1, 0, 2), NARROW, split_axis=0, concat_axis=0, tiled=True
    ).reshape(length, heads, HD)
    grads = attention_backward(queries, keys, values, logsum.transpose(0, 2, 1), head_grad)
    stacked = jnp.stack(grads, 1).astype(BF16).reshape(groups, rows, 3, width)
    mixed_grad = lax.all_to_all(stacked, NARROW, split_axis=0, concat_axis=0, tiled=True)
    mixed_grad = mixed_grad.transpose(1, 2, 0, 3).reshape(rows, 3 * D)
    through_one, gain_one, shift_one = norm_back_one(back_mul(mixed_grad, weights[1]))
    embed_grad = (residual_grad + through_one).astype(BF16)
    grad_norms = jnp.stack([gain_one, gain_two, gain_three, shift_one, shift_two, shift_three])
    lefts = [embed_grad.T, kept.t1, kept.t2, kept.t3, kept.hidden.T, kept.t5]
    rights = [patches, mixed_grad, merge_low, expand_low, shrink_low, gauss_low]
    products = [matmul(left, right) for left, right in zip(lefts, rights)]
    products[0] = products[0].at[:, features : features + kinds].add(grad_norms.T)
    sums = [
        lax.psum_scatter(
            product.astype(BF16), BOTH, scatter_dimension=0, tiled=True
        ).astype(F32)
        for product in products
    ]
    squares = sum(jnp.sum(part * part) for part in sums)
    loss_sum, square_sum = lax.psum((term[0, 0], squares), BOTH)
    return sums, loss_sum, square_sum


def update_kernel(features, total_ref, sums_ref, *refs):
    sources, targets, refs = refs[:27], refs[27:48], refs[48:]
    loss_ref, norm_ref, refs = refs[0], refs[1], refs[2:]
    inside, news, refs = refs[:27], refs[27:48], refs[48:]
    turned, turned_four, in_sem, out_sem = refs
    loads = [pltpu.make_async_copy(source, dest, in_sem.at[i]) for i, (source, dest) in enumerate(zip(sources, inside))]
    stores = [pltpu.make_async_copy(source, dest, out_sem.at[i]) for i, (source, dest) in enumerate(zip(news, targets))]
    for copy in loads:
        copy.start()
    grads, olds = inside[:6], inside[6:]
    square_sum = sums_ref[1:2, 0:1]
    grad_norm = jnp.sqrt(square_sum)
    factor = jnp.minimum(1.0, CLIP_NORM / (grad_norm + 1e-06))
    norm_ref[...] = grad_norm
    loss_ref[...] = sums_ref[0:1, 0:1] / total_ref[0].astype(F32)
    width = grads[0].shape[1]
    for which in range(7):
        if which < 6:
            loads[which].wait()
        if which == 0:
            turned[...] = grads[0][:, width - LANES :].T
        if which == 4:
            turned_four[...] = grads[4][...].T
        for copy in loads[6 + 3 * which : 9 + 3 * which]:
            copy.wait()
        weight, first, second = olds[3 * which : 3 * which + 3]
        rows, columns = weight.shape
        chunk = min(8, rows)

        def one(step, carry):
            spot = pl.ds(pl.multiple_of(step * chunk, chunk), chunk)
            if which == 0:
                grad = grads[0][spot, 0:columns]
            elif which == 4:
                grad = turned_four[spot, :]
            elif which == 6:
                grad = turned[features % LANES : features % LANES + rows, 0:columns]
            else:
                grad = grads[which][spot, :]
            values = adamw(weight[spot, :], first[spot, :], second[spot, :], grad * factor, RATES[which])
            for dest, value in zip(news[3 * which : 3 * which + 3], values):
                dest[spot, :] = value
            return carry

        lax.fori_loop(0, rows // chunk, one, 0)
        for copy in stores[3 * which : 3 * which + 3]:
            copy.start()
    for copy in stores:
        copy.wait()


def update_all(olds, sums, totals, pair_total, features):
    vmem = pl.BlockSpec(memory_space=pltpu.VMEM)
    smem = pl.BlockSpec(memory_space=pltpu.SMEM)
    hbm = pl.BlockSpec(memory_space=pltpu.HBM)
    shapes = [jax.ShapeDtypeStruct(old.shape, F32) for old in olds]
    inside = [pltpu.VMEM(value.shape, F32) for value in list(sums) + list(olds)]
    return pl.pallas_call(
        functools.partial(update_kernel, features),
        out_shape=shapes + [jax.ShapeDtypeStruct((1, 1), F32)] * 2,
        in_specs=[smem, vmem] + [hbm] * 27,
        out_specs=[hbm] * 21 + [vmem] * 2,
        scratch_shapes=inside
        + [pltpu.VMEM(old.shape, F32) for old in olds]
        + [
            pltpu.VMEM((LANES, sums[0].shape[0]), F32),
            pltpu.VMEM(olds[12].shape, F32),
            pltpu.SemaphoreType.DMA((27,)),
            pltpu.SemaphoreType.DMA((21,)),
        ],
        compiler_params=pltpu.CompilerParams(vmem_limit_bytes=60 * MIB),
        name="update",
    )(pair_total, totals, *sums, *olds)


def body(
    views,
    render_w,
    targets,
    pix_mask,
    pairs,
    view_count,
    pair_total,
    embed_weight,
    embed_first,
    embed_second,
    mixer_weight,
    mixer_first,
    mixer_second,
    merge_weight,
    merge_first,
    merge_second,
    expand_weight,
    expand_first,
    expand_second,
    shrink_weight,
    shrink_first,
    shrink_second,
    unpatch_weight,
    unpatch_first,
    unpatch_second,
    norm_params,
    norm_first,
    norm_second,
):
    masters = (embed_weight, mixer_weight, merge_weight, expand_weight, shrink_weight, unpatch_weight, norm_params)
    firsts = (embed_first, mixer_first, merge_first, expand_first, shrink_first, unpatch_first, norm_first)
    seconds = (embed_second, mixer_second, merge_second, expand_second, shrink_second, unpatch_second, norm_second)
    groups = lax.axis_size(NARROW)
    wide_count = lax.axis_size(WIDE)
    features = embed_weight.shape[0]
    kinds = norm_params.shape[0]
    padded = -(-(features + kinds) // LANES) * LANES
    fill = padded - features - kinds
    by_kernel = mixer_weight.shape[0] % 16 == 0 and shrink_weight.shape[0] % LANES == 0

    patches = views.reshape(-1, features)
    if by_kernel:
        raw = (embed_weight.T,) + masters[1:6]
        wanted, valid = scene_targets(targets[0], pix_mask[0], patches.shape[0] // NVIEW)
        scene = (render_w[0], wanted, valid, pairs[0], view_count, pair_total)
        kept = forward_all(raw, norm_params, patches, scene, wide_count, groups)
        *sums, totals = backward_all(
            kept, kept.padded, kept.gauss, kept.term, features % LANES, wide_count, groups
        )
        olds = []
        for triple in zip(masters, firsts, seconds):
            olds += triple
        olds[:3] = [old.T for old in olds[:3]]
        *news, loss, grad_norm = update_all(olds, sums, totals, pair_total, features)
        news[:3] = [new.T for new in news[:3]]
        return tuple(news) + (loss[0, 0], grad_norm[0, 0])
    else:
        patches = jnp.pad(patches, ((0, 0), (0, padded - features)))
        first_shard = jnp.concatenate([embed_weight.T, norm_params.T], 1)
        first_shard = jnp.pad(first_shard.astype(BF16), ((0, 0), (0, fill)))
        shards = [first_shard] + [weight.astype(BF16) for weight in masters[1:6]]
        kept = forward_plain(shards, patches, features, kinds)
    divisor = pair_total[0].astype(F32)
    gauss_low, term = render(
        kept.gaussians, render_w[0], targets[0], pix_mask[0], pairs[0], view_count, pair_total
    )
    sums, loss_sum, square_sum = backward_plain(kept, patches, gauss_low, term, features, kinds)
    first_sum = sums[0].T
    grads = [first_sum[:features]] + list(sums[1:]) + [first_sum[features : features + kinds]]
    loss = loss_sum / divisor
    grad_norm = jnp.sqrt(square_sum)
    factor = jnp.minimum(1.0, CLIP_NORM / (grad_norm + 1e-06))
    results = []
    for which in range(7):
        results += adamw(masters[which], firsts[which], seconds[which], grads[which] * factor, RATES[which])
    return tuple(results) + (loss, grad_norm)


def solution(mesh):
    columns = P(None, BOTH)
    rows = P(BOTH, None)
    weights = (columns,) * 3 + (rows,) * 15 + (columns,) * 3
    return jax.shard_map(
        body,
        mesh=mesh,
        in_specs=(
            P(WIDE, None, NARROW, None),
            P(WIDE, None, None, None, None),
            P(WIDE, None, None, NARROW),
            P(WIDE, None, NARROW),
            P(WIDE, None, NARROW),
            P(WIDE),
            P(),
        )
        + weights,
        out_specs=weights + (P(), P()),
        check_vma=False,
    )
```
